32 devices in a mesh: dp: 8 (over z, y), pipe: 4 (over x, core).
Axes of the slice: x: 2, y: 2, z: 4, core: 2. Of those that a mesh axis runs over, the one named last changes fastest.
Arguments:
- teach_in: bfloat16 [4, 16, 12, 12, 1024], P('pipe', 'dp'), may hold values from -6 to 6
- stud_in: bfloat16 [4, 24, 8, 8, 1024], P('pipe', 'dp'), may hold values from -6 to 6
- params: float32 [4, 4986880], P('pipe', 'dp')
- owners: int32 [4, 8], P('pipe'), may hold values from 0 to 7, as said below
- depth_gates: int32 [4], replicated, may hold values from 0 to 1, as said below
- teach_ids: int32 [4, 16], P(None, 'dp'), may hold values from 0 to 31, as said below
- stud_ids: int32 [4, 24], P(None, 'dp'), may hold values from 0 to 31, as said below
- targets: float32 [32, 2048], replicated, may hold values from -6 to 6
- moment: float32 [4, 4986880], P('pipe', 'dp'), may hold values from -0.00048828125 to 0.00048828125
- second: float32 [4, 4986880], P('pipe', 'dp'), may hold values from 2.475685e-09 to 1.9995918e-08
- gram_stats: float32 [4, 1024, 128], P('pipe', 'dp')
- eigen_basis: float32 [4, 1024, 128], P('pipe', 'dp')
Outputs:
- segment_teach: bfloat16 [4, 4, 16, 6, 6, 2048], P('pipe', None, 'dp')
- segment_stud: bfloat16 [4, 4, 24, 4, 4, 2048], P('pipe', None, 'dp')
- grad_teach: bfloat16 [4, 16, 12, 12, 1024], P('pipe', 'dp')
- grad_stud: bfloat16 [4, 24, 8, 8, 1024], P('pipe', 'dp')
- norm_stats: float32 [4, 4, 8, 2, 3072], P('pipe', None, 'dp')
- grad_norm: float32 [], replicated
- clipped_grads: float32 [4, 4986880], P('pipe', 'dp')
- moment_new: float32 [4, 4986880], P('pipe', 'dp')
- second_new: float32 [4, 4986880], P('pipe', 'dp')
- params_new: float32 [4, 4986880], P('pipe', 'dp')
- gram_new: float32 [4, 1024, 128], P('pipe', 'dp')
- basis_new: float32 [4, 1024, 128], P('pipe', 'dp')
The draws below stay inside these ranges and needn't reach their ends.
Inputs may be any that keep to these rules, and one draw needn't show every extreme that they name: `owners`: each row is a permutation. `depth_gates`: exactly one micro-batch has gate 0. `teach_ids`: every image has exactly two teacher crops. `stud_ids`: every image has exactly three student crops.
All inputs are finite; a program needn't handle non-finite values.
Results may differ from the reference program's by a relative error of at most 0.02.
Values may be sent and summed in bfloat16 or wider, within the bound.
A program may use at most 896 MiB of HBM per device.

```python
import math
import jax
import jax.numpy as jnp
from jax import lax

C_IN = 1024
MID = 512
C_OUT = 2048
IMG_DEV = 1
TS = 12
SH = 8
SW = 8
SECTIONS = 4
STEP = 10
NS_STEPS = 5
OWNERS = 8
TEACH_ALL = 16
STUD_ALL = 24
IMAGES = 32
TO = 6
SOH = 4
SOW = 4
SPAN = 623360
PSEC = 4986880
PCOUNT = 10502144


def draw_layout(section):
    if section == 0:
        return [((C_IN, MID), 0), ((9 * MID, MID), 0), ((C_IN, C_OUT), 0), ((MID,), 1), ((MID,), 2), ((MID,), 1), ((MID,), 2), ((C_OUT,), 1), ((C_OUT,), 2)]
    if section == 2:
        return [((C_OUT, MID), 0), ((9 * MID, MID), 0), ((MID,), 1), ((MID,), 2), ((MID,), 1), ((MID,), 2)]
    return [((MID, C_OUT), 0), ((C_OUT,), 1), ((C_OUT,), 2)]


def owner_table(key):
    table_key = jax.random.fold_in(key, 11)
    section_keys = jax.random.split(table_key, SECTIONS)

    def one_row(row_key):
        return jax.random.permutation(row_key, OWNERS)
    return jax.vmap(one_row)(section_keys).astype(jnp.int32)


def draw_owners(key, part):
    return owner_table(key)


def draw_params(key, part):
    owner_rows = owner_table(key)
    key = jax.random.fold_in(key, 21)
    normal_key, uniform_key = jax.random.split(key)
    normals = jax.random.normal(normal_key, (SECTIONS, PSEC), jnp.float32)
    uniforms = jax.random.uniform(uniform_key, (SECTIONS, PSEC), jnp.float32, -0.5, 0.5)
    rows = []
    for section in range(SECTIONS):
        scale_parts = []
        gain_parts = []
        used = 0
        for entry_shape, entry_kind in draw_layout(section):
            entry_size = math.prod(entry_shape)
            used = used + entry_size
            if entry_kind == 0:
                scale_parts.append(jnp.full((entry_size,), entry_shape[0] ** (-0.5), jnp.float32))
                gain_parts.append(jnp.zeros((entry_size,), jnp.float32))
            elif entry_kind == 1:
                scale_parts.append(jnp.zeros((entry_size,), jnp.float32))
                gain_parts.append(jnp.ones((entry_size,), jnp.float32))
            else:
                scale_parts.append(jnp.full((entry_size,), 0.3, jnp.float32))
                gain_parts.append(jnp.zeros((entry_size,), jnp.float32))
        scale_parts.append(jnp.full((PSEC - used,), 0.02, jnp.float32))
        gain_parts.append(jnp.zeros((PSEC - used,), jnp.float32))
        scales = jnp.concatenate(scale_parts)
        gains = jnp.concatenate(gain_parts)
        real = normals[section] * scales + gains * jnp.exp(uniforms[section])
        blocks = real.reshape(OWNERS, SPAN)
        rows.append(blocks[owner_rows[section]].reshape(PSEC))
    return jnp.stack(rows)


def draw_depth_gates(key, part):
    key = jax.random.fold_in(key, 31)
    order = jax.random.permutation(key, SECTIONS)
    return (order != 0).astype(jnp.int32)


def draw_teach_ids(key, part):
    key = jax.random.fold_in(key, 41)
    order = jax.random.permutation(key, 2 * IMAGES)
    return (order // 2).reshape(SECTIONS, TEACH_ALL).astype(jnp.int32)


def draw_stud_ids(key, part):
    key = jax.random.fold_in(key, 43)
    order = jax.random.permutation(key, 3 * IMAGES)
    return (order // 3).reshape(SECTIONS, STUD_ALL).astype(jnp.int32)


def draw_gram_stats(key, part):
    key = jax.random.fold_in(key, 51)
    diag_key, noise_key = jax.random.split(key)
    base = 0.0526 * (SPAN // 128) / PCOUNT
    diagonal = base * jnp.exp(jax.random.uniform(diag_key, (SECTIONS, OWNERS, 128), jnp.float32, 0.0, math.log(4.0)))
    noise = jax.random.normal(noise_key, (SECTIONS, OWNERS, 128, 128), jnp.float32)
    symmetric = (noise + jnp.swapaxes(noise, 2, 3)) * (0.03 * base)
    identity = jnp.eye(128, dtype=jnp.float32)
    full = symmetric * (1.0 - identity) + identity * diagonal[:, :, None, :]
    return full.reshape(SECTIONS, OWNERS * 128, 128)


def draw_eigen_basis(key, part):
    key = jax.random.fold_in(key, 61)
    noise = jax.random.normal(key, (SECTIONS, OWNERS, 128, 128), jnp.float32)
    identity = jnp.eye(128, dtype=jnp.float32)
    return (identity + 0.03 * noise).reshape(SECTIONS, OWNERS * 128, 128)


def shard_levels(stream_key, shape, cuts, smallest, top_value):
    def one(axis_at, parts):
        draws = jax.random.uniform(jax.random.fold_in(jax.random.fold_in(stream_key, 6), axis_at), (parts,), jnp.float32, smallest / len(cuts), top_value / len(cuts))
        return jnp.repeat(jnp.exp(draws), shape[axis_at] // parts).reshape((-1,) + (1,) * (len(shape) - axis_at - 1))

    level = one(*cuts[0])
    for cut in cuts[1:]:
        level = level * one(*cut)
    return level


def gaussian(rng, extent, deviation, most, cuts=(), kind=jnp.bfloat16):
    values = deviation * jax.random.normal(rng, extent, jnp.float32)
    if cuts:
        values = values * shard_levels(rng, extent, cuts, -0.22, 0.18)
    return jnp.clip(values, -most, most).astype(kind)


def setup_inputs(seed: int = 0) -> dict:
    keys = jax.random.split(jax.random.key(seed), 13)
    return {
        "teach_in": gaussian(keys[0], (SECTIONS, TEACH_ALL, TS, TS, C_IN), 1.0, 6.0, ((0, 4), (1, 8))),
        "stud_in": gaussian(keys[1], (SECTIONS, STUD_ALL, SH, SW, C_IN), 1.0, 6.0, ((0, 4), (1, 8))),
        "params": draw_params(jax.random.fold_in(keys[12], 71), 0),
        "owners": draw_owners(jax.random.fold_in(keys[12], 71), 0),
        "depth_gates": draw_depth_gates(jax.random.fold_in(keys[12], 71), 0),
        "teach_ids": draw_teach_ids(jax.random.fold_in(keys[12], 71), 0),
        "stud_ids": draw_stud_ids(jax.random.fold_in(keys[12], 71), 0),
        "targets": gaussian(keys[7], (IMAGES, C_OUT), 1.0, 6.0, (), jnp.float32),
        "moment": gaussian(keys[8], (SECTIONS, PSEC), (0.111 * PCOUNT ** -0.5), 0.00048828125, ((0, 4), (1, 8)), jnp.float32),
        "second": jnp.clip(jnp.exp(math.log(1.999591781043364e-08) - 2.089011 * jax.random.uniform(keys[9], (SECTIONS, PSEC), jnp.float32) ** shard_levels(keys[9], (SECTIONS, PSEC), ((0, 4), (1, 8)), -0.2, 0.2)), 2.475684990344007e-09, 1.999591781043364e-08),
        "gram_stats": draw_gram_stats(jax.random.fold_in(keys[12], 71), 0),
        "eigen_basis": draw_eigen_basis(jax.random.fold_in(keys[12], 71), 0),
    }


HIGH = lax.Precision.HIGHEST
NORM_EPS = 1e-05
POOL_EPS = 1e-06
CLIP_NORM = 1.0
LEARN_RATE = 0.02
DECAY_FIRST = 0.9
DECAY_SECOND = 0.95
DECAY_STATS = 0.95
ADAM_EPS = 1e-08
WEIGHT_DECAY = 0.01

@jax.custom_vjp
def low(v):
    return lax.optimization_barrier(v.astype(jnp.bfloat16)).astype(jnp.float32)

@jax.custom_vjp
def low_back(v):
    return v

def low_keep(v):
    return (low(v), None)

def low_pass(kept, grad):
    return (grad,)

def back_keep(v):
    return (v, None)

def back_low(kept, grad):
    return (low(grad),)
low.defvjp(low_keep, low_pass)
low_back.defvjp(back_keep, back_low)

def section_shapes(section):
    if section == 0:
        return [('first_conv', (C_IN, MID)), ('middle_conv', (9 * MID, MID)), ('skip_conv', (C_IN, C_OUT)), ('first_gain', (MID,)), ('first_bias', (MID,)), ('middle_gain', (MID,)), ('middle_bias', (MID,)), ('skip_gain', (C_OUT,)), ('skip_bias', (C_OUT,))]
    if section == 2:
        return [('first_conv', (C_OUT, MID)), ('middle_conv', (9 * MID, MID)), ('first_gain', (MID,)), ('first_bias', (MID,)), ('middle_gain', (MID,)), ('middle_bias', (MID,))]
    return [('last_conv', (MID, C_OUT)), ('last_gain', (C_OUT,)), ('last_bias', (C_OUT,))]

def unpack(flat_vector, section):
    pieces = {}
    offset = 0
    for entry_name, entry_shape in section_shapes(section):
        entry_size = math.prod(entry_shape)
        pieces[entry_name] = flat_vector[offset:offset + entry_size].reshape(entry_shape)
        offset = offset + entry_size
    return pieces

def hop(value):
    return low_back(low(value))

def point_conv(groups, weight):
    return tuple((low_back(jnp.einsum('khwc,cd->khwd', portion, weight, precision=HIGH)) for portion in groups))

def patches(portion, stride):
    height = portion.shape[1]
    across = portion.shape[2]
    padded = jnp.pad(portion, ((0, 0), (1, 1), (1, 1), (0, 0)))
    shifted = [padded[:, row_off:row_off + height:stride, col_off:col_off + across:stride, :] for row_off in range(3) for col_off in range(3)]
    return jnp.concatenate(shifted, axis=-1)

def area_conv(groups, weight, stride):
    return tuple((low_back(jnp.einsum('khwc,cd->khwd', patches(portion, stride), weight, precision=HIGH)) for portion in groups))

def batch_norm(groups, gain, bias):
    rows_total = sum((portion.shape[0] * portion.shape[1] * portion.shape[2] for portion in groups))
    centre = sum((lax.optimization_barrier(jnp.sum(portion, axis=(0, 1, 2))) for portion in groups)) / rows_total
    spread = sum((lax.optimization_barrier(jnp.sum(jnp.square(portion - centre), axis=(0, 1, 2))) for portion in groups)) / rows_total
    inverse = lax.rsqrt(spread + NORM_EPS)
    normed = tuple((gain * ((portion - centre) * inverse) + bias for portion in groups))
    return (normed, centre, spread)

def front_section(pieces, inputs):
    first = point_conv(inputs, pieces['first_conv'])
    normed_a, centre_a, spread_a = batch_norm(first, pieces['first_gain'], pieces['first_bias'])
    hidden = tuple((low(jax.nn.softplus(portion)) for portion in normed_a))
    middle = area_conv(hidden, pieces['middle_conv'], 2)
    normed_b, centre_b, spread_b = batch_norm(middle, pieces['middle_gain'], pieces['middle_bias'])
    narrow = tuple((jax.nn.softplus(portion) for portion in normed_b))
    reduced = tuple((portion[:, ::2, ::2, :] for portion in inputs))
    skipped = point_conv(reduced, pieces['skip_conv'])
    wide, centre_p, spread_p = batch_norm(skipped, pieces['skip_gain'], pieces['skip_bias'])
    norm_rows = jnp.stack([jnp.concatenate([centre_a, centre_b, centre_p]), jnp.concatenate([spread_a, spread_b, spread_p])])
    return (wide, narrow, norm_rows)

def join_section(pieces, wide, narrow):
    last = point_conv(narrow, pieces['last_conv'])
    normed, centre, spread = batch_norm(last, pieces['last_gain'], pieces['last_bias'])
    joined = tuple((jax.nn.softplus(skip_part + branch_part) for skip_part, branch_part in zip(wide, normed)))
    filler = jnp.zeros((2 * MID,), jnp.float32)
    norm_rows = jnp.stack([jnp.concatenate([centre, filler]), jnp.concatenate([spread, filler])])
    return (joined, norm_rows)

def split_section(pieces, wide):
    first = point_conv(wide, pieces['first_conv'])
    normed_a, centre_a, spread_a = batch_norm(first, pieces['first_gain'], pieces['first_bias'])
    hidden = tuple((low(jax.nn.softplus(portion)) for portion in normed_a))
    middle = area_conv(hidden, pieces['middle_conv'], 1)
    normed_b, centre_b, spread_b = batch_norm(middle, pieces['middle_gain'], pieces['middle_bias'])
    narrow = tuple((jax.nn.softplus(portion) for portion in normed_b))
    filler = jnp.zeros((C_OUT,), jnp.float32)
    norm_rows = jnp.stack([jnp.concatenate([centre_a, centre_b, filler]), jnp.concatenate([spread_a, spread_b, filler])])
    return (narrow, norm_rows)

def pooled_loss(final, targets, teach_pick, stud_pick):
    loss_sum = jnp.zeros((), jnp.float32)
    for portion, picks in zip(final, (teach_pick, stud_pick)):
        cubes = lax.optimization_barrier(jnp.mean(portion * portion * portion, axis=(1, 2))) + POOL_EPS
        pooled = jnp.exp(jnp.log(cubes) / 3.0)
        pixels = portion.shape[1] * portion.shape[2]
        loss_sum = loss_sum + pixels * jnp.sum(pooled * targets[picks])
    return loss_sum

def one_batch(rounded, teach_x, stud_x, gate, targets, teach_pick, stud_pick):
    inputs = (low(teach_x.reshape(OWNERS, 2 * IMG_DEV, TS, TS, C_IN)), low(stud_x.reshape(OWNERS, 3 * IMG_DEV, SH, SW, C_IN)))
    wide, narrow, stats_front = jax.vmap(front_section, in_axes=(None, 0))(rounded[0], inputs)
    wide = tuple((hop(portion) for portion in wide))
    narrow = tuple((hop(portion) for portion in narrow))
    joined, stats_join = jax.vmap(join_section, in_axes=(None, 0, 0))(rounded[1], wide, narrow)
    joined = tuple((hop(portion) for portion in joined))
    branch, stats_split = jax.vmap(split_section, in_axes=(None, 0))(rounded[2], joined)
    relay = tuple((hop(portion) for portion in joined))
    branch = tuple((hop(portion) for portion in branch))
    ending, stats_last = jax.vmap(join_section, in_axes=(None, 0, 0))(rounded[3], relay, branch)
    final = tuple((jnp.where(gate > 0, end_part, relay_part) for end_part, relay_part in zip(ending, relay)))
    losses = jax.vmap(pooled_loss, in_axes=(0, None, 0, 0))(final, targets, teach_pick.reshape(OWNERS, 2 * IMG_DEV), stud_pick.reshape(OWNERS, 3 * IMG_DEV))
    gate_scale = gate.astype(jnp.float32)
    norm_rows = jnp.stack([stats_front, stats_join, stats_split * gate_scale, stats_last * gate_scale])
    return (jnp.sum(losses), (wide, joined, relay, final, norm_rows))

def objective(flats, teach_all, stud_all, depth_gates, targets, teach_ids, stud_ids):
    rounded = []
    for section in range(SECTIONS):
        pieces = unpack(flats[section], section)
        rounded.append({entry_name: low(entry_value) for entry_name, entry_value in pieces.items()})
    loss_sum = jnp.zeros((), jnp.float32)
    extras_all = []
    checked = jax.checkpoint(one_batch)
    for micro_batch in range(SECTIONS):
        part_loss, extras = checked(rounded, teach_all[micro_batch], stud_all[micro_batch], depth_gates[micro_batch], targets, teach_ids[micro_batch], stud_ids[micro_batch])
        loss_sum = loss_sum + part_loss
        extras_all.append(extras)
    return (loss_sum, extras_all)

def reference(teach_in, stud_in, params, owners, depth_gates, teach_ids, stud_ids, targets, moment, second, gram_stats, eigen_basis):
    inverse = jnp.argsort(owners, axis=1).astype(jnp.int32)
    real_rows = []
    for section in range(SECTIONS):
        blocks = params[section].reshape(OWNERS, SPAN)
        real_rows.append(blocks[inverse[section]].reshape(PSEC))

    def closed(flat_args, teach_all, stud_all):
        return objective(flat_args, teach_all, stud_all, depth_gates, targets, teach_ids, stud_ids)
    loss_sum, pullback, extras_all = jax.vjp(closed, tuple(real_rows), teach_in.astype(jnp.float32), stud_in.astype(jnp.float32), has_aux=True)
    flat_grads, teach_grad, stud_grad = pullback(jnp.ones((), jnp.float32))
    segment_teach = jnp.stack([jnp.stack([extras_all[micro_batch][section][0].reshape(TEACH_ALL, TO, TO, C_OUT) for micro_batch in range(SECTIONS)]) for section in range(SECTIONS)])
    segment_stud = jnp.stack([jnp.stack([extras_all[micro_batch][section][1].reshape(STUD_ALL, SOH, SOW, C_OUT) for micro_batch in range(SECTIONS)]) for section in range(SECTIONS)])
    norm_stats = jnp.stack([extras_all[micro_batch][4] for micro_batch in range(SECTIONS)], axis=1)
    stored = []
    for section in range(SECTIONS):
        blocks = flat_grads[section].reshape(OWNERS, SPAN)
        stored.append(blocks[owners[section]])
    summed_grads = jnp.stack(stored)
    grad_norm = jnp.sqrt(jnp.sum(summed_grads * summed_grads))
    factor = jnp.minimum(1.0, CLIP_NORM / grad_norm)
    clipped = summed_grads * factor
    matrix = clipped.reshape(SECTIONS, OWNERS, SPAN // 128, 128)
    gram_old = gram_stats.reshape(SECTIONS, OWNERS, 128, 128)
    basis_old = eigen_basis.reshape(SECTIONS, OWNERS, 128, 128)
    gram_new = DECAY_STATS * gram_old + (1.0 - DECAY_STATS) * jnp.einsum('sjrk,sjrl->sjkl', matrix, matrix, precision=HIGH)
    product = jnp.einsum('sjkl,sjlm->sjkm', gram_new, basis_old, precision=HIGH)
    magnitude = jnp.sqrt(lax.optimization_barrier(jnp.sum(product * product, axis=(2, 3), keepdims=True)))
    rotation = product / magnitude
    for repeat in range(NS_STEPS):
        square = jnp.einsum('sjlk,sjlm->sjkm', rotation, rotation, precision=HIGH)
        rotation = 1.5 * rotation - 0.5 * jnp.einsum('sjkl,sjlm->sjkm', rotation, square, precision=HIGH)
    moment_old = moment.reshape(SECTIONS, OWNERS, SPAN // 128, 128)
    initial = jnp.einsum('sjrk,sjlk->sjrl', moment_old, basis_old, precision=HIGH)
    blended = DECAY_FIRST * initial + (1.0 - DECAY_FIRST) * matrix
    moment_new = jnp.einsum('sjrk,sjkl->sjrl', blended, rotation, precision=HIGH)
    rotated = jnp.einsum('sjrk,sjkl->sjrl', matrix, rotation, precision=HIGH)
    second_new = DECAY_SECOND * second.reshape(SECTIONS, OWNERS, SPAN // 128, 128) + (1.0 - DECAY_SECOND) * rotated * rotated
    correction = math.sqrt(1.0 - DECAY_SECOND ** STEP) / (1.0 - DECAY_FIRST ** STEP)
    direction = jnp.einsum('sjrl,sjkl->sjrk', moment_new / (jnp.sqrt(second_new) + ADAM_EPS), rotation, precision=HIGH) * correction
    weights = params.reshape(SECTIONS, OWNERS, SPAN // 128, 128)
    params_new = weights - LEARN_RATE * (direction + WEIGHT_DECAY * weights)
    return (segment_teach.astype(jnp.bfloat16), segment_stud.astype(jnp.bfloat16), teach_grad.astype(jnp.bfloat16), stud_grad.astype(jnp.bfloat16), norm_stats, grad_norm, clipped.reshape(SECTIONS, PSEC), moment_new.reshape(SECTIONS, PSEC), second_new.reshape(SECTIONS, PSEC), params_new.reshape(SECTIONS, PSEC), gram_new.reshape(SECTIONS, OWNERS * 128, 128), rotation.reshape(SECTIONS, OWNERS * 128, 128))
```

```python
import math

import jax
import jax.numpy as jnp
from jax import lax
from jax.sharding import PartitionSpec as P

C_IN = 1024
MID = 512
C_OUT = 2048
STEP = 10
NS_STEPS = 5


HIGH = lax.Precision.HIGHEST
NORM_EPS = 1e-05
POOL_EPS = 1e-06
CLIP_NORM = 1.0
LEARN_RATE = 0.02
DECAY_FIRST = 0.9
DECAY_SECOND = 0.95
DECAY_STATS = 0.95
ADAM_EPS = 1e-08
WEIGHT_DECAY = 0.01


def section_shapes(section):
    if section == 0:
        return [
            ("first_conv", (C_IN, MID)),
            ("middle_conv", (9 * MID, MID)),
            ("skip_conv", (C_IN, C_OUT)),
            ("first_gain", (MID,)),
            ("first_bias", (MID,)),
            ("middle_gain", (MID,)),
            ("middle_bias", (MID,)),
            ("skip_gain", (C_OUT,)),
            ("skip_bias", (C_OUT,)),
        ]
    if section == 2:
        return [
            ("first_conv", (C_OUT, MID)),
            ("middle_conv", (9 * MID, MID)),
            ("first_gain", (MID,)),
            ("first_bias", (MID,)),
            ("middle_gain", (MID,)),
            ("middle_bias", (MID,)),
        ]
    return [("last_conv", (MID, C_OUT)), ("last_gain", (C_OUT,)), ("last_bias", (C_OUT,))]


def unpack(flat_vector, section):
    pieces = {}
    offset = 0
    for entry_name, entry_shape in section_shapes(section):
        entry_size = math.prod(entry_shape)
        pieces[entry_name] = flat_vector[offset : offset + entry_size].reshape(entry_shape)
        offset = offset + entry_size
    return pieces


def pack(grads, section, flat_size):
    parts = [grads[entry_name].reshape(-1) for entry_name, entry_shape in section_shapes(section)]
    used = sum((math.prod(entry_shape) for entry_name, entry_shape in section_shapes(section)))
    parts.append(jnp.zeros((flat_size - used,), jnp.float32))
    return jnp.concatenate(parts)


def as_float(vector):
    return vector.astype(jnp.float32)


def to_low(groups):
    return tuple((portion.astype(jnp.bfloat16) for portion in groups))


def to_high(groups):
    return tuple((portion.astype(jnp.float32) for portion in groups))


def point_conv(groups, weight):
    return tuple(
        (
            jnp.einsum("khwc,cd->khwd", portion, weight, preferred_element_type=jnp.float32)
            for portion in groups
        )
    )


def point_back(grad_out, groups, weight):
    low_grads = to_low(grad_out)
    grad_input = tuple(
        (
            jnp.einsum("khwd,cd->khwc", grad_part, weight, preferred_element_type=jnp.float32)
            for grad_part in low_grads
        )
    )
    grad_weight = sum(
        (
            jnp.einsum("khwc,khwd->cd", in_part, grad_part, preferred_element_type=jnp.float32)
            for in_part, grad_part in zip(groups, low_grads)
        )
    )
    return (grad_input, grad_weight)


def patches(portion, stride):
    height = portion.shape[1]
    across = portion.shape[2]
    padded = jnp.pad(portion, ((0, 0), (1, 1), (1, 1), (0, 0)))
    shifted = [
        padded[:, row_off : row_off + height : stride, col_off : col_off + across : stride, :]
        for row_off in range(3)
        for col_off in range(3)
    ]
    return jnp.concatenate(shifted, axis=-1)


def area_conv(groups, weight, stride):
    columns = tuple((patches(portion, stride) for portion in groups))
    return (point_conv(columns, weight), columns)


def unpatch(grad_cols, height, across, stride):
    channels = grad_cols.shape[-1] // 9
    padded = jnp.zeros((grad_cols.shape[0], height + 2, across + 2, channels), jnp.float32)
    for row_off in range(3):
        for col_off in range(3):
            offset = (3 * row_off + col_off) * channels
            padded = padded.at[
                :, row_off : row_off + height : stride, col_off : col_off + across : stride, :
            ].add(grad_cols[..., offset : offset + channels])
    return padded[:, 1 : height + 1, 1 : across + 1, :]


def area_back(grad_out, columns, weight, stride, in_shapes):
    grad_cols, grad_weight = point_back(grad_out, columns, weight)
    grad_input = tuple(
        (
            unpatch(grad_part, shape_item[1], shape_item[2], stride)
            for grad_part, shape_item in zip(grad_cols, in_shapes)
        )
    )
    return (grad_input, grad_weight)


def batch_norm(groups, gain, bias):
    rows_total = sum((portion.shape[0] * portion.shape[1] * portion.shape[2] for portion in groups))
    centre = sum((jnp.sum(portion, axis=(0, 1, 2)) for portion in groups)) / rows_total
    spread = (
        sum((jnp.sum(jnp.square(portion - centre), axis=(0, 1, 2)) for portion in groups))
        / rows_total
    )
    inverse = lax.rsqrt(spread + NORM_EPS)
    standard = tuple(((portion - centre) * inverse for portion in groups))
    normed = tuple((gain * std_part + bias for std_part in standard))
    return (normed, (centre, spread, inverse, standard))


def norm_back(grad_out, gain, saved):
    centre, spread, inverse, standard = saved
    rows_total = sum(
        (portion.shape[0] * portion.shape[1] * portion.shape[2] for portion in standard)
    )
    grad_sum = sum((jnp.sum(grad_part, axis=(0, 1, 2)) for grad_part in grad_out))
    grad_dot = sum(
        (
            jnp.sum(grad_part * std_part, axis=(0, 1, 2))
            for grad_part, std_part in zip(grad_out, standard)
        )
    )
    grad_input = tuple(
        (
            gain
            * inverse
            * (grad_part - grad_sum / rows_total - std_part * (grad_dot / rows_total))
            for grad_part, std_part in zip(grad_out, standard)
        )
    )
    return (grad_input, grad_dot, grad_sum)


def through_softplus(grad_out, pre_values):
    return tuple(
        (grad_part * jax.nn.sigmoid(pre_part) for grad_part, pre_part in zip(grad_out, pre_values))
    )


def front_forward(pieces, inputs):
    first = point_conv(inputs, pieces["first_conv"])
    normed_a, saved_a = batch_norm(
        first, as_float(pieces["first_gain"]), as_float(pieces["first_bias"])
    )
    hidden = tuple((jax.nn.softplus(portion).astype(jnp.bfloat16) for portion in normed_a))
    middle, columns = area_conv(hidden, pieces["middle_conv"], 2)
    normed_b, saved_b = batch_norm(
        middle, as_float(pieces["middle_gain"]), as_float(pieces["middle_bias"])
    )
    narrow = tuple((jax.nn.softplus(portion) for portion in normed_b))
    reduced = tuple((portion[:, ::2, ::2, :] for portion in inputs))
    skipped = point_conv(reduced, pieces["skip_conv"])
    wide, saved_p = batch_norm(
        skipped, as_float(pieces["skip_gain"]), as_float(pieces["skip_bias"])
    )
    norm_rows = jnp.stack(
        [
            jnp.concatenate([saved_a[0], saved_b[0], saved_p[0]]),
            jnp.concatenate([saved_a[1], saved_b[1], saved_p[1]]),
        ]
    )
    kept = (normed_a, hidden, columns, normed_b, reduced, saved_a, saved_b, saved_p)
    return (wide, narrow, norm_rows, kept)


def front_backward(pieces, inputs, grad_wide, grad_narrow):
    wide, narrow, norm_rows, kept = front_forward(pieces, inputs)
    normed_a, hidden, columns, normed_b, reduced, saved_a, saved_b, saved_p = kept
    grads = {}
    grad_pre_b = through_softplus(grad_narrow, normed_b)
    grad_mid, grads["middle_gain"], grads["middle_bias"] = norm_back(
        grad_pre_b, as_float(pieces["middle_gain"]), saved_b
    )
    grad_hidden, grads["middle_conv"] = area_back(
        grad_mid, columns, pieces["middle_conv"], 2, [portion.shape for portion in hidden]
    )
    grad_pre_a = through_softplus(grad_hidden, normed_a)
    grad_first, grads["first_gain"], grads["first_bias"] = norm_back(
        grad_pre_a, as_float(pieces["first_gain"]), saved_a
    )
    grad_inputs, grads["first_conv"] = point_back(grad_first, inputs, pieces["first_conv"])
    grad_skip, grads["skip_gain"], grads["skip_bias"] = norm_back(
        grad_wide, as_float(pieces["skip_gain"]), saved_p
    )
    grad_reduced, grads["skip_conv"] = point_back(grad_skip, reduced, pieces["skip_conv"])
    grad_inputs = tuple(
        (
            full_part.at[:, ::2, ::2, :].add(part_reduced)
            for full_part, part_reduced in zip(grad_inputs, grad_reduced)
        )
    )
    return (grad_inputs, grads)


def join_forward(pieces, wide, narrow):
    last = point_conv(narrow, pieces["last_conv"])
    normed, saved = batch_norm(last, as_float(pieces["last_gain"]), as_float(pieces["last_bias"]))
    pre_values = tuple(
        (
            skip_part.astype(jnp.float32) + branch_part
            for skip_part, branch_part in zip(wide, normed)
        )
    )
    ending = tuple((jax.nn.softplus(pre_part) for pre_part in pre_values))
    filler = jnp.zeros((2 * MID,), jnp.float32)
    norm_rows = jnp.stack(
        [jnp.concatenate([saved[0], filler]), jnp.concatenate([saved[1], filler])]
    )
    return (ending, norm_rows, (pre_values, saved))


def join_grads(pieces, narrow, kept, grad_out, gate):
    pre_values, saved = kept
    grad_pre = tuple(
        (
            grad_part * jax.nn.sigmoid(pre_part) * gate
            for grad_part, pre_part in zip(grad_out, pre_values)
        )
    )
    grad_wide = tuple(
        (pre_grad + grad_part * (1.0 - gate) for pre_grad, grad_part in zip(grad_pre, grad_out))
    )
    grad_last, gain_grad, bias_grad = norm_back(grad_pre, as_float(pieces["last_gain"]), saved)
    grad_narrow, weight_grad = point_back(grad_last, narrow, pieces["last_conv"])
    grads = {"last_conv": weight_grad, "last_gain": gain_grad, "last_bias": bias_grad}
    return (grad_wide, grad_narrow, grads)


def split_forward(pieces, wide):
    first = point_conv(wide, pieces["first_conv"])
    normed_a, saved_a = batch_norm(
        first, as_float(pieces["first_gain"]), as_float(pieces["first_bias"])
    )
    hidden = tuple((jax.nn.softplus(portion).astype(jnp.bfloat16) for portion in normed_a))
    middle, columns = area_conv(hidden, pieces["middle_conv"], 1)
    normed_b, saved_b = batch_norm(
        middle, as_float(pieces["middle_gain"]), as_float(pieces["middle_bias"])
    )
    narrow = tuple((jax.nn.softplus(portion) for portion in normed_b))
    filler = jnp.zeros((C_OUT,), jnp.float32)
    norm_rows = jnp.stack(
        [
            jnp.concatenate([saved_a[0], saved_b[0], filler]),
            jnp.concatenate([saved_a[1], saved_b[1], filler]),
        ]
    )
    return (narrow, norm_rows, (normed_a, hidden, columns, normed_b, saved_a, saved_b))


def split_backward(pieces, wide, grad_relay, grad_narrow):
    narrow, norm_rows, kept = split_forward(pieces, wide)
    normed_a, hidden, columns, normed_b, saved_a, saved_b = kept
    grads = {}
    grad_pre_b = through_softplus(grad_narrow, normed_b)
    grad_mid, grads["middle_gain"], grads["middle_bias"] = norm_back(
        grad_pre_b, as_float(pieces["middle_gain"]), saved_b
    )
    grad_hidden, grads["middle_conv"] = area_back(
        grad_mid, columns, pieces["middle_conv"], 1, [portion.shape for portion in hidden]
    )
    grad_pre_a = through_softplus(grad_hidden, normed_a)
    grad_first, grads["first_gain"], grads["first_bias"] = norm_back(
        grad_pre_a, as_float(pieces["first_gain"]), saved_a
    )
    grad_conv_in, grads["first_conv"] = point_back(grad_first, wide, pieces["first_conv"])
    grad_wide = tuple(
        (relay_part + conv_part for relay_part, conv_part in zip(grad_relay, grad_conv_in))
    )
    return (grad_wide, grads)


def pool_grad(final, targets, picks):
    result = []
    for portion, pick_ids in zip(final, picks):
        cubes = jnp.mean(portion * portion * portion, axis=(1, 2)) + POOL_EPS
        factor = jnp.exp(jnp.log(cubes) * (-2.0 / 3.0)) * targets[pick_ids]
        result.append(factor[:, None, None, :] * portion * portion)
    return tuple(result)


def used_size(section):
    return sum((math.prod(entry_shape) for entry_name, entry_shape in section_shapes(section)))


def batch_pass(reals, inputs, gate, targets, picks):
    pieces = [unpack(reals[section], section) for section in range(4)]
    wide_f, narrow_f, rows_0, _ = front_forward(pieces[0], inputs)
    wide_0, narrow_0 = to_low(wide_f), to_low(narrow_f)
    ending_1, rows_1, kept_1 = join_forward(pieces[1], wide_0, narrow_0)
    wide_1 = to_low(ending_1)
    narrow_f, rows_2, _ = split_forward(pieces[2], wide_1)
    narrow_2 = to_low(narrow_f)
    ending_3, rows_3, kept_3 = join_forward(pieces[3], wide_1, narrow_2)
    final = tuple(
        (
            jnp.where(gate > 0, end_part, relay_part.astype(jnp.float32))
            for end_part, relay_part in zip(ending_3, wide_1)
        )
    )
    cotangent = pool_grad(final, targets, picks)
    grad_wide, grad_narrow, grads_3 = join_grads(pieces[3], narrow_2, kept_3, cotangent, gate)
    grad_wide, grads_2 = split_backward(
        pieces[2], wide_1, to_high(to_low(grad_wide)), to_high(to_low(grad_narrow))
    )
    grad_wide, grad_narrow, grads_1 = join_grads(
        pieces[1], narrow_0, kept_1, to_high(to_low(grad_wide)), 1.0
    )
    grad_inputs, grads_0 = front_backward(
        pieces[0], inputs, to_high(to_low(grad_wide)), to_high(to_low(grad_narrow))
    )
    outs = (wide_0, wide_1, wide_1, to_low(final))
    stats = jnp.stack([rows_0, rows_1, rows_2 * gate, rows_3 * gate])
    return (outs, stats, to_low(grad_inputs), (grads_0, grads_1, grads_2, grads_3))


def on_device(
    teach_in,
    stud_in,
    params,
    owners,
    depth_gates,
    teach_ids,
    stud_ids,
    targets,
    moment,
    second,
    gram_stats,
    eigen_basis,
):
    sections = lax.axis_size("pipe")
    rank = lax.axis_index("pipe")
    owner_count = lax.axis_size("dp")
    span_size = params.shape[1]
    flat_size = span_size * owner_count
    owner_rows = lax.all_gather(owners, "pipe", axis=0, tiled=True)
    gathered = lax.all_gather(params[0].astype(jnp.bfloat16), ("pipe", "dp"), axis=0)
    gathered = gathered.reshape(sections, owner_count, span_size)
    reals = []
    for section in range(sections):
        inverse = jnp.argsort(owner_rows[section]).astype(jnp.int32)
        blocks = -(-used_size(section) // span_size)
        reals.append(gathered[section][inverse[:blocks]].reshape(blocks * span_size))
    inputs = (teach_in[0], stud_in[0])
    gate = depth_gates[rank].astype(jnp.float32)
    outs, stats, (teach_grad, stud_grad), grads = batch_pass(
        reals, inputs, gate, targets, (teach_ids[rank], stud_ids[rank])
    )
    segment_teach = lax.all_to_all(
        jnp.stack([part[0] for part in outs]), "pipe", split_axis=0, concat_axis=0, tiled=True
    )
    segment_stud = lax.all_to_all(
        jnp.stack([part[1] for part in outs]), "pipe", split_axis=0, concat_axis=0, tiled=True
    )
    stats = lax.all_to_all(stats, "pipe", split_axis=0, concat_axis=0, tiled=True)
    rows = []
    for section in range(sections):
        flat = pack(grads[section], section, flat_size).reshape(owner_count, span_size)
        rows.append(flat[owner_rows[section]])
    span_total = lax.psum_scatter(
        jnp.stack(rows).reshape(sections * owner_count, span_size),
        ("pipe", "dp"),
        scatter_dimension=0,
        tiled=True,
    ).reshape(span_size)
    total_squares = lax.psum(jnp.sum(span_total * span_total), ("dp", "pipe"))
    grad_norm = jnp.sqrt(total_squares)
    factor = jnp.minimum(1.0, CLIP_NORM / grad_norm)
    clipped = span_total * factor
    matrix = clipped.reshape(span_size // 128, 128)
    gram_old = gram_stats[0]
    basis_old = eigen_basis[0]
    gram_new = DECAY_STATS * gram_old + (1.0 - DECAY_STATS) * jnp.dot(
        matrix.T, matrix, precision=HIGH
    )
    product = jnp.dot(gram_new, basis_old, precision=HIGH)
    rotation = product / jnp.sqrt(jnp.sum(product * product))
    for repeat in range(NS_STEPS):
        square = jnp.dot(rotation.T, rotation, precision=HIGH)
        rotation = 1.5 * rotation - 0.5 * jnp.dot(rotation, square, precision=HIGH)
    moment_old = moment.reshape(span_size // 128, 128)
    initial = jnp.dot(moment_old, basis_old.T, precision=HIGH)
    blended = DECAY_FIRST * initial + (1.0 - DECAY_FIRST) * matrix
    moment_new = jnp.dot(blended, rotation, precision=HIGH)
    rotated = jnp.dot(matrix, rotation, precision=HIGH)
    second_new = (
        DECAY_SECOND * second.reshape(span_size // 128, 128)
        + (1.0 - DECAY_SECOND) * rotated * rotated
    )
    correction = math.sqrt(1.0 - DECAY_SECOND**STEP) / (1.0 - DECAY_FIRST**STEP)
    direction = (
        jnp.dot(moment_new / (jnp.sqrt(second_new) + ADAM_EPS), rotation.T, precision=HIGH)
        * correction
    )
    weights = params.reshape(span_size // 128, 128)
    params_new = weights - LEARN_RATE * (direction + WEIGHT_DECAY * weights)
    return (
        segment_teach[None],
        segment_stud[None],
        teach_grad[None],
        stud_grad[None],
        stats[None, :, None],
        grad_norm,
        clipped.reshape(1, span_size),
        moment_new.reshape(1, span_size),
        second_new.reshape(1, span_size),
        params_new.reshape(1, span_size),
        gram_new[None],
        rotation[None],
    )


def solution(mesh):
    placed = (
        P("pipe", "dp", None, None, None),
        P("pipe", "dp", None, None, None),
        P("pipe", "dp"),
        P("pipe", None),
        P(),
        P(None, "dp"),
        P(None, "dp"),
        P(),
        P("pipe", "dp"),
        P("pipe", "dp"),
        P("pipe", "dp", None),
        P("pipe", "dp", None),
    )
    return jax.shard_map(
        on_device,
        mesh=mesh,
        in_specs=placed,
        out_specs=(
            P("pipe", None, "dp", None, None, None),
            P("pipe", None, "dp", None, None, None),
            P("pipe", "dp", None, None, None),
            P("pipe", "dp", None, None, None),
            P("pipe", None, "dp", None, None),
            P(),
            P("pipe", "dp"),
            P("pipe", "dp"),
            P("pipe", "dp"),
            P("pipe", "dp"),
            P("pipe", "dp", None),
            P("pipe", "dp", None),
        ),
        check_vma=False,
    )
```

```python
import math

import jax
import jax.numpy as jnp
import numpy as np
from jax import lax
from jax.experimental import pallas as pl
from jax.experimental.pallas import tpu as pltpu
from jax.sharding import PartitionSpec as P

C_IN = 1024
MID = 512
C_OUT = 2048
STEP = 10
NS_STEPS = 5


HIGH = lax.Precision.HIGHEST
NORM_EPS = 1e-05
POOL_EPS = 1e-06
CLIP_NORM = 1.0
LEARN_RATE = 0.02
DECAY_FIRST = 0.9
DECAY_SECOND = 0.95
DECAY_STATS = 0.95
ADAM_EPS = 1e-08
WEIGHT_DECAY = 0.01


def section_shapes(section):
    if section == 0:
        return [
            ("first_conv", (C_IN, MID)),
            ("middle_conv", (9 * MID, MID)),
            ("skip_conv", (C_IN, C_OUT)),
            ("first_gain", (MID,)),
            ("first_bias", (MID,)),
            ("middle_gain", (MID,)),
            ("middle_bias", (MID,)),
            ("skip_gain", (C_OUT,)),
            ("skip_bias", (C_OUT,)),
        ]
    if section == 2:
        return [
            ("first_conv", (C_OUT, MID)),
            ("middle_conv", (9 * MID, MID)),
            ("first_gain", (MID,)),
            ("first_bias", (MID,)),
            ("middle_gain", (MID,)),
            ("middle_bias", (MID,)),
        ]
    return [("last_conv", (MID, C_OUT)), ("last_gain", (C_OUT,)), ("last_bias", (C_OUT,))]


def unpack(flat_vector, section):
    pieces = {}
    offset = 0
    for entry_name, entry_shape in section_shapes(section):
        entry_size = math.prod(entry_shape)
        pieces[entry_name] = flat_vector[offset : offset + entry_size].reshape(entry_shape)
        offset = offset + entry_size
    return pieces


def pack(grads, section, flat_size):
    parts = [grads[entry_name].reshape(-1) for entry_name, entry_shape in section_shapes(section)]
    used = sum((math.prod(entry_shape) for entry_name, entry_shape in section_shapes(section)))
    parts.append(jnp.zeros((flat_size - used,), jnp.float32))
    return jnp.concatenate(parts)


def as_float(vector):
    return vector.astype(jnp.float32)


def to_low(groups):
    return tuple((portion.astype(jnp.bfloat16) for portion in groups))


def to_high(groups):
    return tuple((portion.astype(jnp.float32) for portion in groups))


def point_conv(groups, weight):
    return tuple(
        (
            jnp.einsum("khwc,cd->khwd", portion, weight, preferred_element_type=jnp.float32)
            for portion in groups
        )
    )


def point_back(grad_out, groups, weight):
    low_grads = to_low(grad_out)
    grad_input = tuple(
        (
            jnp.einsum("khwd,cd->khwc", grad_part, weight, preferred_element_type=jnp.float32)
            for grad_part in low_grads
        )
    )
    grad_weight = sum(
        (
            jnp.einsum("khwc,khwd->cd", in_part, grad_part, preferred_element_type=jnp.float32)
            for in_part, grad_part in zip(groups, low_grads)
        )
    )
    return (grad_input, grad_weight)


def patches(portion, stride):
    height = portion.shape[1]
    across = portion.shape[2]
    padded = jnp.pad(portion, ((0, 0), (1, 1), (1, 1), (0, 0)))
    shifted = [
        padded[:, row_off : row_off + height : stride, col_off : col_off + across : stride, :]
        for row_off in range(3)
        for col_off in range(3)
    ]
    return jnp.concatenate(shifted, axis=-1)


def area_conv(groups, weight, stride):
    columns = tuple((patches(portion, stride) for portion in groups))
    return (point_conv(columns, weight), columns)


def unpatch(grad_cols, height, across, stride):
    channels = grad_cols.shape[-1] // 9
    padded = jnp.zeros((grad_cols.shape[0], height + 2, across + 2, channels), jnp.float32)
    for row_off in range(3):
        for col_off in range(3):
            offset = (3 * row_off + col_off) * channels
            padded = padded.at[
                :, row_off : row_off + height : stride, col_off : col_off + across : stride, :
            ].add(grad_cols[..., offset : offset + channels])
    return padded[:, 1 : height + 1, 1 : across + 1, :]


def area_back(grad_out, columns, weight, stride, in_shapes):
    grad_cols, grad_weight = point_back(grad_out, columns, weight)
    grad_input = tuple(
        (
            unpatch(grad_part, shape_item[1], shape_item[2], stride)
            for grad_part, shape_item in zip(grad_cols, in_shapes)
        )
    )
    return (grad_input, grad_weight)


def batch_norm(groups, gain, bias):
    rows_total = sum((portion.shape[0] * portion.shape[1] * portion.shape[2] for portion in groups))
    centre = sum((jnp.sum(portion, axis=(0, 1, 2)) for portion in groups)) / rows_total
    spread = (
        sum((jnp.sum(jnp.square(portion - centre), axis=(0, 1, 2)) for portion in groups))
        / rows_total
    )
    inverse = lax.rsqrt(spread + NORM_EPS)
    standard = tuple(((portion - centre) * inverse for portion in groups))
    normed = tuple((gain * std_part + bias for std_part in standard))
    return (normed, (centre, spread, inverse, standard))


def norm_back(grad_out, gain, saved):
    centre, spread, inverse, standard = saved
    rows_total = sum(
        (portion.shape[0] * portion.shape[1] * portion.shape[2] for portion in standard)
    )
    grad_sum = sum((jnp.sum(grad_part, axis=(0, 1, 2)) for grad_part in grad_out))
    grad_dot = sum(
        (
            jnp.sum(grad_part * std_part, axis=(0, 1, 2))
            for grad_part, std_part in zip(grad_out, standard)
        )
    )
    grad_input = tuple(
        (
            gain
            * inverse
            * (grad_part - grad_sum / rows_total - std_part * (grad_dot / rows_total))
            for grad_part, std_part in zip(grad_out, standard)
        )
    )
    return (grad_input, grad_dot, grad_sum)


def through_softplus(grad_out, pre_values):
    return tuple(
        (grad_part * jax.nn.sigmoid(pre_part) for grad_part, pre_part in zip(grad_out, pre_values))
    )


def front_forward(pieces, inputs):
    first = point_conv(inputs, pieces["first_conv"])
    normed_a, saved_a = batch_norm(
        first, as_float(pieces["first_gain"]), as_float(pieces["first_bias"])
    )
    hidden = tuple((jax.nn.softplus(portion).astype(jnp.bfloat16) for portion in normed_a))
    middle, columns = area_conv(hidden, pieces["middle_conv"], 2)
    normed_b, saved_b = batch_norm(
        middle, as_float(pieces["middle_gain"]), as_float(pieces["middle_bias"])
    )
    narrow = tuple((jax.nn.softplus(portion) for portion in normed_b))
    reduced = tuple((portion[:, ::2, ::2, :] for portion in inputs))
    skipped = point_conv(reduced, pieces["skip_conv"])
    wide, saved_p = batch_norm(
        skipped, as_float(pieces["skip_gain"]), as_float(pieces["skip_bias"])
    )
    norm_rows = jnp.stack(
        [
            jnp.concatenate([saved_a[0], saved_b[0], saved_p[0]]),
            jnp.concatenate([saved_a[1], saved_b[1], saved_p[1]]),
        ]
    )
    kept = (normed_a, hidden, columns, normed_b, reduced, saved_a, saved_b, saved_p)
    return (wide, narrow, norm_rows, kept)


def front_backward(pieces, inputs, grad_wide, grad_narrow):
    wide, narrow, norm_rows, kept = front_forward(pieces, inputs)
    normed_a, hidden, columns, normed_b, reduced, saved_a, saved_b, saved_p = kept
    grads = {}
    grad_pre_b = through_softplus(grad_narrow, normed_b)
    grad_mid, grads["middle_gain"], grads["middle_bias"] = norm_back(
        grad_pre_b, as_float(pieces["middle_gain"]), saved_b
    )
    grad_hidden, grads["middle_conv"] = area_back(
        grad_mid, columns, pieces["middle_conv"], 2, [portion.shape for portion in hidden]
    )
    grad_pre_a = through_softplus(grad_hidden, normed_a)
    grad_first, grads["first_gain"], grads["first_bias"] = norm_back(
        grad_pre_a, as_float(pieces["first_gain"]), saved_a
    )
    grad_inputs, grads["first_conv"] = point_back(grad_first, inputs, pieces["first_conv"])
    grad_skip, grads["skip_gain"], grads["skip_bias"] = norm_back(
        grad_wide, as_float(pieces["skip_gain"]), saved_p
    )
    grad_reduced, grads["skip_conv"] = point_back(grad_skip, reduced, pieces["skip_conv"])
    grad_inputs = tuple(
        (
            full_part.at[:, ::2, ::2, :].add(part_reduced)
            for full_part, part_reduced in zip(grad_inputs, grad_reduced)
        )
    )
    return (grad_inputs, grads)


def join_forward(pieces, wide, narrow):
    last = point_conv(narrow, pieces["last_conv"])
    normed, saved = batch_norm(last, as_float(pieces["last_gain"]), as_float(pieces["last_bias"]))
    pre_values = tuple(
        (
            skip_part.astype(jnp.float32) + branch_part
            for skip_part, branch_part in zip(wide, normed)
        )
    )
    ending = tuple((jax.nn.softplus(pre_part) for pre_part in pre_values))
    filler = jnp.zeros((2 * MID,), jnp.float32)
    norm_rows = jnp.stack(
        [jnp.concatenate([saved[0], filler]), jnp.concatenate([saved[1], filler])]
    )
    return (ending, norm_rows, (pre_values, saved))


def join_grads(pieces, narrow, kept, grad_out, gate):
    pre_values, saved = kept
    grad_pre = tuple(
        (
            grad_part * jax.nn.sigmoid(pre_part) * gate
            for grad_part, pre_part in zip(grad_out, pre_values)
        )
    )
    grad_wide = tuple(
        (pre_grad + grad_part * (1.0 - gate) for pre_grad, grad_part in zip(grad_pre, grad_out))
    )
    grad_last, gain_grad, bias_grad = norm_back(grad_pre, as_float(pieces["last_gain"]), saved)
    grad_narrow, weight_grad = point_back(grad_last, narrow, pieces["last_conv"])
    grads = {"last_conv": weight_grad, "last_gain": gain_grad, "last_bias": bias_grad}
    return (grad_wide, grad_narrow, grads)


def split_forward(pieces, wide):
    first = point_conv(wide, pieces["first_conv"])
    normed_a, saved_a = batch_norm(
        first, as_float(pieces["first_gain"]), as_float(pieces["first_bias"])
    )
    hidden = tuple((jax.nn.softplus(portion).astype(jnp.bfloat16) for portion in normed_a))
    middle, columns = area_conv(hidden, pieces["middle_conv"], 1)
    normed_b, saved_b = batch_norm(
        middle, as_float(pieces["middle_gain"]), as_float(pieces["middle_bias"])
    )
    narrow = tuple((jax.nn.softplus(portion) for portion in normed_b))
    filler = jnp.zeros((C_OUT,), jnp.float32)
    norm_rows = jnp.stack(
        [
            jnp.concatenate([saved_a[0], saved_b[0], filler]),
            jnp.concatenate([saved_a[1], saved_b[1], filler]),
        ]
    )
    return (narrow, norm_rows, (normed_a, hidden, columns, normed_b, saved_a, saved_b))


def split_backward(pieces, wide, grad_relay, grad_narrow):
    narrow, norm_rows, kept = split_forward(pieces, wide)
    normed_a, hidden, columns, normed_b, saved_a, saved_b = kept
    grads = {}
    grad_pre_b = through_softplus(grad_narrow, normed_b)
    grad_mid, grads["middle_gain"], grads["middle_bias"] = norm_back(
        grad_pre_b, as_float(pieces["middle_gain"]), saved_b
    )
    grad_hidden, grads["middle_conv"] = area_back(
        grad_mid, columns, pieces["middle_conv"], 1, [portion.shape for portion in hidden]
    )
    grad_pre_a = through_softplus(grad_hidden, normed_a)
    grad_first, grads["first_gain"], grads["first_bias"] = norm_back(
        grad_pre_a, as_float(pieces["first_gain"]), saved_a
    )
    grad_conv_in, grads["first_conv"] = point_back(grad_first, wide, pieces["first_conv"])
    grad_wide = tuple(
        (relay_part + conv_part for relay_part, conv_part in zip(grad_relay, grad_conv_in))
    )
    return (grad_wide, grads)


def pool_grad(final, targets, picks):
    result = []
    for portion, pick_ids in zip(final, picks):
        cubes = jnp.mean(portion * portion * portion, axis=(1, 2)) + POOL_EPS
        factor = jnp.exp(jnp.log(cubes) * (-2.0 / 3.0)) * targets[pick_ids]
        result.append(factor[:, None, None, :] * portion * portion)
    return tuple(result)


def used_size(section):
    return sum((math.prod(entry_shape) for entry_name, entry_shape in section_shapes(section)))


def batch_pass(reals, inputs, gate, targets, picks):
    pieces = [unpack(reals[section], section) for section in range(4)]
    wide_f, narrow_f, rows_0, _ = front_forward(pieces[0], inputs)
    wide_0, narrow_0 = to_low(wide_f), to_low(narrow_f)
    ending_1, rows_1, kept_1 = join_forward(pieces[1], wide_0, narrow_0)
    wide_1 = to_low(ending_1)
    narrow_f, rows_2, _ = split_forward(pieces[2], wide_1)
    narrow_2 = to_low(narrow_f)
    ending_3, rows_3, kept_3 = join_forward(pieces[3], wide_1, narrow_2)
    final = tuple(
        (
            jnp.where(gate > 0, end_part, relay_part.astype(jnp.float32))
            for end_part, relay_part in zip(ending_3, wide_1)
        )
    )
    cotangent = pool_grad(final, targets, picks)
    grad_wide, grad_narrow, grads_3 = join_grads(pieces[3], narrow_2, kept_3, cotangent, gate)
    grad_wide, grads_2 = split_backward(
        pieces[2], wide_1, to_high(to_low(grad_wide)), to_high(to_low(grad_narrow))
    )
    grad_wide, grad_narrow, grads_1 = join_grads(
        pieces[1], narrow_0, kept_1, to_high(to_low(grad_wide)), 1.0
    )
    grad_inputs, grads_0 = front_backward(
        pieces[0], inputs, to_high(to_low(grad_wide)), to_high(to_low(grad_narrow))
    )
    outs = (wide_0, wide_1, wide_1, to_low(final))
    stats = jnp.stack([rows_0, rows_1, rows_2 * gate, rows_3 * gate])
    return (outs, stats, to_low(grad_inputs), (grads_0, grads_1, grads_2, grads_3))


def on_device(
    teach_in,
    stud_in,
    params,
    owners,
    depth_gates,
    teach_ids,
    stud_ids,
    targets,
    moment,
    second,
    gram_stats,
    eigen_basis,
):
    sections = lax.axis_size("pipe")
    rank = lax.axis_index("pipe")
    owner_count = lax.axis_size("dp")
    span_size = params.shape[1]
    flat_size = span_size * owner_count
    owner_rows = lax.all_gather(owners, "pipe", axis=0, tiled=True)
    gathered = lax.all_gather(params[0].astype(jnp.bfloat16), ("pipe", "dp"), axis=0)
    gathered = gathered.reshape(sections, owner_count, span_size)
    reals = []
    for section in range(sections):
        inverse = jnp.argsort(owner_rows[section]).astype(jnp.int32)
        blocks = -(-used_size(section) // span_size)
        reals.append(gathered[section][inverse[:blocks]].reshape(blocks * span_size))
    inputs = (teach_in[0], stud_in[0])
    gate = depth_gates[rank].astype(jnp.float32)
    outs, stats, (teach_grad, stud_grad), grads = batch_pass(
        reals, inputs, gate, targets, (teach_ids[rank], stud_ids[rank])
    )
    segment_teach = lax.all_to_all(
        jnp.stack([part[0] for part in outs]), "pipe", split_axis=0, concat_axis=0, tiled=True
    )
    segment_stud = lax.all_to_all(
        jnp.stack([part[1] for part in outs]), "pipe", split_axis=0, concat_axis=0, tiled=True
    )
    stats = lax.all_to_all(stats, "pipe", split_axis=0, concat_axis=0, tiled=True)
    rows = []
    for section in range(sections):
        flat = pack(grads[section], section, flat_size).reshape(owner_count, span_size)
        rows.append(flat[owner_rows[section]])
    span_total = lax.psum_scatter(
        jnp.stack(rows).reshape(sections * owner_count, span_size),
        ("pipe", "dp"),
        scatter_dimension=0,
        tiled=True,
    ).reshape(span_size)
    total_squares = lax.psum(jnp.sum(span_total * span_total), ("dp", "pipe"))
    grad_norm = jnp.sqrt(total_squares)
    factor = jnp.minimum(1.0, CLIP_NORM / grad_norm)
    clipped = span_total * factor
    matrix = clipped.reshape(span_size // 128, 128)
    gram_old = gram_stats[0]
    basis_old = eigen_basis[0]
    gram_new = DECAY_STATS * gram_old + (1.0 - DECAY_STATS) * jnp.dot(
        matrix.T, matrix, precision=HIGH
    )
    product = jnp.dot(gram_new, basis_old, precision=HIGH)
    rotation = product / jnp.sqrt(jnp.sum(product * product))
    for repeat in range(NS_STEPS):
        square = jnp.dot(rotation.T, rotation, precision=HIGH)
        rotation = 1.5 * rotation - 0.5 * jnp.dot(rotation, square, precision=HIGH)
    moment_old = moment.reshape(span_size // 128, 128)
    initial = jnp.dot(moment_old, basis_old.T, precision=HIGH)
    blended = DECAY_FIRST * initial + (1.0 - DECAY_FIRST) * matrix
    moment_new = jnp.dot(blended, rotation, precision=HIGH)
    rotated = jnp.dot(matrix, rotation, precision=HIGH)
    second_new = (
        DECAY_SECOND * second.reshape(span_size // 128, 128)
        + (1.0 - DECAY_SECOND) * rotated * rotated
    )
    correction = math.sqrt(1.0 - DECAY_SECOND**STEP) / (1.0 - DECAY_FIRST**STEP)
    direction = (
        jnp.dot(moment_new / (jnp.sqrt(second_new) + ADAM_EPS), rotation.T, precision=HIGH)
        * correction
    )
    weights = params.reshape(span_size // 128, 128)
    params_new = weights - LEARN_RATE * (direction + WEIGHT_DECAY * weights)
    return (
        segment_teach[None],
        segment_stud[None],
        teach_grad[None],
        stud_grad[None],
        stats[None, :, None],
        grad_norm,
        clipped.reshape(1, span_size),
        moment_new.reshape(1, span_size),
        second_new.reshape(1, span_size),
        params_new.reshape(1, span_size),
        gram_new[None],
        rotation[None],
    )


MESH = pl.DeviceIdType.MESH
LOW = jnp.bfloat16
FULL = jnp.float32
TILE = 256
WINDOW = 20
STRIDE = 19
VEC_TILE = (152, 32, 104, 32)
USED_TILES = (153, 33, 105, 33)
FRONT_WIDE = 88
SMALL_ROWS = 1056
ROWS = 120
PADDED = 128
TEACH_ROWS = 72


def any_spec():
    return pl.BlockSpec(memory_space=pl.ANY)


def smem_spec():
    return pl.BlockSpec(memory_space=pltpu.SMEM)


def vmem_spec():
    return pl.BlockSpec(memory_space=pltpu.VMEM)


def tile_forms(section, tile):
    even = lax.rem(section, 2) == 0
    vector = jnp.where(section == 0, 152, jnp.where(section == 2, 104, 32))
    narrow_end = jnp.where(section == 0, FRONT_WIDE, jnp.where(section == 2, 104, 0))
    narrow = even & (tile < narrow_end)
    plain = tile == vector
    return narrow, plain


def prepare_kernel(place, params, big, small, flat, sem):
    block, section = place[0], place[1]

    @pl.loop(0, WINDOW)
    def _(r):
        flat[pl.ds(TILE * r, TILE)] = jnp.zeros((TILE, 128), FULL)

    copy = pltpu.make_async_copy(params.at[:, 0, :], flat.at[pl.ds(6 * block, params.shape[0])], sem)
    copy.start()

    @pl.loop(0, small.shape[0])
    def _(r):
        small[r] = jnp.zeros((TILE, 128), LOW)

    copy.wait()

    @pl.loop(0, WINDOW)
    def _(r):
        tile = STRIDE * block + r
        narrow, plain = tile_forms(section, tile)
        base = TILE * r

        @pl.when(narrow)
        def _():
            for j in range(4):
                big[r, 64 * j : 64 * j + 64, :] = flat[pl.ds(base + j, 64, 4), :].astype(LOW)

        @pl.when(plain)
        def _():
            big[r] = flat[pl.ds(base, TILE), :].astype(LOW)

        @pl.when(jnp.logical_not(narrow | plain))
        def _():
            for j in range(16):
                big[r, 16 * j : 16 * j + 16, :] = flat[pl.ds(base + j, 16, 16), :].astype(LOW)

        @pl.when(tile < small.shape[0])
        def _():
            small[tile] = big[r]


def prepare(place, params):
    return pl.pallas_call(
        prepare_kernel,
        name="prepare",
        out_shape=(
            jax.ShapeDtypeStruct((WINDOW, TILE, 128), LOW),
            jax.ShapeDtypeStruct((USED_TILES[1], TILE, 128), LOW),
        ),
        in_specs=[smem_spec(), any_spec()],
        out_specs=(vmem_spec(), vmem_spec()),
        scratch_shapes=[pltpu.VMEM((WINDOW * TILE, 128), FULL), pltpu.SemaphoreType.DMA],
        compiler_params=pltpu.CompilerParams(vmem_limit_bytes=32 << 20),
    )(place, params.reshape(-1, 1, 128))


class Place:
    def __init__(self):
        self.dp = lax.axis_index("dp")
        self.pipe = lax.axis_index("pipe")
        self.x, self.core = self.pipe // 2, self.pipe % 2
        self.z, self.y = self.dp // 2, self.dp % 2

    def device(self, x=None, core=None, z=None, y=None):
        x = self.x if x is None else x
        core = self.core if core is None else core
        z = self.z if z is None else z
        y = self.y if y is None else y
        return {"dp": 2 * z + y, "pipe": 2 * x + core}

    def enter(self):
        barrier = pltpu.get_barrier_semaphore()
        for step in range(1, 8):
            other = lax.rem(self.dp + step, 8)
            pl.semaphore_signal(
                barrier, inc=1, device_id={"dp": other, "pipe": self.pipe}, device_id_type=MESH
            )
        for target in (self.device(x=1 - self.x), self.device(core=1 - self.core)):
            pl.semaphore_signal(barrier, inc=1, device_id=target, device_id_type=MESH)
        pl.semaphore_wait(barrier, 9)


def remote(src, dst, send, recv, target):
    return pltpu.make_async_remote_copy(
        src_ref=src, dst_ref=dst, send_sem=send, recv_sem=recv, device_id=target, device_id_type=MESH
    )


def gather_kernel(big, small, all_big, all_small, early, chunk, early_send, early_recv,
                  z_send, z_recv, x_send, x_recv, y_send, y_recv, dx_send, dx_recv, dy_send, dy_recv,
                  s_send, s_recv, own_sem):
    me = Place()
    me.enter()
    x, y, z, core = me.x, me.y, me.z, me.core
    up, down = me.device(z=z + 1), me.device(z=z - 1)
    x_side, y_side, sibling = me.device(x=1 - x), me.device(y=1 - y), me.device(core=1 - core)

    def plane(out, other, own):
        rows = out.shape[2]
        half = rows // 2
        copy = pltpu.make_async_copy(own, out.at[x, me.dp], own_sem)
        copy.start()
        copy.wait()

        def spread(origin):
            block = out.at[x, 2 * origin + y]
            remote(block, block, x_send.at[origin], x_recv.at[origin], x_side).start()
            remote(block, block, y_send.at[origin], y_recv.at[origin], y_side).start()
            share(x, 2 * origin + y)

        def share(xo, jo):
            block = out.at[xo, jo]
            remote(block, block, s_send.at[8 * xo + jo], s_recv.at[8 * xo + jo], sibling).start()

        def move_z(origin, target, slot):
            block = out.at[x, 2 * origin + y]
            return remote(block, block, z_send.at[slot, origin], z_recv.at[origin], target)

        def half_x(origin):
            part = out.at[x, 2 * origin + (1 - y), pl.ds(half, half)]
            return remote(part, part, dx_send.at[origin], dx_recv.at[origin], x_side)

        def half_y(origin):
            part = out.at[1 - x, 2 * origin + y, pl.ds(0, half)]
            return remote(part, part, dy_send.at[origin], dy_recv.at[origin], y_side)

        def wait_z(origin):
            block = out.at[x, 2 * origin + y]
            remote(block, block, z_send.at[0, origin], z_recv.at[origin], up).wait_recv()

        def wait_sides(origin):
            block = out.at[1 - x, 2 * origin + y]
            remote(block, block, x_send.at[origin], x_recv.at[origin], x_side).wait_recv()
            half_y(origin).start()
            share(1 - x, 2 * origin + y)
            block = out.at[x, 2 * origin + (1 - y)]
            remote(block, block, y_send.at[origin], y_recv.at[origin], y_side).wait_recv()
            half_x(origin).start()
            share(x, 2 * origin + (1 - y))

        def wait_diagonal(origin):
            part = out.at[1 - x, 2 * origin + (1 - y), pl.ds(half, half)]
            remote(part, part, dx_send.at[origin], dx_recv.at[origin], x_side).wait_recv()
            part = out.at[1 - x, 2 * origin + (1 - y), pl.ds(0, half)]
            remote(part, part, dy_send.at[origin], dy_recv.at[origin], y_side).wait_recv()
            share(1 - x, 2 * origin + (1 - y))

        def each(step, action):
            if step == 0:
                action(z)
            else:
                pl.when(z >= step)(lambda: action(z - step))
                pl.when(z + step <= 3)(lambda: action(z + step))

        for step in range(6):
            if step == 0:
                pl.when(z < 3)(lambda: move_z(z, up, 0).start())
                pl.when(z > 0)(lambda: move_z(z, down, 1).start())
                spread(z)
            elif step < 4:

                @pl.when(z >= step)
                def _():
                    wait_z(z - step)
                    pl.when(z < 3)(lambda: move_z(z - step, up, 0).start())
                    spread(z - step)

                @pl.when(z + step <= 3)
                def _():
                    wait_z(z + step)
                    pl.when(z > 0)(lambda: move_z(z + step, down, 1).start())
                    spread(z + step)

            if 1 <= step < 5:
                each(step - 1, wait_sides)
            if step >= 2:
                each(step - 2, wait_diagonal)

        for origin in range(4):
            block = out.at[x, 2 * origin + y]
            remote(block, block, x_send.at[origin], x_recv.at[origin], x_side).wait_send()
            remote(block, block, y_send.at[origin], y_recv.at[origin], y_side).wait_send()
            half_x(origin).wait_send()
            half_y(origin).wait_send()
            pl.when((z < 3) & (origin <= z))(lambda: move_z(origin, up, 0).wait_send())
            pl.when((z > 0) & (origin >= z))(lambda: move_z(origin, down, 1).wait_send())
        for xo in range(2):
            for jo in range(8):
                mine, theirs = out.at[xo, jo], other.at[xo, jo]
                at = 8 * xo + jo
                remote(mine, mine, s_send.at[at], s_recv.at[at], sibling).wait_send()
                remote(theirs, theirs, s_send.at[at], s_recv.at[at], sibling).wait_recv()

    @pl.when(core == 0)
    def _():
        plane(all_big, all_small, big)

    @pl.when(core == 1)
    def _():
        def early_copy(step):
            target = lax.rem(me.dp + step, 8)
            return remote(
                small.at[target], early.at[step], early_send.at[step], early_recv.at[step],
                {"dp": target, "pipe": me.pipe},
            )

        for step in range(1, 8):
            early_copy(step).start()
        copy = pltpu.make_async_copy(small.at[me.dp], early.at[0], own_sem)
        copy.start()
        copy.wait()
        for step in range(1, 8):
            early_copy(step).wait()

        @pl.loop(0, 6)
        def _(i):
            part = pl.ds(pl.multiple_of(176 * i, 16), 176)
            total = early[0, part, :].astype(FULL)
            for step in range(1, 8):
                total = total + early[step, part, :].astype(FULL)
            chunk[part, :] = total.astype(LOW)

        plane(all_small, all_big, chunk)


def gather_all(big, small):
    sem = pltpu.SemaphoreType.DMA
    return pl.pallas_call(
        gather_kernel,
        name="gather_all",
        out_shape=(
            jax.ShapeDtypeStruct((2, 8, WINDOW * TILE, 128), LOW),
            jax.ShapeDtypeStruct((2, 8, SMALL_ROWS, 128), LOW),
        ),
        in_specs=[any_spec(), any_spec()],
        out_specs=(any_spec(), any_spec()),
        scratch_shapes=[
            pltpu.VMEM((8, SMALL_ROWS, 128), LOW),
            pltpu.VMEM((SMALL_ROWS, 128), LOW),
            sem((8,)), sem((8,)),
            sem((2, 4)), sem((4,)),
            sem((4,)), sem((4,)), sem((4,)), sem((4,)),
            sem((4,)), sem((4,)), sem((4,)), sem((4,)),
            sem((16,)), sem((16,)),
            sem,
        ],
        compiler_params=pltpu.CompilerParams(
            collective_id=0, has_side_effects=True, vmem_limit_bytes=60 << 20
        ),
    )(big.reshape(WINDOW * TILE, 128), small.reshape(8, SMALL_ROWS, 128))


def soft(value):
    return jnp.maximum(value, 0.0) + jnp.log1p(jnp.exp(-jnp.abs(value)))


def gate_of(value):
    small = jnp.exp(-jnp.abs(value))
    share = 1.0 / (1.0 + small)
    return jnp.where(value >= 0, share, small * share)


def standardize(z):
    count = z.shape[0]
    centre = jnp.sum(z, axis=0, keepdims=True) / count
    away = z - centre
    spread = jnp.sum(away * away, axis=0, keepdims=True) / count
    inverse = lax.rsqrt(spread + NORM_EPS)
    return away * inverse, centre, spread, inverse


def unstandardize(grad, standard, gain, inverse):
    count = grad.shape[0]
    grad_sum = jnp.sum(grad, axis=0, keepdims=True)
    grad_dot = jnp.sum(grad * standard, axis=0, keepdims=True)
    result = gain * inverse * (grad - grad_sum / count - standard * (grad_dot / count))
    return result, grad_dot, grad_sum


def pad_low(value):
    zeros = jnp.zeros((PADDED - ROWS, value.shape[1]), FULL)
    return jnp.concatenate([value, zeros], axis=0).astype(LOW)


def mul(a, b):
    return jnp.dot(a, b, preferred_element_type=FULL)


def mul_t(a, b):
    return lax.dot_general(a, b, (((1,), (1,)), ((), ())), preferred_element_type=FULL)


def narrow_part(ref, start, count, blocks=range(4)):
    return jnp.concatenate(
        [ref[pl.ds(start, count), 64 * j : 64 * j + 64, :].reshape(64 * count, 128) for j in blocks],
        axis=1,
    )


def put_narrow(ref, start, count, value):
    for j in range(4):
        ref[pl.ds(start, count), 64 * j : 64 * j + 64, :] = (
            value[:, 128 * j : 128 * j + 128].astype(LOW).reshape(count, 64, 128)
        )


def wide_part(ref, start, count, c):
    return jnp.concatenate(
        [
            ref[start : start + count, pl.ds(pl.multiple_of(32 * c + 16 * h, 16), 16), :].reshape(
                16 * count, 128
            )
            for h in range(2)
        ],
        axis=1,
    )


def put_wide(ref, start, count, c, value):
    for h in range(2):
        ref[start : start + count, pl.ds(pl.multiple_of(32 * c + 16 * h, 16), 16), :] = (
            value[:, 128 * h : 128 * h + 128].astype(LOW).reshape(count, 16, 128)
        )


def step_kernel(inv, gate_ref, all_big, all_small, x, wanted, grid,
                wide0, wide1, final, stats, grad_x, out_big, out_small,
                w0, w1, w2, w3, edges, vec, grad_vec, raw,
                std_a, std_b, std_p, std_1, std_c, std_d, hidden, cols0, cols2,
                nar0, nar2, turned, relay, dz_a, dz_n, acc, acc_x, grad_h, in_sem, edge_sem, out_sem):
    gate = gate_ref[0]
    weights = (w0, w1, w2, w3)
    loads = {0: [], 1: [], 2: [], 3: []}
    for b in range(8):
        count = 20 if b == 7 else 19
        loads[0].append(pltpu.make_async_copy(
            all_big.at[0, inv[b], pl.ds(0, count)], w0.at[pl.ds(19 * b, count)], in_sem.at[b]))
        if b < 7:
            loads[0].append(pltpu.make_async_copy(
                all_big.at[0, inv[b], pl.ds(19, 1)], edges.at[pl.ds(b, 1)], edge_sem.at[b]))
    for b in range(6):
        count = 10 if b == 5 else 19
        loads[2].append(pltpu.make_async_copy(
            all_big.at[1, inv[8 + b], pl.ds(0, count)], w2.at[pl.ds(19 * b, count)], in_sem.at[8 + b]))
        if b < 5:
            loads[2].append(pltpu.make_async_copy(
                all_big.at[1, inv[8 + b], pl.ds(19, 1)], edges.at[pl.ds(7 + b, 1)], edge_sem.at[7 + b]))
    loads[1].append(pltpu.make_async_copy(all_small.at[0], w1, in_sem.at[14]))
    loads[3].append(pltpu.make_async_copy(all_small.at[1], w3, in_sem.at[15]))
    for section in range(4):
        for load in loads[section]:
            load.start()

    raw[...] = jnp.zeros_like(raw)
    grad_vec[...] = jnp.zeros_like(grad_vec)

    def settle(section):
        for load in loads[section]:
            load.wait()
        if section == 0:
            for b in range(7):
                w0[19 * b + 19] = (w0[19 * b + 19].astype(FULL) + edges[b].astype(FULL)).astype(LOW)
        if section == 2:
            for b in range(5):
                w2[19 * b + 19] = (
                    w2[19 * b + 19].astype(FULL) + edges[7 + b].astype(FULL)
                ).astype(LOW)
        vec[section] = weights[section][VEC_TILE[section], 0:48, :].astype(FULL)

    def row(section, start):
        return jnp.concatenate(
            [vec[section, pl.ds(start + h, 1), :] for h in range(2)], axis=1
        )

    def put_row(section, start, value):
        for h in range(2):
            grad_vec[section, pl.ds(start + h, 1), :] = value[:, 128 * h : 128 * h + 128]

    def put_stats(section, column, centre, spread):
        raw[2 * section : 2 * section + 1, pl.ds(column, 256)] = centre
        raw[2 * section + 1 : 2 * section + 2, pl.ds(column, 256)] = spread

    def inverse_of(section, column):
        return lax.rsqrt(raw[2 * section + 1 : 2 * section + 2, pl.ds(column, 256)] + NORM_EPS)

    def lanes(c):
        return pl.ds(pl.multiple_of(256 * c, 256), 256)

    at_row, at_col, side = grid[0], grid[1], grid[2]

    def masked(value, dr, dc):
        ok = (at_row + dr >= 0) & (at_row + dr < side) & (at_col + dc >= 0) & (at_col + dc < side)
        return jnp.concatenate(
            [jnp.where(ok, value[:, 128 * j : 128 * j + 128], 0.0) for j in range(4)], axis=1
        )

    def rolled(value, sign, dr, dc):
        parts = []
        for start, end, width in ((0, TEACH_ROWS, 6), (TEACH_ROWS, ROWS, 4)):
            by = (sign * (dr * width + dc)) % (end - start)
            part = value[start:end]
            parts.append(part if by == 0 else pltpu.roll(part, by, 0))
        return jnp.concatenate(parts, axis=0)

    def taps(stride):
        for t in range(9):
            r, q = t // 3, t % 3
            if stride == 1:
                yield t, 0, r - 1, q - 1
            else:
                phase = 2 * (1 if r != 1 else 0) + (1 if q != 1 else 0)
                yield t, phase, -1 if r == 0 else 0, -1 if q == 0 else 0

    settle(0)
    whole_x = x[...].reshape(4 * PADDED, C_IN)
    for c in range(2):
        z = mul(whole_x, narrow_part(w0, 0, 16, (2 * c, 2 * c + 1)))
        z = jnp.concatenate([z[PADDED * p : PADDED * p + ROWS] for p in range(4)], axis=0)
        standard, centre, spread, _ = standardize(z)
        put_stats(0, 256 * c, centre, spread)
        std_a[:, 256 * c : 256 * c + 256] = standard
        hidden[:, 256 * c : 256 * c + 256] = (
            soft(row(0, 2 * c) * standard + row(0, 4 + 2 * c)).astype(LOW).astype(FULL)
        )

    for t, phase, dr, dc in taps(2):
        cols0[t] = pad_low(masked(rolled(hidden[ROWS * phase : ROWS * phase + ROWS, :], -1, dr, dc), dr, dc))
    acc[...] = jnp.zeros_like(acc)

    @pl.loop(0, 9)
    def _(t):
        acc[...] += mul(cols0[t], narrow_part(w0, 16 + 8 * t, 8))

    def middle(section, std, nar):
        for c in range(2):
            at = slice(256 * c, 256 * c + 256)
            standard, centre, spread, _ = standardize(acc[0:ROWS, at])
            put_stats(section, MID + 256 * c, centre, spread)
            std[:, at] = standard
            nar[:, at] = pad_low(soft(row(section, 8 + 2 * c) * standard + row(section, 12 + 2 * c)))

    middle(0, std_b, nar0)
    acc[...] = jnp.zeros_like(acc)
    settle(1)
    settle(2)

    @pl.loop(0, 8)
    def _(c):
        at = lanes(c)
        standard, centre, spread, _ = standardize(mul(x[0], wide_part(w0, FRONT_WIDE, 64, c))[0:ROWS])
        put_stats(0, 2 * MID + pl.multiple_of(256 * c, 256), centre, spread)
        std_p[:, at] = standard
        low = pad_low(row(0, 16 + 2 * c) * standard + row(0, 32 + 2 * c))
        wide0[:, at] = low
        standard, centre, spread, _ = standardize(mul(nar0[...], wide_part(w1, 0, 32, c))[0:ROWS])
        put_stats(1, pl.multiple_of(256 * c, 256), centre, spread)
        std_1[:, at] = standard
        pre = low.astype(FULL)[0:ROWS] + row(1, 2 * c) * standard + row(1, 16 + 2 * c)
        low = pad_low(soft(pre))
        wide1[:, at] = low
        acc[...] += mul(low, narrow_part(w2, 4 * c, 4))

    for c in range(2):
        at = slice(256 * c, 256 * c + 256)
        standard, centre, spread, _ = standardize(acc[0:ROWS, at])
        put_stats(2, 256 * c, centre, spread)
        std_c[:, at] = standard
        hidden[0:ROWS, at] = soft(row(2, 2 * c) * standard + row(2, 4 + 2 * c)).astype(LOW).astype(FULL)
    for t, phase, dr, dc in taps(1):
        cols2[t] = pad_low(masked(rolled(hidden[0:ROWS, :], -1, dr, dc), dr, dc))
    acc[...] = jnp.zeros_like(acc)

    @pl.loop(0, 9)
    def _(t):
        acc[...] += mul(cols2[t], narrow_part(w2, 32 + 8 * t, 8))

    middle(2, std_d, nar2)

    turned[...] = nar2[...].T
    acc[...] = jnp.zeros_like(acc)
    settle(3)

    def spread_rows(values):
        head = lax.broadcasted_iota(jnp.int32, (8, 256), 0) < 4
        first, second = (jnp.broadcast_to(value, (8, 256)) for value in values[0:2])
        parts = [jnp.broadcast_to(values[0], (32, 256)), jnp.where(head, first, second)]
        parts.append(jnp.broadcast_to(values[1], (32, 256)))
        parts.extend(jnp.broadcast_to(value, (16, 256)) for value in values[2:5])
        return jnp.concatenate(parts, axis=0)

    def crop_sums(value):
        head = lax.broadcasted_iota(jnp.int32, (8, 256), 0) < 4
        between = value[32:40]

        def total(part):
            return jnp.sum(part, axis=0, keepdims=True)

        return [
            total(value[0:32]) + total(jnp.where(head, between, 0.0)),
            total(value[40:72]) + total(jnp.where(head, 0.0, between)),
            total(value[72:88]),
            total(value[88:104]),
            total(value[104:120]),
        ]

    @pl.loop(0, 8)
    def _(c):
        at = lanes(c)
        weight = wide_part(w3, 0, 32, c)
        standard, centre, spread, inverse = standardize(mul(nar2[...], weight)[0:ROWS])
        put_stats(3, pl.multiple_of(256 * c, 256), centre, spread)
        gain = row(3, 2 * c)
        before = wide1[:, at].astype(FULL)[0:ROWS]
        pre = before + gain * standard + row(3, 16 + 2 * c)
        ending = jnp.where(gate > 0, soft(pre), before)
        final[:, at] = pad_low(ending)
        square = ending * ending
        factors = []
        for crop, total in enumerate(crop_sums(square * ending)):
            mean = total / (36.0 if crop < 2 else 16.0) + POOL_EPS
            factors.append(jnp.exp(jnp.log(mean) * (-2.0 / 3.0)) * wanted[crop : crop + 1, at])
        cotangent = spread_rows(factors) * square
        grad_pre = cotangent * gate_of(pre) * gate
        relay[:, at] = pad_low(grad_pre + cotangent * (1.0 - gate))
        result, grad_gain, grad_bias = unstandardize(grad_pre, standard, gain, inverse)
        put_row(3, 2 * c, grad_gain)
        put_row(3, 16 + 2 * c, grad_bias)
        low = pad_low(result)
        acc[...] += mul_t(low, weight)
        put_wide(w3, 0, 32, c, mul(turned[...], low))

    def flush(section):
        weights[section][VEC_TILE[section]] = grad_vec[section].astype(LOW)

    flush(3)
    stores = [pltpu.make_async_copy(w3, out_small.at[1], out_sem.at[15])]
    stores[-1].start()

    def middle_back(section, std):
        for c in range(2):
            at = slice(256 * c, 256 * c + 256)
            gain, bias = row(section, 8 + 2 * c), row(section, 12 + 2 * c)
            grad = acc[0:ROWS, at].astype(LOW).astype(FULL) * gate_of(gain * std[:, at] + bias)
            result, grad_gain, grad_bias = unstandardize(
                grad, std[:, at], gain, inverse_of(section, MID + 256 * c)
            )
            put_row(section, 8 + 2 * c, grad_gain)
            put_row(section, 12 + 2 * c, grad_bias)
            dz_n[:, at] = pad_low(result)

    def taps_back(weight, start, cols, stride, phases):
        grad_h[0 : ROWS * phases, :] = jnp.zeros((ROWS * phases, MID), FULL)
        for t, phase, dr, dc in taps(stride):
            part = mul_t(dz_n[...], narrow_part(weight, start + 8 * t, 8))[0:ROWS]
            at = slice(ROWS * phase, ROWS * phase + ROWS)
            grad_h[at, :] += rolled(masked(part, dr, dc), 1, dr, dc)
            put_narrow(weight, start + 8 * t, 8, mul(cols[t].T, dz_n[...]))

    middle_back(2, std_d)
    taps_back(w2, 32, cols2, 1, 1)
    for c in range(2):
        at = slice(256 * c, 256 * c + 256)
        gain, bias = row(2, 2 * c), row(2, 4 + 2 * c)
        grad = grad_h[0:ROWS, at] * gate_of(gain * std_c[:, at] + bias)
        result, grad_gain, grad_bias = unstandardize(grad, std_c[:, at], gain, inverse_of(2, 256 * c))
        put_row(2, 2 * c, grad_gain)
        put_row(2, 4 + 2 * c, grad_bias)
        dz_n[:, at] = pad_low(result)
    turned[...] = nar0[...].T
    acc[...] = jnp.zeros_like(acc)
    acc_x[...] = jnp.zeros_like(acc_x)

    @pl.loop(0, 8)
    def _(c):
        at = lanes(c)
        low = dz_n[...]
        grad = relay[:, at].astype(FULL) + mul_t(low, narrow_part(w2, 4 * c, 4))
        put_narrow(w2, 4 * c, 4, mul(wide1[:, at].T, low))
        grad = grad.astype(LOW).astype(FULL)[0:ROWS]
        gain = row(1, 2 * c)
        pre = wide0[:, at].astype(FULL)[0:ROWS] + gain * std_1[:, at] + row(1, 16 + 2 * c)
        grad = grad * gate_of(pre)
        result, grad_gain, grad_bias = unstandardize(
            grad, std_1[:, at], gain, inverse_of(1, pl.multiple_of(256 * c, 256))
        )
        put_row(1, 2 * c, grad_gain)
        put_row(1, 16 + 2 * c, grad_bias)
        low = pad_low(result)
        acc[...] += mul_t(low, wide_part(w1, 0, 32, c))
        put_wide(w1, 0, 32, c, mul(turned[...], low))
        grad = grad.astype(LOW).astype(FULL)
        result, grad_gain, grad_bias = unstandardize(
            grad, std_p[:, at], row(0, 16 + 2 * c), inverse_of(0, 2 * MID + pl.multiple_of(256 * c, 256))
        )
        put_row(0, 16 + 2 * c, grad_gain)
        put_row(0, 32 + 2 * c, grad_bias)
        low = pad_low(result)
        acc_x[...] += mul_t(low, wide_part(w0, FRONT_WIDE, 64, c))
        put_wide(w0, FRONT_WIDE, 64, c, mul(x[0].T, low))

    flush(1)
    flush(2)
    w2[105:115] = jnp.zeros((10, TILE, 128), LOW)
    stores.append(pltpu.make_async_copy(w1, out_small.at[0], out_sem.at[14]))
    stores[-1].start()
    for b in range(8):
        if b < 6:
            stores.append(pltpu.make_async_copy(
                w2.at[pl.ds(19 * b, 20)], out_big.at[1, inv[8 + b]], out_sem.at[8 + b]))
            stores[-1].start()
        else:
            for h in range(2):
                stores.append(pltpu.make_async_copy(
                    w2.at[pl.ds(105, 10)], out_big.at[1, inv[8 + b], pl.ds(10 * h, 10)],
                    out_sem.at[16 + 2 * (b - 6) + h]))
                stores[-1].start()

    middle_back(0, std_b)
    taps_back(w0, 16, cols0, 2, 4)
    for c in range(2):
        at = slice(256 * c, 256 * c + 256)
        gain, bias = row(0, 2 * c), row(0, 4 + 2 * c)
        grad = grad_h[:, at] * gate_of(gain * std_a[:, at] + bias)
        result, grad_gain, grad_bias = unstandardize(grad, std_a[:, at], gain, inverse_of(0, 256 * c))
        put_row(0, 2 * c, grad_gain)
        put_row(0, 4 + 2 * c, grad_bias)
        for p in range(4):
            dz_a[PADDED * p : PADDED * p + PADDED, at] = pad_low(result[ROWS * p : ROWS * p + ROWS])

    @pl.loop(0, 4)
    def _(c):
        at = lanes(c)
        low = dz_a[...]
        part = mul_t(low, narrow_part(w0, 4 * c, 4))
        grad_x[0, :, at] = (part[0:PADDED] + acc_x[:, at]).astype(LOW)
        for p in range(1, 4):
            grad_x[p, :, at] = part[PADDED * p : PADDED * p + PADDED].astype(LOW)
        turned_x = x[:, :, at].reshape(4 * PADDED, 256).T
        put_narrow(w0, 4 * c, 4, mul(turned_x, low))

    flush(0)
    for b in range(8):
        stores.append(pltpu.make_async_copy(
            w0.at[pl.ds(19 * b, 20)], out_big.at[0, inv[b]], out_sem.at[b]))
        stores[-1].start()
    stats[0:4] = raw[0:4]
    stats[4:8] = raw[4:8] * gate
    for store in stores:
        store.wait()


def run_step(inv, gate, all_big, all_small, phases, wanted):
    spots = np.zeros((3, ROWS, 128), np.int32)
    for r in range(ROWS):
        width = 6 if r < TEACH_ROWS else 4
        at = r % 36 if r < TEACH_ROWS else (r - TEACH_ROWS) % 16
        spots[0, r], spots[1, r], spots[2, r] = at // width, at % width, width
    sem = pltpu.SemaphoreType.DMA
    wide = jax.ShapeDtypeStruct((PADDED, C_OUT), LOW)
    vm = pltpu.VMEM
    return pl.pallas_call(
        step_kernel,
        name="step",
        out_shape=(
            wide, wide, wide,
            jax.ShapeDtypeStruct((8, 2 * MID + C_OUT), FULL),
            jax.ShapeDtypeStruct((4, PADDED, C_IN), LOW),
            jax.ShapeDtypeStruct((2, 8, WINDOW, TILE, 128), LOW),
            jax.ShapeDtypeStruct((2, USED_TILES[1], TILE, 128), LOW),
        ),
        in_specs=[smem_spec(), smem_spec(), any_spec(), any_spec(), vmem_spec(), vmem_spec(), vmem_spec()],
        out_specs=(vmem_spec(),) * 5 + (any_spec(),) * 2,
        scratch_shapes=[
            vm((153, TILE, 128), LOW), vm((33, TILE, 128), LOW), vm((115, TILE, 128), LOW), vm((33, TILE, 128), LOW),
            vm((12, TILE, 128), LOW), vm((4, 48, 128), FULL), vm((4, TILE, 128), FULL),
            vm((8, 2 * MID + C_OUT), FULL),
            vm((4 * ROWS, MID), FULL), vm((ROWS, MID), FULL), vm((ROWS, C_OUT), FULL), vm((ROWS, C_OUT), FULL),
            vm((ROWS, MID), FULL), vm((ROWS, MID), FULL), vm((4 * ROWS, MID), FULL),
            vm((9, PADDED, MID), LOW), vm((9, PADDED, MID), LOW),
            vm((PADDED, MID), LOW), vm((PADDED, MID), LOW), vm((MID, PADDED), LOW),
            vm((PADDED, C_OUT), LOW), vm((4 * PADDED, MID), LOW), vm((PADDED, MID), LOW),
            vm((PADDED, MID), FULL), vm((PADDED, C_IN), FULL), vm((4 * ROWS, MID), FULL),
            sem((16,)), sem((12,)), sem((20,)),
        ],
        compiler_params=pltpu.CompilerParams(vmem_limit_bytes=60 << 20),
    )(inv, gate, all_big, all_small, phases, wanted, jnp.asarray(spots))


def reduce_kernel(big, small, out_big, out_small, got, halves_x, halves_y, from_x, from_y, from_low, from_high,
                  stage, total, late, s_send, s_recv, hx_send, hx_recv, hy_send, hy_recv, x_send, x_recv,
                  y_send, y_recv, zu_send, zu_recv, zd_send, zd_recv, stage_sem, out_sem, late_send, late_recv):
    me = Place()
    me.enter()
    x, y, z, core = me.x, me.y, me.z, me.core
    up, down = me.device(z=z + 1), me.device(z=z - 1)
    x_side, y_side, sibling = me.device(x=1 - x), me.device(y=1 - y), me.device(core=1 - core)
    order = [
        jnp.where(z < 2, 3, 0),
        jnp.where(z == 0, 2, jnp.where(z == 1, 0, jnp.where(z == 2, 3, 1))),
        jnp.where(z == 0, 1, jnp.where(z == 1, 2, jnp.where(z == 2, 1, 2))),
        z,
    ]
    columns = ((1 - x, 1 - y), (x, 1 - y), (1 - x, y), (x, y))

    def plane(own, theirs, piece, finish):
        rows, their_rows = own.shape[2], theirs.shape[2]
        half = rows // 2

        def slot(at, count=rows):
            return got.at[at, pl.ds(0, count)]

        def share(group, k):
            xo, yo = columns[group]
            at = 4 * group + k
            return remote(
                theirs.at[xo, 2 * order[k] + yo], slot(at, their_rows), s_send.at[at], s_recv.at[at], sibling
            )

        def arrive(group, k):
            at = 4 * group + k
            remote(own.at[0, 0], slot(at), s_send.at[at], s_recv.at[at], sibling).wait_recv()

        def fetch(at):
            xo, yo = columns[at // 4]
            return pltpu.make_async_copy(
                own.at[xo, 2 * order[at % 4] + yo], stage.at[at % 4, pl.ds(0, rows)], stage_sem.at[at % 4]
            )

        def add(at, start, count, extras):
            @pl.loop(0, count // piece)
            def _(i):
                part = pl.ds(pl.multiple_of(start + piece * i, 16), piece)
                here = pl.ds(pl.multiple_of(piece * i, 16), piece)
                sums = got[at, part, :].astype(FULL) + stage[at % 4, part, :].astype(FULL)
                for ref, k in extras:
                    sums = sums + ref[k, here, :].astype(FULL)
                got[at, part, :] = sums.astype(LOW)

        def merge(at, ref, k):
            @pl.loop(0, rows // piece)
            def _(i):
                part = pl.ds(pl.multiple_of(piece * i, 16), piece)
                sums = got[at, part, :].astype(FULL) + ref[k, part, :].astype(FULL)
                got[at, part, :] = sums.astype(LOW)

        def send_half_x(k):
            return remote(got.at[k, pl.ds(half, half)], halves_x.at[k, pl.ds(0, half)],
                          hx_send.at[k], hx_recv.at[k], x_side)

        def send_half_y(k):
            return remote(got.at[k, pl.ds(0, half)], halves_y.at[k, pl.ds(0, half)],
                          hy_send.at[k], hy_recv.at[k], y_side)

        def send_y(k):
            return remote(slot(4 + k), from_y.at[k, pl.ds(0, rows)], y_send.at[k], y_recv.at[k], y_side)

        def send_x(k):
            return remote(slot(8 + k), from_x.at[k, pl.ds(0, rows)], x_send.at[k], x_recv.at[k], x_side)

        def send_up(at, zd):
            return remote(slot(at), from_low.at[zd - 1, pl.ds(0, rows)], zu_send.at[zd - 1], zu_recv.at[zd - 1], up)

        def send_down(at, zd):
            return remote(slot(at), from_high.at[zd, pl.ds(0, rows)], zd_send.at[zd], zd_recv.at[zd], down)

        for group in range(4):
            for k in range(4):
                share(group, k).start()
        for at in range(2):
            fetch(at).start()
        for at in range(16):
            group, k = at // 4, at % 4
            if at + 2 < 16:
                fetch(at + 2).start()
            fetch(at).wait()
            arrive(group, k)
            if group == 0:
                add(at, 0, rows, [])
                send_half_x(k).start()
                send_half_y(k).start()
            elif group == 1:
                send_half_x(k).wait_recv()
                add(at, 0, half, [])
                add(at, half, half, [(halves_x, k)])
                send_y(k).start()
            elif group == 2:
                send_half_y(k).wait_recv()
                add(at, 0, half, [(halves_y, k)])
                add(at, half, half, [])
                send_x(k).start()
            else:
                send_x(k).wait_recv()
                send_y(k).wait_recv()
                add(at, 0, rows, [(from_x, k), (from_y, k)])
                if k < 3:
                    zd = order[k]

                    @pl.when(zd > z)
                    def _(at=at, zd=zd):
                        @pl.when(z > 0)
                        def _():
                            send_up(at, zd).wait_recv()
                            merge(at, from_low, zd - 1)

                        send_up(at, zd).start()

                    @pl.when(zd < z)
                    def _(at=at, zd=zd):
                        @pl.when(z < 3)
                        def _():
                            send_down(at, zd).wait_recv()
                            merge(at, from_high, zd)

                        send_down(at, zd).start()

        def end(low, high):
            @pl.loop(0, rows // piece)
            def _(i):
                part = pl.ds(pl.multiple_of(piece * i, 16), piece)
                sums = got[15, part, :].astype(FULL)
                if low:
                    sums = sums + from_low[z - 1, part, :].astype(FULL)
                if high:
                    sums = sums + from_high[z, part, :].astype(FULL)
                total[part, :] = sums

        @pl.when(z == 0)
        def _():
            send_down(15, z).wait_recv()
            end(False, True)

        @pl.when((z > 0) & (z < 3))
        def _():
            send_up(15, z).wait_recv()
            send_down(15, z).wait_recv()
            end(True, True)

        @pl.when(z == 3)
        def _():
            send_up(15, z).wait_recv()
            end(True, False)

        finish()
        for k in range(4):
            send_half_x(k).wait_send()
            send_half_y(k).wait_send()
            send_x(k).wait_send()
            send_y(k).wait_send()
            for group in range(4):
                share(group, k).wait_send()
        for k in range(3):
            zd, at = order[k], 12 + k

            @pl.when(zd > z)
            def _(at=at, zd=zd):
                send_up(at, zd).wait_send()

            @pl.when(zd < z)
            def _(at=at, zd=zd):
                send_down(at, zd).wait_send()

    @pl.when(core == 0)
    def _():
        def finish():
            copy = pltpu.make_async_copy(total, out_big, out_sem)
            copy.start()
            copy.wait()

        plane(big, small, 512, finish)

    @pl.when(core == 1)
    def _():
        def finish():
            late[...] = total[0:SMALL_ROWS, :].astype(LOW)
            copy = pltpu.make_async_copy(late, out_small.at[me.dp], out_sem)
            copy.start()
            for step in range(1, 8):
                remote(
                    late, out_small.at[me.dp], late_send.at[step], late_recv.at[step],
                    {"dp": lax.rem(me.dp + step, 8), "pipe": me.pipe},
                ).start()
            copy.wait()
            for step in range(1, 8):
                move = remote(
                    late, out_small.at[lax.rem(me.dp + 8 - step, 8)], late_send.at[step], late_recv.at[step],
                    {"dp": lax.rem(me.dp + step, 8), "pipe": me.pipe},
                )
                move.wait_recv()
                move.wait_send()

        plane(small, big, 176, finish)


def reduce_all(big, small):
    sem = pltpu.SemaphoreType.DMA
    rows = WINDOW * TILE
    vm = pltpu.VMEM
    return pl.pallas_call(
        reduce_kernel,
        name="reduce_all",
        out_shape=(
            jax.ShapeDtypeStruct((rows, 128), FULL),
            jax.ShapeDtypeStruct((8, SMALL_ROWS, 128), LOW),
        ),
        in_specs=[any_spec(), any_spec()],
        out_specs=(any_spec(), any_spec()),
        scratch_shapes=[
            vm((16, rows, 128), LOW), vm((4, rows // 2, 128), LOW), vm((4, rows // 2, 128), LOW),
            vm((4, rows, 128), LOW), vm((4, rows, 128), LOW),
            vm((3, rows, 128), LOW), vm((3, rows, 128), LOW),
            vm((4, rows, 128), LOW), vm((rows, 128), FULL), vm((SMALL_ROWS, 128), LOW),
            sem((16,)), sem((16,)),
            sem((4,)), sem((4,)), sem((4,)), sem((4,)), sem((4,)), sem((4,)), sem((4,)), sem((4,)),
            sem((3,)), sem((3,)), sem((3,)), sem((3,)),
            sem((4,)), sem, sem((8,)), sem((8,)),
        ],
        compiler_params=pltpu.CompilerParams(
            collective_id=1, has_side_effects=True, vmem_limit_bytes=62 << 20
        ),
    )(big.reshape(2, 8, rows, 128), small.reshape(2, 8, SMALL_ROWS, 128))


def high_dot(a, b, dims=((1,), (0,))):
    return lax.dot_general(a, b, (dims, ((), ())), precision=HIGH, preferred_element_type=FULL)


def collect_kernel(place, big, small, flat, gram, squares, tiles, low, sem):
    block, section = place[0], place[1]
    even = lax.rem(section, 2) == 0

    @pl.when(even)
    def _():
        copy = pltpu.make_async_copy(big, tiles, sem)
        copy.start()
        copy.wait()

    @pl.when(jnp.logical_not(even))
    def _():
        low[...] = jnp.zeros_like(low)

        @pl.when(block == 0)
        def _():
            copy = pltpu.make_async_copy(small.at[0:20], low, sem)
            copy.start()
            copy.wait()

        @pl.when(block == 1)
        def _():
            copy = pltpu.make_async_copy(small.at[19:33], low.at[0:14], sem)
            copy.start()
            copy.wait()

        @pl.loop(0, WINDOW)
        def _(r):
            tiles[r] = low[r].astype(FULL)

    @pl.loop(0, WINDOW)
    def _(r):
        narrow, plain = tile_forms(section, STRIDE * block + r)
        base = TILE * r

        @pl.when(narrow)
        def _():
            for j in range(4):
                flat[pl.ds(base + j, 64, 4), :] = tiles[r, 64 * j : 64 * j + 64, :]

        @pl.when(plain)
        def _():
            flat[pl.ds(base, TILE), :] = tiles[r]

        @pl.when(jnp.logical_not(narrow | plain))
        def _():
            for j in range(16):
                flat[pl.ds(base + j, 16, 16), :] = tiles[r, 16 * j : 16 * j + 16, :]

    span = 4870
    at = lax.broadcasted_iota(jnp.int32, (TILE, 128), 0)
    first = pl.ds(0, TILE)
    flat[first, :] = jnp.where(at >= 6 * block, flat[first, :], 0.0)
    edge = TILE * (WINDOW - 1)
    last = pl.ds(edge, TILE)
    flat[last, :] = jnp.where(at + edge < span + 6 * block, flat[last, :], 0.0)
    gram[...] = jnp.zeros_like(gram)
    squares[...] = jnp.zeros_like(squares)

    @pl.loop(0, WINDOW)
    def _(r):
        part = flat[pl.ds(pl.multiple_of(TILE * r, TILE), TILE), :]
        gram[...] += high_dot(part, part, ((0,), (0,)))
        squares[...] += jnp.sum((part * part).reshape(TILE // 8, 8, 128), axis=0)


def collect(place, big, small):
    rows = WINDOW * TILE
    return pl.pallas_call(
        collect_kernel,
        name="collect",
        out_shape=(
            jax.ShapeDtypeStruct((rows, 128), FULL),
            jax.ShapeDtypeStruct((128, 128), FULL),
            jax.ShapeDtypeStruct((8, 128), FULL),
        ),
        in_specs=[smem_spec(), any_spec(), any_spec()],
        out_specs=(vmem_spec(),) * 3,
        scratch_shapes=[
            pltpu.VMEM((WINDOW, TILE, 128), FULL), pltpu.VMEM((WINDOW, TILE, 128), LOW),
            pltpu.SemaphoreType.DMA,
        ],
        compiler_params=pltpu.CompilerParams(vmem_limit_bytes=32 << 20),
    )(place, big.reshape(WINDOW, TILE, 128), small.reshape(USED_TILES[1], TILE, 128))


PIECES = 7


def finish_kernel(place, factor_ref, flat, gram_raw, gram_old, basis_old, params, moment, second,
                  clipped, moment_new, second_new, params_new, gram_new, basis_new,
                  grad, held, rotated, weights, in_sem, out_sem):
    factor = factor_ref[0]
    span = params.shape[0]
    piece = grad.shape[0] // PIECES

    def loads(i):
        count = min(piece, span - piece * i)
        part = pl.ds(piece * i, count)
        yield pltpu.make_async_copy(
            flat.at[pl.ds(6 * place[0] + piece * i, count)], grad.at[part], in_sem.at[0, i])
        for n, (src, dst) in enumerate(((params, weights), (moment, held), (second, rotated))):
            yield pltpu.make_async_copy(src.at[part, 0, :], dst.at[part], in_sem.at[n + 1, i])

    def stores(i):
        part = pl.ds(piece * i, min(piece, span - piece * i))
        pairs = ((grad, clipped), (held, moment_new), (rotated, second_new), (weights, params_new))
        for n, (src, dst) in enumerate(pairs):
            yield pltpu.make_async_copy(src.at[part], dst.at[part, 0, :], out_sem.at[n, i])

    for i in range(PIECES):
        for load in loads(i):
            load.start()
    old = basis_old[...]
    gram = DECAY_STATS * gram_old[...] + (1.0 - DECAY_STATS) * (gram_raw[...] * (factor * factor))
    gram_new[...] = gram
    product = high_dot(gram, old)
    rotation = product / jnp.sqrt(jnp.sum(product * product))
    for repeat in range(NS_STEPS):
        square = high_dot(rotation, rotation, ((0,), (0,)))
        rotation = 1.5 * rotation - 0.5 * high_dot(rotation, square)
    basis_new[...] = rotation
    change = high_dot(old, rotation, ((0,), (0,)))
    correction = math.sqrt(1.0 - DECAY_SECOND**STEP) / (1.0 - DECAY_FIRST**STEP)
    for i in range(PIECES):
        for load in loads(i):
            load.wait()
        part = slice(piece * i, piece * i + piece)
        clip = grad[part, :] * factor
        grad[part, :] = clip
        turned = high_dot(clip, rotation)
        first = DECAY_FIRST * high_dot(held[part, :], change) + (1.0 - DECAY_FIRST) * turned
        power = DECAY_SECOND * rotated[part, :] + (1.0 - DECAY_SECOND) * turned * turned
        held[part, :] = first
        rotated[part, :] = power
        direction = high_dot(first / (jnp.sqrt(power) + ADAM_EPS), rotation, ((1,), (1,))) * correction
        before = weights[part, :]
        weights[part, :] = before - LEARN_RATE * (direction + WEIGHT_DECAY * before)
        for store in stores(i):
            store.start()
    for i in range(PIECES):
        for store in stores(i):
            store.wait()


def finish(place, factor, flat, gram_raw, gram_old, basis_old, params, moment, second):
    span = params.shape[1] // 128
    rows = -(-span // (8 * PIECES)) * 8 * PIECES
    flat_shape = jax.ShapeDtypeStruct((span, 1, 128), FULL)
    square = jax.ShapeDtypeStruct((128, 128), FULL)
    sem = pltpu.SemaphoreType.DMA
    outs = pl.pallas_call(
        finish_kernel,
        name="finish",
        out_shape=(flat_shape,) * 4 + (square,) * 2,
        in_specs=[smem_spec(), smem_spec(), any_spec()] + [vmem_spec()] * 3 + [any_spec()] * 3,
        out_specs=(any_spec(),) * 4 + (vmem_spec(),) * 2,
        scratch_shapes=[pltpu.VMEM((rows, 128), FULL)] * 4 + [sem((4, PIECES)), sem((4, PIECES))],
        compiler_params=pltpu.CompilerParams(vmem_limit_bytes=48 << 20),
    )(place, factor, flat, gram_raw, gram_old, basis_old,
      params.reshape(span, 1, 128), moment.reshape(span, 1, 128), second.reshape(span, 1, 128))
    return tuple(out.reshape(1, span * 128) for out in outs[:4]) + outs[4:]


def to_phases(teach, stud):
    def split(part):
        crops, high, across, channels = part.shape
        part = part.reshape(crops, high // 2, 2, across // 2, 2, channels).transpose(2, 4, 0, 1, 3, 5)
        return part.reshape(4, -1, channels)

    zeros = jnp.zeros((4, PADDED - ROWS, teach.shape[-1]), teach.dtype)
    return jnp.concatenate([split(teach), split(stud), zeros], axis=1)


def from_phases(phases, shape):
    crops, high, across, channels = shape
    part = phases.reshape(2, 2, crops, high // 2, across // 2, channels)
    return part.transpose(2, 3, 0, 4, 1, 5).reshape(shape)


def on_small_slice(
    teach_in,
    stud_in,
    params,
    owners,
    depth_gates,
    teach_ids,
    stud_ids,
    targets,
    moment,
    second,
    gram_stats,
    eigen_basis,
):
    rank = lax.axis_index("pipe")
    place = jnp.stack([owners[0, lax.axis_index("dp")], rank])
    owner_rows = lax.all_gather(owners, "pipe", axis=0, tiled=True)
    inverse = jnp.argsort(owner_rows[0::2], axis=1).astype(jnp.int32).reshape(-1)
    phases = to_phases(teach_in[0], stud_in[0])
    picks = jnp.concatenate([teach_ids[rank], stud_ids[rank]])
    wanted = jnp.pad(targets[picks], ((0, 8 - picks.shape[0]), (0, 0)))
    gate = depth_gates[rank].astype(jnp.float32).reshape(1)
    big, small = prepare(place, params)
    all_big, all_small = gather_all(big, small)
    wide_0, wide_1, final, stats, grad_x, out_big, out_small = run_step(
        inverse,
        gate,
        all_big.reshape(2, 8, WINDOW, TILE, 128),
        all_small.reshape(2, USED_TILES[1], TILE, 128),
        phases,
        wanted,
    )
    sum_big, sum_small = reduce_all(out_big, out_small)
    flat, gram_raw, squares = collect(place, sum_big, sum_small)
    outs = jnp.stack([wide_0, wide_1, wide_1, final])
    segments = lax.all_to_all(outs, "pipe", split_axis=0, concat_axis=0, tiled=True)
    teach_shape, stud_shape = teach_in.shape[1:], stud_in.shape[1:]
    small_teach = (teach_shape[0], teach_shape[1] // 2, teach_shape[2] // 2, C_OUT)
    small_stud = (stud_shape[0], stud_shape[1] // 2, stud_shape[2] // 2, C_OUT)
    segment_teach = segments[:, :TEACH_ROWS].reshape((4,) + small_teach)
    segment_stud = segments[:, TEACH_ROWS:ROWS].reshape((4,) + small_stud)
    stats = lax.all_to_all(
        stats.reshape(4, 2, -1), "pipe", split_axis=0, concat_axis=0, tiled=True
    )
    teach_grad = from_phases(grad_x[:, :TEACH_ROWS], teach_shape)
    stud_grad = from_phases(grad_x[:, TEACH_ROWS:ROWS], stud_shape)
    grad_norm = jnp.sqrt(lax.psum(jnp.sum(squares), ("dp", "pipe")))
    factor = jnp.minimum(1.0, CLIP_NORM / grad_norm)
    clipped, moment_new, second_new, params_new, gram_new, rotation = finish(
        place, factor.reshape(1), flat, gram_raw, gram_stats[0], eigen_basis[0], params, moment, second
    )
    return (
        segment_teach[None],
        segment_stud[None],
        teach_grad[None],
        stud_grad[None],
        stats[None, :, None],
        grad_norm,
        clipped,
        moment_new,
        second_new,
        params_new,
        gram_new[None],
        rotation[None],
    )


def solution(mesh):
    placed = (
        P("pipe", "dp", None, None, None),
        P("pipe", "dp", None, None, None),
        P("pipe", "dp"),
        P("pipe", None),
        P(),
        P(None, "dp"),
        P(None, "dp"),
        P(),
        P("pipe", "dp"),
        P("pipe", "dp"),
        P("pipe", "dp", None),
        P("pipe", "dp", None),
    )
    small_slice = mesh.shape["dp"] == 8 and mesh.shape["pipe"] == 4
    return jax.shard_map(
        on_small_slice if small_slice else on_device,
        mesh=mesh,
        in_specs=placed,
        out_specs=(
            P("pipe", None, "dp", None, None, None),
            P("pipe", None, "dp", None, None, None),
            P("pipe", "dp", None, None, None),
            P("pipe", "dp", None, None, None),
            P("pipe", None, "dp", None, None),
            P(),
            P("pipe", "dp"),
            P("pipe", "dp"),
            P("pipe", "dp"),
            P("pipe", "dp"),
            P("pipe", "dp", None),
            P("pipe", "dp", None),
        ),
        check_vma=False,
    )
```

```python
import math

import jax
import jax.numpy as jnp
import numpy as np
from jax import lax
from jax.experimental import pallas as pl
from jax.experimental.pallas import tpu as pltpu
from jax.sharding import PartitionSpec as P

C_IN = 1024
MID = 512
C_OUT = 2048
STEP = 10
NS_STEPS = 5


HIGH = lax.Precision.HIGHEST
NORM_EPS = 1e-05
POOL_EPS = 1e-06
CLIP_NORM = 1.0
LEARN_RATE = 0.02
DECAY_FIRST = 0.9
DECAY_SECOND = 0.95
DECAY_STATS = 0.95
ADAM_EPS = 1e-08
WEIGHT_DECAY = 0.01


def section_shapes(section):
    if section == 0:
        return [
            ("first_conv", (C_IN, MID)),
            ("middle_conv", (9 * MID, MID)),
            ("skip_conv", (C_IN, C_OUT)),
            ("first_gain", (MID,)),
            ("first_bias", (MID,)),
            ("middle_gain", (MID,)),
            ("middle_bias", (MID,)),
            ("skip_gain", (C_OUT,)),
            ("skip_bias", (C_OUT,)),
        ]
    if section == 2:
        return [
            ("first_conv", (C_OUT, MID)),
            ("middle_conv", (9 * MID, MID)),
            ("first_gain", (MID,)),
            ("first_bias", (MID,)),
            ("middle_gain", (MID,)),
            ("middle_bias", (MID,)),
        ]
    return [("last_conv", (MID, C_OUT)), ("last_gain", (C_OUT,)), ("last_bias", (C_OUT,))]


def unpack(flat_vector, section):
    pieces = {}
    offset = 0
    for entry_name, entry_shape in section_shapes(section):
        entry_size = math.prod(entry_shape)
        pieces[entry_name] = flat_vector[offset : offset + entry_size].reshape(entry_shape)
        offset = offset + entry_size
    return pieces


def pack(grads, section, flat_size):
    parts = [grads[entry_name].reshape(-1) for entry_name, entry_shape in section_shapes(section)]
    used = sum((math.prod(entry_shape) for entry_name, entry_shape in section_shapes(section)))
    parts.append(jnp.zeros((flat_size - used,), jnp.float32))
    return jnp.concatenate(parts)


def as_float(vector):
    return vector.astype(jnp.float32)


def to_low(groups):
    return tuple((portion.astype(jnp.bfloat16) for portion in groups))


def to_high(groups):
    return tuple((portion.astype(jnp.float32) for portion in groups))


def point_conv(groups, weight):
    return tuple(
        (
            jnp.einsum("khwc,cd->khwd", portion, weight, preferred_element_type=jnp.float32)
            for portion in groups
        )
    )


def point_back(grad_out, groups, weight):
    low_grads = to_low(grad_out)
    grad_input = tuple(
        (
            jnp.einsum("khwd,cd->khwc", grad_part, weight, preferred_element_type=jnp.float32)
            for grad_part in low_grads
        )
    )
    grad_weight = sum(
        (
            jnp.einsum("khwc,khwd->cd", in_part, grad_part, preferred_element_type=jnp.float32)
            for in_part, grad_part in zip(groups, low_grads)
        )
    )
    return (grad_input, grad_weight)


def patches(portion, stride):
    height = portion.shape[1]
    across = portion.shape[2]
    padded = jnp.pad(portion, ((0, 0), (1, 1), (1, 1), (0, 0)))
    shifted = [
        padded[:, row_off : row_off + height : stride, col_off : col_off + across : stride, :]
        for row_off in range(3)
        for col_off in range(3)
    ]
    return jnp.concatenate(shifted, axis=-1)


def area_conv(groups, weight, stride):
    columns = tuple((patches(portion, stride) for portion in groups))
    return (point_conv(columns, weight), columns)


def unpatch(grad_cols, height, across, stride):
    channels = grad_cols.shape[-1] // 9
    padded = jnp.zeros((grad_cols.shape[0], height + 2, across + 2, channels), jnp.float32)
    for row_off in range(3):
        for col_off in range(3):
            offset = (3 * row_off + col_off) * channels
            padded = padded.at[
                :, row_off : row_off + height : stride, col_off : col_off + across : stride, :
            ].add(grad_cols[..., offset : offset + channels])
    return padded[:, 1 : height + 1, 1 : across + 1, :]


def area_back(grad_out, columns, weight, stride, in_shapes):
    grad_cols, grad_weight = point_back(grad_out, columns, weight)
    grad_input = tuple(
        (
            unpatch(grad_part, shape_item[1], shape_item[2], stride)
            for grad_part, shape_item in zip(grad_cols, in_shapes)
        )
    )
    return (grad_input, grad_weight)


def batch_norm(groups, gain, bias):
    rows_total = sum((portion.shape[0] * portion.shape[1] * portion.shape[2] for portion in groups))
    centre = sum((jnp.sum(portion, axis=(0, 1, 2)) for portion in groups)) / rows_total
    spread = (
        sum((jnp.sum(jnp.square(portion - centre), axis=(0, 1, 2)) for portion in groups))
        / rows_total
    )
    inverse = lax.rsqrt(spread + NORM_EPS)
    standard = tuple(((portion - centre) * inverse for portion in groups))
    normed = tuple((gain * std_part + bias for std_part in standard))
    return (normed, (centre, spread, inverse, standard))


def norm_back(grad_out, gain, saved):
    centre, spread, inverse, standard = saved
    rows_total = sum(
        (portion.shape[0] * portion.shape[1] * portion.shape[2] for portion in standard)
    )
    grad_sum = sum((jnp.sum(grad_part, axis=(0, 1, 2)) for grad_part in grad_out))
    grad_dot = sum(
        (
            jnp.sum(grad_part * std_part, axis=(0, 1, 2))
            for grad_part, std_part in zip(grad_out, standard)
        )
    )
    grad_input = tuple(
        (
            gain
            * inverse
            * (grad_part - grad_sum / rows_total - std_part * (grad_dot / rows_total))
            for grad_part, std_part in zip(grad_out, standard)
        )
    )
    return (grad_input, grad_dot, grad_sum)


def through_softplus(grad_out, pre_values):
    return tuple(
        (grad_part * jax.nn.sigmoid(pre_part) for grad_part, pre_part in zip(grad_out, pre_values))
    )


def front_forward(pieces, inputs):
    first = point_conv(inputs, pieces["first_conv"])
    normed_a, saved_a = batch_norm(
        first, as_float(pieces["first_gain"]), as_float(pieces["first_bias"])
    )
    hidden = tuple((jax.nn.softplus(portion).astype(jnp.bfloat16) for portion in normed_a))
    middle, columns = area_conv(hidden, pieces["middle_conv"], 2)
    normed_b, saved_b = batch_norm(
        middle, as_float(pieces["middle_gain"]), as_float(pieces["middle_bias"])
    )
    narrow = tuple((jax.nn.softplus(portion) for portion in normed_b))
    reduced = tuple((portion[:, ::2, ::2, :] for portion in inputs))
    skipped = point_conv(reduced, pieces["skip_conv"])
    wide, saved_p = batch_norm(
        skipped, as_float(pieces["skip_gain"]), as_float(pieces["skip_bias"])
    )
    norm_rows = jnp.stack(
        [
            jnp.concatenate([saved_a[0], saved_b[0], saved_p[0]]),
            jnp.concatenate([saved_a[1], saved_b[1], saved_p[1]]),
        ]
    )
    kept = (normed_a, hidden, columns, normed_b, reduced, saved_a, saved_b, saved_p)
    return (wide, narrow, norm_rows, kept)


def front_backward(pieces, inputs, grad_wide, grad_narrow):
    wide, narrow, norm_rows, kept = front_forward(pieces, inputs)
    normed_a, hidden, columns, normed_b, reduced, saved_a, saved_b, saved_p = kept
    grads = {}
    grad_pre_b = through_softplus(grad_narrow, normed_b)
    grad_mid, grads["middle_gain"], grads["middle_bias"] = norm_back(
        grad_pre_b, as_float(pieces["middle_gain"]), saved_b
    )
    grad_hidden, grads["middle_conv"] = area_back(
        grad_mid, columns, pieces["middle_conv"], 2, [portion.shape for portion in hidden]
    )
    grad_pre_a = through_softplus(grad_hidden, normed_a)
    grad_first, grads["first_gain"], grads["first_bias"] = norm_back(
        grad_pre_a, as_float(pieces["first_gain"]), saved_a
    )
    grad_inputs, grads["first_conv"] = point_back(grad_first, inputs, pieces["first_conv"])
    grad_skip, grads["skip_gain"], grads["skip_bias"] = norm_back(
        grad_wide, as_float(pieces["skip_gain"]), saved_p
    )
    grad_reduced, grads["skip_conv"] = point_back(grad_skip, reduced, pieces["skip_conv"])
    grad_inputs = tuple(
        (
            full_part.at[:, ::2, ::2, :].add(part_reduced)
            for full_part, part_reduced in zip(grad_inputs, grad_reduced)
        )
    )
    return (grad_inputs, grads)


def join_forward(pieces, wide, narrow):
    last = point_conv(narrow, pieces["last_conv"])
    normed, saved = batch_norm(last, as_float(pieces["last_gain"]), as_float(pieces["last_bias"]))
    pre_values = tuple(
        (
            skip_part.astype(jnp.float32) + branch_part
            for skip_part, branch_part in zip(wide, normed)
        )
    )
    ending = tuple((jax.nn.softplus(pre_part) for pre_part in pre_values))
    filler = jnp.zeros((2 * MID,), jnp.float32)
    norm_rows = jnp.stack(
        [jnp.concatenate([saved[0], filler]), jnp.concatenate([saved[1], filler])]
    )
    return (ending, norm_rows, (pre_values, saved))


def join_grads(pieces, narrow, kept, grad_out, gate):
    pre_values, saved = kept
    grad_pre = tuple(
        (
            grad_part * jax.nn.sigmoid(pre_part) * gate
            for grad_part, pre_part in zip(grad_out, pre_values)
        )
    )
    grad_wide = tuple(
        (pre_grad + grad_part * (1.0 - gate) for pre_grad, grad_part in zip(grad_pre, grad_out))
    )
    grad_last, gain_grad, bias_grad = norm_back(grad_pre, as_float(pieces["last_gain"]), saved)
    grad_narrow, weight_grad = point_back(grad_last, narrow, pieces["last_conv"])
    grads = {"last_conv": weight_grad, "last_gain": gain_grad, "last_bias": bias_grad}
    return (grad_wide, grad_narrow, grads)


def split_forward(pieces, wide):
    first = point_conv(wide, pieces["first_conv"])
    normed_a, saved_a = batch_norm(
        first, as_float(pieces["first_gain"]), as_float(pieces["first_bias"])
    )
    hidden = tuple((jax.nn.softplus(portion).astype(jnp.bfloat16) for portion in normed_a))
    middle, columns = area_conv(hidden, pieces["middle_conv"], 1)
    normed_b, saved_b = batch_norm(
        middle, as_float(pieces["middle_gain"]), as_float(pieces["middle_bias"])
    )
    narrow = tuple((jax.nn.softplus(portion) for portion in normed_b))
    filler = jnp.zeros((C_OUT,), jnp.float32)
    norm_rows = jnp.stack(
        [
            jnp.concatenate([saved_a[0], saved_b[0], filler]),
            jnp.concatenate([saved_a[1], saved_b[1], filler]),
        ]
    )
    return (narrow, norm_rows, (normed_a, hidden, columns, normed_b, saved_a, saved_b))


def split_backward(pieces, wide, grad_relay, grad_narrow):
    narrow, norm_rows, kept = split_forward(pieces, wide)
    normed_a, hidden, columns, normed_b, saved_a, saved_b = kept
    grads = {}
    grad_pre_b = through_softplus(grad_narrow, normed_b)
    grad_mid, grads["middle_gain"], grads["middle_bias"] = norm_back(
        grad_pre_b, as_float(pieces["middle_gain"]), saved_b
    )
    grad_hidden, grads["middle_conv"] = area_back(
        grad_mid, columns, pieces["middle_conv"], 1, [portion.shape for portion in hidden]
    )
    grad_pre_a = through_softplus(grad_hidden, normed_a)
    grad_first, grads["first_gain"], grads["first_bias"] = norm_back(
        grad_pre_a, as_float(pieces["first_gain"]), saved_a
    )
    grad_conv_in, grads["first_conv"] = point_back(grad_first, wide, pieces["first_conv"])
    grad_wide = tuple(
        (relay_part + conv_part for relay_part, conv_part in zip(grad_relay, grad_conv_in))
    )
    return (grad_wide, grads)


def pool_grad(final, targets, picks):
    result = []
    for portion, pick_ids in zip(final, picks):
        cubes = jnp.mean(portion * portion * portion, axis=(1, 2)) + POOL_EPS
        factor = jnp.exp(jnp.log(cubes) * (-2.0 / 3.0)) * targets[pick_ids]
        result.append(factor[:, None, None, :] * portion * portion)
    return tuple(result)


def used_size(section):
    return sum((math.prod(entry_shape) for entry_name, entry_shape in section_shapes(section)))


def batch_pass(reals, inputs, gate, targets, picks):
    pieces = [unpack(reals[section], section) for section in range(4)]
    wide_f, narrow_f, rows_0, _ = front_forward(pieces[0], inputs)
    wide_0, narrow_0 = to_low(wide_f), to_low(narrow_f)
    ending_1, rows_1, kept_1 = join_forward(pieces[1], wide_0, narrow_0)
    wide_1 = to_low(ending_1)
    narrow_f, rows_2, _ = split_forward(pieces[2], wide_1)
    narrow_2 = to_low(narrow_f)
    ending_3, rows_3, kept_3 = join_forward(pieces[3], wide_1, narrow_2)
    final = tuple(
        (
            jnp.where(gate > 0, end_part, relay_part.astype(jnp.float32))
            for end_part, relay_part in zip(ending_3, wide_1)
        )
    )
    cotangent = pool_grad(final, targets, picks)
    grad_wide, grad_narrow, grads_3 = join_grads(pieces[3], narrow_2, kept_3, cotangent, gate)
    grad_wide, grads_2 = split_backward(
        pieces[2], wide_1, to_high(to_low(grad_wide)), to_high(to_low(grad_narrow))
    )
    grad_wide, grad_narrow, grads_1 = join_grads(
        pieces[1], narrow_0, kept_1, to_high(to_low(grad_wide)), 1.0
    )
    grad_inputs, grads_0 = front_backward(
        pieces[0], inputs, to_high(to_low(grad_wide)), to_high(to_low(grad_narrow))
    )
    outs = (wide_0, wide_1, wide_1, to_low(final))
    stats = jnp.stack([rows_0, rows_1, rows_2 * gate, rows_3 * gate])
    return (outs, stats, to_low(grad_inputs), (grads_0, grads_1, grads_2, grads_3))


def on_device(
    teach_in,
    stud_in,
    params,
    owners,
    depth_gates,
    teach_ids,
    stud_ids,
    targets,
    moment,
    second,
    gram_stats,
    eigen_basis,
):
    sections = lax.axis_size("pipe")
    rank = lax.axis_index("pipe")
    owner_count = lax.axis_size("dp")
    span_size = params.shape[1]
    flat_size = span_size * owner_count
    owner_rows = lax.all_gather(owners, "pipe", axis=0, tiled=True)
    gathered = lax.all_gather(params[0].astype(jnp.bfloat16), ("pipe", "dp"), axis=0)
    gathered = gathered.reshape(sections, owner_count, span_size)
    reals = []
    for section in range(sections):
        inverse = jnp.argsort(owner_rows[section]).astype(jnp.int32)
        blocks = -(-used_size(section) // span_size)
        reals.append(gathered[section][inverse[:blocks]].reshape(blocks * span_size))
    inputs = (teach_in[0], stud_in[0])
    gate = depth_gates[rank].astype(jnp.float32)
    outs, stats, (teach_grad, stud_grad), grads = batch_pass(
        reals, inputs, gate, targets, (teach_ids[rank], stud_ids[rank])
    )
    segment_teach = lax.all_to_all(
        jnp.stack([part[0] for part in outs]), "pipe", split_axis=0, concat_axis=0, tiled=True
    )
    segment_stud = lax.all_to_all(
        jnp.stack([part[1] for part in outs]), "pipe", split_axis=0, concat_axis=0, tiled=True
    )
    stats = lax.all_to_all(stats, "pipe", split_axis=0, concat_axis=0, tiled=True)
    rows = []
    for section in range(sections):
        flat = pack(grads[section], section, flat_size).reshape(owner_count, span_size)
        rows.append(flat[owner_rows[section]])
    span_total = lax.psum_scatter(
        jnp.stack(rows).reshape(sections * owner_count, span_size),
        ("pipe", "dp"),
        scatter_dimension=0,
        tiled=True,
    ).reshape(span_size)
    total_squares = lax.psum(jnp.sum(span_total * span_total), ("dp", "pipe"))
    grad_norm = jnp.sqrt(total_squares)
    factor = jnp.minimum(1.0, CLIP_NORM / grad_norm)
    clipped = span_total * factor
    matrix = clipped.reshape(span_size // 128, 128)
    gram_old = gram_stats[0]
    basis_old = eigen_basis[0]
    gram_new = DECAY_STATS * gram_old + (1.0 - DECAY_STATS) * jnp.dot(
        matrix.T, matrix, precision=HIGH
    )
    product = jnp.dot(gram_new, basis_old, precision=HIGH)
    rotation = product / jnp.sqrt(jnp.sum(product * product))
    for repeat in range(NS_STEPS):
        square = jnp.dot(rotation.T, rotation, precision=HIGH)
        rotation = 1.5 * rotation - 0.5 * jnp.dot(rotation, square, precision=HIGH)
    moment_old = moment.reshape(span_size // 128, 128)
    initial = jnp.dot(moment_old, basis_old.T, precision=HIGH)
    blended = DECAY_FIRST * initial + (1.0 - DECAY_FIRST) * matrix
    moment_new = jnp.dot(blended, rotation, precision=HIGH)
    rotated = jnp.dot(matrix, rotation, precision=HIGH)
    second_new = (
        DECAY_SECOND * second.reshape(span_size // 128, 128)
        + (1.0 - DECAY_SECOND) * rotated * rotated
    )
    correction = math.sqrt(1.0 - DECAY_SECOND**STEP) / (1.0 - DECAY_FIRST**STEP)
    direction = (
        jnp.dot(moment_new / (jnp.sqrt(second_new) + ADAM_EPS), rotation.T, precision=HIGH)
        * correction
    )
    weights = params.reshape(span_size // 128, 128)
    params_new = weights - LEARN_RATE * (direction + WEIGHT_DECAY * weights)
    return (
        segment_teach[None],
        segment_stud[None],
        teach_grad[None],
        stud_grad[None],
        stats[None, :, None],
        grad_norm,
        clipped.reshape(1, span_size),
        moment_new.reshape(1, span_size),
        second_new.reshape(1, span_size),
        params_new.reshape(1, span_size),
        gram_new[None],
        rotation[None],
    )


MESH = pl.DeviceIdType.MESH
LOW = jnp.bfloat16
FULL = jnp.float32
TILE = 256
WINDOW = 20
STRIDE = 19
VEC_TILE = (152, 32, 104, 32)
USED_TILES = (153, 33, 105, 33)
FRONT_WIDE = 88
SMALL_ROWS = 1056
ROWS = 120
PADDED = 128
TEACH_ROWS = 72


def any_spec():
    return pl.BlockSpec(memory_space=pl.ANY)


def smem_spec():
    return pl.BlockSpec(memory_space=pltpu.SMEM)


def vmem_spec():
    return pl.BlockSpec(memory_space=pltpu.VMEM)


def tile_forms(section, tile):
    even = lax.rem(section, 2) == 0
    vector = jnp.where(section == 0, 152, jnp.where(section == 2, 104, 32))
    narrow_end = jnp.where(section == 0, FRONT_WIDE, jnp.where(section == 2, 104, 0))
    narrow = even & (tile < narrow_end)
    plain = tile == vector
    return narrow, plain


def prepare_kernel(owners, params, big, small, ids, flat, sem):
    block, section = owners[0, lax.axis_index("dp")], lax.axis_index("pipe")

    @pl.loop(0, WINDOW)
    def _(r):
        flat[pl.ds(TILE * r, TILE)] = jnp.zeros((TILE, 128), FULL)

    copy = pltpu.make_async_copy(params.at[:, 0, :], flat.at[pl.ds(6 * block, params.shape[0])], sem)
    copy.start()

    @pl.loop(0, small.shape[0])
    def _(r):
        small[r] = jnp.zeros((TILE, 128), LOW)

    lane = lax.broadcasted_iota(jnp.int32, (8, 128), 1)
    row = jnp.zeros((8, 128), jnp.int32)
    for j in range(8):
        row = jnp.where(lane == j, owners[0, j], row)
    ids[...] = row
    copy.wait()

    @pl.loop(0, WINDOW)
    def _(r):
        tile = STRIDE * block + r
        narrow, plain = tile_forms(section, tile)
        base = TILE * r

        @pl.when(narrow)
        def _():
            for j in range(4):
                big[r, 64 * j : 64 * j + 64, :] = flat[pl.ds(base + j, 64, 4), :].astype(LOW)

        @pl.when(plain)
        def _():
            big[r] = flat[pl.ds(base, TILE), :].astype(LOW)

        @pl.when(jnp.logical_not(narrow | plain))
        def _():
            for j in range(16):
                big[r, 16 * j : 16 * j + 16, :] = flat[pl.ds(base + j, 16, 16), :].astype(LOW)

        @pl.when(tile < small.shape[0])
        def _():
            small[tile] = big[r]


def prepare(owners, params):
    return pl.pallas_call(
        prepare_kernel,
        name="prepare",
        out_shape=(
            jax.ShapeDtypeStruct((WINDOW, TILE, 128), LOW),
            jax.ShapeDtypeStruct((USED_TILES[1], TILE, 128), LOW),
            jax.ShapeDtypeStruct((8, 128), jnp.int32),
        ),
        in_specs=[smem_spec(), any_spec()],
        out_specs=(vmem_spec(),) * 3,
        scratch_shapes=[pltpu.VMEM((WINDOW * TILE, 128), FULL), pltpu.SemaphoreType.DMA],
        compiler_params=pltpu.CompilerParams(vmem_limit_bytes=60 << 20),
    )(owners, params.reshape(-1, 1, 128))


class Place:
    def __init__(self):
        self.dp = lax.axis_index("dp")
        self.pipe = lax.axis_index("pipe")
        self.x, self.core = self.pipe // 2, self.pipe % 2
        self.z, self.y = self.dp // 2, self.dp % 2

    def device(self, x=None, core=None, z=None, y=None):
        x = self.x if x is None else x
        core = self.core if core is None else core
        z = self.z if z is None else z
        y = self.y if y is None else y
        return {"dp": 2 * z + y, "pipe": 2 * x + core}

    def enter(self):
        barrier = pltpu.get_barrier_semaphore()
        for step in range(1, 8):
            other = lax.rem(self.dp + step, 8)
            pl.semaphore_signal(
                barrier, inc=1, device_id={"dp": other, "pipe": self.pipe}, device_id_type=MESH
            )
        for step in range(1, 4):
            other = lax.rem(self.pipe + step, 4)
            pl.semaphore_signal(
                barrier, inc=1, device_id={"dp": self.dp, "pipe": other}, device_id_type=MESH
            )
        pl.semaphore_wait(barrier, 10)


def remote(src, dst, send, recv, target):
    return pltpu.make_async_remote_copy(
        src_ref=src, dst_ref=dst, send_sem=send, recv_sem=recv, device_id=target, device_id_type=MESH
    )


BIG_HALF = WINDOW * TILE // 2
SMALL_HALF = SMALL_ROWS // 2


def gather_kernel(big, small, ids, all_big, all_small, table, early, chunk, early_send, early_recv,
                  z_send, z_recv, x_send, x_recv, y_send, y_recv, dx_send, dx_recv, dy_send, dy_recv,
                  s_send, s_recv, first_send, first_recv, own_sem, id_send, id_recv):
    me = Place()
    me.enter()
    x, y, z, core = me.x, me.y, me.z, me.core
    up, down = me.device(z=z + 1), me.device(z=z - 1)
    x_side, y_side, sibling = me.device(x=1 - x), me.device(y=1 - y), me.device(core=1 - core)

    class Stream:
        def __init__(self, n, out, cut):
            self.n, self.out, self.cut, self.rows = n, out, cut, out.shape[3]

        def block(self, xo, origin, yo):
            return self.out.at[xo, 2 * origin + yo, core]

        def move_x(self, origin):
            block = self.block(x, origin, y)
            return remote(block, block, x_send.at[self.n, origin], x_recv.at[self.n, origin], x_side)

        def move_y(self, origin):
            block = self.block(x, origin, y)
            return remote(block, block, y_send.at[self.n, origin], y_recv.at[self.n, origin], y_side)

        def share(self, xo, origin, yo):
            block = self.block(xo, origin, yo)
            at = 8 * xo + 2 * origin + yo
            return remote(block, block, s_send.at[self.n, at], s_recv.at[self.n, at], sibling)

        def move_z(self, origin, target, way):
            block = self.block(x, origin, y)
            return remote(block, block, z_send.at[self.n, way, origin], z_recv.at[self.n, origin], target)

        def half_x(self, origin, xo, yo):
            part = self.out.at[xo, 2 * origin + yo, core, pl.ds(self.cut, self.rows - self.cut)]
            return remote(part, part, dx_send.at[self.n, origin], dx_recv.at[self.n, origin], x_side)

        def half_y(self, origin, xo, yo):
            part = self.out.at[xo, 2 * origin + yo, core, pl.ds(0, self.cut)]
            return remote(part, part, dy_send.at[self.n, origin], dy_recv.at[self.n, origin], y_side)

        def spread(self, origin):
            self.move_x(origin).start()
            self.move_y(origin).start()
            self.share(x, origin, y).start()

        def from_sides(self, origin):
            self.move_x(origin).wait_recv()
            self.half_y(origin, 1 - x, y).start()
            self.share(1 - x, origin, y).start()
            self.move_y(origin).wait_recv()
            self.half_x(origin, x, 1 - y).start()
            self.share(x, origin, 1 - y).start()

        def from_diagonal(self, origin):
            self.half_x(origin, 1 - x, 1 - y).wait_recv()
            self.half_y(origin, 1 - x, 1 - y).wait_recv()
            self.share(1 - x, origin, 1 - y).start()

        def each(self, step, action):
            if step == 0:
                action(z)
            else:
                pl.when(z >= step)(lambda: action(z - step))
                pl.when(z + step <= 3)(lambda: action(z + step))

        def step(self, k):
            if k == 0:
                pl.when(z < 3)(lambda: self.move_z(z, up, 0).start())
                pl.when(z > 0)(lambda: self.move_z(z, down, 1).start())
                self.spread(z)
            elif k < 4:

                @pl.when(z >= k)
                def _():
                    self.move_z(z - k, up, 0).wait_recv()
                    pl.when(z < 3)(lambda: self.move_z(z - k, up, 0).start())
                    self.spread(z - k)

                @pl.when(z + k <= 3)
                def _():
                    self.move_z(z + k, down, 1).wait_recv()
                    pl.when(z > 0)(lambda: self.move_z(z + k, down, 1).start())
                    self.spread(z + k)

            if 1 <= k < 5:
                self.each(k - 1, self.from_sides)
            if k >= 2:
                self.each(k - 2, self.from_diagonal)

        def close(self):
            for origin in range(4):
                self.move_x(origin).wait_send()
                self.move_y(origin).wait_send()
                self.half_x(origin, x, 1 - y).wait_send()
                self.half_y(origin, 1 - x, y).wait_send()
                pl.when((z < 3) & (origin <= z))(lambda: self.move_z(origin, up, 0).wait_send())
                pl.when((z > 0) & (origin >= z))(lambda: self.move_z(origin, down, 1).wait_send())
                for xo in range(2):
                    for yo in range(2):
                        self.share(xo, origin, yo).wait_send()
                        theirs = self.out.at[xo, 2 * origin + yo, 1 - core]
                        at = 8 * xo + 2 * origin + yo
                        remote(theirs, theirs, s_send.at[self.n, at], s_recv.at[self.n, at], sibling).wait_recv()

    bulk = Stream(0, all_big, BIG_HALF // 2)
    light = Stream(1, all_small, 256)

    def early_copy(step):
        target = lax.rem(me.dp + step, 8)
        return remote(
            small.at[target], early.at[step], early_send.at[step], early_recv.at[step],
            {"dp": target, "pipe": me.pipe},
        )

    big_half = all_big.at[x, me.dp, 1]
    big_first = remote(big.at[pl.ds(BIG_HALF, BIG_HALF)], big_half, first_send.at[0], first_recv.at[0], sibling)
    small_half = all_small.at[x, me.dp, 0]
    small_first = remote(chunk.at[pl.ds(0, SMALL_HALF)], small_half, first_send.at[1], first_recv.at[1], sibling)

    @pl.when(core == 0)
    def _():
        big_first.start()
        copy = pltpu.make_async_copy(big.at[pl.ds(0, BIG_HALF)], all_big.at[x, me.dp, 0], own_sem.at[0])
        copy.start()
        copy.wait()

    @pl.when(core == 1)
    def _():
        for step in range(1, 8):
            early_copy(step).start()
        pltpu.make_async_copy(small.at[me.dp], early.at[0], own_sem.at[1]).start()
        big_first.wait_recv()

    bulk.step(0)
    row = pltpu.make_async_copy(ids, table.at[me.pipe], own_sem.at[2])
    row.start()
    for step in range(1, 4):
        remote(
            ids, table.at[me.pipe], id_send.at[step], id_recv.at[step],
            {"dp": me.dp, "pipe": lax.rem(me.pipe + step, 4)},
        ).start()

    @pl.when(core == 0)
    def _():
        small_first.wait_recv()

    @pl.when(core == 1)
    def _():
        pltpu.make_async_copy(small.at[me.dp], early.at[0], own_sem.at[1]).wait()
        for step in range(1, 8):
            early_copy(step).wait()

        @pl.loop(0, 6)
        def _(i):
            part = pl.ds(pl.multiple_of(176 * i, 16), 176)
            total = early[0, part, :].astype(FULL)
            for step in range(1, 8):
                total = total + early[step, part, :].astype(FULL)
            chunk[part, :] = total.astype(LOW)

        small_first.start()
        copy = pltpu.make_async_copy(chunk.at[pl.ds(SMALL_HALF, SMALL_HALF)], all_small.at[x, me.dp, 1], own_sem.at[0])
        copy.start()
        copy.wait()

    light.step(0)
    for k in range(1, 6):
        bulk.step(k)
        light.step(k)
    bulk.close()
    light.close()
    row.wait()
    for step in range(1, 4):
        here = lax.rem(me.pipe + 4 - step, 4)
        move = remote(
            ids, table.at[here], id_send.at[step], id_recv.at[step],
            {"dp": me.dp, "pipe": lax.rem(me.pipe + step, 4)},
        )
        move.wait_recv()
        move.wait_send()

    @pl.when(core == 0)
    def _():
        big_first.wait_send()

    @pl.when(core == 1)
    def _():
        small_first.wait_send()


def gather_all(big, small, ids):
    sem = pltpu.SemaphoreType.DMA
    return pl.pallas_call(
        gather_kernel,
        name="gather_all",
        out_shape=(
            jax.ShapeDtypeStruct((2, 8, 2, BIG_HALF, 128), LOW),
            jax.ShapeDtypeStruct((2, 8, 2, SMALL_HALF, 128), LOW),
            jax.ShapeDtypeStruct((4, 8, 128), jnp.int32),
        ),
        in_specs=[any_spec()] * 3,
        out_specs=(any_spec(),) * 3,
        scratch_shapes=[
            pltpu.VMEM((8, SMALL_ROWS, 128), LOW),
            pltpu.VMEM((SMALL_ROWS, 128), LOW),
            sem((8,)), sem((8,)),
            sem((2, 2, 4)), sem((2, 4)),
            sem((2, 4)), sem((2, 4)), sem((2, 4)), sem((2, 4)),
            sem((2, 4)), sem((2, 4)), sem((2, 4)), sem((2, 4)),
            sem((2, 16)), sem((2, 16)),
            sem((2,)), sem((2,)), sem((3,)), sem((4,)), sem((4,)),
        ],
        compiler_params=pltpu.CompilerParams(
            collective_id=0, has_side_effects=True, vmem_limit_bytes=60 << 20
        ),
    )(big.reshape(WINDOW * TILE, 128), small.reshape(8, SMALL_ROWS, 128), ids)


def soft(value):
    return jnp.maximum(value, 0.0) + jnp.log1p(jnp.exp(-jnp.abs(value)))


def gate_of(value):
    small = jnp.exp(-jnp.abs(value))
    share = 1.0 / (1.0 + small)
    return jnp.where(value >= 0, share, small * share)


def standardize(z):
    count = z.shape[0]
    centre = jnp.sum(z, axis=0, keepdims=True) / count
    away = z - centre
    spread = jnp.sum(away * away, axis=0, keepdims=True) / count
    inverse = lax.rsqrt(spread + NORM_EPS)
    return away * inverse, centre, spread, inverse


def unstandardize(grad, standard, gain, inverse):
    count = grad.shape[0]
    grad_sum = jnp.sum(grad, axis=0, keepdims=True)
    grad_dot = jnp.sum(grad * standard, axis=0, keepdims=True)
    result = gain * inverse * (grad - grad_sum / count - standard * (grad_dot / count))
    return result, grad_dot, grad_sum


def pad_low(value):
    zeros = jnp.zeros((PADDED - ROWS, value.shape[1]), FULL)
    return jnp.concatenate([value, zeros], axis=0).astype(LOW)


def mul(a, b):
    return jnp.dot(a, b, preferred_element_type=FULL)


def mul_t(a, b):
    return lax.dot_general(a, b, (((1,), (1,)), ((), ())), preferred_element_type=FULL)


def narrow_part(ref, start, count, blocks=range(4)):
    return jnp.concatenate(
        [ref[pl.ds(start, count), 64 * j : 64 * j + 64, :].reshape(64 * count, 128) for j in blocks],
        axis=1,
    )


def put_narrow(ref, start, count, value):
    for j in range(4):
        ref[pl.ds(start, count), 64 * j : 64 * j + 64, :] = (
            value[:, 128 * j : 128 * j + 128].astype(LOW).reshape(count, 64, 128)
        )


def wide_part(ref, start, count, c):
    return jnp.concatenate(
        [
            ref[start : start + count, pl.ds(pl.multiple_of(32 * c + 16 * h, 16), 16), :].reshape(
                16 * count, 128
            )
            for h in range(2)
        ],
        axis=1,
    )


def put_wide(ref, start, count, c, value):
    for h in range(2):
        ref[start : start + count, pl.ds(pl.multiple_of(32 * c + 16 * h, 16), 16), :] = (
            value[:, 128 * h : 128 * h + 128].astype(LOW).reshape(count, 16, 128)
        )


def step_kernel(table, gates, teach_ids, stud_ids, all_big, all_small, x, targets, grid,
                wide0, wide1, final, stats, grad_x, out_big, out_small,
                w0, w1, w2, w3, edges, vec, grad_vec, raw,
                std_a, std_b, std_p, std_1, std_c, std_d, hidden, cols0, cols2,
                nar0, nar2, turned, relay, dz_a, dz_n, acc, acc_x, grad_h,
                wanted, inv, in_sem, edge_sem, out_sem):
    rank = lax.axis_index("pipe")
    gate = gates[rank].astype(FULL)
    for group in range(2):
        for j in range(8):
            inv[8 * group + table[2 * group, 0, j]] = j
    picks = [teach_ids[rank, k] for k in range(2)] + [stud_ids[rank, k] for k in range(3)]
    rows = [
        pltpu.make_async_copy(targets.at[pl.ds(pick, 1)], wanted.at[pl.ds(k, 1)], edge_sem.at[12 + k])
        for k, pick in enumerate(picks)
    ]
    for fetched in rows:
        fetched.start()
    weights = (w0, w1, w2, w3)
    loads = {0: [], 1: [], 2: [], 3: []}
    for group, weight, blocks in ((0, w0, 8), (1, w2, 6)):
        for b in range(blocks):
            first, here = 19 * b, inv[8 * group + b]
            at = 8 * group + b
            loads[2 * group].append(pltpu.make_async_copy(
                all_big.at[group, here, 0], weight.at[pl.ds(first, 10)], in_sem.at[0, at]))
            if first + 10 < USED_TILES[2 * group]:
                count = 10 if b == 7 else 9
                loads[2 * group].append(pltpu.make_async_copy(
                    all_big.at[group, here, 1, pl.ds(0, count)], weight.at[pl.ds(first + 10, count)],
                    in_sem.at[1, at]))
            if b < blocks - 1:
                at = 7 * group + b
                loads[2 * group].append(pltpu.make_async_copy(
                    all_big.at[group, here, 1, pl.ds(9, 1)], edges.at[pl.ds(at, 1)], edge_sem.at[at]))
    loads[1].append(pltpu.make_async_copy(all_small.at[0], w1, in_sem.at[0, 14]))
    loads[3].append(pltpu.make_async_copy(all_small.at[1], w3, in_sem.at[0, 15]))
    for section in range(4):
        for load in loads[section]:
            load.start()

    raw[...] = jnp.zeros_like(raw)
    grad_vec[...] = jnp.zeros_like(grad_vec)

    def settle(section):
        for load in loads[section]:
            load.wait()
        if section == 0:
            for b in range(7):
                w0[19 * b + 19] = (w0[19 * b + 19].astype(FULL) + edges[b].astype(FULL)).astype(LOW)
        if section == 2:
            for b in range(5):
                w2[19 * b + 19] = (
                    w2[19 * b + 19].astype(FULL) + edges[7 + b].astype(FULL)
                ).astype(LOW)
        vec[section] = weights[section][VEC_TILE[section], 0:48, :].astype(FULL)

    def row(section, start):
        return jnp.concatenate(
            [vec[section, pl.ds(start + h, 1), :] for h in range(2)], axis=1
        )

    def put_row(section, start, value):
        for h in range(2):
            grad_vec[section, pl.ds(start + h, 1), :] = value[:, 128 * h : 128 * h + 128]

    def put_stats(section, column, centre, spread):
        raw[2 * section : 2 * section + 1, pl.ds(column, 256)] = centre
        raw[2 * section + 1 : 2 * section + 2, pl.ds(column, 256)] = spread

    def inverse_of(section, column):
        return lax.rsqrt(raw[2 * section + 1 : 2 * section + 2, pl.ds(column, 256)] + NORM_EPS)

    def lanes(c):
        return pl.ds(pl.multiple_of(256 * c, 256), 256)

    at_row, at_col, side = grid[0], grid[1], grid[2]

    def masked(value, dr, dc):
        ok = (at_row + dr >= 0) & (at_row + dr < side) & (at_col + dc >= 0) & (at_col + dc < side)
        return jnp.concatenate(
            [jnp.where(ok, value[:, 128 * j : 128 * j + 128], 0.0) for j in range(4)], axis=1
        )

    def rolled(value, sign, dr, dc):
        parts = []
        for start, end, width in ((0, TEACH_ROWS, 6), (TEACH_ROWS, ROWS, 4)):
            by = (sign * (dr * width + dc)) % (end - start)
            part = value[start:end]
            parts.append(part if by == 0 else pltpu.roll(part, by, 0))
        return jnp.concatenate(parts, axis=0)

    def taps(stride):
        for t in range(9):
            r, q = t // 3, t % 3
            if stride == 1:
                yield t, 0, r - 1, q - 1
            else:
                phase = 2 * (1 if r != 1 else 0) + (1 if q != 1 else 0)
                yield t, phase, -1 if r == 0 else 0, -1 if q == 0 else 0

    settle(0)
    whole_x = x[...].reshape(4 * PADDED, C_IN)
    for c in range(2):
        z = mul(whole_x, narrow_part(w0, 0, 16, (2 * c, 2 * c + 1)))
        z = jnp.concatenate([z[PADDED * p : PADDED * p + ROWS] for p in range(4)], axis=0)
        standard, centre, spread, _ = standardize(z)
        put_stats(0, 256 * c, centre, spread)
        std_a[:, 256 * c : 256 * c + 256] = standard
        hidden[:, 256 * c : 256 * c + 256] = (
            soft(row(0, 2 * c) * standard + row(0, 4 + 2 * c)).astype(LOW).astype(FULL)
        )

    for t, phase, dr, dc in taps(2):
        cols0[t] = pad_low(masked(rolled(hidden[ROWS * phase : ROWS * phase + ROWS, :], -1, dr, dc), dr, dc))
    acc[...] = jnp.zeros_like(acc)

    @pl.loop(0, 9)
    def _(t):
        acc[...] += mul(cols0[t], narrow_part(w0, 16 + 8 * t, 8))

    def middle(section, std, nar):
        for c in range(2):
            at = slice(256 * c, 256 * c + 256)
            standard, centre, spread, _ = standardize(acc[0:ROWS, at])
            put_stats(section, MID + 256 * c, centre, spread)
            std[:, at] = standard
            nar[:, at] = pad_low(soft(row(section, 8 + 2 * c) * standard + row(section, 12 + 2 * c)))

    middle(0, std_b, nar0)
    acc[...] = jnp.zeros_like(acc)
    settle(1)
    settle(2)

    @pl.loop(0, 8)
    def _(c):
        at = lanes(c)
        standard, centre, spread, _ = standardize(mul(x[0], wide_part(w0, FRONT_WIDE, 64, c))[0:ROWS])
        put_stats(0, 2 * MID + pl.multiple_of(256 * c, 256), centre, spread)
        std_p[:, at] = standard
        low = pad_low(row(0, 16 + 2 * c) * standard + row(0, 32 + 2 * c))
        wide0[:, at] = low
        standard, centre, spread, _ = standardize(mul(nar0[...], wide_part(w1, 0, 32, c))[0:ROWS])
        put_stats(1, pl.multiple_of(256 * c, 256), centre, spread)
        std_1[:, at] = standard
        pre = low.astype(FULL)[0:ROWS] + row(1, 2 * c) * standard + row(1, 16 + 2 * c)
        low = pad_low(soft(pre))
        wide1[:, at] = low
        acc[...] += mul(low, narrow_part(w2, 4 * c, 4))

    for c in range(2):
        at = slice(256 * c, 256 * c + 256)
        standard, centre, spread, _ = standardize(acc[0:ROWS, at])
        put_stats(2, 256 * c, centre, spread)
        std_c[:, at] = standard
        hidden[0:ROWS, at] = soft(row(2, 2 * c) * standard + row(2, 4 + 2 * c)).astype(LOW).astype(FULL)
    for t, phase, dr, dc in taps(1):
        cols2[t] = pad_low(masked(rolled(hidden[0:ROWS, :], -1, dr, dc), dr, dc))
    acc[...] = jnp.zeros_like(acc)

    @pl.loop(0, 9)
    def _(t):
        acc[...] += mul(cols2[t], narrow_part(w2, 32 + 8 * t, 8))

    middle(2, std_d, nar2)

    turned[...] = nar2[...].T
    acc[...] = jnp.zeros_like(acc)
    settle(3)
    for fetched in rows:
        fetched.wait()

    def spread_rows(values):
        head = lax.broadcasted_iota(jnp.int32, (8, 256), 0) < 4
        first, second = (jnp.broadcast_to(value, (8, 256)) for value in values[0:2])
        parts = [jnp.broadcast_to(values[0], (32, 256)), jnp.where(head, first, second)]
        parts.append(jnp.broadcast_to(values[1], (32, 256)))
        parts.extend(jnp.broadcast_to(value, (16, 256)) for value in values[2:5])
        return jnp.concatenate(parts, axis=0)

    def crop_sums(value):
        head = lax.broadcasted_iota(jnp.int32, (8, 256), 0) < 4
        between = value[32:40]

        def total(part):
            return jnp.sum(part, axis=0, keepdims=True)

        return [
            total(value[0:32]) + total(jnp.where(head, between, 0.0)),
            total(value[40:72]) + total(jnp.where(head, 0.0, between)),
            total(value[72:88]),
            total(value[88:104]),
            total(value[104:120]),
        ]

    @pl.loop(0, 8)
    def _(c):
        at = lanes(c)
        weight = wide_part(w3, 0, 32, c)
        standard, centre, spread, inverse = standardize(mul(nar2[...], weight)[0:ROWS])
        put_stats(3, pl.multiple_of(256 * c, 256), centre, spread)
        gain = row(3, 2 * c)
        before = wide1[:, at].astype(FULL)[0:ROWS]
        pre = before + gain * standard + row(3, 16 + 2 * c)
        ending = jnp.where(gate > 0, soft(pre), before)
        final[:, at] = pad_low(ending)
        square = ending * ending
        factors = []
        for crop, total in enumerate(crop_sums(square * ending)):
            mean = total / (36.0 if crop < 2 else 16.0) + POOL_EPS
            factors.append(jnp.exp(jnp.log(mean) * (-2.0 / 3.0)) * wanted[crop : crop + 1, at])
        cotangent = spread_rows(factors) * square
        grad_pre = cotangent * gate_of(pre) * gate
        relay[:, at] = pad_low(grad_pre + cotangent * (1.0 - gate))
        result, grad_gain, grad_bias = unstandardize(grad_pre, standard, gain, inverse)
        put_row(3, 2 * c, grad_gain)
        put_row(3, 16 + 2 * c, grad_bias)
        low = pad_low(result)
        acc[...] += mul_t(low, weight)
        put_wide(w3, 0, 32, c, mul(turned[...], low))

    def flush(section):
        weights[section][VEC_TILE[section]] = grad_vec[section].astype(LOW)

    flush(3)
    stores = [pltpu.make_async_copy(w3, out_small.at[1], out_sem.at[15])]
    stores[-1].start()

    def middle_back(section, std):
        for c in range(2):
            at = slice(256 * c, 256 * c + 256)
            gain, bias = row(section, 8 + 2 * c), row(section, 12 + 2 * c)
            grad = acc[0:ROWS, at].astype(LOW).astype(FULL) * gate_of(gain * std[:, at] + bias)
            result, grad_gain, grad_bias = unstandardize(
                grad, std[:, at], gain, inverse_of(section, MID + 256 * c)
            )
            put_row(section, 8 + 2 * c, grad_gain)
            put_row(section, 12 + 2 * c, grad_bias)
            dz_n[:, at] = pad_low(result)

    def taps_back(weight, start, cols, stride, phases):
        grad_h[0 : ROWS * phases, :] = jnp.zeros((ROWS * phases, MID), FULL)
        for t, phase, dr, dc in taps(stride):
            part = mul_t(dz_n[...], narrow_part(weight, start + 8 * t, 8))[0:ROWS]
            at = slice(ROWS * phase, ROWS * phase + ROWS)
            grad_h[at, :] += rolled(masked(part, dr, dc), 1, dr, dc)
            put_narrow(weight, start + 8 * t, 8, mul(cols[t].T, dz_n[...]))

    middle_back(2, std_d)
    taps_back(w2, 32, cols2, 1, 1)
    for c in range(2):
        at = slice(256 * c, 256 * c + 256)
        gain, bias = row(2, 2 * c), row(2, 4 + 2 * c)
        grad = grad_h[0:ROWS, at] * gate_of(gain * std_c[:, at] + bias)
        result, grad_gain, grad_bias = unstandardize(grad, std_c[:, at], gain, inverse_of(2, 256 * c))
        put_row(2, 2 * c, grad_gain)
        put_row(2, 4 + 2 * c, grad_bias)
        dz_n[:, at] = pad_low(result)
    turned[...] = nar0[...].T
    acc[...] = jnp.zeros_like(acc)
    acc_x[...] = jnp.zeros_like(acc_x)

    @pl.loop(0, 8)
    def _(c):
        at = lanes(c)
        low = dz_n[...]
        grad = relay[:, at].astype(FULL) + mul_t(low, narrow_part(w2, 4 * c, 4))
        put_narrow(w2, 4 * c, 4, mul(wide1[:, at].T, low))
        grad = grad.astype(LOW).astype(FULL)[0:ROWS]
        gain = row(1, 2 * c)
        pre = wide0[:, at].astype(FULL)[0:ROWS] + gain * std_1[:, at] + row(1, 16 + 2 * c)
        grad = grad * gate_of(pre)
        result, grad_gain, grad_bias = unstandardize(
            grad, std_1[:, at], gain, inverse_of(1, pl.multiple_of(256 * c, 256))
        )
        put_row(1, 2 * c, grad_gain)
        put_row(1, 16 + 2 * c, grad_bias)
        low = pad_low(result)
        acc[...] += mul_t(low, wide_part(w1, 0, 32, c))
        put_wide(w1, 0, 32, c, mul(turned[...], low))
        grad = grad.astype(LOW).astype(FULL)
        result, grad_gain, grad_bias = unstandardize(
            grad, std_p[:, at], row(0, 16 + 2 * c), inverse_of(0, 2 * MID + pl.multiple_of(256 * c, 256))
        )
        put_row(0, 16 + 2 * c, grad_gain)
        put_row(0, 32 + 2 * c, grad_bias)
        low = pad_low(result)
        acc_x[...] += mul_t(low, wide_part(w0, FRONT_WIDE, 64, c))
        put_wide(w0, FRONT_WIDE, 64, c, mul(x[0].T, low))

    flush(1)
    flush(2)
    w2[105:115] = jnp.zeros((10, TILE, 128), LOW)
    stores.append(pltpu.make_async_copy(w1, out_small.at[0], out_sem.at[14]))
    stores[-1].start()
    for b in range(8):
        if b < 6:
            stores.append(pltpu.make_async_copy(
                w2.at[pl.ds(19 * b, 20)], out_big.at[1, inv[8 + b]], out_sem.at[8 + b]))
            stores[-1].start()
        else:
            for h in range(2):
                stores.append(pltpu.make_async_copy(
                    w2.at[pl.ds(105, 10)], out_big.at[1, inv[8 + b], pl.ds(10 * h, 10)],
                    out_sem.at[16 + 2 * (b - 6) + h]))
                stores[-1].start()

    middle_back(0, std_b)
    taps_back(w0, 16, cols0, 2, 4)
    for c in range(2):
        at = slice(256 * c, 256 * c + 256)
        gain, bias = row(0, 2 * c), row(0, 4 + 2 * c)
        grad = grad_h[:, at] * gate_of(gain * std_a[:, at] + bias)
        result, grad_gain, grad_bias = unstandardize(grad, std_a[:, at], gain, inverse_of(0, 256 * c))
        put_row(0, 2 * c, grad_gain)
        put_row(0, 4 + 2 * c, grad_bias)
        for p in range(4):
            dz_a[PADDED * p : PADDED * p + PADDED, at] = pad_low(result[ROWS * p : ROWS * p + ROWS])

    @pl.loop(0, 4)
    def _(c):
        at = lanes(c)
        low = dz_a[...]
        part = mul_t(low, narrow_part(w0, 4 * c, 4))
        grad_x[0, :, at] = (part[0:PADDED] + acc_x[:, at]).astype(LOW)
        for p in range(1, 4):
            grad_x[p, :, at] = part[PADDED * p : PADDED * p + PADDED].astype(LOW)
        turned_x = x[:, :, at].reshape(4 * PADDED, 256).T
        put_narrow(w0, 4 * c, 4, mul(turned_x, low))

    flush(0)
    for b in range(8):
        stores.append(pltpu.make_async_copy(
            w0.at[pl.ds(19 * b, 20)], out_big.at[0, inv[b]], out_sem.at[b]))
        stores[-1].start()
    for section in range(4):
        part = raw[2 * section : 2 * section + 2]
        stats[section, 0:2] = part if section < 2 else part * gate
        stats[section, 2:8] = jnp.zeros((6, 2 * MID + C_OUT), FULL)
    for store in stores:
        store.wait()


def run_step(table, gates, teach_ids, stud_ids, all_big, all_small, phases, targets):
    spots = np.zeros((3, ROWS, 128), np.int32)
    for r in range(ROWS):
        width = 6 if r < TEACH_ROWS else 4
        at = r % 36 if r < TEACH_ROWS else (r - TEACH_ROWS) % 16
        spots[0, r], spots[1, r], spots[2, r] = at // width, at % width, width
    sem = pltpu.SemaphoreType.DMA
    wide = jax.ShapeDtypeStruct((PADDED, C_OUT), LOW)
    vm = pltpu.VMEM
    return pl.pallas_call(
        step_kernel,
        name="step",
        out_shape=(
            wide, wide, wide,
            jax.ShapeDtypeStruct((4, 8, 2 * MID + C_OUT), FULL),
            jax.ShapeDtypeStruct((4, PADDED, C_IN), LOW),
            jax.ShapeDtypeStruct((2, 8, WINDOW, TILE, 128), LOW),
            jax.ShapeDtypeStruct((2, USED_TILES[1], TILE, 128), LOW),
        ),
        in_specs=[smem_spec()] * 4 + [any_spec(), any_spec(), vmem_spec(), any_spec(), vmem_spec()],
        out_specs=(vmem_spec(),) * 5 + (any_spec(),) * 2,
        scratch_shapes=[
            vm((153, TILE, 128), LOW), vm((33, TILE, 128), LOW), vm((115, TILE, 128), LOW), vm((33, TILE, 128), LOW),
            vm((12, TILE, 128), LOW), vm((4, 48, 128), FULL), vm((4, TILE, 128), FULL),
            vm((8, 2 * MID + C_OUT), FULL),
            vm((4 * ROWS, MID), FULL), vm((ROWS, MID), FULL), vm((ROWS, C_OUT), FULL), vm((ROWS, C_OUT), FULL),
            vm((ROWS, MID), FULL), vm((ROWS, MID), FULL), vm((4 * ROWS, MID), FULL),
            vm((9, PADDED, MID), LOW), vm((9, PADDED, MID), LOW),
            vm((PADDED, MID), LOW), vm((PADDED, MID), LOW), vm((MID, PADDED), LOW),
            vm((PADDED, C_OUT), LOW), vm((4 * PADDED, MID), LOW), vm((PADDED, MID), LOW),
            vm((PADDED, MID), FULL), vm((PADDED, C_IN), FULL), vm((4 * ROWS, MID), FULL),
            vm((8, C_OUT), FULL), pltpu.SMEM((16,), jnp.int32),
            sem((2, 16)), sem((17,)), sem((20,)),
        ],
        compiler_params=pltpu.CompilerParams(vmem_limit_bytes=60 << 20),
    )(table, gates, teach_ids, stud_ids, all_big, all_small, phases, targets, jnp.asarray(spots))


RED_ROWS = BIG_HALF + SMALL_HALF
RED_CUT = 1536


def reduce_kernel(big, small, wide0, wide1, final, stats, out_big, out_small, segments, out_stats,
                  got, halves_x, halves_y, from_x, from_y, from_low, from_high, stage, total, late, late_half,
                  s_send, s_recv, hx_send, hx_recv, hy_send, hy_recv, x_send, x_recv,
                  y_send, y_recv, zu_send, zu_recv, zd_send, zd_recv, stage_sem, out_sem, late_send, late_recv,
                  join_send, join_recv, seg_send, seg_recv, stat_send, stat_recv):
    me = Place()
    me.enter()
    x, y, z, core = me.x, me.y, me.z, me.core
    up, down = me.device(z=z + 1), me.device(z=z - 1)
    x_side, y_side, sibling = me.device(x=1 - x), me.device(y=1 - y), me.device(core=1 - core)
    order = [
        jnp.where(z < 2, 3, 0),
        jnp.where(z == 0, 2, jnp.where(z == 1, 0, jnp.where(z == 2, 3, 1))),
        jnp.where(z == 0, 1, jnp.where(z == 1, 2, jnp.where(z == 2, 1, 2))),
        z,
    ]
    columns = ((1 - x, 1 - y), (x, 1 - y), (1 - x, y), (x, y))
    sequence = []
    for wave in range(6):
        for group, lag in ((0, 0), (1, 1), (2, 1), (3, 2)):
            if 0 <= wave - lag < 4:
                sequence.append((group, wave - lag))

    def spans(start, count):
        for begin in range(start, start + count, 512):
            yield begin, min(512, start + count - begin)

    def share(group, k):
        xo, yo = columns[group]
        at, jo = 4 * group + k, 2 * order[k] + yo
        return (
            remote(big.at[xo, jo, 1 - core], got.at[at, pl.ds(0, BIG_HALF)],
                   s_send.at[0, at], s_recv.at[0, at], sibling),
            remote(small.at[xo, jo, 1 - core], got.at[at, pl.ds(BIG_HALF, SMALL_HALF)],
                   s_send.at[1, at], s_recv.at[1, at], sibling),
        )

    def fetch(n):
        group, k = sequence[n]
        xo, yo = columns[group]
        jo = 2 * order[k] + yo
        return (
            pltpu.make_async_copy(big.at[xo, jo, core], stage.at[n % 4, pl.ds(0, BIG_HALF)], stage_sem.at[0, n % 4]),
            pltpu.make_async_copy(
                small.at[xo, jo, core], stage.at[n % 4, pl.ds(BIG_HALF, SMALL_HALF)], stage_sem.at[1, n % 4]),
        )

    def add(n, start, count, extras):
        group, k = sequence[n]
        at = 4 * group + k

        def piece(begin, size):
            part = pl.ds(begin, size)
            sums = got[at, part, :].astype(FULL) + stage[n % 4, part, :].astype(FULL)
            for ref in extras:
                sums = sums + ref[k, pl.ds(begin - start, size), :].astype(FULL)
            got[at, part, :] = sums.astype(LOW)

        over(start, count, piece)

    def over(start, count, piece):
        whole = count // 512

        @pl.loop(0, whole)
        def _(i):
            piece(pl.multiple_of(start + 512 * i, 16), 512)

        if count % 512:
            piece(start + 512 * whole, count % 512)

    def merge(at, ref, k):
        def piece(begin, size):
            part = pl.ds(begin, size)
            got[at, part, :] = (got[at, part, :].astype(FULL) + ref[k, part, :].astype(FULL)).astype(LOW)

        over(0, RED_ROWS, piece)

    def send_half_x(k):
        return remote(got.at[k, pl.ds(RED_CUT, RED_ROWS - RED_CUT)], halves_x.at[k],
                      hx_send.at[k], hx_recv.at[k], x_side)

    def send_half_y(k):
        return remote(got.at[k, pl.ds(0, RED_CUT)], halves_y.at[k], hy_send.at[k], hy_recv.at[k], y_side)

    def send_y(k):
        return remote(got.at[4 + k], from_y.at[k], y_send.at[k], y_recv.at[k], y_side)

    def send_x(k):
        return remote(got.at[8 + k], from_x.at[k], x_send.at[k], x_recv.at[k], x_side)

    def send_up(at, zd):
        return remote(got.at[at], from_low.at[zd - 1], zu_send.at[zd - 1], zu_recv.at[zd - 1], up)

    def send_down(at, zd):
        return remote(got.at[at], from_high.at[zd], zd_send.at[zd], zd_recv.at[zd], down)

    leaving = (wide0, wide1, wide1, final)

    def exchange(section):
        target = {"dp": me.dp, "pipe": section}
        yield remote(leaving[section], segments.at[me.pipe], seg_send.at[section], seg_recv.at[me.pipe], target)
        yield remote(stats.at[section], out_stats.at[me.pipe], stat_send.at[section], stat_recv.at[me.pipe], target)

    def keep(section):
        yield pltpu.make_async_copy(leaving[section], segments.at[me.pipe], seg_send.at[section])
        yield pltpu.make_async_copy(stats.at[section], out_stats.at[me.pipe], stat_send.at[section])

    def arriving(micro):
        target = {"dp": me.dp, "pipe": micro}
        yield remote(wide0, segments.at[micro], seg_send.at[micro], seg_recv.at[micro], target)
        yield remote(stats.at[0], out_stats.at[micro], stat_send.at[micro], stat_recv.at[micro], target)

    def all_of(copies, act):
        for copy in copies:
            act(copy)

    for group, k in sequence:
        all_of(share(group, k), lambda copy: copy.start())
    for n in range(2):
        all_of(fetch(n), lambda copy: copy.start())
    for n, (group, k) in enumerate(sequence):
        at = 4 * group + k
        if n + 2 < 16:
            all_of(fetch(n + 2), lambda copy: copy.start())
        all_of(fetch(n), lambda copy: copy.wait())
        all_of(share(group, k), lambda copy: copy.wait_recv())
        if group == 0:
            add(n, 0, RED_ROWS, [])
            send_half_x(k).start()
            send_half_y(k).start()
        elif group == 1:
            send_half_x(k).wait_recv()
            add(n, 0, RED_CUT, [])
            add(n, RED_CUT, RED_ROWS - RED_CUT, [halves_x])
            send_y(k).start()
        elif group == 2:
            send_half_y(k).wait_recv()
            add(n, 0, RED_CUT, [halves_y])
            add(n, RED_CUT, RED_ROWS - RED_CUT, [])
            send_x(k).start()
            if k == 3:
                for section in range(4):
                    @pl.when(me.pipe == section)
                    def _(section=section):
                        all_of(keep(section), lambda copy: copy.start())

                    @pl.when(me.pipe != section)
                    def _(section=section):
                        all_of(exchange(section), lambda copy: copy.start())
        else:
            send_x(k).wait_recv()
            send_y(k).wait_recv()
            add(n, 0, RED_ROWS, [from_x, from_y])
            if k < 3:
                zd = order[k]

                @pl.when(zd > z)
                def _(at=at, zd=zd):
                    @pl.when(z > 0)
                    def _():
                        send_up(at, zd).wait_recv()
                        merge(at, from_low, zd - 1)

                    send_up(at, zd).start()

                @pl.when(zd < z)
                def _(at=at, zd=zd):
                    @pl.when(z < 3)
                    def _():
                        send_down(at, zd).wait_recv()
                        merge(at, from_high, zd)

                    send_down(at, zd).start()

    def end(low, high):
        def piece(begin, size):
            part = pl.ds(begin, size)
            sums = got[15, part, :].astype(FULL)
            if low:
                sums = sums + from_low[z - 1, part, :].astype(FULL)
            if high:
                sums = sums + from_high[z, part, :].astype(FULL)
            total[part, :] = sums

        over(0, RED_ROWS, piece)

    @pl.when(z == 0)
    def _():
        send_down(15, z).wait_recv()
        end(False, True)

    @pl.when((z > 0) & (z < 3))
    def _():
        send_up(15, z).wait_recv()
        send_down(15, z).wait_recv()
        end(True, True)

    @pl.when(z == 3)
    def _():
        send_up(15, z).wait_recv()
        end(True, False)

    big_part = total.at[pl.ds(0, BIG_HALF)]
    big_join = remote(big_part, out_big.at[1], join_send.at[0], join_recv.at[0], sibling)
    small_join = remote(late_half, late.at[pl.ds(0, SMALL_HALF)], join_send.at[1], join_recv.at[1], sibling)

    @pl.when(core == 0)
    def _():
        late_half[...] = total[BIG_HALF:RED_ROWS, :].astype(LOW)
        small_join.start()
        copy = pltpu.make_async_copy(big_part, out_big.at[0], out_sem)
        copy.start()
        copy.wait()
        big_join.wait_recv()
        small_join.wait_send()

    @pl.when(core == 1)
    def _():
        big_join.start()
        late[SMALL_HALF:SMALL_ROWS, :] = total[BIG_HALF:RED_ROWS, :].astype(LOW)
        small_join.wait_recv()
        copy = pltpu.make_async_copy(late, out_small.at[me.dp], out_sem)
        copy.start()

        def late_copy(step, slot):
            target = {"dp": lax.rem(me.dp + step, 8), "pipe": me.pipe}
            return remote(late, out_small.at[slot], late_send.at[step], late_recv.at[step], target)

        for step in range(1, 8):
            late_copy(step, me.dp).start()
        copy.wait()
        for step in range(1, 8):
            late_copy(step, lax.rem(me.dp + 8 - step, 8)).wait_recv()
            late_copy(step, me.dp).wait_send()
        big_join.wait_send()

    for other in range(4):
        @pl.when(me.pipe == other)
        def _(other=other):
            all_of(keep(other), lambda copy: copy.wait())

        @pl.when(me.pipe != other)
        def _(other=other):
            all_of(exchange(other), lambda copy: copy.wait_send())
            all_of(arriving(other), lambda copy: copy.wait_recv())

    for k in range(4):
        send_half_x(k).wait_send()
        send_half_y(k).wait_send()
        send_x(k).wait_send()
        send_y(k).wait_send()
        for group in range(4):
            all_of(share(group, k), lambda copy: copy.wait_send())
    for k in range(3):
        zd, at = order[k], 12 + k

        @pl.when(zd > z)
        def _(at=at, zd=zd):
            send_up(at, zd).wait_send()

        @pl.when(zd < z)
        def _(at=at, zd=zd):
            send_down(at, zd).wait_send()


def reduce_all(big, small, wide0, wide1, final, stats):
    sem = pltpu.SemaphoreType.DMA
    vm = pltpu.VMEM
    return pl.pallas_call(
        reduce_kernel,
        name="reduce_all",
        out_shape=(
            jax.ShapeDtypeStruct((2, BIG_HALF, 128), FULL),
            jax.ShapeDtypeStruct((8, SMALL_ROWS, 128), LOW),
            jax.ShapeDtypeStruct((4,) + wide0.shape, LOW),
            jax.ShapeDtypeStruct((4,) + stats.shape[1:], FULL),
        ),
        in_specs=[any_spec()] * 6,
        out_specs=(any_spec(),) * 4,
        scratch_shapes=[
            vm((16, RED_ROWS, 128), LOW), vm((4, RED_ROWS - RED_CUT, 128), LOW), vm((4, RED_CUT, 128), LOW),
            vm((4, RED_ROWS, 128), LOW), vm((4, RED_ROWS, 128), LOW),
            vm((3, RED_ROWS, 128), LOW), vm((3, RED_ROWS, 128), LOW),
            vm((4, RED_ROWS, 128), LOW), vm((RED_ROWS, 128), FULL),
            vm((SMALL_ROWS, 128), LOW), vm((SMALL_HALF, 128), LOW),
            sem((2, 16)), sem((2, 16)),
            sem((4,)), sem((4,)), sem((4,)), sem((4,)), sem((4,)), sem((4,)), sem((4,)), sem((4,)),
            sem((3,)), sem((3,)), sem((3,)), sem((3,)),
            sem((2, 4)), sem, sem((8,)), sem((8,)), sem((2,)), sem((2,)),
            sem((4,)), sem((4,)), sem((4,)), sem((4,)),
        ],
        compiler_params=pltpu.CompilerParams(
            collective_id=1, has_side_effects=True, vmem_limit_bytes=62 << 20
        ),
    )(big.reshape(2, 8, 2, BIG_HALF, 128), small.reshape(2, 8, 2, SMALL_HALF, 128), wide0, wide1, final, stats)


def high_dot(a, b, dims=((1,), (0,))):
    return lax.dot_general(a, b, (dims, ((), ())), precision=HIGH, preferred_element_type=FULL)


def collect_kernel(owners, big, small, flat, gram, squares, tiles, low, sem):
    block, section = owners[0, lax.axis_index("dp")], lax.axis_index("pipe")
    even = lax.rem(section, 2) == 0

    @pl.when(even)
    def _():
        copy = pltpu.make_async_copy(big, tiles, sem)
        copy.start()
        copy.wait()

    @pl.when(jnp.logical_not(even))
    def _():
        low[...] = jnp.zeros_like(low)

        @pl.when(block == 0)
        def _():
            copy = pltpu.make_async_copy(small.at[0:20], low, sem)
            copy.start()
            copy.wait()

        @pl.when(block == 1)
        def _():
            copy = pltpu.make_async_copy(small.at[19:33], low.at[0:14], sem)
            copy.start()
            copy.wait()

        @pl.loop(0, WINDOW)
        def _(r):
            tiles[r] = low[r].astype(FULL)

    @pl.loop(0, WINDOW)
    def _(r):
        narrow, plain = tile_forms(section, STRIDE * block + r)
        base = TILE * r

        @pl.when(narrow)
        def _():
            for j in range(4):
                flat[pl.ds(base + j, 64, 4), :] = tiles[r, 64 * j : 64 * j + 64, :]

        @pl.when(plain)
        def _():
            flat[pl.ds(base, TILE), :] = tiles[r]

        @pl.when(jnp.logical_not(narrow | plain))
        def _():
            for j in range(16):
                flat[pl.ds(base + j, 16, 16), :] = tiles[r, 16 * j : 16 * j + 16, :]

    span = 4870
    at = lax.broadcasted_iota(jnp.int32, (TILE, 128), 0)
    first = pl.ds(0, TILE)
    flat[first, :] = jnp.where(at >= 6 * block, flat[first, :], 0.0)
    edge = TILE * (WINDOW - 1)
    last = pl.ds(edge, TILE)
    flat[last, :] = jnp.where(at + edge < span + 6 * block, flat[last, :], 0.0)
    gram[...] = jnp.zeros_like(gram)
    squares[...] = jnp.zeros_like(squares)

    @pl.loop(0, WINDOW)
    def _(r):
        part = flat[pl.ds(pl.multiple_of(TILE * r, TILE), TILE), :]
        gram[...] += high_dot(part, part, ((0,), (0,)))
        squares[...] += jnp.sum((part * part).reshape(TILE // 8, 8, 128), axis=0)


def collect(owners, big, small):
    rows = WINDOW * TILE
    return pl.pallas_call(
        collect_kernel,
        name="collect",
        out_shape=(
            jax.ShapeDtypeStruct((rows, 128), FULL),
            jax.ShapeDtypeStruct((128, 128), FULL),
            jax.ShapeDtypeStruct((8, 128), FULL),
        ),
        in_specs=[smem_spec(), any_spec(), any_spec()],
        out_specs=(vmem_spec(),) * 3,
        scratch_shapes=[
            pltpu.VMEM((WINDOW, TILE, 128), FULL), pltpu.VMEM((WINDOW, TILE, 128), LOW),
            pltpu.SemaphoreType.DMA,
        ],
        compiler_params=pltpu.CompilerParams(vmem_limit_bytes=60 << 20),
    )(owners, big.reshape(WINDOW, TILE, 128), small.reshape(USED_TILES[1], TILE, 128))


def norm_kernel(squares, norm, factor, by_pipe, by_dp, part, p_send, p_recv, d_send, d_recv):
    me = Place()
    me.enter()
    by_pipe[me.pipe] = squares[...]

    def along_pipe(step, slot):
        target = {"dp": me.dp, "pipe": lax.rem(me.pipe + step, 4)}
        return remote(squares, by_pipe.at[slot], p_send.at[step], p_recv.at[step], target)

    def along_dp(step, slot):
        target = {"dp": lax.rem(me.dp + step, 8), "pipe": me.pipe}
        return remote(part, by_dp.at[slot], d_send.at[step], d_recv.at[step], target)

    for step in range(1, 4):
        along_pipe(step, me.pipe).start()
    for step in range(1, 4):
        along_pipe(step, lax.rem(me.pipe + 4 - step, 4)).wait_recv()
    part[...] = jnp.sum(by_pipe[...], axis=0)
    by_dp[me.dp] = part[...]
    for step in range(1, 8):
        along_dp(step, me.dp).start()
    for step in range(1, 8):
        along_dp(step, lax.rem(me.dp + 8 - step, 8)).wait_recv()
    whole = jnp.sum(jnp.sum(by_dp[...], axis=0), axis=0, keepdims=True)
    length = jnp.sqrt(jnp.broadcast_to(jnp.sum(whole, axis=1, keepdims=True), (8, 128)))
    norm[...] = length
    factor[...] = jnp.minimum(1.0, CLIP_NORM / length)
    for step in range(1, 4):
        along_pipe(step, me.pipe).wait_send()
    for step in range(1, 8):
        along_dp(step, me.dp).wait_send()


def global_norm(squares):
    sem = pltpu.SemaphoreType.DMA
    shape = jax.ShapeDtypeStruct((8, 128), FULL)
    return pl.pallas_call(
        norm_kernel,
        name="global_norm",
        out_shape=(shape, shape),
        in_specs=[vmem_spec()],
        out_specs=(vmem_spec(),) * 2,
        scratch_shapes=[
            pltpu.VMEM((4, 8, 128), FULL), pltpu.VMEM((8, 8, 128), FULL), pltpu.VMEM((8, 128), FULL),
            sem((4,)), sem((4,)), sem((8,)), sem((8,)),
        ],
        compiler_params=pltpu.CompilerParams(collective_id=2, has_side_effects=True),
    )(squares)


PIECES = 7


def finish_kernel(owners, factor_ref, flat, gram_raw, gram_old, basis_old, params, moment, second,
                  clipped, moment_new, second_new, params_new, gram_new, basis_new,
                  grad, held, rotated, weights, in_sem, out_sem):
    factor = factor_ref[0:1, :]
    block = owners[0, lax.axis_index("dp")]
    span = params.shape[0]
    piece = grad.shape[0] // PIECES

    def loads(i):
        count = min(piece, span - piece * i)
        part = pl.ds(piece * i, count)
        yield pltpu.make_async_copy(
            flat.at[pl.ds(6 * block + piece * i, count)], grad.at[part], in_sem.at[0, i])
        for n, (src, dst) in enumerate(((params, weights), (moment, held), (second, rotated))):
            yield pltpu.make_async_copy(src.at[part, 0, :], dst.at[part], in_sem.at[n + 1, i])

    def stores(i):
        part = pl.ds(piece * i, min(piece, span - piece * i))
        pairs = ((grad, clipped), (held, moment_new), (rotated, second_new), (weights, params_new))
        for n, (src, dst) in enumerate(pairs):
            yield pltpu.make_async_copy(src.at[part], dst.at[part, 0, :], out_sem.at[n, i])

    for i in range(PIECES):
        for load in loads(i):
            load.start()
    old = basis_old[...]
    gram = DECAY_STATS * gram_old[...] + (1.0 - DECAY_STATS) * (gram_raw[...] * (factor * factor))
    gram_new[...] = gram
    product = high_dot(gram, old)
    rotation = product / jnp.sqrt(jnp.sum(product * product))
    for repeat in range(NS_STEPS):
        square = high_dot(rotation, rotation, ((0,), (0,)))
        rotation = 1.5 * rotation - 0.5 * high_dot(rotation, square)
    basis_new[...] = rotation
    change = high_dot(old, rotation, ((0,), (0,)))
    correction = math.sqrt(1.0 - DECAY_SECOND**STEP) / (1.0 - DECAY_FIRST**STEP)
    for i in range(PIECES):
        for load in loads(i):
            load.wait()
        part = slice(piece * i, piece * i + piece)
        clip = grad[part, :] * factor
        grad[part, :] = clip
        turned = high_dot(clip, rotation)
        first = DECAY_FIRST * high_dot(held[part, :], change) + (1.0 - DECAY_FIRST) * turned
        power = DECAY_SECOND * rotated[part, :] + (1.0 - DECAY_SECOND) * turned * turned
        held[part, :] = first
        rotated[part, :] = power
        direction = high_dot(first / (jnp.sqrt(power) + ADAM_EPS), rotation, ((1,), (1,))) * correction
        before = weights[part, :]
        weights[part, :] = before - LEARN_RATE * (direction + WEIGHT_DECAY * before)
        for store in stores(i):
            store.start()
    for i in range(PIECES):
        for store in stores(i):
            store.wait()


def finish(owners, factor, flat, gram_raw, gram_old, basis_old, params, moment, second):
    span = params.shape[1] // 128
    rows = -(-span // (8 * PIECES)) * 8 * PIECES
    flat_shape = jax.ShapeDtypeStruct((span, 1, 128), FULL)
    square = jax.ShapeDtypeStruct((128, 128), FULL)
    sem = pltpu.SemaphoreType.DMA
    outs = pl.pallas_call(
        finish_kernel,
        name="finish",
        out_shape=(flat_shape,) * 4 + (square,) * 2,
        in_specs=[smem_spec(), vmem_spec(), any_spec()] + [vmem_spec()] * 3 + [any_spec()] * 3,
        out_specs=(any_spec(),) * 4 + (vmem_spec(),) * 2,
        scratch_shapes=[pltpu.VMEM((rows, 128), FULL)] * 4 + [sem((4, PIECES)), sem((4, PIECES))],
        compiler_params=pltpu.CompilerParams(vmem_limit_bytes=60 << 20),
    )(owners, factor, flat, gram_raw, gram_old, basis_old,
      params.reshape(span, 1, 128), moment.reshape(span, 1, 128), second.reshape(span, 1, 128))
    return tuple(out.reshape(1, span * 128) for out in outs[:4]) + outs[4:]


def to_phases(teach, stud):
    def split(part):
        crops, high, across, channels = part.shape
        part = part.reshape(crops, high // 2, 2, across // 2, 2, channels).transpose(2, 4, 0, 1, 3, 5)
        return part.reshape(4, -1, channels)

    zeros = jnp.zeros((4, PADDED - ROWS, teach.shape[-1]), teach.dtype)
    return jnp.concatenate([split(teach), split(stud), zeros], axis=1)


def from_phases(phases, shape):
    crops, high, across, channels = shape
    part = phases.reshape(2, 2, crops, high // 2, across // 2, channels)
    return part.transpose(2, 3, 0, 4, 1, 5).reshape(shape)


def on_small_slice(
    teach_in,
    stud_in,
    params,
    owners,
    depth_gates,
    teach_ids,
    stud_ids,
    targets,
    moment,
    second,
    gram_stats,
    eigen_basis,
):
    phases = to_phases(teach_in[0], stud_in[0])
    big, small, ids = prepare(owners, params)
    all_big, all_small, table = gather_all(big, small, ids)
    wide_0, wide_1, final, stats, grad_x, out_big, out_small = run_step(
        table,
        depth_gates,
        teach_ids,
        stud_ids,
        all_big.reshape(2, 8, 2, WINDOW // 2, TILE, 128),
        all_small.reshape(2, USED_TILES[1], TILE, 128),
        phases,
        targets,
    )
    sum_big, sum_small, segments, stats = reduce_all(out_big, out_small, wide_0, wide_1, final, stats)
    flat, gram_raw, squares = collect(owners, sum_big, sum_small)
    norm, factor = global_norm(squares)
    clipped, moment_new, second_new, params_new, gram_new, rotation = finish(
        owners, factor, flat, gram_raw, gram_stats[0], eigen_basis[0], params, moment, second
    )
    teach_shape, stud_shape = teach_in.shape[1:], stud_in.shape[1:]
    small_teach = (teach_shape[0], teach_shape[1] // 2, teach_shape[2] // 2, C_OUT)
    small_stud = (stud_shape[0], stud_shape[1] // 2, stud_shape[2] // 2, C_OUT)
    segment_teach = segments[:, :TEACH_ROWS].reshape((4,) + small_teach)
    segment_stud = segments[:, TEACH_ROWS:ROWS].reshape((4,) + small_stud)
    stats = stats[:, 0:2]
    teach_grad = from_phases(grad_x[:, :TEACH_ROWS], teach_shape)
    stud_grad = from_phases(grad_x[:, TEACH_ROWS:ROWS], stud_shape)
    grad_norm = norm[0, 0]
    return (
        segment_teach[None],
        segment_stud[None],
        teach_grad[None],
        stud_grad[None],
        stats[None, :, None],
        grad_norm,
        clipped,
        moment_new,
        second_new,
        params_new,
        gram_new[None],
        rotation[None],
    )


def solution(mesh):
    placed = (
        P("pipe", "dp", None, None, None),
        P("pipe", "dp", None, None, None),
        P("pipe", "dp"),
        P("pipe", None),
        P(),
        P(None, "dp"),
        P(None, "dp"),
        P(),
        P("pipe", "dp"),
        P("pipe", "dp"),
        P("pipe", "dp", None),
        P("pipe", "dp", None),
    )
    small_slice = mesh.shape["dp"] == 8 and mesh.shape["pipe"] == 4
    return jax.shard_map(
        on_small_slice if small_slice else on_device,
        mesh=mesh,
        in_specs=placed,
        out_specs=(
            P("pipe", None, "dp", None, None, None),
            P("pipe", None, "dp", None, None, None),
            P("pipe", "dp", None, None, None),
            P("pipe", "dp", None, None, None),
            P("pipe", None, "dp", None, None),
            P(),
            P("pipe", "dp"),
            P("pipe", "dp"),
            P("pipe", "dp"),
            P("pipe", "dp"),
            P("pipe", "dp", None),
            P("pipe", "dp", None),
        ),
        check_vma=False,
    )
```

```python
import math

import jax
import jax.numpy as jnp
import numpy as np
from jax import lax
from jax.experimental import pallas as pl
from jax.experimental.pallas import tpu as pltpu
from jax.sharding import PartitionSpec as P

C_IN = 1024
MID = 512
C_OUT = 2048
STEP = 10
NS_STEPS = 5


HIGH = lax.Precision.HIGHEST
NORM_EPS = 1e-05
POOL_EPS = 1e-06
CLIP_NORM = 1.0
LEARN_RATE = 0.02
DECAY_FIRST = 0.9
DECAY_SECOND = 0.95
DECAY_STATS = 0.95
ADAM_EPS = 1e-08
WEIGHT_DECAY = 0.01


def section_shapes(section):
    if section == 0:
        return [
            ("first_conv", (C_IN, MID)),
            ("middle_conv", (9 * MID, MID)),
            ("skip_conv", (C_IN, C_OUT)),
            ("first_gain", (MID,)),
            ("first_bias", (MID,)),
            ("middle_gain", (MID,)),
            ("middle_bias", (MID,)),
            ("skip_gain", (C_OUT,)),
            ("skip_bias", (C_OUT,)),
        ]
    if section == 2:
        return [
            ("first_conv", (C_OUT, MID)),
            ("middle_conv", (9 * MID, MID)),
            ("first_gain", (MID,)),
            ("first_bias", (MID,)),
            ("middle_gain", (MID,)),
            ("middle_bias", (MID,)),
        ]
    return [("last_conv", (MID, C_OUT)), ("last_gain", (C_OUT,)), ("last_bias", (C_OUT,))]


def unpack(flat_vector, section):
    pieces = {}
    offset = 0
    for entry_name, entry_shape in section_shapes(section):
        entry_size = math.prod(entry_shape)
        pieces[entry_name] = flat_vector[offset : offset + entry_size].reshape(entry_shape)
        offset = offset + entry_size
    return pieces


def pack(grads, section, flat_size):
    parts = [grads[entry_name].reshape(-1) for entry_name, entry_shape in section_shapes(section)]
    used = sum((math.prod(entry_shape) for entry_name, entry_shape in section_shapes(section)))
    parts.append(jnp.zeros((flat_size - used,), jnp.float32))
    return jnp.concatenate(parts)


def as_float(vector):
    return vector.astype(jnp.float32)


def to_low(groups):
    return tuple((portion.astype(jnp.bfloat16) for portion in groups))


def to_high(groups):
    return tuple((portion.astype(jnp.float32) for portion in groups))


def point_conv(groups, weight):
    return tuple(
        (
            jnp.einsum("khwc,cd->khwd", portion, weight, preferred_element_type=jnp.float32)
            for portion in groups
        )
    )


def point_back(grad_out, groups, weight):
    low_grads = to_low(grad_out)
    grad_input = tuple(
        (
            jnp.einsum("khwd,cd->khwc", grad_part, weight, preferred_element_type=jnp.float32)
            for grad_part in low_grads
        )
    )
    grad_weight = sum(
        (
            jnp.einsum("khwc,khwd->cd", in_part, grad_part, preferred_element_type=jnp.float32)
            for in_part, grad_part in zip(groups, low_grads)
        )
    )
    return (grad_input, grad_weight)


def patches(portion, stride):
    height = portion.shape[1]
    across = portion.shape[2]
    padded = jnp.pad(portion, ((0, 0), (1, 1), (1, 1), (0, 0)))
    shifted = [
        padded[:, row_off : row_off + height : stride, col_off : col_off + across : stride, :]
        for row_off in range(3)
        for col_off in range(3)
    ]
    return jnp.concatenate(shifted, axis=-1)


def area_conv(groups, weight, stride):
    columns = tuple((patches(portion, stride) for portion in groups))
    return (point_conv(columns, weight), columns)


def unpatch(grad_cols, height, across, stride):
    channels = grad_cols.shape[-1] // 9
    padded = jnp.zeros((grad_cols.shape[0], height + 2, across + 2, channels), jnp.float32)
    for row_off in range(3):
        for col_off in range(3):
            offset = (3 * row_off + col_off) * channels
            padded = padded.at[
                :, row_off : row_off + height : stride, col_off : col_off + across : stride, :
            ].add(grad_cols[..., offset : offset + channels])
    return padded[:, 1 : height + 1, 1 : across + 1, :]


def area_back(grad_out, columns, weight, stride, in_shapes):
    grad_cols, grad_weight = point_back(grad_out, columns, weight)
    grad_input = tuple(
        (
            unpatch(grad_part, shape_item[1], shape_item[2], stride)
            for grad_part, shape_item in zip(grad_cols, in_shapes)
        )
    )
    return (grad_input, grad_weight)


def batch_norm(groups, gain, bias):
    rows_total = sum((portion.shape[0] * portion.shape[1] * portion.shape[2] for portion in groups))
    centre = sum((jnp.sum(portion, axis=(0, 1, 2)) for portion in groups)) / rows_total
    spread = (
        sum((jnp.sum(jnp.square(portion - centre), axis=(0, 1, 2)) for portion in groups))
        / rows_total
    )
    inverse = lax.rsqrt(spread + NORM_EPS)
    standard = tuple(((portion - centre) * inverse for portion in groups))
    normed = tuple((gain * std_part + bias for std_part in standard))
    return (normed, (centre, spread, inverse, standard))


def norm_back(grad_out, gain, saved):
    centre, spread, inverse, standard = saved
    rows_total = sum(
        (portion.shape[0] * portion.shape[1] * portion.shape[2] for portion in standard)
    )
    grad_sum = sum((jnp.sum(grad_part, axis=(0, 1, 2)) for grad_part in grad_out))
    grad_dot = sum(
        (
            jnp.sum(grad_part * std_part, axis=(0, 1, 2))
            for grad_part, std_part in zip(grad_out, standard)
        )
    )
    grad_input = tuple(
        (
            gain
            * inverse
            * (grad_part - grad_sum / rows_total - std_part * (grad_dot / rows_total))
            for grad_part, std_part in zip(grad_out, standard)
        )
    )
    return (grad_input, grad_dot, grad_sum)


def through_softplus(grad_out, pre_values):
    return tuple(
        (grad_part * jax.nn.sigmoid(pre_part) for grad_part, pre_part in zip(grad_out, pre_values))
    )


def front_forward(pieces, inputs):
    first = point_conv(inputs, pieces["first_conv"])
    normed_a, saved_a = batch_norm(
        first, as_float(pieces["first_gain"]), as_float(pieces["first_bias"])
    )
    hidden = tuple((jax.nn.softplus(portion).astype(jnp.bfloat16) for portion in normed_a))
    middle, columns = area_conv(hidden, pieces["middle_conv"], 2)
    normed_b, saved_b = batch_norm(
        middle, as_float(pieces["middle_gain"]), as_float(pieces["middle_bias"])
    )
    narrow = tuple((jax.nn.softplus(portion) for portion in normed_b))
    reduced = tuple((portion[:, ::2, ::2, :] for portion in inputs))
    skipped = point_conv(reduced, pieces["skip_conv"])
    wide, saved_p = batch_norm(
        skipped, as_float(pieces["skip_gain"]), as_float(pieces["skip_bias"])
    )
    norm_rows = jnp.stack(
        [
            jnp.concatenate([saved_a[0], saved_b[0], saved_p[0]]),
            jnp.concatenate([saved_a[1], saved_b[1], saved_p[1]]),
        ]
    )
    kept = (normed_a, hidden, columns, normed_b, reduced, saved_a, saved_b, saved_p)
    return (wide, narrow, norm_rows, kept)


def front_backward(pieces, inputs, grad_wide, grad_narrow):
    wide, narrow, norm_rows, kept = front_forward(pieces, inputs)
    normed_a, hidden, columns, normed_b, reduced, saved_a, saved_b, saved_p = kept
    grads = {}
    grad_pre_b = through_softplus(grad_narrow, normed_b)
    grad_mid, grads["middle_gain"], grads["middle_bias"] = norm_back(
        grad_pre_b, as_float(pieces["middle_gain"]), saved_b
    )
    grad_hidden, grads["middle_conv"] = area_back(
        grad_mid, columns, pieces["middle_conv"], 2, [portion.shape for portion in hidden]
    )
    grad_pre_a = through_softplus(grad_hidden, normed_a)
    grad_first, grads["first_gain"], grads["first_bias"] = norm_back(
        grad_pre_a, as_float(pieces["first_gain"]), saved_a
    )
    grad_inputs, grads["first_conv"] = point_back(grad_first, inputs, pieces["first_conv"])
    grad_skip, grads["skip_gain"], grads["skip_bias"] = norm_back(
        grad_wide, as_float(pieces["skip_gain"]), saved_p
    )
    grad_reduced, grads["skip_conv"] = point_back(grad_skip, reduced, pieces["skip_conv"])
    grad_inputs = tuple(
        (
            full_part.at[:, ::2, ::2, :].add(part_reduced)
            for full_part, part_reduced in zip(grad_inputs, grad_reduced)
        )
    )
    return (grad_inputs, grads)


def join_forward(pieces, wide, narrow):
    last = point_conv(narrow, pieces["last_conv"])
    normed, saved = batch_norm(last, as_float(pieces["last_gain"]), as_float(pieces["last_bias"]))
    pre_values = tuple(
        (
            skip_part.astype(jnp.float32) + branch_part
            for skip_part, branch_part in zip(wide, normed)
        )
    )
    ending = tuple((jax.nn.softplus(pre_part) for pre_part in pre_values))
    filler = jnp.zeros((2 * MID,), jnp.float32)
    norm_rows = jnp.stack(
        [jnp.concatenate([saved[0], filler]), jnp.concatenate([saved[1], filler])]
    )
    return (ending, norm_rows, (pre_values, saved))


def join_grads(pieces, narrow, kept, grad_out, gate):
    pre_values, saved = kept
    grad_pre = tuple(
        (
            grad_part * jax.nn.sigmoid(pre_part) * gate
            for grad_part, pre_part in zip(grad_out, pre_values)
        )
    )
    grad_wide = tuple(
        (pre_grad + grad_part * (1.0 - gate) for pre_grad, grad_part in zip(grad_pre, grad_out))
    )
    grad_last, gain_grad, bias_grad = norm_back(grad_pre, as_float(pieces["last_gain"]), saved)
    grad_narrow, weight_grad = point_back(grad_last, narrow, pieces["last_conv"])
    grads = {"last_conv": weight_grad, "last_gain": gain_grad, "last_bias": bias_grad}
    return (grad_wide, grad_narrow, grads)


def split_forward(pieces, wide):
    first = point_conv(wide, pieces["first_conv"])
    normed_a, saved_a = batch_norm(
        first, as_float(pieces["first_gain"]), as_float(pieces["first_bias"])
    )
    hidden = tuple((jax.nn.softplus(portion).astype(jnp.bfloat16) for portion in normed_a))
    middle, columns = area_conv(hidden, pieces["middle_conv"], 1)
    normed_b, saved_b = batch_norm(
        middle, as_float(pieces["middle_gain"]), as_float(pieces["middle_bias"])
    )
    narrow = tuple((jax.nn.softplus(portion) for portion in normed_b))
    filler = jnp.zeros((C_OUT,), jnp.float32)
    norm_rows = jnp.stack(
        [
            jnp.concatenate([saved_a[0], saved_b[0], filler]),
            jnp.concatenate([saved_a[1], saved_b[1], filler]),
        ]
    )
    return (narrow, norm_rows, (normed_a, hidden, columns, normed_b, saved_a, saved_b))


def split_backward(pieces, wide, grad_relay, grad_narrow):
    narrow, norm_rows, kept = split_forward(pieces, wide)
    normed_a, hidden, columns, normed_b, saved_a, saved_b = kept
    grads = {}
    grad_pre_b = through_softplus(grad_narrow, normed_b)
    grad_mid, grads["middle_gain"], grads["middle_bias"] = norm_back(
        grad_pre_b, as_float(pieces["middle_gain"]), saved_b
    )
    grad_hidden, grads["middle_conv"] = area_back(
        grad_mid, columns, pieces["middle_conv"], 1, [portion.shape for portion in hidden]
    )
    grad_pre_a = through_softplus(grad_hidden, normed_a)
    grad_first, grads["first_gain"], grads["first_bias"] = norm_back(
        grad_pre_a, as_float(pieces["first_gain"]), saved_a
    )
    grad_conv_in, grads["first_conv"] = point_back(grad_first, wide, pieces["first_conv"])
    grad_wide = tuple(
        (relay_part + conv_part for relay_part, conv_part in zip(grad_relay, grad_conv_in))
    )
    return (grad_wide, grads)


def pool_grad(final, targets, picks):
    result = []
    for portion, pick_ids in zip(final, picks):
        cubes = jnp.mean(portion * portion * portion, axis=(1, 2)) + POOL_EPS
        factor = jnp.exp(jnp.log(cubes) * (-2.0 / 3.0)) * targets[pick_ids]
        result.append(factor[:, None, None, :] * portion * portion)
    return tuple(result)


def used_size(section):
    return sum((math.prod(entry_shape) for entry_name, entry_shape in section_shapes(section)))


def batch_pass(reals, inputs, gate, targets, picks):
    pieces = [unpack(reals[section], section) for section in range(4)]
    wide_f, narrow_f, rows_0, _ = front_forward(pieces[0], inputs)
    wide_0, narrow_0 = to_low(wide_f), to_low(narrow_f)
    ending_1, rows_1, kept_1 = join_forward(pieces[1], wide_0, narrow_0)
    wide_1 = to_low(ending_1)
    narrow_f, rows_2, _ = split_forward(pieces[2], wide_1)
    narrow_2 = to_low(narrow_f)
    ending_3, rows_3, kept_3 = join_forward(pieces[3], wide_1, narrow_2)
    final = tuple(
        (
            jnp.where(gate > 0, end_part, relay_part.astype(jnp.float32))
            for end_part, relay_part in zip(ending_3, wide_1)
        )
    )
    cotangent = pool_grad(final, targets, picks)
    grad_wide, grad_narrow, grads_3 = join_grads(pieces[3], narrow_2, kept_3, cotangent, gate)
    grad_wide, grads_2 = split_backward(
        pieces[2], wide_1, to_high(to_low(grad_wide)), to_high(to_low(grad_narrow))
    )
    grad_wide, grad_narrow, grads_1 = join_grads(
        pieces[1], narrow_0, kept_1, to_high(to_low(grad_wide)), 1.0
    )
    grad_inputs, grads_0 = front_backward(
        pieces[0], inputs, to_high(to_low(grad_wide)), to_high(to_low(grad_narrow))
    )
    outs = (wide_0, wide_1, wide_1, to_low(final))
    stats = jnp.stack([rows_0, rows_1, rows_2 * gate, rows_3 * gate])
    return (outs, stats, to_low(grad_inputs), (grads_0, grads_1, grads_2, grads_3))


def on_device(
    teach_in,
    stud_in,
    params,
    owners,
    depth_gates,
    teach_ids,
    stud_ids,
    targets,
    moment,
    second,
    gram_stats,
    eigen_basis,
):
    sections = lax.axis_size("pipe")
    rank = lax.axis_index("pipe")
    owner_count = lax.axis_size("dp")
    span_size = params.shape[1]
    flat_size = span_size * owner_count
    owner_rows = lax.all_gather(owners, "pipe", axis=0, tiled=True)
    gathered = lax.all_gather(params[0].astype(jnp.bfloat16), ("pipe", "dp"), axis=0)
    gathered = gathered.reshape(sections, owner_count, span_size)
    reals = []
    for section in range(sections):
        inverse = jnp.argsort(owner_rows[section]).astype(jnp.int32)
        blocks = -(-used_size(section) // span_size)
        reals.append(gathered[section][inverse[:blocks]].reshape(blocks * span_size))
    inputs = (teach_in[0], stud_in[0])
    gate = depth_gates[rank].astype(jnp.float32)
    outs, stats, (teach_grad, stud_grad), grads = batch_pass(
        reals, inputs, gate, targets, (teach_ids[rank], stud_ids[rank])
    )
    segment_teach = lax.all_to_all(
        jnp.stack([part[0] for part in outs]), "pipe", split_axis=0, concat_axis=0, tiled=True
    )
    segment_stud = lax.all_to_all(
        jnp.stack([part[1] for part in outs]), "pipe", split_axis=0, concat_axis=0, tiled=True
    )
    stats = lax.all_to_all(stats, "pipe", split_axis=0, concat_axis=0, tiled=True)
    rows = []
    for section in range(sections):
        flat = pack(grads[section], section, flat_size).reshape(owner_count, span_size)
        rows.append(flat[owner_rows[section]])
    span_total = lax.psum_scatter(
        jnp.stack(rows).reshape(sections * owner_count, span_size),
        ("pipe", "dp"),
        scatter_dimension=0,
        tiled=True,
    ).reshape(span_size)
    total_squares = lax.psum(jnp.sum(span_total * span_total), ("dp", "pipe"))
    grad_norm = jnp.sqrt(total_squares)
    factor = jnp.minimum(1.0, CLIP_NORM / grad_norm)
    clipped = span_total * factor
    matrix = clipped.reshape(span_size // 128, 128)
    gram_old = gram_stats[0]
    basis_old = eigen_basis[0]
    gram_new = DECAY_STATS * gram_old + (1.0 - DECAY_STATS) * jnp.dot(
        matrix.T, matrix, precision=HIGH
    )
    product = jnp.dot(gram_new, basis_old, precision=HIGH)
    rotation = product / jnp.sqrt(jnp.sum(product * product))
    for repeat in range(NS_STEPS):
        square = jnp.dot(rotation.T, rotation, precision=HIGH)
        rotation = 1.5 * rotation - 0.5 * jnp.dot(rotation, square, precision=HIGH)
    moment_old = moment.reshape(span_size // 128, 128)
    initial = jnp.dot(moment_old, basis_old.T, precision=HIGH)
    blended = DECAY_FIRST * initial + (1.0 - DECAY_FIRST) * matrix
    moment_new = jnp.dot(blended, rotation, precision=HIGH)
    rotated = jnp.dot(matrix, rotation, precision=HIGH)
    second_new = (
        DECAY_SECOND * second.reshape(span_size // 128, 128)
        + (1.0 - DECAY_SECOND) * rotated * rotated
    )
    correction = math.sqrt(1.0 - DECAY_SECOND**STEP) / (1.0 - DECAY_FIRST**STEP)
    direction = (
        jnp.dot(moment_new / (jnp.sqrt(second_new) + ADAM_EPS), rotation.T, precision=HIGH)
        * correction
    )
    weights = params.reshape(span_size // 128, 128)
    params_new = weights - LEARN_RATE * (direction + WEIGHT_DECAY * weights)
    return (
        segment_teach[None],
        segment_stud[None],
        teach_grad[None],
        stud_grad[None],
        stats[None, :, None],
        grad_norm,
        clipped.reshape(1, span_size),
        moment_new.reshape(1, span_size),
        second_new.reshape(1, span_size),
        params_new.reshape(1, span_size),
        gram_new[None],
        rotation[None],
    )


MESH = pl.DeviceIdType.MESH
LOW = jnp.bfloat16
FULL = jnp.float32
TILE = 256
WINDOW = 20
STRIDE = 19
VEC_TILE = (152, 32, 104, 32)
USED_TILES = (153, 33, 105, 33)
FRONT_WIDE = 88
SMALL_ROWS = 1056
ROWS = 120
PADDED = 128
TEACH_ROWS = 72


def any_spec():
    return pl.BlockSpec(memory_space=pl.ANY)


def smem_spec():
    return pl.BlockSpec(memory_space=pltpu.SMEM)


def vmem_spec():
    return pl.BlockSpec(memory_space=pltpu.VMEM)


def tile_forms(section, tile):
    even = lax.rem(section, 2) == 0
    vector = jnp.where(section == 0, 152, jnp.where(section == 2, 104, 32))
    narrow_end = jnp.where(section == 0, FRONT_WIDE, jnp.where(section == 2, 104, 0))
    narrow = even & (tile < narrow_end)
    plain = tile == vector
    return narrow, plain


def prepare_kernel(owners, params, big, small, ids, flat, sem):
    block, section = owners[0, lax.axis_index("dp")], lax.axis_index("pipe")

    @pl.loop(0, WINDOW)
    def _(r):
        flat[pl.ds(TILE * r, TILE)] = jnp.zeros((TILE, 128), FULL)

    copy = pltpu.make_async_copy(params.at[:, 0, :], flat.at[pl.ds(6 * block, params.shape[0])], sem)
    copy.start()

    @pl.loop(0, small.shape[0])
    def _(r):
        small[r] = jnp.zeros((TILE, 128), LOW)

    lane = lax.broadcasted_iota(jnp.int32, (8, 128), 1)
    row = jnp.zeros((8, 128), jnp.int32)
    for j in range(8):
        row = jnp.where(lane == j, owners[0, j], row)
    ids[...] = row
    copy.wait()

    @pl.loop(0, WINDOW)
    def _(r):
        tile = STRIDE * block + r
        narrow, plain = tile_forms(section, tile)
        base = TILE * r

        @pl.when(narrow)
        def _():
            for j in range(4):
                big[r, 64 * j : 64 * j + 64, :] = flat[pl.ds(base + j, 64, 4), :].astype(LOW)

        @pl.when(plain)
        def _():
            big[r] = flat[pl.ds(base, TILE), :].astype(LOW)

        @pl.when(jnp.logical_not(narrow | plain))
        def _():
            for j in range(16):
                big[r, 16 * j : 16 * j + 16, :] = flat[pl.ds(base + j, 16, 16), :].astype(LOW)

        @pl.when(tile < small.shape[0])
        def _():
            small[tile] = big[r]


def prepare(owners, params):
    return pl.pallas_call(
        prepare_kernel,
        name="prepare",
        out_shape=(
            jax.ShapeDtypeStruct((WINDOW, TILE, 128), LOW),
            jax.ShapeDtypeStruct((USED_TILES[1], TILE, 128), LOW),
            jax.ShapeDtypeStruct((8, 128), jnp.int32),
        ),
        in_specs=[smem_spec(), any_spec()],
        out_specs=(vmem_spec(),) * 3,
        scratch_shapes=[pltpu.VMEM((WINDOW * TILE, 128), FULL), pltpu.SemaphoreType.DMA],
        compiler_params=pltpu.CompilerParams(vmem_limit_bytes=60 << 20),
    )(owners, params.reshape(-1, 1, 128))


class Place:
    def __init__(self):
        self.dp = lax.axis_index("dp")
        self.pipe = lax.axis_index("pipe")
        self.x, self.core = self.pipe // 2, self.pipe % 2
        self.z, self.y = self.dp // 2, self.dp % 2

    def device(self, x=None, core=None, z=None, y=None):
        x = self.x if x is None else x
        core = self.core if core is None else core
        z = self.z if z is None else z
        y = self.y if y is None else y
        return {"dp": 2 * z + y, "pipe": 2 * x + core}

    def enter(self):
        barrier = pltpu.get_barrier_semaphore()
        for step in range(1, 8):
            other = lax.rem(self.dp + step, 8)
            pl.semaphore_signal(
                barrier, inc=1, device_id={"dp": other, "pipe": self.pipe}, device_id_type=MESH
            )
        for step in range(1, 4):
            other = lax.rem(self.pipe + step, 4)
            pl.semaphore_signal(
                barrier, inc=1, device_id={"dp": self.dp, "pipe": other}, device_id_type=MESH
            )
        pl.semaphore_wait(barrier, 10)


def remote(src, dst, send, recv, target):
    return pltpu.make_async_remote_copy(
        src_ref=src, dst_ref=dst, send_sem=send, recv_sem=recv, device_id=target, device_id_type=MESH
    )


BIG_HALF = WINDOW * TILE // 2
SMALL_HALF = SMALL_ROWS // 2
BULK_CUT = 1056
LIGHT_CUT = 256


def gather_kernel(big, small, ids, all_big, all_small, table, early, chunk, early_send, early_recv,
                  z_send, z_recv, x_send, x_recv, y_send, y_recv, dx_send, dx_recv, dy_send, dy_recv,
                  s_send, s_recv, first_send, first_recv, own_sem, id_send, id_recv, lz_send, lz_recv):
    me = Place()
    me.enter()
    x, y, z, core = me.x, me.y, me.z, me.core
    up, down = me.device(z=z + 1), me.device(z=z - 1)
    x_side, y_side, sibling = me.device(x=1 - x), me.device(y=1 - y), me.device(core=1 - core)

    class Stream:
        def __init__(self, n, out, cut):
            self.n, self.out, self.cut, self.rows = n, out, cut, out.shape[3]

        def block(self, xo, origin, yo):
            return self.out.at[xo, 2 * origin + yo, core]

        def move_x(self, origin):
            block = self.block(x, origin, y)
            return remote(block, block, x_send.at[self.n, origin], x_recv.at[self.n, origin], x_side)

        def move_y(self, origin):
            block = self.block(x, origin, y)
            return remote(block, block, y_send.at[self.n, origin], y_recv.at[self.n, origin], y_side)

        def share(self, xo, origin, yo):
            block = self.block(xo, origin, yo)
            at = 8 * xo + 2 * origin + yo
            return remote(block, block, s_send.at[self.n, at], s_recv.at[self.n, at], sibling)

        def move_z(self, origin, target, way):
            block = self.block(x, origin, y)
            return remote(block, block, z_send.at[self.n, way, origin], z_recv.at[self.n, origin], target)

        def half_x(self, origin, xo, yo):
            part = self.out.at[xo, 2 * origin + yo, core, pl.ds(self.cut, self.rows - self.cut)]
            return remote(part, part, dx_send.at[self.n, origin], dx_recv.at[self.n, origin], x_side)

        def half_y(self, origin, xo, yo):
            part = self.out.at[xo, 2 * origin + yo, core, pl.ds(0, self.cut)]
            return remote(part, part, dy_send.at[self.n, origin], dy_recv.at[self.n, origin], y_side)

        def spread(self, origin):
            self.move_x(origin).start()
            self.move_y(origin).start()
            self.share(x, origin, y).start()

        def from_sides(self, origin):
            self.move_x(origin).wait_recv()
            self.half_y(origin, 1 - x, y).start()
            self.share(1 - x, origin, y).start()
            self.move_y(origin).wait_recv()
            self.half_x(origin, x, 1 - y).start()
            self.share(x, origin, 1 - y).start()

        def from_diagonal(self, origin):
            self.half_x(origin, 1 - x, 1 - y).wait_recv()
            self.half_y(origin, 1 - x, 1 - y).wait_recv()
            self.share(1 - x, origin, 1 - y).start()

        def each(self, step, action):
            if step == 0:
                action(z)
            else:
                pl.when(z >= step)(lambda: action(z - step))
                pl.when(z + step <= 3)(lambda: action(z + step))

        def step(self, k):
            if k == 0:
                pl.when(z < 3)(lambda: self.move_z(z, up, 0).start())
                pl.when(z > 0)(lambda: self.move_z(z, down, 1).start())
                self.spread(z)
            elif k < 4:

                @pl.when(z >= k)
                def _():
                    self.move_z(z - k, up, 0).wait_recv()
                    pl.when(z < 3)(lambda: self.move_z(z - k, up, 0).start())
                    self.spread(z - k)

                @pl.when(z + k <= 3)
                def _():
                    self.move_z(z + k, down, 1).wait_recv()
                    pl.when(z > 0)(lambda: self.move_z(z + k, down, 1).start())
                    self.spread(z + k)

            if 1 <= k < 5:
                self.each(k - 1, self.from_sides)
            if k >= 2:
                self.each(k - 2, self.from_diagonal)

        def close(self):
            for origin in range(4):
                self.move_x(origin).wait_send()
                self.move_y(origin).wait_send()
                self.half_x(origin, x, 1 - y).wait_send()
                self.half_y(origin, 1 - x, y).wait_send()
                pl.when((z < 3) & (origin <= z))(lambda: self.move_z(origin, up, 0).wait_send())
                pl.when((z > 0) & (origin >= z))(lambda: self.move_z(origin, down, 1).wait_send())
            self.close_shares()

        def close_shares(self):
            for origin in range(4):
                for xo in range(2):
                    for yo in range(2):
                        self.share(xo, origin, yo).wait_send()
                        theirs = self.out.at[xo, 2 * origin + yo, 1 - core]
                        at = 8 * xo + 2 * origin + yo
                        remote(theirs, theirs, s_send.at[self.n, at], s_recv.at[self.n, at], sibling).wait_recv()

    class Late(Stream):
        def column_z(self, xo, origin, yo, target, way):
            block = self.block(xo, origin, yo)
            at = 2 * xo + yo
            return remote(
                block, block, lz_send.at[way, at, origin], lz_recv.at[at, origin], target
            )

        def leave(self, xo, yo):
            pl.when(z < 3)(lambda: self.column_z(xo, z, yo, up, 0).start())
            pl.when(z > 0)(lambda: self.column_z(xo, z, yo, down, 1).start())
            self.share(xo, z, yo).start()

        def step(self, k):
            if k == 0:
                self.move_x(z).start()
                self.move_y(z).start()
                self.leave(x, y)
            elif k == 1:
                self.move_x(z).wait_recv()
                self.half_y(z, 1 - x, y).start()
                self.leave(1 - x, y)
                self.move_y(z).wait_recv()
                self.half_x(z, x, 1 - y).start()
                self.leave(x, 1 - y)
            elif k == 2:
                self.half_x(z, 1 - x, 1 - y).wait_recv()
                self.half_y(z, 1 - x, 1 - y).wait_recv()
                self.leave(1 - x, 1 - y)
            else:
                gap = k - 2

                @pl.when(z >= gap)
                def _():
                    for xo, yo in columns:
                        self.column_z(xo, z - gap, yo, up, 0).wait_recv()
                        pl.when(z < 3)(lambda: self.column_z(xo, z - gap, yo, up, 0).start())
                        self.share(xo, z - gap, yo).start()

                @pl.when(z + gap <= 3)
                def _():
                    for xo, yo in columns:
                        self.column_z(xo, z + gap, yo, down, 1).wait_recv()
                        pl.when(z > 0)(lambda: self.column_z(xo, z + gap, yo, down, 1).start())
                        self.share(xo, z + gap, yo).start()

        def close(self):
            self.move_x(z).wait_send()
            self.move_y(z).wait_send()
            self.half_x(z, x, 1 - y).wait_send()
            self.half_y(z, 1 - x, y).wait_send()
            for origin in range(4):
                for xo, yo in columns:
                    pl.when((z < 3) & (origin <= z))(
                        lambda: self.column_z(xo, origin, yo, up, 0).wait_send())
                    pl.when((z > 0) & (origin >= z))(
                        lambda: self.column_z(xo, origin, yo, down, 1).wait_send())
            self.close_shares()

    columns = ((x, y), (1 - x, y), (x, 1 - y), (1 - x, 1 - y))
    bulk = Stream(0, all_big, BULK_CUT)
    light = Late(1, all_small, LIGHT_CUT)

    def early_copy(step):
        target = lax.rem(me.dp + step, 8)
        return remote(
            small.at[target], early.at[step], early_send.at[step], early_recv.at[step],
            {"dp": target, "pipe": me.pipe},
        )

    big_half = all_big.at[x, me.dp, 1]
    big_first = remote(big.at[pl.ds(BIG_HALF, BIG_HALF)], big_half, first_send.at[0], first_recv.at[0], sibling)
    small_half = all_small.at[x, me.dp, 0]
    small_first = remote(chunk.at[pl.ds(0, SMALL_HALF)], small_half, first_send.at[1], first_recv.at[1], sibling)

    @pl.when(core == 0)
    def _():
        big_first.start()
        copy = pltpu.make_async_copy(big.at[pl.ds(0, BIG_HALF)], all_big.at[x, me.dp, 0], own_sem.at[0])
        copy.start()
        copy.wait()

    @pl.when(core == 1)
    def _():
        for step in range(1, 8):
            early_copy(step).start()
        pltpu.make_async_copy(small.at[me.dp], early.at[0], own_sem.at[1]).start()
        big_first.wait_recv()

    bulk.step(0)
    row = pltpu.make_async_copy(ids, table.at[me.pipe], own_sem.at[2])
    row.start()
    for step in range(1, 4):
        remote(
            ids, table.at[me.pipe], id_send.at[step], id_recv.at[step],
            {"dp": me.dp, "pipe": lax.rem(me.pipe + step, 4)},
        ).start()

    @pl.when(core == 0)
    def _():
        small_first.wait_recv()

    @pl.when(core == 1)
    def _():
        pltpu.make_async_copy(small.at[me.dp], early.at[0], own_sem.at[1]).wait()
        for step in range(1, 8):
            early_copy(step).wait()

        @pl.loop(0, 6)
        def _(i):
            part = pl.ds(pl.multiple_of(176 * i, 16), 176)
            total = early[0, part, :].astype(FULL)
            for step in range(1, 8):
                total = total + early[step, part, :].astype(FULL)
            chunk[part, :] = total.astype(LOW)

        small_first.start()
        copy = pltpu.make_async_copy(chunk.at[pl.ds(SMALL_HALF, SMALL_HALF)], all_small.at[x, me.dp, 1], own_sem.at[0])
        copy.start()
        copy.wait()

    light.step(0)
    for k in range(1, 6):
        bulk.step(k)
        light.step(k)
    bulk.close()
    light.close()
    row.wait()
    for step in range(1, 4):
        here = lax.rem(me.pipe + 4 - step, 4)
        move = remote(
            ids, table.at[here], id_send.at[step], id_recv.at[step],
            {"dp": me.dp, "pipe": lax.rem(me.pipe + step, 4)},
        )
        move.wait_recv()
        move.wait_send()

    @pl.when(core == 0)
    def _():
        big_first.wait_send()

    @pl.when(core == 1)
    def _():
        small_first.wait_send()


def gather_all(big, small, ids):
    sem = pltpu.SemaphoreType.DMA
    return pl.pallas_call(
        gather_kernel,
        name="gather_all",
        out_shape=(
            jax.ShapeDtypeStruct((2, 8, 2, BIG_HALF, 128), LOW),
            jax.ShapeDtypeStruct((2, 8, 2, SMALL_HALF, 128), LOW),
            jax.ShapeDtypeStruct((4, 8, 128), jnp.int32),
        ),
        in_specs=[any_spec()] * 3,
        out_specs=(any_spec(),) * 3,
        scratch_shapes=[
            pltpu.VMEM((8, SMALL_ROWS, 128), LOW),
            pltpu.VMEM((SMALL_ROWS, 128), LOW),
            sem((8,)), sem((8,)),
            sem((2, 2, 4)), sem((2, 4)),
            sem((2, 4)), sem((2, 4)), sem((2, 4)), sem((2, 4)),
            sem((2, 4)), sem((2, 4)), sem((2, 4)), sem((2, 4)),
            sem((2, 16)), sem((2, 16)),
            sem((2,)), sem((2,)), sem((3,)), sem((4,)), sem((4,)), sem((2, 4, 4)), sem((4, 4)),
        ],
        compiler_params=pltpu.CompilerParams(
            collective_id=0, has_side_effects=True, vmem_limit_bytes=60 << 20
        ),
    )(big.reshape(WINDOW * TILE, 128), small.reshape(8, SMALL_ROWS, 128), ids)


def soft(value):
    return jnp.maximum(value, 0.0) + jnp.log1p(jnp.exp(-jnp.abs(value)))


def gate_of(value):
    small = jnp.exp(-jnp.abs(value))
    share = 1.0 / (1.0 + small)
    return jnp.where(value >= 0, share, small * share)


def standardize(z):
    count = z.shape[0]
    centre = jnp.sum(z, axis=0, keepdims=True) / count
    away = z - centre
    spread = jnp.sum(away * away, axis=0, keepdims=True) / count
    inverse = lax.rsqrt(spread + NORM_EPS)
    return away * inverse, centre, spread, inverse


def unstandardize(grad, standard, gain, inverse):
    count = grad.shape[0]
    grad_sum = jnp.sum(grad, axis=0, keepdims=True)
    grad_dot = jnp.sum(grad * standard, axis=0, keepdims=True)
    result = gain * inverse * (grad - grad_sum / count - standard * (grad_dot / count))
    return result, grad_dot, grad_sum


def pad_low(value):
    zeros = jnp.zeros((PADDED - ROWS, value.shape[1]), FULL)
    return jnp.concatenate([value, zeros], axis=0).astype(LOW)


def mul(a, b):
    return jnp.dot(a, b, preferred_element_type=FULL)


def mul_t(a, b):
    return lax.dot_general(a, b, (((1,), (1,)), ((), ())), preferred_element_type=FULL)


def narrow_part(ref, start, count, blocks=range(4)):
    return jnp.concatenate(
        [ref[pl.ds(start, count), 64 * j : 64 * j + 64, :].reshape(64 * count, 128) for j in blocks],
        axis=1,
    )


def put_narrow(ref, start, count, value):
    for j in range(4):
        ref[pl.ds(start, count), 64 * j : 64 * j + 64, :] = (
            value[:, 128 * j : 128 * j + 128].astype(LOW).reshape(count, 64, 128)
        )


def wide_part(ref, start, count, c):
    return jnp.concatenate(
        [
            ref[start : start + count, pl.ds(pl.multiple_of(32 * c + 16 * h, 16), 16), :].reshape(
                16 * count, 128
            )
            for h in range(2)
        ],
        axis=1,
    )


def put_wide(ref, start, count, c, value):
    for h in range(2):
        ref[start : start + count, pl.ds(pl.multiple_of(32 * c + 16 * h, 16), 16), :] = (
            value[:, 128 * h : 128 * h + 128].astype(LOW).reshape(count, 16, 128)
        )


def step_kernel(table, gates, teach_ids, stud_ids, all_big, all_small, x, targets, grid,
                wide0, wide1, final, stats, grad_x, out_big, out_small,
                w0, w1, w2, w3, edges, vec, grad_vec, raw,
                std_a, std_b, std_p, std_1, std_c, std_d, hidden, cols0, cols2,
                nar0, nar2, turned, relay, dz_a, dz_n, acc, acc_x, grad_h,
                wanted, inv, in_sem, edge_sem, out_sem):
    rank = lax.axis_index("pipe")
    gate = gates[rank].astype(FULL)
    for group in range(2):
        for j in range(8):
            inv[8 * group + table[2 * group, 0, j]] = j
    picks = [teach_ids[rank, k] for k in range(2)] + [stud_ids[rank, k] for k in range(3)]
    rows = [
        pltpu.make_async_copy(targets.at[pl.ds(pick, 1)], wanted.at[pl.ds(k, 1)], edge_sem.at[12 + k])
        for k, pick in enumerate(picks)
    ]
    for fetched in rows:
        fetched.start()
    weights = (w0, w1, w2, w3)
    loads = {0: [], 1: [], 2: [], 3: []}
    for group, weight, blocks in ((0, w0, 8), (1, w2, 6)):
        for b in range(blocks):
            first, here = 19 * b, inv[8 * group + b]
            at = 8 * group + b
            loads[2 * group].append(pltpu.make_async_copy(
                all_big.at[group, here, 0], weight.at[pl.ds(first, 10)], in_sem.at[0, at]))
            if first + 10 < USED_TILES[2 * group]:
                count = 10 if b == 7 else 9
                loads[2 * group].append(pltpu.make_async_copy(
                    all_big.at[group, here, 1, pl.ds(0, count)], weight.at[pl.ds(first + 10, count)],
                    in_sem.at[1, at]))
            if b < blocks - 1:
                at = 7 * group + b
                loads[2 * group].append(pltpu.make_async_copy(
                    all_big.at[group, here, 1, pl.ds(9, 1)], edges.at[pl.ds(at, 1)], edge_sem.at[at]))
    loads[1].append(pltpu.make_async_copy(all_small.at[0], w1, in_sem.at[0, 14]))
    loads[3].append(pltpu.make_async_copy(all_small.at[1], w3, in_sem.at[0, 15]))
    for section in range(4):
        for load in loads[section]:
            load.start()

    raw[...] = jnp.zeros_like(raw)
    grad_vec[...] = jnp.zeros_like(grad_vec)

    def settle(section):
        for load in loads[section]:
            load.wait()
        if section == 0:
            for b in range(7):
                w0[19 * b + 19] = (w0[19 * b + 19].astype(FULL) + edges[b].astype(FULL)).astype(LOW)
        if section == 2:
            for b in range(5):
                w2[19 * b + 19] = (
                    w2[19 * b + 19].astype(FULL) + edges[7 + b].astype(FULL)
                ).astype(LOW)
        vec[section] = weights[section][VEC_TILE[section], 0:48, :].astype(FULL)

    def row(section, start):
        return jnp.concatenate(
            [vec[section, pl.ds(start + h, 1), :] for h in range(2)], axis=1
        )

    def put_row(section, start, value):
        for h in range(2):
            grad_vec[section, pl.ds(start + h, 1), :] = value[:, 128 * h : 128 * h + 128]

    def put_stats(section, column, centre, spread):
        raw[2 * section : 2 * section + 1, pl.ds(column, 256)] = centre
        raw[2 * section + 1 : 2 * section + 2, pl.ds(column, 256)] = spread

    def inverse_of(section, column):
        return lax.rsqrt(raw[2 * section + 1 : 2 * section + 2, pl.ds(column, 256)] + NORM_EPS)

    def lanes(c):
        return pl.ds(pl.multiple_of(256 * c, 256), 256)

    at_row, at_col, side = grid[0], grid[1], grid[2]

    def masked(value, dr, dc):
        ok = (at_row + dr >= 0) & (at_row + dr < side) & (at_col + dc >= 0) & (at_col + dc < side)
        return jnp.concatenate(
            [jnp.where(ok, value[:, 128 * j : 128 * j + 128], 0.0) for j in range(4)], axis=1
        )

    def rolled(value, sign, dr, dc):
        parts = []
        for start, end, width in ((0, TEACH_ROWS, 6), (TEACH_ROWS, ROWS, 4)):
            by = (sign * (dr * width + dc)) % (end - start)
            part = value[start:end]
            parts.append(part if by == 0 else pltpu.roll(part, by, 0))
        return jnp.concatenate(parts, axis=0)

    def taps(stride):
        for t in range(9):
            r, q = t // 3, t % 3
            if stride == 1:
                yield t, 0, r - 1, q - 1
            else:
                phase = 2 * (1 if r != 1 else 0) + (1 if q != 1 else 0)
                yield t, phase, -1 if r == 0 else 0, -1 if q == 0 else 0

    settle(0)
    whole_x = x[...].reshape(4 * PADDED, C_IN)
    for c in range(2):
        z = mul(whole_x, narrow_part(w0, 0, 16, (2 * c, 2 * c + 1)))
        z = jnp.concatenate([z[PADDED * p : PADDED * p + ROWS] for p in range(4)], axis=0)
        standard, centre, spread, _ = standardize(z)
        put_stats(0, 256 * c, centre, spread)
        std_a[:, 256 * c : 256 * c + 256] = standard
        hidden[:, 256 * c : 256 * c + 256] = (
            soft(row(0, 2 * c) * standard + row(0, 4 + 2 * c)).astype(LOW).astype(FULL)
        )

    for t, phase, dr, dc in taps(2):
        cols0[t] = pad_low(masked(rolled(hidden[ROWS * phase : ROWS * phase + ROWS, :], -1, dr, dc), dr, dc))
    acc[...] = jnp.zeros_like(acc)

    @pl.loop(0, 9)
    def _(t):
        acc[...] += mul(cols0[t], narrow_part(w0, 16 + 8 * t, 8))

    def middle(section, std, nar):
        for c in range(2):
            at = slice(256 * c, 256 * c + 256)
            standard, centre, spread, _ = standardize(acc[0:ROWS, at])
            put_stats(section, MID + 256 * c, centre, spread)
            std[:, at] = standard
            nar[:, at] = pad_low(soft(row(section, 8 + 2 * c) * standard + row(section, 12 + 2 * c)))

    middle(0, std_b, nar0)
    acc[...] = jnp.zeros_like(acc)
    settle(1)
    settle(2)

    @pl.loop(0, 8)
    def _(c):
        at = lanes(c)
        standard, centre, spread, _ = standardize(mul(x[0], wide_part(w0, FRONT_WIDE, 64, c))[0:ROWS])
        put_stats(0, 2 * MID + pl.multiple_of(256 * c, 256), centre, spread)
        std_p[:, at] = standard
        low = pad_low(row(0, 16 + 2 * c) * standard + row(0, 32 + 2 * c))
        wide0[:, at] = low
        standard, centre, spread, _ = standardize(mul(nar0[...], wide_part(w1, 0, 32, c))[0:ROWS])
        put_stats(1, pl.multiple_of(256 * c, 256), centre, spread)
        std_1[:, at] = standard
        pre = low.astype(FULL)[0:ROWS] + row(1, 2 * c) * standard + row(1, 16 + 2 * c)
        low = pad_low(soft(pre))
        wide1[:, at] = low
        acc[...] += mul(low, narrow_part(w2, 4 * c, 4))

    for c in range(2):
        at = slice(256 * c, 256 * c + 256)
        standard, centre, spread, _ = standardize(acc[0:ROWS, at])
        put_stats(2, 256 * c, centre, spread)
        std_c[:, at] = standard
        hidden[0:ROWS, at] = soft(row(2, 2 * c) * standard + row(2, 4 + 2 * c)).astype(LOW).astype(FULL)
    for t, phase, dr, dc in taps(1):
        cols2[t] = pad_low(masked(rolled(hidden[0:ROWS, :], -1, dr, dc), dr, dc))
    acc[...] = jnp.zeros_like(acc)

    @pl.loop(0, 9)
    def _(t):
        acc[...] += mul(cols2[t], narrow_part(w2, 32 + 8 * t, 8))

    middle(2, std_d, nar2)

    turned[...] = nar2[...].T
    acc[...] = jnp.zeros_like(acc)
    settle(3)
    for fetched in rows:
        fetched.wait()

    def spread_rows(values):
        head = lax.broadcasted_iota(jnp.int32, (8, 256), 0) < 4
        first, second = (jnp.broadcast_to(value, (8, 256)) for value in values[0:2])
        parts = [jnp.broadcast_to(values[0], (32, 256)), jnp.where(head, first, second)]
        parts.append(jnp.broadcast_to(values[1], (32, 256)))
        parts.extend(jnp.broadcast_to(value, (16, 256)) for value in values[2:5])
        return jnp.concatenate(parts, axis=0)

    def crop_sums(value):
        head = lax.broadcasted_iota(jnp.int32, (8, 256), 0) < 4
        between = value[32:40]

        def total(part):
            return jnp.sum(part, axis=0, keepdims=True)

        return [
            total(value[0:32]) + total(jnp.where(head, between, 0.0)),
            total(value[40:72]) + total(jnp.where(head, 0.0, between)),
            total(value[72:88]),
            total(value[88:104]),
            total(value[104:120]),
        ]

    @pl.loop(0, 8)
    def _(c):
        at = lanes(c)
        weight = wide_part(w3, 0, 32, c)
        standard, centre, spread, inverse = standardize(mul(nar2[...], weight)[0:ROWS])
        put_stats(3, pl.multiple_of(256 * c, 256), centre, spread)
        gain = row(3, 2 * c)
        before = wide1[:, at].astype(FULL)[0:ROWS]
        pre = before + gain * standard + row(3, 16 + 2 * c)
        ending = jnp.where(gate > 0, soft(pre), before)
        final[:, at] = pad_low(ending)
        square = ending * ending
        factors = []
        for crop, total in enumerate(crop_sums(square * ending)):
            mean = total / (36.0 if crop < 2 else 16.0) + POOL_EPS
            factors.append(jnp.exp(jnp.log(mean) * (-2.0 / 3.0)) * wanted[crop : crop + 1, at])
        cotangent = spread_rows(factors) * square
        grad_pre = cotangent * gate_of(pre) * gate
        relay[:, at] = pad_low(grad_pre + cotangent * (1.0 - gate))
        result, grad_gain, grad_bias = unstandardize(grad_pre, standard, gain, inverse)
        put_row(3, 2 * c, grad_gain)
        put_row(3, 16 + 2 * c, grad_bias)
        low = pad_low(result)
        acc[...] += mul_t(low, weight)
        put_wide(w3, 0, 32, c, mul(turned[...], low))

    def flush(section):
        weights[section][VEC_TILE[section]] = grad_vec[section].astype(LOW)

    flush(3)
    stores = [pltpu.make_async_copy(w3, out_small.at[1], out_sem.at[15])]
    stores[-1].start()

    def middle_back(section, std):
        for c in range(2):
            at = slice(256 * c, 256 * c + 256)
            gain, bias = row(section, 8 + 2 * c), row(section, 12 + 2 * c)
            grad = acc[0:ROWS, at].astype(LOW).astype(FULL) * gate_of(gain * std[:, at] + bias)
            result, grad_gain, grad_bias = unstandardize(
                grad, std[:, at], gain, inverse_of(section, MID + 256 * c)
            )
            put_row(section, 8 + 2 * c, grad_gain)
            put_row(section, 12 + 2 * c, grad_bias)
            dz_n[:, at] = pad_low(result)

    def taps_back(weight, start, cols, stride, phases):
        grad_h[0 : ROWS * phases, :] = jnp.zeros((ROWS * phases, MID), FULL)
        for t, phase, dr, dc in taps(stride):
            part = mul_t(dz_n[...], narrow_part(weight, start + 8 * t, 8))[0:ROWS]
            at = slice(ROWS * phase, ROWS * phase + ROWS)
            grad_h[at, :] += rolled(masked(part, dr, dc), 1, dr, dc)
            put_narrow(weight, start + 8 * t, 8, mul(cols[t].T, dz_n[...]))

    middle_back(2, std_d)
    taps_back(w2, 32, cols2, 1, 1)
    for c in range(2):
        at = slice(256 * c, 256 * c + 256)
        gain, bias = row(2, 2 * c), row(2, 4 + 2 * c)
        grad = grad_h[0:ROWS, at] * gate_of(gain * std_c[:, at] + bias)
        result, grad_gain, grad_bias = unstandardize(grad, std_c[:, at], gain, inverse_of(2, 256 * c))
        put_row(2, 2 * c, grad_gain)
        put_row(2, 4 + 2 * c, grad_bias)
        dz_n[:, at] = pad_low(result)
    turned[...] = nar0[...].T
    acc[...] = jnp.zeros_like(acc)
    acc_x[...] = jnp.zeros_like(acc_x)

    @pl.loop(0, 8)
    def _(c):
        at = lanes(c)
        low = dz_n[...]
        grad = relay[:, at].astype(FULL) + mul_t(low, narrow_part(w2, 4 * c, 4))
        put_narrow(w2, 4 * c, 4, mul(wide1[:, at].T, low))
        grad = grad.astype(LOW).astype(FULL)[0:ROWS]
        gain = row(1, 2 * c)
        pre = wide0[:, at].astype(FULL)[0:ROWS] + gain * std_1[:, at] + row(1, 16 + 2 * c)
        grad = grad * gate_of(pre)
        result, grad_gain, grad_bias = unstandardize(
            grad, std_1[:, at], gain, inverse_of(1, pl.multiple_of(256 * c, 256))
        )
        put_row(1, 2 * c, grad_gain)
        put_row(1, 16 + 2 * c, grad_bias)
        low = pad_low(result)
        acc[...] += mul_t(low, wide_part(w1, 0, 32, c))
        put_wide(w1, 0, 32, c, mul(turned[...], low))
        grad = grad.astype(LOW).astype(FULL)
        result, grad_gain, grad_bias = unstandardize(
            grad, std_p[:, at], row(0, 16 + 2 * c), inverse_of(0, 2 * MID + pl.multiple_of(256 * c, 256))
        )
        put_row(0, 16 + 2 * c, grad_gain)
        put_row(0, 32 + 2 * c, grad_bias)
        low = pad_low(result)
        acc_x[...] += mul_t(low, wide_part(w0, FRONT_WIDE, 64, c))
        put_wide(w0, FRONT_WIDE, 64, c, mul(x[0].T, low))

    flush(1)
    flush(2)
    w2[105:115] = jnp.zeros((10, TILE, 128), LOW)
    stores.append(pltpu.make_async_copy(w1, out_small.at[0], out_sem.at[14]))
    stores[-1].start()
    for b in range(8):
        if b < 6:
            stores.append(pltpu.make_async_copy(
                w2.at[pl.ds(19 * b, 20)], out_big.at[1, inv[8 + b]], out_sem.at[8 + b]))
            stores[-1].start()
        else:
            for h in range(2):
                stores.append(pltpu.make_async_copy(
                    w2.at[pl.ds(105, 10)], out_big.at[1, inv[8 + b], pl.ds(10 * h, 10)],
                    out_sem.at[16 + 2 * (b - 6) + h]))
                stores[-1].start()

    middle_back(0, std_b)
    taps_back(w0, 16, cols0, 2, 4)
    for c in range(2):
        at = slice(256 * c, 256 * c + 256)
        gain, bias = row(0, 2 * c), row(0, 4 + 2 * c)
        grad = grad_h[:, at] * gate_of(gain * std_a[:, at] + bias)
        result, grad_gain, grad_bias = unstandardize(grad, std_a[:, at], gain, inverse_of(0, 256 * c))
        put_row(0, 2 * c, grad_gain)
        put_row(0, 4 + 2 * c, grad_bias)
        for p in range(4):
            dz_a[PADDED * p : PADDED * p + PADDED, at] = pad_low(result[ROWS * p : ROWS * p + ROWS])

    @pl.loop(0, 4)
    def _(c):
        at = lanes(c)
        low = dz_a[...]
        part = mul_t(low, narrow_part(w0, 4 * c, 4))
        grad_x[0, :, at] = (part[0:PADDED] + acc_x[:, at]).astype(LOW)
        for p in range(1, 4):
            grad_x[p, :, at] = part[PADDED * p : PADDED * p + PADDED].astype(LOW)
        turned_x = x[:, :, at].reshape(4 * PADDED, 256).T
        put_narrow(w0, 4 * c, 4, mul(turned_x, low))

    flush(0)
    for b in range(8):
        stores.append(pltpu.make_async_copy(
            w0.at[pl.ds(19 * b, 20)], out_big.at[0, inv[b]], out_sem.at[b]))
        stores[-1].start()
    for section in range(4):
        part = raw[2 * section : 2 * section + 2]
        stats[section, 0:2] = part if section < 2 else part * gate
        stats[section, 2:8] = jnp.zeros((6, 2 * MID + C_OUT), FULL)
    for store in stores:
        store.wait()


def run_step(table, gates, teach_ids, stud_ids, all_big, all_small, phases, targets):
    spots = np.zeros((3, ROWS, 128), np.int32)
    for r in range(ROWS):
        width = 6 if r < TEACH_ROWS else 4
        at = r % 36 if r < TEACH_ROWS else (r - TEACH_ROWS) % 16
        spots[0, r], spots[1, r], spots[2, r] = at // width, at % width, width
    sem = pltpu.SemaphoreType.DMA
    wide = jax.ShapeDtypeStruct((PADDED, C_OUT), LOW)
    vm = pltpu.VMEM
    return pl.pallas_call(
        step_kernel,
        name="step",
        out_shape=(
            wide, wide, wide,
            jax.ShapeDtypeStruct((4, 8, 2 * MID + C_OUT), FULL),
            jax.ShapeDtypeStruct((4, PADDED, C_IN), LOW),
            jax.ShapeDtypeStruct((2, 8, WINDOW, TILE, 128), LOW),
            jax.ShapeDtypeStruct((2, USED_TILES[1], TILE, 128), LOW),
        ),
        in_specs=[smem_spec()] * 4 + [any_spec(), any_spec(), vmem_spec(), any_spec(), vmem_spec()],
        out_specs=(vmem_spec(),) * 5 + (any_spec(),) * 2,
        scratch_shapes=[
            vm((153, TILE, 128), LOW), vm((33, TILE, 128), LOW), vm((115, TILE, 128), LOW), vm((33, TILE, 128), LOW),
            vm((12, TILE, 128), LOW), vm((4, 48, 128), FULL), vm((4, TILE, 128), FULL),
            vm((8, 2 * MID + C_OUT), FULL),
            vm((4 * ROWS, MID), FULL), vm((ROWS, MID), FULL), vm((ROWS, C_OUT), FULL), vm((ROWS, C_OUT), FULL),
            vm((ROWS, MID), FULL), vm((ROWS, MID), FULL), vm((4 * ROWS, MID), FULL),
            vm((9, PADDED, MID), LOW), vm((9, PADDED, MID), LOW),
            vm((PADDED, MID), LOW), vm((PADDED, MID), LOW), vm((MID, PADDED), LOW),
            vm((PADDED, C_OUT), LOW), vm((4 * PADDED, MID), LOW), vm((PADDED, MID), LOW),
            vm((PADDED, MID), FULL), vm((PADDED, C_IN), FULL), vm((4 * ROWS, MID), FULL),
            vm((8, C_OUT), FULL), pltpu.SMEM((16,), jnp.int32),
            sem((2, 16)), sem((17,)), sem((20,)),
        ],
        compiler_params=pltpu.CompilerParams(vmem_limit_bytes=60 << 20),
    )(table, gates, teach_ids, stud_ids, all_big, all_small, phases, targets, jnp.asarray(spots))


def reduce_kernel(big, small, wide0, wide1, final, stats, table,
                  out_big, out_small, segments, out_stats, norm, factor,
                  got, halves_x, halves_y, from_x, from_y, from_low, from_high, stage, total,
                  l_got, l_stage, l_low, l_high, l_halves_x, l_halves_y, l_from_x, l_from_y, l_total,
                  late, late_half, owner_row, by_pipe, by_dp, mine, part_sum,
                  s_send, s_recv, hx_send, hx_recv, hy_send, hy_recv, x_send, x_recv, y_send, y_recv,
                  zu_send, zu_recv, zd_send, zd_recv, lu_send, lu_recv, ld_send, ld_recv,
                  stage_sem, l_stage_sem, out_sem, late_send, late_recv, join_send, join_recv,
                  seg_send, seg_recv, stat_send, stat_recv, p_send, p_recv, d_send, d_recv):
    me = Place()
    me.enter()
    x, y, z, core = me.x, me.y, me.z, me.core
    up, down = me.device(z=z + 1), me.device(z=z - 1)
    x_side, y_side, sibling = me.device(x=1 - x), me.device(y=1 - y), me.device(core=1 - core)
    order = [
        jnp.where(z < 2, 3, 0),
        jnp.where(z == 0, 2, jnp.where(z == 1, 0, jnp.where(z == 2, 3, 1))),
        jnp.where(z == 0, 1, jnp.where(z == 1, 2, jnp.where(z == 2, 1, 2))),
        z,
    ]
    columns = ((1 - x, 1 - y), (x, 1 - y), (1 - x, y), (x, y))
    sequence = []
    for wave in range(6):
        for group, lag in ((0, 0), (1, 1), (2, 1), (3, 2)):
            if 0 <= wave - lag < 4:
                sequence.append((group, wave - lag))
    l_sequence = [(group, k) for k in range(4) for group in range(4)]

    def all_of(copies, act):
        for copy in copies:
            act(copy)

    def over(start, count, piece):
        whole = count // 512
        if whole:

            @pl.loop(0, whole)
            def _(i):
                piece(pl.multiple_of(start + 512 * i, 16), 512)

        if count % 512:
            piece(start + 512 * whole, count % 512)

    def source(array, group, k, half):
        xo, yo = columns[group]
        return array.at[xo, 2 * order[k] + yo, half]

    def share(group, k):
        at = 4 * group + k
        return remote(source(big, group, k, 1 - core), got.at[at], s_send.at[0, at], s_recv.at[0, at], sibling)

    def l_share(group, k):
        at = 4 * group + k
        return remote(source(small, group, k, 1 - core), l_got.at[at], s_send.at[1, at], s_recv.at[1, at], sibling)

    def fetch(n):
        return pltpu.make_async_copy(source(big, *sequence[n], core), stage.at[n % 4], stage_sem.at[n % 4])

    def l_fetch(group, k):
        at = 4 * group + k
        return pltpu.make_async_copy(source(small, group, k, core), l_stage.at[at], l_stage_sem.at[at])

    def add(target, at, other, slot, start, count, extras):
        def piece(begin, size):
            part = pl.ds(begin, size)
            sums = target[at, part, :].astype(FULL) + other[slot, part, :].astype(FULL)
            for ref, k in extras:
                sums = sums + ref[k, pl.ds(begin - start, size), :].astype(FULL)
            target[at, part, :] = sums.astype(LOW)

        over(start, count, piece)

    def send_half_x(k):
        return remote(got.at[k, pl.ds(BULK_CUT, BIG_HALF - BULK_CUT)], halves_x.at[k],
                      hx_send.at[k], hx_recv.at[k], x_side)

    def send_half_y(k):
        return remote(got.at[k, pl.ds(0, BULK_CUT)], halves_y.at[k], hy_send.at[k], hy_recv.at[k], y_side)

    def send_y(k):
        return remote(got.at[4 + k], from_y.at[k], y_send.at[k], y_recv.at[k], y_side)

    def send_x(k):
        return remote(got.at[8 + k], from_x.at[k], x_send.at[k], x_recv.at[k], x_side)

    def send_up(at, zd):
        return remote(got.at[at], from_low.at[zd - 1], zu_send.at[zd - 1], zu_recv.at[zd - 1], up)

    def send_down(at, zd):
        return remote(got.at[at], from_high.at[zd], zd_send.at[zd], zd_recv.at[zd], down)

    def l_column(group):
        xo, yo = columns[group]
        return 2 * xo + yo

    def l_up(group, k):
        at, zd = l_column(group), order[k] - 1
        return remote(l_got.at[4 * group + k], l_low.at[at, zd], lu_send.at[at, zd], lu_recv.at[at, zd], up)

    def l_down(group, k):
        at, zd = l_column(group), order[k]
        return remote(l_got.at[4 * group + k], l_high.at[at, zd], ld_send.at[at, zd], ld_recv.at[at, zd], down)

    def l_half_x():
        return remote(l_got.at[3, pl.ds(LIGHT_CUT, SMALL_HALF - LIGHT_CUT)], l_halves_x,
                      hx_send.at[4], hx_recv.at[4], x_side)

    def l_half_y():
        return remote(l_got.at[3, pl.ds(0, LIGHT_CUT)], l_halves_y, hy_send.at[4], hy_recv.at[4], y_side)

    def l_send_y():
        return remote(l_got.at[7], l_from_y, y_send.at[4], y_recv.at[4], y_side)

    def l_send_x():
        return remote(l_got.at[11], l_from_x, x_send.at[4], x_recv.at[4], x_side)

    leaving = (wide0, wide1, wide1, final)

    def exchange(section):
        target = {"dp": me.dp, "pipe": section}
        yield remote(leaving[section], segments.at[me.pipe], seg_send.at[section], seg_recv.at[me.pipe], target)
        yield remote(stats.at[section], out_stats.at[me.pipe], stat_send.at[section], stat_recv.at[me.pipe], target)

    def keep(section):
        yield pltpu.make_async_copy(leaving[section], segments.at[me.pipe], seg_send.at[section])
        yield pltpu.make_async_copy(stats.at[section], out_stats.at[me.pipe], stat_send.at[section])

    def arriving(micro):
        target = {"dp": me.dp, "pipe": micro}
        yield remote(wide0, segments.at[micro], seg_send.at[micro], seg_recv.at[micro], target)
        yield remote(stats.at[0], out_stats.at[micro], stat_send.at[micro], stat_recv.at[micro], target)

    for n in range(16):
        share(*sequence[n]).start()
        l_share(*l_sequence[n]).start()
    for n in range(2):
        fetch(n).start()
    for group, k in l_sequence:
        l_fetch(group, k).start()
    row_copy = pltpu.make_async_copy(table.at[2 * x], owner_row, out_sem.at[2])
    row_copy.start()

    def bulk_item(n):
        group, k = sequence[n]
        at, slot = 4 * group + k, n % 4
        if n + 2 < 16:
            fetch(n + 2).start()
        fetch(n).wait()
        share(group, k).wait_recv()
        if group == 0:
            add(got, at, stage, slot, 0, BIG_HALF, [])
            send_half_x(k).start()
            send_half_y(k).start()
        elif group == 1:
            send_half_x(k).wait_recv()
            add(got, at, stage, slot, 0, BULK_CUT, [])
            add(got, at, stage, slot, BULK_CUT, BIG_HALF - BULK_CUT, [(halves_x, k)])
            send_y(k).start()
        elif group == 2:
            send_half_y(k).wait_recv()
            add(got, at, stage, slot, 0, BULK_CUT, [(halves_y, k)])
            add(got, at, stage, slot, BULK_CUT, BIG_HALF - BULK_CUT, [])
            send_x(k).start()
        else:
            send_x(k).wait_recv()
            send_y(k).wait_recv()
            add(got, at, stage, slot, 0, BIG_HALF, [(from_x, k), (from_y, k)])
            if k == 3:
                return
            zd = order[k]

            @pl.when(zd > z)
            def _():
                @pl.when(z > 0)
                def _():
                    send_up(at, zd).wait_recv()
                    add(got, at, from_low, zd - 1, 0, BIG_HALF, [])

                send_up(at, zd).start()

            @pl.when(zd < z)
            def _():
                @pl.when(z < 3)
                def _():
                    send_down(at, zd).wait_recv()
                    add(got, at, from_high, zd, 0, BIG_HALF, [])

                send_down(at, zd).start()

    def light_item(group, k):
        at, zd, column = 4 * group + k, order[k], l_column(group)
        l_fetch(group, k).wait()
        l_share(group, k).wait_recv()
        add(l_got, at, l_stage, at, 0, SMALL_HALF, [])

        def merge(ref, slot):
            l_got[at] = (l_got[at].astype(FULL) + ref[column, slot].astype(FULL)).astype(LOW)

        if k < 3:

            @pl.when(zd > z)
            def _():
                @pl.when(z > 0)
                def _():
                    l_up(group, k).wait_recv()
                    merge(l_low, zd - 1)

                l_up(group, k).start()

            @pl.when(zd < z)
            def _():
                @pl.when(z < 3)
                def _():
                    l_down(group, k).wait_recv()
                    merge(l_high, zd)

                l_down(group, k).start()

        else:

            @pl.when(z > 0)
            def _():
                l_up(group, k).wait_recv()
                merge(l_low, zd - 1)

            @pl.when(z < 3)
            def _():
                l_down(group, k).wait_recv()
                merge(l_high, zd)

            if group == 0:
                l_half_x().start()
                l_half_y().start()

    def light_sides():
        l_half_x().wait_recv()
        l_got[7, LIGHT_CUT:SMALL_HALF, :] = (
            l_got[7, LIGHT_CUT:SMALL_HALF, :].astype(FULL) + l_halves_x[...].astype(FULL)
        ).astype(LOW)
        l_send_y().start()
        l_half_y().wait_recv()
        l_got[11, 0:LIGHT_CUT, :] = (
            l_got[11, 0:LIGHT_CUT, :].astype(FULL) + l_halves_y[...].astype(FULL)
        ).astype(LOW)
        l_send_x().start()

    def light_end():
        l_send_x().wait_recv()
        l_send_y().wait_recv()
        l_total[...] = l_got[15].astype(FULL) + l_from_x[...].astype(FULL) + l_from_y[...].astype(FULL)

    small_join = remote(late_half, late.at[pl.ds(0, SMALL_HALF)], join_send.at[1], join_recv.at[1], sibling)
    own_late = pltpu.make_async_copy(late, out_small.at[me.dp], out_sem.at[1])

    def late_copy(step, slot):
        target = {"dp": lax.rem(me.dp + step, 8), "pipe": me.pipe}
        return remote(late, out_small.at[slot], late_send.at[step], late_recv.at[step], target)

    for n in range(16):
        bulk_item(n)
        if n < 12:
            light_item(*l_sequence[n])
        if n == 12:
            for item in l_sequence[12:]:
                light_item(*item)
            light_sides()
        if n == 13:
            light_end()

            @pl.when(core == 0)
            def _():
                late_half[...] = l_total[...].astype(LOW)
                small_join.start()

            @pl.when(core == 1)
            def _():
                late[SMALL_HALF:SMALL_ROWS, :] = l_total[...].astype(LOW)

        if n == 14:

            @pl.when(core == 1)
            def _():
                small_join.wait_recv()
                own_late.start()
                for step in range(1, 8):
                    late_copy(step, me.dp).start()

            for section in range(4):
                @pl.when(me.pipe == section)
                def _(section=section):
                    all_of(keep(section), lambda copy: copy.start())

                @pl.when(me.pipe != section)
                def _(section=section):
                    all_of(exchange(section), lambda copy: copy.start())

    row_copy.wait()
    part_sum[...] = jnp.sum((l_total[...] * l_total[...]).reshape(SMALL_HALF // 8, 8, 128), axis=0)
    lane = lax.broadcasted_iota(jnp.int32, (8, 128), 1)
    is_last = jnp.where((lane == me.dp) & (owner_row[...] == 7), 1.0, 0.0)
    weight = jnp.broadcast_to(jnp.sum(is_last, axis=1, keepdims=True), (8, 128))
    weight = jnp.where(core == 0, jnp.ones((8, 128), FULL), weight)

    def end(low, high):
        def piece(begin, size, scale):
            part = pl.ds(begin, size)
            sums = got[15, part, :].astype(FULL)
            if low:
                sums = sums + from_low[z - 1, part, :].astype(FULL)
            if high:
                sums = sums + from_high[z, part, :].astype(FULL)
            total[part, :] = sums
            squares = jnp.sum((sums * sums).reshape(size // 8, 8, 128), axis=0)
            part_sum[...] += squares if scale is None else squares * scale

        over(0, BIG_HALF - 256, lambda begin, size: piece(begin, size, None))
        piece(BIG_HALF - 256, 256, weight)

    @pl.when(z == 0)
    def _():
        send_down(15, z).wait_recv()
        end(False, True)

    @pl.when((z > 0) & (z < 3))
    def _():
        send_up(15, z).wait_recv()
        send_down(15, z).wait_recv()
        end(True, True)

    @pl.when(z == 3)
    def _():
        send_up(15, z).wait_recv()
        end(True, False)

    big_join = remote(total, out_big.at[1], join_send.at[0], join_recv.at[0], sibling)
    own_big = pltpu.make_async_copy(total, out_big.at[0], out_sem.at[0])

    @pl.when(core == 0)
    def _():
        own_big.start()

    @pl.when(core == 1)
    def _():
        big_join.start()

    def along_pipe(step, slot):
        target = {"dp": me.dp, "pipe": lax.rem(me.pipe + step, 4)}
        return remote(part_sum, by_pipe.at[slot], p_send.at[step], p_recv.at[step], target)

    def along_dp(step, slot):
        target = {"dp": lax.rem(me.dp + step, 8), "pipe": me.pipe}
        return remote(mine, by_dp.at[slot], d_send.at[step], d_recv.at[step], target)

    for step in range(1, 4):
        along_pipe(step, me.pipe).start()
    by_pipe[me.pipe] = part_sum[...]
    for step in range(1, 4):
        along_pipe(step, lax.rem(me.pipe + 4 - step, 4)).wait_recv()
    mine[...] = jnp.sum(by_pipe[...], axis=0)
    for step in range(1, 8):
        along_dp(step, me.dp).start()
    by_dp[me.dp] = mine[...]
    for step in range(1, 8):
        along_dp(step, lax.rem(me.dp + 8 - step, 8)).wait_recv()
    whole = jnp.sum(jnp.sum(by_dp[...], axis=0), axis=0, keepdims=True)
    length = jnp.sqrt(jnp.broadcast_to(jnp.sum(whole, axis=1, keepdims=True), (8, 128)))
    norm[...] = length
    factor[...] = jnp.minimum(1.0, CLIP_NORM / length)

    @pl.when(core == 0)
    def _():
        own_big.wait()
        big_join.wait_recv()
        small_join.wait_send()

    @pl.when(core == 1)
    def _():
        big_join.wait_send()
        own_late.wait()
        for step in range(1, 8):
            late_copy(step, lax.rem(me.dp + 8 - step, 8)).wait_recv()
            late_copy(step, me.dp).wait_send()

    for other in range(4):
        @pl.when(me.pipe == other)
        def _(other=other):
            all_of(keep(other), lambda copy: copy.wait())

        @pl.when(me.pipe != other)
        def _(other=other):
            all_of(exchange(other), lambda copy: copy.wait_send())
            all_of(arriving(other), lambda copy: copy.wait_recv())

    for step in range(1, 4):
        along_pipe(step, me.pipe).wait_send()
    for step in range(1, 8):
        along_dp(step, me.dp).wait_send()
    for copy in (l_half_x(), l_half_y(), l_send_x(), l_send_y()):
        copy.wait_send()
    for k in range(4):
        send_half_x(k).wait_send()
        send_half_y(k).wait_send()
        send_x(k).wait_send()
        send_y(k).wait_send()
        for group in range(4):
            share(group, k).wait_send()
            l_share(group, k).wait_send()
    for k in range(3):
        zd, at = order[k], 12 + k

        @pl.when(zd > z)
        def _(at=at, zd=zd, k=k):
            send_up(at, zd).wait_send()
            for group in range(4):
                l_up(group, k).wait_send()

        @pl.when(zd < z)
        def _(at=at, zd=zd, k=k):
            send_down(at, zd).wait_send()
            for group in range(4):
                l_down(group, k).wait_send()


def reduce_all(big, small, wide0, wide1, final, stats, table):
    sem = pltpu.SemaphoreType.DMA
    vm = pltpu.VMEM
    lane_tile = jax.ShapeDtypeStruct((8, 128), FULL)
    return pl.pallas_call(
        reduce_kernel,
        name="reduce_all",
        out_shape=(
            jax.ShapeDtypeStruct((2, BIG_HALF, 128), FULL),
            jax.ShapeDtypeStruct((8, SMALL_ROWS, 128), LOW),
            jax.ShapeDtypeStruct((4,) + wide0.shape, LOW),
            jax.ShapeDtypeStruct((4,) + stats.shape[1:], FULL),
            lane_tile,
            lane_tile,
        ),
        in_specs=[any_spec()] * 7,
        out_specs=(any_spec(),) * 4 + (vmem_spec(),) * 2,
        scratch_shapes=[
            vm((16, BIG_HALF, 128), LOW), vm((4, BIG_HALF - BULK_CUT, 128), LOW), vm((4, BULK_CUT, 128), LOW),
            vm((4, BIG_HALF, 128), LOW), vm((4, BIG_HALF, 128), LOW),
            vm((3, BIG_HALF, 128), LOW), vm((3, BIG_HALF, 128), LOW),
            vm((4, BIG_HALF, 128), LOW), vm((BIG_HALF, 128), FULL),
            vm((16, SMALL_HALF, 128), LOW), vm((16, SMALL_HALF, 128), LOW),
            vm((4, 3, SMALL_HALF, 128), LOW), vm((4, 3, SMALL_HALF, 128), LOW),
            vm((SMALL_HALF - LIGHT_CUT, 128), LOW), vm((LIGHT_CUT, 128), LOW),
            vm((SMALL_HALF, 128), LOW), vm((SMALL_HALF, 128), LOW), vm((SMALL_HALF, 128), FULL),
            vm((SMALL_ROWS, 128), LOW), vm((SMALL_HALF, 128), LOW), vm((8, 128), jnp.int32),
            vm((4, 8, 128), FULL), vm((8, 8, 128), FULL), vm((8, 128), FULL), vm((8, 128), FULL),
            sem((2, 16)), sem((2, 16)),
            sem((5,)), sem((5,)), sem((5,)), sem((5,)), sem((5,)), sem((5,)), sem((5,)), sem((5,)),
            sem((3,)), sem((3,)), sem((3,)), sem((3,)),
            sem((4, 3)), sem((4, 3)), sem((4, 3)), sem((4, 3)),
            sem((4,)), sem((16,)), sem((3,)), sem((8,)), sem((8,)), sem((2,)), sem((2,)),
            sem((4,)), sem((4,)), sem((4,)), sem((4,)), sem((4,)), sem((4,)), sem((8,)), sem((8,)),
        ],
        compiler_params=pltpu.CompilerParams(
            collective_id=1, has_side_effects=True, vmem_limit_bytes=62 << 20
        ),
    )(big.reshape(2, 8, 2, BIG_HALF, 128), small.reshape(2, 8, 2, SMALL_HALF, 128),
      wide0, wide1, final, stats, table)


def high_dot(a, b, dims=((1,), (0,))):
    return lax.dot_general(a, b, (dims, ((), ())), precision=HIGH, preferred_element_type=FULL)


PIECES = 7
FRONT = 48


def update_kernel(owners, factor_ref, big, small, gram_old, basis_old, params, moment, second,
                  clipped, moment_new, second_new, params_new, gram_new, basis_new,
                  tiles, low, grad, held, rotated, weights, gram, in_sem, out_sem, tile_sem):
    factor = factor_ref[0:1, :]
    block, section = owners[0, lax.axis_index("dp")], lax.axis_index("pipe")
    even = lax.rem(section, 2) == 0
    span = params.shape[0]
    piece = held.shape[0] // PIECES

    @pl.when(even)
    def _():
        pltpu.make_async_copy(big, tiles, tile_sem).start()

    def loads(i):
        part = pl.ds(piece * i, min(piece, span - piece * i))
        for n, (src, dst) in enumerate(((params, weights), (moment, held), (second, rotated))):
            yield pltpu.make_async_copy(src.at[part, 0, :], dst.at[part], in_sem.at[n, i])

    def stores(i):
        count = min(piece, span - piece * i)
        part = pl.ds(piece * i, count)
        yield pltpu.make_async_copy(
            grad.at[pl.ds(FRONT + piece * i, count)], clipped.at[part, 0, :], out_sem.at[3, i])
        pairs = ((held, moment_new), (rotated, second_new), (weights, params_new))
        for n, (src, dst) in enumerate(pairs):
            yield pltpu.make_async_copy(src.at[part], dst.at[part, 0, :], out_sem.at[n, i])

    for i in range(PIECES):
        for load in loads(i):
            load.start()

    @pl.when(even)
    def _():
        pltpu.make_async_copy(big, tiles, tile_sem).wait()

    @pl.when(jnp.logical_not(even))
    def _():
        low[...] = jnp.zeros_like(low)

        @pl.when(block == 0)
        def _():
            copy = pltpu.make_async_copy(small.at[0:20], low, tile_sem)
            copy.start()
            copy.wait()

        @pl.when(block == 1)
        def _():
            copy = pltpu.make_async_copy(small.at[19:33], low.at[0:14], tile_sem)
            copy.start()
            copy.wait()

        @pl.loop(0, WINDOW)
        def _(r):
            tiles[r] = low[r].astype(FULL)

    @pl.loop(0, WINDOW)
    def _(r):
        narrow, plain = tile_forms(section, STRIDE * block + r)
        base = FRONT - 6 * block + TILE * r

        @pl.when(narrow)
        def _():
            for j in range(4):
                grad[pl.ds(base + j, 64, 4), :] = tiles[r, 64 * j : 64 * j + 64, :]

        @pl.when(plain)
        def _():
            grad[pl.ds(base, TILE), :] = tiles[r]

        @pl.when(jnp.logical_not(narrow | plain))
        def _():
            for j in range(16):
                grad[pl.ds(base + j, 16, 16), :] = tiles[r, 16 * j : 16 * j + 16, :]

    tail = piece * PIECES - 8
    rest = lax.broadcasted_iota(jnp.int32, (8, 128), 0) + tail
    grad[FRONT + tail : FRONT + tail + 8, :] = jnp.where(
        rest < span, grad[FRONT + tail : FRONT + tail + 8, :], 0.0
    )
    gram[...] = jnp.zeros_like(gram)

    def halves(value):
        high = value.astype(LOW)
        return high, (value - high.astype(FULL)).astype(LOW)

    def split_dot(a, b, dims=((1,), (0,))):
        def dot(left, right):
            return lax.dot_general(left, right, (dims, ((), ())), preferred_element_type=FULL)

        return dot(a[0], b[0]) + (dot(a[0], b[1]) + dot(a[1], b[0]))

    @pl.loop(0, PIECES)
    def _(i):
        part = halves(grad[pl.ds(pl.multiple_of(FRONT + piece * i, 8), piece), :])
        gram[...] += split_dot(part, part, ((0,), (0,)))

    old = basis_old[...]
    fresh = DECAY_STATS * gram_old[...] + (1.0 - DECAY_STATS) * (gram[...] * (factor * factor))
    gram_new[...] = fresh
    product = high_dot(fresh, old)
    rotation = product / jnp.sqrt(jnp.sum(product * product))
    for repeat in range(NS_STEPS):
        square = high_dot(rotation, rotation, ((0,), (0,)))
        rotation = 1.5 * rotation - 0.5 * high_dot(rotation, square)
    basis_new[...] = rotation
    change = halves(high_dot(old, rotation, ((0,), (0,))))
    turn = halves(rotation)
    correction = math.sqrt(1.0 - DECAY_SECOND**STEP) / (1.0 - DECAY_FIRST**STEP)
    for i in range(PIECES):
        for load in loads(i):
            load.wait()
        at = slice(FRONT + piece * i, FRONT + piece * i + piece)
        part = slice(piece * i, piece * i + piece)
        clip = grad[at, :] * factor
        grad[at, :] = clip
        turned = split_dot(halves(clip), turn)
        first = DECAY_FIRST * split_dot(halves(held[part, :]), change) + (1.0 - DECAY_FIRST) * turned
        power = DECAY_SECOND * rotated[part, :] + (1.0 - DECAY_SECOND) * turned * turned
        held[part, :] = first
        rotated[part, :] = power
        scaled = halves(first / (jnp.sqrt(power) + ADAM_EPS))
        direction = split_dot(scaled, turn, ((1,), (1,))) * correction
        before = weights[part, :]
        weights[part, :] = before - LEARN_RATE * (direction + WEIGHT_DECAY * before)
        for store in stores(i):
            store.start()
    for i in range(PIECES):
        for store in stores(i):
            store.wait()


def update(owners, factor, big, small, gram_old, basis_old, params, moment, second):
    span = params.shape[1] // 128
    rows = -(-span // (8 * PIECES)) * 8 * PIECES
    flat_shape = jax.ShapeDtypeStruct((span, 1, 128), FULL)
    square = jax.ShapeDtypeStruct((128, 128), FULL)
    sem = pltpu.SemaphoreType.DMA
    vm = pltpu.VMEM
    outs = pl.pallas_call(
        update_kernel,
        name="update",
        out_shape=(flat_shape,) * 4 + (square,) * 2,
        in_specs=[smem_spec(), vmem_spec()] + [any_spec()] * 2 + [vmem_spec()] * 2 + [any_spec()] * 3,
        out_specs=(any_spec(),) * 4 + (vmem_spec(),) * 2,
        scratch_shapes=[
            vm((WINDOW, TILE, 128), FULL), vm((WINDOW, TILE, 128), LOW),
            vm((FRONT + WINDOW * TILE, 128), FULL), vm((rows, 128), FULL), vm((rows, 128), FULL),
            vm((rows, 128), FULL), vm((128, 128), FULL), sem((3, PIECES)), sem((4, PIECES)), sem,
        ],
        compiler_params=pltpu.CompilerParams(vmem_limit_bytes=60 << 20),
    )(owners, factor, big.reshape(WINDOW, TILE, 128), small.reshape(USED_TILES[1], TILE, 128),
      gram_old, basis_old, params.reshape(span, 1, 128), moment.reshape(span, 1, 128),
      second.reshape(span, 1, 128))
    return tuple(out.reshape(1, span * 128) for out in outs[:4]) + outs[4:]


def to_phases(teach, stud):
    def split(part):
        crops, high, across, channels = part.shape
        part = part.reshape(crops, high // 2, 2, across // 2, 2, channels).transpose(2, 4, 0, 1, 3, 5)
        return part.reshape(4, -1, channels)

    zeros = jnp.zeros((4, PADDED - ROWS, teach.shape[-1]), teach.dtype)
    return jnp.concatenate([split(teach), split(stud), zeros], axis=1)


def from_phases(phases, shape):
    crops, high, across, channels = shape
    part = phases.reshape(2, 2, crops, high // 2, across // 2, channels)
    return part.transpose(2, 3, 0, 4, 1, 5).reshape(shape)


def on_small_slice(
    teach_in,
    stud_in,
    params,
    owners,
    depth_gates,
    teach_ids,
    stud_ids,
    targets,
    moment,
    second,
    gram_stats,
    eigen_basis,
):
    phases = to_phases(teach_in[0], stud_in[0])
    big, small, ids = prepare(owners, params)
    all_big, all_small, table = gather_all(big, small, ids)
    wide_0, wide_1, final, stats, grad_x, out_big, out_small = run_step(
        table,
        depth_gates,
        teach_ids,
        stud_ids,
        all_big.reshape(2, 8, 2, WINDOW // 2, TILE, 128),
        all_small.reshape(2, USED_TILES[1], TILE, 128),
        phases,
        targets,
    )
    sum_big, sum_small, segments, stats, norm, factor = reduce_all(
        out_big, out_small, wide_0, wide_1, final, stats, table
    )
    clipped, moment_new, second_new, params_new, gram_new, rotation = update(
        owners, factor, sum_big, sum_small, gram_stats[0], eigen_basis[0], params, moment, second
    )
    teach_shape, stud_shape = teach_in.shape[1:], stud_in.shape[1:]
    small_teach = (teach_shape[0], teach_shape[1] // 2, teach_shape[2] // 2, C_OUT)
    small_stud = (stud_shape[0], stud_shape[1] // 2, stud_shape[2] // 2, C_OUT)
    segment_teach = segments[:, :TEACH_ROWS].reshape((4,) + small_teach)
    segment_stud = segments[:, TEACH_ROWS:ROWS].reshape((4,) + small_stud)
    stats = stats[:, 0:2]
    teach_grad = from_phases(grad_x[:, :TEACH_ROWS], teach_shape)
    stud_grad = from_phases(grad_x[:, TEACH_ROWS:ROWS], stud_shape)
    grad_norm = norm[0, 0]
    return (
        segment_teach[None],
        segment_stud[None],
        teach_grad[None],
        stud_grad[None],
        stats[None, :, None],
        grad_norm,
        clipped,
        moment_new,
        second_new,
        params_new,
        gram_new[None],
        rotation[None],
    )


def solution(mesh):
    placed = (
        P("pipe", "dp", None, None, None),
        P("pipe", "dp", None, None, None),
        P("pipe", "dp"),
        P("pipe", None),
        P(),
        P(None, "dp"),
        P(None, "dp"),
        P(),
        P("pipe", "dp"),
        P("pipe", "dp"),
        P("pipe", "dp", None),
        P("pipe", "dp", None),
    )
    small_slice = mesh.shape["dp"] == 8 and mesh.shape["pipe"] == 4
    return jax.shard_map(
        on_small_slice if small_slice else on_device,
        mesh=mesh,
        in_specs=placed,
        out_specs=(
            P("pipe", None, "dp", None, None, None),
            P("pipe", None, "dp", None, None, None),
            P("pipe", "dp", None, None, None),
            P("pipe", "dp", None, None, None),
            P("pipe", None, "dp", None, None),
            P(),
            P("pipe", "dp"),
            P("pipe", "dp"),
            P("pipe", "dp"),
            P("pipe", "dp"),
            P("pipe", "dp", None),
            P("pipe", "dp", None),
        ),
        check_vma=False,
    )
```

```python
import math

import jax
import jax.numpy as jnp
import numpy as np
from jax import lax
from jax.experimental import pallas as pl
from jax.experimental.pallas import tpu as pltpu
from jax.sharding import PartitionSpec as P

C_IN = 1024
MID = 512
C_OUT = 2048
STEP = 10
NS_STEPS = 5


HIGH = lax.Precision.HIGHEST
NORM_EPS = 1e-05
POOL_EPS = 1e-06
CLIP_NORM = 1.0
LEARN_RATE = 0.02
DECAY_FIRST = 0.9
DECAY_SECOND = 0.95
DECAY_STATS = 0.95
ADAM_EPS = 1e-08
WEIGHT_DECAY = 0.01


def section_shapes(section):
    if section == 0:
        return [
            ("first_conv", (C_IN, MID)),
            ("middle_conv", (9 * MID, MID)),
            ("skip_conv", (C_IN, C_OUT)),
            ("first_gain", (MID,)),
            ("first_bias", (MID,)),
            ("middle_gain", (MID,)),
            ("middle_bias", (MID,)),
            ("skip_gain", (C_OUT,)),
            ("skip_bias", (C_OUT,)),
        ]
    if section == 2:
        return [
            ("first_conv", (C_OUT, MID)),
            ("middle_conv", (9 * MID, MID)),
            ("first_gain", (MID,)),
            ("first_bias", (MID,)),
            ("middle_gain", (MID,)),
            ("middle_bias", (MID,)),
        ]
    return [("last_conv", (MID, C_OUT)), ("last_gain", (C_OUT,)), ("last_bias", (C_OUT,))]


def unpack(flat_vector, section):
    pieces = {}
    offset = 0
    for entry_name, entry_shape in section_shapes(section):
        entry_size = math.prod(entry_shape)
        pieces[entry_name] = flat_vector[offset : offset + entry_size].reshape(entry_shape)
        offset = offset + entry_size
    return pieces


def pack(grads, section, flat_size):
    parts = [grads[entry_name].reshape(-1) for entry_name, entry_shape in section_shapes(section)]
    used = sum((math.prod(entry_shape) for entry_name, entry_shape in section_shapes(section)))
    parts.append(jnp.zeros((flat_size - used,), jnp.float32))
    return jnp.concatenate(parts)


def as_float(vector):
    return vector.astype(jnp.float32)


def to_low(groups):
    return tuple((portion.astype(jnp.bfloat16) for portion in groups))


def to_high(groups):
    return tuple((portion.astype(jnp.float32) for portion in groups))


def point_conv(groups, weight):
    return tuple(
        (
            jnp.einsum("khwc,cd->khwd", portion, weight, preferred_element_type=jnp.float32)
            for portion in groups
        )
    )


def point_back(grad_out, groups, weight):
    low_grads = to_low(grad_out)
    grad_input = tuple(
        (
            jnp.einsum("khwd,cd->khwc", grad_part, weight, preferred_element_type=jnp.float32)
            for grad_part in low_grads
        )
    )
    grad_weight = sum(
        (
            jnp.einsum("khwc,khwd->cd", in_part, grad_part, preferred_element_type=jnp.float32)
            for in_part, grad_part in zip(groups, low_grads)
        )
    )
    return (grad_input, grad_weight)


def patches(portion, stride):
    height = portion.shape[1]
    across = portion.shape[2]
    padded = jnp.pad(portion, ((0, 0), (1, 1), (1, 1), (0, 0)))
    shifted = [
        padded[:, row_off : row_off + height : stride, col_off : col_off + across : stride, :]
        for row_off in range(3)
        for col_off in range(3)
    ]
    return jnp.concatenate(shifted, axis=-1)


def area_conv(groups, weight, stride):
    columns = tuple((patches(portion, stride) for portion in groups))
    return (point_conv(columns, weight), columns)


def unpatch(grad_cols, height, across, stride):
    channels = grad_cols.shape[-1] // 9
    padded = jnp.zeros((grad_cols.shape[0], height + 2, across + 2, channels), jnp.float32)
    for row_off in range(3):
        for col_off in range(3):
            offset = (3 * row_off + col_off) * channels
            padded = padded.at[
                :, row_off : row_off + height : stride, col_off : col_off + across : stride, :
            ].add(grad_cols[..., offset : offset + channels])
    return padded[:, 1 : height + 1, 1 : across + 1, :]


def area_back(grad_out, columns, weight, stride, in_shapes):
    grad_cols, grad_weight = point_back(grad_out, columns, weight)
    grad_input = tuple(
        (
            unpatch(grad_part, shape_item[1], shape_item[2], stride)
            for grad_part, shape_item in zip(grad_cols, in_shapes)
        )
    )
    return (grad_input, grad_weight)


def batch_norm(groups, gain, bias):
    rows_total = sum((portion.shape[0] * portion.shape[1] * portion.shape[2] for portion in groups))
    centre = sum((jnp.sum(portion, axis=(0, 1, 2)) for portion in groups)) / rows_total
    spread = (
        sum((jnp.sum(jnp.square(portion - centre), axis=(0, 1, 2)) for portion in groups))
        / rows_total
    )
    inverse = lax.rsqrt(spread + NORM_EPS)
    standard = tuple(((portion - centre) * inverse for portion in groups))
    normed = tuple((gain * std_part + bias for std_part in standard))
    return (normed, (centre, spread, inverse, standard))


def norm_back(grad_out, gain, saved):
    centre, spread, inverse, standard = saved
    rows_total = sum(
        (portion.shape[0] * portion.shape[1] * portion.shape[2] for portion in standard)
    )
    grad_sum = sum((jnp.sum(grad_part, axis=(0, 1, 2)) for grad_part in grad_out))
    grad_dot = sum(
        (
            jnp.sum(grad_part * std_part, axis=(0, 1, 2))
            for grad_part, std_part in zip(grad_out, standard)
        )
    )
    grad_input = tuple(
        (
            gain
            * inverse
            * (grad_part - grad_sum / rows_total - std_part * (grad_dot / rows_total))
            for grad_part, std_part in zip(grad_out, standard)
        )
    )
    return (grad_input, grad_dot, grad_sum)


def through_softplus(grad_out, pre_values):
    return tuple(
        (grad_part * jax.nn.sigmoid(pre_part) for grad_part, pre_part in zip(grad_out, pre_values))
    )


def front_forward(pieces, inputs):
    first = point_conv(inputs, pieces["first_conv"])
    normed_a, saved_a = batch_norm(
        first, as_float(pieces["first_gain"]), as_float(pieces["first_bias"])
    )
    hidden = tuple((jax.nn.softplus(portion).astype(jnp.bfloat16) for portion in normed_a))
    middle, columns = area_conv(hidden, pieces["middle_conv"], 2)
    normed_b, saved_b = batch_norm(
        middle, as_float(pieces["middle_gain"]), as_float(pieces["middle_bias"])
    )
    narrow = tuple((jax.nn.softplus(portion) for portion in normed_b))
    reduced = tuple((portion[:, ::2, ::2, :] for portion in inputs))
    skipped = point_conv(reduced, pieces["skip_conv"])
    wide, saved_p = batch_norm(
        skipped, as_float(pieces["skip_gain"]), as_float(pieces["skip_bias"])
    )
    norm_rows = jnp.stack(
        [
            jnp.concatenate([saved_a[0], saved_b[0], saved_p[0]]),
            jnp.concatenate([saved_a[1], saved_b[1], saved_p[1]]),
        ]
    )
    kept = (normed_a, hidden, columns, normed_b, reduced, saved_a, saved_b, saved_p)
    return (wide, narrow, norm_rows, kept)


def front_backward(pieces, inputs, grad_wide, grad_narrow):
    wide, narrow, norm_rows, kept = front_forward(pieces, inputs)
    normed_a, hidden, columns, normed_b, reduced, saved_a, saved_b, saved_p = kept
    grads = {}
    grad_pre_b = through_softplus(grad_narrow, normed_b)
    grad_mid, grads["middle_gain"], grads["middle_bias"] = norm_back(
        grad_pre_b, as_float(pieces["middle_gain"]), saved_b
    )
    grad_hidden, grads["middle_conv"] = area_back(
        grad_mid, columns, pieces["middle_conv"], 2, [portion.shape for portion in hidden]
    )
    grad_pre_a = through_softplus(grad_hidden, normed_a)
    grad_first, grads["first_gain"], grads["first_bias"] = norm_back(
        grad_pre_a, as_float(pieces["first_gain"]), saved_a
    )
    grad_inputs, grads["first_conv"] = point_back(grad_first, inputs, pieces["first_conv"])
    grad_skip, grads["skip_gain"], grads["skip_bias"] = norm_back(
        grad_wide, as_float(pieces["skip_gain"]), saved_p
    )
    grad_reduced, grads["skip_conv"] = point_back(grad_skip, reduced, pieces["skip_conv"])
    grad_inputs = tuple(
        (
            full_part.at[:, ::2, ::2, :].add(part_reduced)
            for full_part, part_reduced in zip(grad_inputs, grad_reduced)
        )
    )
    return (grad_inputs, grads)


def join_forward(pieces, wide, narrow):
    last = point_conv(narrow, pieces["last_conv"])
    normed, saved = batch_norm(last, as_float(pieces["last_gain"]), as_float(pieces["last_bias"]))
    pre_values = tuple(
        (
            skip_part.astype(jnp.float32) + branch_part
            for skip_part, branch_part in zip(wide, normed)
        )
    )
    ending = tuple((jax.nn.softplus(pre_part) for pre_part in pre_values))
    filler = jnp.zeros((2 * MID,), jnp.float32)
    norm_rows = jnp.stack(
        [jnp.concatenate([saved[0], filler]), jnp.concatenate([saved[1], filler])]
    )
    return (ending, norm_rows, (pre_values, saved))


def join_grads(pieces, narrow, kept, grad_out, gate):
    pre_values, saved = kept
    grad_pre = tuple(
        (
            grad_part * jax.nn.sigmoid(pre_part) * gate
            for grad_part, pre_part in zip(grad_out, pre_values)
        )
    )
    grad_wide = tuple(
        (pre_grad + grad_part * (1.0 - gate) for pre_grad, grad_part in zip(grad_pre, grad_out))
    )
    grad_last, gain_grad, bias_grad = norm_back(grad_pre, as_float(pieces["last_gain"]), saved)
    grad_narrow, weight_grad = point_back(grad_last, narrow, pieces["last_conv"])
    grads = {"last_conv": weight_grad, "last_gain": gain_grad, "last_bias": bias_grad}
    return (grad_wide, grad_narrow, grads)


def split_forward(pieces, wide):
    first = point_conv(wide, pieces["first_conv"])
    normed_a, saved_a = batch_norm(
        first, as_float(pieces["first_gain"]), as_float(pieces["first_bias"])
    )
    hidden = tuple((jax.nn.softplus(portion).astype(jnp.bfloat16) for portion in normed_a))
    middle, columns = area_conv(hidden, pieces["middle_conv"], 1)
    normed_b, saved_b = batch_norm(
        middle, as_float(pieces["middle_gain"]), as_float(pieces["middle_bias"])
    )
    narrow = tuple((jax.nn.softplus(portion) for portion in normed_b))
    filler = jnp.zeros((C_OUT,), jnp.float32)
    norm_rows = jnp.stack(
        [
            jnp.concatenate([saved_a[0], saved_b[0], filler]),
            jnp.concatenate([saved_a[1], saved_b[1], filler]),
        ]
    )
    return (narrow, norm_rows, (normed_a, hidden, columns, normed_b, saved_a, saved_b))


def split_backward(pieces, wide, grad_relay, grad_narrow):
    narrow, norm_rows, kept = split_forward(pieces, wide)
    normed_a, hidden, columns, normed_b, saved_a, saved_b = kept
    grads = {}
    grad_pre_b = through_softplus(grad_narrow, normed_b)
    grad_mid, grads["middle_gain"], grads["middle_bias"] = norm_back(
        grad_pre_b, as_float(pieces["middle_gain"]), saved_b
    )
    grad_hidden, grads["middle_conv"] = area_back(
        grad_mid, columns, pieces["middle_conv"], 1, [portion.shape for portion in hidden]
    )
    grad_pre_a = through_softplus(grad_hidden, normed_a)
    grad_first, grads["first_gain"], grads["first_bias"] = norm_back(
        grad_pre_a, as_float(pieces["first_gain"]), saved_a
    )
    grad_conv_in, grads["first_conv"] = point_back(grad_first, wide, pieces["first_conv"])
    grad_wide = tuple(
        (relay_part + conv_part for relay_part, conv_part in zip(grad_relay, grad_conv_in))
    )
    return (grad_wide, grads)


def pool_grad(final, targets, picks):
    result = []
    for portion, pick_ids in zip(final, picks):
        cubes = jnp.mean(portion * portion * portion, axis=(1, 2)) + POOL_EPS
        factor = jnp.exp(jnp.log(cubes) * (-2.0 / 3.0)) * targets[pick_ids]
        result.append(factor[:, None, None, :] * portion * portion)
    return tuple(result)


def used_size(section):
    return sum((math.prod(entry_shape) for entry_name, entry_shape in section_shapes(section)))


def batch_pass(reals, inputs, gate, targets, picks):
    pieces = [unpack(reals[section], section) for section in range(4)]
    wide_f, narrow_f, rows_0, _ = front_forward(pieces[0], inputs)
    wide_0, narrow_0 = to_low(wide_f), to_low(narrow_f)
    ending_1, rows_1, kept_1 = join_forward(pieces[1], wide_0, narrow_0)
    wide_1 = to_low(ending_1)
    narrow_f, rows_2, _ = split_forward(pieces[2], wide_1)
    narrow_2 = to_low(narrow_f)
    ending_3, rows_3, kept_3 = join_forward(pieces[3], wide_1, narrow_2)
    final = tuple(
        (
            jnp.where(gate > 0, end_part, relay_part.astype(jnp.float32))
            for end_part, relay_part in zip(ending_3, wide_1)
        )
    )
    cotangent = pool_grad(final, targets, picks)
    grad_wide, grad_narrow, grads_3 = join_grads(pieces[3], narrow_2, kept_3, cotangent, gate)
    grad_wide, grads_2 = split_backward(
        pieces[2], wide_1, to_high(to_low(grad_wide)), to_high(to_low(grad_narrow))
    )
    grad_wide, grad_narrow, grads_1 = join_grads(
        pieces[1], narrow_0, kept_1, to_high(to_low(grad_wide)), 1.0
    )
    grad_inputs, grads_0 = front_backward(
        pieces[0], inputs, to_high(to_low(grad_wide)), to_high(to_low(grad_narrow))
    )
    outs = (wide_0, wide_1, wide_1, to_low(final))
    stats = jnp.stack([rows_0, rows_1, rows_2 * gate, rows_3 * gate])
    return (outs, stats, to_low(grad_inputs), (grads_0, grads_1, grads_2, grads_3))


def on_device(
    teach_in,
    stud_in,
    params,
    owners,
    depth_gates,
    teach_ids,
    stud_ids,
    targets,
    moment,
    second,
    gram_stats,
    eigen_basis,
):
    sections = lax.axis_size("pipe")
    rank = lax.axis_index("pipe")
    owner_count = lax.axis_size("dp")
    span_size = params.shape[1]
    flat_size = span_size * owner_count
    owner_rows = lax.all_gather(owners, "pipe", axis=0, tiled=True)
    gathered = lax.all_gather(params[0].astype(jnp.bfloat16), ("pipe", "dp"), axis=0)
    gathered = gathered.reshape(sections, owner_count, span_size)
    reals = []
    for section in range(sections):
        inverse = jnp.argsort(owner_rows[section]).astype(jnp.int32)
        blocks = -(-used_size(section) // span_size)
        reals.append(gathered[section][inverse[:blocks]].reshape(blocks * span_size))
    inputs = (teach_in[0], stud_in[0])
    gate = depth_gates[rank].astype(jnp.float32)
    outs, stats, (teach_grad, stud_grad), grads = batch_pass(
        reals, inputs, gate, targets, (teach_ids[rank], stud_ids[rank])
    )
    segment_teach = lax.all_to_all(
        jnp.stack([part[0] for part in outs]), "pipe", split_axis=0, concat_axis=0, tiled=True
    )
    segment_stud = lax.all_to_all(
        jnp.stack([part[1] for part in outs]), "pipe", split_axis=0, concat_axis=0, tiled=True
    )
    stats = lax.all_to_all(stats, "pipe", split_axis=0, concat_axis=0, tiled=True)
    rows = []
    for section in range(sections):
        flat = pack(grads[section], section, flat_size).reshape(owner_count, span_size)
        rows.append(flat[owner_rows[section]])
    span_total = lax.psum_scatter(
        jnp.stack(rows).reshape(sections * owner_count, span_size),
        ("pipe", "dp"),
        scatter_dimension=0,
        tiled=True,
    ).reshape(span_size)
    total_squares = lax.psum(jnp.sum(span_total * span_total), ("dp", "pipe"))
    grad_norm = jnp.sqrt(total_squares)
    factor = jnp.minimum(1.0, CLIP_NORM / grad_norm)
    clipped = span_total * factor
    matrix = clipped.reshape(span_size // 128, 128)
    gram_old = gram_stats[0]
    basis_old = eigen_basis[0]
    gram_new = DECAY_STATS * gram_old + (1.0 - DECAY_STATS) * jnp.dot(
        matrix.T, matrix, precision=HIGH
    )
    product = jnp.dot(gram_new, basis_old, precision=HIGH)
    rotation = product / jnp.sqrt(jnp.sum(product * product))
    for repeat in range(NS_STEPS):
        square = jnp.dot(rotation.T, rotation, precision=HIGH)
        rotation = 1.5 * rotation - 0.5 * jnp.dot(rotation, square, precision=HIGH)
    moment_old = moment.reshape(span_size // 128, 128)
    initial = jnp.dot(moment_old, basis_old.T, precision=HIGH)
    blended = DECAY_FIRST * initial + (1.0 - DECAY_FIRST) * matrix
    moment_new = jnp.dot(blended, rotation, precision=HIGH)
    rotated = jnp.dot(matrix, rotation, precision=HIGH)
    second_new = (
        DECAY_SECOND * second.reshape(span_size // 128, 128)
        + (1.0 - DECAY_SECOND) * rotated * rotated
    )
    correction = math.sqrt(1.0 - DECAY_SECOND**STEP) / (1.0 - DECAY_FIRST**STEP)
    direction = (
        jnp.dot(moment_new / (jnp.sqrt(second_new) + ADAM_EPS), rotation.T, precision=HIGH)
        * correction
    )
    weights = params.reshape(span_size // 128, 128)
    params_new = weights - LEARN_RATE * (direction + WEIGHT_DECAY * weights)
    return (
        segment_teach[None],
        segment_stud[None],
        teach_grad[None],
        stud_grad[None],
        stats[None, :, None],
        grad_norm,
        clipped.reshape(1, span_size),
        moment_new.reshape(1, span_size),
        second_new.reshape(1, span_size),
        params_new.reshape(1, span_size),
        gram_new[None],
        rotation[None],
    )


MESH = pl.DeviceIdType.MESH
LOW = jnp.bfloat16
FULL = jnp.float32
TILE = 256
WINDOW = 20
STRIDE = 19
VEC_TILE = (152, 32, 104, 32)
USED_TILES = (153, 33, 105, 33)
FRONT_WIDE = 88
SMALL_ROWS = 1056
ROWS = 120
PADDED = 128
TEACH_ROWS = 72


def any_spec():
    return pl.BlockSpec(memory_space=pl.ANY)


def smem_spec():
    return pl.BlockSpec(memory_space=pltpu.SMEM)


def vmem_spec():
    return pl.BlockSpec(memory_space=pltpu.VMEM)


def tile_forms(section, tile):
    even = lax.rem(section, 2) == 0
    vector = jnp.where(section == 0, 152, jnp.where(section == 2, 104, 32))
    narrow_end = jnp.where(section == 0, FRONT_WIDE, jnp.where(section == 2, 104, 0))
    narrow = even & (tile < narrow_end)
    plain = tile == vector
    return narrow, plain


def prepare_kernel(owners, params, big, small, ids, flat, sem):
    block, section = owners[0, lax.axis_index("dp")], lax.axis_index("pipe")

    @pl.loop(0, WINDOW)
    def _(r):
        flat[pl.ds(TILE * r, TILE)] = jnp.zeros((TILE, 128), FULL)

    copy = pltpu.make_async_copy(params.at[:, 0, :], flat.at[pl.ds(6 * block, params.shape[0])], sem)
    copy.start()

    @pl.loop(0, small.shape[0])
    def _(r):
        small[r] = jnp.zeros((TILE, 128), LOW)

    lane = lax.broadcasted_iota(jnp.int32, (8, 128), 1)
    row = jnp.zeros((8, 128), jnp.int32)
    for j in range(8):
        row = jnp.where(lane == j, owners[0, j], row)
    ids[...] = row
    copy.wait()

    @pl.loop(0, WINDOW)
    def _(r):
        tile = STRIDE * block + r
        narrow, plain = tile_forms(section, tile)
        base = TILE * r

        @pl.when(narrow)
        def _():
            for j in range(4):
                big[r, 64 * j : 64 * j + 64, :] = flat[pl.ds(base + j, 64, 4), :].astype(LOW)

        @pl.when(plain)
        def _():
            big[r] = flat[pl.ds(base, TILE), :].astype(LOW)

        @pl.when(jnp.logical_not(narrow | plain))
        def _():
            for j in range(16):
                big[r, 16 * j : 16 * j + 16, :] = flat[pl.ds(base + j, 16, 16), :].astype(LOW)

        @pl.when(tile < small.shape[0])
        def _():
            small[tile] = big[r]


def prepare(owners, params):
    return pl.pallas_call(
        prepare_kernel,
        name="prepare",
        out_shape=(
            jax.ShapeDtypeStruct((WINDOW, TILE, 128), LOW),
            jax.ShapeDtypeStruct((USED_TILES[1], TILE, 128), LOW),
            jax.ShapeDtypeStruct((8, 128), jnp.int32),
        ),
        in_specs=[smem_spec(), any_spec()],
        out_specs=(vmem_spec(),) * 3,
        scratch_shapes=[pltpu.VMEM((WINDOW * TILE, 128), FULL), pltpu.SemaphoreType.DMA],
        compiler_params=pltpu.CompilerParams(vmem_limit_bytes=60 << 20),
    )(owners, params.reshape(-1, 1, 128))


class Place:
    def __init__(self):
        self.dp = lax.axis_index("dp")
        self.pipe = lax.axis_index("pipe")
        self.x, self.core = self.pipe // 2, self.pipe % 2
        self.z, self.y = self.dp // 2, self.dp % 2

    def device(self, x=None, core=None, z=None, y=None):
        x = self.x if x is None else x
        core = self.core if core is None else core
        z = self.z if z is None else z
        y = self.y if y is None else y
        return {"dp": 2 * z + y, "pipe": 2 * x + core}

    def enter(self):
        barrier = pltpu.get_barrier_semaphore()
        for step in range(1, 8):
            other = lax.rem(self.dp + step, 8)
            pl.semaphore_signal(
                barrier, inc=1, device_id={"dp": other, "pipe": self.pipe}, device_id_type=MESH
            )
        for step in range(1, 4):
            other = lax.rem(self.pipe + step, 4)
            pl.semaphore_signal(
                barrier, inc=1, device_id={"dp": self.dp, "pipe": other}, device_id_type=MESH
            )
        pl.semaphore_wait(barrier, 10)


def remote(src, dst, send, recv, target):
    return pltpu.make_async_remote_copy(
        src_ref=src, dst_ref=dst, send_sem=send, recv_sem=recv, device_id=target, device_id_type=MESH
    )


BIG_HALF = WINDOW * TILE // 2
SMALL_HALF = SMALL_ROWS // 2
BULK_CUT = 1056
LIGHT_CUT = 256
BACK_CUT = 1488


def gather_kernel(big, small, ids, all_big, all_small, table, early, chunk, early_send, early_recv,
                  z_send, z_recv, x_send, x_recv, y_send, y_recv, dx_send, dx_recv, dy_send, dy_recv,
                  s_send, s_recv, first_send, first_recv, own_sem, id_send, id_recv, lz_send, lz_recv):
    me = Place()
    me.enter()
    x, y, z, core = me.x, me.y, me.z, me.core
    up, down = me.device(z=z + 1), me.device(z=z - 1)
    x_side, y_side, sibling = me.device(x=1 - x), me.device(y=1 - y), me.device(core=1 - core)

    class Stream:
        def __init__(self, n, out, cut):
            self.n, self.out, self.cut, self.rows = n, out, cut, out.shape[3]

        def block(self, xo, origin, yo):
            return self.out.at[xo, 2 * origin + yo, core]

        def move_x(self, origin):
            block = self.block(x, origin, y)
            return remote(block, block, x_send.at[self.n, origin], x_recv.at[self.n, origin], x_side)

        def move_y(self, origin):
            block = self.block(x, origin, y)
            return remote(block, block, y_send.at[self.n, origin], y_recv.at[self.n, origin], y_side)

        def share(self, xo, origin, yo):
            block = self.block(xo, origin, yo)
            at = 8 * xo + 2 * origin + yo
            return remote(block, block, s_send.at[self.n, at], s_recv.at[self.n, at], sibling)

        def move_z(self, origin, target, way):
            block = self.block(x, origin, y)
            return remote(block, block, z_send.at[self.n, way, origin], z_recv.at[self.n, origin], target)

        def half_x(self, origin, xo, yo):
            part = self.out.at[xo, 2 * origin + yo, core, pl.ds(self.cut, self.rows - self.cut)]
            return remote(part, part, dx_send.at[self.n, origin], dx_recv.at[self.n, origin], x_side)

        def half_y(self, origin, xo, yo):
            part = self.out.at[xo, 2 * origin + yo, core, pl.ds(0, self.cut)]
            return remote(part, part, dy_send.at[self.n, origin], dy_recv.at[self.n, origin], y_side)

        def spread(self, origin):
            self.move_x(origin).start()
            self.move_y(origin).start()
            self.share(x, origin, y).start()

        def from_sides(self, origin):
            self.move_x(origin).wait_recv()
            self.half_y(origin, 1 - x, y).start()
            self.share(1 - x, origin, y).start()
            self.move_y(origin).wait_recv()
            self.half_x(origin, x, 1 - y).start()
            self.share(x, origin, 1 - y).start()

        def from_diagonal(self, origin):
            self.half_x(origin, 1 - x, 1 - y).wait_recv()
            self.half_y(origin, 1 - x, 1 - y).wait_recv()
            self.share(1 - x, origin, 1 - y).start()

        def each(self, step, action):
            if step == 0:
                action(z)
            else:
                pl.when(z >= step)(lambda: action(z - step))
                pl.when(z + step <= 3)(lambda: action(z + step))

        def step(self, k):
            if k == 0:
                pl.when(z < 3)(lambda: self.move_z(z, up, 0).start())
                pl.when(z > 0)(lambda: self.move_z(z, down, 1).start())
                self.spread(z)
            elif k < 4:

                @pl.when(z >= k)
                def _():
                    self.move_z(z - k, up, 0).wait_recv()
                    pl.when(z < 3)(lambda: self.move_z(z - k, up, 0).start())
                    self.spread(z - k)

                @pl.when(z + k <= 3)
                def _():
                    self.move_z(z + k, down, 1).wait_recv()
                    pl.when(z > 0)(lambda: self.move_z(z + k, down, 1).start())
                    self.spread(z + k)

            if 1 <= k < 5:
                self.each(k - 1, self.from_sides)
            if k >= 2:
                self.each(k - 2, self.from_diagonal)

        def close(self):
            for origin in range(4):
                self.move_x(origin).wait_send()
                self.move_y(origin).wait_send()
                self.half_x(origin, x, 1 - y).wait_send()
                self.half_y(origin, 1 - x, y).wait_send()
                pl.when((z < 3) & (origin <= z))(lambda: self.move_z(origin, up, 0).wait_send())
                pl.when((z > 0) & (origin >= z))(lambda: self.move_z(origin, down, 1).wait_send())
            self.close_shares()

        def close_shares(self):
            for origin in range(4):
                for xo in range(2):
                    for yo in range(2):
                        self.share(xo, origin, yo).wait_send()
                        theirs = self.out.at[xo, 2 * origin + yo, 1 - core]
                        at = 8 * xo + 2 * origin + yo
                        remote(theirs, theirs, s_send.at[self.n, at], s_recv.at[self.n, at], sibling).wait_recv()

    class Late(Stream):
        def column_z(self, xo, origin, yo, target, way):
            block = self.block(xo, origin, yo)
            at = 2 * xo + yo
            return remote(
                block, block, lz_send.at[way, at, origin], lz_recv.at[at, origin], target
            )

        def leave(self, xo, yo):
            pl.when(z < 3)(lambda: self.column_z(xo, z, yo, up, 0).start())
            pl.when(z > 0)(lambda: self.column_z(xo, z, yo, down, 1).start())
            self.share(xo, z, yo).start()

        def step(self, k):
            if k == 0:
                self.move_x(z).start()
                self.move_y(z).start()
                self.leave(x, y)
            elif k == 1:
                self.move_x(z).wait_recv()
                self.half_y(z, 1 - x, y).start()
                self.leave(1 - x, y)
                self.move_y(z).wait_recv()
                self.half_x(z, x, 1 - y).start()
                self.leave(x, 1 - y)
            elif k == 2:
                self.half_x(z, 1 - x, 1 - y).wait_recv()
                self.half_y(z, 1 - x, 1 - y).wait_recv()
                self.leave(1 - x, 1 - y)
            else:
                gap = k - 2

                @pl.when(z >= gap)
                def _():
                    for xo, yo in columns:
                        self.column_z(xo, z - gap, yo, up, 0).wait_recv()
                        pl.when(z < 3)(lambda: self.column_z(xo, z - gap, yo, up, 0).start())
                        self.share(xo, z - gap, yo).start()

                @pl.when(z + gap <= 3)
                def _():
                    for xo, yo in columns:
                        self.column_z(xo, z + gap, yo, down, 1).wait_recv()
                        pl.when(z > 0)(lambda: self.column_z(xo, z + gap, yo, down, 1).start())
                        self.share(xo, z + gap, yo).start()

        def close(self):
            self.move_x(z).wait_send()
            self.move_y(z).wait_send()
            self.half_x(z, x, 1 - y).wait_send()
            self.half_y(z, 1 - x, y).wait_send()
            for origin in range(4):
                for xo, yo in columns:
                    pl.when((z < 3) & (origin <= z))(
                        lambda: self.column_z(xo, origin, yo, up, 0).wait_send())
                    pl.when((z > 0) & (origin >= z))(
                        lambda: self.column_z(xo, origin, yo, down, 1).wait_send())
            self.close_shares()

    columns = ((x, y), (1 - x, y), (x, 1 - y), (1 - x, 1 - y))
    bulk = Stream(0, all_big, BULK_CUT)
    light = Late(1, all_small, LIGHT_CUT)

    def early_copy(step):
        target = lax.rem(me.dp + step, 8)
        return remote(
            small.at[target], early.at[step], early_send.at[step], early_recv.at[step],
            {"dp": target, "pipe": me.pipe},
        )

    big_half = all_big.at[x, me.dp, 1]
    big_first = remote(big.at[pl.ds(BIG_HALF, BIG_HALF)], big_half, first_send.at[0], first_recv.at[0], sibling)
    small_half = all_small.at[x, me.dp, 0]
    small_first = remote(chunk.at[pl.ds(0, SMALL_HALF)], small_half, first_send.at[1], first_recv.at[1], sibling)

    @pl.when(core == 0)
    def _():
        big_first.start()
        copy = pltpu.make_async_copy(big.at[pl.ds(0, BIG_HALF)], all_big.at[x, me.dp, 0], own_sem.at[0])
        copy.start()
        copy.wait()

    @pl.when(core == 1)
    def _():
        for step in range(1, 8):
            early_copy(step).start()
        pltpu.make_async_copy(small.at[me.dp], early.at[0], own_sem.at[1]).start()
        big_first.wait_recv()

    bulk.step(0)
    row = pltpu.make_async_copy(ids, table.at[me.pipe], own_sem.at[2])
    row.start()
    for step in range(1, 4):
        remote(
            ids, table.at[me.pipe], id_send.at[step], id_recv.at[step],
            {"dp": me.dp, "pipe": lax.rem(me.pipe + step, 4)},
        ).start()

    @pl.when(core == 0)
    def _():
        small_first.wait_recv()

    @pl.when(core == 1)
    def _():
        pltpu.make_async_copy(small.at[me.dp], early.at[0], own_sem.at[1]).wait()
        for step in range(1, 8):
            early_copy(step).wait()

        @pl.loop(0, 6)
        def _(i):
            part = pl.ds(pl.multiple_of(176 * i, 16), 176)
            total = early[0, part, :].astype(FULL)
            for step in range(1, 8):
                total = total + early[step, part, :].astype(FULL)
            chunk[part, :] = total.astype(LOW)

        small_first.start()
        copy = pltpu.make_async_copy(chunk.at[pl.ds(SMALL_HALF, SMALL_HALF)], all_small.at[x, me.dp, 1], own_sem.at[0])
        copy.start()
        copy.wait()

    light.step(0)
    for k, light_steps in ((1, (1,)), (2, (2, 3)), (3, (4,)), (4, (5,)), (5, ())):
        bulk.step(k)
        for light_step in light_steps:
            light.step(light_step)
    bulk.close()
    light.close()
    row.wait()
    for step in range(1, 4):
        here = lax.rem(me.pipe + 4 - step, 4)
        move = remote(
            ids, table.at[here], id_send.at[step], id_recv.at[step],
            {"dp": me.dp, "pipe": lax.rem(me.pipe + step, 4)},
        )
        move.wait_recv()
        move.wait_send()

    @pl.when(core == 0)
    def _():
        big_first.wait_send()

    @pl.when(core == 1)
    def _():
        small_first.wait_send()


def gather_all(big, small, ids):
    sem = pltpu.SemaphoreType.DMA
    return pl.pallas_call(
        gather_kernel,
        name="gather_all",
        out_shape=(
            jax.ShapeDtypeStruct((2, 8, 2, BIG_HALF, 128), LOW),
            jax.ShapeDtypeStruct((2, 8, 2, SMALL_HALF, 128), LOW),
            jax.ShapeDtypeStruct((4, 8, 128), jnp.int32),
        ),
        in_specs=[any_spec()] * 3,
        out_specs=(any_spec(),) * 3,
        scratch_shapes=[
            pltpu.VMEM((8, SMALL_ROWS, 128), LOW),
            pltpu.VMEM((SMALL_ROWS, 128), LOW),
            sem((8,)), sem((8,)),
            sem((2, 2, 4)), sem((2, 4)),
            sem((2, 4)), sem((2, 4)), sem((2, 4)), sem((2, 4)),
            sem((2, 4)), sem((2, 4)), sem((2, 4)), sem((2, 4)),
            sem((2, 16)), sem((2, 16)),
            sem((2,)), sem((2,)), sem((3,)), sem((4,)), sem((4,)), sem((2, 4, 4)), sem((4, 4)),
        ],
        compiler_params=pltpu.CompilerParams(
            collective_id=0, has_side_effects=True, vmem_limit_bytes=60 << 20
        ),
    )(big.reshape(WINDOW * TILE, 128), small.reshape(8, SMALL_ROWS, 128), ids)


def soft(value):
    return jnp.maximum(value, 0.0) + jnp.log1p(jnp.exp(-jnp.abs(value)))


def gate_of(value):
    small = jnp.exp(-jnp.abs(value))
    share = 1.0 / (1.0 + small)
    return jnp.where(value >= 0, share, small * share)


def standardize(z):
    count = z.shape[0]
    centre = jnp.sum(z, axis=0, keepdims=True) / count
    away = z - centre
    spread = jnp.sum(away * away, axis=0, keepdims=True) / count
    inverse = lax.rsqrt(spread + NORM_EPS)
    return away * inverse, centre, spread, inverse


def unstandardize(grad, standard, gain, inverse):
    count = grad.shape[0]
    grad_sum = jnp.sum(grad, axis=0, keepdims=True)
    grad_dot = jnp.sum(grad * standard, axis=0, keepdims=True)
    result = gain * inverse * (grad - grad_sum / count - standard * (grad_dot / count))
    return result, grad_dot, grad_sum


def pad_low(value):
    zeros = jnp.zeros((PADDED - ROWS, value.shape[1]), FULL)
    return jnp.concatenate([value, zeros], axis=0).astype(LOW)


def mul(a, b):
    return jnp.dot(a, b, preferred_element_type=FULL)


def mul_t(a, b):
    return lax.dot_general(a, b, (((1,), (1,)), ((), ())), preferred_element_type=FULL)


def narrow_part(ref, start, count, blocks=range(4)):
    return jnp.concatenate(
        [ref[pl.ds(start, count), 64 * j : 64 * j + 64, :].reshape(64 * count, 128) for j in blocks],
        axis=1,
    )


def put_narrow(ref, start, count, value):
    for j in range(4):
        ref[pl.ds(start, count), 64 * j : 64 * j + 64, :] = (
            value[:, 128 * j : 128 * j + 128].astype(LOW).reshape(count, 64, 128)
        )


def wide_part(ref, start, count, c):
    return jnp.concatenate(
        [
            ref[start : start + count, pl.ds(pl.multiple_of(32 * c + 16 * h, 16), 16), :].reshape(
                16 * count, 128
            )
            for h in range(2)
        ],
        axis=1,
    )


def put_wide(ref, start, count, c, value):
    for h in range(2):
        ref[start : start + count, pl.ds(pl.multiple_of(32 * c + 16 * h, 16), 16), :] = (
            value[:, 128 * h : 128 * h + 128].astype(LOW).reshape(count, 16, 128)
        )


def step_kernel(table, gates, teach_ids, stud_ids, all_big, all_small, x, targets, grid,
                wide0, wide1, final, stats, grad_x, out_big, out_small,
                w0, w1, w2, w3, edges, vec, grad_vec, raw,
                std_a, std_b, std_p, std_1, std_c, std_d, hidden, cols0, cols2,
                nar0, nar2, turned, relay, dz_a, dz_n, acc, acc_x, grad_h,
                wanted, inv, in_sem, edge_sem, out_sem):
    rank = lax.axis_index("pipe")
    gate = gates[rank].astype(FULL)
    for group in range(2):
        for j in range(8):
            inv[8 * group + table[2 * group, 0, j]] = j
    picks = [teach_ids[rank, k] for k in range(2)] + [stud_ids[rank, k] for k in range(3)]
    rows = [
        pltpu.make_async_copy(targets.at[pl.ds(pick, 1)], wanted.at[pl.ds(k, 1)], edge_sem.at[12 + k])
        for k, pick in enumerate(picks)
    ]
    for fetched in rows:
        fetched.start()
    weights = (w0, w1, w2, w3)
    loads = {0: [], 1: [], 2: [], 3: []}
    for group, weight, blocks in ((0, w0, 8), (1, w2, 6)):
        for b in range(blocks):
            first, here = 19 * b, inv[8 * group + b]
            at = 8 * group + b
            loads[2 * group].append(pltpu.make_async_copy(
                all_big.at[group, here, 0], weight.at[pl.ds(first, 10)], in_sem.at[0, at]))
            if first + 10 < USED_TILES[2 * group]:
                count = 10 if b == 7 else 9
                loads[2 * group].append(pltpu.make_async_copy(
                    all_big.at[group, here, 1, pl.ds(0, count)], weight.at[pl.ds(first + 10, count)],
                    in_sem.at[1, at]))
            if b < blocks - 1:
                at = 7 * group + b
                loads[2 * group].append(pltpu.make_async_copy(
                    all_big.at[group, here, 1, pl.ds(9, 1)], edges.at[pl.ds(at, 1)], edge_sem.at[at]))
    loads[1].append(pltpu.make_async_copy(all_small.at[0], w1, in_sem.at[0, 14]))
    loads[3].append(pltpu.make_async_copy(all_small.at[1], w3, in_sem.at[0, 15]))
    for section in range(4):
        for load in loads[section]:
            load.start()

    raw[...] = jnp.zeros_like(raw)
    grad_vec[...] = jnp.zeros_like(grad_vec)

    def settle(section):
        for load in loads[section]:
            load.wait()
        if section == 0:
            for b in range(7):
                w0[19 * b + 19] = (w0[19 * b + 19].astype(FULL) + edges[b].astype(FULL)).astype(LOW)
        if section == 2:
            for b in range(5):
                w2[19 * b + 19] = (
                    w2[19 * b + 19].astype(FULL) + edges[7 + b].astype(FULL)
                ).astype(LOW)
        vec[section] = weights[section][VEC_TILE[section], 0:48, :].astype(FULL)

    def row(section, start):
        return jnp.concatenate(
            [vec[section, pl.ds(start + h, 1), :] for h in range(2)], axis=1
        )

    def put_row(section, start, value):
        for h in range(2):
            grad_vec[section, pl.ds(start + h, 1), :] = value[:, 128 * h : 128 * h + 128]

    def put_stats(section, column, centre, spread):
        raw[2 * section : 2 * section + 1, pl.ds(column, 256)] = centre
        raw[2 * section + 1 : 2 * section + 2, pl.ds(column, 256)] = spread

    def inverse_of(section, column):
        return lax.rsqrt(raw[2 * section + 1 : 2 * section + 2, pl.ds(column, 256)] + NORM_EPS)

    def lanes(c):
        return pl.ds(pl.multiple_of(256 * c, 256), 256)

    at_row, at_col, side = grid[0], grid[1], grid[2]

    def masked(value, dr, dc):
        ok = (at_row + dr >= 0) & (at_row + dr < side) & (at_col + dc >= 0) & (at_col + dc < side)
        return jnp.concatenate(
            [jnp.where(ok, value[:, 128 * j : 128 * j + 128], 0.0) for j in range(4)], axis=1
        )

    def rolled(value, sign, dr, dc):
        parts = []
        for start, end, width in ((0, TEACH_ROWS, 6), (TEACH_ROWS, ROWS, 4)):
            by = (sign * (dr * width + dc)) % (end - start)
            part = value[start:end]
            parts.append(part if by == 0 else pltpu.roll(part, by, 0))
        return jnp.concatenate(parts, axis=0)

    def taps(stride):
        for t in range(9):
            r, q = t // 3, t % 3
            if stride == 1:
                yield t, 0, r - 1, q - 1
            else:
                phase = 2 * (1 if r != 1 else 0) + (1 if q != 1 else 0)
                yield t, phase, -1 if r == 0 else 0, -1 if q == 0 else 0

    settle(0)
    whole_x = x[...].reshape(4 * PADDED, C_IN)
    for c in range(2):
        z = mul(whole_x, narrow_part(w0, 0, 16, (2 * c, 2 * c + 1)))
        z = jnp.concatenate([z[PADDED * p : PADDED * p + ROWS] for p in range(4)], axis=0)
        standard, centre, spread, _ = standardize(z)
        put_stats(0, 256 * c, centre, spread)
        std_a[:, 256 * c : 256 * c + 256] = standard
        hidden[:, 256 * c : 256 * c + 256] = (
            soft(row(0, 2 * c) * standard + row(0, 4 + 2 * c)).astype(LOW).astype(FULL)
        )

    for t, phase, dr, dc in taps(2):
        cols0[t] = pad_low(masked(rolled(hidden[ROWS * phase : ROWS * phase + ROWS, :], -1, dr, dc), dr, dc))
    acc[...] = jnp.zeros_like(acc)

    @pl.loop(0, 9)
    def _(t):
        acc[...] += mul(cols0[t], narrow_part(w0, 16 + 8 * t, 8))

    def middle(section, std, nar):
        for c in range(2):
            at = slice(256 * c, 256 * c + 256)
            standard, centre, spread, _ = standardize(acc[0:ROWS, at])
            put_stats(section, MID + 256 * c, centre, spread)
            std[:, at] = standard
            nar[:, at] = pad_low(soft(row(section, 8 + 2 * c) * standard + row(section, 12 + 2 * c)))

    middle(0, std_b, nar0)
    acc[...] = jnp.zeros_like(acc)
    settle(1)
    settle(2)

    @pl.loop(0, 8)
    def _(c):
        at = lanes(c)
        standard, centre, spread, _ = standardize(mul(x[0], wide_part(w0, FRONT_WIDE, 64, c))[0:ROWS])
        put_stats(0, 2 * MID + pl.multiple_of(256 * c, 256), centre, spread)
        std_p[:, at] = standard
        low = pad_low(row(0, 16 + 2 * c) * standard + row(0, 32 + 2 * c))
        wide0[:, at] = low
        standard, centre, spread, _ = standardize(mul(nar0[...], wide_part(w1, 0, 32, c))[0:ROWS])
        put_stats(1, pl.multiple_of(256 * c, 256), centre, spread)
        std_1[:, at] = standard
        pre = low.astype(FULL)[0:ROWS] + row(1, 2 * c) * standard + row(1, 16 + 2 * c)
        low = pad_low(soft(pre))
        wide1[:, at] = low
        acc[...] += mul(low, narrow_part(w2, 4 * c, 4))

    for c in range(2):
        at = slice(256 * c, 256 * c + 256)
        standard, centre, spread, _ = standardize(acc[0:ROWS, at])
        put_stats(2, 256 * c, centre, spread)
        std_c[:, at] = standard
        hidden[0:ROWS, at] = soft(row(2, 2 * c) * standard + row(2, 4 + 2 * c)).astype(LOW).astype(FULL)
    for t, phase, dr, dc in taps(1):
        cols2[t] = pad_low(masked(rolled(hidden[0:ROWS, :], -1, dr, dc), dr, dc))
    acc[...] = jnp.zeros_like(acc)

    @pl.loop(0, 9)
    def _(t):
        acc[...] += mul(cols2[t], narrow_part(w2, 32 + 8 * t, 8))

    middle(2, std_d, nar2)

    turned[...] = nar2[...].T
    acc[...] = jnp.zeros_like(acc)
    settle(3)
    for fetched in rows:
        fetched.wait()

    def spread_rows(values):
        head = lax.broadcasted_iota(jnp.int32, (8, 256), 0) < 4
        first, second = (jnp.broadcast_to(value, (8, 256)) for value in values[0:2])
        parts = [jnp.broadcast_to(values[0], (32, 256)), jnp.where(head, first, second)]
        parts.append(jnp.broadcast_to(values[1], (32, 256)))
        parts.extend(jnp.broadcast_to(value, (16, 256)) for value in values[2:5])
        return jnp.concatenate(parts, axis=0)

    def crop_sums(value):
        head = lax.broadcasted_iota(jnp.int32, (8, 256), 0) < 4
        between = value[32:40]

        def total(part):
            return jnp.sum(part, axis=0, keepdims=True)

        return [
            total(value[0:32]) + total(jnp.where(head, between, 0.0)),
            total(value[40:72]) + total(jnp.where(head, 0.0, between)),
            total(value[72:88]),
            total(value[88:104]),
            total(value[104:120]),
        ]

    @pl.loop(0, 8)
    def _(c):
        at = lanes(c)
        weight = wide_part(w3, 0, 32, c)
        standard, centre, spread, inverse = standardize(mul(nar2[...], weight)[0:ROWS])
        put_stats(3, pl.multiple_of(256 * c, 256), centre, spread)
        gain = row(3, 2 * c)
        before = wide1[:, at].astype(FULL)[0:ROWS]
        pre = before + gain * standard + row(3, 16 + 2 * c)
        ending = jnp.where(gate > 0, soft(pre), before)
        final[:, at] = pad_low(ending)
        square = ending * ending
        factors = []
        for crop, total in enumerate(crop_sums(square * ending)):
            mean = total / (36.0 if crop < 2 else 16.0) + POOL_EPS
            factors.append(jnp.exp(jnp.log(mean) * (-2.0 / 3.0)) * wanted[crop : crop + 1, at])
        cotangent = spread_rows(factors) * square
        grad_pre = cotangent * gate_of(pre) * gate
        relay[:, at] = pad_low(grad_pre + cotangent * (1.0 - gate))
        result, grad_gain, grad_bias = unstandardize(grad_pre, standard, gain, inverse)
        put_row(3, 2 * c, grad_gain)
        put_row(3, 16 + 2 * c, grad_bias)
        low = pad_low(result)
        acc[...] += mul_t(low, weight)
        put_wide(w3, 0, 32, c, mul(turned[...], low))

    def flush(section):
        weights[section][VEC_TILE[section]] = grad_vec[section].astype(LOW)

    flush(3)
    stores = [pltpu.make_async_copy(w3, out_small.at[1], out_sem.at[15])]
    stores[-1].start()

    def middle_back(section, std):
        for c in range(2):
            at = slice(256 * c, 256 * c + 256)
            gain, bias = row(section, 8 + 2 * c), row(section, 12 + 2 * c)
            grad = acc[0:ROWS, at].astype(LOW).astype(FULL) * gate_of(gain * std[:, at] + bias)
            result, grad_gain, grad_bias = unstandardize(
                grad, std[:, at], gain, inverse_of(section, MID + 256 * c)
            )
            put_row(section, 8 + 2 * c, grad_gain)
            put_row(section, 12 + 2 * c, grad_bias)
            dz_n[:, at] = pad_low(result)

    def taps_back(weight, start, cols, stride, phases):
        grad_h[0 : ROWS * phases, :] = jnp.zeros((ROWS * phases, MID), FULL)
        for t, phase, dr, dc in taps(stride):
            part = mul_t(dz_n[...], narrow_part(weight, start + 8 * t, 8))[0:ROWS]
            at = slice(ROWS * phase, ROWS * phase + ROWS)
            grad_h[at, :] += rolled(masked(part, dr, dc), 1, dr, dc)
            put_narrow(weight, start + 8 * t, 8, mul(cols[t].T, dz_n[...]))

    middle_back(2, std_d)
    taps_back(w2, 32, cols2, 1, 1)
    for c in range(2):
        at = slice(256 * c, 256 * c + 256)
        gain, bias = row(2, 2 * c), row(2, 4 + 2 * c)
        grad = grad_h[0:ROWS, at] * gate_of(gain * std_c[:, at] + bias)
        result, grad_gain, grad_bias = unstandardize(grad, std_c[:, at], gain, inverse_of(2, 256 * c))
        put_row(2, 2 * c, grad_gain)
        put_row(2, 4 + 2 * c, grad_bias)
        dz_n[:, at] = pad_low(result)
    turned[...] = nar0[...].T
    acc[...] = jnp.zeros_like(acc)
    acc_x[...] = jnp.zeros_like(acc_x)

    @pl.loop(0, 8)
    def _(c):
        at = lanes(c)
        low = dz_n[...]
        grad = relay[:, at].astype(FULL) + mul_t(low, narrow_part(w2, 4 * c, 4))
        put_narrow(w2, 4 * c, 4, mul(wide1[:, at].T, low))
        grad = grad.astype(LOW).astype(FULL)[0:ROWS]
        gain = row(1, 2 * c)
        pre = wide0[:, at].astype(FULL)[0:ROWS] + gain * std_1[:, at] + row(1, 16 + 2 * c)
        grad = grad * gate_of(pre)
        result, grad_gain, grad_bias = unstandardize(
            grad, std_1[:, at], gain, inverse_of(1, pl.multiple_of(256 * c, 256))
        )
        put_row(1, 2 * c, grad_gain)
        put_row(1, 16 + 2 * c, grad_bias)
        low = pad_low(result)
        acc[...] += mul_t(low, wide_part(w1, 0, 32, c))
        put_wide(w1, 0, 32, c, mul(turned[...], low))
        grad = grad.astype(LOW).astype(FULL)
        result, grad_gain, grad_bias = unstandardize(
            grad, std_p[:, at], row(0, 16 + 2 * c), inverse_of(0, 2 * MID + pl.multiple_of(256 * c, 256))
        )
        put_row(0, 16 + 2 * c, grad_gain)
        put_row(0, 32 + 2 * c, grad_bias)
        low = pad_low(result)
        acc_x[...] += mul_t(low, wide_part(w0, FRONT_WIDE, 64, c))
        put_wide(w0, FRONT_WIDE, 64, c, mul(x[0].T, low))

    flush(1)
    flush(2)
    w2[105:115] = jnp.zeros((10, TILE, 128), LOW)
    stores.append(pltpu.make_async_copy(w1, out_small.at[0], out_sem.at[14]))
    stores[-1].start()
    for b in range(8):
        if b < 6:
            stores.append(pltpu.make_async_copy(
                w2.at[pl.ds(19 * b, 20)], out_big.at[1, inv[8 + b]], out_sem.at[8 + b]))
            stores[-1].start()
        else:
            for h in range(2):
                stores.append(pltpu.make_async_copy(
                    w2.at[pl.ds(105, 10)], out_big.at[1, inv[8 + b], pl.ds(10 * h, 10)],
                    out_sem.at[16 + 2 * (b - 6) + h]))
                stores[-1].start()

    middle_back(0, std_b)
    taps_back(w0, 16, cols0, 2, 4)
    for c in range(2):
        at = slice(256 * c, 256 * c + 256)
        gain, bias = row(0, 2 * c), row(0, 4 + 2 * c)
        grad = grad_h[:, at] * gate_of(gain * std_a[:, at] + bias)
        result, grad_gain, grad_bias = unstandardize(grad, std_a[:, at], gain, inverse_of(0, 256 * c))
        put_row(0, 2 * c, grad_gain)
        put_row(0, 4 + 2 * c, grad_bias)
        for p in range(4):
            dz_a[PADDED * p : PADDED * p + PADDED, at] = pad_low(result[ROWS * p : ROWS * p + ROWS])

    @pl.loop(0, 4)
    def _(c):
        at = lanes(c)
        low = dz_a[...]
        part = mul_t(low, narrow_part(w0, 4 * c, 4))
        grad_x[0, :, at] = (part[0:PADDED] + acc_x[:, at]).astype(LOW)
        for p in range(1, 4):
            grad_x[p, :, at] = part[PADDED * p : PADDED * p + PADDED].astype(LOW)
        turned_x = x[:, :, at].reshape(4 * PADDED, 256).T
        put_narrow(w0, 4 * c, 4, mul(turned_x, low))

    flush(0)
    for b in range(8):
        stores.append(pltpu.make_async_copy(
            w0.at[pl.ds(19 * b, 20)], out_big.at[0, inv[b]], out_sem.at[b]))
        stores[-1].start()
    for section in range(4):
        part = raw[2 * section : 2 * section + 2]
        stats[section, 0:2] = part if section < 2 else part * gate
        stats[section, 2:8] = jnp.zeros((6, 2 * MID + C_OUT), FULL)
    for store in stores:
        store.wait()


def run_step(table, gates, teach_ids, stud_ids, all_big, all_small, phases, targets):
    spots = np.zeros((3, ROWS, 128), np.int32)
    for r in range(ROWS):
        width = 6 if r < TEACH_ROWS else 4
        at = r % 36 if r < TEACH_ROWS else (r - TEACH_ROWS) % 16
        spots[0, r], spots[1, r], spots[2, r] = at // width, at % width, width
    sem = pltpu.SemaphoreType.DMA
    wide = jax.ShapeDtypeStruct((PADDED, C_OUT), LOW)
    vm = pltpu.VMEM
    return pl.pallas_call(
        step_kernel,
        name="step",
        out_shape=(
            wide, wide, wide,
            jax.ShapeDtypeStruct((4, 8, 2 * MID + C_OUT), FULL),
            jax.ShapeDtypeStruct((4, PADDED, C_IN), LOW),
            jax.ShapeDtypeStruct((2, 8, WINDOW, TILE, 128), LOW),
            jax.ShapeDtypeStruct((2, USED_TILES[1], TILE, 128), LOW),
        ),
        in_specs=[smem_spec()] * 4 + [any_spec(), any_spec(), vmem_spec(), any_spec(), vmem_spec()],
        out_specs=(vmem_spec(),) * 5 + (any_spec(),) * 2,
        scratch_shapes=[
            vm((153, TILE, 128), LOW), vm((33, TILE, 128), LOW), vm((115, TILE, 128), LOW), vm((33, TILE, 128), LOW),
            vm((12, TILE, 128), LOW), vm((4, 48, 128), FULL), vm((4, TILE, 128), FULL),
            vm((8, 2 * MID + C_OUT), FULL),
            vm((4 * ROWS, MID), FULL), vm((ROWS, MID), FULL), vm((ROWS, C_OUT), FULL), vm((ROWS, C_OUT), FULL),
            vm((ROWS, MID), FULL), vm((ROWS, MID), FULL), vm((4 * ROWS, MID), FULL),
            vm((9, PADDED, MID), LOW), vm((9, PADDED, MID), LOW),
            vm((PADDED, MID), LOW), vm((PADDED, MID), LOW), vm((MID, PADDED), LOW),
            vm((PADDED, C_OUT), LOW), vm((4 * PADDED, MID), LOW), vm((PADDED, MID), LOW),
            vm((PADDED, MID), FULL), vm((PADDED, C_IN), FULL), vm((4 * ROWS, MID), FULL),
            vm((8, C_OUT), FULL), pltpu.SMEM((16,), jnp.int32),
            sem((2, 16)), sem((17,)), sem((20,)),
        ],
        compiler_params=pltpu.CompilerParams(vmem_limit_bytes=60 << 20),
    )(table, gates, teach_ids, stud_ids, all_big, all_small, phases, targets, jnp.asarray(spots))


def reduce_kernel(big, small, wide0, wide1, final, stats, table,
                  out_big, out_small, segments, out_stats, norm, factor,
                  got, halves_x, halves_y, from_x, from_y, from_low, from_high, stage, total,
                  l_got, l_stage, l_low, l_high, l_halves_x, l_halves_y, l_from_x, l_from_y, l_total,
                  late, late_half, owner_row, by_pipe, by_dp, mine, part_sum,
                  s_send, s_recv, hx_send, hx_recv, hy_send, hy_recv, x_send, x_recv, y_send, y_recv,
                  zu_send, zu_recv, zd_send, zd_recv, lu_send, lu_recv, ld_send, ld_recv,
                  stage_sem, l_stage_sem, out_sem, late_send, late_recv, join_send, join_recv,
                  seg_send, seg_recv, stat_send, stat_recv, p_send, p_recv, d_send, d_recv):
    me = Place()
    me.enter()
    x, y, z, core = me.x, me.y, me.z, me.core
    up, down = me.device(z=z + 1), me.device(z=z - 1)
    x_side, y_side, sibling = me.device(x=1 - x), me.device(y=1 - y), me.device(core=1 - core)
    order = [
        jnp.where(z < 2, 3, 0),
        jnp.where(z == 0, 2, jnp.where(z == 1, 0, jnp.where(z == 2, 3, 1))),
        jnp.where(z == 0, 1, jnp.where(z == 1, 2, jnp.where(z == 2, 1, 2))),
        z,
    ]
    columns = ((1 - x, 1 - y), (x, 1 - y), (1 - x, y), (x, y))
    sides = [[(1, k), (2, k)] for k in range(4)]
    sequence = [(0, 0), (0, 1), (0, 2), (0, 3)] + sides[0] + sides[1] + [(3, 0)] + sides[2]
    sequence += [(3, 1)] + sides[3] + [(3, 2), (3, 3)]
    l_sequence = [(group, k) for k in range(4) for group in range(4)]

    def all_of(copies, act):
        for copy in copies:
            act(copy)

    def over(start, count, piece):
        whole = count // 512
        if whole:

            @pl.loop(0, whole)
            def _(i):
                piece(pl.multiple_of(start + 512 * i, 16), 512)

        if count % 512:
            piece(start + 512 * whole, count % 512)

    def source(array, group, k, half):
        xo, yo = columns[group]
        return array.at[xo, 2 * order[k] + yo, half]

    def share(group, k):
        at = 4 * group + k
        return remote(source(big, group, k, 1 - core), got.at[at], s_send.at[0, at], s_recv.at[0, at], sibling)

    def l_share(group, k):
        at = 4 * group + k
        return remote(source(small, group, k, 1 - core), l_got.at[at], s_send.at[1, at], s_recv.at[1, at], sibling)

    def fetch(n):
        return pltpu.make_async_copy(source(big, *sequence[n], core), stage.at[n % 4], stage_sem.at[n % 4])

    def l_fetch(group, k):
        at = 4 * group + k
        return pltpu.make_async_copy(source(small, group, k, core), l_stage.at[at], l_stage_sem.at[at])

    def add(target, at, other, slot, start, count, extras):
        def piece(begin, size):
            part = pl.ds(begin, size)
            sums = target[at, part, :].astype(FULL) + other[slot, part, :].astype(FULL)
            for ref, k in extras:
                sums = sums + ref[k, pl.ds(begin - start, size), :].astype(FULL)
            target[at, part, :] = sums.astype(LOW)

        over(start, count, piece)

    def send_half_x(k):
        return remote(got.at[k, pl.ds(BACK_CUT, BIG_HALF - BACK_CUT)], halves_x.at[k],
                      hx_send.at[k], hx_recv.at[k], x_side)

    def send_half_y(k):
        return remote(got.at[k, pl.ds(0, BACK_CUT)], halves_y.at[k], hy_send.at[k], hy_recv.at[k], y_side)

    def send_y(k):
        return remote(got.at[4 + k], from_y.at[k], y_send.at[k], y_recv.at[k], y_side)

    def send_x(k):
        return remote(got.at[8 + k], from_x.at[k], x_send.at[k], x_recv.at[k], x_side)

    def send_up(at, zd):
        return remote(got.at[at], from_low.at[zd - 1], zu_send.at[zd - 1], zu_recv.at[zd - 1], up)

    def send_down(at, zd):
        return remote(got.at[at], from_high.at[zd], zd_send.at[zd], zd_recv.at[zd], down)

    def l_column(group):
        xo, yo = columns[group]
        return 2 * xo + yo

    def l_up(group, k):
        at, zd = l_column(group), order[k] - 1
        return remote(l_got.at[4 * group + k], l_low.at[at, zd], lu_send.at[at, zd], lu_recv.at[at, zd], up)

    def l_down(group, k):
        at, zd = l_column(group), order[k]
        return remote(l_got.at[4 * group + k], l_high.at[at, zd], ld_send.at[at, zd], ld_recv.at[at, zd], down)

    def l_half_x():
        return remote(l_got.at[3, pl.ds(LIGHT_CUT, SMALL_HALF - LIGHT_CUT)], l_halves_x,
                      hx_send.at[4], hx_recv.at[4], x_side)

    def l_half_y():
        return remote(l_got.at[3, pl.ds(0, LIGHT_CUT)], l_halves_y, hy_send.at[4], hy_recv.at[4], y_side)

    def l_send_y():
        return remote(l_got.at[7], l_from_y, y_send.at[4], y_recv.at[4], y_side)

    def l_send_x():
        return remote(l_got.at[11], l_from_x, x_send.at[4], x_recv.at[4], x_side)

    leaving = (wide0, wide1, wide1, final)

    def exchange(section):
        target = {"dp": me.dp, "pipe": section}
        yield remote(leaving[section], segments.at[me.pipe], seg_send.at[section], seg_recv.at[me.pipe], target)
        yield remote(stats.at[section], out_stats.at[me.pipe], stat_send.at[section], stat_recv.at[me.pipe], target)

    def keep(section):
        yield pltpu.make_async_copy(leaving[section], segments.at[me.pipe], seg_send.at[section])
        yield pltpu.make_async_copy(stats.at[section], out_stats.at[me.pipe], stat_send.at[section])

    def arriving(micro):
        target = {"dp": me.dp, "pipe": micro}
        yield remote(wide0, segments.at[micro], seg_send.at[micro], seg_recv.at[micro], target)
        yield remote(stats.at[0], out_stats.at[micro], stat_send.at[micro], stat_recv.at[micro], target)

    for n in range(16):
        share(*sequence[n]).start()
        if n == 3:
            for item in l_sequence:
                l_share(*item).start()
    for n in range(2):
        fetch(n).start()
    for group, k in l_sequence:
        l_fetch(group, k).start()
    row_copy = pltpu.make_async_copy(table.at[2 * x], owner_row, out_sem.at[2])
    row_copy.start()

    def bulk_item(n):
        group, k = sequence[n]
        at, slot = 4 * group + k, n % 4
        if n + 2 < 16:
            fetch(n + 2).start()
        fetch(n).wait()
        share(group, k).wait_recv()
        if group == 0:
            add(got, at, stage, slot, 0, BIG_HALF, [])
            send_half_x(k).start()
            send_half_y(k).start()
        elif group == 1:
            send_half_x(k).wait_recv()
            add(got, at, stage, slot, 0, BACK_CUT, [])
            add(got, at, stage, slot, BACK_CUT, BIG_HALF - BACK_CUT, [(halves_x, k)])
            send_y(k).start()
        elif group == 2:
            send_half_y(k).wait_recv()
            add(got, at, stage, slot, 0, BACK_CUT, [(halves_y, k)])
            add(got, at, stage, slot, BACK_CUT, BIG_HALF - BACK_CUT, [])
            send_x(k).start()
        else:
            send_x(k).wait_recv()
            send_y(k).wait_recv()
            add(got, at, stage, slot, 0, BIG_HALF, [(from_x, k), (from_y, k)])

    def bulk_z(k):
        at, zd = 12 + k, order[k]

        @pl.when(zd > z)
        def _():
            @pl.when(z > 0)
            def _():
                send_up(at, zd).wait_recv()
                add(got, at, from_low, zd - 1, 0, BIG_HALF, [])

            send_up(at, zd).start()

        @pl.when(zd < z)
        def _():
            @pl.when(z < 3)
            def _():
                send_down(at, zd).wait_recv()
                add(got, at, from_high, zd, 0, BIG_HALF, [])

            send_down(at, zd).start()

    def light_item(group, k):
        at, zd, column = 4 * group + k, order[k], l_column(group)
        l_fetch(group, k).wait()
        l_share(group, k).wait_recv()
        add(l_got, at, l_stage, at, 0, SMALL_HALF, [])

        def merge(ref, slot):
            l_got[at] = (l_got[at].astype(FULL) + ref[column, slot].astype(FULL)).astype(LOW)

        if k < 3:

            @pl.when(zd > z)
            def _():
                @pl.when(z > 0)
                def _():
                    l_up(group, k).wait_recv()
                    merge(l_low, zd - 1)

                l_up(group, k).start()

            @pl.when(zd < z)
            def _():
                @pl.when(z < 3)
                def _():
                    l_down(group, k).wait_recv()
                    merge(l_high, zd)

                l_down(group, k).start()

        else:

            @pl.when(z > 0)
            def _():
                l_up(group, k).wait_recv()
                merge(l_low, zd - 1)

            @pl.when(z < 3)
            def _():
                l_down(group, k).wait_recv()
                merge(l_high, zd)

            if group == 0:
                l_half_x().start()
                l_half_y().start()

    def light_sides():
        l_half_x().wait_recv()
        l_got[7, LIGHT_CUT:SMALL_HALF, :] = (
            l_got[7, LIGHT_CUT:SMALL_HALF, :].astype(FULL) + l_halves_x[...].astype(FULL)
        ).astype(LOW)
        l_send_y().start()
        l_half_y().wait_recv()
        l_got[11, 0:LIGHT_CUT, :] = (
            l_got[11, 0:LIGHT_CUT, :].astype(FULL) + l_halves_y[...].astype(FULL)
        ).astype(LOW)
        l_send_x().start()

    def light_end():
        l_send_x().wait_recv()
        l_send_y().wait_recv()
        l_total[...] = l_got[15].astype(FULL) + l_from_x[...].astype(FULL) + l_from_y[...].astype(FULL)

    small_join = remote(late_half, late.at[pl.ds(0, SMALL_HALF)], join_send.at[1], join_recv.at[1], sibling)
    own_late = pltpu.make_async_copy(late, out_small.at[me.dp], out_sem.at[1])

    def late_copy(step, slot):
        target = {"dp": lax.rem(me.dp + step, 8), "pipe": me.pipe}
        return remote(late, out_small.at[slot], late_send.at[step], late_recv.at[step], target)

    def leave():
        for section in range(4):
            @pl.when(me.pipe == section)
            def _(section=section):
                all_of(keep(section), lambda copy: copy.start())

            @pl.when(me.pipe != section)
            def _(section=section):
                all_of(exchange(section), lambda copy: copy.start())

    def late_start():
        light_end()

        @pl.when(core == 0)
        def _():
            late_half[...] = l_total[...].astype(LOW)
            small_join.start()

        @pl.when(core == 1)
        def _():
            late[SMALL_HALF:SMALL_ROWS, :] = l_total[...].astype(LOW)
            small_join.wait_recv()
            own_late.start()
            for step in range(1, 8):
                late_copy(step, me.dp).start()

    def light_round(k):
        for item in l_sequence[4 * k : 4 * k + 4]:
            light_item(*item)

    edge = (z == 0) | (z == 3)

    def early_z(k):
        pl.when(edge)(lambda: bulk_z(k))

    def inner_z(k):
        pl.when(jnp.logical_not(edge))(lambda: bulk_z(k))

    for n in range(4):
        bulk_item(n)
    light_round(0)
    for n in range(4, 8):
        bulk_item(n)
    light_round(1)
    light_round(2)
    light_round(3)
    bulk_item(8)
    early_z(0)
    bulk_item(9)
    bulk_item(10)
    light_sides()
    bulk_item(11)
    early_z(1)
    bulk_item(12)
    bulk_item(13)
    late_start()
    inner_z(0)
    leave()
    bulk_item(14)
    early_z(2)
    inner_z(1)
    bulk_item(15)
    inner_z(2)

    row_copy.wait()
    part_sum[...] = jnp.sum((l_total[...] * l_total[...]).reshape(SMALL_HALF // 8, 8, 128), axis=0)
    lane = lax.broadcasted_iota(jnp.int32, (8, 128), 1)
    is_last = jnp.where((lane == me.dp) & (owner_row[...] == 7), 1.0, 0.0)
    weight = jnp.broadcast_to(jnp.sum(is_last, axis=1, keepdims=True), (8, 128))
    weight = jnp.where(core == 0, jnp.ones((8, 128), FULL), weight)

    def end(low, high):
        def piece(begin, size, scale):
            part = pl.ds(begin, size)
            sums = got[15, part, :].astype(FULL)
            if low:
                sums = sums + from_low[z - 1, part, :].astype(FULL)
            if high:
                sums = sums + from_high[z, part, :].astype(FULL)
            total[part, :] = sums
            squares = jnp.sum((sums * sums).reshape(size // 8, 8, 128), axis=0)
            part_sum[...] += squares if scale is None else squares * scale

        over(0, BIG_HALF - 256, lambda begin, size: piece(begin, size, None))
        piece(BIG_HALF - 256, 256, weight)

    @pl.when(z == 0)
    def _():
        send_down(15, z).wait_recv()
        end(False, True)

    @pl.when((z > 0) & (z < 3))
    def _():
        send_up(15, z).wait_recv()
        send_down(15, z).wait_recv()
        end(True, True)

    @pl.when(z == 3)
    def _():
        send_up(15, z).wait_recv()
        end(True, False)

    big_join = remote(total, out_big.at[1], join_send.at[0], join_recv.at[0], sibling)
    own_big = pltpu.make_async_copy(total, out_big.at[0], out_sem.at[0])

    @pl.when(core == 0)
    def _():
        own_big.start()

    @pl.when(core == 1)
    def _():
        big_join.start()

    def along_pipe(step, slot):
        target = {"dp": me.dp, "pipe": lax.rem(me.pipe + step, 4)}
        return remote(part_sum, by_pipe.at[slot], p_send.at[step], p_recv.at[step], target)

    def along_dp(step, slot):
        target = {"dp": lax.rem(me.dp + step, 8), "pipe": me.pipe}
        return remote(mine, by_dp.at[slot], d_send.at[step], d_recv.at[step], target)

    for step in range(1, 4):
        along_pipe(step, me.pipe).start()
    by_pipe[me.pipe] = part_sum[...]
    for step in range(1, 4):
        along_pipe(step, lax.rem(me.pipe + 4 - step, 4)).wait_recv()
    mine[...] = jnp.sum(by_pipe[...], axis=0)
    for step in range(1, 8):
        along_dp(step, me.dp).start()
    by_dp[me.dp] = mine[...]
    for step in range(1, 8):
        along_dp(step, lax.rem(me.dp + 8 - step, 8)).wait_recv()
    whole = jnp.sum(jnp.sum(by_dp[...], axis=0), axis=0, keepdims=True)
    length = jnp.sqrt(jnp.broadcast_to(jnp.sum(whole, axis=1, keepdims=True), (8, 128)))
    norm[...] = length
    factor[...] = jnp.minimum(1.0, CLIP_NORM / length)

    @pl.when(core == 0)
    def _():
        own_big.wait()
        big_join.wait_recv()
        small_join.wait_send()

    @pl.when(core == 1)
    def _():
        big_join.wait_send()
        own_late.wait()
        for step in range(1, 8):
            late_copy(step, lax.rem(me.dp + 8 - step, 8)).wait_recv()
            late_copy(step, me.dp).wait_send()

    for other in range(4):
        @pl.when(me.pipe == other)
        def _(other=other):
            all_of(keep(other), lambda copy: copy.wait())

        @pl.when(me.pipe != other)
        def _(other=other):
            all_of(exchange(other), lambda copy: copy.wait_send())
            all_of(arriving(other), lambda copy: copy.wait_recv())

    for step in range(1, 4):
        along_pipe(step, me.pipe).wait_send()
    for step in range(1, 8):
        along_dp(step, me.dp).wait_send()
    for copy in (l_half_x(), l_half_y(), l_send_x(), l_send_y()):
        copy.wait_send()
    for k in range(4):
        send_half_x(k).wait_send()
        send_half_y(k).wait_send()
        send_x(k).wait_send()
        send_y(k).wait_send()
        for group in range(4):
            share(group, k).wait_send()
            l_share(group, k).wait_send()
    for k in range(3):
        zd, at = order[k], 12 + k

        @pl.when(zd > z)
        def _(at=at, zd=zd, k=k):
            send_up(at, zd).wait_send()
            for group in range(4):
                l_up(group, k).wait_send()

        @pl.when(zd < z)
        def _(at=at, zd=zd, k=k):
            send_down(at, zd).wait_send()
            for group in range(4):
                l_down(group, k).wait_send()


def reduce_all(big, small, wide0, wide1, final, stats, table):
    sem = pltpu.SemaphoreType.DMA
    vm = pltpu.VMEM
    lane_tile = jax.ShapeDtypeStruct((8, 128), FULL)
    return pl.pallas_call(
        reduce_kernel,
        name="reduce_all",
        out_shape=(
            jax.ShapeDtypeStruct((2, BIG_HALF, 128), FULL),
            jax.ShapeDtypeStruct((8, SMALL_ROWS, 128), LOW),
            jax.ShapeDtypeStruct((4,) + wide0.shape, LOW),
            jax.ShapeDtypeStruct((4,) + stats.shape[1:], FULL),
            lane_tile,
            lane_tile,
        ),
        in_specs=[any_spec()] * 7,
        out_specs=(any_spec(),) * 4 + (vmem_spec(),) * 2,
        scratch_shapes=[
            vm((16, BIG_HALF, 128), LOW), vm((4, BIG_HALF - BACK_CUT, 128), LOW), vm((4, BACK_CUT, 128), LOW),
            vm((4, BIG_HALF, 128), LOW), vm((4, BIG_HALF, 128), LOW),
            vm((3, BIG_HALF, 128), LOW), vm((3, BIG_HALF, 128), LOW),
            vm((4, BIG_HALF, 128), LOW), vm((BIG_HALF, 128), FULL),
            vm((16, SMALL_HALF, 128), LOW), vm((16, SMALL_HALF, 128), LOW),
            vm((4, 3, SMALL_HALF, 128), LOW), vm((4, 3, SMALL_HALF, 128), LOW),
            vm((SMALL_HALF - LIGHT_CUT, 128), LOW), vm((LIGHT_CUT, 128), LOW),
            vm((SMALL_HALF, 128), LOW), vm((SMALL_HALF, 128), LOW), vm((SMALL_HALF, 128), FULL),
            vm((SMALL_ROWS, 128), LOW), vm((SMALL_HALF, 128), LOW), vm((8, 128), jnp.int32),
            vm((4, 8, 128), FULL), vm((8, 8, 128), FULL), vm((8, 128), FULL), vm((8, 128), FULL),
            sem((2, 16)), sem((2, 16)),
            sem((5,)), sem((5,)), sem((5,)), sem((5,)), sem((5,)), sem((5,)), sem((5,)), sem((5,)),
            sem((3,)), sem((3,)), sem((3,)), sem((3,)),
            sem((4, 3)), sem((4, 3)), sem((4, 3)), sem((4, 3)),
            sem((4,)), sem((16,)), sem((3,)), sem((8,)), sem((8,)), sem((2,)), sem((2,)),
            sem((4,)), sem((4,)), sem((4,)), sem((4,)), sem((4,)), sem((4,)), sem((8,)), sem((8,)),
        ],
        compiler_params=pltpu.CompilerParams(
            collective_id=1, has_side_effects=True, vmem_limit_bytes=62 << 20
        ),
    )(big.reshape(2, 8, 2, BIG_HALF, 128), small.reshape(2, 8, 2, SMALL_HALF, 128),
      wide0, wide1, final, stats, table)


def high_dot(a, b, dims=((1,), (0,))):
    return lax.dot_general(a, b, (dims, ((), ())), precision=HIGH, preferred_element_type=FULL)


PIECES = 7
FRONT = 48


def update_kernel(owners, factor_ref, big, small, gram_old, basis_old, params, moment, second,
                  clipped, moment_new, second_new, params_new, gram_new, basis_new,
                  tiles, low, grad, held, rotated, weights, gram, in_sem, out_sem, tile_sem):
    factor = factor_ref[0:1, :]
    block, section = owners[0, lax.axis_index("dp")], lax.axis_index("pipe")
    even = lax.rem(section, 2) == 0
    span = params.shape[0]
    piece = held.shape[0] // PIECES

    @pl.when(even)
    def _():
        pltpu.make_async_copy(big, tiles, tile_sem).start()

    def loads(i):
        part = pl.ds(piece * i, min(piece, span - piece * i))
        for n, (src, dst) in enumerate(((params, weights), (moment, held), (second, rotated))):
            yield pltpu.make_async_copy(src.at[part, 0, :], dst.at[part], in_sem.at[n, i])

    def stores(i):
        count = min(piece, span - piece * i)
        part = pl.ds(piece * i, count)
        yield pltpu.make_async_copy(
            grad.at[pl.ds(FRONT + piece * i, count)], clipped.at[part, 0, :], out_sem.at[3, i])
        pairs = ((held, moment_new), (rotated, second_new), (weights, params_new))
        for n, (src, dst) in enumerate(pairs):
            yield pltpu.make_async_copy(src.at[part], dst.at[part, 0, :], out_sem.at[n, i])

    for i in range(PIECES):
        for load in loads(i):
            load.start()

    @pl.when(even)
    def _():
        pltpu.make_async_copy(big, tiles, tile_sem).wait()

    @pl.when(jnp.logical_not(even))
    def _():
        low[...] = jnp.zeros_like(low)

        @pl.when(block == 0)
        def _():
            copy = pltpu.make_async_copy(small.at[0:20], low, tile_sem)
            copy.start()
            copy.wait()

        @pl.when(block == 1)
        def _():
            copy = pltpu.make_async_copy(small.at[19:33], low.at[0:14], tile_sem)
            copy.start()
            copy.wait()

        @pl.loop(0, WINDOW)
        def _(r):
            tiles[r] = low[r].astype(FULL)

    @pl.loop(0, WINDOW)
    def _(r):
        narrow, plain = tile_forms(section, STRIDE * block + r)
        base = FRONT - 6 * block + TILE * r

        @pl.when(narrow)
        def _():
            for j in range(4):
                grad[pl.ds(base + j, 64, 4), :] = tiles[r, 64 * j : 64 * j + 64, :]

        @pl.when(plain)
        def _():
            grad[pl.ds(base, TILE), :] = tiles[r]

        @pl.when(jnp.logical_not(narrow | plain))
        def _():
            for j in range(16):
                grad[pl.ds(base + j, 16, 16), :] = tiles[r, 16 * j : 16 * j + 16, :]

    tail = piece * PIECES - 8
    rest = lax.broadcasted_iota(jnp.int32, (8, 128), 0) + tail
    grad[FRONT + tail : FRONT + tail + 8, :] = jnp.where(
        rest < span, grad[FRONT + tail : FRONT + tail + 8, :], 0.0
    )
    gram[...] = jnp.zeros_like(gram)

    def halves(value):
        high = value.astype(LOW)
        return high, (value - high.astype(FULL)).astype(LOW)

    def split_dot(a, b, dims=((1,), (0,))):
        def dot(left, right):
            return lax.dot_general(left, right, (dims, ((), ())), preferred_element_type=FULL)

        return dot(a[0], b[0]) + (dot(a[0], b[1]) + dot(a[1], b[0]))

    @pl.loop(0, PIECES)
    def _(i):
        part = halves(grad[pl.ds(pl.multiple_of(FRONT + piece * i, 8), piece), :])
        gram[...] += split_dot(part, part, ((0,), (0,)))

    old = basis_old[...]
    fresh = DECAY_STATS * gram_old[...] + (1.0 - DECAY_STATS) * (gram[...] * (factor * factor))
    gram_new[...] = fresh
    product = high_dot(fresh, old)
    rotation = product / jnp.sqrt(jnp.sum(product * product))
    for repeat in range(NS_STEPS):
        square = high_dot(rotation, rotation, ((0,), (0,)))
        rotation = 1.5 * rotation - 0.5 * high_dot(rotation, square)
    basis_new[...] = rotation
    change = halves(high_dot(old, rotation, ((0,), (0,))))
    turn = halves(rotation)
    correction = math.sqrt(1.0 - DECAY_SECOND**STEP) / (1.0 - DECAY_FIRST**STEP)
    for i in range(PIECES):
        for load in loads(i):
            load.wait()
        at = slice(FRONT + piece * i, FRONT + piece * i + piece)
        part = slice(piece * i, piece * i + piece)
        clip = grad[at, :] * factor
        grad[at, :] = clip
        turned = split_dot(halves(clip), turn)
        first = DECAY_FIRST * split_dot(halves(held[part, :]), change) + (1.0 - DECAY_FIRST) * turned
        power = DECAY_SECOND * rotated[part, :] + (1.0 - DECAY_SECOND) * turned * turned
        held[part, :] = first
        rotated[part, :] = power
        scaled = halves(first / (jnp.sqrt(power) + ADAM_EPS))
        direction = split_dot(scaled, turn, ((1,), (1,))) * correction
        before = weights[part, :]
        weights[part, :] = before - LEARN_RATE * (direction + WEIGHT_DECAY * before)
        for store in stores(i):
            store.start()
    for i in range(PIECES):
        for store in stores(i):
            store.wait()


def update(owners, factor, big, small, gram_old, basis_old, params, moment, second):
    span = params.shape[1] // 128
    rows = -(-span // (8 * PIECES)) * 8 * PIECES
    flat_shape = jax.ShapeDtypeStruct((span, 1, 128), FULL)
    square = jax.ShapeDtypeStruct((128, 128), FULL)
    sem = pltpu.SemaphoreType.DMA
    vm = pltpu.VMEM
    outs = pl.pallas_call(
        update_kernel,
        name="update",
        out_shape=(flat_shape,) * 4 + (square,) * 2,
        in_specs=[smem_spec(), vmem_spec()] + [any_spec()] * 2 + [vmem_spec()] * 2 + [any_spec()] * 3,
        out_specs=(any_spec(),) * 4 + (vmem_spec(),) * 2,
        scratch_shapes=[
            vm((WINDOW, TILE, 128), FULL), vm((WINDOW, TILE, 128), LOW),
            vm((FRONT + WINDOW * TILE, 128), FULL), vm((rows, 128), FULL), vm((rows, 128), FULL),
            vm((rows, 128), FULL), vm((128, 128), FULL), sem((3, PIECES)), sem((4, PIECES)), sem,
        ],
        compiler_params=pltpu.CompilerParams(vmem_limit_bytes=60 << 20),
    )(owners, factor, big.reshape(WINDOW, TILE, 128), small.reshape(USED_TILES[1], TILE, 128),
      gram_old, basis_old, params.reshape(span, 1, 128), moment.reshape(span, 1, 128),
      second.reshape(span, 1, 128))
    return tuple(out.reshape(1, span * 128) for out in outs[:4]) + outs[4:]


def to_phases(teach, stud):
    def split(part):
        crops, high, across, channels = part.shape
        part = part.reshape(crops, high // 2, 2, across // 2, 2, channels).transpose(2, 4, 0, 1, 3, 5)
        return part.reshape(4, -1, channels)

    zeros = jnp.zeros((4, PADDED - ROWS, teach.shape[-1]), teach.dtype)
    return jnp.concatenate([split(teach), split(stud), zeros], axis=1)


def from_phases(phases, shape):
    crops, high, across, channels = shape
    part = phases.reshape(2, 2, crops, high // 2, across // 2, channels)
    return part.transpose(2, 3, 0, 4, 1, 5).reshape(shape)


def on_small_slice(
    teach_in,
    stud_in,
    params,
    owners,
    depth_gates,
    teach_ids,
    stud_ids,
    targets,
    moment,
    second,
    gram_stats,
    eigen_basis,
):
    phases = to_phases(teach_in[0], stud_in[0])
    big, small, ids = prepare(owners, params)
    all_big, all_small, table = gather_all(big, small, ids)
    wide_0, wide_1, final, stats, grad_x, out_big, out_small = run_step(
        table,
        depth_gates,
        teach_ids,
        stud_ids,
        all_big.reshape(2, 8, 2, WINDOW // 2, TILE, 128),
        all_small.reshape(2, USED_TILES[1], TILE, 128),
        phases,
        targets,
    )
    sum_big, sum_small, segments, stats, norm, factor = reduce_all(
        out_big, out_small, wide_0, wide_1, final, stats, table
    )
    clipped, moment_new, second_new, params_new, gram_new, rotation = update(
        owners, factor, sum_big, sum_small, gram_stats[0], eigen_basis[0], params, moment, second
    )
    teach_shape, stud_shape = teach_in.shape[1:], stud_in.shape[1:]
    small_teach = (teach_shape[0], teach_shape[1] // 2, teach_shape[2] // 2, C_OUT)
    small_stud = (stud_shape[0], stud_shape[1] // 2, stud_shape[2] // 2, C_OUT)
    segment_teach = segments[:, :TEACH_ROWS].reshape((4,) + small_teach)
    segment_stud = segments[:, TEACH_ROWS:ROWS].reshape((4,) + small_stud)
    stats = stats[:, 0:2]
    teach_grad = from_phases(grad_x[:, :TEACH_ROWS], teach_shape)
    stud_grad = from_phases(grad_x[:, TEACH_ROWS:ROWS], stud_shape)
    grad_norm = norm[0, 0]
    return (
        segment_teach[None],
        segment_stud[None],
        teach_grad[None],
        stud_grad[None],
        stats[None, :, None],
        grad_norm,
        clipped,
        moment_new,
        second_new,
        params_new,
        gram_new[None],
        rotation[None],
    )


def solution(mesh):
    placed = (
        P("pipe", "dp", None, None, None),
        P("pipe", "dp", None, None, None),
        P("pipe", "dp"),
        P("pipe", None),
        P(),
        P(None, "dp"),
        P(None, "dp"),
        P(),
        P("pipe", "dp"),
        P("pipe", "dp"),
        P("pipe", "dp", None),
        P("pipe", "dp", None),
    )
    small_slice = mesh.shape["dp"] == 8 and mesh.shape["pipe"] == 4
    return jax.shard_map(
        on_small_slice if small_slice else on_device,
        mesh=mesh,
        in_specs=placed,
        out_specs=(
            P("pipe", None, "dp", None, None, None),
            P("pipe", None, "dp", None, None, None),
            P("pipe", "dp", None, None, None),
            P("pipe", "dp", None, None, None),
            P("pipe", None, "dp", None, None),
            P(),
            P("pipe", "dp"),
            P("pipe", "dp"),
            P("pipe", "dp"),
            P("pipe", "dp"),
            P("pipe", "dp", None),
            P("pipe", "dp", None),
        ),
        check_vma=False,
    )
```

```python
import math

import jax
import jax.numpy as jnp
import numpy as np
from jax import lax
from jax.experimental import pallas as pl
from jax.experimental.pallas import tpu as pltpu
from jax.sharding import PartitionSpec as P

C_IN = 1024
MID = 512
C_OUT = 2048
STEP = 10
NS_STEPS = 5


HIGH = lax.Precision.HIGHEST
NORM_EPS = 1e-05
POOL_EPS = 1e-06
CLIP_NORM = 1.0
LEARN_RATE = 0.02
DECAY_FIRST = 0.9
DECAY_SECOND = 0.95
DECAY_STATS = 0.95
ADAM_EPS = 1e-08
WEIGHT_DECAY = 0.01


def section_shapes(section):
    if section == 0:
        return [
            ("first_conv", (C_IN, MID)),
            ("middle_conv", (9 * MID, MID)),
            ("skip_conv", (C_IN, C_OUT)),
            ("first_gain", (MID,)),
            ("first_bias", (MID,)),
            ("middle_gain", (MID,)),
            ("middle_bias", (MID,)),
            ("skip_gain", (C_OUT,)),
            ("skip_bias", (C_OUT,)),
        ]
    if section == 2:
        return [
            ("first_conv", (C_OUT, MID)),
            ("middle_conv", (9 * MID, MID)),
            ("first_gain", (MID,)),
            ("first_bias", (MID,)),
            ("middle_gain", (MID,)),
            ("middle_bias", (MID,)),
        ]
    return [("last_conv", (MID, C_OUT)), ("last_gain", (C_OUT,)), ("last_bias", (C_OUT,))]


def unpack(flat_vector, section):
    pieces = {}
    offset = 0
    for entry_name, entry_shape in section_shapes(section):
        entry_size = math.prod(entry_shape)
        pieces[entry_name] = flat_vector[offset : offset + entry_size].reshape(entry_shape)
        offset = offset + entry_size
    return pieces


def pack(grads, section, flat_size):
    parts = [grads[entry_name].reshape(-1) for entry_name, entry_shape in section_shapes(section)]
    used = sum((math.prod(entry_shape) for entry_name, entry_shape in section_shapes(section)))
    parts.append(jnp.zeros((flat_size - used,), jnp.float32))
    return jnp.concatenate(parts)


def as_float(vector):
    return vector.astype(jnp.float32)


def to_low(groups):
    return tuple((portion.astype(jnp.bfloat16) for portion in groups))


def to_high(groups):
    return tuple((portion.astype(jnp.float32) for portion in groups))


def point_conv(groups, weight):
    return tuple(
        (
            jnp.einsum("khwc,cd->khwd", portion, weight, preferred_element_type=jnp.float32)
            for portion in groups
        )
    )


def point_back(grad_out, groups, weight):
    low_grads = to_low(grad_out)
    grad_input = tuple(
        (
            jnp.einsum("khwd,cd->khwc", grad_part, weight, preferred_element_type=jnp.float32)
            for grad_part in low_grads
        )
    )
    grad_weight = sum(
        (
            jnp.einsum("khwc,khwd->cd", in_part, grad_part, preferred_element_type=jnp.float32)
            for in_part, grad_part in zip(groups, low_grads)
        )
    )
    return (grad_input, grad_weight)


def patches(portion, stride):
    height = portion.shape[1]
    across = portion.shape[2]
    padded = jnp.pad(portion, ((0, 0), (1, 1), (1, 1), (0, 0)))
    shifted = [
        padded[:, row_off : row_off + height : stride, col_off : col_off + across : stride, :]
        for row_off in range(3)
        for col_off in range(3)
    ]
    return jnp.concatenate(shifted, axis=-1)


def area_conv(groups, weight, stride):
    columns = tuple((patches(portion, stride) for portion in groups))
    return (point_conv(columns, weight), columns)


def unpatch(grad_cols, height, across, stride):
    channels = grad_cols.shape[-1] // 9
    padded = jnp.zeros((grad_cols.shape[0], height + 2, across + 2, channels), jnp.float32)
    for row_off in range(3):
        for col_off in range(3):
            offset = (3 * row_off + col_off) * channels
            padded = padded.at[
                :, row_off : row_off + height : stride, col_off : col_off + across : stride, :
            ].add(grad_cols[..., offset : offset + channels])
    return padded[:, 1 : height + 1, 1 : across + 1, :]


def area_back(grad_out, columns, weight, stride, in_shapes):
    grad_cols, grad_weight = point_back(grad_out, columns, weight)
    grad_input = tuple(
        (
            unpatch(grad_part, shape_item[1], shape_item[2], stride)
            for grad_part, shape_item in zip(grad_cols, in_shapes)
        )
    )
    return (grad_input, grad_weight)


def batch_norm(groups, gain, bias):
    rows_total = sum((portion.shape[0] * portion.shape[1] * portion.shape[2] for portion in groups))
    centre = sum((jnp.sum(portion, axis=(0, 1, 2)) for portion in groups)) / rows_total
    spread = (
        sum((jnp.sum(jnp.square(portion - centre), axis=(0, 1, 2)) for portion in groups))
        / rows_total
    )
    inverse = lax.rsqrt(spread + NORM_EPS)
    standard = tuple(((portion - centre) * inverse for portion in groups))
    normed = tuple((gain * std_part + bias for std_part in standard))
    return (normed, (centre, spread, inverse, standard))


def norm_back(grad_out, gain, saved):
    centre, spread, inverse, standard = saved
    rows_total = sum(
        (portion.shape[0] * portion.shape[1] * portion.shape[2] for portion in standard)
    )
    grad_sum = sum((jnp.sum(grad_part, axis=(0, 1, 2)) for grad_part in grad_out))
    grad_dot = sum(
        (
            jnp.sum(grad_part * std_part, axis=(0, 1, 2))
            for grad_part, std_part in zip(grad_out, standard)
        )
    )
    grad_input = tuple(
        (
            gain
            * inverse
            * (grad_part - grad_sum / rows_total - std_part * (grad_dot / rows_total))
            for grad_part, std_part in zip(grad_out, standard)
        )
    )
    return (grad_input, grad_dot, grad_sum)


def through_softplus(grad_out, pre_values):
    return tuple(
        (grad_part * jax.nn.sigmoid(pre_part) for grad_part, pre_part in zip(grad_out, pre_values))
    )


def front_forward(pieces, inputs):
    first = point_conv(inputs, pieces["first_conv"])
    normed_a, saved_a = batch_norm(
        first, as_float(pieces["first_gain"]), as_float(pieces["first_bias"])
    )
    hidden = tuple((jax.nn.softplus(portion).astype(jnp.bfloat16) for portion in normed_a))
    middle, columns = area_conv(hidden, pieces["middle_conv"], 2)
    normed_b, saved_b = batch_norm(
        middle, as_float(pieces["middle_gain"]), as_float(pieces["middle_bias"])
    )
    narrow = tuple((jax.nn.softplus(portion) for portion in normed_b))
    reduced = tuple((portion[:, ::2, ::2, :] for portion in inputs))
    skipped = point_conv(reduced, pieces["skip_conv"])
    wide, saved_p = batch_norm(
        skipped, as_float(pieces["skip_gain"]), as_float(pieces["skip_bias"])
    )
    norm_rows = jnp.stack(
        [
            jnp.concatenate([saved_a[0], saved_b[0], saved_p[0]]),
            jnp.concatenate([saved_a[1], saved_b[1], saved_p[1]]),
        ]
    )
    kept = (normed_a, hidden, columns, normed_b, reduced, saved_a, saved_b, saved_p)
    return (wide, narrow, norm_rows, kept)


def front_backward(pieces, inputs, grad_wide, grad_narrow):
    wide, narrow, norm_rows, kept = front_forward(pieces, inputs)
    normed_a, hidden, columns, normed_b, reduced, saved_a, saved_b, saved_p = kept
    grads = {}
    grad_pre_b = through_softplus(grad_narrow, normed_b)
    grad_mid, grads["middle_gain"], grads["middle_bias"] = norm_back(
        grad_pre_b, as_float(pieces["middle_gain"]), saved_b
    )
    grad_hidden, grads["middle_conv"] = area_back(
        grad_mid, columns, pieces["middle_conv"], 2, [portion.shape for portion in hidden]
    )
    grad_pre_a = through_softplus(grad_hidden, normed_a)
    grad_first, grads["first_gain"], grads["first_bias"] = norm_back(
        grad_pre_a, as_float(pieces["first_gain"]), saved_a
    )
    grad_inputs, grads["first_conv"] = point_back(grad_first, inputs, pieces["first_conv"])
    grad_skip, grads["skip_gain"], grads["skip_bias"] = norm_back(
        grad_wide, as_float(pieces["skip_gain"]), saved_p
    )
    grad_reduced, grads["skip_conv"] = point_back(grad_skip, reduced, pieces["skip_conv"])
    grad_inputs = tuple(
        (
            full_part.at[:, ::2, ::2, :].add(part_reduced)
            for full_part, part_reduced in zip(grad_inputs, grad_reduced)
        )
    )
    return (grad_inputs, grads)


def join_forward(pieces, wide, narrow):
    last = point_conv(narrow, pieces["last_conv"])
    normed, saved = batch_norm(last, as_float(pieces["last_gain"]), as_float(pieces["last_bias"]))
    pre_values = tuple(
        (
            skip_part.astype(jnp.float32) + branch_part
            for skip_part, branch_part in zip(wide, normed)
        )
    )
    ending = tuple((jax.nn.softplus(pre_part) for pre_part in pre_values))
    filler = jnp.zeros((2 * MID,), jnp.float32)
    norm_rows = jnp.stack(
        [jnp.concatenate([saved[0], filler]), jnp.concatenate([saved[1], filler])]
    )
    return (ending, norm_rows, (pre_values, saved))


def join_grads(pieces, narrow, kept, grad_out, gate):
    pre_values, saved = kept
    grad_pre = tuple(
        (
            grad_part * jax.nn.sigmoid(pre_part) * gate
            for grad_part, pre_part in zip(grad_out, pre_values)
        )
    )
    grad_wide = tuple(
        (pre_grad + grad_part * (1.0 - gate) for pre_grad, grad_part in zip(grad_pre, grad_out))
    )
    grad_last, gain_grad, bias_grad = norm_back(grad_pre, as_float(pieces["last_gain"]), saved)
    grad_narrow, weight_grad = point_back(grad_last, narrow, pieces["last_conv"])
    grads = {"last_conv": weight_grad, "last_gain": gain_grad, "last_bias": bias_grad}
    return (grad_wide, grad_narrow, grads)


def split_forward(pieces, wide):
    first = point_conv(wide, pieces["first_conv"])
    normed_a, saved_a = batch_norm(
        first, as_float(pieces["first_gain"]), as_float(pieces["first_bias"])
    )
    hidden = tuple((jax.nn.softplus(portion).astype(jnp.bfloat16) for portion in normed_a))
    middle, columns = area_conv(hidden, pieces["middle_conv"], 1)
    normed_b, saved_b = batch_norm(
        middle, as_float(pieces["middle_gain"]), as_float(pieces["middle_bias"])
    )
    narrow = tuple((jax.nn.softplus(portion) for portion in normed_b))
    filler = jnp.zeros((C_OUT,), jnp.float32)
    norm_rows = jnp.stack(
        [
            jnp.concatenate([saved_a[0], saved_b[0], filler]),
            jnp.concatenate([saved_a[1], saved_b[1], filler]),
        ]
    )
    return (narrow, norm_rows, (normed_a, hidden, columns, normed_b, saved_a, saved_b))


def split_backward(pieces, wide, grad_relay, grad_narrow):
    narrow, norm_rows, kept = split_forward(pieces, wide)
    normed_a, hidden, columns, normed_b, saved_a, saved_b = kept
    grads = {}
    grad_pre_b = through_softplus(grad_narrow, normed_b)
    grad_mid, grads["middle_gain"], grads["middle_bias"] = norm_back(
        grad_pre_b, as_float(pieces["middle_gain"]), saved_b
    )
    grad_hidden, grads["middle_conv"] = area_back(
        grad_mid, columns, pieces["middle_conv"], 1, [portion.shape for portion in hidden]
    )
    grad_pre_a = through_softplus(grad_hidden, normed_a)
    grad_first, grads["first_gain"], grads["first_bias"] = norm_back(
        grad_pre_a, as_float(pieces["first_gain"]), saved_a
    )
    grad_conv_in, grads["first_conv"] = point_back(grad_first, wide, pieces["first_conv"])
    grad_wide = tuple(
        (relay_part + conv_part for relay_part, conv_part in zip(grad_relay, grad_conv_in))
    )
    return (grad_wide, grads)


def pool_grad(final, targets, picks):
    result = []
    for portion, pick_ids in zip(final, picks):
        cubes = jnp.mean(portion * portion * portion, axis=(1, 2)) + POOL_EPS
        factor = jnp.exp(jnp.log(cubes) * (-2.0 / 3.0)) * targets[pick_ids]
        result.append(factor[:, None, None, :] * portion * portion)
    return tuple(result)


def used_size(section):
    return sum((math.prod(entry_shape) for entry_name, entry_shape in section_shapes(section)))


def batch_pass(reals, inputs, gate, targets, picks):
    pieces = [unpack(reals[section], section) for section in range(4)]
    wide_f, narrow_f, rows_0, _ = front_forward(pieces[0], inputs)
    wide_0, narrow_0 = to_low(wide_f), to_low(narrow_f)
    ending_1, rows_1, kept_1 = join_forward(pieces[1], wide_0, narrow_0)
    wide_1 = to_low(ending_1)
    narrow_f, rows_2, _ = split_forward(pieces[2], wide_1)
    narrow_2 = to_low(narrow_f)
    ending_3, rows_3, kept_3 = join_forward(pieces[3], wide_1, narrow_2)
    final = tuple(
        (
            jnp.where(gate > 0, end_part, relay_part.astype(jnp.float32))
            for end_part, relay_part in zip(ending_3, wide_1)
        )
    )
    cotangent = pool_grad(final, targets, picks)
    grad_wide, grad_narrow, grads_3 = join_grads(pieces[3], narrow_2, kept_3, cotangent, gate)
    grad_wide, grads_2 = split_backward(
        pieces[2], wide_1, to_high(to_low(grad_wide)), to_high(to_low(grad_narrow))
    )
    grad_wide, grad_narrow, grads_1 = join_grads(
        pieces[1], narrow_0, kept_1, to_high(to_low(grad_wide)), 1.0
    )
    grad_inputs, grads_0 = front_backward(
        pieces[0], inputs, to_high(to_low(grad_wide)), to_high(to_low(grad_narrow))
    )
    outs = (wide_0, wide_1, wide_1, to_low(final))
    stats = jnp.stack([rows_0, rows_1, rows_2 * gate, rows_3 * gate])
    return (outs, stats, to_low(grad_inputs), (grads_0, grads_1, grads_2, grads_3))


def on_device(
    teach_in,
    stud_in,
    params,
    owners,
    depth_gates,
    teach_ids,
    stud_ids,
    targets,
    moment,
    second,
    gram_stats,
    eigen_basis,
):
    sections = lax.axis_size("pipe")
    rank = lax.axis_index("pipe")
    owner_count = lax.axis_size("dp")
    span_size = params.shape[1]
    flat_size = span_size * owner_count
    owner_rows = lax.all_gather(owners, "pipe", axis=0, tiled=True)
    gathered = lax.all_gather(params[0].astype(jnp.bfloat16), ("pipe", "dp"), axis=0)
    gathered = gathered.reshape(sections, owner_count, span_size)
    reals = []
    for section in range(sections):
        inverse = jnp.argsort(owner_rows[section]).astype(jnp.int32)
        blocks = -(-used_size(section) // span_size)
        reals.append(gathered[section][inverse[:blocks]].reshape(blocks * span_size))
    inputs = (teach_in[0], stud_in[0])
    gate = depth_gates[rank].astype(jnp.float32)
    outs, stats, (teach_grad, stud_grad), grads = batch_pass(
        reals, inputs, gate, targets, (teach_ids[rank], stud_ids[rank])
    )
    segment_teach = lax.all_to_all(
        jnp.stack([part[0] for part in outs]), "pipe", split_axis=0, concat_axis=0, tiled=True
    )
    segment_stud = lax.all_to_all(
        jnp.stack([part[1] for part in outs]), "pipe", split_axis=0, concat_axis=0, tiled=True
    )
    stats = lax.all_to_all(stats, "pipe", split_axis=0, concat_axis=0, tiled=True)
    rows = []
    for section in range(sections):
        flat = pack(grads[section], section, flat_size).reshape(owner_count, span_size)
        rows.append(flat[owner_rows[section]])
    span_total = lax.psum_scatter(
        jnp.stack(rows).reshape(sections * owner_count, span_size),
        ("pipe", "dp"),
        scatter_dimension=0,
        tiled=True,
    ).reshape(span_size)
    total_squares = lax.psum(jnp.sum(span_total * span_total), ("dp", "pipe"))
    grad_norm = jnp.sqrt(total_squares)
    factor = jnp.minimum(1.0, CLIP_NORM / grad_norm)
    clipped = span_total * factor
    matrix = clipped.reshape(span_size // 128, 128)
    gram_old = gram_stats[0]
    basis_old = eigen_basis[0]
    gram_new = DECAY_STATS * gram_old + (1.0 - DECAY_STATS) * jnp.dot(
        matrix.T, matrix, precision=HIGH
    )
    product = jnp.dot(gram_new, basis_old, precision=HIGH)
    rotation = product / jnp.sqrt(jnp.sum(product * product))
    for repeat in range(NS_STEPS):
        square = jnp.dot(rotation.T, rotation, precision=HIGH)
        rotation = 1.5 * rotation - 0.5 * jnp.dot(rotation, square, precision=HIGH)
    moment_old = moment.reshape(span_size // 128, 128)
    initial = jnp.dot(moment_old, basis_old.T, precision=HIGH)
    blended = DECAY_FIRST * initial + (1.0 - DECAY_FIRST) * matrix
    moment_new = jnp.dot(blended, rotation, precision=HIGH)
    rotated = jnp.dot(matrix, rotation, precision=HIGH)
    second_new = (
        DECAY_SECOND * second.reshape(span_size // 128, 128)
        + (1.0 - DECAY_SECOND) * rotated * rotated
    )
    correction = math.sqrt(1.0 - DECAY_SECOND**STEP) / (1.0 - DECAY_FIRST**STEP)
    direction = (
        jnp.dot(moment_new / (jnp.sqrt(second_new) + ADAM_EPS), rotation.T, precision=HIGH)
        * correction
    )
    weights = params.reshape(span_size // 128, 128)
    params_new = weights - LEARN_RATE * (direction + WEIGHT_DECAY * weights)
    return (
        segment_teach[None],
        segment_stud[None],
        teach_grad[None],
        stud_grad[None],
        stats[None, :, None],
        grad_norm,
        clipped.reshape(1, span_size),
        moment_new.reshape(1, span_size),
        second_new.reshape(1, span_size),
        params_new.reshape(1, span_size),
        gram_new[None],
        rotation[None],
    )


MESH = pl.DeviceIdType.MESH
LOW = jnp.bfloat16
FULL = jnp.float32
TILE = 256
WINDOW = 20
STRIDE = 19
VEC_TILE = (152, 32, 104, 32)
USED_TILES = (153, 33, 105, 33)
FRONT_WIDE = 88
SMALL_ROWS = 1056
ROWS = 120
PADDED = 128
TEACH_ROWS = 72


def any_spec():
    return pl.BlockSpec(memory_space=pl.ANY)


def smem_spec():
    return pl.BlockSpec(memory_space=pltpu.SMEM)


def vmem_spec():
    return pl.BlockSpec(memory_space=pltpu.VMEM)


def tile_forms(section, tile):
    even = lax.rem(section, 2) == 0
    vector = jnp.where(section == 0, 152, jnp.where(section == 2, 104, 32))
    narrow_end = jnp.where(section == 0, FRONT_WIDE, jnp.where(section == 2, 104, 0))
    narrow = even & (tile < narrow_end)
    plain = tile == vector
    return narrow, plain


def prepare_kernel(owners, params, big, small, ids, flat, sem):
    block, section = owners[0, lax.axis_index("dp")], lax.axis_index("pipe")

    @pl.loop(0, WINDOW)
    def _(r):
        flat[pl.ds(TILE * r, TILE)] = jnp.zeros((TILE, 128), FULL)

    copy = pltpu.make_async_copy(params.at[:, 0, :], flat.at[pl.ds(6 * block, params.shape[0])], sem)
    copy.start()

    @pl.loop(0, small.shape[0])
    def _(r):
        small[r] = jnp.zeros((TILE, 128), LOW)

    lane = lax.broadcasted_iota(jnp.int32, (8, 128), 1)
    row = jnp.zeros((8, 128), jnp.int32)
    for j in range(8):
        row = jnp.where(lane == j, owners[0, j], row)
    ids[...] = row
    copy.wait()

    @pl.loop(0, WINDOW)
    def _(r):
        tile = STRIDE * block + r
        narrow, plain = tile_forms(section, tile)
        base = TILE * r

        @pl.when(narrow)
        def _():
            for j in range(4):
                big[r, 64 * j : 64 * j + 64, :] = flat[pl.ds(base + j, 64, 4), :].astype(LOW)

        @pl.when(plain)
        def _():
            big[r] = flat[pl.ds(base, TILE), :].astype(LOW)

        @pl.when(jnp.logical_not(narrow | plain))
        def _():
            for j in range(16):
                big[r, 16 * j : 16 * j + 16, :] = flat[pl.ds(base + j, 16, 16), :].astype(LOW)

        @pl.when(tile < small.shape[0])
        def _():
            small[tile] = big[r]


def prepare(owners, params):
    return pl.pallas_call(
        prepare_kernel,
        name="prepare",
        out_shape=(
            jax.ShapeDtypeStruct((WINDOW, TILE, 128), LOW),
            jax.ShapeDtypeStruct((USED_TILES[1], TILE, 128), LOW),
            jax.ShapeDtypeStruct((8, 128), jnp.int32),
        ),
        in_specs=[smem_spec(), any_spec()],
        out_specs=(vmem_spec(),) * 3,
        scratch_shapes=[pltpu.VMEM((WINDOW * TILE, 128), FULL), pltpu.SemaphoreType.DMA],
        compiler_params=pltpu.CompilerParams(vmem_limit_bytes=60 << 20),
    )(owners, params.reshape(-1, 1, 128))


class Place:
    def __init__(self):
        self.dp = lax.axis_index("dp")
        self.pipe = lax.axis_index("pipe")
        self.x, self.core = self.pipe // 2, self.pipe % 2
        self.z, self.y = self.dp // 2, self.dp % 2

    def device(self, x=None, core=None, z=None, y=None):
        x = self.x if x is None else x
        core = self.core if core is None else core
        z = self.z if z is None else z
        y = self.y if y is None else y
        return {"dp": 2 * z + y, "pipe": 2 * x + core}

    def enter(self):
        barrier = pltpu.get_barrier_semaphore()
        for step in range(1, 8):
            other = lax.rem(self.dp + step, 8)
            pl.semaphore_signal(
                barrier, inc=1, device_id={"dp": other, "pipe": self.pipe}, device_id_type=MESH
            )
        for step in range(1, 4):
            other = lax.rem(self.pipe + step, 4)
            pl.semaphore_signal(
                barrier, inc=1, device_id={"dp": self.dp, "pipe": other}, device_id_type=MESH
            )
        pl.semaphore_wait(barrier, 10)


def remote(src, dst, send, recv, target):
    return pltpu.make_async_remote_copy(
        src_ref=src, dst_ref=dst, send_sem=send, recv_sem=recv, device_id=target, device_id_type=MESH
    )


BIG_HALF = WINDOW * TILE // 2
SMALL_HALF = SMALL_ROWS // 2
BULK_CUT = 1056
LIGHT_CUT = 256
BACK_CUT = 1488


def gather_kernel(big, small, ids, all_big, all_small, table, early, chunk, early_send, early_recv,
                  z_send, z_recv, x_send, x_recv, y_send, y_recv, dx_send, dx_recv, dy_send, dy_recv,
                  s_send, s_recv, first_send, first_recv, own_sem, id_send, id_recv, lz_send, lz_recv):
    me = Place()
    me.enter()
    x, y, z, core = me.x, me.y, me.z, me.core
    up, down = me.device(z=z + 1), me.device(z=z - 1)
    x_side, y_side, sibling = me.device(x=1 - x), me.device(y=1 - y), me.device(core=1 - core)

    class Stream:
        def __init__(self, n, out, cut):
            self.n, self.out, self.cut, self.rows = n, out, cut, out.shape[3]

        def block(self, xo, origin, yo):
            return self.out.at[xo, 2 * origin + yo, core]

        def move_x(self, origin):
            block = self.block(x, origin, y)
            return remote(block, block, x_send.at[self.n, origin], x_recv.at[self.n, origin], x_side)

        def move_y(self, origin):
            block = self.block(x, origin, y)
            return remote(block, block, y_send.at[self.n, origin], y_recv.at[self.n, origin], y_side)

        def share(self, xo, origin, yo):
            block = self.block(xo, origin, yo)
            at = 8 * xo + 2 * origin + yo
            return remote(block, block, s_send.at[self.n, at], s_recv.at[self.n, at], sibling)

        def move_z(self, origin, target, way):
            block = self.block(x, origin, y)
            return remote(block, block, z_send.at[self.n, way, origin], z_recv.at[self.n, origin], target)

        def half_x(self, origin, xo, yo):
            part = self.out.at[xo, 2 * origin + yo, core, pl.ds(self.cut, self.rows - self.cut)]
            return remote(part, part, dx_send.at[self.n, origin], dx_recv.at[self.n, origin], x_side)

        def half_y(self, origin, xo, yo):
            part = self.out.at[xo, 2 * origin + yo, core, pl.ds(0, self.cut)]
            return remote(part, part, dy_send.at[self.n, origin], dy_recv.at[self.n, origin], y_side)

        def spread(self, origin):
            self.move_x(origin).start()
            self.move_y(origin).start()
            self.share(x, origin, y).start()

        def from_sides(self, origin):
            self.move_x(origin).wait_recv()
            self.half_y(origin, 1 - x, y).start()
            self.share(1 - x, origin, y).start()
            self.move_y(origin).wait_recv()
            self.half_x(origin, x, 1 - y).start()
            self.share(x, origin, 1 - y).start()

        def from_diagonal(self, origin):
            self.half_x(origin, 1 - x, 1 - y).wait_recv()
            self.half_y(origin, 1 - x, 1 - y).wait_recv()
            self.share(1 - x, origin, 1 - y).start()

        def each(self, step, action):
            if step == 0:
                action(z)
            else:
                pl.when(z >= step)(lambda: action(z - step))
                pl.when(z + step <= 3)(lambda: action(z + step))

        def step(self, k):
            if k == 0:
                pl.when(z < 3)(lambda: self.move_z(z, up, 0).start())
                pl.when(z > 0)(lambda: self.move_z(z, down, 1).start())
                self.spread(z)
            elif k < 4:

                @pl.when(z >= k)
                def _():
                    self.move_z(z - k, up, 0).wait_recv()
                    pl.when(z < 3)(lambda: self.move_z(z - k, up, 0).start())
                    self.spread(z - k)

                @pl.when(z + k <= 3)
                def _():
                    self.move_z(z + k, down, 1).wait_recv()
                    pl.when(z > 0)(lambda: self.move_z(z + k, down, 1).start())
                    self.spread(z + k)

            if 1 <= k < 5:
                self.each(k - 1, self.from_sides)
            if k >= 2:
                self.each(k - 2, self.from_diagonal)

        def close(self):
            for origin in range(4):
                self.move_x(origin).wait_send()
                self.move_y(origin).wait_send()
                self.half_x(origin, x, 1 - y).wait_send()
                self.half_y(origin, 1 - x, y).wait_send()
                pl.when((z < 3) & (origin <= z))(lambda: self.move_z(origin, up, 0).wait_send())
                pl.when((z > 0) & (origin >= z))(lambda: self.move_z(origin, down, 1).wait_send())
            self.close_shares()

        def close_shares(self):
            for origin in range(4):
                for xo in range(2):
                    for yo in range(2):
                        self.share(xo, origin, yo).wait_send()
                        theirs = self.out.at[xo, 2 * origin + yo, 1 - core]
                        at = 8 * xo + 2 * origin + yo
                        remote(theirs, theirs, s_send.at[self.n, at], s_recv.at[self.n, at], sibling).wait_recv()

    class Late(Stream):
        def column_z(self, xo, origin, yo, target, way):
            block = self.block(xo, origin, yo)
            at = 2 * xo + yo
            return remote(
                block, block, lz_send.at[way, at, origin], lz_recv.at[at, origin], target
            )

        def leave(self, xo, yo):
            pl.when(z < 3)(lambda: self.column_z(xo, z, yo, up, 0).start())
            pl.when(z > 0)(lambda: self.column_z(xo, z, yo, down, 1).start())
            self.share(xo, z, yo).start()

        def step(self, k):
            if k == 0:
                self.move_x(z).start()
                self.move_y(z).start()
                self.leave(x, y)
            elif k == 1:
                self.move_x(z).wait_recv()
                self.half_y(z, 1 - x, y).start()
                self.leave(1 - x, y)
                self.move_y(z).wait_recv()
                self.half_x(z, x, 1 - y).start()
                self.leave(x, 1 - y)
            elif k == 2:
                self.half_x(z, 1 - x, 1 - y).wait_recv()
                self.half_y(z, 1 - x, 1 - y).wait_recv()
                self.leave(1 - x, 1 - y)
            else:
                gap = k - 2

                @pl.when(z >= gap)
                def _():
                    for xo, yo in columns:
                        self.column_z(xo, z - gap, yo, up, 0).wait_recv()
                        pl.when(z < 3)(lambda: self.column_z(xo, z - gap, yo, up, 0).start())
                        self.share(xo, z - gap, yo).start()

                @pl.when(z + gap <= 3)
                def _():
                    for xo, yo in columns:
                        self.column_z(xo, z + gap, yo, down, 1).wait_recv()
                        pl.when(z > 0)(lambda: self.column_z(xo, z + gap, yo, down, 1).start())
                        self.share(xo, z + gap, yo).start()

        def close(self):
            self.move_x(z).wait_send()
            self.move_y(z).wait_send()
            self.half_x(z, x, 1 - y).wait_send()
            self.half_y(z, 1 - x, y).wait_send()
            for origin in range(4):
                for xo, yo in columns:
                    pl.when((z < 3) & (origin <= z))(
                        lambda: self.column_z(xo, origin, yo, up, 0).wait_send())
                    pl.when((z > 0) & (origin >= z))(
                        lambda: self.column_z(xo, origin, yo, down, 1).wait_send())
            self.close_shares()

    columns = ((x, y), (1 - x, y), (x, 1 - y), (1 - x, 1 - y))
    bulk = Stream(0, all_big, BULK_CUT)
    light = Late(1, all_small, LIGHT_CUT)

    def early_copy(step):
        target = lax.rem(me.dp + step, 8)
        return remote(
            small.at[target], early.at[step], early_send.at[step], early_recv.at[step],
            {"dp": target, "pipe": me.pipe},
        )

    big_half = all_big.at[x, me.dp, 1]
    big_first = remote(big.at[pl.ds(BIG_HALF, BIG_HALF)], big_half, first_send.at[0], first_recv.at[0], sibling)
    small_half = all_small.at[x, me.dp, 0]
    small_first = remote(chunk.at[pl.ds(0, SMALL_HALF)], small_half, first_send.at[1], first_recv.at[1], sibling)

    @pl.when(core == 0)
    def _():
        big_first.start()
        copy = pltpu.make_async_copy(big.at[pl.ds(0, BIG_HALF)], all_big.at[x, me.dp, 0], own_sem.at[0])
        copy.start()
        copy.wait()

    @pl.when(core == 1)
    def _():
        for step in range(1, 8):
            early_copy(step).start()
        pltpu.make_async_copy(small.at[me.dp], early.at[0], own_sem.at[1]).start()
        big_first.wait_recv()

    bulk.step(0)
    row = pltpu.make_async_copy(ids, table.at[me.pipe], own_sem.at[2])
    row.start()
    for step in range(1, 4):
        remote(
            ids, table.at[me.pipe], id_send.at[step], id_recv.at[step],
            {"dp": me.dp, "pipe": lax.rem(me.pipe + step, 4)},
        ).start()

    @pl.when(core == 0)
    def _():
        small_first.wait_recv()

    @pl.when(core == 1)
    def _():
        pltpu.make_async_copy(small.at[me.dp], early.at[0], own_sem.at[1]).wait()
        for step in range(1, 8):
            early_copy(step).wait()

        @pl.loop(0, 6)
        def _(i):
            part = pl.ds(pl.multiple_of(176 * i, 16), 176)
            total = early[0, part, :].astype(FULL)
            for step in range(1, 8):
                total = total + early[step, part, :].astype(FULL)
            chunk[part, :] = total.astype(LOW)

        small_first.start()
        copy = pltpu.make_async_copy(chunk.at[pl.ds(SMALL_HALF, SMALL_HALF)], all_small.at[x, me.dp, 1], own_sem.at[0])
        copy.start()
        copy.wait()

    light.step(0)
    for k, light_steps in ((1, (1,)), (2, (2, 3)), (3, (4,)), (4, (5,)), (5, ())):
        bulk.step(k)
        for light_step in light_steps:
            light.step(light_step)
    bulk.close()
    light.close()
    row.wait()
    for step in range(1, 4):
        here = lax.rem(me.pipe + 4 - step, 4)
        move = remote(
            ids, table.at[here], id_send.at[step], id_recv.at[step],
            {"dp": me.dp, "pipe": lax.rem(me.pipe + step, 4)},
        )
        move.wait_recv()
        move.wait_send()

    @pl.when(core == 0)
    def _():
        big_first.wait_send()

    @pl.when(core == 1)
    def _():
        small_first.wait_send()


def gather_all(big, small, ids):
    sem = pltpu.SemaphoreType.DMA
    return pl.pallas_call(
        gather_kernel,
        name="gather_all",
        out_shape=(
            jax.ShapeDtypeStruct((2, 8, 2, BIG_HALF, 128), LOW),
            jax.ShapeDtypeStruct((2, 8, 2, SMALL_HALF, 128), LOW),
            jax.ShapeDtypeStruct((4, 8, 128), jnp.int32),
        ),
        in_specs=[any_spec()] * 3,
        out_specs=(any_spec(),) * 3,
        scratch_shapes=[
            pltpu.VMEM((8, SMALL_ROWS, 128), LOW),
            pltpu.VMEM((SMALL_ROWS, 128), LOW),
            sem((8,)), sem((8,)),
            sem((2, 2, 4)), sem((2, 4)),
            sem((2, 4)), sem((2, 4)), sem((2, 4)), sem((2, 4)),
            sem((2, 4)), sem((2, 4)), sem((2, 4)), sem((2, 4)),
            sem((2, 16)), sem((2, 16)),
            sem((2,)), sem((2,)), sem((3,)), sem((4,)), sem((4,)), sem((2, 4, 4)), sem((4, 4)),
        ],
        compiler_params=pltpu.CompilerParams(
            collective_id=0, has_side_effects=True, vmem_limit_bytes=60 << 20
        ),
    )(big.reshape(WINDOW * TILE, 128), small.reshape(8, SMALL_ROWS, 128), ids)


def soft(value):
    return jnp.maximum(value, 0.0) + jnp.log1p(jnp.exp(-jnp.abs(value)))


def gate_of(value):
    small = jnp.exp(-jnp.abs(value))
    share = 1.0 / (1.0 + small)
    return jnp.where(value >= 0, share, small * share)


def standardize(z):
    count = z.shape[0]
    centre = jnp.sum(z, axis=0, keepdims=True) / count
    away = z - centre
    spread = jnp.sum(away * away, axis=0, keepdims=True) / count
    inverse = lax.rsqrt(spread + NORM_EPS)
    return away * inverse, centre, spread, inverse


def unstandardize(grad, standard, gain, inverse):
    count = grad.shape[0]
    grad_sum = jnp.sum(grad, axis=0, keepdims=True)
    grad_dot = jnp.sum(grad * standard, axis=0, keepdims=True)
    result = gain * inverse * (grad - grad_sum / count - standard * (grad_dot / count))
    return result, grad_dot, grad_sum


def pad_low(value):
    zeros = jnp.zeros((PADDED - ROWS, value.shape[1]), FULL)
    return jnp.concatenate([value, zeros], axis=0).astype(LOW)


def mul(a, b):
    return jnp.dot(a, b, preferred_element_type=FULL)


def mul_t(a, b):
    return lax.dot_general(a, b, (((1,), (1,)), ((), ())), preferred_element_type=FULL)


def narrow_part(ref, start, count, blocks=range(4)):
    return jnp.concatenate(
        [ref[pl.ds(start, count), 64 * j : 64 * j + 64, :].reshape(64 * count, 128) for j in blocks],
        axis=1,
    )


def put_narrow(ref, start, count, value):
    for j in range(4):
        ref[pl.ds(start, count), 64 * j : 64 * j + 64, :] = (
            value[:, 128 * j : 128 * j + 128].astype(LOW).reshape(count, 64, 128)
        )


def wide_part(ref, start, count, c):
    return jnp.concatenate(
        [
            ref[start : start + count, pl.ds(pl.multiple_of(32 * c + 16 * h, 16), 16), :].reshape(
                16 * count, 128
            )
            for h in range(2)
        ],
        axis=1,
    )


def put_wide(ref, start, count, c, value):
    for h in range(2):
        ref[start : start + count, pl.ds(pl.multiple_of(32 * c + 16 * h, 16), 16), :] = (
            value[:, 128 * h : 128 * h + 128].astype(LOW).reshape(count, 16, 128)
        )


def step_kernel(table, gates, teach_ids, stud_ids, all_big, all_small, x, targets, grid,
                wide0, wide1, final, stats, grad_x, out_big, out_small,
                w0, w1, w2, w3, edges, vec, grad_vec, raw,
                std_a, std_b, std_p, std_1, std_c, std_d, hidden, cols0, cols2,
                nar0, nar2, turned, relay, dz_a, dz_n, acc, acc_x, grad_h,
                wanted, inv, in_sem, edge_sem, out_sem):
    rank = lax.axis_index("pipe")
    gate = gates[rank].astype(FULL)
    for group in range(2):
        for j in range(8):
            inv[8 * group + table[2 * group, 0, j]] = j
    picks = [teach_ids[rank, k] for k in range(2)] + [stud_ids[rank, k] for k in range(3)]
    rows = [
        pltpu.make_async_copy(targets.at[pl.ds(pick, 1)], wanted.at[pl.ds(k, 1)], edge_sem.at[12 + k])
        for k, pick in enumerate(picks)
    ]
    for fetched in rows:
        fetched.start()
    weights = (w0, w1, w2, w3)
    loads = {0: [], 1: [], 2: [], 3: []}
    for group, weight, blocks in ((0, w0, 8), (1, w2, 6)):
        for b in range(blocks):
            first, here = 19 * b, inv[8 * group + b]
            at = 8 * group + b
            loads[2 * group].append(pltpu.make_async_copy(
                all_big.at[group, here, 0], weight.at[pl.ds(first, 10)], in_sem.at[0, at]))
            if first + 10 < USED_TILES[2 * group]:
                count = 10 if b == 7 else 9
                loads[2 * group].append(pltpu.make_async_copy(
                    all_big.at[group, here, 1, pl.ds(0, count)], weight.at[pl.ds(first + 10, count)],
                    in_sem.at[1, at]))
            if b < blocks - 1:
                at = 7 * group + b
                loads[2 * group].append(pltpu.make_async_copy(
                    all_big.at[group, here, 1, pl.ds(9, 1)], edges.at[pl.ds(at, 1)], edge_sem.at[at]))
    loads[1].append(pltpu.make_async_copy(all_small.at[0], w1, in_sem.at[0, 14]))
    loads[3].append(pltpu.make_async_copy(all_small.at[1], w3, in_sem.at[0, 15]))
    for section in range(4):
        for load in loads[section]:
            load.start()

    raw[...] = jnp.zeros_like(raw)
    grad_vec[...] = jnp.zeros_like(grad_vec)

    def settle(section):
        for load in loads[section]:
            load.wait()
        if section == 0:
            for b in range(7):
                w0[19 * b + 19] = (w0[19 * b + 19].astype(FULL) + edges[b].astype(FULL)).astype(LOW)
        if section == 2:
            for b in range(5):
                w2[19 * b + 19] = (
                    w2[19 * b + 19].astype(FULL) + edges[7 + b].astype(FULL)
                ).astype(LOW)
        vec[section] = weights[section][VEC_TILE[section], 0:48, :].astype(FULL)

    def row(section, start):
        return jnp.concatenate(
            [vec[section, pl.ds(start + h, 1), :] for h in range(2)], axis=1
        )

    def put_row(section, start, value):
        for h in range(2):
            grad_vec[section, pl.ds(start + h, 1), :] = value[:, 128 * h : 128 * h + 128]

    def put_stats(section, column, centre, spread):
        raw[2 * section : 2 * section + 1, pl.ds(column, 256)] = centre
        raw[2 * section + 1 : 2 * section + 2, pl.ds(column, 256)] = spread

    def inverse_of(section, column):
        return lax.rsqrt(raw[2 * section + 1 : 2 * section + 2, pl.ds(column, 256)] + NORM_EPS)

    def lanes(c):
        return pl.ds(pl.multiple_of(256 * c, 256), 256)

    at_row, at_col, side = grid[0], grid[1], grid[2]

    def masked(value, dr, dc):
        ok = (at_row + dr >= 0) & (at_row + dr < side) & (at_col + dc >= 0) & (at_col + dc < side)
        return jnp.concatenate(
            [jnp.where(ok, value[:, 128 * j : 128 * j + 128], 0.0) for j in range(4)], axis=1
        )

    def rolled(value, sign, dr, dc):
        parts = []
        for start, end, width in ((0, TEACH_ROWS, 6), (TEACH_ROWS, ROWS, 4)):
            by = (sign * (dr * width + dc)) % (end - start)
            part = value[start:end]
            parts.append(part if by == 0 else pltpu.roll(part, by, 0))
        return jnp.concatenate(parts, axis=0)

    def taps(stride):
        for t in range(9):
            r, q = t // 3, t % 3
            if stride == 1:
                yield t, 0, r - 1, q - 1
            else:
                phase = 2 * (1 if r != 1 else 0) + (1 if q != 1 else 0)
                yield t, phase, -1 if r == 0 else 0, -1 if q == 0 else 0

    settle(0)
    whole_x = x[...].reshape(4 * PADDED, C_IN)
    for c in range(2):
        z = mul(whole_x, narrow_part(w0, 0, 16, (2 * c, 2 * c + 1)))
        z = jnp.concatenate([z[PADDED * p : PADDED * p + ROWS] for p in range(4)], axis=0)
        standard, centre, spread, _ = standardize(z)
        put_stats(0, 256 * c, centre, spread)
        std_a[:, 256 * c : 256 * c + 256] = standard
        hidden[:, 256 * c : 256 * c + 256] = (
            soft(row(0, 2 * c) * standard + row(0, 4 + 2 * c)).astype(LOW).astype(FULL)
        )

    for t, phase, dr, dc in taps(2):
        cols0[t] = pad_low(masked(rolled(hidden[ROWS * phase : ROWS * phase + ROWS, :], -1, dr, dc), dr, dc))
    acc[...] = jnp.zeros_like(acc)

    @pl.loop(0, 9)
    def _(t):
        acc[...] += mul(cols0[t], narrow_part(w0, 16 + 8 * t, 8))

    def middle(section, std, nar):
        for c in range(2):
            at = slice(256 * c, 256 * c + 256)
            standard, centre, spread, _ = standardize(acc[0:ROWS, at])
            put_stats(section, MID + 256 * c, centre, spread)
            std[:, at] = standard
            nar[:, at] = pad_low(soft(row(section, 8 + 2 * c) * standard + row(section, 12 + 2 * c)))

    middle(0, std_b, nar0)
    acc[...] = jnp.zeros_like(acc)
    settle(1)
    settle(2)

    @pl.loop(0, 8)
    def _(c):
        at = lanes(c)
        standard, centre, spread, _ = standardize(mul(x[0], wide_part(w0, FRONT_WIDE, 64, c))[0:ROWS])
        put_stats(0, 2 * MID + pl.multiple_of(256 * c, 256), centre, spread)
        std_p[:, at] = standard
        low = pad_low(row(0, 16 + 2 * c) * standard + row(0, 32 + 2 * c))
        wide0[:, at] = low
        standard, centre, spread, _ = standardize(mul(nar0[...], wide_part(w1, 0, 32, c))[0:ROWS])
        put_stats(1, pl.multiple_of(256 * c, 256), centre, spread)
        std_1[:, at] = standard
        pre = low.astype(FULL)[0:ROWS] + row(1, 2 * c) * standard + row(1, 16 + 2 * c)
        low = pad_low(soft(pre))
        wide1[:, at] = low
        acc[...] += mul(low, narrow_part(w2, 4 * c, 4))

    for c in range(2):
        at = slice(256 * c, 256 * c + 256)
        standard, centre, spread, _ = standardize(acc[0:ROWS, at])
        put_stats(2, 256 * c, centre, spread)
        std_c[:, at] = standard
        hidden[0:ROWS, at] = soft(row(2, 2 * c) * standard + row(2, 4 + 2 * c)).astype(LOW).astype(FULL)
    for t, phase, dr, dc in taps(1):
        cols2[t] = pad_low(masked(rolled(hidden[0:ROWS, :], -1, dr, dc), dr, dc))
    acc[...] = jnp.zeros_like(acc)

    @pl.loop(0, 9)
    def _(t):
        acc[...] += mul(cols2[t], narrow_part(w2, 32 + 8 * t, 8))

    middle(2, std_d, nar2)

    turned[...] = nar2[...].T
    acc[...] = jnp.zeros_like(acc)
    settle(3)
    for fetched in rows:
        fetched.wait()

    def spread_rows(values):
        head = lax.broadcasted_iota(jnp.int32, (8, 256), 0) < 4
        first, second = (jnp.broadcast_to(value, (8, 256)) for value in values[0:2])
        parts = [jnp.broadcast_to(values[0], (32, 256)), jnp.where(head, first, second)]
        parts.append(jnp.broadcast_to(values[1], (32, 256)))
        parts.extend(jnp.broadcast_to(value, (16, 256)) for value in values[2:5])
        return jnp.concatenate(parts, axis=0)

    def crop_sums(value):
        head = lax.broadcasted_iota(jnp.int32, (8, 256), 0) < 4
        between = value[32:40]

        def total(part):
            return jnp.sum(part, axis=0, keepdims=True)

        return [
            total(value[0:32]) + total(jnp.where(head, between, 0.0)),
            total(value[40:72]) + total(jnp.where(head, 0.0, between)),
            total(value[72:88]),
            total(value[88:104]),
            total(value[104:120]),
        ]

    @pl.loop(0, 8)
    def _(c):
        at = lanes(c)
        weight = wide_part(w3, 0, 32, c)
        standard, centre, spread, inverse = standardize(mul(nar2[...], weight)[0:ROWS])
        put_stats(3, pl.multiple_of(256 * c, 256), centre, spread)
        gain = row(3, 2 * c)
        before = wide1[:, at].astype(FULL)[0:ROWS]
        pre = before + gain * standard + row(3, 16 + 2 * c)
        ending = jnp.where(gate > 0, soft(pre), before)
        final[:, at] = pad_low(ending)
        square = ending * ending
        factors = []
        for crop, total in enumerate(crop_sums(square * ending)):
            mean = total / (36.0 if crop < 2 else 16.0) + POOL_EPS
            factors.append(jnp.exp(jnp.log(mean) * (-2.0 / 3.0)) * wanted[crop : crop + 1, at])
        cotangent = spread_rows(factors) * square
        grad_pre = cotangent * gate_of(pre) * gate
        relay[:, at] = pad_low(grad_pre + cotangent * (1.0 - gate))
        result, grad_gain, grad_bias = unstandardize(grad_pre, standard, gain, inverse)
        put_row(3, 2 * c, grad_gain)
        put_row(3, 16 + 2 * c, grad_bias)
        low = pad_low(result)
        acc[...] += mul_t(low, weight)
        put_wide(w3, 0, 32, c, mul(turned[...], low))

    def flush(section):
        weights[section][VEC_TILE[section]] = grad_vec[section].astype(LOW)

    flush(3)
    stores = [pltpu.make_async_copy(w3, out_small.at[1], out_sem.at[15])]
    stores[-1].start()

    def middle_back(section, std):
        for c in range(2):
            at = slice(256 * c, 256 * c + 256)
            gain, bias = row(section, 8 + 2 * c), row(section, 12 + 2 * c)
            grad = acc[0:ROWS, at].astype(LOW).astype(FULL) * gate_of(gain * std[:, at] + bias)
            result, grad_gain, grad_bias = unstandardize(
                grad, std[:, at], gain, inverse_of(section, MID + 256 * c)
            )
            put_row(section, 8 + 2 * c, grad_gain)
            put_row(section, 12 + 2 * c, grad_bias)
            dz_n[:, at] = pad_low(result)

    def taps_back(weight, start, cols, stride, phases):
        grad_h[0 : ROWS * phases, :] = jnp.zeros((ROWS * phases, MID), FULL)
        for t, phase, dr, dc in taps(stride):
            part = mul_t(dz_n[...], narrow_part(weight, start + 8 * t, 8))[0:ROWS]
            at = slice(ROWS * phase, ROWS * phase + ROWS)
            grad_h[at, :] += rolled(masked(part, dr, dc), 1, dr, dc)
            put_narrow(weight, start + 8 * t, 8, mul(cols[t].T, dz_n[...]))

    middle_back(2, std_d)
    taps_back(w2, 32, cols2, 1, 1)
    for c in range(2):
        at = slice(256 * c, 256 * c + 256)
        gain, bias = row(2, 2 * c), row(2, 4 + 2 * c)
        grad = grad_h[0:ROWS, at] * gate_of(gain * std_c[:, at] + bias)
        result, grad_gain, grad_bias = unstandardize(grad, std_c[:, at], gain, inverse_of(2, 256 * c))
        put_row(2, 2 * c, grad_gain)
        put_row(2, 4 + 2 * c, grad_bias)
        dz_n[:, at] = pad_low(result)
    turned[...] = nar0[...].T
    acc[...] = jnp.zeros_like(acc)
    acc_x[...] = jnp.zeros_like(acc_x)

    @pl.loop(0, 8)
    def _(c):
        at = lanes(c)
        low = dz_n[...]
        grad = relay[:, at].astype(FULL) + mul_t(low, narrow_part(w2, 4 * c, 4))
        put_narrow(w2, 4 * c, 4, mul(wide1[:, at].T, low))
        grad = grad.astype(LOW).astype(FULL)[0:ROWS]
        gain = row(1, 2 * c)
        pre = wide0[:, at].astype(FULL)[0:ROWS] + gain * std_1[:, at] + row(1, 16 + 2 * c)
        grad = grad * gate_of(pre)
        result, grad_gain, grad_bias = unstandardize(
            grad, std_1[:, at], gain, inverse_of(1, pl.multiple_of(256 * c, 256))
        )
        put_row(1, 2 * c, grad_gain)
        put_row(1, 16 + 2 * c, grad_bias)
        low = pad_low(result)
        acc[...] += mul_t(low, wide_part(w1, 0, 32, c))
        put_wide(w1, 0, 32, c, mul(turned[...], low))
        grad = grad.astype(LOW).astype(FULL)
        result, grad_gain, grad_bias = unstandardize(
            grad, std_p[:, at], row(0, 16 + 2 * c), inverse_of(0, 2 * MID + pl.multiple_of(256 * c, 256))
        )
        put_row(0, 16 + 2 * c, grad_gain)
        put_row(0, 32 + 2 * c, grad_bias)
        low = pad_low(result)
        acc_x[...] += mul_t(low, wide_part(w0, FRONT_WIDE, 64, c))
        put_wide(w0, FRONT_WIDE, 64, c, mul(x[0].T, low))

    flush(1)
    flush(2)
    w2[105:115] = jnp.zeros((10, TILE, 128), LOW)
    stores.append(pltpu.make_async_copy(w1, out_small.at[0], out_sem.at[14]))
    stores[-1].start()
    for b in range(8):
        if b < 6:
            stores.append(pltpu.make_async_copy(
                w2.at[pl.ds(19 * b, 20)], out_big.at[1, inv[8 + b]], out_sem.at[8 + b]))
            stores[-1].start()
        else:
            for h in range(2):
                stores.append(pltpu.make_async_copy(
                    w2.at[pl.ds(105, 10)], out_big.at[1, inv[8 + b], pl.ds(10 * h, 10)],
                    out_sem.at[16 + 2 * (b - 6) + h]))
                stores[-1].start()

    middle_back(0, std_b)
    taps_back(w0, 16, cols0, 2, 4)
    for c in range(2):
        at = slice(256 * c, 256 * c + 256)
        gain, bias = row(0, 2 * c), row(0, 4 + 2 * c)
        grad = grad_h[:, at] * gate_of(gain * std_a[:, at] + bias)
        result, grad_gain, grad_bias = unstandardize(grad, std_a[:, at], gain, inverse_of(0, 256 * c))
        put_row(0, 2 * c, grad_gain)
        put_row(0, 4 + 2 * c, grad_bias)
        for p in range(4):
            dz_a[PADDED * p : PADDED * p + PADDED, at] = pad_low(result[ROWS * p : ROWS * p + ROWS])

    @pl.loop(0, 4)
    def _(c):
        at = lanes(c)
        low = dz_a[...]
        part = mul_t(low, narrow_part(w0, 4 * c, 4))
        grad_x[0, :, at] = (part[0:PADDED] + acc_x[:, at]).astype(LOW)
        for p in range(1, 4):
            grad_x[p, :, at] = part[PADDED * p : PADDED * p + PADDED].astype(LOW)
        turned_x = x[:, :, at].reshape(4 * PADDED, 256).T
        put_narrow(w0, 4 * c, 4, mul(turned_x, low))

    flush(0)
    for b in range(8):
        stores.append(pltpu.make_async_copy(
            w0.at[pl.ds(19 * b, 20)], out_big.at[0, inv[b]], out_sem.at[b]))
        stores[-1].start()
    for section in range(4):
        part = raw[2 * section : 2 * section + 2]
        stats[section, 0:2] = part if section < 2 else part * gate
        stats[section, 2:8] = jnp.zeros((6, 2 * MID + C_OUT), FULL)
    for store in stores:
        store.wait()


def run_step(table, gates, teach_ids, stud_ids, all_big, all_small, phases, targets):
    spots = np.zeros((3, ROWS, 128), np.int32)
    for r in range(ROWS):
        width = 6 if r < TEACH_ROWS else 4
        at = r % 36 if r < TEACH_ROWS else (r - TEACH_ROWS) % 16
        spots[0, r], spots[1, r], spots[2, r] = at // width, at % width, width
    sem = pltpu.SemaphoreType.DMA
    wide = jax.ShapeDtypeStruct((PADDED, C_OUT), LOW)
    vm = pltpu.VMEM
    return pl.pallas_call(
        step_kernel,
        name="step",
        out_shape=(
            wide, wide, wide,
            jax.ShapeDtypeStruct((4, 8, 2 * MID + C_OUT), FULL),
            jax.ShapeDtypeStruct((4, PADDED, C_IN), LOW),
            jax.ShapeDtypeStruct((2, 8, WINDOW, TILE, 128), LOW),
            jax.ShapeDtypeStruct((2, USED_TILES[1], TILE, 128), LOW),
        ),
        in_specs=[smem_spec()] * 4 + [any_spec(), any_spec(), vmem_spec(), any_spec(), vmem_spec()],
        out_specs=(vmem_spec(),) * 5 + (any_spec(),) * 2,
        scratch_shapes=[
            vm((153, TILE, 128), LOW), vm((33, TILE, 128), LOW), vm((115, TILE, 128), LOW), vm((33, TILE, 128), LOW),
            vm((12, TILE, 128), LOW), vm((4, 48, 128), FULL), vm((4, TILE, 128), FULL),
            vm((8, 2 * MID + C_OUT), FULL),
            vm((4 * ROWS, MID), FULL), vm((ROWS, MID), FULL), vm((ROWS, C_OUT), FULL), vm((ROWS, C_OUT), FULL),
            vm((ROWS, MID), FULL), vm((ROWS, MID), FULL), vm((4 * ROWS, MID), FULL),
            vm((9, PADDED, MID), LOW), vm((9, PADDED, MID), LOW),
            vm((PADDED, MID), LOW), vm((PADDED, MID), LOW), vm((MID, PADDED), LOW),
            vm((PADDED, C_OUT), LOW), vm((4 * PADDED, MID), LOW), vm((PADDED, MID), LOW),
            vm((PADDED, MID), FULL), vm((PADDED, C_IN), FULL), vm((4 * ROWS, MID), FULL),
            vm((8, C_OUT), FULL), pltpu.SMEM((16,), jnp.int32),
            sem((2, 16)), sem((17,)), sem((20,)),
        ],
        compiler_params=pltpu.CompilerParams(vmem_limit_bytes=60 << 20),
    )(table, gates, teach_ids, stud_ids, all_big, all_small, phases, targets, jnp.asarray(spots))


def reduce_kernel(big, small, wide0, wide1, final, stats, table,
                  out_big, out_small, segments, out_stats, norm, factor,
                  got, halves_x, halves_y, from_x, from_y, from_low, from_high, stage, total,
                  l_got, l_stage, l_low, l_high, l_halves_x, l_halves_y, l_from_x, l_from_y, l_total,
                  late, late_half, owner_row, by_pipe, by_dp, mine, part_sum,
                  s_send, s_recv, hx_send, hx_recv, hy_send, hy_recv, x_send, x_recv, y_send, y_recv,
                  zu_send, zu_recv, zd_send, zd_recv, lu_send, lu_recv, ld_send, ld_recv,
                  stage_sem, l_stage_sem, out_sem, late_send, late_recv, join_send, join_recv,
                  seg_send, seg_recv, stat_send, stat_recv, p_send, p_recv, d_send, d_recv):
    me = Place()
    me.enter()
    x, y, z, core = me.x, me.y, me.z, me.core
    up, down = me.device(z=z + 1), me.device(z=z - 1)
    x_side, y_side, sibling = me.device(x=1 - x), me.device(y=1 - y), me.device(core=1 - core)
    order = [
        jnp.where(z < 2, 3, 0),
        jnp.where(z == 0, 2, jnp.where(z == 1, 0, jnp.where(z == 2, 3, 1))),
        jnp.where(z == 0, 1, jnp.where(z == 1, 2, jnp.where(z == 2, 1, 2))),
        z,
    ]
    columns = ((1 - x, 1 - y), (x, 1 - y), (1 - x, y), (x, y))
    sides = [[(1, k), (2, k)] for k in range(4)]
    sequence = [(0, 0), (0, 1), (0, 2), (0, 3)] + sides[0] + sides[1] + [(3, 0)] + sides[2]
    sequence += [(3, 1)] + sides[3] + [(3, 2), (3, 3)]
    l_sequence = [(group, k) for k in range(4) for group in range(4)]

    def all_of(copies, act):
        for copy in copies:
            act(copy)

    def over(start, count, piece):
        whole = count // 512
        if whole:

            @pl.loop(0, whole)
            def _(i):
                piece(pl.multiple_of(start + 512 * i, 16), 512)

        if count % 512:
            piece(start + 512 * whole, count % 512)

    def source(array, group, k, half):
        xo, yo = columns[group]
        return array.at[xo, 2 * order[k] + yo, half]

    def share(group, k):
        at = 4 * group + k
        return remote(source(big, group, k, 1 - core), got.at[at], s_send.at[0, at], s_recv.at[0, at], sibling)

    def l_share(group, k):
        at = 4 * group + k
        return remote(source(small, group, k, 1 - core), l_got.at[at], s_send.at[1, at], s_recv.at[1, at], sibling)

    def fetch(n):
        return pltpu.make_async_copy(source(big, *sequence[n], core), stage.at[n % 4], stage_sem.at[n % 4])

    def l_fetch(group, k):
        at = 4 * group + k
        return pltpu.make_async_copy(source(small, group, k, core), l_stage.at[at], l_stage_sem.at[at])

    def add(target, at, other, slot, start, count, extras):
        def piece(begin, size):
            part = pl.ds(begin, size)
            sums = target[at, part, :].astype(FULL) + other[slot, part, :].astype(FULL)
            for ref, k in extras:
                sums = sums + ref[k, pl.ds(begin - start, size), :].astype(FULL)
            target[at, part, :] = sums.astype(LOW)

        over(start, count, piece)

    def send_half_x(k):
        return remote(got.at[k, pl.ds(BACK_CUT, BIG_HALF - BACK_CUT)], halves_x.at[k],
                      hx_send.at[k], hx_recv.at[k], x_side)

    def send_half_y(k):
        return remote(got.at[k, pl.ds(0, BACK_CUT)], halves_y.at[k], hy_send.at[k], hy_recv.at[k], y_side)

    def send_y(k):
        return remote(got.at[4 + k], from_y.at[k], y_send.at[k], y_recv.at[k], y_side)

    def send_x(k):
        return remote(got.at[8 + k], from_x.at[k], x_send.at[k], x_recv.at[k], x_side)

    def send_up(at, zd):
        return remote(got.at[at], from_low.at[zd - 1], zu_send.at[zd - 1], zu_recv.at[zd - 1], up)

    def send_down(at, zd):
        return remote(got.at[at], from_high.at[zd], zd_send.at[zd], zd_recv.at[zd], down)

    def l_column(group):
        xo, yo = columns[group]
        return 2 * xo + yo

    def l_up(group, k):
        at, zd = l_column(group), order[k] - 1
        return remote(l_got.at[4 * group + k], l_low.at[at, zd], lu_send.at[at, zd], lu_recv.at[at, zd], up)

    def l_down(group, k):
        at, zd = l_column(group), order[k]
        return remote(l_got.at[4 * group + k], l_high.at[at, zd], ld_send.at[at, zd], ld_recv.at[at, zd], down)

    def l_half_x():
        return remote(l_got.at[3, pl.ds(LIGHT_CUT, SMALL_HALF - LIGHT_CUT)], l_halves_x,
                      hx_send.at[4], hx_recv.at[4], x_side)

    def l_half_y():
        return remote(l_got.at[3, pl.ds(0, LIGHT_CUT)], l_halves_y, hy_send.at[4], hy_recv.at[4], y_side)

    def l_send_y():
        return remote(l_got.at[7], l_from_y, y_send.at[4], y_recv.at[4], y_side)

    def l_send_x():
        return remote(l_got.at[11], l_from_x, x_send.at[4], x_recv.at[4], x_side)

    leaving = (wide0, wide1, wide1, final)

    def exchange(section):
        target = {"dp": me.dp, "pipe": section}
        yield remote(leaving[section], segments.at[me.pipe], seg_send.at[section], seg_recv.at[me.pipe], target)
        yield remote(stats.at[section], out_stats.at[me.pipe], stat_send.at[section], stat_recv.at[me.pipe], target)

    def keep(section):
        yield pltpu.make_async_copy(leaving[section], segments.at[me.pipe], seg_send.at[section])
        yield pltpu.make_async_copy(stats.at[section], out_stats.at[me.pipe], stat_send.at[section])

    def arriving(micro):
        target = {"dp": me.dp, "pipe": micro}
        yield remote(wide0, segments.at[micro], seg_send.at[micro], seg_recv.at[micro], target)
        yield remote(stats.at[0], out_stats.at[micro], stat_send.at[micro], stat_recv.at[micro], target)

    for n in range(4):
        share(*sequence[n]).start()
    for item in l_sequence[0:4]:
        l_share(*item).start()
    for n in range(2):
        fetch(n).start()
    for group, k in l_sequence:
        l_fetch(group, k).start()
    row_copy = pltpu.make_async_copy(table.at[2 * x], owner_row, out_sem.at[2])
    row_copy.start()

    def bulk_item(n):
        group, k = sequence[n]
        at, slot = 4 * group + k, n % 4
        if n + 2 < 16:
            fetch(n + 2).start()
        fetch(n).wait()
        share(group, k).wait_recv()
        if n + 4 < 16:
            share(*sequence[n + 4]).start()
        if group == 0:
            add(got, at, stage, slot, 0, BIG_HALF, [])
            send_half_x(k).start()
            send_half_y(k).start()
        elif group == 1:
            send_half_x(k).wait_recv()
            add(got, at, stage, slot, 0, BACK_CUT, [])
            add(got, at, stage, slot, BACK_CUT, BIG_HALF - BACK_CUT, [(halves_x, k)])
            send_y(k).start()
        elif group == 2:
            send_half_y(k).wait_recv()
            add(got, at, stage, slot, 0, BACK_CUT, [(halves_y, k)])
            add(got, at, stage, slot, BACK_CUT, BIG_HALF - BACK_CUT, [])
            send_x(k).start()
        else:
            send_x(k).wait_recv()
            send_y(k).wait_recv()
            add(got, at, stage, slot, 0, BIG_HALF, [(from_x, k), (from_y, k)])

    def bulk_z(k):
        at, zd = 12 + k, order[k]

        @pl.when(zd > z)
        def _():
            @pl.when(z > 0)
            def _():
                send_up(at, zd).wait_recv()
                add(got, at, from_low, zd - 1, 0, BIG_HALF, [])

            send_up(at, zd).start()

        @pl.when(zd < z)
        def _():
            @pl.when(z < 3)
            def _():
                send_down(at, zd).wait_recv()
                add(got, at, from_high, zd, 0, BIG_HALF, [])

            send_down(at, zd).start()

    def light_item(group, k):
        at, zd, column = 4 * group + k, order[k], l_column(group)
        l_fetch(group, k).wait()
        l_share(group, k).wait_recv()
        add(l_got, at, l_stage, at, 0, SMALL_HALF, [])

        def merge(ref, slot):
            l_got[at] = (l_got[at].astype(FULL) + ref[column, slot].astype(FULL)).astype(LOW)

        if k < 3:

            @pl.when(zd > z)
            def _():
                @pl.when(z > 0)
                def _():
                    l_up(group, k).wait_recv()
                    merge(l_low, zd - 1)

                l_up(group, k).start()

            @pl.when(zd < z)
            def _():
                @pl.when(z < 3)
                def _():
                    l_down(group, k).wait_recv()
                    merge(l_high, zd)

                l_down(group, k).start()

        else:

            @pl.when(z > 0)
            def _():
                l_up(group, k).wait_recv()
                merge(l_low, zd - 1)

            @pl.when(z < 3)
            def _():
                l_down(group, k).wait_recv()
                merge(l_high, zd)

            if group == 0:
                l_half_x().start()
                l_half_y().start()

    def light_sides():
        l_half_x().wait_recv()
        l_got[7, LIGHT_CUT:SMALL_HALF, :] = (
            l_got[7, LIGHT_CUT:SMALL_HALF, :].astype(FULL) + l_halves_x[...].astype(FULL)
        ).astype(LOW)
        l_send_y().start()
        l_half_y().wait_recv()
        l_got[11, 0:LIGHT_CUT, :] = (
            l_got[11, 0:LIGHT_CUT, :].astype(FULL) + l_halves_y[...].astype(FULL)
        ).astype(LOW)
        l_send_x().start()

    def light_end():
        l_send_x().wait_recv()
        l_send_y().wait_recv()
        l_total[...] = l_got[15].astype(FULL) + l_from_x[...].astype(FULL) + l_from_y[...].astype(FULL)

    small_join = remote(late_half, late.at[pl.ds(0, SMALL_HALF)], join_send.at[1], join_recv.at[1], sibling)
    own_late = pltpu.make_async_copy(late, out_small.at[me.dp], out_sem.at[1])

    def late_copy(step, slot):
        target = {"dp": lax.rem(me.dp + step, 8), "pipe": me.pipe}
        return remote(late, out_small.at[slot], late_send.at[step], late_recv.at[step], target)

    def leave():
        for section in range(4):
            @pl.when(me.pipe == section)
            def _(section=section):
                all_of(keep(section), lambda copy: copy.start())

            @pl.when(me.pipe != section)
            def _(section=section):
                all_of(exchange(section), lambda copy: copy.start())

    def late_start():
        light_end()

        @pl.when(core == 0)
        def _():
            late_half[...] = l_total[...].astype(LOW)
            small_join.start()

        @pl.when(core == 1)
        def _():
            late[SMALL_HALF:SMALL_ROWS, :] = l_total[...].astype(LOW)
            small_join.wait_recv()
            own_late.start()
            for step in range(1, 8):
                late_copy(step, me.dp).start()

    def light_round(k):
        for n in range(4 * k, 4 * k + 4):
            light_item(*l_sequence[n])
            if n + 4 < 16:
                l_share(*l_sequence[n + 4]).start()

    edge = (z == 0) | (z == 3)

    def early_z(k):
        pl.when(edge)(lambda: bulk_z(k))

    def inner_z(k):
        pl.when(jnp.logical_not(edge))(lambda: bulk_z(k))

    for n in range(4):
        bulk_item(n)
    light_round(0)
    for n in range(4, 8):
        bulk_item(n)
    light_round(1)
    light_round(2)
    light_round(3)
    bulk_item(8)
    early_z(0)
    bulk_item(9)
    bulk_item(10)
    light_sides()
    bulk_item(11)
    early_z(1)
    bulk_item(12)
    bulk_item(13)
    late_start()
    inner_z(0)
    leave()
    bulk_item(14)
    early_z(2)
    inner_z(1)
    bulk_item(15)
    inner_z(2)

    row_copy.wait()
    part_sum[...] = jnp.sum((l_total[...] * l_total[...]).reshape(SMALL_HALF // 8, 8, 128), axis=0)
    lane = lax.broadcasted_iota(jnp.int32, (8, 128), 1)
    is_last = jnp.where((lane == me.dp) & (owner_row[...] == 7), 1.0, 0.0)
    weight = jnp.broadcast_to(jnp.sum(is_last, axis=1, keepdims=True), (8, 128))
    weight = jnp.where(core == 0, jnp.ones((8, 128), FULL), weight)

    def end(low, high):
        def piece(begin, size, scale):
            part = pl.ds(begin, size)
            sums = got[15, part, :].astype(FULL)
            if low:
                sums = sums + from_low[z - 1, part, :].astype(FULL)
            if high:
                sums = sums + from_high[z, part, :].astype(FULL)
            total[part, :] = sums
            squares = jnp.sum((sums * sums).reshape(size // 8, 8, 128), axis=0)
            part_sum[...] += squares if scale is None else squares * scale

        over(0, BIG_HALF - 256, lambda begin, size: piece(begin, size, None))
        piece(BIG_HALF - 256, 256, weight)

    @pl.when(z == 0)
    def _():
        send_down(15, z).wait_recv()
        end(False, True)

    @pl.when((z > 0) & (z < 3))
    def _():
        send_up(15, z).wait_recv()
        send_down(15, z).wait_recv()
        end(True, True)

    @pl.when(z == 3)
    def _():
        send_up(15, z).wait_recv()
        end(True, False)

    big_join = remote(total, out_big.at[1], join_send.at[0], join_recv.at[0], sibling)
    own_big = pltpu.make_async_copy(total, out_big.at[0], out_sem.at[0])

    @pl.when(core == 0)
    def _():
        own_big.start()

    @pl.when(core == 1)
    def _():
        big_join.start()

    def along_pipe(step, slot):
        target = {"dp": me.dp, "pipe": lax.rem(me.pipe + step, 4)}
        return remote(part_sum, by_pipe.at[slot], p_send.at[step], p_recv.at[step], target)

    def along_dp(step, slot):
        target = {"dp": lax.rem(me.dp + step, 8), "pipe": me.pipe}
        return remote(mine, by_dp.at[slot], d_send.at[step], d_recv.at[step], target)

    for step in range(1, 4):
        along_pipe(step, me.pipe).start()
    by_pipe[me.pipe] = part_sum[...]
    for step in range(1, 4):
        along_pipe(step, lax.rem(me.pipe + 4 - step, 4)).wait_recv()
    mine[...] = jnp.sum(by_pipe[...], axis=0)
    for step in range(1, 8):
        along_dp(step, me.dp).start()
    by_dp[me.dp] = mine[...]
    for step in range(1, 8):
        along_dp(step, lax.rem(me.dp + 8 - step, 8)).wait_recv()
    whole = jnp.sum(jnp.sum(by_dp[...], axis=0), axis=0, keepdims=True)
    length = jnp.sqrt(jnp.broadcast_to(jnp.sum(whole, axis=1, keepdims=True), (8, 128)))
    norm[...] = length
    factor[...] = jnp.minimum(1.0, CLIP_NORM / length)

    @pl.when(core == 0)
    def _():
        own_big.wait()
        big_join.wait_recv()
        small_join.wait_send()

    @pl.when(core == 1)
    def _():
        big_join.wait_send()
        own_late.wait()
        for step in range(1, 8):
            late_copy(step, lax.rem(me.dp + 8 - step, 8)).wait_recv()
            late_copy(step, me.dp).wait_send()

    for other in range(4):
        @pl.when(me.pipe == other)
        def _(other=other):
            all_of(keep(other), lambda copy: copy.wait())

        @pl.when(me.pipe != other)
        def _(other=other):
            all_of(exchange(other), lambda copy: copy.wait_send())
            all_of(arriving(other), lambda copy: copy.wait_recv())

    for step in range(1, 4):
        along_pipe(step, me.pipe).wait_send()
    for step in range(1, 8):
        along_dp(step, me.dp).wait_send()
    for copy in (l_half_x(), l_half_y(), l_send_x(), l_send_y()):
        copy.wait_send()
    for k in range(4):
        send_half_x(k).wait_send()
        send_half_y(k).wait_send()
        send_x(k).wait_send()
        send_y(k).wait_send()
        for group in range(4):
            share(group, k).wait_send()
            l_share(group, k).wait_send()
    for k in range(3):
        zd, at = order[k], 12 + k

        @pl.when(zd > z)
        def _(at=at, zd=zd, k=k):
            send_up(at, zd).wait_send()
            for group in range(4):
                l_up(group, k).wait_send()

        @pl.when(zd < z)
        def _(at=at, zd=zd, k=k):
            send_down(at, zd).wait_send()
            for group in range(4):
                l_down(group, k).wait_send()


def reduce_all(big, small, wide0, wide1, final, stats, table):
    sem = pltpu.SemaphoreType.DMA
    vm = pltpu.VMEM
    lane_tile = jax.ShapeDtypeStruct((8, 128), FULL)
    return pl.pallas_call(
        reduce_kernel,
        name="reduce_all",
        out_shape=(
            jax.ShapeDtypeStruct((2, BIG_HALF, 128), FULL),
            jax.ShapeDtypeStruct((8, SMALL_ROWS, 128), LOW),
            jax.ShapeDtypeStruct((4,) + wide0.shape, LOW),
            jax.ShapeDtypeStruct((4,) + stats.shape[1:], FULL),
            lane_tile,
            lane_tile,
        ),
        in_specs=[any_spec()] * 7,
        out_specs=(any_spec(),) * 4 + (vmem_spec(),) * 2,
        scratch_shapes=[
            vm((16, BIG_HALF, 128), LOW), vm((4, BIG_HALF - BACK_CUT, 128), LOW), vm((4, BACK_CUT, 128), LOW),
            vm((4, BIG_HALF, 128), LOW), vm((4, BIG_HALF, 128), LOW),
            vm((3, BIG_HALF, 128), LOW), vm((3, BIG_HALF, 128), LOW),
            vm((4, BIG_HALF, 128), LOW), vm((BIG_HALF, 128), FULL),
            vm((16, SMALL_HALF, 128), LOW), vm((16, SMALL_HALF, 128), LOW),
            vm((4, 3, SMALL_HALF, 128), LOW), vm((4, 3, SMALL_HALF, 128), LOW),
            vm((SMALL_HALF - LIGHT_CUT, 128), LOW), vm((LIGHT_CUT, 128), LOW),
            vm((SMALL_HALF, 128), LOW), vm((SMALL_HALF, 128), LOW), vm((SMALL_HALF, 128), FULL),
            vm((SMALL_ROWS, 128), LOW), vm((SMALL_HALF, 128), LOW), vm((8, 128), jnp.int32),
            vm((4, 8, 128), FULL), vm((8, 8, 128), FULL), vm((8, 128), FULL), vm((8, 128), FULL),
            sem((2, 16)), sem((2, 16)),
            sem((5,)), sem((5,)), sem((5,)), sem((5,)), sem((5,)), sem((5,)), sem((5,)), sem((5,)),
            sem((3,)), sem((3,)), sem((3,)), sem((3,)),
            sem((4, 3)), sem((4, 3)), sem((4, 3)), sem((4, 3)),
            sem((4,)), sem((16,)), sem((3,)), sem((8,)), sem((8,)), sem((2,)), sem((2,)),
            sem((4,)), sem((4,)), sem((4,)), sem((4,)), sem((4,)), sem((4,)), sem((8,)), sem((8,)),
        ],
        compiler_params=pltpu.CompilerParams(
            collective_id=1, has_side_effects=True, vmem_limit_bytes=62 << 20
        ),
    )(big.reshape(2, 8, 2, BIG_HALF, 128), small.reshape(2, 8, 2, SMALL_HALF, 128),
      wide0, wide1, final, stats, table)


def high_dot(a, b, dims=((1,), (0,))):
    return lax.dot_general(a, b, (dims, ((), ())), precision=HIGH, preferred_element_type=FULL)


PIECES = 7
FRONT = 48


def update_kernel(owners, factor_ref, big, small, gram_old, basis_old, params, moment, second,
                  clipped, moment_new, second_new, params_new, gram_new, basis_new,
                  tiles, low, grad, held, rotated, weights, gram, in_sem, out_sem, tile_sem):
    factor = factor_ref[0:1, :]
    block, section = owners[0, lax.axis_index("dp")], lax.axis_index("pipe")
    even = lax.rem(section, 2) == 0
    span = params.shape[0]
    piece = held.shape[0] // PIECES

    @pl.when(even)
    def _():
        pltpu.make_async_copy(big, tiles, tile_sem).start()

    def loads(i):
        part = pl.ds(piece * i, min(piece, span - piece * i))
        for n, (src, dst) in enumerate(((params, weights), (moment, held), (second, rotated))):
            yield pltpu.make_async_copy(src.at[part, 0, :], dst.at[part], in_sem.at[n, i])

    def stores(i):
        count = min(piece, span - piece * i)
        part = pl.ds(piece * i, count)
        yield pltpu.make_async_copy(
            grad.at[pl.ds(FRONT + piece * i, count)], clipped.at[part, 0, :], out_sem.at[3, i])
        pairs = ((held, moment_new), (rotated, second_new), (weights, params_new))
        for n, (src, dst) in enumerate(pairs):
            yield pltpu.make_async_copy(src.at[part], dst.at[part, 0, :], out_sem.at[n, i])

    for i in range(PIECES):
        for load in loads(i):
            load.start()

    @pl.when(even)
    def _():
        pltpu.make_async_copy(big, tiles, tile_sem).wait()

    @pl.when(jnp.logical_not(even))
    def _():
        low[...] = jnp.zeros_like(low)

        @pl.when(block == 0)
        def _():
            copy = pltpu.make_async_copy(small.at[0:20], low, tile_sem)
            copy.start()
            copy.wait()

        @pl.when(block == 1)
        def _():
            copy = pltpu.make_async_copy(small.at[19:33], low.at[0:14], tile_sem)
            copy.start()
            copy.wait()

        @pl.loop(0, WINDOW)
        def _(r):
            tiles[r] = low[r].astype(FULL)

    @pl.loop(0, WINDOW)
    def _(r):
        narrow, plain = tile_forms(section, STRIDE * block + r)
        base = FRONT - 6 * block + TILE * r

        @pl.when(narrow)
        def _():
            for j in range(4):
                grad[pl.ds(base + j, 64, 4), :] = tiles[r, 64 * j : 64 * j + 64, :]

        @pl.when(plain)
        def _():
            grad[pl.ds(base, TILE), :] = tiles[r]

        @pl.when(jnp.logical_not(narrow | plain))
        def _():
            for j in range(16):
                grad[pl.ds(base + j, 16, 16), :] = tiles[r, 16 * j : 16 * j + 16, :]

    tail = piece * PIECES - 8
    rest = lax.broadcasted_iota(jnp.int32, (8, 128), 0) + tail
    grad[FRONT + tail : FRONT + tail + 8, :] = jnp.where(
        rest < span, grad[FRONT + tail : FRONT + tail + 8, :], 0.0
    )
    gram[...] = jnp.zeros_like(gram)

    def halves(value):
        high = value.astype(LOW)
        return high, (value - high.astype(FULL)).astype(LOW)

    def split_dot(a, b, dims=((1,), (0,))):
        def dot(left, right):
            return lax.dot_general(left, right, (dims, ((), ())), preferred_element_type=FULL)

        return dot(a[0], b[0]) + (dot(a[0], b[1]) + dot(a[1], b[0]))

    @pl.loop(0, PIECES)
    def _(i):
        part = halves(grad[pl.ds(pl.multiple_of(FRONT + piece * i, 8), piece), :])
        gram[...] += split_dot(part, part, ((0,), (0,)))

    old = basis_old[...]
    fresh = DECAY_STATS * gram_old[...] + (1.0 - DECAY_STATS) * (gram[...] * (factor * factor))
    gram_new[...] = fresh
    product = high_dot(fresh, old)
    rotation = product / jnp.sqrt(jnp.sum(product * product))
    for repeat in range(NS_STEPS):
        square = high_dot(rotation, rotation, ((0,), (0,)))
        rotation = 1.5 * rotation - 0.5 * high_dot(rotation, square)
    basis_new[...] = rotation
    change = halves(high_dot(old, rotation, ((0,), (0,))))
    turn = halves(rotation)
    correction = math.sqrt(1.0 - DECAY_SECOND**STEP) / (1.0 - DECAY_FIRST**STEP)
    for i in range(PIECES):
        for load in loads(i):
            load.wait()
        at = slice(FRONT + piece * i, FRONT + piece * i + piece)
        part = slice(piece * i, piece * i + piece)
        clip = grad[at, :] * factor
        grad[at, :] = clip
        turned = split_dot(halves(clip), turn)
        first = DECAY_FIRST * split_dot(halves(held[part, :]), change) + (1.0 - DECAY_FIRST) * turned
        power = DECAY_SECOND * rotated[part, :] + (1.0 - DECAY_SECOND) * turned * turned
        held[part, :] = first
        rotated[part, :] = power
        scaled = halves(first / (jnp.sqrt(power) + ADAM_EPS))
        direction = split_dot(scaled, turn, ((1,), (1,))) * correction
        before = weights[part, :]
        weights[part, :] = before - LEARN_RATE * (direction + WEIGHT_DECAY * before)
        for store in stores(i):
            store.start()
    for i in range(PIECES):
        for store in stores(i):
            store.wait()


def update(owners, factor, big, small, gram_old, basis_old, params, moment, second):
    span = params.shape[1] // 128
    rows = -(-span // (8 * PIECES)) * 8 * PIECES
    flat_shape = jax.ShapeDtypeStruct((span, 1, 128), FULL)
    square = jax.ShapeDtypeStruct((128, 128), FULL)
    sem = pltpu.SemaphoreType.DMA
    vm = pltpu.VMEM
    outs = pl.pallas_call(
        update_kernel,
        name="update",
        out_shape=(flat_shape,) * 4 + (square,) * 2,
        in_specs=[smem_spec(), vmem_spec()] + [any_spec()] * 2 + [vmem_spec()] * 2 + [any_spec()] * 3,
        out_specs=(any_spec(),) * 4 + (vmem_spec(),) * 2,
        scratch_shapes=[
            vm((WINDOW, TILE, 128), FULL), vm((WINDOW, TILE, 128), LOW),
            vm((FRONT + WINDOW * TILE, 128), FULL), vm((rows, 128), FULL), vm((rows, 128), FULL),
            vm((rows, 128), FULL), vm((128, 128), FULL), sem((3, PIECES)), sem((4, PIECES)), sem,
        ],
        compiler_params=pltpu.CompilerParams(vmem_limit_bytes=60 << 20),
    )(owners, factor, big.reshape(WINDOW, TILE, 128), small.reshape(USED_TILES[1], TILE, 128),
      gram_old, basis_old, params.reshape(span, 1, 128), moment.reshape(span, 1, 128),
      second.reshape(span, 1, 128))
    return tuple(out.reshape(1, span * 128) for out in outs[:4]) + outs[4:]


def to_phases(teach, stud):
    def split(part):
        crops, high, across, channels = part.shape
        part = part.reshape(crops, high // 2, 2, across // 2, 2, channels).transpose(2, 4, 0, 1, 3, 5)
        return part.reshape(4, -1, channels)

    zeros = jnp.zeros((4, PADDED - ROWS, teach.shape[-1]), teach.dtype)
    return jnp.concatenate([split(teach), split(stud), zeros], axis=1)


def from_phases(phases, shape):
    crops, high, across, channels = shape
    part = phases.reshape(2, 2, crops, high // 2, across // 2, channels)
    return part.transpose(2, 3, 0, 4, 1, 5).reshape(shape)


def on_small_slice(
    teach_in,
    stud_in,
    params,
    owners,
    depth_gates,
    teach_ids,
    stud_ids,
    targets,
    moment,
    second,
    gram_stats,
    eigen_basis,
):
    phases = to_phases(teach_in[0], stud_in[0])
    big, small, ids = prepare(owners, params)
    all_big, all_small, table = gather_all(big, small, ids)
    wide_0, wide_1, final, stats, grad_x, out_big, out_small = run_step(
        table,
        depth_gates,
        teach_ids,
        stud_ids,
        all_big.reshape(2, 8, 2, WINDOW // 2, TILE, 128),
        all_small.reshape(2, USED_TILES[1], TILE, 128),
        phases,
        targets,
    )
    sum_big, sum_small, segments, stats, norm, factor = reduce_all(
        out_big, out_small, wide_0, wide_1, final, stats, table
    )
    clipped, moment_new, second_new, params_new, gram_new, rotation = update(
        owners, factor, sum_big, sum_small, gram_stats[0], eigen_basis[0], params, moment, second
    )
    teach_shape, stud_shape = teach_in.shape[1:], stud_in.shape[1:]
    small_teach = (teach_shape[0], teach_shape[1] // 2, teach_shape[2] // 2, C_OUT)
    small_stud = (stud_shape[0], stud_shape[1] // 2, stud_shape[2] // 2, C_OUT)
    segment_teach = segments[:, :TEACH_ROWS].reshape((4,) + small_teach)
    segment_stud = segments[:, TEACH_ROWS:ROWS].reshape((4,) + small_stud)
    stats = stats[:, 0:2]
    teach_grad = from_phases(grad_x[:, :TEACH_ROWS], teach_shape)
    stud_grad = from_phases(grad_x[:, TEACH_ROWS:ROWS], stud_shape)
    grad_norm = norm[0, 0]
    return (
        segment_teach[None],
        segment_stud[None],
        teach_grad[None],
        stud_grad[None],
        stats[None, :, None],
        grad_norm,
        clipped,
        moment_new,
        second_new,
        params_new,
        gram_new[None],
        rotation[None],
    )


def solution(mesh):
    placed = (
        P("pipe", "dp", None, None, None),
        P("pipe", "dp", None, None, None),
        P("pipe", "dp"),
        P("pipe", None),
        P(),
        P(None, "dp"),
        P(None, "dp"),
        P(),
        P("pipe", "dp"),
        P("pipe", "dp"),
        P("pipe", "dp", None),
        P("pipe", "dp", None),
    )
    small_slice = mesh.shape["dp"] == 8 and mesh.shape["pipe"] == 4
    return jax.shard_map(
        on_small_slice if small_slice else on_device,
        mesh=mesh,
        in_specs=placed,
        out_specs=(
            P("pipe", None, "dp", None, None, None),
            P("pipe", None, "dp", None, None, None),
            P("pipe", "dp", None, None, None),
            P("pipe", "dp", None, None, None),
            P("pipe", None, "dp", None, None),
            P(),
            P("pipe", "dp"),
            P("pipe", "dp"),
            P("pipe", "dp"),
            P("pipe", "dp"),
            P("pipe", "dp", None),
            P("pipe", "dp", None),
        ),
        check_vma=False,
    )
```

```python
import functools
import math

import jax
import jax.numpy as jnp
import numpy as np
from jax import lax
from jax.experimental import pallas as pl
from jax.experimental.pallas import tpu as pltpu
from jax.sharding import PartitionSpec as P

C_IN = 1024
MID = 512
C_OUT = 2048
STEP = 10
NS_STEPS = 5


HIGH = lax.Precision.HIGHEST
NORM_EPS = 1e-05
POOL_EPS = 1e-06
CLIP_NORM = 1.0
LEARN_RATE = 0.02
DECAY_FIRST = 0.9
DECAY_SECOND = 0.95
DECAY_STATS = 0.95
ADAM_EPS = 1e-08
WEIGHT_DECAY = 0.01


def section_shapes(section):
    if section == 0:
        return [
            ("first_conv", (C_IN, MID)),
            ("middle_conv", (9 * MID, MID)),
            ("skip_conv", (C_IN, C_OUT)),
            ("first_gain", (MID,)),
            ("first_bias", (MID,)),
            ("middle_gain", (MID,)),
            ("middle_bias", (MID,)),
            ("skip_gain", (C_OUT,)),
            ("skip_bias", (C_OUT,)),
        ]
    if section == 2:
        return [
            ("first_conv", (C_OUT, MID)),
            ("middle_conv", (9 * MID, MID)),
            ("first_gain", (MID,)),
            ("first_bias", (MID,)),
            ("middle_gain", (MID,)),
            ("middle_bias", (MID,)),
        ]
    return [("last_conv", (MID, C_OUT)), ("last_gain", (C_OUT,)), ("last_bias", (C_OUT,))]


def unpack(flat_vector, section):
    pieces = {}
    offset = 0
    for entry_name, entry_shape in section_shapes(section):
        entry_size = math.prod(entry_shape)
        pieces[entry_name] = flat_vector[offset : offset + entry_size].reshape(entry_shape)
        offset = offset + entry_size
    return pieces


def pack(grads, section, flat_size):
    parts = [grads[entry_name].reshape(-1) for entry_name, entry_shape in section_shapes(section)]
    used = sum((math.prod(entry_shape) for entry_name, entry_shape in section_shapes(section)))
    parts.append(jnp.zeros((flat_size - used,), jnp.float32))
    return jnp.concatenate(parts)


def as_float(vector):
    return vector.astype(jnp.float32)


def to_low(groups):
    return tuple((portion.astype(jnp.bfloat16) for portion in groups))


def to_high(groups):
    return tuple((portion.astype(jnp.float32) for portion in groups))


def point_conv(groups, weight):
    return tuple(
        (
            jnp.einsum("khwc,cd->khwd", portion, weight, preferred_element_type=jnp.float32)
            for portion in groups
        )
    )


def point_back(grad_out, groups, weight):
    low_grads = to_low(grad_out)
    grad_input = tuple(
        (
            jnp.einsum("khwd,cd->khwc", grad_part, weight, preferred_element_type=jnp.float32)
            for grad_part in low_grads
        )
    )
    grad_weight = sum(
        (
            jnp.einsum("khwc,khwd->cd", in_part, grad_part, preferred_element_type=jnp.float32)
            for in_part, grad_part in zip(groups, low_grads)
        )
    )
    return (grad_input, grad_weight)


def patches(portion, stride):
    height = portion.shape[1]
    across = portion.shape[2]
    padded = jnp.pad(portion, ((0, 0), (1, 1), (1, 1), (0, 0)))
    shifted = [
        padded[:, row_off : row_off + height : stride, col_off : col_off + across : stride, :]
        for row_off in range(3)
        for col_off in range(3)
    ]
    return jnp.concatenate(shifted, axis=-1)


def area_conv(groups, weight, stride):
    columns = tuple((patches(portion, stride) for portion in groups))
    return (point_conv(columns, weight), columns)


def unpatch(grad_cols, height, across, stride):
    channels = grad_cols.shape[-1] // 9
    padded = jnp.zeros((grad_cols.shape[0], height + 2, across + 2, channels), jnp.float32)
    for row_off in range(3):
        for col_off in range(3):
            offset = (3 * row_off + col_off) * channels
            padded = padded.at[
                :, row_off : row_off + height : stride, col_off : col_off + across : stride, :
            ].add(grad_cols[..., offset : offset + channels])
    return padded[:, 1 : height + 1, 1 : across + 1, :]


def area_back(grad_out, columns, weight, stride, in_shapes):
    grad_cols, grad_weight = point_back(grad_out, columns, weight)
    grad_input = tuple(
        (
            unpatch(grad_part, shape_item[1], shape_item[2], stride)
            for grad_part, shape_item in zip(grad_cols, in_shapes)
        )
    )
    return (grad_input, grad_weight)


def batch_norm(groups, gain, bias):
    rows_total = sum((portion.shape[0] * portion.shape[1] * portion.shape[2] for portion in groups))
    centre = sum((jnp.sum(portion, axis=(0, 1, 2)) for portion in groups)) / rows_total
    spread = (
        sum((jnp.sum(jnp.square(portion - centre), axis=(0, 1, 2)) for portion in groups))
        / rows_total
    )
    inverse = lax.rsqrt(spread + NORM_EPS)
    standard = tuple(((portion - centre) * inverse for portion in groups))
    normed = tuple((gain * std_part + bias for std_part in standard))
    return (normed, (centre, spread, inverse, standard))


def norm_back(grad_out, gain, saved):
    centre, spread, inverse, standard = saved
    rows_total = sum(
        (portion.shape[0] * portion.shape[1] * portion.shape[2] for portion in standard)
    )
    grad_sum = sum((jnp.sum(grad_part, axis=(0, 1, 2)) for grad_part in grad_out))
    grad_dot = sum(
        (
            jnp.sum(grad_part * std_part, axis=(0, 1, 2))
            for grad_part, std_part in zip(grad_out, standard)
        )
    )
    grad_input = tuple(
        (
            gain
            * inverse
            * (grad_part - grad_sum / rows_total - std_part * (grad_dot / rows_total))
            for grad_part, std_part in zip(grad_out, standard)
        )
    )
    return (grad_input, grad_dot, grad_sum)


def through_softplus(grad_out, pre_values):
    return tuple(
        (grad_part * jax.nn.sigmoid(pre_part) for grad_part, pre_part in zip(grad_out, pre_values))
    )


def front_forward(pieces, inputs):
    first = point_conv(inputs, pieces["first_conv"])
    normed_a, saved_a = batch_norm(
        first, as_float(pieces["first_gain"]), as_float(pieces["first_bias"])
    )
    hidden = tuple((jax.nn.softplus(portion).astype(jnp.bfloat16) for portion in normed_a))
    middle, columns = area_conv(hidden, pieces["middle_conv"], 2)
    normed_b, saved_b = batch_norm(
        middle, as_float(pieces["middle_gain"]), as_float(pieces["middle_bias"])
    )
    narrow = tuple((jax.nn.softplus(portion) for portion in normed_b))
    reduced = tuple((portion[:, ::2, ::2, :] for portion in inputs))
    skipped = point_conv(reduced, pieces["skip_conv"])
    wide, saved_p = batch_norm(
        skipped, as_float(pieces["skip_gain"]), as_float(pieces["skip_bias"])
    )
    norm_rows = jnp.stack(
        [
            jnp.concatenate([saved_a[0], saved_b[0], saved_p[0]]),
            jnp.concatenate([saved_a[1], saved_b[1], saved_p[1]]),
        ]
    )
    kept = (normed_a, hidden, columns, normed_b, reduced, saved_a, saved_b, saved_p)
    return (wide, narrow, norm_rows, kept)


def front_backward(pieces, inputs, grad_wide, grad_narrow):
    wide, narrow, norm_rows, kept = front_forward(pieces, inputs)
    normed_a, hidden, columns, normed_b, reduced, saved_a, saved_b, saved_p = kept
    grads = {}
    grad_pre_b = through_softplus(grad_narrow, normed_b)
    grad_mid, grads["middle_gain"], grads["middle_bias"] = norm_back(
        grad_pre_b, as_float(pieces["middle_gain"]), saved_b
    )
    grad_hidden, grads["middle_conv"] = area_back(
        grad_mid, columns, pieces["middle_conv"], 2, [portion.shape for portion in hidden]
    )
    grad_pre_a = through_softplus(grad_hidden, normed_a)
    grad_first, grads["first_gain"], grads["first_bias"] = norm_back(
        grad_pre_a, as_float(pieces["first_gain"]), saved_a
    )
    grad_inputs, grads["first_conv"] = point_back(grad_first, inputs, pieces["first_conv"])
    grad_skip, grads["skip_gain"], grads["skip_bias"] = norm_back(
        grad_wide, as_float(pieces["skip_gain"]), saved_p
    )
    grad_reduced, grads["skip_conv"] = point_back(grad_skip, reduced, pieces["skip_conv"])
    grad_inputs = tuple(
        (
            full_part.at[:, ::2, ::2, :].add(part_reduced)
            for full_part, part_reduced in zip(grad_inputs, grad_reduced)
        )
    )
    return (grad_inputs, grads)


def join_forward(pieces, wide, narrow):
    last = point_conv(narrow, pieces["last_conv"])
    normed, saved = batch_norm(last, as_float(pieces["last_gain"]), as_float(pieces["last_bias"]))
    pre_values = tuple(
        (
            skip_part.astype(jnp.float32) + branch_part
            for skip_part, branch_part in zip(wide, normed)
        )
    )
    ending = tuple((jax.nn.softplus(pre_part) for pre_part in pre_values))
    filler = jnp.zeros((2 * MID,), jnp.float32)
    norm_rows = jnp.stack(
        [jnp.concatenate([saved[0], filler]), jnp.concatenate([saved[1], filler])]
    )
    return (ending, norm_rows, (pre_values, saved))


def join_grads(pieces, narrow, kept, grad_out, gate):
    pre_values, saved = kept
    grad_pre = tuple(
        (
            grad_part * jax.nn.sigmoid(pre_part) * gate
            for grad_part, pre_part in zip(grad_out, pre_values)
        )
    )
    grad_wide = tuple(
        (pre_grad + grad_part * (1.0 - gate) for pre_grad, grad_part in zip(grad_pre, grad_out))
    )
    grad_last, gain_grad, bias_grad = norm_back(grad_pre, as_float(pieces["last_gain"]), saved)
    grad_narrow, weight_grad = point_back(grad_last, narrow, pieces["last_conv"])
    grads = {"last_conv": weight_grad, "last_gain": gain_grad, "last_bias": bias_grad}
    return (grad_wide, grad_narrow, grads)


def split_forward(pieces, wide):
    first = point_conv(wide, pieces["first_conv"])
    normed_a, saved_a = batch_norm(
        first, as_float(pieces["first_gain"]), as_float(pieces["first_bias"])
    )
    hidden = tuple((jax.nn.softplus(portion).astype(jnp.bfloat16) for portion in normed_a))
    middle, columns = area_conv(hidden, pieces["middle_conv"], 1)
    normed_b, saved_b = batch_norm(
        middle, as_float(pieces["middle_gain"]), as_float(pieces["middle_bias"])
    )
    narrow = tuple((jax.nn.softplus(portion) for portion in normed_b))
    filler = jnp.zeros((C_OUT,), jnp.float32)
    norm_rows = jnp.stack(
        [
            jnp.concatenate([saved_a[0], saved_b[0], filler]),
            jnp.concatenate([saved_a[1], saved_b[1], filler]),
        ]
    )
    return (narrow, norm_rows, (normed_a, hidden, columns, normed_b, saved_a, saved_b))


def split_backward(pieces, wide, grad_relay, grad_narrow):
    narrow, norm_rows, kept = split_forward(pieces, wide)
    normed_a, hidden, columns, normed_b, saved_a, saved_b = kept
    grads = {}
    grad_pre_b = through_softplus(grad_narrow, normed_b)
    grad_mid, grads["middle_gain"], grads["middle_bias"] = norm_back(
        grad_pre_b, as_float(pieces["middle_gain"]), saved_b
    )
    grad_hidden, grads["middle_conv"] = area_back(
        grad_mid, columns, pieces["middle_conv"], 1, [portion.shape for portion in hidden]
    )
    grad_pre_a = through_softplus(grad_hidden, normed_a)
    grad_first, grads["first_gain"], grads["first_bias"] = norm_back(
        grad_pre_a, as_float(pieces["first_gain"]), saved_a
    )
    grad_conv_in, grads["first_conv"] = point_back(grad_first, wide, pieces["first_conv"])
    grad_wide = tuple(
        (relay_part + conv_part for relay_part, conv_part in zip(grad_relay, grad_conv_in))
    )
    return (grad_wide, grads)


def pool_grad(final, targets, picks):
    result = []
    for portion, pick_ids in zip(final, picks):
        cubes = jnp.mean(portion * portion * portion, axis=(1, 2)) + POOL_EPS
        factor = jnp.exp(jnp.log(cubes) * (-2.0 / 3.0)) * targets[pick_ids]
        result.append(factor[:, None, None, :] * portion * portion)
    return tuple(result)


def used_size(section):
    return sum((math.prod(entry_shape) for entry_name, entry_shape in section_shapes(section)))


def batch_pass(reals, inputs, gate, targets, picks):
    pieces = [unpack(reals[section], section) for section in range(4)]
    wide_f, narrow_f, rows_0, _ = front_forward(pieces[0], inputs)
    wide_0, narrow_0 = to_low(wide_f), to_low(narrow_f)
    ending_1, rows_1, kept_1 = join_forward(pieces[1], wide_0, narrow_0)
    wide_1 = to_low(ending_1)
    narrow_f, rows_2, _ = split_forward(pieces[2], wide_1)
    narrow_2 = to_low(narrow_f)
    ending_3, rows_3, kept_3 = join_forward(pieces[3], wide_1, narrow_2)
    final = tuple(
        (
            jnp.where(gate > 0, end_part, relay_part.astype(jnp.float32))
            for end_part, relay_part in zip(ending_3, wide_1)
        )
    )
    cotangent = pool_grad(final, targets, picks)
    grad_wide, grad_narrow, grads_3 = join_grads(pieces[3], narrow_2, kept_3, cotangent, gate)
    grad_wide, grads_2 = split_backward(
        pieces[2], wide_1, to_high(to_low(grad_wide)), to_high(to_low(grad_narrow))
    )
    grad_wide, grad_narrow, grads_1 = join_grads(
        pieces[1], narrow_0, kept_1, to_high(to_low(grad_wide)), 1.0
    )
    grad_inputs, grads_0 = front_backward(
        pieces[0], inputs, to_high(to_low(grad_wide)), to_high(to_low(grad_narrow))
    )
    outs = (wide_0, wide_1, wide_1, to_low(final))
    stats = jnp.stack([rows_0, rows_1, rows_2 * gate, rows_3 * gate])
    return (outs, stats, to_low(grad_inputs), (grads_0, grads_1, grads_2, grads_3))


def on_device(
    teach_in,
    stud_in,
    params,
    owners,
    depth_gates,
    teach_ids,
    stud_ids,
    targets,
    moment,
    second,
    gram_stats,
    eigen_basis,
):
    sections = lax.axis_size("pipe")
    rank = lax.axis_index("pipe")
    owner_count = lax.axis_size("dp")
    span_size = params.shape[1]
    flat_size = span_size * owner_count
    owner_rows = lax.all_gather(owners, "pipe", axis=0, tiled=True)
    gathered = lax.all_gather(params[0].astype(jnp.bfloat16), ("pipe", "dp"), axis=0)
    gathered = gathered.reshape(sections, owner_count, span_size)
    reals = []
    for section in range(sections):
        inverse = jnp.argsort(owner_rows[section]).astype(jnp.int32)
        blocks = -(-used_size(section) // span_size)
        reals.append(gathered[section][inverse[:blocks]].reshape(blocks * span_size))
    inputs = (teach_in[0], stud_in[0])
    gate = depth_gates[rank].astype(jnp.float32)
    outs, stats, (teach_grad, stud_grad), grads = batch_pass(
        reals, inputs, gate, targets, (teach_ids[rank], stud_ids[rank])
    )
    segment_teach = lax.all_to_all(
        jnp.stack([part[0] for part in outs]), "pipe", split_axis=0, concat_axis=0, tiled=True
    )
    segment_stud = lax.all_to_all(
        jnp.stack([part[1] for part in outs]), "pipe", split_axis=0, concat_axis=0, tiled=True
    )
    stats = lax.all_to_all(stats, "pipe", split_axis=0, concat_axis=0, tiled=True)
    rows = []
    for section in range(sections):
        flat = pack(grads[section], section, flat_size).reshape(owner_count, span_size)
        rows.append(flat[owner_rows[section]])
    span_total = lax.psum_scatter(
        jnp.stack(rows).reshape(sections * owner_count, span_size),
        ("pipe", "dp"),
        scatter_dimension=0,
        tiled=True,
    ).reshape(span_size)
    total_squares = lax.psum(jnp.sum(span_total * span_total), ("dp", "pipe"))
    grad_norm = jnp.sqrt(total_squares)
    factor = jnp.minimum(1.0, CLIP_NORM / grad_norm)
    clipped = span_total * factor
    matrix = clipped.reshape(span_size // 128, 128)
    gram_old = gram_stats[0]
    basis_old = eigen_basis[0]
    gram_new = DECAY_STATS * gram_old + (1.0 - DECAY_STATS) * jnp.dot(
        matrix.T, matrix, precision=HIGH
    )
    product = jnp.dot(gram_new, basis_old, precision=HIGH)
    rotation = product / jnp.sqrt(jnp.sum(product * product))
    for repeat in range(NS_STEPS):
        square = jnp.dot(rotation.T, rotation, precision=HIGH)
        rotation = 1.5 * rotation - 0.5 * jnp.dot(rotation, square, precision=HIGH)
    moment_old = moment.reshape(span_size // 128, 128)
    initial = jnp.dot(moment_old, basis_old.T, precision=HIGH)
    blended = DECAY_FIRST * initial + (1.0 - DECAY_FIRST) * matrix
    moment_new = jnp.dot(blended, rotation, precision=HIGH)
    rotated = jnp.dot(matrix, rotation, precision=HIGH)
    second_new = (
        DECAY_SECOND * second.reshape(span_size // 128, 128)
        + (1.0 - DECAY_SECOND) * rotated * rotated
    )
    correction = math.sqrt(1.0 - DECAY_SECOND**STEP) / (1.0 - DECAY_FIRST**STEP)
    direction = (
        jnp.dot(moment_new / (jnp.sqrt(second_new) + ADAM_EPS), rotation.T, precision=HIGH)
        * correction
    )
    weights = params.reshape(span_size // 128, 128)
    params_new = weights - LEARN_RATE * (direction + WEIGHT_DECAY * weights)
    return (
        segment_teach[None],
        segment_stud[None],
        teach_grad[None],
        stud_grad[None],
        stats[None, :, None],
        grad_norm,
        clipped.reshape(1, span_size),
        moment_new.reshape(1, span_size),
        second_new.reshape(1, span_size),
        params_new.reshape(1, span_size),
        gram_new[None],
        rotation[None],
    )


MESH = pl.DeviceIdType.MESH
LOW = jnp.bfloat16
FULL = jnp.float32
TILE = 256
WINDOW = 20
STRIDE = 19
VEC_TILE = (152, 32, 104, 32)
USED_TILES = (153, 33, 105, 33)
FRONT_WIDE = 88
SMALL_ROWS = 1056
ROWS = 120
PADDED = 128
TEACH_ROWS = 72


def any_spec():
    return pl.BlockSpec(memory_space=pl.ANY)


def smem_spec():
    return pl.BlockSpec(memory_space=pltpu.SMEM)


def vmem_spec():
    return pl.BlockSpec(memory_space=pltpu.VMEM)


def tile_forms(section, tile):
    even = lax.rem(section, 2) == 0
    vector = jnp.where(section == 0, 152, jnp.where(section == 2, 104, 32))
    narrow_end = jnp.where(section == 0, FRONT_WIDE, jnp.where(section == 2, 104, 0))
    narrow = even & (tile < narrow_end)
    plain = tile == vector
    return narrow, plain


def prepare_kernel(owners, params, big, small, ids, flat, sem):
    block, section = owners[0, lax.axis_index("dp")], lax.axis_index("pipe")

    @pl.loop(0, WINDOW)
    def _(r):
        flat[pl.ds(TILE * r, TILE)] = jnp.zeros((TILE, 128), FULL)

    copy = pltpu.make_async_copy(params.at[:, 0, :], flat.at[pl.ds(6 * block, params.shape[0])], sem)
    copy.start()

    @pl.loop(0, small.shape[0])
    def _(r):
        small[r] = jnp.zeros((TILE, 128), LOW)

    lane = lax.broadcasted_iota(jnp.int32, (8, 128), 1)
    row = jnp.zeros((8, 128), jnp.int32)
    for j in range(8):
        row = jnp.where(lane == j, owners[0, j], row)
    ids[...] = row
    copy.wait()

    @pl.loop(0, WINDOW)
    def _(r):
        tile = STRIDE * block + r
        narrow, plain = tile_forms(section, tile)
        base = TILE * r

        @pl.when(narrow)
        def _():
            for j in range(4):
                big[r, 64 * j : 64 * j + 64, :] = flat[pl.ds(base + j, 64, 4), :].astype(LOW)

        @pl.when(plain)
        def _():
            big[r] = flat[pl.ds(base, TILE), :].astype(LOW)

        @pl.when(jnp.logical_not(narrow | plain))
        def _():
            for j in range(16):
                big[r, 16 * j : 16 * j + 16, :] = flat[pl.ds(base + j, 16, 16), :].astype(LOW)

        @pl.when(tile < small.shape[0])
        def _():
            small[tile] = big[r]


def prepare(owners, params):
    return pl.pallas_call(
        prepare_kernel,
        name="prepare",
        out_shape=(
            jax.ShapeDtypeStruct((WINDOW, TILE, 128), LOW),
            jax.ShapeDtypeStruct((USED_TILES[1], TILE, 128), LOW),
            jax.ShapeDtypeStruct((8, 128), jnp.int32),
        ),
        in_specs=[smem_spec(), any_spec()],
        out_specs=(vmem_spec(),) * 3,
        scratch_shapes=[pltpu.VMEM((WINDOW * TILE, 128), FULL), pltpu.SemaphoreType.DMA],
        compiler_params=pltpu.CompilerParams(vmem_limit_bytes=60 << 20),
    )(owners, params.reshape(-1, 1, 128))


class Place:
    def __init__(self):
        self.dp = lax.axis_index("dp")
        self.pipe = lax.axis_index("pipe")
        self.x, self.core = self.pipe // 2, self.pipe % 2
        self.z, self.y = self.dp // 2, self.dp % 2

    def device(self, x=None, core=None, z=None, y=None):
        x = self.x if x is None else x
        core = self.core if core is None else core
        z = self.z if z is None else z
        y = self.y if y is None else y
        return {"dp": 2 * z + y, "pipe": 2 * x + core}

    def enter(self):
        barrier = pltpu.get_barrier_semaphore()
        for step in range(1, 8):
            other = lax.rem(self.dp + step, 8)
            pl.semaphore_signal(
                barrier, inc=1, device_id={"dp": other, "pipe": self.pipe}, device_id_type=MESH
            )
        for step in range(1, 4):
            other = lax.rem(self.pipe + step, 4)
            pl.semaphore_signal(
                barrier, inc=1, device_id={"dp": self.dp, "pipe": other}, device_id_type=MESH
            )
        pl.semaphore_wait(barrier, 10)


def remote(src, dst, send, recv, target):
    return pltpu.make_async_remote_copy(
        src_ref=src, dst_ref=dst, send_sem=send, recv_sem=recv, device_id=target, device_id_type=MESH
    )


BIG_HALF = WINDOW * TILE // 2
SMALL_HALF = SMALL_ROWS // 2
BULK_CUT = 992
LIGHT_CUT = 256
BACK_CUT = 1280
GATHER_ORDER = (
    "EY", "Z1", "EC0", "EC1", "S0", "Z2", "Z3", "EC2", "EC3", "L0", "S1", "D0", "L1", "S2", "D1",
    "S3", "L2", "M1", "D2", "M2", "D3", "M3",
)
REDUCE_ORDER = (
    "A0", "A1", "A2", "A3", "L0", "L1", "B0", "L2", "L3", "LS", "B1", "LE", "B2", "O0", "E0", "O1",
    "I0", "T1", "T2", "E1", "B3", "O2", "I1", "E2", "G", "T3", "I2", "O3",
)


def gather_kernel(big, small, ids, all_big, all_small, table, early, chunk, rising, falling,
                  early_send, early_recv, eu_send, eu_recv, ed_send, ed_recv,
                  z_send, z_recv, x_send, x_recv, y_send, y_recv, dx_send, dx_recv, dy_send, dy_recv,
                  s_send, s_recv, first_send, first_recv, own_sem, id_send, id_recv, lz_send, lz_recv):
    me = Place()
    me.enter()
    x, y, z, core = me.x, me.y, me.z, me.core
    up, down = me.device(z=z + 1), me.device(z=z - 1)
    x_side, y_side, sibling = me.device(x=1 - x), me.device(y=1 - y), me.device(core=1 - core)

    class Stream:
        def __init__(self, n, out, cut):
            self.n, self.out, self.cut, self.rows = n, out, cut, out.shape[3]

        def block(self, xo, origin, yo):
            return self.out.at[xo, 2 * origin + yo, core]

        def move_x(self, origin):
            block = self.block(x, origin, y)
            return remote(block, block, x_send.at[self.n, origin], x_recv.at[self.n, origin], x_side)

        def move_y(self, origin):
            block = self.block(x, origin, y)
            return remote(block, block, y_send.at[self.n, origin], y_recv.at[self.n, origin], y_side)

        def share(self, xo, origin, yo):
            block = self.block(xo, origin, yo)
            at = 8 * xo + 2 * origin + yo
            return remote(block, block, s_send.at[self.n, at], s_recv.at[self.n, at], sibling)

        def move_z(self, origin, target, way):
            block = self.block(x, origin, y)
            return remote(block, block, z_send.at[self.n, way, origin], z_recv.at[self.n, origin], target)

        def half_x(self, origin, xo, yo):
            part = self.out.at[xo, 2 * origin + yo, core, pl.ds(self.cut, self.rows - self.cut)]
            return remote(part, part, dx_send.at[self.n, origin], dx_recv.at[self.n, origin], x_side)

        def half_y(self, origin, xo, yo):
            part = self.out.at[xo, 2 * origin + yo, core, pl.ds(0, self.cut)]
            return remote(part, part, dy_send.at[self.n, origin], dy_recv.at[self.n, origin], y_side)

        def spread(self, origin):
            self.move_x(origin).start()
            self.move_y(origin).start()
            self.share(x, origin, y).start()

        def from_sides(self, origin):
            self.move_x(origin).wait_recv()
            self.half_y(origin, 1 - x, y).start()
            self.share(1 - x, origin, y).start()
            self.move_y(origin).wait_recv()
            self.half_x(origin, x, 1 - y).start()
            self.share(x, origin, 1 - y).start()

        def from_diagonal(self, origin):
            self.half_x(origin, 1 - x, 1 - y).wait_recv()
            self.half_y(origin, 1 - x, 1 - y).wait_recv()
            self.share(1 - x, origin, 1 - y).start()

        def each(self, step, action):
            if step == 0:
                action(z)
            else:
                pl.when(z >= step)(lambda: action(z - step))
                pl.when(z + step <= 3)(lambda: action(z + step))

        def begin(self):
            pl.when(z < 3)(lambda: self.move_z(z, up, 0).start())
            pl.when(z > 0)(lambda: self.move_z(z, down, 1).start())
            self.spread(z)

        def from_z(self, k):
            @pl.when(z >= k)
            def _():
                self.move_z(z - k, up, 0).wait_recv()
                pl.when(z < 3)(lambda: self.move_z(z - k, up, 0).start())
                self.spread(z - k)

            @pl.when(z + k <= 3)
            def _():
                self.move_z(z + k, down, 1).wait_recv()
                pl.when(z > 0)(lambda: self.move_z(z + k, down, 1).start())
                self.spread(z + k)

        def close(self):
            for origin in range(4):
                self.move_x(origin).wait_send()
                self.move_y(origin).wait_send()
                self.half_x(origin, x, 1 - y).wait_send()
                self.half_y(origin, 1 - x, y).wait_send()
                pl.when((z < 3) & (origin <= z))(lambda: self.move_z(origin, up, 0).wait_send())
                pl.when((z > 0) & (origin >= z))(lambda: self.move_z(origin, down, 1).wait_send())
            self.close_shares()

        def close_shares(self):
            for origin in range(4):
                for xo in range(2):
                    for yo in range(2):
                        self.share(xo, origin, yo).wait_send()
                        theirs = self.out.at[xo, 2 * origin + yo, 1 - core]
                        at = 8 * xo + 2 * origin + yo
                        remote(theirs, theirs, s_send.at[self.n, at], s_recv.at[self.n, at], sibling).wait_recv()

    class Late(Stream):
        def column_z(self, xo, origin, yo, target, way):
            block = self.block(xo, origin, yo)
            at = 2 * xo + yo
            return remote(
                block, block, lz_send.at[way, at, origin], lz_recv.at[at, origin], target
            )

        def leave(self, xo, yo):
            pl.when(z < 3)(lambda: self.column_z(xo, z, yo, up, 0).start())
            pl.when(z > 0)(lambda: self.column_z(xo, z, yo, down, 1).start())
            self.share(xo, z, yo).start()

        def step(self, k):
            if k == 0:
                self.move_x(z).start()
                self.move_y(z).start()
                self.leave(x, y)
            elif k == 1:
                self.move_x(z).wait_recv()
                self.half_y(z, 1 - x, y).start()
                self.leave(1 - x, y)
                self.move_y(z).wait_recv()
                self.half_x(z, x, 1 - y).start()
                self.leave(x, 1 - y)
            elif k == 2:
                self.half_x(z, 1 - x, 1 - y).wait_recv()
                self.half_y(z, 1 - x, 1 - y).wait_recv()
                self.leave(1 - x, 1 - y)
            else:
                gap = k - 2

                @pl.when(z >= gap)
                def _():
                    for xo, yo in columns:
                        self.column_z(xo, z - gap, yo, up, 0).wait_recv()
                        pl.when(z < 3)(lambda: self.column_z(xo, z - gap, yo, up, 0).start())
                        self.share(xo, z - gap, yo).start()

                @pl.when(z + gap <= 3)
                def _():
                    for xo, yo in columns:
                        self.column_z(xo, z + gap, yo, down, 1).wait_recv()
                        pl.when(z > 0)(lambda: self.column_z(xo, z + gap, yo, down, 1).start())
                        self.share(xo, z + gap, yo).start()

        def close(self):
            self.move_x(z).wait_send()
            self.move_y(z).wait_send()
            self.half_x(z, x, 1 - y).wait_send()
            self.half_y(z, 1 - x, y).wait_send()
            for origin in range(4):
                for xo, yo in columns:
                    pl.when((z < 3) & (origin <= z))(
                        lambda: self.column_z(xo, origin, yo, up, 0).wait_send())
                    pl.when((z > 0) & (origin >= z))(
                        lambda: self.column_z(xo, origin, yo, down, 1).wait_send())
            self.close_shares()

    columns = ((x, y), (1 - x, y), (x, 1 - y), (1 - x, 1 - y))
    bulk = Stream(0, all_big, BULK_CUT)
    light = Late(1, all_small, LIGHT_CUT)

    order = [
        jnp.where(z < 2, 3, 0),
        jnp.where(z == 0, 2, jnp.where(z == 1, 0, jnp.where(z == 2, 3, 1))),
        jnp.where(z == 0, 1, jnp.where(z == 1, 2, jnp.where(z == 2, 1, 2))),
        z,
    ]

    def cross(k):
        return remote(small.at[2 * order[k] + (1 - y)], early.at[k], early_send.at[k], early_recv.at[k], y_side)

    def own_early(k):
        return pltpu.make_async_copy(small.at[2 * order[k] + y], chunk.at[k], own_sem.at[3 + k])

    def rise(k):
        slot = order[k] - 1
        return remote(chunk.at[k], rising.at[slot], eu_send.at[slot], eu_recv.at[slot], up)

    def fall(k):
        slot = order[k]
        return remote(chunk.at[k], falling.at[slot], ed_send.at[slot], ed_recv.at[slot], down)

    def merge(k, ref, slot):
        @pl.loop(0, 3)
        def _(i):
            part = pl.ds(pl.multiple_of(352 * i, 16), 352)
            chunk[k, part, :] = (chunk[k, part, :].astype(FULL) + ref[slot, part, :].astype(FULL)).astype(LOW)

    big_half = all_big.at[x, me.dp, 1]
    big_first = remote(big.at[pl.ds(BIG_HALF, BIG_HALF)], big_half, first_send.at[0], first_recv.at[0], sibling)
    small_half = all_small.at[x, me.dp, 0]
    small_first = remote(
        chunk.at[3, pl.ds(0, SMALL_HALF)], small_half, first_send.at[1], first_recv.at[1], sibling)

    def early_cross():
        @pl.when(core == 1)
        def _():
            for k in range(4):
                own_early(k).wait()
                cross(k).wait_recv()
                merge(k, early, k)

    def early_chain(k):
        @pl.when(core == 1)
        def _():
            if k < 3:

                @pl.when(order[k] > z)
                def _():
                    @pl.when(z > 0)
                    def _():
                        rise(k).wait_recv()
                        merge(k, rising, order[k] - 1)

                    rise(k).start()

                @pl.when(order[k] < z)
                def _():
                    @pl.when(z < 3)
                    def _():
                        fall(k).wait_recv()
                        merge(k, falling, order[k])

                    fall(k).start()

            else:

                @pl.when(z > 0)
                def _():
                    rise(k).wait_recv()
                    merge(k, rising, z - 1)

                @pl.when(z < 3)
                def _():
                    fall(k).wait_recv()
                    merge(k, falling, z)

                small_first.start()
                copy = pltpu.make_async_copy(
                    chunk.at[3, pl.ds(SMALL_HALF, SMALL_HALF)], all_small.at[x, me.dp, 1], own_sem.at[0])
                copy.start()
                copy.wait()

    def light_begin():
        @pl.when(core == 0)
        def _():
            small_first.wait_recv()

        light.step(0)

    @pl.when(core == 0)
    def _():
        big_first.start()
        copy = pltpu.make_async_copy(big.at[pl.ds(0, BIG_HALF)], all_big.at[x, me.dp, 0], own_sem.at[0])
        copy.start()
        copy.wait()

    @pl.when(core == 1)
    def _():
        for k in range(4):
            cross(k).start()
            own_early(k).start()
        big_first.wait_recv()

    bulk.begin()
    row = pltpu.make_async_copy(ids, table.at[me.pipe], own_sem.at[2])
    row.start()
    for step in range(1, 4):
        remote(
            ids, table.at[me.pipe], id_send.at[step], id_recv.at[step],
            {"dp": me.dp, "pipe": lax.rem(me.pipe + step, 4)},
        ).start()

    actions = {"EY": early_cross, "L0": light_begin}
    for k in range(4):
        actions["EC%d" % k] = functools.partial(early_chain, k)
        actions["S%d" % k] = functools.partial(bulk.each, k, bulk.from_sides)
        actions["D%d" % k] = functools.partial(bulk.each, k, bulk.from_diagonal)
        if k:
            actions["Z%d" % k] = functools.partial(bulk.from_z, k)
            actions["M%d" % k] = functools.partial(light.step, k + 2)
            if k < 3:
                actions["L%d" % k] = functools.partial(light.step, k)
    for event in GATHER_ORDER:
        actions[event]()
    bulk.close()
    light.close()
    row.wait()
    for step in range(1, 4):
        here = lax.rem(me.pipe + 4 - step, 4)
        move = remote(
            ids, table.at[here], id_send.at[step], id_recv.at[step],
            {"dp": me.dp, "pipe": lax.rem(me.pipe + step, 4)},
        )
        move.wait_recv()
        move.wait_send()

    @pl.when(core == 0)
    def _():
        big_first.wait_send()

    @pl.when(core == 1)
    def _():
        small_first.wait_send()
        for k in range(4):
            cross(k).wait_send()
        for k in range(3):
            pl.when(order[k] > z)(lambda: rise(k).wait_send())
            pl.when(order[k] < z)(lambda: fall(k).wait_send())


def gather_all(big, small, ids):
    sem = pltpu.SemaphoreType.DMA
    return pl.pallas_call(
        gather_kernel,
        name="gather_all",
        out_shape=(
            jax.ShapeDtypeStruct((2, 8, 2, BIG_HALF, 128), LOW),
            jax.ShapeDtypeStruct((2, 8, 2, SMALL_HALF, 128), LOW),
            jax.ShapeDtypeStruct((4, 8, 128), jnp.int32),
        ),
        in_specs=[any_spec()] * 3,
        out_specs=(any_spec(),) * 3,
        scratch_shapes=[
            pltpu.VMEM((4, SMALL_ROWS, 128), LOW), pltpu.VMEM((4, SMALL_ROWS, 128), LOW),
            pltpu.VMEM((3, SMALL_ROWS, 128), LOW), pltpu.VMEM((3, SMALL_ROWS, 128), LOW),
            sem((4,)), sem((4,)), sem((3,)), sem((3,)), sem((3,)), sem((3,)),
            sem((2, 2, 4)), sem((2, 4)),
            sem((2, 4)), sem((2, 4)), sem((2, 4)), sem((2, 4)),
            sem((2, 4)), sem((2, 4)), sem((2, 4)), sem((2, 4)),
            sem((2, 16)), sem((2, 16)),
            sem((2,)), sem((2,)), sem((7,)), sem((4,)), sem((4,)), sem((2, 4, 4)), sem((4, 4)),
        ],
        compiler_params=pltpu.CompilerParams(
            collective_id=0, has_side_effects=True, vmem_limit_bytes=60 << 20
        ),
    )(big.reshape(WINDOW * TILE, 128), small.reshape(8, SMALL_ROWS, 128), ids)


def soft(value):
    return jnp.maximum(value, 0.0) + jnp.log1p(jnp.exp(-jnp.abs(value)))


def gate_of(value):
    small = jnp.exp(-jnp.abs(value))
    share = 1.0 / (1.0 + small)
    return jnp.where(value >= 0, share, small * share)


def standardize(z):
    count = z.shape[0]
    centre = jnp.sum(z, axis=0, keepdims=True) / count
    away = z - centre
    spread = jnp.sum(away * away, axis=0, keepdims=True) / count
    inverse = lax.rsqrt(spread + NORM_EPS)
    return away * inverse, centre, spread, inverse


def unstandardize(grad, standard, gain, inverse):
    count = grad.shape[0]
    grad_sum = jnp.sum(grad, axis=0, keepdims=True)
    grad_dot = jnp.sum(grad * standard, axis=0, keepdims=True)
    result = gain * inverse * (grad - grad_sum / count - standard * (grad_dot / count))
    return result, grad_dot, grad_sum


def pad_low(value):
    zeros = jnp.zeros((PADDED - ROWS, value.shape[1]), FULL)
    return jnp.concatenate([value, zeros], axis=0).astype(LOW)


def mul(a, b):
    return jnp.dot(a, b, preferred_element_type=FULL)


def mul_t(a, b):
    return lax.dot_general(a, b, (((1,), (1,)), ((), ())), preferred_element_type=FULL)


def narrow_part(ref, start, count, blocks=range(4)):
    return jnp.concatenate(
        [ref[pl.ds(start, count), 64 * j : 64 * j + 64, :].reshape(64 * count, 128) for j in blocks],
        axis=1,
    )


def put_narrow(ref, start, count, value):
    for j in range(4):
        ref[pl.ds(start, count), 64 * j : 64 * j + 64, :] = (
            value[:, 128 * j : 128 * j + 128].astype(LOW).reshape(count, 64, 128)
        )


def wide_part(ref, start, count, c):
    return jnp.concatenate(
        [
            ref[start : start + count, pl.ds(pl.multiple_of(32 * c + 16 * h, 16), 16), :].reshape(
                16 * count, 128
            )
            for h in range(2)
        ],
        axis=1,
    )


def put_wide(ref, start, count, c, value):
    for h in range(2):
        ref[start : start + count, pl.ds(pl.multiple_of(32 * c + 16 * h, 16), 16), :] = (
            value[:, 128 * h : 128 * h + 128].astype(LOW).reshape(count, 16, 128)
        )


def step_kernel(table, gates, teach_ids, stud_ids, all_big, all_small, x, targets, grid,
                wide0, wide1, final, stats, grad_x, out_big, out_small,
                w0, w1, w2, w3, edges, vec, grad_vec, raw,
                std_a, std_b, std_p, std_1, std_c, std_d, hidden, cols0, cols2,
                nar0, nar2, turned, relay, dz_a, dz_n, acc, acc_x, grad_h,
                wanted, inv, in_sem, edge_sem, out_sem):
    rank = lax.axis_index("pipe")
    gate = gates[rank].astype(FULL)
    for group in range(2):
        for j in range(8):
            inv[8 * group + table[2 * group, 0, j]] = j
    picks = [teach_ids[rank, k] for k in range(2)] + [stud_ids[rank, k] for k in range(3)]
    rows = [
        pltpu.make_async_copy(targets.at[pl.ds(pick, 1)], wanted.at[pl.ds(k, 1)], edge_sem.at[12 + k])
        for k, pick in enumerate(picks)
    ]
    for fetched in rows:
        fetched.start()
    weights = (w0, w1, w2, w3)
    loads = {0: [], 1: [], 2: [], 3: []}
    for group, weight, blocks in ((0, w0, 8), (1, w2, 6)):
        for b in range(blocks):
            first, here = 19 * b, inv[8 * group + b]
            at = 8 * group + b
            loads[2 * group].append(pltpu.make_async_copy(
                all_big.at[group, here, 0], weight.at[pl.ds(first, 10)], in_sem.at[0, at]))
            if first + 10 < USED_TILES[2 * group]:
                count = 10 if b == 7 else 9
                loads[2 * group].append(pltpu.make_async_copy(
                    all_big.at[group, here, 1, pl.ds(0, count)], weight.at[pl.ds(first + 10, count)],
                    in_sem.at[1, at]))
            if b < blocks - 1:
                at = 7 * group + b
                loads[2 * group].append(pltpu.make_async_copy(
                    all_big.at[group, here, 1, pl.ds(9, 1)], edges.at[pl.ds(at, 1)], edge_sem.at[at]))
    loads[1].append(pltpu.make_async_copy(all_small.at[0], w1, in_sem.at[0, 14]))
    loads[3].append(pltpu.make_async_copy(all_small.at[1], w3, in_sem.at[0, 15]))
    for section in range(4):
        for load in loads[section]:
            load.start()

    raw[...] = jnp.zeros_like(raw)
    grad_vec[...] = jnp.zeros_like(grad_vec)

    def settle(section):
        for load in loads[section]:
            load.wait()
        if section == 0:
            for b in range(7):
                w0[19 * b + 19] = (w0[19 * b + 19].astype(FULL) + edges[b].astype(FULL)).astype(LOW)
        if section == 2:
            for b in range(5):
                w2[19 * b + 19] = (
                    w2[19 * b + 19].astype(FULL) + edges[7 + b].astype(FULL)
                ).astype(LOW)
        vec[section] = weights[section][VEC_TILE[section], 0:48, :].astype(FULL)

    def row(section, start):
        return jnp.concatenate(
            [vec[section, pl.ds(start + h, 1), :] for h in range(2)], axis=1
        )

    def put_row(section, start, value):
        for h in range(2):
            grad_vec[section, pl.ds(start + h, 1), :] = value[:, 128 * h : 128 * h + 128]

    def put_stats(section, column, centre, spread):
        raw[2 * section : 2 * section + 1, pl.ds(column, 256)] = centre
        raw[2 * section + 1 : 2 * section + 2, pl.ds(column, 256)] = spread

    def inverse_of(section, column):
        return lax.rsqrt(raw[2 * section + 1 : 2 * section + 2, pl.ds(column, 256)] + NORM_EPS)

    def lanes(c):
        return pl.ds(pl.multiple_of(256 * c, 256), 256)

    at_row, at_col, side = grid[0], grid[1], grid[2]

    def masked(value, dr, dc):
        ok = (at_row + dr >= 0) & (at_row + dr < side) & (at_col + dc >= 0) & (at_col + dc < side)
        return jnp.concatenate(
            [jnp.where(ok, value[:, 128 * j : 128 * j + 128], 0.0) for j in range(4)], axis=1
        )

    def rolled(value, sign, dr, dc):
        parts = []
        for start, end, width in ((0, TEACH_ROWS, 6), (TEACH_ROWS, ROWS, 4)):
            by = (sign * (dr * width + dc)) % (end - start)
            part = value[start:end]
            parts.append(part if by == 0 else pltpu.roll(part, by, 0))
        return jnp.concatenate(parts, axis=0)

    def taps(stride):
        for t in range(9):
            r, q = t // 3, t % 3
            if stride == 1:
                yield t, 0, r - 1, q - 1
            else:
                phase = 2 * (1 if r != 1 else 0) + (1 if q != 1 else 0)
                yield t, phase, -1 if r == 0 else 0, -1 if q == 0 else 0

    settle(0)
    whole_x = x[...].reshape(4 * PADDED, C_IN)
    for c in range(2):
        z = mul(whole_x, narrow_part(w0, 0, 16, (2 * c, 2 * c + 1)))
        z = jnp.concatenate([z[PADDED * p : PADDED * p + ROWS] for p in range(4)], axis=0)
        standard, centre, spread, _ = standardize(z)
        put_stats(0, 256 * c, centre, spread)
        std_a[:, 256 * c : 256 * c + 256] = standard
        hidden[:, 256 * c : 256 * c + 256] = (
            soft(row(0, 2 * c) * standard + row(0, 4 + 2 * c)).astype(LOW).astype(FULL)
        )

    for t, phase, dr, dc in taps(2):
        cols0[t] = pad_low(masked(rolled(hidden[ROWS * phase : ROWS * phase + ROWS, :], -1, dr, dc), dr, dc))
    acc[...] = jnp.zeros_like(acc)

    @pl.loop(0, 9)
    def _(t):
        acc[...] += mul(cols0[t], narrow_part(w0, 16 + 8 * t, 8))

    def middle(section, std, nar):
        for c in range(2):
            at = slice(256 * c, 256 * c + 256)
            standard, centre, spread, _ = standardize(acc[0:ROWS, at])
            put_stats(section, MID + 256 * c, centre, spread)
            std[:, at] = standard
            nar[:, at] = pad_low(soft(row(section, 8 + 2 * c) * standard + row(section, 12 + 2 * c)))

    middle(0, std_b, nar0)
    acc[...] = jnp.zeros_like(acc)
    settle(1)
    settle(2)

    @pl.loop(0, 8)
    def _(c):
        at = lanes(c)
        standard, centre, spread, _ = standardize(mul(x[0], wide_part(w0, FRONT_WIDE, 64, c))[0:ROWS])
        put_stats(0, 2 * MID + pl.multiple_of(256 * c, 256), centre, spread)
        std_p[:, at] = standard
        low = pad_low(row(0, 16 + 2 * c) * standard + row(0, 32 + 2 * c))
        wide0[:, at] = low
        standard, centre, spread, _ = standardize(mul(nar0[...], wide_part(w1, 0, 32, c))[0:ROWS])
        put_stats(1, pl.multiple_of(256 * c, 256), centre, spread)
        std_1[:, at] = standard
        pre = low.astype(FULL)[0:ROWS] + row(1, 2 * c) * standard + row(1, 16 + 2 * c)
        low = pad_low(soft(pre))
        wide1[:, at] = low
        acc[...] += mul(low, narrow_part(w2, 4 * c, 4))

    for c in range(2):
        at = slice(256 * c, 256 * c + 256)
        standard, centre, spread, _ = standardize(acc[0:ROWS, at])
        put_stats(2, 256 * c, centre, spread)
        std_c[:, at] = standard
        hidden[0:ROWS, at] = soft(row(2, 2 * c) * standard + row(2, 4 + 2 * c)).astype(LOW).astype(FULL)
    for t, phase, dr, dc in taps(1):
        cols2[t] = pad_low(masked(rolled(hidden[0:ROWS, :], -1, dr, dc), dr, dc))
    acc[...] = jnp.zeros_like(acc)

    @pl.loop(0, 9)
    def _(t):
        acc[...] += mul(cols2[t], narrow_part(w2, 32 + 8 * t, 8))

    middle(2, std_d, nar2)

    turned[...] = nar2[...].T
    acc[...] = jnp.zeros_like(acc)
    settle(3)
    for fetched in rows:
        fetched.wait()

    def spread_rows(values):
        head = lax.broadcasted_iota(jnp.int32, (8, 256), 0) < 4
        first, second = (jnp.broadcast_to(value, (8, 256)) for value in values[0:2])
        parts = [jnp.broadcast_to(values[0], (32, 256)), jnp.where(head, first, second)]
        parts.append(jnp.broadcast_to(values[1], (32, 256)))
        parts.extend(jnp.broadcast_to(value, (16, 256)) for value in values[2:5])
        return jnp.concatenate(parts, axis=0)

    def crop_sums(value):
        head = lax.broadcasted_iota(jnp.int32, (8, 256), 0) < 4
        between = value[32:40]

        def total(part):
            return jnp.sum(part, axis=0, keepdims=True)

        return [
            total(value[0:32]) + total(jnp.where(head, between, 0.0)),
            total(value[40:72]) + total(jnp.where(head, 0.0, between)),
            total(value[72:88]),
            total(value[88:104]),
            total(value[104:120]),
        ]

    @pl.loop(0, 8)
    def _(c):
        at = lanes(c)
        weight = wide_part(w3, 0, 32, c)
        standard, centre, spread, inverse = standardize(mul(nar2[...], weight)[0:ROWS])
        put_stats(3, pl.multiple_of(256 * c, 256), centre, spread)
        gain = row(3, 2 * c)
        before = wide1[:, at].astype(FULL)[0:ROWS]
        pre = before + gain * standard + row(3, 16 + 2 * c)
        ending = jnp.where(gate > 0, soft(pre), before)
        final[:, at] = pad_low(ending)
        square = ending * ending
        factors = []
        for crop, total in enumerate(crop_sums(square * ending)):
            mean = total / (36.0 if crop < 2 else 16.0) + POOL_EPS
            factors.append(jnp.exp(jnp.log(mean) * (-2.0 / 3.0)) * wanted[crop : crop + 1, at])
        cotangent = spread_rows(factors) * square
        grad_pre = cotangent * gate_of(pre) * gate
        relay[:, at] = pad_low(grad_pre + cotangent * (1.0 - gate))
        result, grad_gain, grad_bias = unstandardize(grad_pre, standard, gain, inverse)
        put_row(3, 2 * c, grad_gain)
        put_row(3, 16 + 2 * c, grad_bias)
        low = pad_low(result)
        acc[...] += mul_t(low, weight)
        put_wide(w3, 0, 32, c, mul(turned[...], low))

    def flush(section):
        weights[section][VEC_TILE[section]] = grad_vec[section].astype(LOW)

    flush(3)
    stores = [pltpu.make_async_copy(w3, out_small.at[1], out_sem.at[15])]
    stores[-1].start()

    def middle_back(section, std):
        for c in range(2):
            at = slice(256 * c, 256 * c + 256)
            gain, bias = row(section, 8 + 2 * c), row(section, 12 + 2 * c)
            grad = acc[0:ROWS, at].astype(LOW).astype(FULL) * gate_of(gain * std[:, at] + bias)
            result, grad_gain, grad_bias = unstandardize(
                grad, std[:, at], gain, inverse_of(section, MID + 256 * c)
            )
            put_row(section, 8 + 2 * c, grad_gain)
            put_row(section, 12 + 2 * c, grad_bias)
            dz_n[:, at] = pad_low(result)

    def taps_back(weight, start, cols, stride, phases):
        grad_h[0 : ROWS * phases, :] = jnp.zeros((ROWS * phases, MID), FULL)
        for t, phase, dr, dc in taps(stride):
            part = mul_t(dz_n[...], narrow_part(weight, start + 8 * t, 8))[0:ROWS]
            at = slice(ROWS * phase, ROWS * phase + ROWS)
            grad_h[at, :] += rolled(masked(part, dr, dc), 1, dr, dc)
            put_narrow(weight, start + 8 * t, 8, mul(cols[t].T, dz_n[...]))

    middle_back(2, std_d)
    taps_back(w2, 32, cols2, 1, 1)
    for c in range(2):
        at = slice(256 * c, 256 * c + 256)
        gain, bias = row(2, 2 * c), row(2, 4 + 2 * c)
        grad = grad_h[0:ROWS, at] * gate_of(gain * std_c[:, at] + bias)
        result, grad_gain, grad_bias = unstandardize(grad, std_c[:, at], gain, inverse_of(2, 256 * c))
        put_row(2, 2 * c, grad_gain)
        put_row(2, 4 + 2 * c, grad_bias)
        dz_n[:, at] = pad_low(result)
    turned[...] = nar0[...].T
    acc[...] = jnp.zeros_like(acc)
    acc_x[...] = jnp.zeros_like(acc_x)

    @pl.loop(0, 8)
    def _(c):
        at = lanes(c)
        low = dz_n[...]
        grad = relay[:, at].astype(FULL) + mul_t(low, narrow_part(w2, 4 * c, 4))
        put_narrow(w2, 4 * c, 4, mul(wide1[:, at].T, low))
        grad = grad.astype(LOW).astype(FULL)[0:ROWS]
        gain = row(1, 2 * c)
        pre = wide0[:, at].astype(FULL)[0:ROWS] + gain * std_1[:, at] + row(1, 16 + 2 * c)
        grad = grad * gate_of(pre)
        result, grad_gain, grad_bias = unstandardize(
            grad, std_1[:, at], gain, inverse_of(1, pl.multiple_of(256 * c, 256))
        )
        put_row(1, 2 * c, grad_gain)
        put_row(1, 16 + 2 * c, grad_bias)
        low = pad_low(result)
        acc[...] += mul_t(low, wide_part(w1, 0, 32, c))
        put_wide(w1, 0, 32, c, mul(turned[...], low))
        grad = grad.astype(LOW).astype(FULL)
        result, grad_gain, grad_bias = unstandardize(
            grad, std_p[:, at], row(0, 16 + 2 * c), inverse_of(0, 2 * MID + pl.multiple_of(256 * c, 256))
        )
        put_row(0, 16 + 2 * c, grad_gain)
        put_row(0, 32 + 2 * c, grad_bias)
        low = pad_low(result)
        acc_x[...] += mul_t(low, wide_part(w0, FRONT_WIDE, 64, c))
        put_wide(w0, FRONT_WIDE, 64, c, mul(x[0].T, low))

    flush(1)
    flush(2)
    w2[105:115] = jnp.zeros((10, TILE, 128), LOW)
    stores.append(pltpu.make_async_copy(w1, out_small.at[0], out_sem.at[14]))
    stores[-1].start()
    for b in range(8):
        if b < 6:
            stores.append(pltpu.make_async_copy(
                w2.at[pl.ds(19 * b, 20)], out_big.at[1, inv[8 + b]], out_sem.at[8 + b]))
            stores[-1].start()
        else:
            for h in range(2):
                stores.append(pltpu.make_async_copy(
                    w2.at[pl.ds(105, 10)], out_big.at[1, inv[8 + b], pl.ds(10 * h, 10)],
                    out_sem.at[16 + 2 * (b - 6) + h]))
                stores[-1].start()

    middle_back(0, std_b)
    taps_back(w0, 16, cols0, 2, 4)
    for c in range(2):
        at = slice(256 * c, 256 * c + 256)
        gain, bias = row(0, 2 * c), row(0, 4 + 2 * c)
        grad = grad_h[:, at] * gate_of(gain * std_a[:, at] + bias)
        result, grad_gain, grad_bias = unstandardize(grad, std_a[:, at], gain, inverse_of(0, 256 * c))
        put_row(0, 2 * c, grad_gain)
        put_row(0, 4 + 2 * c, grad_bias)
        for p in range(4):
            dz_a[PADDED * p : PADDED * p + PADDED, at] = pad_low(result[ROWS * p : ROWS * p + ROWS])

    @pl.loop(0, 4)
    def _(c):
        at = lanes(c)
        low = dz_a[...]
        part = mul_t(low, narrow_part(w0, 4 * c, 4))
        grad_x[0, :, at] = (part[0:PADDED] + acc_x[:, at]).astype(LOW)
        for p in range(1, 4):
            grad_x[p, :, at] = part[PADDED * p : PADDED * p + PADDED].astype(LOW)
        turned_x = x[:, :, at].reshape(4 * PADDED, 256).T
        put_narrow(w0, 4 * c, 4, mul(turned_x, low))

    flush(0)
    for b in range(8):
        stores.append(pltpu.make_async_copy(
            w0.at[pl.ds(19 * b, 20)], out_big.at[0, inv[b]], out_sem.at[b]))
        stores[-1].start()
    for section in range(4):
        part = raw[2 * section : 2 * section + 2]
        stats[section, 0:2] = part if section < 2 else part * gate
        stats[section, 2:8] = jnp.zeros((6, 2 * MID + C_OUT), FULL)
    for store in stores:
        store.wait()


def run_step(table, gates, teach_ids, stud_ids, all_big, all_small, phases, targets):
    spots = np.zeros((3, ROWS, 128), np.int32)
    for r in range(ROWS):
        width = 6 if r < TEACH_ROWS else 4
        at = r % 36 if r < TEACH_ROWS else (r - TEACH_ROWS) % 16
        spots[0, r], spots[1, r], spots[2, r] = at // width, at % width, width
    sem = pltpu.SemaphoreType.DMA
    wide = jax.ShapeDtypeStruct((PADDED, C_OUT), LOW)
    vm = pltpu.VMEM
    return pl.pallas_call(
        step_kernel,
        name="step",
        out_shape=(
            wide, wide, wide,
            jax.ShapeDtypeStruct((4, 8, 2 * MID + C_OUT), FULL),
            jax.ShapeDtypeStruct((4, PADDED, C_IN), LOW),
            jax.ShapeDtypeStruct((2, 8, WINDOW, TILE, 128), LOW),
            jax.ShapeDtypeStruct((2, USED_TILES[1], TILE, 128), LOW),
        ),
        in_specs=[smem_spec()] * 4 + [any_spec(), any_spec(), vmem_spec(), any_spec(), vmem_spec()],
        out_specs=(vmem_spec(),) * 5 + (any_spec(),) * 2,
        scratch_shapes=[
            vm((153, TILE, 128), LOW), vm((33, TILE, 128), LOW), vm((115, TILE, 128), LOW), vm((33, TILE, 128), LOW),
            vm((12, TILE, 128), LOW), vm((4, 48, 128), FULL), vm((4, TILE, 128), FULL),
            vm((8, 2 * MID + C_OUT), FULL),
            vm((4 * ROWS, MID), FULL), vm((ROWS, MID), FULL), vm((ROWS, C_OUT), FULL), vm((ROWS, C_OUT), FULL),
            vm((ROWS, MID), FULL), vm((ROWS, MID), FULL), vm((4 * ROWS, MID), FULL),
            vm((9, PADDED, MID), LOW), vm((9, PADDED, MID), LOW),
            vm((PADDED, MID), LOW), vm((PADDED, MID), LOW), vm((MID, PADDED), LOW),
            vm((PADDED, C_OUT), LOW), vm((4 * PADDED, MID), LOW), vm((PADDED, MID), LOW),
            vm((PADDED, MID), FULL), vm((PADDED, C_IN), FULL), vm((4 * ROWS, MID), FULL),
            vm((8, C_OUT), FULL), pltpu.SMEM((16,), jnp.int32),
            sem((2, 16)), sem((17,)), sem((20,)),
        ],
        compiler_params=pltpu.CompilerParams(vmem_limit_bytes=60 << 20),
    )(table, gates, teach_ids, stud_ids, all_big, all_small, phases, targets, jnp.asarray(spots))


def reduce_kernel(big, small, wide0, wide1, final, stats, table,
                  out_big, out_small, segments, out_stats, norm, factor,
                  got, halves_x, halves_y, from_x, from_y, from_low, from_high, stage, total,
                  l_got, l_stage, l_low, l_high, l_halves_x, l_halves_y, l_from_x, l_from_y, l_total,
                  late, late_half, owner_row, by_pipe, by_dp, mine, part_sum,
                  s_send, s_recv, hx_send, hx_recv, hy_send, hy_recv, x_send, x_recv, y_send, y_recv,
                  zu_send, zu_recv, zd_send, zd_recv, lu_send, lu_recv, ld_send, ld_recv,
                  stage_sem, l_stage_sem, out_sem, late_send, late_recv, join_send, join_recv,
                  seg_send, seg_recv, stat_send, stat_recv, p_send, p_recv, d_send, d_recv):
    me = Place()
    me.enter()
    x, y, z, core = me.x, me.y, me.z, me.core
    up, down = me.device(z=z + 1), me.device(z=z - 1)
    x_side, y_side, sibling = me.device(x=1 - x), me.device(y=1 - y), me.device(core=1 - core)
    order = [
        jnp.where(z < 2, 3, 0),
        jnp.where(z == 0, 2, jnp.where(z == 1, 0, jnp.where(z == 2, 3, 1))),
        jnp.where(z == 0, 1, jnp.where(z == 1, 2, jnp.where(z == 2, 1, 2))),
        z,
    ]
    columns = ((1 - x, 1 - y), (x, 1 - y), (1 - x, y), (x, y))
    groups = {"A": (0,), "B": (1, 2), "O": (3,)}
    sequence = [
        (group, int(event[1])) for event in REDUCE_ORDER for group in groups.get(event[0], ())
    ]
    l_sequence = [(group, k) for k in range(4) for group in range(4)]

    def all_of(copies, act):
        for copy in copies:
            act(copy)

    def over(start, count, piece):
        whole = count // 512
        if whole:

            @pl.loop(0, whole)
            def _(i):
                piece(pl.multiple_of(start + 512 * i, 16), 512)

        if count % 512:
            piece(start + 512 * whole, count % 512)

    def source(array, group, k, half):
        xo, yo = columns[group]
        return array.at[xo, 2 * order[k] + yo, half]

    def share(group, k):
        at = 4 * group + k
        return remote(source(big, group, k, 1 - core), got.at[at], s_send.at[0, at], s_recv.at[0, at], sibling)

    def l_share(group, k):
        at = 4 * group + k
        return remote(source(small, group, k, 1 - core), l_got.at[at], s_send.at[1, at], s_recv.at[1, at], sibling)

    def fetch(n):
        return pltpu.make_async_copy(source(big, *sequence[n], core), stage.at[n % 4], stage_sem.at[n % 4])

    def l_fetch(group, k):
        at = 4 * group + k
        return pltpu.make_async_copy(source(small, group, k, core), l_stage.at[at], l_stage_sem.at[at])

    def add(target, at, other, slot, start, count, extras):
        def piece(begin, size):
            part = pl.ds(begin, size)
            sums = target[at, part, :].astype(FULL) + other[slot, part, :].astype(FULL)
            for ref, k in extras:
                sums = sums + ref[k, pl.ds(begin - start, size), :].astype(FULL)
            target[at, part, :] = sums.astype(LOW)

        over(start, count, piece)

    def send_half_x(k):
        return remote(got.at[k, pl.ds(BACK_CUT, BIG_HALF - BACK_CUT)], halves_x.at[k],
                      hx_send.at[k], hx_recv.at[k], x_side)

    def send_half_y(k):
        return remote(got.at[k, pl.ds(0, BACK_CUT)], halves_y.at[k], hy_send.at[k], hy_recv.at[k], y_side)

    def send_y(k):
        return remote(got.at[4 + k], from_y.at[k], y_send.at[k], y_recv.at[k], y_side)

    def send_x(k):
        return remote(got.at[8 + k], from_x.at[k], x_send.at[k], x_recv.at[k], x_side)

    def send_up(at, zd):
        return remote(got.at[at], from_low.at[zd - 1], zu_send.at[zd - 1], zu_recv.at[zd - 1], up)

    def send_down(at, zd):
        return remote(got.at[at], from_high.at[zd], zd_send.at[zd], zd_recv.at[zd], down)

    def l_column(group):
        xo, yo = columns[group]
        return 2 * xo + yo

    def l_up(group, k):
        at, zd = l_column(group), order[k] - 1
        return remote(l_got.at[4 * group + k], l_low.at[at, zd], lu_send.at[at, zd], lu_recv.at[at, zd], up)

    def l_down(group, k):
        at, zd = l_column(group), order[k]
        return remote(l_got.at[4 * group + k], l_high.at[at, zd], ld_send.at[at, zd], ld_recv.at[at, zd], down)

    def l_half_x():
        return remote(l_got.at[3, pl.ds(LIGHT_CUT, SMALL_HALF - LIGHT_CUT)], l_halves_x,
                      hx_send.at[4], hx_recv.at[4], x_side)

    def l_half_y():
        return remote(l_got.at[3, pl.ds(0, LIGHT_CUT)], l_halves_y, hy_send.at[4], hy_recv.at[4], y_side)

    def l_send_y():
        return remote(l_got.at[7], l_from_y, y_send.at[4], y_recv.at[4], y_side)

    def l_send_x():
        return remote(l_got.at[11], l_from_x, x_send.at[4], x_recv.at[4], x_side)

    leaving = (wide0, wide1, wide1, final)

    def exchange(section):
        target = {"dp": me.dp, "pipe": section}
        yield remote(leaving[section], segments.at[me.pipe], seg_send.at[section], seg_recv.at[me.pipe], target)
        yield remote(stats.at[section], out_stats.at[me.pipe], stat_send.at[section], stat_recv.at[me.pipe], target)

    def keep(section):
        yield pltpu.make_async_copy(leaving[section], segments.at[me.pipe], seg_send.at[section])
        yield pltpu.make_async_copy(stats.at[section], out_stats.at[me.pipe], stat_send.at[section])

    def arriving(micro):
        target = {"dp": me.dp, "pipe": micro}
        yield remote(wide0, segments.at[micro], seg_send.at[micro], seg_recv.at[micro], target)
        yield remote(stats.at[0], out_stats.at[micro], stat_send.at[micro], stat_recv.at[micro], target)

    for n in range(16):
        share(*sequence[n]).start()
        if n == 3:
            for item in l_sequence:
                l_share(*item).start()
    for n in range(2):
        fetch(n).start()
    for group, k in l_sequence:
        l_fetch(group, k).start()
    row_copy = pltpu.make_async_copy(table.at[2 * x], owner_row, out_sem.at[2])
    row_copy.start()

    def bulk_item(n):
        group, k = sequence[n]
        at, slot = 4 * group + k, n % 4
        if n + 2 < 16:
            fetch(n + 2).start()
        fetch(n).wait()
        share(group, k).wait_recv()
        if group == 0:
            add(got, at, stage, slot, 0, BIG_HALF, [])
            send_half_x(k).start()
            send_half_y(k).start()
        elif group == 1:
            send_half_x(k).wait_recv()
            add(got, at, stage, slot, 0, BACK_CUT, [])
            add(got, at, stage, slot, BACK_CUT, BIG_HALF - BACK_CUT, [(halves_x, k)])
            send_y(k).start()
        elif group == 2:
            send_half_y(k).wait_recv()
            add(got, at, stage, slot, 0, BACK_CUT, [(halves_y, k)])
            add(got, at, stage, slot, BACK_CUT, BIG_HALF - BACK_CUT, [])
            send_x(k).start()
        else:
            send_x(k).wait_recv()
            send_y(k).wait_recv()
            add(got, at, stage, slot, 0, BIG_HALF, [(from_x, k), (from_y, k)])

    def bulk_z(k):
        at, zd = 12 + k, order[k]

        @pl.when(zd > z)
        def _():
            @pl.when(z > 0)
            def _():
                send_up(at, zd).wait_recv()
                add(got, at, from_low, zd - 1, 0, BIG_HALF, [])

            send_up(at, zd).start()

        @pl.when(zd < z)
        def _():
            @pl.when(z < 3)
            def _():
                send_down(at, zd).wait_recv()
                add(got, at, from_high, zd, 0, BIG_HALF, [])

            send_down(at, zd).start()

    def light_item(group, k):
        at, zd, column = 4 * group + k, order[k], l_column(group)
        l_fetch(group, k).wait()
        l_share(group, k).wait_recv()
        add(l_got, at, l_stage, at, 0, SMALL_HALF, [])

        def merge(ref, slot):
            l_got[at] = (l_got[at].astype(FULL) + ref[column, slot].astype(FULL)).astype(LOW)

        if k < 3:

            @pl.when(zd > z)
            def _():
                @pl.when(z > 0)
                def _():
                    l_up(group, k).wait_recv()
                    merge(l_low, zd - 1)

                l_up(group, k).start()

            @pl.when(zd < z)
            def _():
                @pl.when(z < 3)
                def _():
                    l_down(group, k).wait_recv()
                    merge(l_high, zd)

                l_down(group, k).start()

        else:

            @pl.when(z > 0)
            def _():
                l_up(group, k).wait_recv()
                merge(l_low, zd - 1)

            @pl.when(z < 3)
            def _():
                l_down(group, k).wait_recv()
                merge(l_high, zd)

            if group == 0:
                l_half_x().start()
                l_half_y().start()

    def light_sides():
        l_half_x().wait_recv()
        l_got[7, LIGHT_CUT:SMALL_HALF, :] = (
            l_got[7, LIGHT_CUT:SMALL_HALF, :].astype(FULL) + l_halves_x[...].astype(FULL)
        ).astype(LOW)
        l_send_y().start()
        l_half_y().wait_recv()
        l_got[11, 0:LIGHT_CUT, :] = (
            l_got[11, 0:LIGHT_CUT, :].astype(FULL) + l_halves_y[...].astype(FULL)
        ).astype(LOW)
        l_send_x().start()

    def light_end():
        l_send_x().wait_recv()
        l_send_y().wait_recv()
        l_total[...] = l_got[15].astype(FULL) + l_from_x[...].astype(FULL) + l_from_y[...].astype(FULL)

    small_join = remote(late_half, late.at[pl.ds(0, SMALL_HALF)], join_send.at[1], join_recv.at[1], sibling)
    own_late = pltpu.make_async_copy(late, out_small.at[me.dp], out_sem.at[1])

    def late_z(origin, target, way):
        block = out_small.at[2 * origin + y]
        return remote(block, block, late_send.at[way, origin], late_recv.at[0, origin], target)

    def late_y(origin, yo):
        block = out_small.at[2 * origin + yo]
        return remote(block, block, late_send.at[2, origin], late_recv.at[1, origin], y_side)

    def late_step(k):
        @pl.when((core == 1) & (z >= k))
        def _():
            late_z(z - k, up, 0).wait_recv()
            pl.when(z < 3)(lambda: late_z(z - k, up, 0).start())
            late_y(z - k, y).start()

        @pl.when((core == 1) & (z + k <= 3))
        def _():
            late_z(z + k, down, 1).wait_recv()
            pl.when(z > 0)(lambda: late_z(z + k, down, 1).start())
            late_y(z + k, y).start()

    def leave():
        for section in range(4):
            @pl.when(me.pipe == section)
            def _(section=section):
                all_of(keep(section), lambda copy: copy.start())

            @pl.when(me.pipe != section)
            def _(section=section):
                all_of(exchange(section), lambda copy: copy.start())

    def late_start():
        light_end()

        @pl.when(core == 0)
        def _():
            late_half[...] = l_total[...].astype(LOW)
            small_join.start()

        @pl.when(core == 1)
        def _():
            late[SMALL_HALF:SMALL_ROWS, :] = l_total[...].astype(LOW)
            small_join.wait_recv()
            own_late.start()
            own_late.wait()
            pl.when(z < 3)(lambda: late_z(z, up, 0).start())
            pl.when(z > 0)(lambda: late_z(z, down, 1).start())
            late_y(z, y).start()

    def light_round(k):
        for n in range(4 * k, 4 * k + 4):
            light_item(*l_sequence[n])

    edge = (z == 0) | (z == 3)

    def early_z(k):
        pl.when(edge)(lambda: bulk_z(k))

    def inner_z(k):
        pl.when(jnp.logical_not(edge))(lambda: bulk_z(k))

    actions = {"LS": [light_sides], "LE": [late_start], "G": [leave]}
    numbered = {item: n for n, item in enumerate(sequence)}
    for k in range(4):
        actions["A%d" % k] = [functools.partial(bulk_item, numbered[0, k])]
        actions["B%d" % k] = [functools.partial(bulk_item, numbered[group, k]) for group in (1, 2)]
        actions["O%d" % k] = [functools.partial(bulk_item, numbered[3, k])]
        actions["L%d" % k] = [functools.partial(light_round, k)]
        if k < 3:
            actions["E%d" % k] = [functools.partial(early_z, k)]
            actions["I%d" % k] = [functools.partial(inner_z, k)]
        if k:
            actions["T%d" % k] = [functools.partial(late_step, k)]
    for event in REDUCE_ORDER:
        for action in actions[event]:
            action()

    row_copy.wait()
    part_sum[...] = jnp.sum((l_total[...] * l_total[...]).reshape(SMALL_HALF // 8, 8, 128), axis=0)
    lane = lax.broadcasted_iota(jnp.int32, (8, 128), 1)
    is_last = jnp.where((lane == me.dp) & (owner_row[...] == 7), 1.0, 0.0)
    weight = jnp.broadcast_to(jnp.sum(is_last, axis=1, keepdims=True), (8, 128))
    weight = jnp.where(core == 0, jnp.ones((8, 128), FULL), weight)

    def end(low, high):
        def piece(begin, size, scale):
            part = pl.ds(begin, size)
            sums = got[15, part, :].astype(FULL)
            if low:
                sums = sums + from_low[z - 1, part, :].astype(FULL)
            if high:
                sums = sums + from_high[z, part, :].astype(FULL)
            total[part, :] = sums
            squares = jnp.sum((sums * sums).reshape(size // 8, 8, 128), axis=0)
            part_sum[...] += squares if scale is None else squares * scale

        over(0, BIG_HALF - 256, lambda begin, size: piece(begin, size, None))
        piece(BIG_HALF - 256, 256, weight)

    @pl.when(z == 0)
    def _():
        send_down(15, z).wait_recv()
        end(False, True)

    @pl.when((z > 0) & (z < 3))
    def _():
        send_up(15, z).wait_recv()
        send_down(15, z).wait_recv()
        end(True, True)

    @pl.when(z == 3)
    def _():
        send_up(15, z).wait_recv()
        end(True, False)

    big_join = remote(total, out_big.at[1], join_send.at[0], join_recv.at[0], sibling)
    own_big = pltpu.make_async_copy(total, out_big.at[0], out_sem.at[0])

    @pl.when(core == 0)
    def _():
        own_big.start()

    @pl.when(core == 1)
    def _():
        big_join.start()

    def along_pipe(step, slot):
        target = {"dp": me.dp, "pipe": lax.rem(me.pipe + step, 4)}
        return remote(part_sum, by_pipe.at[slot], p_send.at[step], p_recv.at[step], target)

    def along_dp(step, slot):
        target = {"dp": lax.rem(me.dp + step, 8), "pipe": me.pipe}
        return remote(mine, by_dp.at[slot], d_send.at[step], d_recv.at[step], target)

    for step in range(1, 4):
        along_pipe(step, me.pipe).start()
    by_pipe[me.pipe] = part_sum[...]
    for step in range(1, 4):
        along_pipe(step, lax.rem(me.pipe + 4 - step, 4)).wait_recv()
    mine[...] = jnp.sum(by_pipe[...], axis=0)
    for step in range(1, 8):
        along_dp(step, me.dp).start()
    by_dp[me.dp] = mine[...]
    for step in range(1, 8):
        along_dp(step, lax.rem(me.dp + 8 - step, 8)).wait_recv()
    whole = jnp.sum(jnp.sum(by_dp[...], axis=0), axis=0, keepdims=True)
    length = jnp.sqrt(jnp.broadcast_to(jnp.sum(whole, axis=1, keepdims=True), (8, 128)))
    norm[...] = length
    factor[...] = jnp.minimum(1.0, CLIP_NORM / length)

    @pl.when(core == 0)
    def _():
        own_big.wait()
        big_join.wait_recv()
        small_join.wait_send()

    @pl.when(core == 1)
    def _():
        big_join.wait_send()
        for origin in range(4):
            late_y(origin, 1 - y).wait_recv()
            late_y(origin, y).wait_send()
            pl.when((z < 3) & (origin <= z))(lambda: late_z(origin, up, 0).wait_send())
            pl.when((z > 0) & (origin >= z))(lambda: late_z(origin, down, 1).wait_send())

    for other in range(4):
        @pl.when(me.pipe == other)
        def _(other=other):
            all_of(keep(other), lambda copy: copy.wait())

        @pl.when(me.pipe != other)
        def _(other=other):
            all_of(exchange(other), lambda copy: copy.wait_send())
            all_of(arriving(other), lambda copy: copy.wait_recv())

    for step in range(1, 4):
        along_pipe(step, me.pipe).wait_send()
    for step in range(1, 8):
        along_dp(step, me.dp).wait_send()
    for copy in (l_half_x(), l_half_y(), l_send_x(), l_send_y()):
        copy.wait_send()
    for k in range(4):
        send_half_x(k).wait_send()
        send_half_y(k).wait_send()
        send_x(k).wait_send()
        send_y(k).wait_send()
        for group in range(4):
            share(group, k).wait_send()
            l_share(group, k).wait_send()
    for k in range(3):
        zd, at = order[k], 12 + k

        @pl.when(zd > z)
        def _(at=at, zd=zd, k=k):
            send_up(at, zd).wait_send()
            for group in range(4):
                l_up(group, k).wait_send()

        @pl.when(zd < z)
        def _(at=at, zd=zd, k=k):
            send_down(at, zd).wait_send()
            for group in range(4):
                l_down(group, k).wait_send()


def reduce_all(big, small, wide0, wide1, final, stats, table):
    sem = pltpu.SemaphoreType.DMA
    vm = pltpu.VMEM
    lane_tile = jax.ShapeDtypeStruct((8, 128), FULL)
    return pl.pallas_call(
        reduce_kernel,
        name="reduce_all",
        out_shape=(
            jax.ShapeDtypeStruct((2, BIG_HALF, 128), FULL),
            jax.ShapeDtypeStruct((8, SMALL_ROWS, 128), LOW),
            jax.ShapeDtypeStruct((4,) + wide0.shape, LOW),
            jax.ShapeDtypeStruct((4,) + stats.shape[1:], FULL),
            lane_tile,
            lane_tile,
        ),
        in_specs=[any_spec()] * 7,
        out_specs=(any_spec(),) * 4 + (vmem_spec(),) * 2,
        scratch_shapes=[
            vm((16, BIG_HALF, 128), LOW), vm((4, BIG_HALF - BACK_CUT, 128), LOW), vm((4, BACK_CUT, 128), LOW),
            vm((4, BIG_HALF, 128), LOW), vm((4, BIG_HALF, 128), LOW),
            vm((3, BIG_HALF, 128), LOW), vm((3, BIG_HALF, 128), LOW),
            vm((4, BIG_HALF, 128), LOW), vm((BIG_HALF, 128), FULL),
            vm((16, SMALL_HALF, 128), LOW), vm((16, SMALL_HALF, 128), LOW),
            vm((4, 3, SMALL_HALF, 128), LOW), vm((4, 3, SMALL_HALF, 128), LOW),
            vm((SMALL_HALF - LIGHT_CUT, 128), LOW), vm((LIGHT_CUT, 128), LOW),
            vm((SMALL_HALF, 128), LOW), vm((SMALL_HALF, 128), LOW), vm((SMALL_HALF, 128), FULL),
            vm((SMALL_ROWS, 128), LOW), vm((SMALL_HALF, 128), LOW), vm((8, 128), jnp.int32),
            vm((4, 8, 128), FULL), vm((8, 8, 128), FULL), vm((8, 128), FULL), vm((8, 128), FULL),
            sem((2, 16)), sem((2, 16)),
            sem((5,)), sem((5,)), sem((5,)), sem((5,)), sem((5,)), sem((5,)), sem((5,)), sem((5,)),
            sem((3,)), sem((3,)), sem((3,)), sem((3,)),
            sem((4, 3)), sem((4, 3)), sem((4, 3)), sem((4, 3)),
            sem((4,)), sem((16,)), sem((3,)), sem((3, 4)), sem((2, 4)), sem((2,)), sem((2,)),
            sem((4,)), sem((4,)), sem((4,)), sem((4,)), sem((4,)), sem((4,)), sem((8,)), sem((8,)),
        ],
        compiler_params=pltpu.CompilerParams(
            collective_id=1, has_side_effects=True, vmem_limit_bytes=62 << 20
        ),
    )(big.reshape(2, 8, 2, BIG_HALF, 128), small.reshape(2, 8, 2, SMALL_HALF, 128),
      wide0, wide1, final, stats, table)


def high_dot(a, b, dims=((1,), (0,))):
    return lax.dot_general(a, b, (dims, ((), ())), precision=HIGH, preferred_element_type=FULL)


PIECES = 7
FRONT = 48


def update_kernel(owners, factor_ref, big, small, gram_old, basis_old, params, moment, second,
                  clipped, moment_new, second_new, params_new, gram_new, basis_new,
                  tiles, low, grad, held, rotated, weights, gram, in_sem, out_sem, tile_sem):
    factor = factor_ref[0:1, :]
    block, section = owners[0, lax.axis_index("dp")], lax.axis_index("pipe")
    even = lax.rem(section, 2) == 0
    span = params.shape[0]
    piece = held.shape[0] // PIECES

    @pl.when(even)
    def _():
        pltpu.make_async_copy(big, tiles, tile_sem).start()

    def loads(i):
        part = pl.ds(piece * i, min(piece, span - piece * i))
        for n, (src, dst) in enumerate(((params, weights), (moment, held), (second, rotated))):
            yield pltpu.make_async_copy(src.at[part, 0, :], dst.at[part], in_sem.at[n, i])

    def stores(i):
        count = min(piece, span - piece * i)
        part = pl.ds(piece * i, count)
        yield pltpu.make_async_copy(
            grad.at[pl.ds(FRONT + piece * i, count)], clipped.at[part, 0, :], out_sem.at[3, i])
        pairs = ((held, moment_new), (rotated, second_new), (weights, params_new))
        for n, (src, dst) in enumerate(pairs):
            yield pltpu.make_async_copy(src.at[part], dst.at[part, 0, :], out_sem.at[n, i])

    for i in range(PIECES):
        for load in loads(i):
            load.start()

    @pl.when(even)
    def _():
        pltpu.make_async_copy(big, tiles, tile_sem).wait()

    @pl.when(jnp.logical_not(even))
    def _():
        low[...] = jnp.zeros_like(low)

        @pl.when(block == 0)
        def _():
            copy = pltpu.make_async_copy(small.at[0:20], low, tile_sem)
            copy.start()
            copy.wait()

        @pl.when(block == 1)
        def _():
            copy = pltpu.make_async_copy(small.at[19:33], low.at[0:14], tile_sem)
            copy.start()
            copy.wait()

        @pl.loop(0, WINDOW)
        def _(r):
            tiles[r] = low[r].astype(FULL)

    @pl.loop(0, WINDOW)
    def _(r):
        narrow, plain = tile_forms(section, STRIDE * block + r)
        base = FRONT - 6 * block + TILE * r

        @pl.when(narrow)
        def _():
            for j in range(4):
                grad[pl.ds(base + j, 64, 4), :] = tiles[r, 64 * j : 64 * j + 64, :]

        @pl.when(plain)
        def _():
            grad[pl.ds(base, TILE), :] = tiles[r]

        @pl.when(jnp.logical_not(narrow | plain))
        def _():
            for j in range(16):
                grad[pl.ds(base + j, 16, 16), :] = tiles[r, 16 * j : 16 * j + 16, :]

    tail = piece * PIECES - 8
    rest = lax.broadcasted_iota(jnp.int32, (8, 128), 0) + tail
    grad[FRONT + tail : FRONT + tail + 8, :] = jnp.where(
        rest < span, grad[FRONT + tail : FRONT + tail + 8, :], 0.0
    )
    gram[...] = jnp.zeros_like(gram)

    def halves(value):
        high = value.astype(LOW)
        return high, (value - high.astype(FULL)).astype(LOW)

    def split_dot(a, b, dims=((1,), (0,))):
        def dot(left, right):
            return lax.dot_general(left, right, (dims, ((), ())), preferred_element_type=FULL)

        return dot(a[0], b[0]) + (dot(a[0], b[1]) + dot(a[1], b[0]))

    @pl.loop(0, PIECES)
    def _(i):
        part = halves(grad[pl.ds(pl.multiple_of(FRONT + piece * i, 8), piece), :])
        gram[...] += split_dot(part, part, ((0,), (0,)))

    old = basis_old[...]
    fresh = DECAY_STATS * gram_old[...] + (1.0 - DECAY_STATS) * (gram[...] * (factor * factor))
    gram_new[...] = fresh
    product = high_dot(fresh, old)
    rotation = product / jnp.sqrt(jnp.sum(product * product))
    for repeat in range(NS_STEPS):
        square = high_dot(rotation, rotation, ((0,), (0,)))
        rotation = 1.5 * rotation - 0.5 * high_dot(rotation, square)
    basis_new[...] = rotation
    change = halves(high_dot(old, rotation, ((0,), (0,))))
    turn = halves(rotation)
    correction = math.sqrt(1.0 - DECAY_SECOND**STEP) / (1.0 - DECAY_FIRST**STEP)
    for i in range(PIECES):
        for load in loads(i):
            load.wait()
        at = slice(FRONT + piece * i, FRONT + piece * i + piece)
        part = slice(piece * i, piece * i + piece)
        clip = grad[at, :] * factor
        grad[at, :] = clip
        turned = split_dot(halves(clip), turn)
        first = DECAY_FIRST * split_dot(halves(held[part, :]), change) + (1.0 - DECAY_FIRST) * turned
        power = DECAY_SECOND * rotated[part, :] + (1.0 - DECAY_SECOND) * turned * turned
        held[part, :] = first
        rotated[part, :] = power
        scaled = halves(first / (jnp.sqrt(power) + ADAM_EPS))
        direction = split_dot(scaled, turn, ((1,), (1,))) * correction
        before = weights[part, :]
        weights[part, :] = before - LEARN_RATE * (direction + WEIGHT_DECAY * before)
        for store in stores(i):
            store.start()
    for i in range(PIECES):
        for store in stores(i):
            store.wait()


def update(owners, factor, big, small, gram_old, basis_old, params, moment, second):
    span = params.shape[1] // 128
    rows = -(-span // (8 * PIECES)) * 8 * PIECES
    flat_shape = jax.ShapeDtypeStruct((span, 1, 128), FULL)
    square = jax.ShapeDtypeStruct((128, 128), FULL)
    sem = pltpu.SemaphoreType.DMA
    vm = pltpu.VMEM
    outs = pl.pallas_call(
        update_kernel,
        name="update",
        out_shape=(flat_shape,) * 4 + (square,) * 2,
        in_specs=[smem_spec(), vmem_spec()] + [any_spec()] * 2 + [vmem_spec()] * 2 + [any_spec()] * 3,
        out_specs=(any_spec(),) * 4 + (vmem_spec(),) * 2,
        scratch_shapes=[
            vm((WINDOW, TILE, 128), FULL), vm((WINDOW, TILE, 128), LOW),
            vm((FRONT + WINDOW * TILE, 128), FULL), vm((rows, 128), FULL), vm((rows, 128), FULL),
            vm((rows, 128), FULL), vm((128, 128), FULL), sem((3, PIECES)), sem((4, PIECES)), sem,
        ],
        compiler_params=pltpu.CompilerParams(vmem_limit_bytes=60 << 20),
    )(owners, factor, big.reshape(WINDOW, TILE, 128), small.reshape(USED_TILES[1], TILE, 128),
      gram_old, basis_old, params.reshape(span, 1, 128), moment.reshape(span, 1, 128),
      second.reshape(span, 1, 128))
    return tuple(out.reshape(1, span * 128) for out in outs[:4]) + outs[4:]


def to_phases(teach, stud):
    def split(part):
        crops, high, across, channels = part.shape
        part = part.reshape(crops, high // 2, 2, across // 2, 2, channels).transpose(2, 4, 0, 1, 3, 5)
        return part.reshape(4, -1, channels)

    zeros = jnp.zeros((4, PADDED - ROWS, teach.shape[-1]), teach.dtype)
    return jnp.concatenate([split(teach), split(stud), zeros], axis=1)


def from_phases(phases, shape):
    crops, high, across, channels = shape
    part = phases.reshape(2, 2, crops, high // 2, across // 2, channels)
    return part.transpose(2, 3, 0, 4, 1, 5).reshape(shape)


def on_small_slice(
    teach_in,
    stud_in,
    params,
    owners,
    depth_gates,
    teach_ids,
    stud_ids,
    targets,
    moment,
    second,
    gram_stats,
    eigen_basis,
):
    phases = to_phases(teach_in[0], stud_in[0])
    big, small, ids = prepare(owners, params)
    all_big, all_small, table = gather_all(big, small, ids)
    wide_0, wide_1, final, stats, grad_x, out_big, out_small = run_step(
        table,
        depth_gates,
        teach_ids,
        stud_ids,
        all_big.reshape(2, 8, 2, WINDOW // 2, TILE, 128),
        all_small.reshape(2, USED_TILES[1], TILE, 128),
        phases,
        targets,
    )
    sum_big, sum_small, segments, stats, norm, factor = reduce_all(
        out_big, out_small, wide_0, wide_1, final, stats, table
    )
    clipped, moment_new, second_new, params_new, gram_new, rotation = update(
        owners, factor, sum_big, sum_small, gram_stats[0], eigen_basis[0], params, moment, second
    )
    teach_shape, stud_shape = teach_in.shape[1:], stud_in.shape[1:]
    small_teach = (teach_shape[0], teach_shape[1] // 2, teach_shape[2] // 2, C_OUT)
    small_stud = (stud_shape[0], stud_shape[1] // 2, stud_shape[2] // 2, C_OUT)
    segment_teach = segments[:, :TEACH_ROWS].reshape((4,) + small_teach)
    segment_stud = segments[:, TEACH_ROWS:ROWS].reshape((4,) + small_stud)
    stats = stats[:, 0:2]
    teach_grad = from_phases(grad_x[:, :TEACH_ROWS], teach_shape)
    stud_grad = from_phases(grad_x[:, TEACH_ROWS:ROWS], stud_shape)
    grad_norm = norm[0, 0]
    return (
        segment_teach[None],
        segment_stud[None],
        teach_grad[None],
        stud_grad[None],
        stats[None, :, None],
        grad_norm,
        clipped,
        moment_new,
        second_new,
        params_new,
        gram_new[None],
        rotation[None],
    )


def solution(mesh):
    placed = (
        P("pipe", "dp", None, None, None),
        P("pipe", "dp", None, None, None),
        P("pipe", "dp"),
        P("pipe", None),
        P(),
        P(None, "dp"),
        P(None, "dp"),
        P(),
        P("pipe", "dp"),
        P("pipe", "dp"),
        P("pipe", "dp", None),
        P("pipe", "dp", None),
    )
    small_slice = mesh.shape["dp"] == 8 and mesh.shape["pipe"] == 4
    return jax.shard_map(
        on_small_slice if small_slice else on_device,
        mesh=mesh,
        in_specs=placed,
        out_specs=(
            P("pipe", None, "dp", None, None, None),
            P("pipe", None, "dp", None, None, None),
            P("pipe", "dp", None, None, None),
            P("pipe", "dp", None, None, None),
            P("pipe", None, "dp", None, None),
            P(),
            P("pipe", "dp"),
            P("pipe", "dp"),
            P("pipe", "dp"),
            P("pipe", "dp"),
            P("pipe", "dp", None),
            P("pipe", "dp", None),
        ),
        check_vma=False,
    )
```

```python
import functools
import math

import jax
import jax.numpy as jnp
import numpy as np
from jax import lax
from jax.experimental import pallas as pl
from jax.experimental.pallas import tpu as pltpu
from jax.sharding import PartitionSpec as P

C_IN = 1024
MID = 512
C_OUT = 2048
STEP = 10
NS_STEPS = 5


HIGH = lax.Precision.HIGHEST
NORM_EPS = 1e-05
POOL_EPS = 1e-06
CLIP_NORM = 1.0
LEARN_RATE = 0.02
DECAY_FIRST = 0.9
DECAY_SECOND = 0.95
DECAY_STATS = 0.95
ADAM_EPS = 1e-08
WEIGHT_DECAY = 0.01


def section_shapes(section):
    if section == 0:
        return [
            ("first_conv", (C_IN, MID)),
            ("middle_conv", (9 * MID, MID)),
            ("skip_conv", (C_IN, C_OUT)),
            ("first_gain", (MID,)),
            ("first_bias", (MID,)),
            ("middle_gain", (MID,)),
            ("middle_bias", (MID,)),
            ("skip_gain", (C_OUT,)),
            ("skip_bias", (C_OUT,)),
        ]
    if section == 2:
        return [
            ("first_conv", (C_OUT, MID)),
            ("middle_conv", (9 * MID, MID)),
            ("first_gain", (MID,)),
            ("first_bias", (MID,)),
            ("middle_gain", (MID,)),
            ("middle_bias", (MID,)),
        ]
    return [("last_conv", (MID, C_OUT)), ("last_gain", (C_OUT,)), ("last_bias", (C_OUT,))]


def unpack(flat_vector, section):
    pieces = {}
    offset = 0
    for entry_name, entry_shape in section_shapes(section):
        entry_size = math.prod(entry_shape)
        pieces[entry_name] = flat_vector[offset : offset + entry_size].reshape(entry_shape)
        offset = offset + entry_size
    return pieces


def pack(grads, section, flat_size):
    parts = [grads[entry_name].reshape(-1) for entry_name, entry_shape in section_shapes(section)]
    used = sum((math.prod(entry_shape) for entry_name, entry_shape in section_shapes(section)))
    parts.append(jnp.zeros((flat_size - used,), jnp.float32))
    return jnp.concatenate(parts)


def as_float(vector):
    return vector.astype(jnp.float32)


def to_low(groups):
    return tuple((portion.astype(jnp.bfloat16) for portion in groups))


def to_high(groups):
    return tuple((portion.astype(jnp.float32) for portion in groups))


def point_conv(groups, weight):
    return tuple(
        (
            jnp.einsum("khwc,cd->khwd", portion, weight, preferred_element_type=jnp.float32)
            for portion in groups
        )
    )


def point_back(grad_out, groups, weight):
    low_grads = to_low(grad_out)
    grad_input = tuple(
        (
            jnp.einsum("khwd,cd->khwc", grad_part, weight, preferred_element_type=jnp.float32)
            for grad_part in low_grads
        )
    )
    grad_weight = sum(
        (
            jnp.einsum("khwc,khwd->cd", in_part, grad_part, preferred_element_type=jnp.float32)
            for in_part, grad_part in zip(groups, low_grads)
        )
    )
    return (grad_input, grad_weight)


def patches(portion, stride):
    height = portion.shape[1]
    across = portion.shape[2]
    padded = jnp.pad(portion, ((0, 0), (1, 1), (1, 1), (0, 0)))
    shifted = [
        padded[:, row_off : row_off + height : stride, col_off : col_off + across : stride, :]
        for row_off in range(3)
        for col_off in range(3)
    ]
    return jnp.concatenate(shifted, axis=-1)


def area_conv(groups, weight, stride):
    columns = tuple((patches(portion, stride) for portion in groups))
    return (point_conv(columns, weight), columns)


def unpatch(grad_cols, height, across, stride):
    channels = grad_cols.shape[-1] // 9
    padded = jnp.zeros((grad_cols.shape[0], height + 2, across + 2, channels), jnp.float32)
    for row_off in range(3):
        for col_off in range(3):
            offset = (3 * row_off + col_off) * channels
            padded = padded.at[
                :, row_off : row_off + height : stride, col_off : col_off + across : stride, :
            ].add(grad_cols[..., offset : offset + channels])
    return padded[:, 1 : height + 1, 1 : across + 1, :]


def area_back(grad_out, columns, weight, stride, in_shapes):
    grad_cols, grad_weight = point_back(grad_out, columns, weight)
    grad_input = tuple(
        (
            unpatch(grad_part, shape_item[1], shape_item[2], stride)
            for grad_part, shape_item in zip(grad_cols, in_shapes)
        )
    )
    return (grad_input, grad_weight)


def batch_norm(groups, gain, bias):
    rows_total = sum((portion.shape[0] * portion.shape[1] * portion.shape[2] for portion in groups))
    centre = sum((jnp.sum(portion, axis=(0, 1, 2)) for portion in groups)) / rows_total
    spread = (
        sum((jnp.sum(jnp.square(portion - centre), axis=(0, 1, 2)) for portion in groups))
        / rows_total
    )
    inverse = lax.rsqrt(spread + NORM_EPS)
    standard = tuple(((portion - centre) * inverse for portion in groups))
    normed = tuple((gain * std_part + bias for std_part in standard))
    return (normed, (centre, spread, inverse, standard))


def norm_back(grad_out, gain, saved):
    centre, spread, inverse, standard = saved
    rows_total = sum(
        (portion.shape[0] * portion.shape[1] * portion.shape[2] for portion in standard)
    )
    grad_sum = sum((jnp.sum(grad_part, axis=(0, 1, 2)) for grad_part in grad_out))
    grad_dot = sum(
        (
            jnp.sum(grad_part * std_part, axis=(0, 1, 2))
            for grad_part, std_part in zip(grad_out, standard)
        )
    )
    grad_input = tuple(
        (
            gain
            * inverse
            * (grad_part - grad_sum / rows_total - std_part * (grad_dot / rows_total))
            for grad_part, std_part in zip(grad_out, standard)
        )
    )
    return (grad_input, grad_dot, grad_sum)


def through_softplus(grad_out, pre_values):
    return tuple(
        (grad_part * jax.nn.sigmoid(pre_part) for grad_part, pre_part in zip(grad_out, pre_values))
    )


def front_forward(pieces, inputs):
    first = point_conv(inputs, pieces["first_conv"])
    normed_a, saved_a = batch_norm(
        first, as_float(pieces["first_gain"]), as_float(pieces["first_bias"])
    )
    hidden = tuple((jax.nn.softplus(portion).astype(jnp.bfloat16) for portion in normed_a))
    middle, columns = area_conv(hidden, pieces["middle_conv"], 2)
    normed_b, saved_b = batch_norm(
        middle, as_float(pieces["middle_gain"]), as_float(pieces["middle_bias"])
    )
    narrow = tuple((jax.nn.softplus(portion) for portion in normed_b))
    reduced = tuple((portion[:, ::2, ::2, :] for portion in inputs))
    skipped = point_conv(reduced, pieces["skip_conv"])
    wide, saved_p = batch_norm(
        skipped, as_float(pieces["skip_gain"]), as_float(pieces["skip_bias"])
    )
    norm_rows = jnp.stack(
        [
            jnp.concatenate([saved_a[0], saved_b[0], saved_p[0]]),
            jnp.concatenate([saved_a[1], saved_b[1], saved_p[1]]),
        ]
    )
    kept = (normed_a, hidden, columns, normed_b, reduced, saved_a, saved_b, saved_p)
    return (wide, narrow, norm_rows, kept)


def front_backward(pieces, inputs, grad_wide, grad_narrow):
    wide, narrow, norm_rows, kept = front_forward(pieces, inputs)
    normed_a, hidden, columns, normed_b, reduced, saved_a, saved_b, saved_p = kept
    grads = {}
    grad_pre_b = through_softplus(grad_narrow, normed_b)
    grad_mid, grads["middle_gain"], grads["middle_bias"] = norm_back(
        grad_pre_b, as_float(pieces["middle_gain"]), saved_b
    )
    grad_hidden, grads["middle_conv"] = area_back(
        grad_mid, columns, pieces["middle_conv"], 2, [portion.shape for portion in hidden]
    )
    grad_pre_a = through_softplus(grad_hidden, normed_a)
    grad_first, grads["first_gain"], grads["first_bias"] = norm_back(
        grad_pre_a, as_float(pieces["first_gain"]), saved_a
    )
    grad_inputs, grads["first_conv"] = point_back(grad_first, inputs, pieces["first_conv"])
    grad_skip, grads["skip_gain"], grads["skip_bias"] = norm_back(
        grad_wide, as_float(pieces["skip_gain"]), saved_p
    )
    grad_reduced, grads["skip_conv"] = point_back(grad_skip, reduced, pieces["skip_conv"])
    grad_inputs = tuple(
        (
            full_part.at[:, ::2, ::2, :].add(part_reduced)
            for full_part, part_reduced in zip(grad_inputs, grad_reduced)
        )
    )
    return (grad_inputs, grads)


def join_forward(pieces, wide, narrow):
    last = point_conv(narrow, pieces["last_conv"])
    normed, saved = batch_norm(last, as_float(pieces["last_gain"]), as_float(pieces["last_bias"]))
    pre_values = tuple(
        (
            skip_part.astype(jnp.float32) + branch_part
            for skip_part, branch_part in zip(wide, normed)
        )
    )
    ending = tuple((jax.nn.softplus(pre_part) for pre_part in pre_values))
    filler = jnp.zeros((2 * MID,), jnp.float32)
    norm_rows = jnp.stack(
        [jnp.concatenate([saved[0], filler]), jnp.concatenate([saved[1], filler])]
    )
    return (ending, norm_rows, (pre_values, saved))


def join_grads(pieces, narrow, kept, grad_out, gate):
    pre_values, saved = kept
    grad_pre = tuple(
        (
            grad_part * jax.nn.sigmoid(pre_part) * gate
            for grad_part, pre_part in zip(grad_out, pre_values)
        )
    )
    grad_wide = tuple(
        (pre_grad + grad_part * (1.0 - gate) for pre_grad, grad_part in zip(grad_pre, grad_out))
    )
    grad_last, gain_grad, bias_grad = norm_back(grad_pre, as_float(pieces["last_gain"]), saved)
    grad_narrow, weight_grad = point_back(grad_last, narrow, pieces["last_conv"])
    grads = {"last_conv": weight_grad, "last_gain": gain_grad, "last_bias": bias_grad}
    return (grad_wide, grad_narrow, grads)


def split_forward(pieces, wide):
    first = point_conv(wide, pieces["first_conv"])
    normed_a, saved_a = batch_norm(
        first, as_float(pieces["first_gain"]), as_float(pieces["first_bias"])
    )
    hidden = tuple((jax.nn.softplus(portion).astype(jnp.bfloat16) for portion in normed_a))
    middle, columns = area_conv(hidden, pieces["middle_conv"], 1)
    normed_b, saved_b = batch_norm(
        middle, as_float(pieces["middle_gain"]), as_float(pieces["middle_bias"])
    )
    narrow = tuple((jax.nn.softplus(portion) for portion in normed_b))
    filler = jnp.zeros((C_OUT,), jnp.float32)
    norm_rows = jnp.stack(
        [
            jnp.concatenate([saved_a[0], saved_b[0], filler]),
            jnp.concatenate([saved_a[1], saved_b[1], filler]),
        ]
    )
    return (narrow, norm_rows, (normed_a, hidden, columns, normed_b, saved_a, saved_b))


def split_backward(pieces, wide, grad_relay, grad_narrow):
    narrow, norm_rows, kept = split_forward(pieces, wide)
    normed_a, hidden, columns, normed_b, saved_a, saved_b = kept
    grads = {}
    grad_pre_b = through_softplus(grad_narrow, normed_b)
    grad_mid, grads["middle_gain"], grads["middle_bias"] = norm_back(
        grad_pre_b, as_float(pieces["middle_gain"]), saved_b
    )
    grad_hidden, grads["middle_conv"] = area_back(
        grad_mid, columns, pieces["middle_conv"], 1, [portion.shape for portion in hidden]
    )
    grad_pre_a = through_softplus(grad_hidden, normed_a)
    grad_first, grads["first_gain"], grads["first_bias"] = norm_back(
        grad_pre_a, as_float(pieces["first_gain"]), saved_a
    )
    grad_conv_in, grads["first_conv"] = point_back(grad_first, wide, pieces["first_conv"])
    grad_wide = tuple(
        (relay_part + conv_part for relay_part, conv_part in zip(grad_relay, grad_conv_in))
    )
    return (grad_wide, grads)


def pool_grad(final, targets, picks):
    result = []
    for portion, pick_ids in zip(final, picks):
        cubes = jnp.mean(portion * portion * portion, axis=(1, 2)) + POOL_EPS
        factor = jnp.exp(jnp.log(cubes) * (-2.0 / 3.0)) * targets[pick_ids]
        result.append(factor[:, None, None, :] * portion * portion)
    return tuple(result)


def used_size(section):
    return sum((math.prod(entry_shape) for entry_name, entry_shape in section_shapes(section)))


def batch_pass(reals, inputs, gate, targets, picks):
    pieces = [unpack(reals[section], section) for section in range(4)]
    wide_f, narrow_f, rows_0, _ = front_forward(pieces[0], inputs)
    wide_0, narrow_0 = to_low(wide_f), to_low(narrow_f)
    ending_1, rows_1, kept_1 = join_forward(pieces[1], wide_0, narrow_0)
    wide_1 = to_low(ending_1)
    narrow_f, rows_2, _ = split_forward(pieces[2], wide_1)
    narrow_2 = to_low(narrow_f)
    ending_3, rows_3, kept_3 = join_forward(pieces[3], wide_1, narrow_2)
    final = tuple(
        (
            jnp.where(gate > 0, end_part, relay_part.astype(jnp.float32))
            for end_part, relay_part in zip(ending_3, wide_1)
        )
    )
    cotangent = pool_grad(final, targets, picks)
    grad_wide, grad_narrow, grads_3 = join_grads(pieces[3], narrow_2, kept_3, cotangent, gate)
    grad_wide, grads_2 = split_backward(
        pieces[2], wide_1, to_high(to_low(grad_wide)), to_high(to_low(grad_narrow))
    )
    grad_wide, grad_narrow, grads_1 = join_grads(
        pieces[1], narrow_0, kept_1, to_high(to_low(grad_wide)), 1.0
    )
    grad_inputs, grads_0 = front_backward(
        pieces[0], inputs, to_high(to_low(grad_wide)), to_high(to_low(grad_narrow))
    )
    outs = (wide_0, wide_1, wide_1, to_low(final))
    stats = jnp.stack([rows_0, rows_1, rows_2 * gate, rows_3 * gate])
    return (outs, stats, to_low(grad_inputs), (grads_0, grads_1, grads_2, grads_3))


def on_device(
    teach_in,
    stud_in,
    params,
    owners,
    depth_gates,
    teach_ids,
    stud_ids,
    targets,
    moment,
    second,
    gram_stats,
    eigen_basis,
):
    sections = lax.axis_size("pipe")
    rank = lax.axis_index("pipe")
    owner_count = lax.axis_size("dp")
    span_size = params.shape[1]
    flat_size = span_size * owner_count
    owner_rows = lax.all_gather(owners, "pipe", axis=0, tiled=True)
    gathered = lax.all_gather(params[0].astype(jnp.bfloat16), ("pipe", "dp"), axis=0)
    gathered = gathered.reshape(sections, owner_count, span_size)
    reals = []
    for section in range(sections):
        inverse = jnp.argsort(owner_rows[section]).astype(jnp.int32)
        blocks = -(-used_size(section) // span_size)
        reals.append(gathered[section][inverse[:blocks]].reshape(blocks * span_size))
    inputs = (teach_in[0], stud_in[0])
    gate = depth_gates[rank].astype(jnp.float32)
    outs, stats, (teach_grad, stud_grad), grads = batch_pass(
        reals, inputs, gate, targets, (teach_ids[rank], stud_ids[rank])
    )
    segment_teach = lax.all_to_all(
        jnp.stack([part[0] for part in outs]), "pipe", split_axis=0, concat_axis=0, tiled=True
    )
    segment_stud = lax.all_to_all(
        jnp.stack([part[1] for part in outs]), "pipe", split_axis=0, concat_axis=0, tiled=True
    )
    stats = lax.all_to_all(stats, "pipe", split_axis=0, concat_axis=0, tiled=True)
    rows = []
    for section in range(sections):
        flat = pack(grads[section], section, flat_size).reshape(owner_count, span_size)
        rows.append(flat[owner_rows[section]])
    span_total = lax.psum_scatter(
        jnp.stack(rows).reshape(sections * owner_count, span_size),
        ("pipe", "dp"),
        scatter_dimension=0,
        tiled=True,
    ).reshape(span_size)
    total_squares = lax.psum(jnp.sum(span_total * span_total), ("dp", "pipe"))
    grad_norm = jnp.sqrt(total_squares)
    factor = jnp.minimum(1.0, CLIP_NORM / grad_norm)
    clipped = span_total * factor
    matrix = clipped.reshape(span_size // 128, 128)
    gram_old = gram_stats[0]
    basis_old = eigen_basis[0]
    gram_new = DECAY_STATS * gram_old + (1.0 - DECAY_STATS) * jnp.dot(
        matrix.T, matrix, precision=HIGH
    )
    product = jnp.dot(gram_new, basis_old, precision=HIGH)
    rotation = product / jnp.sqrt(jnp.sum(product * product))
    for repeat in range(NS_STEPS):
        square = jnp.dot(rotation.T, rotation, precision=HIGH)
        rotation = 1.5 * rotation - 0.5 * jnp.dot(rotation, square, precision=HIGH)
    moment_old = moment.reshape(span_size // 128, 128)
    initial = jnp.dot(moment_old, basis_old.T, precision=HIGH)
    blended = DECAY_FIRST * initial + (1.0 - DECAY_FIRST) * matrix
    moment_new = jnp.dot(blended, rotation, precision=HIGH)
    rotated = jnp.dot(matrix, rotation, precision=HIGH)
    second_new = (
        DECAY_SECOND * second.reshape(span_size // 128, 128)
        + (1.0 - DECAY_SECOND) * rotated * rotated
    )
    correction = math.sqrt(1.0 - DECAY_SECOND**STEP) / (1.0 - DECAY_FIRST**STEP)
    direction = (
        jnp.dot(moment_new / (jnp.sqrt(second_new) + ADAM_EPS), rotation.T, precision=HIGH)
        * correction
    )
    weights = params.reshape(span_size // 128, 128)
    params_new = weights - LEARN_RATE * (direction + WEIGHT_DECAY * weights)
    return (
        segment_teach[None],
        segment_stud[None],
        teach_grad[None],
        stud_grad[None],
        stats[None, :, None],
        grad_norm,
        clipped.reshape(1, span_size),
        moment_new.reshape(1, span_size),
        second_new.reshape(1, span_size),
        params_new.reshape(1, span_size),
        gram_new[None],
        rotation[None],
    )


MESH = pl.DeviceIdType.MESH
LOW = jnp.bfloat16
FULL = jnp.float32
TILE = 256
WINDOW = 20
STRIDE = 19
VEC_TILE = (152, 32, 104, 32)
USED_TILES = (153, 33, 105, 33)
FRONT_WIDE = 88
SMALL_ROWS = 1056
ROWS = 120
PADDED = 128
TEACH_ROWS = 72


def any_spec():
    return pl.BlockSpec(memory_space=pl.ANY)


def smem_spec():
    return pl.BlockSpec(memory_space=pltpu.SMEM)


def vmem_spec():
    return pl.BlockSpec(memory_space=pltpu.VMEM)


def tile_forms(section, tile):
    even = lax.rem(section, 2) == 0
    vector = jnp.where(section == 0, 152, jnp.where(section == 2, 104, 32))
    narrow_end = jnp.where(section == 0, FRONT_WIDE, jnp.where(section == 2, 104, 0))
    narrow = even & (tile < narrow_end)
    plain = tile == vector
    return narrow, plain


def prepare_kernel(owners, params, big, small, ids, flat, sem):
    block, section = owners[0, lax.axis_index("dp")], lax.axis_index("pipe")

    @pl.loop(0, WINDOW)
    def _(r):
        flat[pl.ds(TILE * r, TILE)] = jnp.zeros((TILE, 128), FULL)

    copy = pltpu.make_async_copy(params.at[:, 0, :], flat.at[pl.ds(6 * block, params.shape[0])], sem)
    copy.start()

    @pl.loop(0, small.shape[0])
    def _(r):
        small[r] = jnp.zeros((TILE, 128), LOW)

    lane = lax.broadcasted_iota(jnp.int32, (8, 128), 1)
    row = jnp.zeros((8, 128), jnp.int32)
    for j in range(8):
        row = jnp.where(lane == j, owners[0, j], row)
    ids[...] = row
    copy.wait()

    @pl.loop(0, WINDOW)
    def _(r):
        tile = STRIDE * block + r
        narrow, plain = tile_forms(section, tile)
        base = TILE * r

        @pl.when(narrow)
        def _():
            for j in range(4):
                big[r, 64 * j : 64 * j + 64, :] = flat[pl.ds(base + j, 64, 4), :].astype(LOW)

        @pl.when(plain)
        def _():
            big[r] = flat[pl.ds(base, TILE), :].astype(LOW)

        @pl.when(jnp.logical_not(narrow | plain))
        def _():
            for j in range(16):
                big[r, 16 * j : 16 * j + 16, :] = flat[pl.ds(base + j, 16, 16), :].astype(LOW)

        @pl.when(tile < small.shape[0])
        def _():
            small[tile] = big[r]


def prepare(owners, params):
    return pl.pallas_call(
        prepare_kernel,
        name="prepare",
        out_shape=(
            jax.ShapeDtypeStruct((WINDOW, TILE, 128), LOW),
            jax.ShapeDtypeStruct((USED_TILES[1], TILE, 128), LOW),
            jax.ShapeDtypeStruct((8, 128), jnp.int32),
        ),
        in_specs=[smem_spec(), any_spec()],
        out_specs=(vmem_spec(),) * 3,
        scratch_shapes=[pltpu.VMEM((WINDOW * TILE, 128), FULL), pltpu.SemaphoreType.DMA],
        compiler_params=pltpu.CompilerParams(vmem_limit_bytes=60 << 20),
    )(owners, params.reshape(-1, 1, 128))


class Place:
    def __init__(self):
        self.dp = lax.axis_index("dp")
        self.pipe = lax.axis_index("pipe")
        self.x, self.core = self.pipe // 2, self.pipe % 2
        self.z, self.y = self.dp // 2, self.dp % 2

    def device(self, x=None, core=None, z=None, y=None):
        x = self.x if x is None else x
        core = self.core if core is None else core
        z = self.z if z is None else z
        y = self.y if y is None else y
        return {"dp": 2 * z + y, "pipe": 2 * x + core}

    def enter(self):
        barrier = pltpu.get_barrier_semaphore()
        for step in range(1, 8):
            other = lax.rem(self.dp + step, 8)
            pl.semaphore_signal(
                barrier, inc=1, device_id={"dp": other, "pipe": self.pipe}, device_id_type=MESH
            )
        for step in range(1, 4):
            other = lax.rem(self.pipe + step, 4)
            pl.semaphore_signal(
                barrier, inc=1, device_id={"dp": self.dp, "pipe": other}, device_id_type=MESH
            )
        pl.semaphore_wait(barrier, 10)


def remote(src, dst, send, recv, target):
    return pltpu.make_async_remote_copy(
        src_ref=src, dst_ref=dst, send_sem=send, recv_sem=recv, device_id=target, device_id_type=MESH
    )


BIG_HALF = WINDOW * TILE // 2
SMALL_HALF = SMALL_ROWS // 2
BULK_CUT = 992
LIGHT_CUT = 256
BACK_CUT = 1280
GATHER_ORDER = (
    "EY", "Z1", "EC0", "EC1", "S0", "Z2", "Z3", "EC2", "EC3", "L0", "S1", "D0", "L1", "S2", "D1",
    "S3", "L2", "M1", "D2", "M2", "D3", "M3",
)
REDUCE_ORDER = (
    "A0", "A1", "A2", "A3", "L0", "L1", "B0", "L2", "L3", "LS", "B1", "LE", "B2", "O0", "E0", "O1",
    "I0", "T1", "T2", "E1", "B3", "O2", "I1", "E2", "G", "T3", "I2", "O3",
)


def gather_kernel(big, small, ids, all_big, all_small, table, early, chunk, rising, falling,
                  early_send, early_recv, eu_send, eu_recv, ed_send, ed_recv,
                  z_send, z_recv, x_send, x_recv, y_send, y_recv, dx_send, dx_recv, dy_send, dy_recv,
                  s_send, s_recv, first_send, first_recv, own_sem, id_send, id_recv, lz_send, lz_recv):
    me = Place()
    me.enter()
    x, y, z, core = me.x, me.y, me.z, me.core
    up, down = me.device(z=z + 1), me.device(z=z - 1)
    x_side, y_side, sibling = me.device(x=1 - x), me.device(y=1 - y), me.device(core=1 - core)

    class Stream:
        def __init__(self, n, out, cut):
            self.n, self.out, self.cut, self.rows = n, out, cut, out.shape[3]

        def block(self, xo, origin, yo):
            return self.out.at[xo, 2 * origin + yo, core]

        def move_x(self, origin):
            block = self.block(x, origin, y)
            return remote(block, block, x_send.at[self.n, origin], x_recv.at[self.n, origin], x_side)

        def move_y(self, origin):
            block = self.block(x, origin, y)
            return remote(block, block, y_send.at[self.n, origin], y_recv.at[self.n, origin], y_side)

        def share(self, xo, origin, yo):
            block = self.block(xo, origin, yo)
            at = 8 * xo + 2 * origin + yo
            return remote(block, block, s_send.at[self.n, at], s_recv.at[self.n, at], sibling)

        def move_z(self, origin, target, way):
            block = self.block(x, origin, y)
            return remote(block, block, z_send.at[self.n, way, origin], z_recv.at[self.n, origin], target)

        def half_x(self, origin, xo, yo):
            part = self.out.at[xo, 2 * origin + yo, core, pl.ds(self.cut, self.rows - self.cut)]
            return remote(part, part, dx_send.at[self.n, origin], dx_recv.at[self.n, origin], x_side)

        def half_y(self, origin, xo, yo):
            part = self.out.at[xo, 2 * origin + yo, core, pl.ds(0, self.cut)]
            return remote(part, part, dy_send.at[self.n, origin], dy_recv.at[self.n, origin], y_side)

        def spread(self, origin):
            self.move_x(origin).start()
            self.move_y(origin).start()
            self.share(x, origin, y).start()

        def from_sides(self, origin):
            self.move_x(origin).wait_recv()
            self.half_y(origin, 1 - x, y).start()
            self.share(1 - x, origin, y).start()
            self.move_y(origin).wait_recv()
            self.half_x(origin, x, 1 - y).start()
            self.share(x, origin, 1 - y).start()

        def from_diagonal(self, origin):
            self.half_x(origin, 1 - x, 1 - y).wait_recv()
            self.half_y(origin, 1 - x, 1 - y).wait_recv()
            self.share(1 - x, origin, 1 - y).start()

        def each(self, step, action):
            if step == 0:
                action(z)
            else:
                pl.when(z >= step)(lambda: action(z - step))
                pl.when(z + step <= 3)(lambda: action(z + step))

        def begin(self):
            pl.when(z < 3)(lambda: self.move_z(z, up, 0).start())
            pl.when(z > 0)(lambda: self.move_z(z, down, 1).start())
            self.spread(z)

        def from_z(self, k):
            @pl.when(z >= k)
            def _():
                self.move_z(z - k, up, 0).wait_recv()
                pl.when(z < 3)(lambda: self.move_z(z - k, up, 0).start())
                self.spread(z - k)

            @pl.when(z + k <= 3)
            def _():
                self.move_z(z + k, down, 1).wait_recv()
                pl.when(z > 0)(lambda: self.move_z(z + k, down, 1).start())
                self.spread(z + k)

        def close(self):
            for origin in range(4):
                self.move_x(origin).wait_send()
                self.move_y(origin).wait_send()
                self.half_x(origin, x, 1 - y).wait_send()
                self.half_y(origin, 1 - x, y).wait_send()
                pl.when((z < 3) & (origin <= z))(lambda: self.move_z(origin, up, 0).wait_send())
                pl.when((z > 0) & (origin >= z))(lambda: self.move_z(origin, down, 1).wait_send())
            self.close_shares()

        def close_shares(self):
            for origin in range(4):
                for xo in range(2):
                    for yo in range(2):
                        self.share(xo, origin, yo).wait_send()
                        theirs = self.out.at[xo, 2 * origin + yo, 1 - core]
                        at = 8 * xo + 2 * origin + yo
                        remote(theirs, theirs, s_send.at[self.n, at], s_recv.at[self.n, at], sibling).wait_recv()

    class Late(Stream):
        def column_z(self, xo, origin, yo, target, way):
            block = self.block(xo, origin, yo)
            at = 2 * xo + yo
            return remote(
                block, block, lz_send.at[way, at, origin], lz_recv.at[at, origin], target
            )

        def leave(self, xo, yo):
            pl.when(z < 3)(lambda: self.column_z(xo, z, yo, up, 0).start())
            pl.when(z > 0)(lambda: self.column_z(xo, z, yo, down, 1).start())
            self.share(xo, z, yo).start()

        def step(self, k):
            if k == 0:
                self.move_x(z).start()
                self.move_y(z).start()
                self.leave(x, y)
            elif k == 1:
                self.move_x(z).wait_recv()
                self.half_y(z, 1 - x, y).start()
                self.leave(1 - x, y)
                self.move_y(z).wait_recv()
                self.half_x(z, x, 1 - y).start()
                self.leave(x, 1 - y)
            elif k == 2:
                self.half_x(z, 1 - x, 1 - y).wait_recv()
                self.half_y(z, 1 - x, 1 - y).wait_recv()
                self.leave(1 - x, 1 - y)
            else:
                gap = k - 2

                @pl.when(z >= gap)
                def _():
                    for xo, yo in columns:
                        self.column_z(xo, z - gap, yo, up, 0).wait_recv()
                        pl.when(z < 3)(lambda: self.column_z(xo, z - gap, yo, up, 0).start())
                        self.share(xo, z - gap, yo).start()

                @pl.when(z + gap <= 3)
                def _():
                    for xo, yo in columns:
                        self.column_z(xo, z + gap, yo, down, 1).wait_recv()
                        pl.when(z > 0)(lambda: self.column_z(xo, z + gap, yo, down, 1).start())
                        self.share(xo, z + gap, yo).start()

        def close(self):
            self.move_x(z).wait_send()
            self.move_y(z).wait_send()
            self.half_x(z, x, 1 - y).wait_send()
            self.half_y(z, 1 - x, y).wait_send()
            for origin in range(4):
                for xo, yo in columns:
                    pl.when((z < 3) & (origin <= z))(
                        lambda: self.column_z(xo, origin, yo, up, 0).wait_send())
                    pl.when((z > 0) & (origin >= z))(
                        lambda: self.column_z(xo, origin, yo, down, 1).wait_send())
            self.close_shares()

    columns = ((x, y), (1 - x, y), (x, 1 - y), (1 - x, 1 - y))
    bulk = Stream(0, all_big, BULK_CUT)
    light = Late(1, all_small, LIGHT_CUT)

    order = [
        jnp.where(z < 2, 3, 0),
        jnp.where(z == 0, 2, jnp.where(z == 1, 0, jnp.where(z == 2, 3, 1))),
        jnp.where(z == 0, 1, jnp.where(z == 1, 2, jnp.where(z == 2, 1, 2))),
        z,
    ]

    def cross(k):
        return remote(small.at[2 * order[k] + (1 - y)], early.at[k], early_send.at[k], early_recv.at[k], y_side)

    def own_early(k):
        return pltpu.make_async_copy(small.at[2 * order[k] + y], chunk.at[k], own_sem.at[3 + k])

    def rise(k):
        slot = order[k] - 1
        return remote(chunk.at[k], rising.at[slot], eu_send.at[slot], eu_recv.at[slot], up)

    def fall(k):
        slot = order[k]
        return remote(chunk.at[k], falling.at[slot], ed_send.at[slot], ed_recv.at[slot], down)

    def merge(k, ref, slot):
        @pl.loop(0, 3)
        def _(i):
            part = pl.ds(pl.multiple_of(352 * i, 16), 352)
            chunk[k, part, :] = (chunk[k, part, :].astype(FULL) + ref[slot, part, :].astype(FULL)).astype(LOW)

    big_half = all_big.at[x, me.dp, 1]
    big_first = remote(big.at[pl.ds(BIG_HALF, BIG_HALF)], big_half, first_send.at[0], first_recv.at[0], sibling)
    small_half = all_small.at[x, me.dp, 0]
    small_first = remote(
        chunk.at[3, pl.ds(0, SMALL_HALF)], small_half, first_send.at[1], first_recv.at[1], sibling)

    def early_cross():
        @pl.when(core == 1)
        def _():
            for k in range(4):
                own_early(k).wait()
                cross(k).wait_recv()
                merge(k, early, k)

    def early_chain(k):
        @pl.when(core == 1)
        def _():
            if k < 3:

                @pl.when(order[k] > z)
                def _():
                    @pl.when(z > 0)
                    def _():
                        rise(k).wait_recv()
                        merge(k, rising, order[k] - 1)

                    rise(k).start()

                @pl.when(order[k] < z)
                def _():
                    @pl.when(z < 3)
                    def _():
                        fall(k).wait_recv()
                        merge(k, falling, order[k])

                    fall(k).start()

            else:

                @pl.when(z > 0)
                def _():
                    rise(k).wait_recv()
                    merge(k, rising, z - 1)

                @pl.when(z < 3)
                def _():
                    fall(k).wait_recv()
                    merge(k, falling, z)

                small_first.start()
                copy = pltpu.make_async_copy(
                    chunk.at[3, pl.ds(SMALL_HALF, SMALL_HALF)], all_small.at[x, me.dp, 1], own_sem.at[0])
                copy.start()
                copy.wait()

    def light_begin():
        @pl.when(core == 0)
        def _():
            small_first.wait_recv()

        light.step(0)

    @pl.when(core == 0)
    def _():
        big_first.start()
        copy = pltpu.make_async_copy(big.at[pl.ds(0, BIG_HALF)], all_big.at[x, me.dp, 0], own_sem.at[0])
        copy.start()
        copy.wait()

    @pl.when(core == 1)
    def _():
        for k in range(4):
            cross(k).start()
            own_early(k).start()
        big_first.wait_recv()

    bulk.begin()
    row = pltpu.make_async_copy(ids, table.at[me.pipe], own_sem.at[2])
    row.start()
    for step in range(1, 4):
        remote(
            ids, table.at[me.pipe], id_send.at[step], id_recv.at[step],
            {"dp": me.dp, "pipe": lax.rem(me.pipe + step, 4)},
        ).start()

    actions = {"EY": early_cross, "L0": light_begin}
    for k in range(4):
        actions["EC%d" % k] = functools.partial(early_chain, k)
        actions["S%d" % k] = functools.partial(bulk.each, k, bulk.from_sides)
        actions["D%d" % k] = functools.partial(bulk.each, k, bulk.from_diagonal)
        if k:
            actions["Z%d" % k] = functools.partial(bulk.from_z, k)
            actions["M%d" % k] = functools.partial(light.step, k + 2)
            if k < 3:
                actions["L%d" % k] = functools.partial(light.step, k)
    for event in GATHER_ORDER:
        actions[event]()
    bulk.close()
    light.close()
    row.wait()
    for step in range(1, 4):
        here = lax.rem(me.pipe + 4 - step, 4)
        move = remote(
            ids, table.at[here], id_send.at[step], id_recv.at[step],
            {"dp": me.dp, "pipe": lax.rem(me.pipe + step, 4)},
        )
        move.wait_recv()
        move.wait_send()

    @pl.when(core == 0)
    def _():
        big_first.wait_send()

    @pl.when(core == 1)
    def _():
        small_first.wait_send()
        for k in range(4):
            cross(k).wait_send()
        for k in range(3):
            pl.when(order[k] > z)(lambda: rise(k).wait_send())
            pl.when(order[k] < z)(lambda: fall(k).wait_send())


def gather_all(big, small, ids):
    sem = pltpu.SemaphoreType.DMA
    return pl.pallas_call(
        gather_kernel,
        name="gather_all",
        out_shape=(
            jax.ShapeDtypeStruct((2, 8, 2, BIG_HALF, 128), LOW),
            jax.ShapeDtypeStruct((2, 8, 2, SMALL_HALF, 128), LOW),
            jax.ShapeDtypeStruct((4, 8, 128), jnp.int32),
        ),
        in_specs=[any_spec()] * 3,
        out_specs=(any_spec(),) * 3,
        scratch_shapes=[
            pltpu.VMEM((4, SMALL_ROWS, 128), LOW), pltpu.VMEM((4, SMALL_ROWS, 128), LOW),
            pltpu.VMEM((3, SMALL_ROWS, 128), LOW), pltpu.VMEM((3, SMALL_ROWS, 128), LOW),
            sem((4,)), sem((4,)), sem((3,)), sem((3,)), sem((3,)), sem((3,)),
            sem((2, 2, 4)), sem((2, 4)),
            sem((2, 4)), sem((2, 4)), sem((2, 4)), sem((2, 4)),
            sem((2, 4)), sem((2, 4)), sem((2, 4)), sem((2, 4)),
            sem((2, 16)), sem((2, 16)),
            sem((2,)), sem((2,)), sem((7,)), sem((4,)), sem((4,)), sem((2, 4, 4)), sem((4, 4)),
        ],
        compiler_params=pltpu.CompilerParams(
            collective_id=0, has_side_effects=True, vmem_limit_bytes=60 << 20
        ),
    )(big.reshape(WINDOW * TILE, 128), small.reshape(8, SMALL_ROWS, 128), ids)


def soft(value):
    return jnp.maximum(value, 0.0) + jnp.log1p(jnp.exp(-jnp.abs(value)))


def gate_of(value):
    small = jnp.exp(-jnp.abs(value))
    share = 1.0 / (1.0 + small)
    return jnp.where(value >= 0, share, small * share)


def standardize(z):
    count = z.shape[0]
    centre = jnp.sum(z, axis=0, keepdims=True) / count
    away = z - centre
    spread = jnp.sum(away * away, axis=0, keepdims=True) / count
    inverse = lax.rsqrt(spread + NORM_EPS)
    return away * inverse, centre, spread, inverse


def unstandardize(grad, standard, gain, inverse):
    count = grad.shape[0]
    grad_sum = jnp.sum(grad, axis=0, keepdims=True)
    grad_dot = jnp.sum(grad * standard, axis=0, keepdims=True)
    result = gain * inverse * (grad - grad_sum / count - standard * (grad_dot / count))
    return result, grad_dot, grad_sum


def pad_low(value):
    zeros = jnp.zeros((PADDED - ROWS, value.shape[1]), FULL)
    return jnp.concatenate([value, zeros], axis=0).astype(LOW)


def mul(a, b):
    return jnp.dot(a, b, preferred_element_type=FULL)


def mul_t(a, b):
    return lax.dot_general(a, b, (((1,), (1,)), ((), ())), preferred_element_type=FULL)


def narrow_part(ref, start, count, blocks=range(4)):
    return jnp.concatenate(
        [ref[pl.ds(start, count), 64 * j : 64 * j + 64, :].reshape(64 * count, 128) for j in blocks],
        axis=1,
    )


def put_narrow(ref, start, count, value):
    for j in range(4):
        ref[pl.ds(start, count), 64 * j : 64 * j + 64, :] = (
            value[:, 128 * j : 128 * j + 128].astype(LOW).reshape(count, 64, 128)
        )


def wide_part(ref, start, count, c):
    return jnp.concatenate(
        [
            ref[start : start + count, 32 * c + 16 * h : 32 * c + 16 * h + 16, :].reshape(
                16 * count, 128
            )
            for h in range(2)
        ],
        axis=1,
    )


def put_wide(ref, start, count, c, value):
    for h in range(2):
        ref[start : start + count, 32 * c + 16 * h : 32 * c + 16 * h + 16, :] = (
            value[:, 128 * h : 128 * h + 128].astype(LOW).reshape(count, 16, 128)
        )


def chunks(count):
    def run(body):
        for c in range(count):
            body(c)

    return run


def step_kernel(table, gates, teach_ids, stud_ids, all_big, all_small, x, targets, grid,
                wide0, wide1, final, stats, grad_x, out_big, out_small,
                w0, w1, w2, w3, edges, vec, grad_vec, raw,
                std_a, std_b, std_p, std_1, std_c, std_d, hidden, cols0, cols2,
                nar0, nar2, turned, relay, dz_a, dz_n, acc, acc_x, grad_h,
                wanted, inv, in_sem, edge_sem, out_sem):
    rank = lax.axis_index("pipe")
    gate = gates[rank].astype(FULL)
    for group in range(2):
        for j in range(8):
            inv[8 * group + table[2 * group, 0, j]] = j
    picks = [teach_ids[k, rank] for k in range(2)] + [stud_ids[rank, k] for k in range(3)]
    rows = [
        pltpu.make_async_copy(targets.at[pl.ds(pick, 1)], wanted.at[pl.ds(k, 1)], edge_sem.at[12 + k])
        for k, pick in enumerate(picks)
    ]
    for fetched in rows:
        fetched.start()
    weights = (w0, w1, w2, w3)
    loads = {0: [], 1: [], 2: [], 3: []}
    for group, weight, blocks in ((0, w0, 8), (1, w2, 6)):
        for b in range(blocks):
            first, here = 19 * b, inv[8 * group + b]
            at = 8 * group + b
            loads[2 * group].append(pltpu.make_async_copy(
                all_big.at[group, here, 0], weight.at[pl.ds(first, 10)], in_sem.at[0, at]))
            if first + 10 < USED_TILES[2 * group]:
                count = 10 if b == 7 else 9
                loads[2 * group].append(pltpu.make_async_copy(
                    all_big.at[group, here, 1, pl.ds(0, count)], weight.at[pl.ds(first + 10, count)],
                    in_sem.at[1, at]))
            if b < blocks - 1:
                at = 7 * group + b
                loads[2 * group].append(pltpu.make_async_copy(
                    all_big.at[group, here, 1, pl.ds(9, 1)], edges.at[pl.ds(at, 1)], edge_sem.at[at]))
    loads[1].append(pltpu.make_async_copy(all_small.at[0], w1, in_sem.at[0, 14]))
    loads[3].append(pltpu.make_async_copy(all_small.at[1], w3, in_sem.at[0, 15]))
    for section in range(4):
        for load in loads[section]:
            load.start()

    raw[...] = jnp.zeros_like(raw)
    grad_vec[...] = jnp.zeros_like(grad_vec)

    def merge_edge(ref, tile, at):
        ref[tile] = (ref[tile].astype(FULL) + edges[at].astype(FULL)).astype(LOW)

    def settle(section, blocks=None):
        if section == 0:
            for b in blocks:
                for load in loads[0][3 * b : 3 * b + 3]:
                    load.wait()
            if 7 in blocks:
                vec[0] = w0[VEC_TILE[0], 0:48, :].astype(FULL)
            else:
                for b in range(7):
                    merge_edge(w0, 19 * b + 19, b)
            return
        for load in loads[section]:
            load.wait()
        if section == 2:
            for b in range(5):
                merge_edge(w2, 19 * b + 19, 7 + b)
        vec[section] = weights[section][VEC_TILE[section], 0:48, :].astype(FULL)

    def row(section, start):
        return jnp.concatenate(
            [vec[section, pl.ds(start + h, 1), :] for h in range(2)], axis=1
        )

    def put_row(section, start, value):
        for h in range(2):
            grad_vec[section, pl.ds(start + h, 1), :] = value[:, 128 * h : 128 * h + 128]

    def put_stats(section, column, centre, spread):
        raw[2 * section : 2 * section + 1, pl.ds(column, 256)] = centre
        raw[2 * section + 1 : 2 * section + 2, pl.ds(column, 256)] = spread

    def inverse_of(section, column):
        return lax.rsqrt(raw[2 * section + 1 : 2 * section + 2, pl.ds(column, 256)] + NORM_EPS)

    def lanes(c):
        return slice(256 * c, 256 * c + 256)

    at_row, at_col, side = grid[0], grid[1], grid[2]

    def masked(value, dr, dc):
        ok = (at_row + dr >= 0) & (at_row + dr < side) & (at_col + dc >= 0) & (at_col + dc < side)
        return jnp.concatenate(
            [jnp.where(ok, value[:, 128 * j : 128 * j + 128], 0.0) for j in range(4)], axis=1
        )

    def rolled(value, sign, dr, dc):
        parts = []
        for start, end, width in ((0, TEACH_ROWS, 6), (TEACH_ROWS, ROWS, 4)):
            by = (sign * (dr * width + dc)) % (end - start)
            part = value[start:end]
            parts.append(part if by == 0 else pltpu.roll(part, by, 0))
        return jnp.concatenate(parts, axis=0)

    def taps(stride):
        for t in range(9):
            r, q = t // 3, t % 3
            if stride == 1:
                yield t, 0, r - 1, q - 1
            else:
                phase = 2 * (1 if r != 1 else 0) + (1 if q != 1 else 0)
                yield t, phase, -1 if r == 0 else 0, -1 if q == 0 else 0

    settle(0, (0, 7))
    whole_x = x[...].reshape(4 * PADDED, C_IN)
    for c in range(2):
        z = mul(whole_x, narrow_part(w0, 0, 16, (2 * c, 2 * c + 1)))
        z = jnp.concatenate([z[PADDED * p : PADDED * p + ROWS] for p in range(4)], axis=0)
        standard, centre, spread, _ = standardize(z)
        put_stats(0, 256 * c, centre, spread)
        std_a[:, 256 * c : 256 * c + 256] = standard
        hidden[:, 256 * c : 256 * c + 256] = (
            soft(row(0, 2 * c) * standard + row(0, 4 + 2 * c)).astype(LOW).astype(FULL)
        )

    for t, phase, dr, dc in taps(2):
        cols0[t] = pad_low(masked(rolled(hidden[ROWS * phase : ROWS * phase + ROWS, :], -1, dr, dc), dr, dc))
    acc[...] = jnp.zeros_like(acc)
    settle(0, (1, 2, 3, 4, 5, 6))

    @chunks(9)
    def _(t):
        acc[...] += mul(cols0[t], narrow_part(w0, 16 + 8 * t, 8))

    def middle(section, std, nar):
        for c in range(2):
            at = slice(256 * c, 256 * c + 256)
            standard, centre, spread, _ = standardize(acc[0:ROWS, at])
            put_stats(section, MID + 256 * c, centre, spread)
            std[:, at] = standard
            nar[:, at] = pad_low(soft(row(section, 8 + 2 * c) * standard + row(section, 12 + 2 * c)))

    middle(0, std_b, nar0)
    acc[...] = jnp.zeros_like(acc)
    settle(1)
    settle(2)

    @chunks(8)
    def _(c):
        at = lanes(c)
        standard, centre, spread, _ = standardize(mul(x[0], wide_part(w0, FRONT_WIDE, 64, c))[0:ROWS])
        put_stats(0, 2 * MID + 256 * c, centre, spread)
        std_p[:, at] = standard
        low = pad_low(row(0, 16 + 2 * c) * standard + row(0, 32 + 2 * c))
        wide0[:, at] = low
        standard, centre, spread, _ = standardize(mul(nar0[...], wide_part(w1, 0, 32, c))[0:ROWS])
        put_stats(1, 256 * c, centre, spread)
        std_1[:, at] = standard
        pre = low.astype(FULL)[0:ROWS] + row(1, 2 * c) * standard + row(1, 16 + 2 * c)
        low = pad_low(soft(pre))
        wide1[:, at] = low
        acc[...] += mul(low, narrow_part(w2, 4 * c, 4))

    for c in range(2):
        at = slice(256 * c, 256 * c + 256)
        standard, centre, spread, _ = standardize(acc[0:ROWS, at])
        put_stats(2, 256 * c, centre, spread)
        std_c[:, at] = standard
        hidden[0:ROWS, at] = soft(row(2, 2 * c) * standard + row(2, 4 + 2 * c)).astype(LOW).astype(FULL)
    for t, phase, dr, dc in taps(1):
        cols2[t] = pad_low(masked(rolled(hidden[0:ROWS, :], -1, dr, dc), dr, dc))
    acc[...] = jnp.zeros_like(acc)

    @chunks(9)
    def _(t):
        acc[...] += mul(cols2[t], narrow_part(w2, 32 + 8 * t, 8))

    middle(2, std_d, nar2)

    turned[...] = nar2[...].T
    acc[...] = jnp.zeros_like(acc)
    settle(3)
    for fetched in rows:
        fetched.wait()

    def spread_rows(values):
        head = lax.broadcasted_iota(jnp.int32, (8, 256), 0) < 4
        first, second = (jnp.broadcast_to(value, (8, 256)) for value in values[0:2])
        parts = [jnp.broadcast_to(values[0], (32, 256)), jnp.where(head, first, second)]
        parts.append(jnp.broadcast_to(values[1], (32, 256)))
        parts.extend(jnp.broadcast_to(value, (16, 256)) for value in values[2:5])
        return jnp.concatenate(parts, axis=0)

    def crop_sums(value):
        head = lax.broadcasted_iota(jnp.int32, (8, 256), 0) < 4
        between = value[32:40]

        def total(part):
            return jnp.sum(part, axis=0, keepdims=True)

        return [
            total(value[0:32]) + total(jnp.where(head, between, 0.0)),
            total(value[40:72]) + total(jnp.where(head, 0.0, between)),
            total(value[72:88]),
            total(value[88:104]),
            total(value[104:120]),
        ]

    @chunks(8)
    def _(c):
        at = lanes(c)
        weight = wide_part(w3, 0, 32, c)
        standard, centre, spread, inverse = standardize(mul(nar2[...], weight)[0:ROWS])
        put_stats(3, 256 * c, centre, spread)
        gain = row(3, 2 * c)
        before = wide1[:, at].astype(FULL)[0:ROWS]
        pre = before + gain * standard + row(3, 16 + 2 * c)
        ending = jnp.where(gate > 0, soft(pre), before)
        final[:, at] = pad_low(ending)
        square = ending * ending
        factors = []
        for crop, total in enumerate(crop_sums(square * ending)):
            mean = total / (36.0 if crop < 2 else 16.0) + POOL_EPS
            factors.append(jnp.exp(jnp.log(mean) * (-2.0 / 3.0)) * wanted[crop : crop + 1, at])
        cotangent = spread_rows(factors) * square
        grad_pre = cotangent * gate_of(pre) * gate
        relay[:, at] = pad_low(grad_pre + cotangent * (1.0 - gate))
        result, grad_gain, grad_bias = unstandardize(grad_pre, standard, gain, inverse)
        put_row(3, 2 * c, grad_gain)
        put_row(3, 16 + 2 * c, grad_bias)
        low = pad_low(result)
        acc[...] += mul_t(low, weight)
        put_wide(w3, 0, 32, c, mul(turned[...], low))

    def flush(section):
        weights[section][VEC_TILE[section]] = grad_vec[section].astype(LOW)

    flush(3)
    stores = [pltpu.make_async_copy(w3, out_small.at[1], out_sem.at[15])]
    stores[-1].start()

    def middle_back(section, std):
        for c in range(2):
            at = slice(256 * c, 256 * c + 256)
            gain, bias = row(section, 8 + 2 * c), row(section, 12 + 2 * c)
            grad = acc[0:ROWS, at].astype(LOW).astype(FULL) * gate_of(gain * std[:, at] + bias)
            result, grad_gain, grad_bias = unstandardize(
                grad, std[:, at], gain, inverse_of(section, MID + 256 * c)
            )
            put_row(section, 8 + 2 * c, grad_gain)
            put_row(section, 12 + 2 * c, grad_bias)
            dz_n[:, at] = pad_low(result)

    def taps_back(weight, start, cols, stride, phases):
        grad_h[0 : ROWS * phases, :] = jnp.zeros((ROWS * phases, MID), FULL)
        for t, phase, dr, dc in taps(stride):
            part = mul_t(dz_n[...], narrow_part(weight, start + 8 * t, 8))[0:ROWS]
            at = slice(ROWS * phase, ROWS * phase + ROWS)
            grad_h[at, :] += rolled(masked(part, dr, dc), 1, dr, dc)
            put_narrow(weight, start + 8 * t, 8, mul(cols[t].T, dz_n[...]))

    middle_back(2, std_d)
    taps_back(w2, 32, cols2, 1, 1)
    for c in range(2):
        at = slice(256 * c, 256 * c + 256)
        gain, bias = row(2, 2 * c), row(2, 4 + 2 * c)
        grad = grad_h[0:ROWS, at] * gate_of(gain * std_c[:, at] + bias)
        result, grad_gain, grad_bias = unstandardize(grad, std_c[:, at], gain, inverse_of(2, 256 * c))
        put_row(2, 2 * c, grad_gain)
        put_row(2, 4 + 2 * c, grad_bias)
        dz_n[:, at] = pad_low(result)
    turned[...] = nar0[...].T
    acc[...] = jnp.zeros_like(acc)
    acc_x[...] = jnp.zeros_like(acc_x)

    @chunks(8)
    def _(c):
        at = lanes(c)
        low = dz_n[...]
        grad = relay[:, at].astype(FULL) + mul_t(low, narrow_part(w2, 4 * c, 4))
        put_narrow(w2, 4 * c, 4, mul(wide1[:, at].T, low))
        grad = grad.astype(LOW).astype(FULL)[0:ROWS]
        gain = row(1, 2 * c)
        pre = wide0[:, at].astype(FULL)[0:ROWS] + gain * std_1[:, at] + row(1, 16 + 2 * c)
        grad = grad * gate_of(pre)
        result, grad_gain, grad_bias = unstandardize(
            grad, std_1[:, at], gain, inverse_of(1, 256 * c)
        )
        put_row(1, 2 * c, grad_gain)
        put_row(1, 16 + 2 * c, grad_bias)
        low = pad_low(result)
        acc[...] += mul_t(low, wide_part(w1, 0, 32, c))
        put_wide(w1, 0, 32, c, mul(turned[...], low))
        grad = grad.astype(LOW).astype(FULL)
        result, grad_gain, grad_bias = unstandardize(
            grad, std_p[:, at], row(0, 16 + 2 * c), inverse_of(0, 2 * MID + 256 * c)
        )
        put_row(0, 16 + 2 * c, grad_gain)
        put_row(0, 32 + 2 * c, grad_bias)
        low = pad_low(result)
        acc_x[...] += mul_t(low, wide_part(w0, FRONT_WIDE, 64, c))
        put_wide(w0, FRONT_WIDE, 64, c, mul(x[0].T, low))

    flush(1)
    flush(2)
    w2[105:115] = jnp.zeros((10, TILE, 128), LOW)
    stores.append(pltpu.make_async_copy(w1, out_small.at[0], out_sem.at[14]))
    stores[-1].start()
    for b in range(8):
        if b < 6:
            stores.append(pltpu.make_async_copy(
                w2.at[pl.ds(19 * b, 20)], out_big.at[1, inv[8 + b]], out_sem.at[8 + b]))
            stores[-1].start()
        else:
            for h in range(2):
                stores.append(pltpu.make_async_copy(
                    w2.at[pl.ds(105, 10)], out_big.at[1, inv[8 + b], pl.ds(10 * h, 10)],
                    out_sem.at[16 + 2 * (b - 6) + h]))
                stores[-1].start()

    def store_front(blocks):
        for b in blocks:
            stores.append(pltpu.make_async_copy(
                w0.at[pl.ds(19 * b, 20)], out_big.at[0, inv[b]], out_sem.at[b]))
            stores[-1].start()

    store_front((5, 6))
    middle_back(0, std_b)
    taps_back(w0, 16, cols0, 2, 4)
    store_front((1, 2, 3, 4))
    for c in range(2):
        at = slice(256 * c, 256 * c + 256)
        gain, bias = row(0, 2 * c), row(0, 4 + 2 * c)
        grad = grad_h[:, at] * gate_of(gain * std_a[:, at] + bias)
        result, grad_gain, grad_bias = unstandardize(grad, std_a[:, at], gain, inverse_of(0, 256 * c))
        put_row(0, 2 * c, grad_gain)
        put_row(0, 4 + 2 * c, grad_bias)
        for p in range(4):
            dz_a[PADDED * p : PADDED * p + PADDED, at] = pad_low(result[ROWS * p : ROWS * p + ROWS])

    @chunks(4)
    def _(c):
        at = lanes(c)
        low = dz_a[...]
        part = mul_t(low, narrow_part(w0, 4 * c, 4))
        grad_x[0, :, at] = (part[0:PADDED] + acc_x[:, at]).astype(LOW)
        for p in range(1, 4):
            grad_x[p, :, at] = part[PADDED * p : PADDED * p + PADDED].astype(LOW)
        turned_x = x[:, :, at].reshape(4 * PADDED, 256).T
        put_narrow(w0, 4 * c, 4, mul(turned_x, low))

    flush(0)
    store_front((0, 7))
    for section in range(4):
        part = raw[2 * section : 2 * section + 2]
        stats[section, 0:2] = part if section < 2 else part * gate
        stats[section, 2:8] = jnp.zeros((6, 2 * MID + C_OUT), FULL)
    for store in stores:
        store.wait()


def run_step(table, gates, teach_ids, stud_ids, all_big, all_small, phases, targets):
    spots = np.zeros((3, ROWS, 128), np.int32)
    for r in range(ROWS):
        width = 6 if r < TEACH_ROWS else 4
        at = r % 36 if r < TEACH_ROWS else (r - TEACH_ROWS) % 16
        spots[0, r], spots[1, r], spots[2, r] = at // width, at % width, width
    sem = pltpu.SemaphoreType.DMA
    wide = jax.ShapeDtypeStruct((PADDED, C_OUT), LOW)
    vm = pltpu.VMEM
    return pl.pallas_call(
        step_kernel,
        name="step",
        out_shape=(
            wide, wide, wide,
            jax.ShapeDtypeStruct((4, 8, 2 * MID + C_OUT), FULL),
            jax.ShapeDtypeStruct((4, PADDED, C_IN), LOW),
            jax.ShapeDtypeStruct((2, 8, WINDOW, TILE, 128), LOW),
            jax.ShapeDtypeStruct((2, USED_TILES[1], TILE, 128), LOW),
        ),
        in_specs=[smem_spec()] * 4 + [any_spec(), any_spec(), vmem_spec(), any_spec(), vmem_spec()],
        out_specs=(vmem_spec(),) * 5 + (any_spec(),) * 2,
        scratch_shapes=[
            vm((153, TILE, 128), LOW), vm((33, TILE, 128), LOW), vm((115, TILE, 128), LOW), vm((33, TILE, 128), LOW),
            vm((12, TILE, 128), LOW), vm((4, 48, 128), FULL), vm((4, TILE, 128), FULL),
            vm((8, 2 * MID + C_OUT), FULL),
            vm((4 * ROWS, MID), FULL), vm((ROWS, MID), FULL), vm((ROWS, C_OUT), FULL), vm((ROWS, C_OUT), FULL),
            vm((ROWS, MID), FULL), vm((ROWS, MID), FULL), vm((4 * ROWS, MID), FULL),
            vm((9, PADDED, MID), LOW), vm((9, PADDED, MID), LOW),
            vm((PADDED, MID), LOW), vm((PADDED, MID), LOW), vm((MID, PADDED), LOW),
            vm((PADDED, C_OUT), LOW), vm((4 * PADDED, MID), LOW), vm((PADDED, MID), LOW),
            vm((PADDED, MID), FULL), vm((PADDED, C_IN), FULL), vm((4 * ROWS, MID), FULL),
            vm((8, C_OUT), FULL), pltpu.SMEM((16,), jnp.int32),
            sem((2, 16)), sem((17,)), sem((20,)),
        ],
        compiler_params=pltpu.CompilerParams(vmem_limit_bytes=60 << 20),
    )(table, gates, teach_ids, stud_ids, all_big, all_small, phases, targets, jnp.asarray(spots))


def reduce_kernel(big, small, wide0, wide1, final, stats, table,
                  out_big, out_small, segments, out_stats, norm, factor,
                  got, halves_x, halves_y, from_x, from_y, from_low, from_high, stage, total,
                  l_got, l_stage, l_low, l_high, l_halves_x, l_halves_y, l_from_x, l_from_y, l_total,
                  late, late_half, owner_row, by_pipe, by_dp, mine, part_sum,
                  s_send, s_recv, hx_send, hx_recv, hy_send, hy_recv, x_send, x_recv, y_send, y_recv,
                  zu_send, zu_recv, zd_send, zd_recv, lu_send, lu_recv, ld_send, ld_recv,
                  stage_sem, l_stage_sem, out_sem, late_send, late_recv, join_send, join_recv,
                  seg_send, seg_recv, stat_send, stat_recv, p_send, p_recv, d_send, d_recv):
    me = Place()
    me.enter()
    x, y, z, core = me.x, me.y, me.z, me.core
    up, down = me.device(z=z + 1), me.device(z=z - 1)
    x_side, y_side, sibling = me.device(x=1 - x), me.device(y=1 - y), me.device(core=1 - core)
    order = [
        jnp.where(z < 2, 3, 0),
        jnp.where(z == 0, 2, jnp.where(z == 1, 0, jnp.where(z == 2, 3, 1))),
        jnp.where(z == 0, 1, jnp.where(z == 1, 2, jnp.where(z == 2, 1, 2))),
        z,
    ]
    columns = ((1 - x, 1 - y), (x, 1 - y), (1 - x, y), (x, y))
    groups = {"A": (0,), "B": (1, 2), "O": (3,)}
    sequence = [
        (group, int(event[1])) for event in REDUCE_ORDER for group in groups.get(event[0], ())
    ]
    l_sequence = [(group, k) for k in range(4) for group in range(4)]

    def all_of(copies, act):
        for copy in copies:
            act(copy)

    def over(start, count, piece):
        whole = count // 512
        if whole:

            @pl.loop(0, whole)
            def _(i):
                piece(pl.multiple_of(start + 512 * i, 16), 512)

        if count % 512:
            piece(start + 512 * whole, count % 512)

    def source(array, group, k, half):
        xo, yo = columns[group]
        return array.at[xo, 2 * order[k] + yo, half]

    def share(group, k):
        at = 4 * group + k
        return remote(source(big, group, k, 1 - core), got.at[at], s_send.at[0, at], s_recv.at[0, at], sibling)

    def l_share(group, k):
        at = 4 * group + k
        return remote(source(small, group, k, 1 - core), l_got.at[at], s_send.at[1, at], s_recv.at[1, at], sibling)

    def fetch(n):
        return pltpu.make_async_copy(source(big, *sequence[n], core), stage.at[n % 4], stage_sem.at[n % 4])

    def l_fetch(group, k):
        at = 4 * group + k
        return pltpu.make_async_copy(source(small, group, k, core), l_stage.at[at], l_stage_sem.at[at])

    def add(target, at, other, slot, start, count, extras):
        def piece(begin, size):
            part = pl.ds(begin, size)
            sums = target[at, part, :].astype(FULL) + other[slot, part, :].astype(FULL)
            for ref, k in extras:
                sums = sums + ref[k, pl.ds(begin - start, size), :].astype(FULL)
            target[at, part, :] = sums.astype(LOW)

        over(start, count, piece)

    def send_half_x(k):
        return remote(got.at[k, pl.ds(BACK_CUT, BIG_HALF - BACK_CUT)], halves_x.at[k],
                      hx_send.at[k], hx_recv.at[k], x_side)

    def send_half_y(k):
        return remote(got.at[k, pl.ds(0, BACK_CUT)], halves_y.at[k], hy_send.at[k], hy_recv.at[k], y_side)

    def send_y(k):
        return remote(got.at[4 + k], from_y.at[k], y_send.at[k], y_recv.at[k], y_side)

    def send_x(k):
        return remote(got.at[8 + k], from_x.at[k], x_send.at[k], x_recv.at[k], x_side)

    def send_up(at, zd):
        return remote(got.at[at], from_low.at[zd - 1], zu_send.at[zd - 1], zu_recv.at[zd - 1], up)

    def send_down(at, zd):
        return remote(got.at[at], from_high.at[zd], zd_send.at[zd], zd_recv.at[zd], down)

    def l_column(group):
        xo, yo = columns[group]
        return 2 * xo + yo

    def l_up(group, k):
        at, zd = l_column(group), order[k] - 1
        return remote(l_got.at[4 * group + k], l_low.at[at, zd], lu_send.at[at, zd], lu_recv.at[at, zd], up)

    def l_down(group, k):
        at, zd = l_column(group), order[k]
        return remote(l_got.at[4 * group + k], l_high.at[at, zd], ld_send.at[at, zd], ld_recv.at[at, zd], down)

    def l_half_x():
        return remote(l_got.at[3, pl.ds(LIGHT_CUT, SMALL_HALF - LIGHT_CUT)], l_halves_x,
                      hx_send.at[4], hx_recv.at[4], x_side)

    def l_half_y():
        return remote(l_got.at[3, pl.ds(0, LIGHT_CUT)], l_halves_y, hy_send.at[4], hy_recv.at[4], y_side)

    def l_send_y():
        return remote(l_got.at[7], l_from_y, y_send.at[4], y_recv.at[4], y_side)

    def l_send_x():
        return remote(l_got.at[11], l_from_x, x_send.at[4], x_recv.at[4], x_side)

    leaving = (wide0, wide1, wide1, final)

    def exchange(section):
        target = {"dp": me.dp, "pipe": section}
        yield remote(leaving[section], segments.at[me.pipe], seg_send.at[section], seg_recv.at[me.pipe], target)
        yield remote(stats.at[section], out_stats.at[me.pipe], stat_send.at[section], stat_recv.at[me.pipe], target)

    def keep(section):
        yield pltpu.make_async_copy(leaving[section], segments.at[me.pipe], seg_send.at[section])
        yield pltpu.make_async_copy(stats.at[section], out_stats.at[me.pipe], stat_send.at[section])

    def arriving(micro):
        target = {"dp": me.dp, "pipe": micro}
        yield remote(wide0, segments.at[micro], seg_send.at[micro], seg_recv.at[micro], target)
        yield remote(stats.at[0], out_stats.at[micro], stat_send.at[micro], stat_recv.at[micro], target)

    for n in range(16):
        share(*sequence[n]).start()
        if n == 3:
            for item in l_sequence:
                l_share(*item).start()
    for n in range(2):
        fetch(n).start()
    for group, k in l_sequence:
        l_fetch(group, k).start()
    row_copy = pltpu.make_async_copy(table.at[2 * x], owner_row, out_sem.at[2])
    row_copy.start()

    def bulk_item(n):
        group, k = sequence[n]
        at, slot = 4 * group + k, n % 4
        if n + 2 < 16:
            fetch(n + 2).start()
        fetch(n).wait()
        share(group, k).wait_recv()
        if group == 0:
            add(got, at, stage, slot, 0, BIG_HALF, [])
            send_half_x(k).start()
            send_half_y(k).start()
        elif group == 1:
            send_half_x(k).wait_recv()
            add(got, at, stage, slot, 0, BACK_CUT, [])
            add(got, at, stage, slot, BACK_CUT, BIG_HALF - BACK_CUT, [(halves_x, k)])
            send_y(k).start()
        elif group == 2:
            send_half_y(k).wait_recv()
            add(got, at, stage, slot, 0, BACK_CUT, [(halves_y, k)])
            add(got, at, stage, slot, BACK_CUT, BIG_HALF - BACK_CUT, [])
            send_x(k).start()
        else:
            send_x(k).wait_recv()
            send_y(k).wait_recv()
            add(got, at, stage, slot, 0, BIG_HALF, [(from_x, k), (from_y, k)])

    def bulk_z(k):
        at, zd = 12 + k, order[k]

        @pl.when(zd > z)
        def _():
            @pl.when(z > 0)
            def _():
                send_up(at, zd).wait_recv()
                add(got, at, from_low, zd - 1, 0, BIG_HALF, [])

            send_up(at, zd).start()

        @pl.when(zd < z)
        def _():
            @pl.when(z < 3)
            def _():
                send_down(at, zd).wait_recv()
                add(got, at, from_high, zd, 0, BIG_HALF, [])

            send_down(at, zd).start()

    def light_item(group, k):
        at, zd, column = 4 * group + k, order[k], l_column(group)
        l_fetch(group, k).wait()
        l_share(group, k).wait_recv()
        add(l_got, at, l_stage, at, 0, SMALL_HALF, [])

        def merge(ref, slot):
            l_got[at] = (l_got[at].astype(FULL) + ref[column, slot].astype(FULL)).astype(LOW)

        if k < 3:

            @pl.when(zd > z)
            def _():
                @pl.when(z > 0)
                def _():
                    l_up(group, k).wait_recv()
                    merge(l_low, zd - 1)

                l_up(group, k).start()

            @pl.when(zd < z)
            def _():
                @pl.when(z < 3)
                def _():
                    l_down(group, k).wait_recv()
                    merge(l_high, zd)

                l_down(group, k).start()

        else:

            @pl.when(z > 0)
            def _():
                l_up(group, k).wait_recv()
                merge(l_low, zd - 1)

            @pl.when(z < 3)
            def _():
                l_down(group, k).wait_recv()
                merge(l_high, zd)

            if group == 0:
                l_half_x().start()
                l_half_y().start()

    def light_sides():
        l_half_x().wait_recv()
        l_got[7, LIGHT_CUT:SMALL_HALF, :] = (
            l_got[7, LIGHT_CUT:SMALL_HALF, :].astype(FULL) + l_halves_x[...].astype(FULL)
        ).astype(LOW)
        l_send_y().start()
        l_half_y().wait_recv()
        l_got[11, 0:LIGHT_CUT, :] = (
            l_got[11, 0:LIGHT_CUT, :].astype(FULL) + l_halves_y[...].astype(FULL)
        ).astype(LOW)
        l_send_x().start()

    def light_end():
        l_send_x().wait_recv()
        l_send_y().wait_recv()
        l_total[...] = l_got[15].astype(FULL) + l_from_x[...].astype(FULL) + l_from_y[...].astype(FULL)

    small_join = remote(late_half, late.at[pl.ds(0, SMALL_HALF)], join_send.at[1], join_recv.at[1], sibling)
    own_late = pltpu.make_async_copy(late, out_small.at[me.dp], out_sem.at[1])

    def late_z(origin, target, way):
        block = out_small.at[2 * origin + y]
        return remote(block, block, late_send.at[way, origin], late_recv.at[0, origin], target)

    def late_y(origin, yo):
        block = out_small.at[2 * origin + yo]
        return remote(block, block, late_send.at[2, origin], late_recv.at[1, origin], y_side)

    def late_step(k):
        @pl.when((core == 1) & (z >= k))
        def _():
            late_z(z - k, up, 0).wait_recv()
            pl.when(z < 3)(lambda: late_z(z - k, up, 0).start())
            late_y(z - k, y).start()

        @pl.when((core == 1) & (z + k <= 3))
        def _():
            late_z(z + k, down, 1).wait_recv()
            pl.when(z > 0)(lambda: late_z(z + k, down, 1).start())
            late_y(z + k, y).start()

    def leave():
        for section in range(4):
            @pl.when(me.pipe == section)
            def _(section=section):
                all_of(keep(section), lambda copy: copy.start())

            @pl.when(me.pipe != section)
            def _(section=section):
                all_of(exchange(section), lambda copy: copy.start())

    def late_start():
        light_end()

        @pl.when(core == 0)
        def _():
            late_half[...] = l_total[...].astype(LOW)
            small_join.start()

        @pl.when(core == 1)
        def _():
            late[SMALL_HALF:SMALL_ROWS, :] = l_total[...].astype(LOW)
            small_join.wait_recv()
            own_late.start()
            own_late.wait()
            pl.when(z < 3)(lambda: late_z(z, up, 0).start())
            pl.when(z > 0)(lambda: late_z(z, down, 1).start())
            late_y(z, y).start()

    def light_round(k):
        for n in range(4 * k, 4 * k + 4):
            light_item(*l_sequence[n])

    edge = (z == 0) | (z == 3)

    def early_z(k):
        pl.when(edge)(lambda: bulk_z(k))

    def inner_z(k):
        pl.when(jnp.logical_not(edge))(lambda: bulk_z(k))

    actions = {"LS": [light_sides], "LE": [late_start], "G": [leave]}
    numbered = {item: n for n, item in enumerate(sequence)}
    for k in range(4):
        actions["A%d" % k] = [functools.partial(bulk_item, numbered[0, k])]
        actions["B%d" % k] = [functools.partial(bulk_item, numbered[group, k]) for group in (1, 2)]
        actions["O%d" % k] = [functools.partial(bulk_item, numbered[3, k])]
        actions["L%d" % k] = [functools.partial(light_round, k)]
        if k < 3:
            actions["E%d" % k] = [functools.partial(early_z, k)]
            actions["I%d" % k] = [functools.partial(inner_z, k)]
        if k:
            actions["T%d" % k] = [functools.partial(late_step, k)]
    for event in REDUCE_ORDER:
        for action in actions[event]:
            action()

    row_copy.wait()
    part_sum[...] = jnp.sum((l_total[...] * l_total[...]).reshape(SMALL_HALF // 8, 8, 128), axis=0)
    lane = lax.broadcasted_iota(jnp.int32, (8, 128), 1)
    is_last = jnp.where((lane == me.dp) & (owner_row[...] == 7), 1.0, 0.0)
    weight = jnp.broadcast_to(jnp.sum(is_last, axis=1, keepdims=True), (8, 128))
    weight = jnp.where(core == 0, jnp.ones((8, 128), FULL), weight)

    def end(low, high):
        def piece(begin, size, scale):
            part = pl.ds(begin, size)
            sums = got[15, part, :].astype(FULL)
            if low:
                sums = sums + from_low[z - 1, part, :].astype(FULL)
            if high:
                sums = sums + from_high[z, part, :].astype(FULL)
            total[part, :] = sums
            squares = jnp.sum((sums * sums).reshape(size // 8, 8, 128), axis=0)
            part_sum[...] += squares if scale is None else squares * scale

        over(0, BIG_HALF - 256, lambda begin, size: piece(begin, size, None))
        piece(BIG_HALF - 256, 256, weight)

    @pl.when(z == 0)
    def _():
        send_down(15, z).wait_recv()
        end(False, True)

    @pl.when((z > 0) & (z < 3))
    def _():
        send_up(15, z).wait_recv()
        send_down(15, z).wait_recv()
        end(True, True)

    @pl.when(z == 3)
    def _():
        send_up(15, z).wait_recv()
        end(True, False)

    big_join = remote(total, out_big.at[1], join_send.at[0], join_recv.at[0], sibling)
    own_big = pltpu.make_async_copy(total, out_big.at[0], out_sem.at[0])

    @pl.when(core == 0)
    def _():
        own_big.start()

    @pl.when(core == 1)
    def _():
        big_join.start()

    def along_pipe(step, slot):
        target = {"dp": me.dp, "pipe": lax.rem(me.pipe + step, 4)}
        return remote(part_sum, by_pipe.at[slot], p_send.at[step], p_recv.at[step], target)

    def along_dp(step, slot):
        target = {"dp": lax.rem(me.dp + step, 8), "pipe": me.pipe}
        return remote(mine, by_dp.at[slot], d_send.at[step], d_recv.at[step], target)

    for step in range(1, 4):
        along_pipe(step, me.pipe).start()
    by_pipe[me.pipe] = part_sum[...]
    for step in range(1, 4):
        along_pipe(step, lax.rem(me.pipe + 4 - step, 4)).wait_recv()
    mine[...] = jnp.sum(by_pipe[...], axis=0)
    for step in range(1, 8):
        along_dp(step, me.dp).start()
    by_dp[me.dp] = mine[...]
    for step in range(1, 8):
        along_dp(step, lax.rem(me.dp + 8 - step, 8)).wait_recv()
    whole = jnp.sum(jnp.sum(by_dp[...], axis=0), axis=0, keepdims=True)
    length = jnp.sqrt(jnp.broadcast_to(jnp.sum(whole, axis=1, keepdims=True), (8, 128)))
    norm[...] = length
    factor[...] = jnp.minimum(1.0, CLIP_NORM / length)

    @pl.when(core == 0)
    def _():
        own_big.wait()
        big_join.wait_recv()
        small_join.wait_send()

    @pl.when(core == 1)
    def _():
        big_join.wait_send()
        for origin in range(4):
            late_y(origin, 1 - y).wait_recv()
            late_y(origin, y).wait_send()
            pl.when((z < 3) & (origin <= z))(lambda: late_z(origin, up, 0).wait_send())
            pl.when((z > 0) & (origin >= z))(lambda: late_z(origin, down, 1).wait_send())

    for other in range(4):
        @pl.when(me.pipe == other)
        def _(other=other):
            all_of(keep(other), lambda copy: copy.wait())

        @pl.when(me.pipe != other)
        def _(other=other):
            all_of(exchange(other), lambda copy: copy.wait_send())
            all_of(arriving(other), lambda copy: copy.wait_recv())

    for step in range(1, 4):
        along_pipe(step, me.pipe).wait_send()
    for step in range(1, 8):
        along_dp(step, me.dp).wait_send()
    for copy in (l_half_x(), l_half_y(), l_send_x(), l_send_y()):
        copy.wait_send()
    for k in range(4):
        send_half_x(k).wait_send()
        send_half_y(k).wait_send()
        send_x(k).wait_send()
        send_y(k).wait_send()
        for group in range(4):
            share(group, k).wait_send()
            l_share(group, k).wait_send()
    for k in range(3):
        zd, at = order[k], 12 + k

        @pl.when(zd > z)
        def _(at=at, zd=zd, k=k):
            send_up(at, zd).wait_send()
            for group in range(4):
                l_up(group, k).wait_send()

        @pl.when(zd < z)
        def _(at=at, zd=zd, k=k):
            send_down(at, zd).wait_send()
            for group in range(4):
                l_down(group, k).wait_send()


def reduce_all(big, small, wide0, wide1, final, stats, table):
    sem = pltpu.SemaphoreType.DMA
    vm = pltpu.VMEM
    lane_tile = jax.ShapeDtypeStruct((8, 128), FULL)
    return pl.pallas_call(
        reduce_kernel,
        name="reduce_all",
        out_shape=(
            jax.ShapeDtypeStruct((2, BIG_HALF, 128), FULL),
            jax.ShapeDtypeStruct((8, SMALL_ROWS, 128), LOW),
            jax.ShapeDtypeStruct((4,) + wide0.shape, LOW),
            jax.ShapeDtypeStruct((4,) + stats.shape[1:], FULL),
            lane_tile,
            lane_tile,
        ),
        in_specs=[any_spec()] * 7,
        out_specs=(any_spec(),) * 4 + (vmem_spec(),) * 2,
        scratch_shapes=[
            vm((16, BIG_HALF, 128), LOW), vm((4, BIG_HALF - BACK_CUT, 128), LOW), vm((4, BACK_CUT, 128), LOW),
            vm((4, BIG_HALF, 128), LOW), vm((4, BIG_HALF, 128), LOW),
            vm((3, BIG_HALF, 128), LOW), vm((3, BIG_HALF, 128), LOW),
            vm((4, BIG_HALF, 128), LOW), vm((BIG_HALF, 128), FULL),
            vm((16, SMALL_HALF, 128), LOW), vm((16, SMALL_HALF, 128), LOW),
            vm((4, 3, SMALL_HALF, 128), LOW), vm((4, 3, SMALL_HALF, 128), LOW),
            vm((SMALL_HALF - LIGHT_CUT, 128), LOW), vm((LIGHT_CUT, 128), LOW),
            vm((SMALL_HALF, 128), LOW), vm((SMALL_HALF, 128), LOW), vm((SMALL_HALF, 128), FULL),
            vm((SMALL_ROWS, 128), LOW), vm((SMALL_HALF, 128), LOW), vm((8, 128), jnp.int32),
            vm((4, 8, 128), FULL), vm((8, 8, 128), FULL), vm((8, 128), FULL), vm((8, 128), FULL),
            sem((2, 16)), sem((2, 16)),
            sem((5,)), sem((5,)), sem((5,)), sem((5,)), sem((5,)), sem((5,)), sem((5,)), sem((5,)),
            sem((3,)), sem((3,)), sem((3,)), sem((3,)),
            sem((4, 3)), sem((4, 3)), sem((4, 3)), sem((4, 3)),
            sem((4,)), sem((16,)), sem((3,)), sem((3, 4)), sem((2, 4)), sem((2,)), sem((2,)),
            sem((4,)), sem((4,)), sem((4,)), sem((4,)), sem((4,)), sem((4,)), sem((8,)), sem((8,)),
        ],
        compiler_params=pltpu.CompilerParams(
            collective_id=1, has_side_effects=True, vmem_limit_bytes=62 << 20
        ),
    )(big.reshape(2, 8, 2, BIG_HALF, 128), small.reshape(2, 8, 2, SMALL_HALF, 128),
      wide0, wide1, final, stats, table)


def high_dot(a, b, dims=((1,), (0,))):
    return lax.dot_general(a, b, (dims, ((), ())), precision=HIGH, preferred_element_type=FULL)


PIECES = 7
FRONT = 48


def update_kernel(owners, factor_ref, norm, big, small, gram_old, basis_old, params, moment, second,
                  clipped, moment_new, second_new, params_new, gram_new, basis_new, length,
                  tiles, low, grad, held, rotated, weights, gram, in_sem, out_sem, tile_sem):
    factor = factor_ref[0:1, :]
    length[0, 0] = jnp.max(norm[...])
    block, section = owners[0, lax.axis_index("dp")], lax.axis_index("pipe")
    even = lax.rem(section, 2) == 0
    span = params.shape[0]
    piece = held.shape[0] // PIECES

    @pl.when(even)
    def _():
        pltpu.make_async_copy(big, tiles, tile_sem).start()

    def loads(i):
        part = pl.ds(piece * i, min(piece, span - piece * i))
        for n, (src, dst) in enumerate(((params, weights), (moment, held), (second, rotated))):
            yield pltpu.make_async_copy(src.at[part, 0, :], dst.at[part], in_sem.at[n, i])

    def stores(i):
        count = min(piece, span - piece * i)
        part = pl.ds(piece * i, count)
        yield pltpu.make_async_copy(
            grad.at[pl.ds(FRONT + piece * i, count)], clipped.at[part, 0, :], out_sem.at[3, i])
        pairs = ((held, moment_new), (rotated, second_new), (weights, params_new))
        for n, (src, dst) in enumerate(pairs):
            yield pltpu.make_async_copy(src.at[part], dst.at[part, 0, :], out_sem.at[n, i])

    for i in range(PIECES):
        for load in loads(i):
            load.start()

    @pl.when(even)
    def _():
        pltpu.make_async_copy(big, tiles, tile_sem).wait()

    @pl.when(jnp.logical_not(even))
    def _():
        low[...] = jnp.zeros_like(low)

        @pl.when(block == 0)
        def _():
            copy = pltpu.make_async_copy(small.at[0:20], low, tile_sem)
            copy.start()
            copy.wait()

        @pl.when(block == 1)
        def _():
            copy = pltpu.make_async_copy(small.at[19:33], low.at[0:14], tile_sem)
            copy.start()
            copy.wait()

        @pl.loop(0, WINDOW)
        def _(r):
            tiles[r] = low[r].astype(FULL)

    @pl.loop(0, WINDOW)
    def _(r):
        narrow, plain = tile_forms(section, STRIDE * block + r)
        base = FRONT - 6 * block + TILE * r

        @pl.when(narrow)
        def _():
            for j in range(4):
                grad[pl.ds(base + j, 64, 4), :] = tiles[r, 64 * j : 64 * j + 64, :]

        @pl.when(plain)
        def _():
            grad[pl.ds(base, TILE), :] = tiles[r]

        @pl.when(jnp.logical_not(narrow | plain))
        def _():
            for j in range(16):
                grad[pl.ds(base + j, 16, 16), :] = tiles[r, 16 * j : 16 * j + 16, :]

    tail = piece * PIECES - 8
    rest = lax.broadcasted_iota(jnp.int32, (8, 128), 0) + tail
    grad[FRONT + tail : FRONT + tail + 8, :] = jnp.where(
        rest < span, grad[FRONT + tail : FRONT + tail + 8, :], 0.0
    )
    gram[...] = jnp.zeros_like(gram)

    def halves(value):
        high = value.astype(LOW)
        return high, (value - high.astype(FULL)).astype(LOW)

    def split_dot(a, b, dims=((1,), (0,))):
        def dot(left, right):
            return lax.dot_general(left, right, (dims, ((), ())), preferred_element_type=FULL)

        return dot(a[0], b[0]) + (dot(a[0], b[1]) + dot(a[1], b[0]))

    @pl.loop(0, PIECES)
    def _(i):
        part = halves(grad[pl.ds(pl.multiple_of(FRONT + piece * i, 8), piece), :])
        gram[...] += split_dot(part, part, ((0,), (0,)))

    old = basis_old[...]
    fresh = DECAY_STATS * gram_old[...] + (1.0 - DECAY_STATS) * (gram[...] * (factor * factor))
    gram_new[...] = fresh
    product = high_dot(fresh, old)
    rotation = product / jnp.sqrt(jnp.sum(product * product))
    for repeat in range(NS_STEPS):
        square = high_dot(rotation, rotation, ((0,), (0,)))
        rotation = 1.5 * rotation - 0.5 * high_dot(rotation, square)
    basis_new[...] = rotation
    change = halves(high_dot(old, rotation, ((0,), (0,))))
    turn = halves(rotation)
    correction = math.sqrt(1.0 - DECAY_SECOND**STEP) / (1.0 - DECAY_FIRST**STEP)
    for i in range(PIECES):
        for load in loads(i):
            load.wait()
        at = slice(FRONT + piece * i, FRONT + piece * i + piece)
        part = slice(piece * i, piece * i + piece)
        clip = grad[at, :] * factor
        grad[at, :] = clip
        turned = split_dot(halves(clip), turn)
        first = DECAY_FIRST * split_dot(halves(held[part, :]), change) + (1.0 - DECAY_FIRST) * turned
        power = DECAY_SECOND * rotated[part, :] + (1.0 - DECAY_SECOND) * turned * turned
        held[part, :] = first
        rotated[part, :] = power
        scaled = halves(first / (jnp.sqrt(power) + ADAM_EPS))
        direction = split_dot(scaled, turn, ((1,), (1,))) * correction
        before = weights[part, :]
        weights[part, :] = before - LEARN_RATE * (direction + WEIGHT_DECAY * before)
        for store in stores(i):
            store.start()
    for i in range(PIECES):
        for store in stores(i):
            store.wait()


def update(owners, factor, norm, big, small, gram_old, basis_old, params, moment, second):
    span = params.shape[1] // 128
    rows = -(-span // (8 * PIECES)) * 8 * PIECES
    flat_shape = jax.ShapeDtypeStruct((span, 1, 128), FULL)
    square = jax.ShapeDtypeStruct((128, 128), FULL)
    sem = pltpu.SemaphoreType.DMA
    vm = pltpu.VMEM
    outs = pl.pallas_call(
        update_kernel,
        name="update",
        out_shape=(flat_shape,) * 4 + (square,) * 2 + (jax.ShapeDtypeStruct((1, 1), FULL),),
        in_specs=[smem_spec()] + [vmem_spec()] * 2 + [any_spec()] * 2 + [vmem_spec()] * 2 + [any_spec()] * 3,
        out_specs=(any_spec(),) * 4 + (vmem_spec(),) * 2 + (smem_spec(),),
        scratch_shapes=[
            vm((WINDOW, TILE, 128), FULL), vm((WINDOW, TILE, 128), LOW),
            vm((FRONT + WINDOW * TILE, 128), FULL), vm((rows, 128), FULL), vm((rows, 128), FULL),
            vm((rows, 128), FULL), vm((128, 128), FULL), sem((3, PIECES)), sem((4, PIECES)), sem,
        ],
        compiler_params=pltpu.CompilerParams(vmem_limit_bytes=60 << 20),
    )(owners, factor, norm, big.reshape(WINDOW, TILE, 128), small.reshape(USED_TILES[1], TILE, 128),
      gram_old, basis_old, params.reshape(span, 1, 128), moment.reshape(span, 1, 128),
      second.reshape(span, 1, 128))
    return tuple(out.reshape(1, span * 128) for out in outs[:4]) + outs[4:]


def to_phases(teach, stud):
    def split(part):
        crops, high, across, channels = part.shape
        part = part.reshape(crops, high // 2, 2, across // 2, 2, channels).transpose(2, 4, 0, 1, 3, 5)
        return part.reshape(4, -1, channels)

    zeros = jnp.zeros((4, PADDED - ROWS, teach.shape[-1]), teach.dtype)
    return jnp.concatenate([split(teach), split(stud), zeros], axis=1)


def from_phases(phases, shape):
    crops, high, across, channels = shape
    part = phases.reshape(2, 2, crops, high // 2, across // 2, channels)
    return part.transpose(2, 3, 0, 4, 1, 5).reshape(shape)


def on_small_slice(
    teach_in,
    stud_in,
    params,
    owners,
    depth_gates,
    teach_ids,
    stud_ids,
    targets,
    moment,
    second,
    gram_stats,
    eigen_basis,
):
    phases = to_phases(teach_in[0], stud_in[0])
    big, small, ids = prepare(owners, params)
    all_big, all_small, table = gather_all(big, small, ids)
    wide_0, wide_1, final, stats, grad_x, out_big, out_small = run_step(
        table,
        depth_gates,
        teach_ids.T,
        stud_ids,
        all_big.reshape(2, 8, 2, WINDOW // 2, TILE, 128),
        all_small.reshape(2, USED_TILES[1], TILE, 128),
        phases,
        targets,
    )
    sum_big, sum_small, segments, stats, norm, factor = reduce_all(
        out_big, out_small, wide_0, wide_1, final, stats, table
    )
    clipped, moment_new, second_new, params_new, gram_new, rotation, length = update(
        owners, factor, norm, sum_big, sum_small, gram_stats[0], eigen_basis[0], params, moment, second
    )
    teach_shape, stud_shape = teach_in.shape[1:], stud_in.shape[1:]
    small_teach = (teach_shape[0], teach_shape[1] // 2, teach_shape[2] // 2, C_OUT)
    small_stud = (stud_shape[0], stud_shape[1] // 2, stud_shape[2] // 2, C_OUT)
    segment_teach = segments[:, :TEACH_ROWS].reshape((4,) + small_teach)
    segment_stud = segments[:, TEACH_ROWS:ROWS].reshape((4,) + small_stud)
    stats = stats[:, 0:2]
    teach_grad = from_phases(grad_x[:, :TEACH_ROWS], teach_shape)
    stud_grad = from_phases(grad_x[:, TEACH_ROWS:ROWS], stud_shape)
    grad_norm = length.reshape(())
    return (
        segment_teach[None],
        segment_stud[None],
        teach_grad[None],
        stud_grad[None],
        stats[None, :, None],
        grad_norm,
        clipped,
        moment_new,
        second_new,
        params_new,
        gram_new[None],
        rotation[None],
    )


def solution(mesh):
    placed = (
        P("pipe", "dp", None, None, None),
        P("pipe", "dp", None, None, None),
        P("pipe", "dp"),
        P("pipe", None),
        P(),
        P(None, "dp"),
        P(None, "dp"),
        P(),
        P("pipe", "dp"),
        P("pipe", "dp"),
        P("pipe", "dp", None),
        P("pipe", "dp", None),
    )
    small_slice = mesh.shape["dp"] == 8 and mesh.shape["pipe"] == 4
    return jax.shard_map(
        on_small_slice if small_slice else on_device,
        mesh=mesh,
        in_specs=placed,
        out_specs=(
            P("pipe", None, "dp", None, None, None),
            P("pipe", None, "dp", None, None, None),
            P("pipe", "dp", None, None, None),
            P("pipe", "dp", None, None, None),
            P("pipe", None, "dp", None, None),
            P(),
            P("pipe", "dp"),
            P("pipe", "dp"),
            P("pipe", "dp"),
            P("pipe", "dp"),
            P("pipe", "dp", None),
            P("pipe", "dp", None),
        ),
        check_vma=False,
    )
```

```python
import functools
import math

import jax
import jax.numpy as jnp
import numpy as np
from jax import lax
from jax.experimental import pallas as pl
from jax.experimental.pallas import tpu as pltpu
from jax.sharding import PartitionSpec as P

C_IN = 1024
MID = 512
C_OUT = 2048
STEP = 10
NS_STEPS = 5


HIGH = lax.Precision.HIGHEST
NORM_EPS = 1e-05
POOL_EPS = 1e-06
CLIP_NORM = 1.0
LEARN_RATE = 0.02
DECAY_FIRST = 0.9
DECAY_SECOND = 0.95
DECAY_STATS = 0.95
ADAM_EPS = 1e-08
WEIGHT_DECAY = 0.01


def section_shapes(section):
    if section == 0:
        return [
            ("first_conv", (C_IN, MID)),
            ("middle_conv", (9 * MID, MID)),
            ("skip_conv", (C_IN, C_OUT)),
            ("first_gain", (MID,)),
            ("first_bias", (MID,)),
            ("middle_gain", (MID,)),
            ("middle_bias", (MID,)),
            ("skip_gain", (C_OUT,)),
            ("skip_bias", (C_OUT,)),
        ]
    if section == 2:
        return [
            ("first_conv", (C_OUT, MID)),
            ("middle_conv", (9 * MID, MID)),
            ("first_gain", (MID,)),
            ("first_bias", (MID,)),
            ("middle_gain", (MID,)),
            ("middle_bias", (MID,)),
        ]
    return [("last_conv", (MID, C_OUT)), ("last_gain", (C_OUT,)), ("last_bias", (C_OUT,))]


def unpack(flat_vector, section):
    pieces = {}
    offset = 0
    for entry_name, entry_shape in section_shapes(section):
        entry_size = math.prod(entry_shape)
        pieces[entry_name] = flat_vector[offset : offset + entry_size].reshape(entry_shape)
        offset = offset + entry_size
    return pieces


def pack(grads, section, flat_size):
    parts = [grads[entry_name].reshape(-1) for entry_name, entry_shape in section_shapes(section)]
    used = sum((math.prod(entry_shape) for entry_name, entry_shape in section_shapes(section)))
    parts.append(jnp.zeros((flat_size - used,), jnp.float32))
    return jnp.concatenate(parts)


def as_float(vector):
    return vector.astype(jnp.float32)


def to_low(groups):
    return tuple((portion.astype(jnp.bfloat16) for portion in groups))


def to_high(groups):
    return tuple((portion.astype(jnp.float32) for portion in groups))


def point_conv(groups, weight):
    return tuple(
        (
            jnp.einsum("khwc,cd->khwd", portion, weight, preferred_element_type=jnp.float32)
            for portion in groups
        )
    )


def point_back(grad_out, groups, weight):
    low_grads = to_low(grad_out)
    grad_input = tuple(
        (
            jnp.einsum("khwd,cd->khwc", grad_part, weight, preferred_element_type=jnp.float32)
            for grad_part in low_grads
        )
    )
    grad_weight = sum(
        (
            jnp.einsum("khwc,khwd->cd", in_part, grad_part, preferred_element_type=jnp.float32)
            for in_part, grad_part in zip(groups, low_grads)
        )
    )
    return (grad_input, grad_weight)


def patches(portion, stride):
    height = portion.shape[1]
    across = portion.shape[2]
    padded = jnp.pad(portion, ((0, 0), (1, 1), (1, 1), (0, 0)))
    shifted = [
        padded[:, row_off : row_off + height : stride, col_off : col_off + across : stride, :]
        for row_off in range(3)
        for col_off in range(3)
    ]
    return jnp.concatenate(shifted, axis=-1)


def area_conv(groups, weight, stride):
    columns = tuple((patches(portion, stride) for portion in groups))
    return (point_conv(columns, weight), columns)


def unpatch(grad_cols, height, across, stride):
    channels = grad_cols.shape[-1] // 9
    padded = jnp.zeros((grad_cols.shape[0], height + 2, across + 2, channels), jnp.float32)
    for row_off in range(3):
        for col_off in range(3):
            offset = (3 * row_off + col_off) * channels
            padded = padded.at[
                :, row_off : row_off + height : stride, col_off : col_off + across : stride, :
            ].add(grad_cols[..., offset : offset + channels])
    return padded[:, 1 : height + 1, 1 : across + 1, :]


def area_back(grad_out, columns, weight, stride, in_shapes):
    grad_cols, grad_weight = point_back(grad_out, columns, weight)
    grad_input = tuple(
        (
            unpatch(grad_part, shape_item[1], shape_item[2], stride)
            for grad_part, shape_item in zip(grad_cols, in_shapes)
        )
    )
    return (grad_input, grad_weight)


def batch_norm(groups, gain, bias):
    rows_total = sum((portion.shape[0] * portion.shape[1] * portion.shape[2] for portion in groups))
    centre = sum((jnp.sum(portion, axis=(0, 1, 2)) for portion in groups)) / rows_total
    spread = (
        sum((jnp.sum(jnp.square(portion - centre), axis=(0, 1, 2)) for portion in groups))
        / rows_total
    )
    inverse = lax.rsqrt(spread + NORM_EPS)
    standard = tuple(((portion - centre) * inverse for portion in groups))
    normed = tuple((gain * std_part + bias for std_part in standard))
    return (normed, (centre, spread, inverse, standard))


def norm_back(grad_out, gain, saved):
    centre, spread, inverse, standard = saved
    rows_total = sum(
        (portion.shape[0] * portion.shape[1] * portion.shape[2] for portion in standard)
    )
    grad_sum = sum((jnp.sum(grad_part, axis=(0, 1, 2)) for grad_part in grad_out))
    grad_dot = sum(
        (
            jnp.sum(grad_part * std_part, axis=(0, 1, 2))
            for grad_part, std_part in zip(grad_out, standard)
        )
    )
    grad_input = tuple(
        (
            gain
            * inverse
            * (grad_part - grad_sum / rows_total - std_part * (grad_dot / rows_total))
            for grad_part, std_part in zip(grad_out, standard)
        )
    )
    return (grad_input, grad_dot, grad_sum)


def through_softplus(grad_out, pre_values):
    return tuple(
        (grad_part * jax.nn.sigmoid(pre_part) for grad_part, pre_part in zip(grad_out, pre_values))
    )


def front_forward(pieces, inputs):
    first = point_conv(inputs, pieces["first_conv"])
    normed_a, saved_a = batch_norm(
        first, as_float(pieces["first_gain"]), as_float(pieces["first_bias"])
    )
    hidden = tuple((jax.nn.softplus(portion).astype(jnp.bfloat16) for portion in normed_a))
    middle, columns = area_conv(hidden, pieces["middle_conv"], 2)
    normed_b, saved_b = batch_norm(
        middle, as_float(pieces["middle_gain"]), as_float(pieces["middle_bias"])
    )
    narrow = tuple((jax.nn.softplus(portion) for portion in normed_b))
    reduced = tuple((portion[:, ::2, ::2, :] for portion in inputs))
    skipped = point_conv(reduced, pieces["skip_conv"])
    wide, saved_p = batch_norm(
        skipped, as_float(pieces["skip_gain"]), as_float(pieces["skip_bias"])
    )
    norm_rows = jnp.stack(
        [
            jnp.concatenate([saved_a[0], saved_b[0], saved_p[0]]),
            jnp.concatenate([saved_a[1], saved_b[1], saved_p[1]]),
        ]
    )
    kept = (normed_a, hidden, columns, normed_b, reduced, saved_a, saved_b, saved_p)
    return (wide, narrow, norm_rows, kept)


def front_backward(pieces, inputs, grad_wide, grad_narrow):
    wide, narrow, norm_rows, kept = front_forward(pieces, inputs)
    normed_a, hidden, columns, normed_b, reduced, saved_a, saved_b, saved_p = kept
    grads = {}
    grad_pre_b = through_softplus(grad_narrow, normed_b)
    grad_mid, grads["middle_gain"], grads["middle_bias"] = norm_back(
        grad_pre_b, as_float(pieces["middle_gain"]), saved_b
    )
    grad_hidden, grads["middle_conv"] = area_back(
        grad_mid, columns, pieces["middle_conv"], 2, [portion.shape for portion in hidden]
    )
    grad_pre_a = through_softplus(grad_hidden, normed_a)
    grad_first, grads["first_gain"], grads["first_bias"] = norm_back(
        grad_pre_a, as_float(pieces["first_gain"]), saved_a
    )
    grad_inputs, grads["first_conv"] = point_back(grad_first, inputs, pieces["first_conv"])
    grad_skip, grads["skip_gain"], grads["skip_bias"] = norm_back(
        grad_wide, as_float(pieces["skip_gain"]), saved_p
    )
    grad_reduced, grads["skip_conv"] = point_back(grad_skip, reduced, pieces["skip_conv"])
    grad_inputs = tuple(
        (
            full_part.at[:, ::2, ::2, :].add(part_reduced)
            for full_part, part_reduced in zip(grad_inputs, grad_reduced)
        )
    )
    return (grad_inputs, grads)


def join_forward(pieces, wide, narrow):
    last = point_conv(narrow, pieces["last_conv"])
    normed, saved = batch_norm(last, as_float(pieces["last_gain"]), as_float(pieces["last_bias"]))
    pre_values = tuple(
        (
            skip_part.astype(jnp.float32) + branch_part
            for skip_part, branch_part in zip(wide, normed)
        )
    )
    ending = tuple((jax.nn.softplus(pre_part) for pre_part in pre_values))
    filler = jnp.zeros((2 * MID,), jnp.float32)
    norm_rows = jnp.stack(
        [jnp.concatenate([saved[0], filler]), jnp.concatenate([saved[1], filler])]
    )
    return (ending, norm_rows, (pre_values, saved))


def join_grads(pieces, narrow, kept, grad_out, gate):
    pre_values, saved = kept
    grad_pre = tuple(
        (
            grad_part * jax.nn.sigmoid(pre_part) * gate
            for grad_part, pre_part in zip(grad_out, pre_values)
        )
    )
    grad_wide = tuple(
        (pre_grad + grad_part * (1.0 - gate) for pre_grad, grad_part in zip(grad_pre, grad_out))
    )
    grad_last, gain_grad, bias_grad = norm_back(grad_pre, as_float(pieces["last_gain"]), saved)
    grad_narrow, weight_grad = point_back(grad_last, narrow, pieces["last_conv"])
    grads = {"last_conv": weight_grad, "last_gain": gain_grad, "last_bias": bias_grad}
    return (grad_wide, grad_narrow, grads)


def split_forward(pieces, wide):
    first = point_conv(wide, pieces["first_conv"])
    normed_a, saved_a = batch_norm(
        first, as_float(pieces["first_gain"]), as_float(pieces["first_bias"])
    )
    hidden = tuple((jax.nn.softplus(portion).astype(jnp.bfloat16) for portion in normed_a))
    middle, columns = area_conv(hidden, pieces["middle_conv"], 1)
    normed_b, saved_b = batch_norm(
        middle, as_float(pieces["middle_gain"]), as_float(pieces["middle_bias"])
    )
    narrow = tuple((jax.nn.softplus(portion) for portion in normed_b))
    filler = jnp.zeros((C_OUT,), jnp.float32)
    norm_rows = jnp.stack(
        [
            jnp.concatenate([saved_a[0], saved_b[0], filler]),
            jnp.concatenate([saved_a[1], saved_b[1], filler]),
        ]
    )
    return (narrow, norm_rows, (normed_a, hidden, columns, normed_b, saved_a, saved_b))


def split_backward(pieces, wide, grad_relay, grad_narrow):
    narrow, norm_rows, kept = split_forward(pieces, wide)
    normed_a, hidden, columns, normed_b, saved_a, saved_b = kept
    grads = {}
    grad_pre_b = through_softplus(grad_narrow, normed_b)
    grad_mid, grads["middle_gain"], grads["middle_bias"] = norm_back(
        grad_pre_b, as_float(pieces["middle_gain"]), saved_b
    )
    grad_hidden, grads["middle_conv"] = area_back(
        grad_mid, columns, pieces["middle_conv"], 1, [portion.shape for portion in hidden]
    )
    grad_pre_a = through_softplus(grad_hidden, normed_a)
    grad_first, grads["first_gain"], grads["first_bias"] = norm_back(
        grad_pre_a, as_float(pieces["first_gain"]), saved_a
    )
    grad_conv_in, grads["first_conv"] = point_back(grad_first, wide, pieces["first_conv"])
    grad_wide = tuple(
        (relay_part + conv_part for relay_part, conv_part in zip(grad_relay, grad_conv_in))
    )
    return (grad_wide, grads)


def pool_grad(final, targets, picks):
    result = []
    for portion, pick_ids in zip(final, picks):
        cubes = jnp.mean(portion * portion * portion, axis=(1, 2)) + POOL_EPS
        factor = jnp.exp(jnp.log(cubes) * (-2.0 / 3.0)) * targets[pick_ids]
        result.append(factor[:, None, None, :] * portion * portion)
    return tuple(result)


def used_size(section):
    return sum((math.prod(entry_shape) for entry_name, entry_shape in section_shapes(section)))


def batch_pass(reals, inputs, gate, targets, picks):
    pieces = [unpack(reals[section], section) for section in range(4)]
    wide_f, narrow_f, rows_0, _ = front_forward(pieces[0], inputs)
    wide_0, narrow_0 = to_low(wide_f), to_low(narrow_f)
    ending_1, rows_1, kept_1 = join_forward(pieces[1], wide_0, narrow_0)
    wide_1 = to_low(ending_1)
    narrow_f, rows_2, _ = split_forward(pieces[2], wide_1)
    narrow_2 = to_low(narrow_f)
    ending_3, rows_3, kept_3 = join_forward(pieces[3], wide_1, narrow_2)
    final = tuple(
        (
            jnp.where(gate > 0, end_part, relay_part.astype(jnp.float32))
            for end_part, relay_part in zip(ending_3, wide_1)
        )
    )
    cotangent = pool_grad(final, targets, picks)
    grad_wide, grad_narrow, grads_3 = join_grads(pieces[3], narrow_2, kept_3, cotangent, gate)
    grad_wide, grads_2 = split_backward(
        pieces[2], wide_1, to_high(to_low(grad_wide)), to_high(to_low(grad_narrow))
    )
    grad_wide, grad_narrow, grads_1 = join_grads(
        pieces[1], narrow_0, kept_1, to_high(to_low(grad_wide)), 1.0
    )
    grad_inputs, grads_0 = front_backward(
        pieces[0], inputs, to_high(to_low(grad_wide)), to_high(to_low(grad_narrow))
    )
    outs = (wide_0, wide_1, wide_1, to_low(final))
    stats = jnp.stack([rows_0, rows_1, rows_2 * gate, rows_3 * gate])
    return (outs, stats, to_low(grad_inputs), (grads_0, grads_1, grads_2, grads_3))


def on_device(
    teach_in,
    stud_in,
    params,
    owners,
    depth_gates,
    teach_ids,
    stud_ids,
    targets,
    moment,
    second,
    gram_stats,
    eigen_basis,
):
    sections = lax.axis_size("pipe")
    rank = lax.axis_index("pipe")
    owner_count = lax.axis_size("dp")
    span_size = params.shape[1]
    flat_size = span_size * owner_count
    owner_rows = lax.all_gather(owners, "pipe", axis=0, tiled=True)
    gathered = lax.all_gather(params[0].astype(jnp.bfloat16), ("pipe", "dp"), axis=0)
    gathered = gathered.reshape(sections, owner_count, span_size)
    reals = []
    for section in range(sections):
        inverse = jnp.argsort(owner_rows[section]).astype(jnp.int32)
        blocks = -(-used_size(section) // span_size)
        reals.append(gathered[section][inverse[:blocks]].reshape(blocks * span_size))
    inputs = (teach_in[0], stud_in[0])
    gate = depth_gates[rank].astype(jnp.float32)
    outs, stats, (teach_grad, stud_grad), grads = batch_pass(
        reals, inputs, gate, targets, (teach_ids[rank], stud_ids[rank])
    )
    segment_teach = lax.all_to_all(
        jnp.stack([part[0] for part in outs]), "pipe", split_axis=0, concat_axis=0, tiled=True
    )
    segment_stud = lax.all_to_all(
        jnp.stack([part[1] for part in outs]), "pipe", split_axis=0, concat_axis=0, tiled=True
    )
    stats = lax.all_to_all(stats, "pipe", split_axis=0, concat_axis=0, tiled=True)
    rows = []
    for section in range(sections):
        flat = pack(grads[section], section, flat_size).reshape(owner_count, span_size)
        rows.append(flat[owner_rows[section]])
    span_total = lax.psum_scatter(
        jnp.stack(rows).reshape(sections * owner_count, span_size),
        ("pipe", "dp"),
        scatter_dimension=0,
        tiled=True,
    ).reshape(span_size)
    total_squares = lax.psum(jnp.sum(span_total * span_total), ("dp", "pipe"))
    grad_norm = jnp.sqrt(total_squares)
    factor = jnp.minimum(1.0, CLIP_NORM / grad_norm)
    clipped = span_total * factor
    matrix = clipped.reshape(span_size // 128, 128)
    gram_old = gram_stats[0]
    basis_old = eigen_basis[0]
    gram_new = DECAY_STATS * gram_old + (1.0 - DECAY_STATS) * jnp.dot(
        matrix.T, matrix, precision=HIGH
    )
    product = jnp.dot(gram_new, basis_old, precision=HIGH)
    rotation = product / jnp.sqrt(jnp.sum(product * product))
    for repeat in range(NS_STEPS):
        square = jnp.dot(rotation.T, rotation, precision=HIGH)
        rotation = 1.5 * rotation - 0.5 * jnp.dot(rotation, square, precision=HIGH)
    moment_old = moment.reshape(span_size // 128, 128)
    initial = jnp.dot(moment_old, basis_old.T, precision=HIGH)
    blended = DECAY_FIRST * initial + (1.0 - DECAY_FIRST) * matrix
    moment_new = jnp.dot(blended, rotation, precision=HIGH)
    rotated = jnp.dot(matrix, rotation, precision=HIGH)
    second_new = (
        DECAY_SECOND * second.reshape(span_size // 128, 128)
        + (1.0 - DECAY_SECOND) * rotated * rotated
    )
    correction = math.sqrt(1.0 - DECAY_SECOND**STEP) / (1.0 - DECAY_FIRST**STEP)
    direction = (
        jnp.dot(moment_new / (jnp.sqrt(second_new) + ADAM_EPS), rotation.T, precision=HIGH)
        * correction
    )
    weights = params.reshape(span_size // 128, 128)
    params_new = weights - LEARN_RATE * (direction + WEIGHT_DECAY * weights)
    return (
        segment_teach[None],
        segment_stud[None],
        teach_grad[None],
        stud_grad[None],
        stats[None, :, None],
        grad_norm,
        clipped.reshape(1, span_size),
        moment_new.reshape(1, span_size),
        second_new.reshape(1, span_size),
        params_new.reshape(1, span_size),
        gram_new[None],
        rotation[None],
    )


MESH = pl.DeviceIdType.MESH
LOW = jnp.bfloat16
FULL = jnp.float32
TILE = 256
WINDOW = 20
STRIDE = 19
EDGE = 64
BIG_ROWS = STRIDE * TILE + EDGE
VEC_TILE = (152, 32, 104, 32)
USED_TILES = (153, 33, 105, 33)
FRONT_WIDE = 88
SMALL_ROWS = 1056
ROWS = 120
PADDED = 128
TEACH_ROWS = 72


def any_spec():
    return pl.BlockSpec(memory_space=pl.ANY)


def smem_spec():
    return pl.BlockSpec(memory_space=pltpu.SMEM)


def vmem_spec():
    return pl.BlockSpec(memory_space=pltpu.VMEM)


def tile_forms(section, tile):
    even = lax.rem(section, 2) == 0
    vector = jnp.where(section == 0, 152, jnp.where(section == 2, 104, 32))
    narrow_end = jnp.where(section == 0, FRONT_WIDE, jnp.where(section == 2, 104, 0))
    narrow = even & (tile < narrow_end)
    plain = tile == vector
    return narrow, plain


def prepare_kernel(owners, params, big, small, ids, flat, sem):
    block, section = owners[0, lax.axis_index("dp")], lax.axis_index("pipe")

    even = lax.rem(section, 2) == 0
    flat[0:EDGE, :] = jnp.zeros((EDGE, 128), FULL)
    flat[STRIDE * TILE : WINDOW * TILE, :] = jnp.zeros((TILE, 128), FULL)
    copy = pltpu.make_async_copy(params.at[:, 0, :], flat.at[pl.ds(6 * block, params.shape[0])], sem)
    copy.start()

    @pl.when(jnp.logical_not(even))
    def _():
        @pl.loop(0, small.shape[0])
        def _(r):
            small[r] = jnp.zeros((TILE, 128), LOW)

    lane = lax.broadcasted_iota(jnp.int32, (8, 128), 1)
    row = jnp.zeros((8, 128), jnp.int32)
    for j in range(8):
        row = jnp.where(lane == j, owners[0, j], row)
    ids[...] = row
    copy.wait()

    def wide_tile(base):
        return [flat[pl.ds(base + j, 16, 16), :].astype(LOW) for j in range(16)]

    @pl.when(even)
    def _():
        @pl.loop(0, STRIDE)
        def _(r):
            narrow, plain = tile_forms(section, STRIDE * block + r)
            base = pl.multiple_of(TILE * r, TILE)

            @pl.when(narrow)
            def _():
                for j in range(4):
                    big[pl.ds(base + 64 * j, 64), :] = flat[pl.ds(base + j, 64, 4), :].astype(LOW)

            @pl.when(plain)
            def _():
                big[pl.ds(base, TILE), :] = flat[pl.ds(base, TILE), :].astype(LOW)

            @pl.when(jnp.logical_not(narrow | plain))
            def _():
                for j, part in enumerate(wide_tile(base)):
                    big[pl.ds(base + 16 * j, 16), :] = part

        big[STRIDE * TILE : BIG_ROWS, :] = flat[STRIDE * TILE : BIG_ROWS, :].astype(LOW)

    @pl.when(jnp.logical_not(even))
    def _():
        @pl.loop(0, WINDOW)
        def _(r):
            tile = STRIDE * block + r
            base = pl.multiple_of(TILE * r, TILE)

            @pl.when(tile == VEC_TILE[1])
            def _():
                small[tile] = flat[pl.ds(base, TILE), :].astype(LOW)

            @pl.when(tile < VEC_TILE[1])
            def _():
                for j, part in enumerate(wide_tile(base)):
                    small[tile, 16 * j : 16 * j + 16, :] = part


def prepare(owners, params):
    return pl.pallas_call(
        prepare_kernel,
        name="prepare",
        out_shape=(
            jax.ShapeDtypeStruct((BIG_ROWS, 128), LOW),
            jax.ShapeDtypeStruct((USED_TILES[1], TILE, 128), LOW),
            jax.ShapeDtypeStruct((8, 128), jnp.int32),
        ),
        in_specs=[smem_spec(), any_spec()],
        out_specs=(vmem_spec(),) * 3,
        scratch_shapes=[pltpu.VMEM((WINDOW * TILE, 128), FULL), pltpu.SemaphoreType.DMA],
        compiler_params=pltpu.CompilerParams(vmem_limit_bytes=60 << 20),
    )(owners, params.reshape(-1, 1, 128))


class Place:
    def __init__(self):
        self.dp = lax.axis_index("dp")
        self.pipe = lax.axis_index("pipe")
        self.x, self.core = self.pipe // 2, self.pipe % 2
        self.z, self.y = self.dp // 2, self.dp % 2

    def device(self, x=None, core=None, z=None, y=None):
        x = self.x if x is None else x
        core = self.core if core is None else core
        z = self.z if z is None else z
        y = self.y if y is None else y
        return {"dp": 2 * z + y, "pipe": 2 * x + core}

    def enter(self):
        barrier = pltpu.get_barrier_semaphore()
        for step in range(1, 8):
            other = lax.rem(self.dp + step, 8)
            pl.semaphore_signal(
                barrier, inc=1, device_id={"dp": other, "pipe": self.pipe}, device_id_type=MESH
            )
        for step in range(1, 4):
            other = lax.rem(self.pipe + step, 4)
            pl.semaphore_signal(
                barrier, inc=1, device_id={"dp": self.dp, "pipe": other}, device_id_type=MESH
            )
        pl.semaphore_wait(barrier, 10)


def remote(src, dst, send, recv, target):
    return pltpu.make_async_remote_copy(
        src_ref=src, dst_ref=dst, send_sem=send, recv_sem=recv, device_id=target, device_id_type=MESH
    )


BIG_HALF = BIG_ROWS // 2
SMALL_HALF = SMALL_ROWS // 2
BULK_CUT = 960
LIGHT_CUT = 256
BACK_CUT = 1520
GATHER_ORDER = (
    "X0", "EY", "Z1", "EC0", "Y0", "X1", "EC1", "EC2", "Y1", "S0", "EC3", "R0", "L0", "Z2", "X2",
    "Z3", "Y2", "L1", "S1", "D0", "X3", "R1", "Y3", "S2", "L2", "R2", "D1", "S3", "M1", "R3", "M2",
    "D2", "D3", "M3",
)
REDUCE_ORDER = (
    "A0", "A1", "A2", "A3", "L0", "B0", "C0", "B1", "L1", "L2", "L3", "LS", "C1", "C2", "C3", "O0",
    "B2", "LE", "E0", "T1", "B3", "I0", "G", "O1", "I1", "E1", "O2", "E2", "I2", "T2", "T3", "O3",
)


def gather_kernel(big, small, ids, all_big, all_small, table, early, chunk, rising, falling,
                  early_send, early_recv, eu_send, eu_recv, ed_send, ed_recv,
                  z_send, z_recv, x_send, x_recv, y_send, y_recv, dx_send, dx_recv, dy_send, dy_recv,
                  s_send, s_recv, first_send, first_recv, own_sem, id_send, id_recv, lz_send, lz_recv):
    me = Place()
    me.enter()
    x, y, z, core = me.x, me.y, me.z, me.core
    up, down = me.device(z=z + 1), me.device(z=z - 1)
    x_side, y_side, sibling = me.device(x=1 - x), me.device(y=1 - y), me.device(core=1 - core)

    class Stream:
        def __init__(self, n, out, cut):
            self.n, self.out, self.cut, self.rows = n, out, cut, out.shape[3]

        def block(self, xo, origin, yo):
            return self.out.at[xo, 2 * origin + yo, core]

        def move_x(self, origin):
            block = self.block(x, origin, y)
            return remote(block, block, x_send.at[self.n, origin], x_recv.at[self.n, origin], x_side)

        def move_y(self, origin):
            block = self.block(x, origin, y)
            return remote(block, block, y_send.at[self.n, origin], y_recv.at[self.n, origin], y_side)

        def share(self, xo, origin, yo):
            block = self.block(xo, origin, yo)
            at = 8 * xo + 2 * origin + yo
            return remote(block, block, s_send.at[self.n, at], s_recv.at[self.n, at], sibling)

        def move_z(self, origin, target, way):
            block = self.block(x, origin, y)
            return remote(block, block, z_send.at[self.n, way, origin], z_recv.at[self.n, origin], target)

        def half_x(self, origin, xo, yo):
            part = self.out.at[xo, 2 * origin + yo, core, pl.ds(self.cut, self.rows - self.cut)]
            return remote(part, part, dx_send.at[self.n, origin], dx_recv.at[self.n, origin], x_side)

        def half_y(self, origin, xo, yo):
            part = self.out.at[xo, 2 * origin + yo, core, pl.ds(0, self.cut)]
            return remote(part, part, dy_send.at[self.n, origin], dy_recv.at[self.n, origin], y_side)

        def to_x(self, origin):
            self.move_x(origin).start()

        def to_y(self, origin):
            self.move_y(origin).start()

        def from_x(self, origin):
            self.move_x(origin).wait_recv()
            self.half_y(origin, 1 - x, y).start()
            self.share(1 - x, origin, y).start()

        def from_y(self, origin):
            self.move_y(origin).wait_recv()
            self.half_x(origin, x, 1 - y).start()
            self.share(x, origin, 1 - y).start()

        def from_diagonal(self, origin):
            self.half_x(origin, 1 - x, 1 - y).wait_recv()
            self.half_y(origin, 1 - x, 1 - y).wait_recv()
            self.share(1 - x, origin, 1 - y).start()

        def each(self, step, action):
            if step == 0:
                action(z)
            else:
                pl.when(z >= step)(lambda: action(z - step))
                pl.when(z + step <= 3)(lambda: action(z + step))

        def begin(self):
            pl.when(z < 3)(lambda: self.move_z(z, up, 0).start())
            pl.when(z > 0)(lambda: self.move_z(z, down, 1).start())
            self.share(x, z, y).start()

        def from_z(self, k):
            @pl.when(z >= k)
            def _():
                self.move_z(z - k, up, 0).wait_recv()
                pl.when(z < 3)(lambda: self.move_z(z - k, up, 0).start())
                self.share(x, z - k, y).start()

            @pl.when(z + k <= 3)
            def _():
                self.move_z(z + k, down, 1).wait_recv()
                pl.when(z > 0)(lambda: self.move_z(z + k, down, 1).start())
                self.share(x, z + k, y).start()

        def close(self):
            for origin in range(4):
                self.move_x(origin).wait_send()
                self.move_y(origin).wait_send()
                self.half_x(origin, x, 1 - y).wait_send()
                self.half_y(origin, 1 - x, y).wait_send()
                pl.when((z < 3) & (origin <= z))(lambda: self.move_z(origin, up, 0).wait_send())
                pl.when((z > 0) & (origin >= z))(lambda: self.move_z(origin, down, 1).wait_send())
            self.close_shares()

        def close_shares(self):
            for origin in range(4):
                for xo in range(2):
                    for yo in range(2):
                        self.share(xo, origin, yo).wait_send()
                        theirs = self.out.at[xo, 2 * origin + yo, 1 - core]
                        at = 8 * xo + 2 * origin + yo
                        remote(theirs, theirs, s_send.at[self.n, at], s_recv.at[self.n, at], sibling).wait_recv()

    class Late(Stream):
        def column_z(self, xo, origin, yo, target, way):
            block = self.block(xo, origin, yo)
            at = 2 * xo + yo
            return remote(
                block, block, lz_send.at[way, at, origin], lz_recv.at[at, origin], target
            )

        def leave(self, xo, yo):
            pl.when(z < 3)(lambda: self.column_z(xo, z, yo, up, 0).start())
            pl.when(z > 0)(lambda: self.column_z(xo, z, yo, down, 1).start())
            self.share(xo, z, yo).start()

        def step(self, k):
            if k == 0:
                self.move_x(z).start()
                self.move_y(z).start()
                self.leave(x, y)
            elif k == 1:
                self.move_x(z).wait_recv()
                self.half_y(z, 1 - x, y).start()
                self.leave(1 - x, y)
                self.move_y(z).wait_recv()
                self.half_x(z, x, 1 - y).start()
                self.leave(x, 1 - y)
            elif k == 2:
                self.half_x(z, 1 - x, 1 - y).wait_recv()
                self.half_y(z, 1 - x, 1 - y).wait_recv()
                self.leave(1 - x, 1 - y)
            else:
                gap = k - 2

                @pl.when(z >= gap)
                def _():
                    for xo, yo in columns:
                        self.column_z(xo, z - gap, yo, up, 0).wait_recv()
                        pl.when(z < 3)(lambda: self.column_z(xo, z - gap, yo, up, 0).start())
                        self.share(xo, z - gap, yo).start()

                @pl.when(z + gap <= 3)
                def _():
                    for xo, yo in columns:
                        self.column_z(xo, z + gap, yo, down, 1).wait_recv()
                        pl.when(z > 0)(lambda: self.column_z(xo, z + gap, yo, down, 1).start())
                        self.share(xo, z + gap, yo).start()

        def close(self):
            self.move_x(z).wait_send()
            self.move_y(z).wait_send()
            self.half_x(z, x, 1 - y).wait_send()
            self.half_y(z, 1 - x, y).wait_send()
            for origin in range(4):
                for xo, yo in columns:
                    pl.when((z < 3) & (origin <= z))(
                        lambda: self.column_z(xo, origin, yo, up, 0).wait_send())
                    pl.when((z > 0) & (origin >= z))(
                        lambda: self.column_z(xo, origin, yo, down, 1).wait_send())
            self.close_shares()

    columns = ((x, y), (1 - x, y), (x, 1 - y), (1 - x, 1 - y))
    bulk = Stream(0, all_big, BULK_CUT)
    light = Late(1, all_small, LIGHT_CUT)

    order = [
        jnp.where(z < 2, 3, 0),
        jnp.where(z == 0, 2, jnp.where(z == 1, 0, jnp.where(z == 2, 3, 1))),
        jnp.where(z == 0, 1, jnp.where(z == 1, 2, jnp.where(z == 2, 1, 2))),
        z,
    ]

    def cross(k):
        return remote(small.at[2 * order[k] + (1 - y)], early.at[k], early_send.at[k], early_recv.at[k], y_side)

    def own_early(k):
        return pltpu.make_async_copy(small.at[2 * order[k] + y], chunk.at[k], own_sem.at[3 + k])

    def rise(k):
        slot = order[k] - 1
        return remote(chunk.at[k], rising.at[slot], eu_send.at[slot], eu_recv.at[slot], up)

    def fall(k):
        slot = order[k]
        return remote(chunk.at[k], falling.at[slot], ed_send.at[slot], ed_recv.at[slot], down)

    def merge(k, ref, slot):
        @pl.loop(0, 3)
        def _(i):
            part = pl.ds(pl.multiple_of(352 * i, 16), 352)
            chunk[k, part, :] = (chunk[k, part, :].astype(FULL) + ref[slot, part, :].astype(FULL)).astype(LOW)

    big_half = all_big.at[x, me.dp, 1]
    big_first = remote(big.at[pl.ds(BIG_HALF, BIG_HALF)], big_half, first_send.at[0], first_recv.at[0], sibling)
    small_half = all_small.at[x, me.dp, 0]
    small_first = remote(
        chunk.at[3, pl.ds(0, SMALL_HALF)], small_half, first_send.at[1], first_recv.at[1], sibling)

    def early_cross():
        @pl.when(core == 1)
        def _():
            for k in range(4):
                own_early(k).wait()
                cross(k).wait_recv()
                merge(k, early, k)

    def early_chain(k):
        @pl.when(core == 1)
        def _():
            if k < 3:

                @pl.when(order[k] > z)
                def _():
                    @pl.when(z > 0)
                    def _():
                        rise(k).wait_recv()
                        merge(k, rising, order[k] - 1)

                    rise(k).start()

                @pl.when(order[k] < z)
                def _():
                    @pl.when(z < 3)
                    def _():
                        fall(k).wait_recv()
                        merge(k, falling, order[k])

                    fall(k).start()

            else:

                @pl.when(z > 0)
                def _():
                    rise(k).wait_recv()
                    merge(k, rising, z - 1)

                @pl.when(z < 3)
                def _():
                    fall(k).wait_recv()
                    merge(k, falling, z)

                small_first.start()
                copy = pltpu.make_async_copy(
                    chunk.at[3, pl.ds(SMALL_HALF, SMALL_HALF)], all_small.at[x, me.dp, 1], own_sem.at[0])
                copy.start()
                copy.wait()

    def light_begin():
        @pl.when(core == 0)
        def _():
            small_first.wait_recv()

        light.step(0)

    @pl.when(core == 0)
    def _():
        big_first.start()
        copy = pltpu.make_async_copy(big.at[pl.ds(0, BIG_HALF)], all_big.at[x, me.dp, 0], own_sem.at[0])
        copy.start()
        copy.wait()

    @pl.when(core == 1)
    def _():
        for k in range(4):
            cross(k).start()
            own_early(k).start()
        big_first.wait_recv()

    bulk.begin()
    row = pltpu.make_async_copy(ids, table.at[me.pipe], own_sem.at[2])
    row.start()
    for step in range(1, 4):
        remote(
            ids, table.at[me.pipe], id_send.at[step], id_recv.at[step],
            {"dp": me.dp, "pipe": lax.rem(me.pipe + step, 4)},
        ).start()

    actions = {"EY": early_cross, "L0": light_begin}
    for k in range(4):
        actions["EC%d" % k] = functools.partial(early_chain, k)
        actions["X%d" % k] = functools.partial(bulk.each, k, bulk.to_x)
        actions["Y%d" % k] = functools.partial(bulk.each, k, bulk.to_y)
        actions["S%d" % k] = functools.partial(bulk.each, k, bulk.from_x)
        actions["R%d" % k] = functools.partial(bulk.each, k, bulk.from_y)
        actions["D%d" % k] = functools.partial(bulk.each, k, bulk.from_diagonal)
        if k:
            actions["Z%d" % k] = functools.partial(bulk.from_z, k)
            actions["M%d" % k] = functools.partial(light.step, k + 2)
            if k < 3:
                actions["L%d" % k] = functools.partial(light.step, k)
    for event in GATHER_ORDER:
        actions[event]()
    bulk.close()
    light.close()
    row.wait()
    for step in range(1, 4):
        here = lax.rem(me.pipe + 4 - step, 4)
        move = remote(
            ids, table.at[here], id_send.at[step], id_recv.at[step],
            {"dp": me.dp, "pipe": lax.rem(me.pipe + step, 4)},
        )
        move.wait_recv()
        move.wait_send()

    @pl.when(core == 0)
    def _():
        big_first.wait_send()

    @pl.when(core == 1)
    def _():
        small_first.wait_send()
        for k in range(4):
            cross(k).wait_send()
        for k in range(3):
            pl.when(order[k] > z)(lambda: rise(k).wait_send())
            pl.when(order[k] < z)(lambda: fall(k).wait_send())


def gather_all(big, small, ids):
    sem = pltpu.SemaphoreType.DMA
    return pl.pallas_call(
        gather_kernel,
        name="gather_all",
        out_shape=(
            jax.ShapeDtypeStruct((2, 8, 2, BIG_HALF, 128), LOW),
            jax.ShapeDtypeStruct((2, 8, 2, SMALL_HALF, 128), LOW),
            jax.ShapeDtypeStruct((4, 8, 128), jnp.int32),
        ),
        in_specs=[any_spec()] * 3,
        out_specs=(any_spec(),) * 3,
        scratch_shapes=[
            pltpu.VMEM((4, SMALL_ROWS, 128), LOW), pltpu.VMEM((4, SMALL_ROWS, 128), LOW),
            pltpu.VMEM((3, SMALL_ROWS, 128), LOW), pltpu.VMEM((3, SMALL_ROWS, 128), LOW),
            sem((4,)), sem((4,)), sem((3,)), sem((3,)), sem((3,)), sem((3,)),
            sem((2, 2, 4)), sem((2, 4)),
            sem((2, 4)), sem((2, 4)), sem((2, 4)), sem((2, 4)),
            sem((2, 4)), sem((2, 4)), sem((2, 4)), sem((2, 4)),
            sem((2, 16)), sem((2, 16)),
            sem((2,)), sem((2,)), sem((7,)), sem((4,)), sem((4,)), sem((2, 4, 4)), sem((4, 4)),
        ],
        compiler_params=pltpu.CompilerParams(
            collective_id=0, has_side_effects=True, vmem_limit_bytes=60 << 20
        ),
    )(big, small.reshape(8, SMALL_ROWS, 128), ids)


def soft(value):
    return jnp.maximum(value, 0.0) + jnp.log1p(jnp.exp(-jnp.abs(value)))


def gate_of(value):
    small = jnp.exp(-jnp.abs(value))
    share = 1.0 / (1.0 + small)
    return jnp.where(value >= 0, share, small * share)


def standardize(z):
    count = z.shape[0]
    centre = jnp.sum(z, axis=0, keepdims=True) / count
    away = z - centre
    spread = jnp.sum(away * away, axis=0, keepdims=True) / count
    inverse = lax.rsqrt(spread + NORM_EPS)
    return away * inverse, centre, spread, inverse


def unstandardize(grad, standard, gain, inverse):
    count = grad.shape[0]
    grad_sum = jnp.sum(grad, axis=0, keepdims=True)
    grad_dot = jnp.sum(grad * standard, axis=0, keepdims=True)
    result = gain * inverse * (grad - grad_sum / count - standard * (grad_dot / count))
    return result, grad_dot, grad_sum


def pad_low(value):
    zeros = jnp.zeros((PADDED - ROWS, value.shape[1]), FULL)
    return jnp.concatenate([value, zeros], axis=0).astype(LOW)


def mul(a, b):
    return jnp.dot(a, b, preferred_element_type=FULL)


def mul_t(a, b):
    return lax.dot_general(a, b, (((1,), (1,)), ((), ())), preferred_element_type=FULL)


def narrow_part(ref, start, count, blocks=range(4)):
    return jnp.concatenate(
        [ref[pl.ds(start, count), 64 * j : 64 * j + 64, :].reshape(64 * count, 128) for j in blocks],
        axis=1,
    )


def put_narrow(ref, start, count, value):
    for j in range(4):
        ref[pl.ds(start, count), 64 * j : 64 * j + 64, :] = (
            value[:, 128 * j : 128 * j + 128].astype(LOW).reshape(count, 64, 128)
        )


def wide_part(ref, start, count, c):
    return jnp.concatenate(
        [
            ref[start : start + count, 32 * c + 16 * h : 32 * c + 16 * h + 16, :].reshape(
                16 * count, 128
            )
            for h in range(2)
        ],
        axis=1,
    )


def put_wide(ref, start, count, c, value):
    for h in range(2):
        ref[start : start + count, 32 * c + 16 * h : 32 * c + 16 * h + 16, :] = (
            value[:, 128 * h : 128 * h + 128].astype(LOW).reshape(count, 16, 128)
        )


def chunks(count):
    def run(body):
        for c in range(count):
            body(c)

    return run


def step_kernel(table, gates, teach_ids, stud_ids, all_big, all_small, x, targets, grid,
                wide0, wide1, final, stats, grad_x, out_big, out_small,
                w0, w1, w2, w3, edges, loose, vec, grad_vec, raw,
                std_a, std_b, std_p, std_1, std_c, std_d, hidden, cols0, cols2,
                nar0, nar2, turned, relay, dz_a, dz_n, acc, acc_x, grad_h,
                wanted, inv, in_sem, edge_sem, out_sem):
    rank = lax.axis_index("pipe")
    gate = gates[rank].astype(FULL)
    for group in range(2):
        for j in range(8):
            inv[8 * group + table[2 * group, 0, j]] = j
    picks = [teach_ids[k, rank] for k in range(2)] + [stud_ids[rank, k] for k in range(3)]
    rows = [
        pltpu.make_async_copy(targets.at[pl.ds(pick, 1)], wanted.at[pl.ds(k, 1)], edge_sem.at[12 + k])
        for k, pick in enumerate(picks)
    ]
    for fetched in rows:
        fetched.start()
    weights = (w0, w1, w2, w3)
    loads = {0: [], 1: [], 2: [], 3: []}
    front, split = w0.reshape(USED_TILES[0] * TILE, 128), w2.reshape(115 * TILE, 128)
    for group, weight, blocks in ((0, front, 8), (1, split, 6)):
        for b in range(blocks):
            at, here = 8 * group + b, inv[8 * group + b]
            count = min(STRIDE, VEC_TILE[2 * group] + 1 - STRIDE * b) * TILE
            loads[2 * group].append(pltpu.make_async_copy(
                all_big.at[group, here, pl.ds(0, count)], weight.at[pl.ds(STRIDE * TILE * b, count)],
                in_sem.at[0, at]))
            if b < blocks - 1:
                loads[2 * group].append(pltpu.make_async_copy(
                    all_big.at[group, here, pl.ds(STRIDE * TILE, EDGE)], edges.at[7 * group + b],
                    edge_sem.at[7 * group + b]))
            elif group == 0:
                loads[0].append(pltpu.make_async_copy(
                    all_big.at[0, here, pl.ds(STRIDE * TILE, EDGE)],
                    front.at[pl.ds(VEC_TILE[0] * TILE, EDGE)], edge_sem.at[17]))
    loads[1].append(pltpu.make_async_copy(all_small.at[0], w1, in_sem.at[0, 14]))
    loads[3].append(pltpu.make_async_copy(all_small.at[1], w3, in_sem.at[0, 15]))
    for section in range(4):
        for load in loads[section]:
            load.start()

    raw[...] = jnp.zeros_like(raw)
    loose[...] = jnp.zeros_like(loose)
    grad_vec[...] = jnp.zeros_like(grad_vec)

    def edge_parts(tile, is_narrow):
        count, size = (4, 64) if is_narrow else (16, 16)
        for j in range(count):
            yield pl.ds(j, 16, count), slice(size * j, size * j + 16)

    def is_narrow(section, tile):
        return section == 2 or tile < FRONT_WIDE

    def merge_edge(section, tile, at):
        ref = weights[section]
        loose[0:EDGE, :] = edges[at].astype(FULL)
        for lying, here in edge_parts(tile, is_narrow(section, tile)):
            ref[tile, here, :] = (ref[tile, here, :].astype(FULL) + loose[lying, :]).astype(LOW)

    def take_edge(section, tile, at):
        ref = weights[section]
        for lying, here in edge_parts(tile, is_narrow(section, tile)):
            loose[lying, :] = ref[tile, here, :].astype(FULL)
        edges[at] = loose[0:EDGE, :].astype(LOW)

    def settle(section, blocks=None):
        if section == 0:
            for b in blocks:
                for load in loads[0][2 * b : 2 * b + 2]:
                    load.wait()
            if 7 in blocks:
                vec[0] = w0[VEC_TILE[0], 0:48, :].astype(FULL)
            else:
                for b in range(7):
                    merge_edge(0, 19 * b + 19, b)
            return
        for load in loads[section]:
            load.wait()
        if section == 2:
            for b in range(5):
                merge_edge(2, 19 * b + 19, 7 + b)
        vec[section] = weights[section][VEC_TILE[section], 0:48, :].astype(FULL)

    def row(section, start):
        return jnp.concatenate(
            [vec[section, pl.ds(start + h, 1), :] for h in range(2)], axis=1
        )

    def put_row(section, start, value):
        for h in range(2):
            grad_vec[section, pl.ds(start + h, 1), :] = value[:, 128 * h : 128 * h + 128]

    def put_stats(section, column, centre, spread):
        raw[2 * section : 2 * section + 1, pl.ds(column, 256)] = centre
        raw[2 * section + 1 : 2 * section + 2, pl.ds(column, 256)] = spread

    def inverse_of(section, column):
        return lax.rsqrt(raw[2 * section + 1 : 2 * section + 2, pl.ds(column, 256)] + NORM_EPS)

    def lanes(c):
        return slice(256 * c, 256 * c + 256)

    at_row, at_col, side = grid[0], grid[1], grid[2]

    def masked(value, dr, dc):
        ok = (at_row + dr >= 0) & (at_row + dr < side) & (at_col + dc >= 0) & (at_col + dc < side)
        return jnp.concatenate(
            [jnp.where(ok, value[:, 128 * j : 128 * j + 128], 0.0) for j in range(4)], axis=1
        )

    def rolled(value, sign, dr, dc):
        parts = []
        for start, end, across, down in ((0, TEACH_ROWS, 2, 12), (TEACH_ROWS, ROWS, 1, 4)):
            by = (sign * (dr * down + dc * across)) % (end - start)
            part = value[start:end]
            parts.append(part if by == 0 else pltpu.roll(part, by, 0))
        return jnp.concatenate(parts, axis=0)

    def taps(stride):
        for t in range(9):
            r, q = t // 3, t % 3
            if stride == 1:
                yield t, 0, r - 1, q - 1
            else:
                phase = 2 * (1 if r != 1 else 0) + (1 if q != 1 else 0)
                yield t, phase, -1 if r == 0 else 0, -1 if q == 0 else 0

    settle(0, (0, 7))
    whole_x = x[...].reshape(4 * PADDED, C_IN)
    for c in range(2):
        z = mul(whole_x, narrow_part(w0, 0, 16, (2 * c, 2 * c + 1)))
        z = jnp.concatenate([z[PADDED * p : PADDED * p + ROWS] for p in range(4)], axis=0)
        standard, centre, spread, _ = standardize(z)
        put_stats(0, 256 * c, centre, spread)
        std_a[:, 256 * c : 256 * c + 256] = standard
        hidden[:, 256 * c : 256 * c + 256] = (
            soft(row(0, 2 * c) * standard + row(0, 4 + 2 * c)).astype(LOW).astype(FULL)
        )

    for t, phase, dr, dc in taps(2):
        cols0[t] = pad_low(masked(rolled(hidden[ROWS * phase : ROWS * phase + ROWS, :], -1, dr, dc), dr, dc))
    acc[...] = jnp.zeros_like(acc)
    settle(0, (1, 2, 3, 4, 5, 6))

    @chunks(9)
    def _(t):
        acc[...] += mul(cols0[t], narrow_part(w0, 16 + 8 * t, 8))

    def middle(section, std, nar):
        for c in range(2):
            at = slice(256 * c, 256 * c + 256)
            standard, centre, spread, _ = standardize(acc[0:ROWS, at])
            put_stats(section, MID + 256 * c, centre, spread)
            std[:, at] = standard
            nar[:, at] = pad_low(soft(row(section, 8 + 2 * c) * standard + row(section, 12 + 2 * c)))

    middle(0, std_b, nar0)
    acc[...] = jnp.zeros_like(acc)
    settle(1)
    settle(2)

    @chunks(8)
    def _(c):
        at = lanes(c)
        standard, centre, spread, _ = standardize(mul(x[0], wide_part(w0, FRONT_WIDE, 64, c))[0:ROWS])
        put_stats(0, 2 * MID + 256 * c, centre, spread)
        std_p[:, at] = standard
        low = pad_low(row(0, 16 + 2 * c) * standard + row(0, 32 + 2 * c))
        wide0[:, at] = low
        standard, centre, spread, _ = standardize(mul(nar0[...], wide_part(w1, 0, 32, c))[0:ROWS])
        put_stats(1, 256 * c, centre, spread)
        std_1[:, at] = standard
        pre = low.astype(FULL)[0:ROWS] + row(1, 2 * c) * standard + row(1, 16 + 2 * c)
        low = pad_low(soft(pre))
        wide1[:, at] = low
        acc[...] += mul(low, narrow_part(w2, 4 * c, 4))

    for c in range(2):
        at = slice(256 * c, 256 * c + 256)
        standard, centre, spread, _ = standardize(acc[0:ROWS, at])
        put_stats(2, 256 * c, centre, spread)
        std_c[:, at] = standard
        hidden[0:ROWS, at] = soft(row(2, 2 * c) * standard + row(2, 4 + 2 * c)).astype(LOW).astype(FULL)
    for t, phase, dr, dc in taps(1):
        cols2[t] = pad_low(masked(rolled(hidden[0:ROWS, :], -1, dr, dc), dr, dc))
    acc[...] = jnp.zeros_like(acc)

    @chunks(9)
    def _(t):
        acc[...] += mul(cols2[t], narrow_part(w2, 32 + 8 * t, 8))

    middle(2, std_d, nar2)

    turned[...] = nar2[...].T
    acc[...] = jnp.zeros_like(acc)
    settle(3)
    for fetched in rows:
        fetched.wait()

    first_crop = lax.rem(lax.broadcasted_iota(jnp.int32, (TEACH_ROWS, 256), 0), 2) == 0

    def spread_rows(values):
        first, second = (jnp.broadcast_to(value, (TEACH_ROWS, 256)) for value in values[0:2])
        parts = [jnp.where(first_crop, first, second)]
        parts.extend(jnp.broadcast_to(value, (16, 256)) for value in values[2:5])
        return jnp.concatenate(parts, axis=0)

    def crop_sums(value):
        def total(part):
            return jnp.sum(part, axis=0, keepdims=True)

        teach = value[0:TEACH_ROWS]
        return [
            total(jnp.where(first_crop, teach, 0.0)),
            total(jnp.where(first_crop, 0.0, teach)),
            total(value[72:88]),
            total(value[88:104]),
            total(value[104:120]),
        ]

    @chunks(8)
    def _(c):
        at = lanes(c)
        weight = wide_part(w3, 0, 32, c)
        standard, centre, spread, inverse = standardize(mul(nar2[...], weight)[0:ROWS])
        put_stats(3, 256 * c, centre, spread)
        gain = row(3, 2 * c)
        before = wide1[:, at].astype(FULL)[0:ROWS]
        pre = before + gain * standard + row(3, 16 + 2 * c)
        ending = jnp.where(gate > 0, soft(pre), before)
        final[:, at] = pad_low(ending)
        square = ending * ending
        factors = []
        for crop, total in enumerate(crop_sums(square * ending)):
            mean = total / (36.0 if crop < 2 else 16.0) + POOL_EPS
            factors.append(jnp.exp(jnp.log(mean) * (-2.0 / 3.0)) * wanted[crop : crop + 1, at])
        cotangent = spread_rows(factors) * square
        grad_pre = cotangent * gate_of(pre) * gate
        relay[:, at] = pad_low(grad_pre + cotangent * (1.0 - gate))
        result, grad_gain, grad_bias = unstandardize(grad_pre, standard, gain, inverse)
        put_row(3, 2 * c, grad_gain)
        put_row(3, 16 + 2 * c, grad_bias)
        low = pad_low(result)
        acc[...] += mul_t(low, weight)
        put_wide(w3, 0, 32, c, mul(turned[...], low))

    def flush(section):
        weights[section][VEC_TILE[section]] = grad_vec[section].astype(LOW)

    flush(3)
    stores = [pltpu.make_async_copy(w3, out_small.at[1], out_sem.at[16])]
    stores[-1].start()

    def middle_back(section, std):
        for c in range(2):
            at = slice(256 * c, 256 * c + 256)
            gain, bias = row(section, 8 + 2 * c), row(section, 12 + 2 * c)
            grad = acc[0:ROWS, at].astype(LOW).astype(FULL) * gate_of(gain * std[:, at] + bias)
            result, grad_gain, grad_bias = unstandardize(
                grad, std[:, at], gain, inverse_of(section, MID + 256 * c)
            )
            put_row(section, 8 + 2 * c, grad_gain)
            put_row(section, 12 + 2 * c, grad_bias)
            dz_n[:, at] = pad_low(result)

    def taps_back(weight, start, cols, stride, phases):
        grad_h[0 : ROWS * phases, :] = jnp.zeros((ROWS * phases, MID), FULL)
        for t, phase, dr, dc in taps(stride):
            part = mul_t(dz_n[...], narrow_part(weight, start + 8 * t, 8))[0:ROWS]
            at = slice(ROWS * phase, ROWS * phase + ROWS)
            grad_h[at, :] += rolled(masked(part, dr, dc), 1, dr, dc)
            put_narrow(weight, start + 8 * t, 8, mul(cols[t].T, dz_n[...]))

    middle_back(2, std_d)
    taps_back(w2, 32, cols2, 1, 1)
    for c in range(2):
        at = slice(256 * c, 256 * c + 256)
        gain, bias = row(2, 2 * c), row(2, 4 + 2 * c)
        grad = grad_h[0:ROWS, at] * gate_of(gain * std_c[:, at] + bias)
        result, grad_gain, grad_bias = unstandardize(grad, std_c[:, at], gain, inverse_of(2, 256 * c))
        put_row(2, 2 * c, grad_gain)
        put_row(2, 4 + 2 * c, grad_bias)
        dz_n[:, at] = pad_low(result)
    turned[...] = nar0[...].T
    acc[...] = jnp.zeros_like(acc)
    acc_x[...] = jnp.zeros_like(acc_x)

    @chunks(8)
    def _(c):
        at = lanes(c)
        low = dz_n[...]
        grad = relay[:, at].astype(FULL) + mul_t(low, narrow_part(w2, 4 * c, 4))
        put_narrow(w2, 4 * c, 4, mul(wide1[:, at].T, low))
        grad = grad.astype(LOW).astype(FULL)[0:ROWS]
        gain = row(1, 2 * c)
        pre = wide0[:, at].astype(FULL)[0:ROWS] + gain * std_1[:, at] + row(1, 16 + 2 * c)
        grad = grad * gate_of(pre)
        result, grad_gain, grad_bias = unstandardize(
            grad, std_1[:, at], gain, inverse_of(1, 256 * c)
        )
        put_row(1, 2 * c, grad_gain)
        put_row(1, 16 + 2 * c, grad_bias)
        low = pad_low(result)
        acc[...] += mul_t(low, wide_part(w1, 0, 32, c))
        put_wide(w1, 0, 32, c, mul(turned[...], low))
        grad = grad.astype(LOW).astype(FULL)
        result, grad_gain, grad_bias = unstandardize(
            grad, std_p[:, at], row(0, 16 + 2 * c), inverse_of(0, 2 * MID + 256 * c)
        )
        put_row(0, 16 + 2 * c, grad_gain)
        put_row(0, 32 + 2 * c, grad_bias)
        low = pad_low(result)
        acc_x[...] += mul_t(low, wide_part(w0, FRONT_WIDE, 64, c))
        put_wide(w0, FRONT_WIDE, 64, c, mul(x[0].T, low))

    flush(1)
    flush(2)
    w2[105:115] = jnp.zeros((10, TILE, 128), LOW)
    stores.append(pltpu.make_async_copy(w1, out_small.at[0], out_sem.at[17]))
    stores[-1].start()
    def store(source, group, b, start, semaphore):
        count = source.shape[0]
        stores.append(pltpu.make_async_copy(
            source, out_big.at[group, inv[8 * group + b], pl.ds(start, count)], out_sem.at[semaphore]))
        stores[-1].start()

    for b in range(8):
        if b < 5:
            take_edge(2, 19 * b + 19, 7 + b)
            store(split.at[pl.ds(STRIDE * TILE * b, STRIDE * TILE)], 1, b, 0, 8 + b)
            store(edges.at[7 + b], 1, b, STRIDE * TILE, 20 + b)
        else:
            first = 95 if b == 5 else 105
            store(split.at[pl.ds(TILE * first, 10 * TILE)], 1, b, 0, 8 + b)
            store(split.at[pl.ds(TILE * 105, BIG_ROWS - 10 * TILE)], 1, b, 10 * TILE, 20 + b)

    def store_front(blocks):
        for b in blocks:
            if b == 7:
                edges[12] = w0[VEC_TILE[0], 0:EDGE, :]
            else:
                take_edge(0, 19 * b + 19, b)
            store(front.at[pl.ds(STRIDE * TILE * b, STRIDE * TILE)], 0, b, 0, b)
            store(edges.at[12 if b == 7 else b], 0, b, STRIDE * TILE, 28 + b)

    store_front((5, 6))
    middle_back(0, std_b)
    taps_back(w0, 16, cols0, 2, 4)
    store_front((1, 2, 3, 4))
    for c in range(2):
        at = slice(256 * c, 256 * c + 256)
        gain, bias = row(0, 2 * c), row(0, 4 + 2 * c)
        grad = grad_h[:, at] * gate_of(gain * std_a[:, at] + bias)
        result, grad_gain, grad_bias = unstandardize(grad, std_a[:, at], gain, inverse_of(0, 256 * c))
        put_row(0, 2 * c, grad_gain)
        put_row(0, 4 + 2 * c, grad_bias)
        for p in range(4):
            dz_a[PADDED * p : PADDED * p + PADDED, at] = pad_low(result[ROWS * p : ROWS * p + ROWS])

    @chunks(4)
    def _(c):
        at = lanes(c)
        low = dz_a[...]
        part = mul_t(low, narrow_part(w0, 4 * c, 4))
        grad_x[0, :, at] = (part[0:PADDED] + acc_x[:, at]).astype(LOW)
        for p in range(1, 4):
            grad_x[p, :, at] = part[PADDED * p : PADDED * p + PADDED].astype(LOW)
        turned_x = x[:, :, at].reshape(4 * PADDED, 256).T
        put_narrow(w0, 4 * c, 4, mul(turned_x, low))

    flush(0)
    store_front((0, 7))
    for section in range(4):
        part = raw[2 * section : 2 * section + 2]
        stats[section, 0:2] = part if section < 2 else part * gate
        stats[section, 2:8] = jnp.zeros((6, 2 * MID + C_OUT), FULL)
    for store in stores:
        store.wait()


def run_step(table, gates, teach_ids, stud_ids, all_big, all_small, phases, targets):
    spots = np.zeros((3, ROWS, 128), np.int32)
    for r in range(ROWS):
        width = 6 if r < TEACH_ROWS else 4
        at = r // 2 if r < TEACH_ROWS else (r - TEACH_ROWS) % 16
        spots[0, r], spots[1, r], spots[2, r] = at // width, at % width, width
    sem = pltpu.SemaphoreType.DMA
    wide = jax.ShapeDtypeStruct((PADDED, C_OUT), LOW)
    vm = pltpu.VMEM
    return pl.pallas_call(
        step_kernel,
        name="step",
        out_shape=(
            wide, wide, wide,
            jax.ShapeDtypeStruct((4, 8, 2 * MID + C_OUT), FULL),
            jax.ShapeDtypeStruct((4, PADDED, C_IN), LOW),
            jax.ShapeDtypeStruct((2, 8, BIG_ROWS, 128), LOW),
            jax.ShapeDtypeStruct((2, USED_TILES[1], TILE, 128), LOW),
        ),
        in_specs=[smem_spec()] * 4 + [any_spec(), any_spec(), vmem_spec(), any_spec(), vmem_spec()],
        out_specs=(vmem_spec(),) * 5 + (any_spec(),) * 2,
        scratch_shapes=[
            vm((153, TILE, 128), LOW), vm((33, TILE, 128), LOW), vm((115, TILE, 128), LOW), vm((33, TILE, 128), LOW),
            vm((13, EDGE, 128), LOW), vm((TILE, 128), FULL), vm((4, 48, 128), FULL), vm((4, TILE, 128), FULL),
            vm((8, 2 * MID + C_OUT), FULL),
            vm((4 * ROWS, MID), FULL), vm((ROWS, MID), FULL), vm((ROWS, C_OUT), FULL), vm((ROWS, C_OUT), FULL),
            vm((ROWS, MID), FULL), vm((ROWS, MID), FULL), vm((4 * ROWS, MID), FULL),
            vm((9, PADDED, MID), LOW), vm((9, PADDED, MID), LOW),
            vm((PADDED, MID), LOW), vm((PADDED, MID), LOW), vm((MID, PADDED), LOW),
            vm((PADDED, C_OUT), LOW), vm((4 * PADDED, MID), LOW), vm((PADDED, MID), LOW),
            vm((PADDED, MID), FULL), vm((PADDED, C_IN), FULL), vm((4 * ROWS, MID), FULL),
            vm((8, C_OUT), FULL), pltpu.SMEM((16,), jnp.int32),
            sem((2, 16)), sem((18,)), sem((36,)),
        ],
        compiler_params=pltpu.CompilerParams(vmem_limit_bytes=60 << 20),
    )(table, gates, teach_ids, stud_ids, all_big, all_small, phases, targets, jnp.asarray(spots))


def reduce_kernel(big, small, wide0, wide1, final, stats, table,
                  out_big, out_small, segments, out_stats, norm, factor,
                  got, halves_x, halves_y, from_x, from_y, from_low, from_high, stage, total,
                  l_got, l_stage, l_low, l_high, l_halves_x, l_halves_y, l_from_x, l_from_y, l_total,
                  late, late_half, owner_row, by_pipe, by_dp, mine, part_sum,
                  s_send, s_recv, hx_send, hx_recv, hy_send, hy_recv, x_send, x_recv, y_send, y_recv,
                  zu_send, zu_recv, zd_send, zd_recv, lu_send, lu_recv, ld_send, ld_recv,
                  stage_sem, l_stage_sem, out_sem, late_send, late_recv, join_send, join_recv,
                  seg_send, seg_recv, stat_send, stat_recv, p_send, p_recv, d_send, d_recv):
    me = Place()
    me.enter()
    x, y, z, core = me.x, me.y, me.z, me.core
    up, down = me.device(z=z + 1), me.device(z=z - 1)
    x_side, y_side, sibling = me.device(x=1 - x), me.device(y=1 - y), me.device(core=1 - core)
    order = [
        jnp.where(z < 2, 3, 0),
        jnp.where(z == 0, 2, jnp.where(z == 1, 0, jnp.where(z == 2, 3, 1))),
        jnp.where(z == 0, 1, jnp.where(z == 1, 2, jnp.where(z == 2, 1, 2))),
        z,
    ]
    columns = ((1 - x, 1 - y), (x, 1 - y), (1 - x, y), (x, y))
    groups = {"A": (0,), "C": (1,), "B": (2,), "O": (3,)}
    sequence = [
        (group, int(event[1])) for event in REDUCE_ORDER for group in groups.get(event[0], ())
    ]
    l_sequence = [(group, k) for k in range(4) for group in range(4)]

    def all_of(copies, act):
        for copy in copies:
            act(copy)

    def over(start, count, piece):
        whole = count // 512
        if whole:

            @pl.loop(0, whole)
            def _(i):
                piece(pl.multiple_of(start + 512 * i, 16), 512)

        if count % 512:
            piece(start + 512 * whole, count % 512)

    def source(array, group, k, half):
        xo, yo = columns[group]
        return array.at[xo, 2 * order[k] + yo, half]

    def share(group, k):
        at = 4 * group + k
        return remote(source(big, group, k, 1 - core), got.at[at], s_send.at[0, at], s_recv.at[0, at], sibling)

    def l_share(group, k):
        at = 4 * group + k
        return remote(source(small, group, k, 1 - core), l_got.at[at], s_send.at[1, at], s_recv.at[1, at], sibling)

    def fetch(n):
        return pltpu.make_async_copy(source(big, *sequence[n], core), stage.at[n % 4], stage_sem.at[n % 4])

    def l_fetch(group, k):
        at = 4 * group + k
        return pltpu.make_async_copy(source(small, group, k, core), l_stage.at[at], l_stage_sem.at[at])

    def add(target, at, other, slot, start, count, extras):
        def piece(begin, size):
            part = pl.ds(begin, size)
            sums = target[at, part, :].astype(FULL) + other[slot, part, :].astype(FULL)
            for ref, k in extras:
                sums = sums + ref[k, pl.ds(begin - start, size), :].astype(FULL)
            target[at, part, :] = sums.astype(LOW)

        over(start, count, piece)

    def send_half_x(k):
        return remote(got.at[k, pl.ds(BACK_CUT, BIG_HALF - BACK_CUT)], halves_x.at[k],
                      hx_send.at[k], hx_recv.at[k], x_side)

    def send_half_y(k):
        return remote(got.at[k, pl.ds(0, BACK_CUT)], halves_y.at[k], hy_send.at[k], hy_recv.at[k], y_side)

    def send_y(k):
        return remote(got.at[4 + k], from_y.at[k], y_send.at[k], y_recv.at[k], y_side)

    def send_x(k):
        return remote(got.at[8 + k], from_x.at[k], x_send.at[k], x_recv.at[k], x_side)

    def send_up(at, zd):
        return remote(got.at[at], from_low.at[zd - 1], zu_send.at[zd - 1], zu_recv.at[zd - 1], up)

    def send_down(at, zd):
        return remote(got.at[at], from_high.at[zd], zd_send.at[zd], zd_recv.at[zd], down)

    def l_column(group):
        xo, yo = columns[group]
        return 2 * xo + yo

    def l_up(group, k):
        at, zd = l_column(group), order[k] - 1
        return remote(l_got.at[4 * group + k], l_low.at[at, zd], lu_send.at[at, zd], lu_recv.at[at, zd], up)

    def l_down(group, k):
        at, zd = l_column(group), order[k]
        return remote(l_got.at[4 * group + k], l_high.at[at, zd], ld_send.at[at, zd], ld_recv.at[at, zd], down)

    def l_half_x():
        return remote(l_got.at[3, pl.ds(LIGHT_CUT, SMALL_HALF - LIGHT_CUT)], l_halves_x,
                      hx_send.at[4], hx_recv.at[4], x_side)

    def l_half_y():
        return remote(l_got.at[3, pl.ds(0, LIGHT_CUT)], l_halves_y, hy_send.at[4], hy_recv.at[4], y_side)

    def l_send_y():
        return remote(l_got.at[7], l_from_y, y_send.at[4], y_recv.at[4], y_side)

    def l_send_x():
        return remote(l_got.at[11], l_from_x, x_send.at[4], x_recv.at[4], x_side)

    leaving = (wide0, wide1, wide1, final)

    def exchange(section):
        target = {"dp": me.dp, "pipe": section}
        yield remote(leaving[section], segments.at[me.pipe], seg_send.at[section], seg_recv.at[me.pipe], target)
        yield remote(stats.at[section], out_stats.at[me.pipe], stat_send.at[section], stat_recv.at[me.pipe], target)

    def keep(section):
        yield pltpu.make_async_copy(leaving[section], segments.at[me.pipe], seg_send.at[section])
        yield pltpu.make_async_copy(stats.at[section], out_stats.at[me.pipe], stat_send.at[section])

    def arriving(micro):
        target = {"dp": me.dp, "pipe": micro}
        yield remote(wide0, segments.at[micro], seg_send.at[micro], seg_recv.at[micro], target)
        yield remote(stats.at[0], out_stats.at[micro], stat_send.at[micro], stat_recv.at[micro], target)

    for n in range(16):
        share(*sequence[n]).start()
        if n == 3:
            for item in l_sequence:
                l_share(*item).start()
    for n in range(2):
        fetch(n).start()
    for group, k in l_sequence:
        l_fetch(group, k).start()
    row_copy = pltpu.make_async_copy(table.at[2 * x], owner_row, out_sem.at[2])
    row_copy.start()

    def bulk_item(n):
        group, k = sequence[n]
        at, slot = 4 * group + k, n % 4
        if n + 2 < 16:
            fetch(n + 2).start()
        fetch(n).wait()
        share(group, k).wait_recv()
        if group == 0:
            add(got, at, stage, slot, 0, BIG_HALF, [])
            send_half_x(k).start()
            send_half_y(k).start()
        elif group == 1:
            send_half_x(k).wait_recv()
            add(got, at, stage, slot, 0, BACK_CUT, [])
            add(got, at, stage, slot, BACK_CUT, BIG_HALF - BACK_CUT, [(halves_x, k)])
            send_y(k).start()
        elif group == 2:
            send_half_y(k).wait_recv()
            add(got, at, stage, slot, 0, BACK_CUT, [(halves_y, k)])
            add(got, at, stage, slot, BACK_CUT, BIG_HALF - BACK_CUT, [])
            send_x(k).start()
        else:
            send_x(k).wait_recv()
            send_y(k).wait_recv()
            add(got, at, stage, slot, 0, BIG_HALF, [(from_x, k), (from_y, k)])

    def bulk_z(k):
        at, zd = 12 + k, order[k]

        @pl.when(zd > z)
        def _():
            @pl.when(z > 0)
            def _():
                send_up(at, zd).wait_recv()
                add(got, at, from_low, zd - 1, 0, BIG_HALF, [])

            send_up(at, zd).start()

        @pl.when(zd < z)
        def _():
            @pl.when(z < 3)
            def _():
                send_down(at, zd).wait_recv()
                add(got, at, from_high, zd, 0, BIG_HALF, [])

            send_down(at, zd).start()

    def light_item(group, k):
        at, zd, column = 4 * group + k, order[k], l_column(group)
        l_fetch(group, k).wait()
        l_share(group, k).wait_recv()
        add(l_got, at, l_stage, at, 0, SMALL_HALF, [])

        def merge(ref, slot):
            l_got[at] = (l_got[at].astype(FULL) + ref[column, slot].astype(FULL)).astype(LOW)

        if k < 3:

            @pl.when(zd > z)
            def _():
                @pl.when(z > 0)
                def _():
                    l_up(group, k).wait_recv()
                    merge(l_low, zd - 1)

                l_up(group, k).start()

            @pl.when(zd < z)
            def _():
                @pl.when(z < 3)
                def _():
                    l_down(group, k).wait_recv()
                    merge(l_high, zd)

                l_down(group, k).start()

        else:

            @pl.when(z > 0)
            def _():
                l_up(group, k).wait_recv()
                merge(l_low, zd - 1)

            @pl.when(z < 3)
            def _():
                l_down(group, k).wait_recv()
                merge(l_high, zd)

            if group == 0:
                l_half_x().start()
                l_half_y().start()

    def light_sides():
        l_half_x().wait_recv()
        l_got[7, LIGHT_CUT:SMALL_HALF, :] = (
            l_got[7, LIGHT_CUT:SMALL_HALF, :].astype(FULL) + l_halves_x[...].astype(FULL)
        ).astype(LOW)
        l_send_y().start()
        l_half_y().wait_recv()
        l_got[11, 0:LIGHT_CUT, :] = (
            l_got[11, 0:LIGHT_CUT, :].astype(FULL) + l_halves_y[...].astype(FULL)
        ).astype(LOW)
        l_send_x().start()

    def light_end():
        l_send_x().wait_recv()
        l_send_y().wait_recv()
        l_total[...] = l_got[15].astype(FULL) + l_from_x[...].astype(FULL) + l_from_y[...].astype(FULL)

    small_join = remote(late_half, late.at[pl.ds(0, SMALL_HALF)], join_send.at[1], join_recv.at[1], sibling)
    own_late = pltpu.make_async_copy(late, out_small.at[me.dp], out_sem.at[1])

    def late_z(origin, target, way):
        block = out_small.at[2 * origin + y]
        return remote(block, block, late_send.at[way, origin], late_recv.at[0, origin], target)

    def late_y(origin, yo):
        block = out_small.at[2 * origin + yo]
        return remote(block, block, late_send.at[2, origin], late_recv.at[1, origin], y_side)

    def late_step(k):
        @pl.when((core == 1) & (z >= k))
        def _():
            late_z(z - k, up, 0).wait_recv()
            pl.when(z < 3)(lambda: late_z(z - k, up, 0).start())
            late_y(z - k, y).start()

        @pl.when((core == 1) & (z + k <= 3))
        def _():
            late_z(z + k, down, 1).wait_recv()
            pl.when(z > 0)(lambda: late_z(z + k, down, 1).start())
            late_y(z + k, y).start()

    def leave():
        for section in range(4):
            @pl.when(me.pipe == section)
            def _(section=section):
                all_of(keep(section), lambda copy: copy.start())

            @pl.when(me.pipe != section)
            def _(section=section):
                all_of(exchange(section), lambda copy: copy.start())

    def late_start():
        light_end()

        @pl.when(core == 0)
        def _():
            late_half[...] = l_total[...].astype(LOW)
            small_join.start()

        @pl.when(core == 1)
        def _():
            late[SMALL_HALF:SMALL_ROWS, :] = l_total[...].astype(LOW)
            small_join.wait_recv()
            own_late.start()
            own_late.wait()
            pl.when(z < 3)(lambda: late_z(z, up, 0).start())
            pl.when(z > 0)(lambda: late_z(z, down, 1).start())
            late_y(z, y).start()

    def light_round(k):
        for n in range(4 * k, 4 * k + 4):
            light_item(*l_sequence[n])

    edge = (z == 0) | (z == 3)

    def early_z(k):
        pl.when(edge)(lambda: bulk_z(k))

    def inner_z(k):
        pl.when(jnp.logical_not(edge))(lambda: bulk_z(k))

    actions = {"LS": [light_sides], "LE": [late_start], "G": [leave]}
    numbered = {item: n for n, item in enumerate(sequence)}
    for k in range(4):
        actions["A%d" % k] = [functools.partial(bulk_item, numbered[0, k])]
        actions["C%d" % k] = [functools.partial(bulk_item, numbered[1, k])]
        actions["B%d" % k] = [functools.partial(bulk_item, numbered[2, k])]
        actions["O%d" % k] = [functools.partial(bulk_item, numbered[3, k])]
        actions["L%d" % k] = [functools.partial(light_round, k)]
        if k < 3:
            actions["E%d" % k] = [functools.partial(early_z, k)]
            actions["I%d" % k] = [functools.partial(inner_z, k)]
        if k:
            actions["T%d" % k] = [functools.partial(late_step, k)]
    for event in REDUCE_ORDER:
        for action in actions[event]:
            action()

    row_copy.wait()
    part_sum[...] = jnp.sum((l_total[...] * l_total[...]).reshape(SMALL_HALF // 8, 8, 128), axis=0)
    lane = lax.broadcasted_iota(jnp.int32, (8, 128), 1)
    is_last = jnp.where((lane == me.dp) & (owner_row[...] == 7), 1.0, 0.0)
    weight = jnp.broadcast_to(jnp.sum(is_last, axis=1, keepdims=True), (8, 128))
    weight = jnp.where(core == 0, jnp.ones((8, 128), FULL), weight)

    def end(low, high):
        def piece(begin, size, scale):
            part = pl.ds(begin, size)
            sums = got[15, part, :].astype(FULL)
            if low:
                sums = sums + from_low[z - 1, part, :].astype(FULL)
            if high:
                sums = sums + from_high[z, part, :].astype(FULL)
            total[part, :] = sums
            squares = jnp.sum((sums * sums).reshape(size // 8, 8, 128), axis=0)
            part_sum[...] += squares if scale is None else squares * scale

        over(0, BIG_HALF - EDGE, lambda begin, size: piece(begin, size, None))
        piece(BIG_HALF - EDGE, EDGE, weight)

    @pl.when(z == 0)
    def _():
        send_down(15, z).wait_recv()
        end(False, True)

    @pl.when((z > 0) & (z < 3))
    def _():
        send_up(15, z).wait_recv()
        send_down(15, z).wait_recv()
        end(True, True)

    @pl.when(z == 3)
    def _():
        send_up(15, z).wait_recv()
        end(True, False)

    big_join = remote(total, out_big.at[1], join_send.at[0], join_recv.at[0], sibling)
    own_big = pltpu.make_async_copy(total, out_big.at[0], out_sem.at[0])

    @pl.when(core == 0)
    def _():
        own_big.start()

    @pl.when(core == 1)
    def _():
        big_join.start()

    def along_pipe(step, slot):
        target = {"dp": me.dp, "pipe": lax.rem(me.pipe + step, 4)}
        return remote(part_sum, by_pipe.at[slot], p_send.at[step], p_recv.at[step], target)

    def along_dp(step, slot):
        target = {"dp": lax.rem(me.dp + step, 8), "pipe": me.pipe}
        return remote(mine, by_dp.at[slot], d_send.at[step], d_recv.at[step], target)

    for step in range(1, 4):
        along_pipe(step, me.pipe).start()
    by_pipe[me.pipe] = part_sum[...]
    for step in range(1, 4):
        along_pipe(step, lax.rem(me.pipe + 4 - step, 4)).wait_recv()
    mine[...] = jnp.sum(by_pipe[...], axis=0)
    for step in range(1, 8):
        along_dp(step, me.dp).start()
    by_dp[me.dp] = mine[...]
    for step in range(1, 8):
        along_dp(step, lax.rem(me.dp + 8 - step, 8)).wait_recv()
    whole = jnp.sum(jnp.sum(by_dp[...], axis=0), axis=0, keepdims=True)
    length = jnp.sqrt(jnp.broadcast_to(jnp.sum(whole, axis=1, keepdims=True), (8, 128)))
    norm[...] = length
    factor[...] = jnp.minimum(1.0, CLIP_NORM / length)

    @pl.when(core == 0)
    def _():
        own_big.wait()
        big_join.wait_recv()
        small_join.wait_send()

    @pl.when(core == 1)
    def _():
        big_join.wait_send()
        for origin in range(4):
            late_y(origin, 1 - y).wait_recv()
            late_y(origin, y).wait_send()
            pl.when((z < 3) & (origin <= z))(lambda: late_z(origin, up, 0).wait_send())
            pl.when((z > 0) & (origin >= z))(lambda: late_z(origin, down, 1).wait_send())

    for other in range(4):
        @pl.when(me.pipe == other)
        def _(other=other):
            all_of(keep(other), lambda copy: copy.wait())

        @pl.when(me.pipe != other)
        def _(other=other):
            all_of(exchange(other), lambda copy: copy.wait_send())
            all_of(arriving(other), lambda copy: copy.wait_recv())

    for step in range(1, 4):
        along_pipe(step, me.pipe).wait_send()
    for step in range(1, 8):
        along_dp(step, me.dp).wait_send()
    for copy in (l_half_x(), l_half_y(), l_send_x(), l_send_y()):
        copy.wait_send()
    for k in range(4):
        send_half_x(k).wait_send()
        send_half_y(k).wait_send()
        send_x(k).wait_send()
        send_y(k).wait_send()
        for group in range(4):
            share(group, k).wait_send()
            l_share(group, k).wait_send()
    for k in range(3):
        zd, at = order[k], 12 + k

        @pl.when(zd > z)
        def _(at=at, zd=zd, k=k):
            send_up(at, zd).wait_send()
            for group in range(4):
                l_up(group, k).wait_send()

        @pl.when(zd < z)
        def _(at=at, zd=zd, k=k):
            send_down(at, zd).wait_send()
            for group in range(4):
                l_down(group, k).wait_send()


def reduce_all(big, small, wide0, wide1, final, stats, table):
    sem = pltpu.SemaphoreType.DMA
    vm = pltpu.VMEM
    lane_tile = jax.ShapeDtypeStruct((8, 128), FULL)
    return pl.pallas_call(
        reduce_kernel,
        name="reduce_all",
        out_shape=(
            jax.ShapeDtypeStruct((2, BIG_HALF, 128), FULL),
            jax.ShapeDtypeStruct((8, SMALL_ROWS, 128), LOW),
            jax.ShapeDtypeStruct((4,) + wide0.shape, LOW),
            jax.ShapeDtypeStruct((4,) + stats.shape[1:], FULL),
            lane_tile,
            lane_tile,
        ),
        in_specs=[any_spec()] * 7,
        out_specs=(any_spec(),) * 4 + (vmem_spec(),) * 2,
        scratch_shapes=[
            vm((16, BIG_HALF, 128), LOW), vm((4, BIG_HALF - BACK_CUT, 128), LOW), vm((4, BACK_CUT, 128), LOW),
            vm((4, BIG_HALF, 128), LOW), vm((4, BIG_HALF, 128), LOW),
            vm((3, BIG_HALF, 128), LOW), vm((3, BIG_HALF, 128), LOW),
            vm((4, BIG_HALF, 128), LOW), vm((BIG_HALF, 128), FULL),
            vm((16, SMALL_HALF, 128), LOW), vm((16, SMALL_HALF, 128), LOW),
            vm((4, 3, SMALL_HALF, 128), LOW), vm((4, 3, SMALL_HALF, 128), LOW),
            vm((SMALL_HALF - LIGHT_CUT, 128), LOW), vm((LIGHT_CUT, 128), LOW),
            vm((SMALL_HALF, 128), LOW), vm((SMALL_HALF, 128), LOW), vm((SMALL_HALF, 128), FULL),
            vm((SMALL_ROWS, 128), LOW), vm((SMALL_HALF, 128), LOW), vm((8, 128), jnp.int32),
            vm((4, 8, 128), FULL), vm((8, 8, 128), FULL), vm((8, 128), FULL), vm((8, 128), FULL),
            sem((2, 16)), sem((2, 16)),
            sem((5,)), sem((5,)), sem((5,)), sem((5,)), sem((5,)), sem((5,)), sem((5,)), sem((5,)),
            sem((3,)), sem((3,)), sem((3,)), sem((3,)),
            sem((4, 3)), sem((4, 3)), sem((4, 3)), sem((4, 3)),
            sem((4,)), sem((16,)), sem((3,)), sem((3, 4)), sem((2, 4)), sem((2,)), sem((2,)),
            sem((4,)), sem((4,)), sem((4,)), sem((4,)), sem((4,)), sem((4,)), sem((8,)), sem((8,)),
        ],
        compiler_params=pltpu.CompilerParams(
            collective_id=1, has_side_effects=True, vmem_limit_bytes=62 << 20
        ),
    )(big.reshape(2, 8, 2, BIG_HALF, 128), small.reshape(2, 8, 2, SMALL_HALF, 128),
      wide0, wide1, final, stats, table)


def high_dot(a, b, dims=((1,), (0,))):
    return lax.dot_general(a, b, (dims, ((), ())), precision=HIGH, preferred_element_type=FULL)


PIECES = 7
FRONT = 48


def update_kernel(owners, factor_ref, norm, big, small, gram_old, basis_old, params, moment, second,
                  clipped, moment_new, second_new, params_new, gram_new, basis_new, length,
                  tiles, low, grad, held, rotated, weights, gram, in_sem, out_sem, tile_sem):
    factor = factor_ref[0:1, :]
    length[0, 0] = jnp.max(norm[...])
    block, section = owners[0, lax.axis_index("dp")], lax.axis_index("pipe")
    even = lax.rem(section, 2) == 0
    span = params.shape[0]
    piece = held.shape[0] // PIECES

    @pl.when(even)
    def _():
        pltpu.make_async_copy(big, tiles.at[pl.ds(0, BIG_ROWS)], tile_sem).start()

    def loads(i):
        part = pl.ds(piece * i, min(piece, span - piece * i))
        for n, (src, dst) in enumerate(((params, weights), (moment, held), (second, rotated))):
            yield pltpu.make_async_copy(src.at[part, 0, :], dst.at[part], in_sem.at[n, i])

    def stores(i):
        count = min(piece, span - piece * i)
        part = pl.ds(piece * i, count)
        yield pltpu.make_async_copy(
            grad.at[pl.ds(FRONT + piece * i, count)], clipped.at[part, 0, :], out_sem.at[3, i])
        pairs = ((held, moment_new), (rotated, second_new), (weights, params_new))
        for n, (src, dst) in enumerate(pairs):
            yield pltpu.make_async_copy(src.at[part], dst.at[part, 0, :], out_sem.at[n, i])

    for i in range(PIECES):
        for load in loads(i):
            load.start()

    @pl.when(even)
    def _():
        pltpu.make_async_copy(big, tiles.at[pl.ds(0, BIG_ROWS)], tile_sem).wait()

    @pl.when(jnp.logical_not(even))
    def _():
        low[...] = jnp.zeros_like(low)

        @pl.when(block == 0)
        def _():
            copy = pltpu.make_async_copy(small.at[0:20], low, tile_sem)
            copy.start()
            copy.wait()

        @pl.when(block == 1)
        def _():
            copy = pltpu.make_async_copy(small.at[19:33], low.at[0:14], tile_sem)
            copy.start()
            copy.wait()

        @pl.loop(0, WINDOW)
        def _(r):
            tiles[pl.ds(pl.multiple_of(TILE * r, TILE), TILE), :] = low[r].astype(FULL)

    @pl.loop(0, WINDOW)
    def _(r):
        narrow, plain = tile_forms(section, STRIDE * block + r)
        edge = even & (r == STRIDE)
        narrow, plain = narrow & jnp.logical_not(edge), plain | edge
        base = FRONT - 6 * block + TILE * r
        here = pl.multiple_of(TILE * r, TILE)

        @pl.when(narrow)
        def _():
            for j in range(4):
                grad[pl.ds(base + j, 64, 4), :] = tiles[pl.ds(here + 64 * j, 64), :]

        @pl.when(plain)
        def _():
            grad[pl.ds(base, TILE), :] = tiles[pl.ds(here, TILE), :]

        @pl.when(jnp.logical_not(narrow | plain))
        def _():
            for j in range(16):
                grad[pl.ds(base + j, 16, 16), :] = tiles[pl.ds(here + 16 * j, 16), :]

    tail = piece * PIECES - 8
    rest = lax.broadcasted_iota(jnp.int32, (8, 128), 0) + tail
    grad[FRONT + tail : FRONT + tail + 8, :] = jnp.where(
        rest < span, grad[FRONT + tail : FRONT + tail + 8, :], 0.0
    )
    gram[...] = jnp.zeros_like(gram)

    def halves(value):
        high = value.astype(LOW)
        return high, (value - high.astype(FULL)).astype(LOW)

    def split_dot(a, b, dims=((1,), (0,))):
        def dot(left, right):
            return lax.dot_general(left, right, (dims, ((), ())), preferred_element_type=FULL)

        return dot(a[0], b[0]) + (dot(a[0], b[1]) + dot(a[1], b[0]))

    @pl.loop(0, PIECES)
    def _(i):
        part = halves(grad[pl.ds(pl.multiple_of(FRONT + piece * i, 8), piece), :])
        gram[...] += split_dot(part, part, ((0,), (0,)))

    old = basis_old[...]
    fresh = DECAY_STATS * gram_old[...] + (1.0 - DECAY_STATS) * (gram[...] * (factor * factor))
    gram_new[...] = fresh
    product = high_dot(fresh, old)
    rotation = product / jnp.sqrt(jnp.sum(product * product))
    for repeat in range(NS_STEPS):
        square = high_dot(rotation, rotation, ((0,), (0,)))
        rotation = 1.5 * rotation - 0.5 * high_dot(rotation, square)
    basis_new[...] = rotation
    change = halves(high_dot(old, rotation, ((0,), (0,))))
    turn = halves(rotation)
    correction = math.sqrt(1.0 - DECAY_SECOND**STEP) / (1.0 - DECAY_FIRST**STEP)
    for i in range(PIECES):
        for load in loads(i):
            load.wait()
        at = slice(FRONT + piece * i, FRONT + piece * i + piece)
        part = slice(piece * i, piece * i + piece)
        clip = grad[at, :] * factor
        grad[at, :] = clip
        turned = split_dot(halves(clip), turn)
        first = DECAY_FIRST * split_dot(halves(held[part, :]), change) + (1.0 - DECAY_FIRST) * turned
        power = DECAY_SECOND * rotated[part, :] + (1.0 - DECAY_SECOND) * turned * turned
        held[part, :] = first
        rotated[part, :] = power
        scaled = halves(first / (jnp.sqrt(power) + ADAM_EPS))
        direction = split_dot(scaled, turn, ((1,), (1,))) * correction
        before = weights[part, :]
        weights[part, :] = before - LEARN_RATE * (direction + WEIGHT_DECAY * before)
        for store in stores(i):
            store.start()
    for i in range(PIECES):
        for store in stores(i):
            store.wait()


def update(owners, factor, norm, big, small, gram_old, basis_old, params, moment, second):
    span = params.shape[1] // 128
    rows = -(-span // (8 * PIECES)) * 8 * PIECES
    flat_shape = jax.ShapeDtypeStruct((span, 1, 128), FULL)
    square = jax.ShapeDtypeStruct((128, 128), FULL)
    sem = pltpu.SemaphoreType.DMA
    vm = pltpu.VMEM
    outs = pl.pallas_call(
        update_kernel,
        name="update",
        out_shape=(flat_shape,) * 4 + (square,) * 2 + (jax.ShapeDtypeStruct((1, 1), FULL),),
        in_specs=[smem_spec()] + [vmem_spec()] * 2 + [any_spec()] * 2 + [vmem_spec()] * 2 + [any_spec()] * 3,
        out_specs=(any_spec(),) * 4 + (vmem_spec(),) * 2 + (smem_spec(),),
        scratch_shapes=[
            vm((WINDOW * TILE, 128), FULL), vm((WINDOW, TILE, 128), LOW),
            vm((FRONT + WINDOW * TILE, 128), FULL), vm((rows, 128), FULL), vm((rows, 128), FULL),
            vm((rows, 128), FULL), vm((128, 128), FULL), sem((3, PIECES)), sem((4, PIECES)), sem,
        ],
        compiler_params=pltpu.CompilerParams(vmem_limit_bytes=60 << 20),
    )(owners, factor, norm, big.reshape(BIG_ROWS, 128), small.reshape(USED_TILES[1], TILE, 128),
      gram_old, basis_old, params.reshape(span, 1, 128), moment.reshape(span, 1, 128),
      second.reshape(span, 1, 128))
    return tuple(out.reshape(1, span * 128) for out in outs[:4]) + outs[4:]


def to_phases(teach, stud):
    def split(part, axes):
        crops, high, across, channels = part.shape
        part = part.reshape(crops, high // 2, 2, across // 2, 2, channels).transpose(axes)
        return part.reshape(4, -1, channels)

    zeros = jnp.zeros((4, PADDED - ROWS, teach.shape[-1]), teach.dtype)
    parts = [split(teach, (2, 4, 1, 3, 0, 5)), split(stud, (2, 4, 0, 1, 3, 5)), zeros]
    return jnp.concatenate(parts, axis=1)


def from_phases(phases, shape, crops_last):
    crops, high, across, channels = shape
    if crops_last:
        part = phases.reshape(2, 2, high // 2, across // 2, crops, channels).transpose(4, 2, 0, 3, 1, 5)
    else:
        part = phases.reshape(2, 2, crops, high // 2, across // 2, channels).transpose(2, 3, 0, 4, 1, 5)
    return part.reshape(shape)


def on_small_slice(
    teach_in,
    stud_in,
    params,
    owners,
    depth_gates,
    teach_ids,
    stud_ids,
    targets,
    moment,
    second,
    gram_stats,
    eigen_basis,
):
    phases = to_phases(teach_in[0], stud_in[0])
    big, small, ids = prepare(owners, params)
    all_big, all_small, table = gather_all(big, small, ids)
    wide_0, wide_1, final, stats, grad_x, out_big, out_small = run_step(
        table,
        depth_gates,
        teach_ids.T,
        stud_ids,
        all_big.reshape(2, 8, BIG_ROWS, 128),
        all_small.reshape(2, USED_TILES[1], TILE, 128),
        phases,
        targets,
    )
    sum_big, sum_small, segments, stats, norm, factor = reduce_all(
        out_big, out_small, wide_0, wide_1, final, stats, table
    )
    clipped, moment_new, second_new, params_new, gram_new, rotation, length = update(
        owners, factor, norm, sum_big, sum_small, gram_stats[0], eigen_basis[0], params, moment, second
    )
    teach_shape, stud_shape = teach_in.shape[1:], stud_in.shape[1:]
    small_teach = (teach_shape[1] // 2, teach_shape[2] // 2, teach_shape[0], C_OUT)
    small_stud = (stud_shape[0], stud_shape[1] // 2, stud_shape[2] // 2, C_OUT)
    segment_teach = segments[:, :TEACH_ROWS].reshape((4,) + small_teach).transpose(0, 3, 1, 2, 4)
    segment_stud = segments[:, TEACH_ROWS:ROWS].reshape((4,) + small_stud)
    stats = stats[:, 0:2]
    teach_grad = from_phases(grad_x[:, :TEACH_ROWS], teach_shape, True)
    stud_grad = from_phases(grad_x[:, TEACH_ROWS:ROWS], stud_shape, False)
    grad_norm = length.reshape(())
    return (
        segment_teach[None],
        segment_stud[None],
        teach_grad[None],
        stud_grad[None],
        stats[None, :, None],
        grad_norm,
        clipped,
        moment_new,
        second_new,
        params_new,
        gram_new[None],
        rotation[None],
    )


def solution(mesh):
    placed = (
        P("pipe", "dp", None, None, None),
        P("pipe", "dp", None, None, None),
        P("pipe", "dp"),
        P("pipe", None),
        P(),
        P(None, "dp"),
        P(None, "dp"),
        P(),
        P("pipe", "dp"),
        P("pipe", "dp"),
        P("pipe", "dp", None),
        P("pipe", "dp", None),
    )
    small_slice = mesh.shape["dp"] == 8 and mesh.shape["pipe"] == 4
    return jax.shard_map(
        on_small_slice if small_slice else on_device,
        mesh=mesh,
        in_specs=placed,
        out_specs=(
            P("pipe", None, "dp", None, None, None),
            P("pipe", None, "dp", None, None, None),
            P("pipe", "dp", None, None, None),
            P("pipe", "dp", None, None, None),
            P("pipe", None, "dp", None, None),
            P(),
            P("pipe", "dp"),
            P("pipe", "dp"),
            P("pipe", "dp"),
            P("pipe", "dp"),
            P("pipe", "dp", None),
            P("pipe", "dp", None),
        ),
        check_vma=False,
    )
```

```python
import functools
import math

import jax
import jax.numpy as jnp
import numpy as np
from jax import lax
from jax.experimental import pallas as pl
from jax.experimental.pallas import tpu as pltpu
from jax.sharding import PartitionSpec as P

C_IN = 1024
MID = 512
C_OUT = 2048
STEP = 10
NS_STEPS = 5


HIGH = lax.Precision.HIGHEST
NORM_EPS = 1e-05
POOL_EPS = 1e-06
CLIP_NORM = 1.0
LEARN_RATE = 0.02
DECAY_FIRST = 0.9
DECAY_SECOND = 0.95
DECAY_STATS = 0.95
ADAM_EPS = 1e-08
WEIGHT_DECAY = 0.01


def section_shapes(section):
    if section == 0:
        return [
            ("first_conv", (C_IN, MID)),
            ("middle_conv", (9 * MID, MID)),
            ("skip_conv", (C_IN, C_OUT)),
            ("first_gain", (MID,)),
            ("first_bias", (MID,)),
            ("middle_gain", (MID,)),
            ("middle_bias", (MID,)),
            ("skip_gain", (C_OUT,)),
            ("skip_bias", (C_OUT,)),
        ]
    if section == 2:
        return [
            ("first_conv", (C_OUT, MID)),
            ("middle_conv", (9 * MID, MID)),
            ("first_gain", (MID,)),
            ("first_bias", (MID,)),
            ("middle_gain", (MID,)),
            ("middle_bias", (MID,)),
        ]
    return [("last_conv", (MID, C_OUT)), ("last_gain", (C_OUT,)), ("last_bias", (C_OUT,))]


def unpack(flat_vector, section):
    pieces = {}
    offset = 0
    for entry_name, entry_shape in section_shapes(section):
        entry_size = math.prod(entry_shape)
        pieces[entry_name] = flat_vector[offset : offset + entry_size].reshape(entry_shape)
        offset = offset + entry_size
    return pieces


def pack(grads, section, flat_size):
    parts = [grads[entry_name].reshape(-1) for entry_name, entry_shape in section_shapes(section)]
    used = sum((math.prod(entry_shape) for entry_name, entry_shape in section_shapes(section)))
    parts.append(jnp.zeros((flat_size - used,), jnp.float32))
    return jnp.concatenate(parts)


def as_float(vector):
    return vector.astype(jnp.float32)


def to_low(groups):
    return tuple((portion.astype(jnp.bfloat16) for portion in groups))


def to_high(groups):
    return tuple((portion.astype(jnp.float32) for portion in groups))


def point_conv(groups, weight):
    return tuple(
        (
            jnp.einsum("khwc,cd->khwd", portion, weight, preferred_element_type=jnp.float32)
            for portion in groups
        )
    )


def point_back(grad_out, groups, weight):
    low_grads = to_low(grad_out)
    grad_input = tuple(
        (
            jnp.einsum("khwd,cd->khwc", grad_part, weight, preferred_element_type=jnp.float32)
            for grad_part in low_grads
        )
    )
    grad_weight = sum(
        (
            jnp.einsum("khwc,khwd->cd", in_part, grad_part, preferred_element_type=jnp.float32)
            for in_part, grad_part in zip(groups, low_grads)
        )
    )
    return (grad_input, grad_weight)


def patches(portion, stride):
    height = portion.shape[1]
    across = portion.shape[2]
    padded = jnp.pad(portion, ((0, 0), (1, 1), (1, 1), (0, 0)))
    shifted = [
        padded[:, row_off : row_off + height : stride, col_off : col_off + across : stride, :]
        for row_off in range(3)
        for col_off in range(3)
    ]
    return jnp.concatenate(shifted, axis=-1)


def area_conv(groups, weight, stride):
    columns = tuple((patches(portion, stride) for portion in groups))
    return (point_conv(columns, weight), columns)


def unpatch(grad_cols, height, across, stride):
    channels = grad_cols.shape[-1] // 9
    padded = jnp.zeros((grad_cols.shape[0], height + 2, across + 2, channels), jnp.float32)
    for row_off in range(3):
        for col_off in range(3):
            offset = (3 * row_off + col_off) * channels
            padded = padded.at[
                :, row_off : row_off + height : stride, col_off : col_off + across : stride, :
            ].add(grad_cols[..., offset : offset + channels])
    return padded[:, 1 : height + 1, 1 : across + 1, :]


def area_back(grad_out, columns, weight, stride, in_shapes):
    grad_cols, grad_weight = point_back(grad_out, columns, weight)
    grad_input = tuple(
        (
            unpatch(grad_part, shape_item[1], shape_item[2], stride)
            for grad_part, shape_item in zip(grad_cols, in_shapes)
        )
    )
    return (grad_input, grad_weight)


def batch_norm(groups, gain, bias):
    rows_total = sum((portion.shape[0] * portion.shape[1] * portion.shape[2] for portion in groups))
    centre = sum((jnp.sum(portion, axis=(0, 1, 2)) for portion in groups)) / rows_total
    spread = (
        sum((jnp.sum(jnp.square(portion - centre), axis=(0, 1, 2)) for portion in groups))
        / rows_total
    )
    inverse = lax.rsqrt(spread + NORM_EPS)
    standard = tuple(((portion - centre) * inverse for portion in groups))
    normed = tuple((gain * std_part + bias for std_part in standard))
    return (normed, (centre, spread, inverse, standard))


def norm_back(grad_out, gain, saved):
    centre, spread, inverse, standard = saved
    rows_total = sum(
        (portion.shape[0] * portion.shape[1] * portion.shape[2] for portion in standard)
    )
    grad_sum = sum((jnp.sum(grad_part, axis=(0, 1, 2)) for grad_part in grad_out))
    grad_dot = sum(
        (
            jnp.sum(grad_part * std_part, axis=(0, 1, 2))
            for grad_part, std_part in zip(grad_out, standard)
        )
    )
    grad_input = tuple(
        (
            gain
            * inverse
            * (grad_part - grad_sum / rows_total - std_part * (grad_dot / rows_total))
            for grad_part, std_part in zip(grad_out, standard)
        )
    )
    return (grad_input, grad_dot, grad_sum)


def through_softplus(grad_out, pre_values):
    return tuple(
        (grad_part * jax.nn.sigmoid(pre_part) for grad_part, pre_part in zip(grad_out, pre_values))
    )


def front_forward(pieces, inputs):
    first = point_conv(inputs, pieces["first_conv"])
    normed_a, saved_a = batch_norm(
        first, as_float(pieces["first_gain"]), as_float(pieces["first_bias"])
    )
    hidden = tuple((jax.nn.softplus(portion).astype(jnp.bfloat16) for portion in normed_a))
    middle, columns = area_conv(hidden, pieces["middle_conv"], 2)
    normed_b, saved_b = batch_norm(
        middle, as_float(pieces["middle_gain"]), as_float(pieces["middle_bias"])
    )
    narrow = tuple((jax.nn.softplus(portion) for portion in normed_b))
    reduced = tuple((portion[:, ::2, ::2, :] for portion in inputs))
    skipped = point_conv(reduced, pieces["skip_conv"])
    wide, saved_p = batch_norm(
        skipped, as_float(pieces["skip_gain"]), as_float(pieces["skip_bias"])
    )
    norm_rows = jnp.stack(
        [
            jnp.concatenate([saved_a[0], saved_b[0], saved_p[0]]),
            jnp.concatenate([saved_a[1], saved_b[1], saved_p[1]]),
        ]
    )
    kept = (normed_a, hidden, columns, normed_b, reduced, saved_a, saved_b, saved_p)
    return (wide, narrow, norm_rows, kept)


def front_backward(pieces, inputs, grad_wide, grad_narrow):
    wide, narrow, norm_rows, kept = front_forward(pieces, inputs)
    normed_a, hidden, columns, normed_b, reduced, saved_a, saved_b, saved_p = kept
    grads = {}
    grad_pre_b = through_softplus(grad_narrow, normed_b)
    grad_mid, grads["middle_gain"], grads["middle_bias"] = norm_back(
        grad_pre_b, as_float(pieces["middle_gain"]), saved_b
    )
    grad_hidden, grads["middle_conv"] = area_back(
        grad_mid, columns, pieces["middle_conv"], 2, [portion.shape for portion in hidden]
    )
    grad_pre_a = through_softplus(grad_hidden, normed_a)
    grad_first, grads["first_gain"], grads["first_bias"] = norm_back(
        grad_pre_a, as_float(pieces["first_gain"]), saved_a
    )
    grad_inputs, grads["first_conv"] = point_back(grad_first, inputs, pieces["first_conv"])
    grad_skip, grads["skip_gain"], grads["skip_bias"] = norm_back(
        grad_wide, as_float(pieces["skip_gain"]), saved_p
    )
    grad_reduced, grads["skip_conv"] = point_back(grad_skip, reduced, pieces["skip_conv"])
    grad_inputs = tuple(
        (
            full_part.at[:, ::2, ::2, :].add(part_reduced)
            for full_part, part_reduced in zip(grad_inputs, grad_reduced)
        )
    )
    return (grad_inputs, grads)


def join_forward(pieces, wide, narrow):
    last = point_conv(narrow, pieces["last_conv"])
    normed, saved = batch_norm(last, as_float(pieces["last_gain"]), as_float(pieces["last_bias"]))
    pre_values = tuple(
        (
            skip_part.astype(jnp.float32) + branch_part
            for skip_part, branch_part in zip(wide, normed)
        )
    )
    ending = tuple((jax.nn.softplus(pre_part) for pre_part in pre_values))
    filler = jnp.zeros((2 * MID,), jnp.float32)
    norm_rows = jnp.stack(
        [jnp.concatenate([saved[0], filler]), jnp.concatenate([saved[1], filler])]
    )
    return (ending, norm_rows, (pre_values, saved))


def join_grads(pieces, narrow, kept, grad_out, gate):
    pre_values, saved = kept
    grad_pre = tuple(
        (
            grad_part * jax.nn.sigmoid(pre_part) * gate
            for grad_part, pre_part in zip(grad_out, pre_values)
        )
    )
    grad_wide = tuple(
        (pre_grad + grad_part * (1.0 - gate) for pre_grad, grad_part in zip(grad_pre, grad_out))
    )
    grad_last, gain_grad, bias_grad = norm_back(grad_pre, as_float(pieces["last_gain"]), saved)
    grad_narrow, weight_grad = point_back(grad_last, narrow, pieces["last_conv"])
    grads = {"last_conv": weight_grad, "last_gain": gain_grad, "last_bias": bias_grad}
    return (grad_wide, grad_narrow, grads)


def split_forward(pieces, wide):
    first = point_conv(wide, pieces["first_conv"])
    normed_a, saved_a = batch_norm(
        first, as_float(pieces["first_gain"]), as_float(pieces["first_bias"])
    )
    hidden = tuple((jax.nn.softplus(portion).astype(jnp.bfloat16) for portion in normed_a))
    middle, columns = area_conv(hidden, pieces["middle_conv"], 1)
    normed_b, saved_b = batch_norm(
        middle, as_float(pieces["middle_gain"]), as_float(pieces["middle_bias"])
    )
    narrow = tuple((jax.nn.softplus(portion) for portion in normed_b))
    filler = jnp.zeros((C_OUT,), jnp.float32)
    norm_rows = jnp.stack(
        [
            jnp.concatenate([saved_a[0], saved_b[0], filler]),
            jnp.concatenate([saved_a[1], saved_b[1], filler]),
        ]
    )
    return (narrow, norm_rows, (normed_a, hidden, columns, normed_b, saved_a, saved_b))


def split_backward(pieces, wide, grad_relay, grad_narrow):
    narrow, norm_rows, kept = split_forward(pieces, wide)
    normed_a, hidden, columns, normed_b, saved_a, saved_b = kept
    grads = {}
    grad_pre_b = through_softplus(grad_narrow, normed_b)
    grad_mid, grads["middle_gain"], grads["middle_bias"] = norm_back(
        grad_pre_b, as_float(pieces["middle_gain"]), saved_b
    )
    grad_hidden, grads["middle_conv"] = area_back(
        grad_mid, columns, pieces["middle_conv"], 1, [portion.shape for portion in hidden]
    )
    grad_pre_a = through_softplus(grad_hidden, normed_a)
    grad_first, grads["first_gain"], grads["first_bias"] = norm_back(
        grad_pre_a, as_float(pieces["first_gain"]), saved_a
    )
    grad_conv_in, grads["first_conv"] = point_back(grad_first, wide, pieces["first_conv"])
    grad_wide = tuple(
        (relay_part + conv_part for relay_part, conv_part in zip(grad_relay, grad_conv_in))
    )
    return (grad_wide, grads)


def pool_grad(final, targets, picks):
    result = []
    for portion, pick_ids in zip(final, picks):
        cubes = jnp.mean(portion * portion * portion, axis=(1, 2)) + POOL_EPS
        factor = jnp.exp(jnp.log(cubes) * (-2.0 / 3.0)) * targets[pick_ids]
        result.append(factor[:, None, None, :] * portion * portion)
    return tuple(result)


def used_size(section):
    return sum((math.prod(entry_shape) for entry_name, entry_shape in section_shapes(section)))


def batch_pass(reals, inputs, gate, targets, picks):
    pieces = [unpack(reals[section], section) for section in range(4)]
    wide_f, narrow_f, rows_0, _ = front_forward(pieces[0], inputs)
    wide_0, narrow_0 = to_low(wide_f), to_low(narrow_f)
    ending_1, rows_1, kept_1 = join_forward(pieces[1], wide_0, narrow_0)
    wide_1 = to_low(ending_1)
    narrow_f, rows_2, _ = split_forward(pieces[2], wide_1)
    narrow_2 = to_low(narrow_f)
    ending_3, rows_3, kept_3 = join_forward(pieces[3], wide_1, narrow_2)
    final = tuple(
        (
            jnp.where(gate > 0, end_part, relay_part.astype(jnp.float32))
            for end_part, relay_part in zip(ending_3, wide_1)
        )
    )
    cotangent = pool_grad(final, targets, picks)
    grad_wide, grad_narrow, grads_3 = join_grads(pieces[3], narrow_2, kept_3, cotangent, gate)
    grad_wide, grads_2 = split_backward(
        pieces[2], wide_1, to_high(to_low(grad_wide)), to_high(to_low(grad_narrow))
    )
    grad_wide, grad_narrow, grads_1 = join_grads(
        pieces[1], narrow_0, kept_1, to_high(to_low(grad_wide)), 1.0
    )
    grad_inputs, grads_0 = front_backward(
        pieces[0], inputs, to_high(to_low(grad_wide)), to_high(to_low(grad_narrow))
    )
    outs = (wide_0, wide_1, wide_1, to_low(final))
    stats = jnp.stack([rows_0, rows_1, rows_2 * gate, rows_3 * gate])
    return (outs, stats, to_low(grad_inputs), (grads_0, grads_1, grads_2, grads_3))


def on_device(
    teach_in,
    stud_in,
    params,
    owners,
    depth_gates,
    teach_ids,
    stud_ids,
    targets,
    moment,
    second,
    gram_stats,
    eigen_basis,
):
    sections = lax.axis_size("pipe")
    rank = lax.axis_index("pipe")
    owner_count = lax.axis_size("dp")
    span_size = params.shape[1]
    flat_size = span_size * owner_count
    owner_rows = lax.all_gather(owners, "pipe", axis=0, tiled=True)
    gathered = lax.all_gather(params[0].astype(jnp.bfloat16), ("pipe", "dp"), axis=0)
    gathered = gathered.reshape(sections, owner_count, span_size)
    reals = []
    for section in range(sections):
        inverse = jnp.argsort(owner_rows[section]).astype(jnp.int32)
        blocks = -(-used_size(section) // span_size)
        reals.append(gathered[section][inverse[:blocks]].reshape(blocks * span_size))
    inputs = (teach_in[0], stud_in[0])
    gate = depth_gates[rank].astype(jnp.float32)
    outs, stats, (teach_grad, stud_grad), grads = batch_pass(
        reals, inputs, gate, targets, (teach_ids[rank], stud_ids[rank])
    )
    segment_teach = lax.all_to_all(
        jnp.stack([part[0] for part in outs]), "pipe", split_axis=0, concat_axis=0, tiled=True
    )
    segment_stud = lax.all_to_all(
        jnp.stack([part[1] for part in outs]), "pipe", split_axis=0, concat_axis=0, tiled=True
    )
    stats = lax.all_to_all(stats, "pipe", split_axis=0, concat_axis=0, tiled=True)
    rows = []
    for section in range(sections):
        flat = pack(grads[section], section, flat_size).reshape(owner_count, span_size)
        rows.append(flat[owner_rows[section]])
    span_total = lax.psum_scatter(
        jnp.stack(rows).reshape(sections * owner_count, span_size),
        ("pipe", "dp"),
        scatter_dimension=0,
        tiled=True,
    ).reshape(span_size)
    total_squares = lax.psum(jnp.sum(span_total * span_total), ("dp", "pipe"))
    grad_norm = jnp.sqrt(total_squares)
    factor = jnp.minimum(1.0, CLIP_NORM / grad_norm)
    clipped = span_total * factor
    matrix = clipped.reshape(span_size // 128, 128)
    gram_old = gram_stats[0]
    basis_old = eigen_basis[0]
    gram_new = DECAY_STATS * gram_old + (1.0 - DECAY_STATS) * jnp.dot(
        matrix.T, matrix, precision=HIGH
    )
    product = jnp.dot(gram_new, basis_old, precision=HIGH)
    rotation = product / jnp.sqrt(jnp.sum(product * product))
    for repeat in range(NS_STEPS):
        square = jnp.dot(rotation.T, rotation, precision=HIGH)
        rotation = 1.5 * rotation - 0.5 * jnp.dot(rotation, square, precision=HIGH)
    moment_old = moment.reshape(span_size // 128, 128)
    initial = jnp.dot(moment_old, basis_old.T, precision=HIGH)
    blended = DECAY_FIRST * initial + (1.0 - DECAY_FIRST) * matrix
    moment_new = jnp.dot(blended, rotation, precision=HIGH)
    rotated = jnp.dot(matrix, rotation, precision=HIGH)
    second_new = (
        DECAY_SECOND * second.reshape(span_size // 128, 128)
        + (1.0 - DECAY_SECOND) * rotated * rotated
    )
    correction = math.sqrt(1.0 - DECAY_SECOND**STEP) / (1.0 - DECAY_FIRST**STEP)
    direction = (
        jnp.dot(moment_new / (jnp.sqrt(second_new) + ADAM_EPS), rotation.T, precision=HIGH)
        * correction
    )
    weights = params.reshape(span_size // 128, 128)
    params_new = weights - LEARN_RATE * (direction + WEIGHT_DECAY * weights)
    return (
        segment_teach[None],
        segment_stud[None],
        teach_grad[None],
        stud_grad[None],
        stats[None, :, None],
        grad_norm,
        clipped.reshape(1, span_size),
        moment_new.reshape(1, span_size),
        second_new.reshape(1, span_size),
        params_new.reshape(1, span_size),
        gram_new[None],
        rotation[None],
    )


MESH = pl.DeviceIdType.MESH
LOW = jnp.bfloat16
FULL = jnp.float32
TILE = 256
WINDOW = 20
STRIDE = 19
EDGE = 64
BIG_ROWS = STRIDE * TILE + EDGE
VEC_TILE = (152, 32, 104, 32)
USED_TILES = (153, 33, 105, 33)
FRONT_WIDE = 88
SMALL_ROWS = 1056
ROWS = 120
PADDED = 128
STUD_ROWS = 48
TEACH_END = 80


def any_spec():
    return pl.BlockSpec(memory_space=pl.ANY)


def smem_spec():
    return pl.BlockSpec(memory_space=pltpu.SMEM)


def vmem_spec():
    return pl.BlockSpec(memory_space=pltpu.VMEM)


def tile_forms(section, tile):
    even = lax.rem(section, 2) == 0
    vector = jnp.where(section == 0, 152, jnp.where(section == 2, 104, 32))
    narrow_end = jnp.where(section == 0, FRONT_WIDE, jnp.where(section == 2, 104, 0))
    narrow = even & (tile < narrow_end)
    plain = tile == vector
    return narrow, plain


def prepare_kernel(owners, params, big, small, ids, flat, sem):
    block, section = owners[0, lax.axis_index("dp")], lax.axis_index("pipe")

    even = lax.rem(section, 2) == 0
    flat[0:EDGE, :] = jnp.zeros((EDGE, 128), FULL)
    flat[STRIDE * TILE : WINDOW * TILE, :] = jnp.zeros((TILE, 128), FULL)
    copy = pltpu.make_async_copy(params.at[:, 0, :], flat.at[pl.ds(6 * block, params.shape[0])], sem)
    copy.start()

    @pl.when(jnp.logical_not(even))
    def _():
        @pl.loop(0, small.shape[0])
        def _(r):
            small[r] = jnp.zeros((TILE, 128), LOW)

    lane = lax.broadcasted_iota(jnp.int32, (8, 128), 1)
    row = jnp.zeros((8, 128), jnp.int32)
    for j in range(8):
        row = jnp.where(lane == j, owners[0, j], row)
    ids[...] = row
    copy.wait()

    def wide_tile(base):
        return [flat[pl.ds(base + j, 16, 16), :].astype(LOW) for j in range(16)]

    @pl.when(even)
    def _():
        @pl.loop(0, STRIDE)
        def _(r):
            narrow, plain = tile_forms(section, STRIDE * block + r)
            base = pl.multiple_of(TILE * r, TILE)

            @pl.when(narrow)
            def _():
                for j in range(4):
                    big[pl.ds(base + 64 * j, 64), :] = flat[pl.ds(base + j, 64, 4), :].astype(LOW)

            @pl.when(plain)
            def _():
                big[pl.ds(base, TILE), :] = flat[pl.ds(base, TILE), :].astype(LOW)

            @pl.when(jnp.logical_not(narrow | plain))
            def _():
                for j, part in enumerate(wide_tile(base)):
                    big[pl.ds(base + 16 * j, 16), :] = part

        big[STRIDE * TILE : BIG_ROWS, :] = flat[STRIDE * TILE : BIG_ROWS, :].astype(LOW)

    @pl.when(jnp.logical_not(even))
    def _():
        @pl.loop(0, WINDOW)
        def _(r):
            tile = STRIDE * block + r
            base = pl.multiple_of(TILE * r, TILE)

            @pl.when(tile == VEC_TILE[1])
            def _():
                small[tile] = flat[pl.ds(base, TILE), :].astype(LOW)

            @pl.when(tile < VEC_TILE[1])
            def _():
                for j, part in enumerate(wide_tile(base)):
                    small[tile, 16 * j : 16 * j + 16, :] = part


def prepare(owners, params):
    return pl.pallas_call(
        prepare_kernel,
        name="prepare",
        out_shape=(
            jax.ShapeDtypeStruct((BIG_ROWS, 128), LOW),
            jax.ShapeDtypeStruct((USED_TILES[1], TILE, 128), LOW),
            jax.ShapeDtypeStruct((8, 128), jnp.int32),
        ),
        in_specs=[smem_spec(), any_spec()],
        out_specs=(vmem_spec(),) * 3,
        scratch_shapes=[pltpu.VMEM((WINDOW * TILE, 128), FULL), pltpu.SemaphoreType.DMA],
        compiler_params=pltpu.CompilerParams(vmem_limit_bytes=60 << 20),
    )(owners, params.reshape(-1, 1, 128))


class Place:
    def __init__(self):
        self.dp = lax.axis_index("dp")
        self.pipe = lax.axis_index("pipe")
        self.x, self.core = self.pipe // 2, self.pipe % 2
        self.z, self.y = self.dp // 2, self.dp % 2

    def device(self, x=None, core=None, z=None, y=None):
        x = self.x if x is None else x
        core = self.core if core is None else core
        z = self.z if z is None else z
        y = self.y if y is None else y
        return {"dp": 2 * z + y, "pipe": 2 * x + core}

    def enter(self):
        barrier = pltpu.get_barrier_semaphore()
        for step in range(1, 8):
            other = lax.rem(self.dp + step, 8)
            pl.semaphore_signal(
                barrier, inc=1, device_id={"dp": other, "pipe": self.pipe}, device_id_type=MESH
            )
        for step in range(1, 4):
            other = lax.rem(self.pipe + step, 4)
            pl.semaphore_signal(
                barrier, inc=1, device_id={"dp": self.dp, "pipe": other}, device_id_type=MESH
            )
        pl.semaphore_wait(barrier, 10)


def remote(src, dst, send, recv, target):
    return pltpu.make_async_remote_copy(
        src_ref=src, dst_ref=dst, send_sem=send, recv_sem=recv, device_id=target, device_id_type=MESH
    )


BIG_HALF = BIG_ROWS // 2
SMALL_HALF = SMALL_ROWS // 2
BULK_CUT = 960
LIGHT_CUT = 256
BACK_CUT = 1520
GATHER_ORDER = (
    "X0", "EY", "Z1", "EC0", "Y0", "X1", "EC1", "EC2", "Y1", "S0", "EC3", "R0", "L0", "Z2", "X2",
    "Z3", "Y2", "L1", "S1", "D0", "X3", "R1", "Y3", "S2", "L2", "R2", "D1", "S3", "M1", "R3", "M2",
    "D2", "D3", "M3",
)
REDUCE_ORDER = (
    "A0", "A1", "A2", "A3", "L0", "B0", "C0", "B1", "L1", "L2", "L3", "LS", "C1", "C2", "C3", "O0",
    "B2", "LE", "E0", "T1", "B3", "I0", "G", "O1", "I1", "E1", "O2", "E2", "I2", "T2", "T3", "O3",
)


def gather_kernel(big, small, ids, all_big, all_small, table, held_big, held_small, k_sem, early, chunk, rising, falling,
                  early_send, early_recv, eu_send, eu_recv, ed_send, ed_recv,
                  z_send, z_recv, x_send, x_recv, y_send, y_recv, dx_send, dx_recv, dy_send, dy_recv,
                  s_send, s_recv, first_send, first_recv, own_sem, id_send, id_recv, lz_send, lz_recv):
    me = Place()
    me.enter()
    x, y, z, core = me.x, me.y, me.z, me.core
    up, down = me.device(z=z + 1), me.device(z=z - 1)
    x_side, y_side, sibling = me.device(x=1 - x), me.device(y=1 - y), me.device(core=1 - core)

    class Stream:
        def __init__(self, n, held, out, cut):
            self.n, self.held, self.out, self.cut, self.rows = n, held, out, cut, out.shape[3]

        def block(self, xo, origin, yo):
            return self.held.at[xo, 2 * origin + yo]

        def move_x(self, origin):
            block = self.block(x, origin, y)
            return remote(block, block, x_send.at[self.n, origin], x_recv.at[self.n, origin], x_side)

        def move_y(self, origin):
            block = self.block(x, origin, y)
            return remote(block, block, y_send.at[self.n, origin], y_recv.at[self.n, origin], y_side)

        def copies(self, xo, origin, yo):
            block, at = self.block(xo, origin, yo), 8 * xo + 2 * origin + yo
            result = self.out.at[xo, 2 * origin + yo, core]
            return (
                remote(block, result, s_send.at[self.n, at], s_recv.at[self.n, at], sibling),
                pltpu.make_async_copy(block, result, k_sem.at[self.n, at]),
            )

        def share(self, xo, origin, yo):
            for copy in self.copies(xo, origin, yo):
                copy.start()

        def move_z(self, origin, target, way):
            block = self.block(x, origin, y)
            return remote(block, block, z_send.at[self.n, way, origin], z_recv.at[self.n, origin], target)

        def half_x(self, origin, xo, yo):
            part = self.held.at[xo, 2 * origin + yo, pl.ds(self.cut, self.rows - self.cut)]
            return remote(part, part, dx_send.at[self.n, origin], dx_recv.at[self.n, origin], x_side)

        def half_y(self, origin, xo, yo):
            part = self.held.at[xo, 2 * origin + yo, pl.ds(0, self.cut)]
            return remote(part, part, dy_send.at[self.n, origin], dy_recv.at[self.n, origin], y_side)

        def to_x(self, origin):
            self.move_x(origin).start()

        def to_y(self, origin):
            self.move_y(origin).start()

        def from_x(self, origin):
            self.move_x(origin).wait_recv()
            self.half_y(origin, 1 - x, y).start()
            self.share(1 - x, origin, y)

        def from_y(self, origin):
            self.move_y(origin).wait_recv()
            self.half_x(origin, x, 1 - y).start()
            self.share(x, origin, 1 - y)

        def from_diagonal(self, origin):
            self.half_x(origin, 1 - x, 1 - y).wait_recv()
            self.half_y(origin, 1 - x, 1 - y).wait_recv()
            self.share(1 - x, origin, 1 - y)

        def each(self, step, action):
            if step == 0:
                action(z)
            else:
                pl.when(z >= step)(lambda: action(z - step))
                pl.when(z + step <= 3)(lambda: action(z + step))

        def begin(self):
            pl.when(z < 3)(lambda: self.move_z(z, up, 0).start())
            pl.when(z > 0)(lambda: self.move_z(z, down, 1).start())
            self.share(x, z, y)

        def from_z(self, k):
            @pl.when(z >= k)
            def _():
                self.move_z(z - k, up, 0).wait_recv()
                pl.when(z < 3)(lambda: self.move_z(z - k, up, 0).start())
                self.share(x, z - k, y)

            @pl.when(z + k <= 3)
            def _():
                self.move_z(z + k, down, 1).wait_recv()
                pl.when(z > 0)(lambda: self.move_z(z + k, down, 1).start())
                self.share(x, z + k, y)

        def close(self):
            for origin in range(4):
                self.move_x(origin).wait_send()
                self.move_y(origin).wait_send()
                self.half_x(origin, x, 1 - y).wait_send()
                self.half_y(origin, 1 - x, y).wait_send()
                pl.when((z < 3) & (origin <= z))(lambda: self.move_z(origin, up, 0).wait_send())
                pl.when((z > 0) & (origin >= z))(lambda: self.move_z(origin, down, 1).wait_send())
            self.close_shares()

        def close_shares(self):
            for origin in range(4):
                for xo in range(2):
                    for yo in range(2):
                        away, home = self.copies(xo, origin, yo)
                        away.wait_send()
                        home.wait()
                        theirs = self.out.at[xo, 2 * origin + yo, 1 - core]
                        at = 8 * xo + 2 * origin + yo
                        remote(theirs, theirs, s_send.at[self.n, at], s_recv.at[self.n, at], sibling).wait_recv()

    class Late(Stream):
        def column_z(self, xo, origin, yo, target, way):
            block = self.block(xo, origin, yo)
            at = 2 * xo + yo
            return remote(
                block, block, lz_send.at[way, at, origin], lz_recv.at[at, origin], target
            )

        def leave(self, xo, yo):
            pl.when(z < 3)(lambda: self.column_z(xo, z, yo, up, 0).start())
            pl.when(z > 0)(lambda: self.column_z(xo, z, yo, down, 1).start())
            self.share(xo, z, yo)

        def step(self, k):
            if k == 0:
                self.move_x(z).start()
                self.move_y(z).start()
                self.leave(x, y)
            elif k == 1:
                self.move_x(z).wait_recv()
                self.half_y(z, 1 - x, y).start()
                self.leave(1 - x, y)
                self.move_y(z).wait_recv()
                self.half_x(z, x, 1 - y).start()
                self.leave(x, 1 - y)
            elif k == 2:
                self.half_x(z, 1 - x, 1 - y).wait_recv()
                self.half_y(z, 1 - x, 1 - y).wait_recv()
                self.leave(1 - x, 1 - y)
            else:
                gap = k - 2

                @pl.when(z >= gap)
                def _():
                    for xo, yo in columns:
                        self.column_z(xo, z - gap, yo, up, 0).wait_recv()
                        pl.when(z < 3)(lambda: self.column_z(xo, z - gap, yo, up, 0).start())
                        self.share(xo, z - gap, yo)

                @pl.when(z + gap <= 3)
                def _():
                    for xo, yo in columns:
                        self.column_z(xo, z + gap, yo, down, 1).wait_recv()
                        pl.when(z > 0)(lambda: self.column_z(xo, z + gap, yo, down, 1).start())
                        self.share(xo, z + gap, yo)

        def close(self):
            self.move_x(z).wait_send()
            self.move_y(z).wait_send()
            self.half_x(z, x, 1 - y).wait_send()
            self.half_y(z, 1 - x, y).wait_send()
            for origin in range(4):
                for xo, yo in columns:
                    pl.when((z < 3) & (origin <= z))(
                        lambda: self.column_z(xo, origin, yo, up, 0).wait_send())
                    pl.when((z > 0) & (origin >= z))(
                        lambda: self.column_z(xo, origin, yo, down, 1).wait_send())
            self.close_shares()

    columns = ((x, y), (1 - x, y), (x, 1 - y), (1 - x, 1 - y))
    bulk = Stream(0, held_big, all_big, BULK_CUT)
    light = Late(1, held_small, all_small, LIGHT_CUT)

    order = [
        jnp.where(z < 2, 3, 0),
        jnp.where(z == 0, 2, jnp.where(z == 1, 0, jnp.where(z == 2, 3, 1))),
        jnp.where(z == 0, 1, jnp.where(z == 1, 2, jnp.where(z == 2, 1, 2))),
        z,
    ]

    def cross(k):
        return remote(small.at[2 * order[k] + (1 - y)], early.at[k], early_send.at[k], early_recv.at[k], y_side)

    def own_early(k):
        return pltpu.make_async_copy(small.at[2 * order[k] + y], chunk.at[k], own_sem.at[3 + k])

    def rise(k):
        slot = order[k] - 1
        return remote(chunk.at[k], rising.at[slot], eu_send.at[slot], eu_recv.at[slot], up)

    def fall(k):
        slot = order[k]
        return remote(chunk.at[k], falling.at[slot], ed_send.at[slot], ed_recv.at[slot], down)

    def merge(k, ref, slot):
        @pl.loop(0, 3)
        def _(i):
            part = pl.ds(pl.multiple_of(352 * i, 16), 352)
            chunk[k, part, :] = (chunk[k, part, :].astype(FULL) + ref[slot, part, :].astype(FULL)).astype(LOW)

    big_half = held_big.at[x, me.dp]
    big_first = remote(big.at[pl.ds(BIG_HALF, BIG_HALF)], big_half, first_send.at[0], first_recv.at[0], sibling)
    small_half = held_small.at[x, me.dp]
    small_first = remote(
        chunk.at[3, pl.ds(0, SMALL_HALF)], small_half, first_send.at[1], first_recv.at[1], sibling)

    def early_cross():
        @pl.when(core == 1)
        def _():
            for k in range(4):
                own_early(k).wait()
                cross(k).wait_recv()
                merge(k, early, k)

    def early_chain(k):
        @pl.when(core == 1)
        def _():
            if k < 3:

                @pl.when(order[k] > z)
                def _():
                    @pl.when(z > 0)
                    def _():
                        rise(k).wait_recv()
                        merge(k, rising, order[k] - 1)

                    rise(k).start()

                @pl.when(order[k] < z)
                def _():
                    @pl.when(z < 3)
                    def _():
                        fall(k).wait_recv()
                        merge(k, falling, order[k])

                    fall(k).start()

            else:

                @pl.when(z > 0)
                def _():
                    rise(k).wait_recv()
                    merge(k, rising, z - 1)

                @pl.when(z < 3)
                def _():
                    fall(k).wait_recv()
                    merge(k, falling, z)

                small_first.start()
                copy = pltpu.make_async_copy(
                    chunk.at[3, pl.ds(SMALL_HALF, SMALL_HALF)], small_half, own_sem.at[0])
                copy.start()
                copy.wait()

    def light_begin():
        @pl.when(core == 0)
        def _():
            small_first.wait_recv()

        light.step(0)

    @pl.when(core == 0)
    def _():
        big_first.start()
        copy = pltpu.make_async_copy(big.at[pl.ds(0, BIG_HALF)], big_half, own_sem.at[0])
        copy.start()
        copy.wait()

    @pl.when(core == 1)
    def _():
        for k in range(4):
            cross(k).start()
            own_early(k).start()
        big_first.wait_recv()

    bulk.begin()
    row = pltpu.make_async_copy(ids, table.at[me.pipe], own_sem.at[2])
    row.start()
    for step in range(1, 4):
        remote(
            ids, table.at[me.pipe], id_send.at[step], id_recv.at[step],
            {"dp": me.dp, "pipe": lax.rem(me.pipe + step, 4)},
        ).start()

    actions = {"EY": early_cross, "L0": light_begin}
    for k in range(4):
        actions["EC%d" % k] = functools.partial(early_chain, k)
        actions["X%d" % k] = functools.partial(bulk.each, k, bulk.to_x)
        actions["Y%d" % k] = functools.partial(bulk.each, k, bulk.to_y)
        actions["S%d" % k] = functools.partial(bulk.each, k, bulk.from_x)
        actions["R%d" % k] = functools.partial(bulk.each, k, bulk.from_y)
        actions["D%d" % k] = functools.partial(bulk.each, k, bulk.from_diagonal)
        if k:
            actions["Z%d" % k] = functools.partial(bulk.from_z, k)
            actions["M%d" % k] = functools.partial(light.step, k + 2)
            if k < 3:
                actions["L%d" % k] = functools.partial(light.step, k)
    for event in GATHER_ORDER:
        actions[event]()
    bulk.close()
    light.close()
    row.wait()
    for step in range(1, 4):
        here = lax.rem(me.pipe + 4 - step, 4)
        move = remote(
            ids, table.at[here], id_send.at[step], id_recv.at[step],
            {"dp": me.dp, "pipe": lax.rem(me.pipe + step, 4)},
        )
        move.wait_recv()
        move.wait_send()

    @pl.when(core == 0)
    def _():
        big_first.wait_send()

    @pl.when(core == 1)
    def _():
        small_first.wait_send()
        for k in range(4):
            cross(k).wait_send()
        for k in range(3):
            pl.when(order[k] > z)(lambda: rise(k).wait_send())
            pl.when(order[k] < z)(lambda: fall(k).wait_send())


def gather_all(big, small, ids):
    sem = pltpu.SemaphoreType.DMA
    return pl.pallas_call(
        gather_kernel,
        name="gather_all",
        out_shape=(
            jax.ShapeDtypeStruct((2, 8, 2, BIG_HALF, 128), LOW),
            jax.ShapeDtypeStruct((2, 8, 2, SMALL_HALF, 128), LOW),
            jax.ShapeDtypeStruct((4, 8, 128), jnp.int32),
        ),
        in_specs=[any_spec()] * 3,
        out_specs=(any_spec(),) * 3,
        scratch_shapes=[
            pltpu.VMEM((2, 8, BIG_HALF, 128), LOW), pltpu.VMEM((2, 8, SMALL_HALF, 128), LOW), sem((2, 16)),
            pltpu.VMEM((4, SMALL_ROWS, 128), LOW), pltpu.VMEM((4, SMALL_ROWS, 128), LOW),
            pltpu.VMEM((3, SMALL_ROWS, 128), LOW), pltpu.VMEM((3, SMALL_ROWS, 128), LOW),
            sem((4,)), sem((4,)), sem((3,)), sem((3,)), sem((3,)), sem((3,)),
            sem((2, 2, 4)), sem((2, 4)),
            sem((2, 4)), sem((2, 4)), sem((2, 4)), sem((2, 4)),
            sem((2, 4)), sem((2, 4)), sem((2, 4)), sem((2, 4)),
            sem((2, 16)), sem((2, 16)),
            sem((2,)), sem((2,)), sem((7,)), sem((4,)), sem((4,)), sem((2, 4, 4)), sem((4, 4)),
        ],
        compiler_params=pltpu.CompilerParams(
            collective_id=0, has_side_effects=True, vmem_limit_bytes=60 << 20
        ),
    )(big, small.reshape(8, SMALL_ROWS, 128), ids)


def soft(value):
    return jnp.maximum(value, 0.0) + jnp.log1p(jnp.exp(-jnp.abs(value)))


def gate_of(value):
    small = jnp.exp(-jnp.abs(value))
    share = 1.0 / (1.0 + small)
    return jnp.where(value >= 0, share, small * share)


def standardize(z):
    count = z.shape[0]
    centre = jnp.sum(z, axis=0, keepdims=True) / count
    away = z - centre
    spread = jnp.sum(away * away, axis=0, keepdims=True) / count
    inverse = lax.rsqrt(spread + NORM_EPS)
    return away * inverse, centre, spread, inverse


def unstandardize(grad, standard, gain, inverse):
    count = grad.shape[0]
    grad_sum = jnp.sum(grad, axis=0, keepdims=True)
    grad_dot = jnp.sum(grad * standard, axis=0, keepdims=True)
    result = gain * inverse * (grad - grad_sum / count - standard * (grad_dot / count))
    return result, grad_dot, grad_sum


def pad_low(value):
    zeros = jnp.zeros((PADDED - ROWS, value.shape[1]), FULL)
    return jnp.concatenate([value, zeros], axis=0).astype(LOW)


def mul(a, b):
    return jnp.dot(a, b, preferred_element_type=FULL)


def mul_t(a, b):
    return lax.dot_general(a, b, (((1,), (1,)), ((), ())), preferred_element_type=FULL)


def narrow_part(ref, start, count, blocks=range(4)):
    return jnp.concatenate(
        [ref[pl.ds(start, count), 64 * j : 64 * j + 64, :].reshape(64 * count, 128) for j in blocks],
        axis=1,
    )


def put_narrow(ref, start, count, value):
    for j in range(4):
        ref[pl.ds(start, count), 64 * j : 64 * j + 64, :] = (
            value[:, 128 * j : 128 * j + 128].astype(LOW).reshape(count, 64, 128)
        )


def wide_part(ref, start, count, c):
    return jnp.concatenate(
        [
            ref[start : start + count, 32 * c + 16 * h : 32 * c + 16 * h + 16, :].reshape(
                16 * count, 128
            )
            for h in range(2)
        ],
        axis=1,
    )


def put_wide(ref, start, count, c, value):
    for h in range(2):
        ref[start : start + count, 32 * c + 16 * h : 32 * c + 16 * h + 16, :] = (
            value[:, 128 * h : 128 * h + 128].astype(LOW).reshape(count, 16, 128)
        )


def chunks(count):
    def run(body):
        for c in range(count):
            body(c)

    return run


def step_kernel(table, gates, teach_ids, stud_ids, all_big, all_small, x, targets, grid,
                wide0, wide1, final, stats, grad_x, out_big, out_small,
                w0, w1, w2, w3, edges, loose, vec, grad_vec, raw,
                std_a, std_b, std_p, std_1, std_c, std_d, hidden, cols0, cols2,
                nar0, nar2, turned, relay, dz_a, dz_n, acc, acc_x, grad_h,
                wanted, inv, in_sem, edge_sem, out_sem):
    rank = lax.axis_index("pipe")
    gate = gates[rank].astype(FULL)
    for group in range(2):
        for j in range(8):
            inv[8 * group + table[2 * group, 0, j]] = j
    picks = [teach_ids[k, rank] for k in range(2)] + [stud_ids[rank, k] for k in range(3)]
    rows = [
        pltpu.make_async_copy(targets.at[pl.ds(pick, 1)], wanted.at[pl.ds(k, 1)], edge_sem.at[12 + k])
        for k, pick in enumerate(picks)
    ]
    for fetched in rows:
        fetched.start()
    weights = (w0, w1, w2, w3)
    loads = {0: [], 1: [], 2: [], 3: []}
    front, split = w0.reshape(USED_TILES[0] * TILE, 128), w2.reshape(115 * TILE, 128)
    for group, weight, blocks in ((0, front, 8), (1, split, 6)):
        for b in range(blocks):
            at, here = 8 * group + b, inv[8 * group + b]
            count = min(STRIDE, VEC_TILE[2 * group] + 1 - STRIDE * b) * TILE
            loads[2 * group].append(pltpu.make_async_copy(
                all_big.at[group, here, pl.ds(0, count)], weight.at[pl.ds(STRIDE * TILE * b, count)],
                in_sem.at[0, at]))
            if b < blocks - 1:
                loads[2 * group].append(pltpu.make_async_copy(
                    all_big.at[group, here, pl.ds(STRIDE * TILE, EDGE)], edges.at[7 * group + b],
                    edge_sem.at[7 * group + b]))
            elif group == 0:
                loads[0].append(pltpu.make_async_copy(
                    all_big.at[0, here, pl.ds(STRIDE * TILE, EDGE)],
                    front.at[pl.ds(VEC_TILE[0] * TILE, EDGE)], edge_sem.at[17]))
    loads[1].append(pltpu.make_async_copy(all_small.at[0], w1, in_sem.at[0, 14]))
    loads[3].append(pltpu.make_async_copy(all_small.at[1], w3, in_sem.at[0, 15]))
    for section in range(4):
        for load in loads[section]:
            load.start()

    raw[...] = jnp.zeros_like(raw)
    loose[...] = jnp.zeros_like(loose)
    grad_vec[...] = jnp.zeros_like(grad_vec)

    def edge_parts(tile, is_narrow):
        count, size = (4, 64) if is_narrow else (16, 16)
        for j in range(count):
            yield pl.ds(j, 16, count), slice(size * j, size * j + 16)

    def is_narrow(section, tile):
        return section == 2 or tile < FRONT_WIDE

    def merge_edge(section, tile, at):
        ref = weights[section]
        loose[0:EDGE, :] = edges[at].astype(FULL)
        for lying, here in edge_parts(tile, is_narrow(section, tile)):
            ref[tile, here, :] = (ref[tile, here, :].astype(FULL) + loose[lying, :]).astype(LOW)

    def take_edge(section, tile, at):
        ref = weights[section]
        for lying, here in edge_parts(tile, is_narrow(section, tile)):
            loose[lying, :] = ref[tile, here, :].astype(FULL)
        edges[at] = loose[0:EDGE, :].astype(LOW)

    def settle(section, blocks=None):
        if section == 0:
            for b in blocks:
                for load in loads[0][2 * b : 2 * b + 2]:
                    load.wait()
            if 7 in blocks:
                vec[0] = w0[VEC_TILE[0], 0:48, :].astype(FULL)
            else:
                for b in range(7):
                    merge_edge(0, 19 * b + 19, b)
            return
        for load in loads[section]:
            load.wait()
        if section == 2:
            for b in range(5):
                merge_edge(2, 19 * b + 19, 7 + b)
        vec[section] = weights[section][VEC_TILE[section], 0:48, :].astype(FULL)

    def row(section, start):
        return jnp.concatenate(
            [vec[section, pl.ds(start + h, 1), :] for h in range(2)], axis=1
        )

    def put_row(section, start, value):
        for h in range(2):
            grad_vec[section, pl.ds(start + h, 1), :] = value[:, 128 * h : 128 * h + 128]

    def put_stats(section, column, centre, spread):
        raw[2 * section : 2 * section + 1, pl.ds(column, 256)] = centre
        raw[2 * section + 1 : 2 * section + 2, pl.ds(column, 256)] = spread

    def inverse_of(section, column):
        return lax.rsqrt(raw[2 * section + 1 : 2 * section + 2, pl.ds(column, 256)] + NORM_EPS)

    def lanes(c):
        return slice(256 * c, 256 * c + 256)

    at_row, at_col, side = grid[0], grid[1], grid[2]

    def masked(value, dr, dc):
        ok = (at_row + dr >= 0) & (at_row + dr < side) & (at_col + dc >= 0) & (at_col + dc < side)
        return jnp.concatenate(
            [jnp.where(ok, value[:, 128 * j : 128 * j + 128], 0.0) for j in range(4)], axis=1
        )

    def rolled(value, sign, dr, dc):
        parts = []
        for start, end, across, down in ((0, STUD_ROWS, 1, 4), (STUD_ROWS, ROWS, 2, 12)):
            by = (sign * (dr * down + dc * across)) % (end - start)
            part = value[start:end]
            parts.append(part if by == 0 else pltpu.roll(part, by, 0))
        return jnp.concatenate(parts, axis=0)

    def taps(stride):
        for t in range(9):
            r, q = t // 3, t % 3
            if stride == 1:
                yield t, 0, r - 1, q - 1
            else:
                phase = 2 * (1 if r != 1 else 0) + (1 if q != 1 else 0)
                yield t, phase, -1 if r == 0 else 0, -1 if q == 0 else 0

    settle(0, (0, 7))
    whole_x = x[...].reshape(4 * PADDED, C_IN)
    for c in range(2):
        z = mul(whole_x, narrow_part(w0, 0, 16, (2 * c, 2 * c + 1)))
        z = jnp.concatenate([z[PADDED * p : PADDED * p + ROWS] for p in range(4)], axis=0)
        standard, centre, spread, _ = standardize(z)
        put_stats(0, 256 * c, centre, spread)
        std_a[:, 256 * c : 256 * c + 256] = standard
        hidden[:, 256 * c : 256 * c + 256] = (
            soft(row(0, 2 * c) * standard + row(0, 4 + 2 * c)).astype(LOW).astype(FULL)
        )

    for t, phase, dr, dc in taps(2):
        cols0[t] = pad_low(masked(rolled(hidden[ROWS * phase : ROWS * phase + ROWS, :], -1, dr, dc), dr, dc))
    acc[...] = jnp.zeros_like(acc)
    settle(0, (1, 2, 3, 4, 5, 6))

    @chunks(9)
    def _(t):
        acc[...] += mul(cols0[t], narrow_part(w0, 16 + 8 * t, 8))

    def middle(section, std, nar):
        for c in range(2):
            at = slice(256 * c, 256 * c + 256)
            standard, centre, spread, _ = standardize(acc[0:ROWS, at])
            put_stats(section, MID + 256 * c, centre, spread)
            std[:, at] = standard
            nar[:, at] = pad_low(soft(row(section, 8 + 2 * c) * standard + row(section, 12 + 2 * c)))

    middle(0, std_b, nar0)
    acc[...] = jnp.zeros_like(acc)
    settle(1)
    settle(2)

    @chunks(8)
    def _(c):
        at = lanes(c)
        standard, centre, spread, _ = standardize(mul(x[0], wide_part(w0, FRONT_WIDE, 64, c))[0:ROWS])
        put_stats(0, 2 * MID + 256 * c, centre, spread)
        std_p[:, at] = standard
        low = pad_low(row(0, 16 + 2 * c) * standard + row(0, 32 + 2 * c))
        wide0[:, at] = low
        standard, centre, spread, _ = standardize(mul(nar0[...], wide_part(w1, 0, 32, c))[0:ROWS])
        put_stats(1, 256 * c, centre, spread)
        std_1[:, at] = standard
        pre = low.astype(FULL)[0:ROWS] + row(1, 2 * c) * standard + row(1, 16 + 2 * c)
        low = pad_low(soft(pre))
        wide1[:, at] = low
        acc[...] += mul(low, narrow_part(w2, 4 * c, 4))

    for c in range(2):
        at = slice(256 * c, 256 * c + 256)
        standard, centre, spread, _ = standardize(acc[0:ROWS, at])
        put_stats(2, 256 * c, centre, spread)
        std_c[:, at] = standard
        hidden[0:ROWS, at] = soft(row(2, 2 * c) * standard + row(2, 4 + 2 * c)).astype(LOW).astype(FULL)
    for t, phase, dr, dc in taps(1):
        cols2[t] = pad_low(masked(rolled(hidden[0:ROWS, :], -1, dr, dc), dr, dc))
    acc[...] = jnp.zeros_like(acc)

    @chunks(9)
    def _(t):
        acc[...] += mul(cols2[t], narrow_part(w2, 32 + 8 * t, 8))

    middle(2, std_d, nar2)

    turned[...] = nar2[...].T
    acc[...] = jnp.zeros_like(acc)
    settle(3)
    for fetched in rows:
        fetched.wait()

    teach_rows = ROWS - STUD_ROWS
    first_crop = lax.rem(lax.broadcasted_iota(jnp.int32, (teach_rows, 256), 0), 2) == 0

    def spread_rows(values):
        first, second = (jnp.broadcast_to(value, (teach_rows, 256)) for value in values[0:2])
        parts = [jnp.broadcast_to(value, (16, 256)) for value in values[2:5]]
        parts.append(jnp.where(first_crop, first, second))
        return jnp.concatenate(parts, axis=0)

    def crop_sums(value):
        def total(part):
            return jnp.sum(part, axis=0, keepdims=True)

        teach = value[STUD_ROWS:ROWS]
        return [
            total(jnp.where(first_crop, teach, 0.0)),
            total(jnp.where(first_crop, 0.0, teach)),
            total(value[0:16]),
            total(value[16:32]),
            total(value[32:48]),
        ]

    @chunks(8)
    def _(c):
        at = lanes(c)
        weight = wide_part(w3, 0, 32, c)
        standard, centre, spread, inverse = standardize(mul(nar2[...], weight)[0:ROWS])
        put_stats(3, 256 * c, centre, spread)
        gain = row(3, 2 * c)
        before = wide1[:, at].astype(FULL)[0:ROWS]
        pre = before + gain * standard + row(3, 16 + 2 * c)
        ending = jnp.where(gate > 0, soft(pre), before)
        final[:, at] = pad_low(ending)
        square = ending * ending
        factors = []
        for crop, total in enumerate(crop_sums(square * ending)):
            mean = total / (36.0 if crop < 2 else 16.0) + POOL_EPS
            factors.append(jnp.exp(jnp.log(mean) * (-2.0 / 3.0)) * wanted[crop : crop + 1, at])
        cotangent = spread_rows(factors) * square
        grad_pre = cotangent * gate_of(pre) * gate
        relay[:, at] = pad_low(grad_pre + cotangent * (1.0 - gate))
        result, grad_gain, grad_bias = unstandardize(grad_pre, standard, gain, inverse)
        put_row(3, 2 * c, grad_gain)
        put_row(3, 16 + 2 * c, grad_bias)
        low = pad_low(result)
        acc[...] += mul_t(low, weight)
        put_wide(w3, 0, 32, c, mul(turned[...], low))

    def flush(section):
        weights[section][VEC_TILE[section]] = grad_vec[section].astype(LOW)

    flush(3)
    stores = [pltpu.make_async_copy(w3, out_small.at[1], out_sem.at[16])]
    stores[-1].start()

    def middle_back(section, std):
        for c in range(2):
            at = slice(256 * c, 256 * c + 256)
            gain, bias = row(section, 8 + 2 * c), row(section, 12 + 2 * c)
            grad = acc[0:ROWS, at].astype(LOW).astype(FULL) * gate_of(gain * std[:, at] + bias)
            result, grad_gain, grad_bias = unstandardize(
                grad, std[:, at], gain, inverse_of(section, MID + 256 * c)
            )
            put_row(section, 8 + 2 * c, grad_gain)
            put_row(section, 12 + 2 * c, grad_bias)
            dz_n[:, at] = pad_low(result)

    def taps_back(weight, start, cols, stride, phases):
        grad_h[0 : ROWS * phases, :] = jnp.zeros((ROWS * phases, MID), FULL)
        for t, phase, dr, dc in taps(stride):
            part = mul_t(dz_n[...], narrow_part(weight, start + 8 * t, 8))[0:ROWS]
            at = slice(ROWS * phase, ROWS * phase + ROWS)
            grad_h[at, :] += rolled(masked(part, dr, dc), 1, dr, dc)
            put_narrow(weight, start + 8 * t, 8, mul(cols[t].T, dz_n[...]))

    middle_back(2, std_d)
    taps_back(w2, 32, cols2, 1, 1)
    for c in range(2):
        at = slice(256 * c, 256 * c + 256)
        gain, bias = row(2, 2 * c), row(2, 4 + 2 * c)
        grad = grad_h[0:ROWS, at] * gate_of(gain * std_c[:, at] + bias)
        result, grad_gain, grad_bias = unstandardize(grad, std_c[:, at], gain, inverse_of(2, 256 * c))
        put_row(2, 2 * c, grad_gain)
        put_row(2, 4 + 2 * c, grad_bias)
        dz_n[:, at] = pad_low(result)
    turned[...] = nar0[...].T
    acc[...] = jnp.zeros_like(acc)
    acc_x[...] = jnp.zeros_like(acc_x)

    @chunks(8)
    def _(c):
        at = lanes(c)
        low = dz_n[...]
        grad = relay[:, at].astype(FULL) + mul_t(low, narrow_part(w2, 4 * c, 4))
        put_narrow(w2, 4 * c, 4, mul(wide1[:, at].T, low))
        grad = grad.astype(LOW).astype(FULL)[0:ROWS]
        gain = row(1, 2 * c)
        pre = wide0[:, at].astype(FULL)[0:ROWS] + gain * std_1[:, at] + row(1, 16 + 2 * c)
        grad = grad * gate_of(pre)
        result, grad_gain, grad_bias = unstandardize(
            grad, std_1[:, at], gain, inverse_of(1, 256 * c)
        )
        put_row(1, 2 * c, grad_gain)
        put_row(1, 16 + 2 * c, grad_bias)
        low = pad_low(result)
        acc[...] += mul_t(low, wide_part(w1, 0, 32, c))
        put_wide(w1, 0, 32, c, mul(turned[...], low))
        grad = grad.astype(LOW).astype(FULL)
        result, grad_gain, grad_bias = unstandardize(
            grad, std_p[:, at], row(0, 16 + 2 * c), inverse_of(0, 2 * MID + 256 * c)
        )
        put_row(0, 16 + 2 * c, grad_gain)
        put_row(0, 32 + 2 * c, grad_bias)
        low = pad_low(result)
        acc_x[...] += mul_t(low, wide_part(w0, FRONT_WIDE, 64, c))
        put_wide(w0, FRONT_WIDE, 64, c, mul(x[0].T, low))

    flush(1)
    flush(2)
    w2[105:115] = jnp.zeros((10, TILE, 128), LOW)
    stores.append(pltpu.make_async_copy(w1, out_small.at[0], out_sem.at[17]))
    stores[-1].start()
    def store(source, group, b, start, semaphore):
        count = source.shape[0]
        stores.append(pltpu.make_async_copy(
            source, out_big.at[group, inv[8 * group + b], pl.ds(start, count)], out_sem.at[semaphore]))
        stores[-1].start()

    for b in range(8):
        if b < 5:
            take_edge(2, 19 * b + 19, 7 + b)
            store(split.at[pl.ds(STRIDE * TILE * b, STRIDE * TILE)], 1, b, 0, 8 + b)
            store(edges.at[7 + b], 1, b, STRIDE * TILE, 20 + b)
        else:
            first = 95 if b == 5 else 105
            store(split.at[pl.ds(TILE * first, 10 * TILE)], 1, b, 0, 8 + b)
            store(split.at[pl.ds(TILE * 105, BIG_ROWS - 10 * TILE)], 1, b, 10 * TILE, 20 + b)

    def store_front(blocks):
        for b in blocks:
            if b == 7:
                edges[12] = w0[VEC_TILE[0], 0:EDGE, :]
            else:
                take_edge(0, 19 * b + 19, b)
            store(front.at[pl.ds(STRIDE * TILE * b, STRIDE * TILE)], 0, b, 0, b)
            store(edges.at[12 if b == 7 else b], 0, b, STRIDE * TILE, 28 + b)

    store_front((5, 6))
    middle_back(0, std_b)
    taps_back(w0, 16, cols0, 2, 4)
    store_front((1, 2, 3, 4))
    for c in range(2):
        at = slice(256 * c, 256 * c + 256)
        gain, bias = row(0, 2 * c), row(0, 4 + 2 * c)
        grad = grad_h[:, at] * gate_of(gain * std_a[:, at] + bias)
        result, grad_gain, grad_bias = unstandardize(grad, std_a[:, at], gain, inverse_of(0, 256 * c))
        put_row(0, 2 * c, grad_gain)
        put_row(0, 4 + 2 * c, grad_bias)
        for p in range(4):
            dz_a[PADDED * p : PADDED * p + PADDED, at] = pad_low(result[ROWS * p : ROWS * p + ROWS])

    @chunks(4)
    def _(c):
        at = lanes(c)
        low = dz_a[...]
        part = mul_t(low, narrow_part(w0, 4 * c, 4))
        grad_x[0, :, at] = (part[0:PADDED] + acc_x[:, at]).astype(LOW)
        for p in range(1, 4):
            grad_x[p, :, at] = part[PADDED * p : PADDED * p + PADDED].astype(LOW)
        turned_x = x[:, :, at].reshape(4 * PADDED, 256).T
        put_narrow(w0, 4 * c, 4, mul(turned_x, low))

    flush(0)
    store_front((0, 7))
    for section in range(4):
        part = raw[2 * section : 2 * section + 2]
        stats[section, 0:2] = part if section < 2 else part * gate
        stats[section, 2:8] = jnp.zeros((6, 2 * MID + C_OUT), FULL)
    for store in stores:
        store.wait()


def run_step(table, gates, teach_ids, stud_ids, all_big, all_small, phases, targets):
    spots = np.zeros((3, ROWS, 128), np.int32)
    for r in range(ROWS):
        width = 4 if r < STUD_ROWS else 6
        at = r % 16 if r < STUD_ROWS else (r - STUD_ROWS) // 2
        spots[0, r], spots[1, r], spots[2, r] = at // width, at % width, width
    sem = pltpu.SemaphoreType.DMA
    wide = jax.ShapeDtypeStruct((PADDED, C_OUT), LOW)
    vm = pltpu.VMEM
    return pl.pallas_call(
        step_kernel,
        name="step",
        out_shape=(
            wide, wide, wide,
            jax.ShapeDtypeStruct((4, 8, 2 * MID + C_OUT), FULL),
            jax.ShapeDtypeStruct((4, PADDED, C_IN), LOW),
            jax.ShapeDtypeStruct((2, 8, BIG_ROWS, 128), LOW),
            jax.ShapeDtypeStruct((2, USED_TILES[1], TILE, 128), LOW),
        ),
        in_specs=[smem_spec()] * 4 + [any_spec(), any_spec(), vmem_spec(), any_spec(), vmem_spec()],
        out_specs=(vmem_spec(),) * 5 + (any_spec(),) * 2,
        scratch_shapes=[
            vm((153, TILE, 128), LOW), vm((33, TILE, 128), LOW), vm((115, TILE, 128), LOW), vm((33, TILE, 128), LOW),
            vm((13, EDGE, 128), LOW), vm((TILE, 128), FULL), vm((4, 48, 128), FULL), vm((4, TILE, 128), FULL),
            vm((8, 2 * MID + C_OUT), FULL),
            vm((4 * ROWS, MID), FULL), vm((ROWS, MID), FULL), vm((ROWS, C_OUT), FULL), vm((ROWS, C_OUT), FULL),
            vm((ROWS, MID), FULL), vm((ROWS, MID), FULL), vm((4 * ROWS, MID), FULL),
            vm((9, PADDED, MID), LOW), vm((9, PADDED, MID), LOW),
            vm((PADDED, MID), LOW), vm((PADDED, MID), LOW), vm((MID, PADDED), LOW),
            vm((PADDED, C_OUT), LOW), vm((4 * PADDED, MID), LOW), vm((PADDED, MID), LOW),
            vm((PADDED, MID), FULL), vm((PADDED, C_IN), FULL), vm((4 * ROWS, MID), FULL),
            vm((8, C_OUT), FULL), pltpu.SMEM((16,), jnp.int32),
            sem((2, 16)), sem((18,)), sem((36,)),
        ],
        compiler_params=pltpu.CompilerParams(vmem_limit_bytes=60 << 20),
    )(table, gates, teach_ids, stud_ids, all_big, all_small, phases, targets, jnp.asarray(spots))


def reduce_kernel(big, small, wide0, wide1, final, stats, table,
                  out_big, out_small, seg_stud, seg_teach, out_stats, norm, factor,
                  got, halves_x, halves_y, from_x, from_y, from_low, from_high, stage, total,
                  l_got, l_stage, l_low, l_high, l_halves_x, l_halves_y, l_from_x, l_from_y, l_total,
                  late, late_half, owner_row, by_pipe, by_dp, mine, part_sum,
                  s_send, s_recv, hx_send, hx_recv, hy_send, hy_recv, x_send, x_recv, y_send, y_recv,
                  zu_send, zu_recv, zd_send, zd_recv, lu_send, lu_recv, ld_send, ld_recv,
                  stage_sem, l_stage_sem, out_sem, late_send, late_recv, join_send, join_recv,
                  seg_send, seg_recv, stat_send, stat_recv, p_send, p_recv, d_send, d_recv):
    me = Place()
    me.enter()
    x, y, z, core = me.x, me.y, me.z, me.core
    up, down = me.device(z=z + 1), me.device(z=z - 1)
    x_side, y_side, sibling = me.device(x=1 - x), me.device(y=1 - y), me.device(core=1 - core)
    order = [
        jnp.where(z < 2, 3, 0),
        jnp.where(z == 0, 2, jnp.where(z == 1, 0, jnp.where(z == 2, 3, 1))),
        jnp.where(z == 0, 1, jnp.where(z == 1, 2, jnp.where(z == 2, 1, 2))),
        z,
    ]
    columns = ((1 - x, 1 - y), (x, 1 - y), (1 - x, y), (x, y))
    groups = {"A": (0,), "C": (1,), "B": (2,), "O": (3,)}
    sequence = [
        (group, int(event[1])) for event in REDUCE_ORDER for group in groups.get(event[0], ())
    ]
    l_sequence = [(group, k) for k in range(4) for group in range(4)]

    def all_of(copies, act):
        for copy in copies:
            act(copy)

    def over(start, count, piece):
        whole = count // 512
        if whole:

            @pl.loop(0, whole)
            def _(i):
                piece(pl.multiple_of(start + 512 * i, 16), 512)

        if count % 512:
            piece(start + 512 * whole, count % 512)

    def source(array, group, k, half):
        xo, yo = columns[group]
        return array.at[xo, 2 * order[k] + yo, half]

    def share(group, k):
        at = 4 * group + k
        return remote(source(big, group, k, 1 - core), got.at[at], s_send.at[0, at], s_recv.at[0, at], sibling)

    def l_share(group, k):
        at = 4 * group + k
        return remote(source(small, group, k, 1 - core), l_got.at[at], s_send.at[1, at], s_recv.at[1, at], sibling)

    def fetch(n):
        return pltpu.make_async_copy(source(big, *sequence[n], core), stage.at[n % 4], stage_sem.at[n % 4])

    def l_fetch(group, k):
        at = 4 * group + k
        return pltpu.make_async_copy(source(small, group, k, core), l_stage.at[at], l_stage_sem.at[at])

    def add(target, at, other, slot, start, count, extras):
        def piece(begin, size):
            part = pl.ds(begin, size)
            sums = target[at, part, :].astype(FULL) + other[slot, part, :].astype(FULL)
            for ref, k in extras:
                sums = sums + ref[k, pl.ds(begin - start, size), :].astype(FULL)
            target[at, part, :] = sums.astype(LOW)

        over(start, count, piece)

    def send_half_x(k):
        return remote(got.at[k, pl.ds(BACK_CUT, BIG_HALF - BACK_CUT)], halves_x.at[k],
                      hx_send.at[k], hx_recv.at[k], x_side)

    def send_half_y(k):
        return remote(got.at[k, pl.ds(0, BACK_CUT)], halves_y.at[k], hy_send.at[k], hy_recv.at[k], y_side)

    def send_y(k):
        return remote(got.at[4 + k], from_y.at[k], y_send.at[k], y_recv.at[k], y_side)

    def send_x(k):
        return remote(got.at[8 + k], from_x.at[k], x_send.at[k], x_recv.at[k], x_side)

    def send_up(at, zd):
        return remote(got.at[at], from_low.at[zd - 1], zu_send.at[zd - 1], zu_recv.at[zd - 1], up)

    def send_down(at, zd):
        return remote(got.at[at], from_high.at[zd], zd_send.at[zd], zd_recv.at[zd], down)

    def l_column(group):
        xo, yo = columns[group]
        return 2 * xo + yo

    def l_up(group, k):
        at, zd = l_column(group), order[k] - 1
        return remote(l_got.at[4 * group + k], l_low.at[at, zd], lu_send.at[at, zd], lu_recv.at[at, zd], up)

    def l_down(group, k):
        at, zd = l_column(group), order[k]
        return remote(l_got.at[4 * group + k], l_high.at[at, zd], ld_send.at[at, zd], ld_recv.at[at, zd], down)

    def l_half_x():
        return remote(l_got.at[3, pl.ds(LIGHT_CUT, SMALL_HALF - LIGHT_CUT)], l_halves_x,
                      hx_send.at[4], hx_recv.at[4], x_side)

    def l_half_y():
        return remote(l_got.at[3, pl.ds(0, LIGHT_CUT)], l_halves_y, hy_send.at[4], hy_recv.at[4], y_side)

    def l_send_y():
        return remote(l_got.at[7], l_from_y, y_send.at[4], y_recv.at[4], y_side)

    def l_send_x():
        return remote(l_got.at[11], l_from_x, x_send.at[4], x_recv.at[4], x_side)

    leaving = (wide0, wide1, wide1, final)

    def pairs(section, micro):
        source = leaving[section]
        yield source.at[pl.ds(0, STUD_ROWS)], seg_stud.at[micro], seg_send.at[0, section], seg_recv.at[0, micro]
        yield source.at[pl.ds(STUD_ROWS, TEACH_END)], seg_teach.at[micro], seg_send.at[1, section], seg_recv.at[1, micro]
        yield stats.at[section], out_stats.at[micro], stat_send.at[section], stat_recv.at[micro]

    def exchange(section):
        return [remote(*pair, {"dp": me.dp, "pipe": section}) for pair in pairs(section, me.pipe)]

    def keep(section):
        return [pltpu.make_async_copy(src, dst, send) for src, dst, send, _ in pairs(section, me.pipe)]

    def arriving(micro):
        return [remote(*pair, {"dp": me.dp, "pipe": micro}) for pair in pairs(micro, micro)]

    for n in range(16):
        share(*sequence[n]).start()
        if n == 3:
            for item in l_sequence:
                l_share(*item).start()
    for n in range(2):
        fetch(n).start()
    for group, k in l_sequence:
        l_fetch(group, k).start()
    row_copy = pltpu.make_async_copy(table.at[2 * x], owner_row, out_sem.at[2])
    row_copy.start()

    def bulk_item(n):
        group, k = sequence[n]
        at, slot = 4 * group + k, n % 4
        if n + 2 < 16:
            fetch(n + 2).start()
        fetch(n).wait()
        share(group, k).wait_recv()
        if group == 0:
            add(got, at, stage, slot, 0, BIG_HALF, [])
            send_half_x(k).start()
            send_half_y(k).start()
        elif group == 1:
            send_half_x(k).wait_recv()
            add(got, at, stage, slot, 0, BACK_CUT, [])
            add(got, at, stage, slot, BACK_CUT, BIG_HALF - BACK_CUT, [(halves_x, k)])
            send_y(k).start()
        elif group == 2:
            send_half_y(k).wait_recv()
            add(got, at, stage, slot, 0, BACK_CUT, [(halves_y, k)])
            add(got, at, stage, slot, BACK_CUT, BIG_HALF - BACK_CUT, [])
            send_x(k).start()
        else:
            send_x(k).wait_recv()
            send_y(k).wait_recv()
            add(got, at, stage, slot, 0, BIG_HALF, [(from_x, k), (from_y, k)])

    def bulk_z(k):
        at, zd = 12 + k, order[k]

        @pl.when(zd > z)
        def _():
            @pl.when(z > 0)
            def _():
                send_up(at, zd).wait_recv()
                add(got, at, from_low, zd - 1, 0, BIG_HALF, [])

            send_up(at, zd).start()

        @pl.when(zd < z)
        def _():
            @pl.when(z < 3)
            def _():
                send_down(at, zd).wait_recv()
                add(got, at, from_high, zd, 0, BIG_HALF, [])

            send_down(at, zd).start()

    def light_item(group, k):
        at, zd, column = 4 * group + k, order[k], l_column(group)
        l_fetch(group, k).wait()
        l_share(group, k).wait_recv()
        add(l_got, at, l_stage, at, 0, SMALL_HALF, [])

        def merge(ref, slot):
            l_got[at] = (l_got[at].astype(FULL) + ref[column, slot].astype(FULL)).astype(LOW)

        if k < 3:

            @pl.when(zd > z)
            def _():
                @pl.when(z > 0)
                def _():
                    l_up(group, k).wait_recv()
                    merge(l_low, zd - 1)

                l_up(group, k).start()

            @pl.when(zd < z)
            def _():
                @pl.when(z < 3)
                def _():
                    l_down(group, k).wait_recv()
                    merge(l_high, zd)

                l_down(group, k).start()

        else:

            @pl.when(z > 0)
            def _():
                l_up(group, k).wait_recv()
                merge(l_low, zd - 1)

            @pl.when(z < 3)
            def _():
                l_down(group, k).wait_recv()
                merge(l_high, zd)

            if group == 0:
                l_half_x().start()
                l_half_y().start()

    def light_sides():
        l_half_x().wait_recv()
        l_got[7, LIGHT_CUT:SMALL_HALF, :] = (
            l_got[7, LIGHT_CUT:SMALL_HALF, :].astype(FULL) + l_halves_x[...].astype(FULL)
        ).astype(LOW)
        l_send_y().start()
        l_half_y().wait_recv()
        l_got[11, 0:LIGHT_CUT, :] = (
            l_got[11, 0:LIGHT_CUT, :].astype(FULL) + l_halves_y[...].astype(FULL)
        ).astype(LOW)
        l_send_x().start()

    def light_end():
        l_send_x().wait_recv()
        l_send_y().wait_recv()
        l_total[...] = l_got[15].astype(FULL) + l_from_x[...].astype(FULL) + l_from_y[...].astype(FULL)

    small_join = remote(late_half, late.at[pl.ds(0, SMALL_HALF)], join_send.at[1], join_recv.at[1], sibling)
    own_late = pltpu.make_async_copy(late, out_small.at[me.dp], out_sem.at[1])

    def late_z(origin, target, way):
        block = out_small.at[2 * origin + y]
        return remote(block, block, late_send.at[way, origin], late_recv.at[0, origin], target)

    def late_y(origin, yo):
        block = out_small.at[2 * origin + yo]
        return remote(block, block, late_send.at[2, origin], late_recv.at[1, origin], y_side)

    def late_step(k):
        @pl.when((core == 1) & (z >= k))
        def _():
            late_z(z - k, up, 0).wait_recv()
            pl.when(z < 3)(lambda: late_z(z - k, up, 0).start())
            late_y(z - k, y).start()

        @pl.when((core == 1) & (z + k <= 3))
        def _():
            late_z(z + k, down, 1).wait_recv()
            pl.when(z > 0)(lambda: late_z(z + k, down, 1).start())
            late_y(z + k, y).start()

    def leave():
        for section in range(4):
            @pl.when(me.pipe == section)
            def _(section=section):
                all_of(keep(section), lambda copy: copy.start())

            @pl.when(me.pipe != section)
            def _(section=section):
                all_of(exchange(section), lambda copy: copy.start())

    def late_start():
        light_end()

        @pl.when(core == 0)
        def _():
            late_half[...] = l_total[...].astype(LOW)
            small_join.start()

        @pl.when(core == 1)
        def _():
            late[SMALL_HALF:SMALL_ROWS, :] = l_total[...].astype(LOW)
            small_join.wait_recv()
            own_late.start()
            own_late.wait()
            pl.when(z < 3)(lambda: late_z(z, up, 0).start())
            pl.when(z > 0)(lambda: late_z(z, down, 1).start())
            late_y(z, y).start()

    def light_round(k):
        for n in range(4 * k, 4 * k + 4):
            light_item(*l_sequence[n])

    edge = (z == 0) | (z == 3)

    def early_z(k):
        pl.when(edge)(lambda: bulk_z(k))

    def inner_z(k):
        pl.when(jnp.logical_not(edge))(lambda: bulk_z(k))

    actions = {"LS": [light_sides], "LE": [late_start], "G": [leave]}
    numbered = {item: n for n, item in enumerate(sequence)}
    for k in range(4):
        actions["A%d" % k] = [functools.partial(bulk_item, numbered[0, k])]
        actions["C%d" % k] = [functools.partial(bulk_item, numbered[1, k])]
        actions["B%d" % k] = [functools.partial(bulk_item, numbered[2, k])]
        actions["O%d" % k] = [functools.partial(bulk_item, numbered[3, k])]
        actions["L%d" % k] = [functools.partial(light_round, k)]
        if k < 3:
            actions["E%d" % k] = [functools.partial(early_z, k)]
            actions["I%d" % k] = [functools.partial(inner_z, k)]
        if k:
            actions["T%d" % k] = [functools.partial(late_step, k)]
    for event in REDUCE_ORDER:
        for action in actions[event]:
            action()

    row_copy.wait()
    part_sum[...] = jnp.sum((l_total[...] * l_total[...]).reshape(SMALL_HALF // 8, 8, 128), axis=0)
    lane = lax.broadcasted_iota(jnp.int32, (8, 128), 1)
    is_last = jnp.where((lane == me.dp) & (owner_row[...] == 7), 1.0, 0.0)
    weight = jnp.broadcast_to(jnp.sum(is_last, axis=1, keepdims=True), (8, 128))
    weight = jnp.where(core == 0, jnp.ones((8, 128), FULL), weight)

    def end(low, high):
        def piece(begin, size, scale):
            part = pl.ds(begin, size)
            sums = got[15, part, :].astype(FULL)
            if low:
                sums = sums + from_low[z - 1, part, :].astype(FULL)
            if high:
                sums = sums + from_high[z, part, :].astype(FULL)
            total[part, :] = sums
            squares = jnp.sum((sums * sums).reshape(size // 8, 8, 128), axis=0)
            part_sum[...] += squares if scale is None else squares * scale

        over(0, BIG_HALF - EDGE, lambda begin, size: piece(begin, size, None))
        piece(BIG_HALF - EDGE, EDGE, weight)

    @pl.when(z == 0)
    def _():
        send_down(15, z).wait_recv()
        end(False, True)

    @pl.when((z > 0) & (z < 3))
    def _():
        send_up(15, z).wait_recv()
        send_down(15, z).wait_recv()
        end(True, True)

    @pl.when(z == 3)
    def _():
        send_up(15, z).wait_recv()
        end(True, False)

    big_join = remote(total, out_big.at[1], join_send.at[0], join_recv.at[0], sibling)
    own_big = pltpu.make_async_copy(total, out_big.at[0], out_sem.at[0])

    @pl.when(core == 0)
    def _():
        own_big.start()

    @pl.when(core == 1)
    def _():
        big_join.start()

    def along_pipe(step, slot):
        target = {"dp": me.dp, "pipe": lax.rem(me.pipe + step, 4)}
        return remote(part_sum, by_pipe.at[slot], p_send.at[step], p_recv.at[step], target)

    def along_dp(step, slot):
        target = {"dp": lax.rem(me.dp + step, 8), "pipe": me.pipe}
        return remote(mine, by_dp.at[slot], d_send.at[step], d_recv.at[step], target)

    for step in range(1, 4):
        along_pipe(step, me.pipe).start()
    by_pipe[me.pipe] = part_sum[...]
    for step in range(1, 4):
        along_pipe(step, lax.rem(me.pipe + 4 - step, 4)).wait_recv()
    mine[...] = jnp.sum(by_pipe[...], axis=0)
    for step in range(1, 8):
        along_dp(step, me.dp).start()
    by_dp[me.dp] = mine[...]
    for step in range(1, 8):
        along_dp(step, lax.rem(me.dp + 8 - step, 8)).wait_recv()
    whole = jnp.sum(jnp.sum(by_dp[...], axis=0), axis=0, keepdims=True)
    length = jnp.sqrt(jnp.broadcast_to(jnp.sum(whole, axis=1, keepdims=True), (8, 128)))
    norm[...] = length
    factor[...] = jnp.minimum(1.0, CLIP_NORM / length)

    @pl.when(core == 0)
    def _():
        own_big.wait()
        big_join.wait_recv()
        small_join.wait_send()

    @pl.when(core == 1)
    def _():
        big_join.wait_send()
        for origin in range(4):
            late_y(origin, 1 - y).wait_recv()
            late_y(origin, y).wait_send()
            pl.when((z < 3) & (origin <= z))(lambda: late_z(origin, up, 0).wait_send())
            pl.when((z > 0) & (origin >= z))(lambda: late_z(origin, down, 1).wait_send())

    for other in range(4):
        @pl.when(me.pipe == other)
        def _(other=other):
            all_of(keep(other), lambda copy: copy.wait())

        @pl.when(me.pipe != other)
        def _(other=other):
            all_of(exchange(other), lambda copy: copy.wait_send())
            all_of(arriving(other), lambda copy: copy.wait_recv())

    for step in range(1, 4):
        along_pipe(step, me.pipe).wait_send()
    for step in range(1, 8):
        along_dp(step, me.dp).wait_send()
    for copy in (l_half_x(), l_half_y(), l_send_x(), l_send_y()):
        copy.wait_send()
    for k in range(4):
        send_half_x(k).wait_send()
        send_half_y(k).wait_send()
        send_x(k).wait_send()
        send_y(k).wait_send()
        for group in range(4):
            share(group, k).wait_send()
            l_share(group, k).wait_send()
    for k in range(3):
        zd, at = order[k], 12 + k

        @pl.when(zd > z)
        def _(at=at, zd=zd, k=k):
            send_up(at, zd).wait_send()
            for group in range(4):
                l_up(group, k).wait_send()

        @pl.when(zd < z)
        def _(at=at, zd=zd, k=k):
            send_down(at, zd).wait_send()
            for group in range(4):
                l_down(group, k).wait_send()


def reduce_all(big, small, wide0, wide1, final, stats, table):
    sem = pltpu.SemaphoreType.DMA
    vm = pltpu.VMEM
    lane_tile = jax.ShapeDtypeStruct((8, 128), FULL)
    return pl.pallas_call(
        reduce_kernel,
        name="reduce_all",
        out_shape=(
            jax.ShapeDtypeStruct((2, BIG_HALF, 128), FULL),
            jax.ShapeDtypeStruct((8, SMALL_ROWS, 128), LOW),
            jax.ShapeDtypeStruct((4, STUD_ROWS, C_OUT), LOW),
            jax.ShapeDtypeStruct((4, TEACH_END, C_OUT), LOW),
            jax.ShapeDtypeStruct((4,) + stats.shape[1:], FULL),
            lane_tile,
            lane_tile,
        ),
        in_specs=[any_spec()] * 7,
        out_specs=(any_spec(),) * 5 + (vmem_spec(),) * 2,
        scratch_shapes=[
            vm((16, BIG_HALF, 128), LOW), vm((4, BIG_HALF - BACK_CUT, 128), LOW), vm((4, BACK_CUT, 128), LOW),
            vm((4, BIG_HALF, 128), LOW), vm((4, BIG_HALF, 128), LOW),
            vm((3, BIG_HALF, 128), LOW), vm((3, BIG_HALF, 128), LOW),
            vm((4, BIG_HALF, 128), LOW), vm((BIG_HALF, 128), FULL),
            vm((16, SMALL_HALF, 128), LOW), vm((16, SMALL_HALF, 128), LOW),
            vm((4, 3, SMALL_HALF, 128), LOW), vm((4, 3, SMALL_HALF, 128), LOW),
            vm((SMALL_HALF - LIGHT_CUT, 128), LOW), vm((LIGHT_CUT, 128), LOW),
            vm((SMALL_HALF, 128), LOW), vm((SMALL_HALF, 128), LOW), vm((SMALL_HALF, 128), FULL),
            vm((SMALL_ROWS, 128), LOW), vm((SMALL_HALF, 128), LOW), vm((8, 128), jnp.int32),
            vm((4, 8, 128), FULL), vm((8, 8, 128), FULL), vm((8, 128), FULL), vm((8, 128), FULL),
            sem((2, 16)), sem((2, 16)),
            sem((5,)), sem((5,)), sem((5,)), sem((5,)), sem((5,)), sem((5,)), sem((5,)), sem((5,)),
            sem((3,)), sem((3,)), sem((3,)), sem((3,)),
            sem((4, 3)), sem((4, 3)), sem((4, 3)), sem((4, 3)),
            sem((4,)), sem((16,)), sem((3,)), sem((3, 4)), sem((2, 4)), sem((2,)), sem((2,)),
            sem((2, 4)), sem((2, 4)), sem((4,)), sem((4,)), sem((4,)), sem((4,)), sem((8,)), sem((8,)),
        ],
        compiler_params=pltpu.CompilerParams(
            collective_id=1, has_side_effects=True, vmem_limit_bytes=62 << 20
        ),
    )(big.reshape(2, 8, 2, BIG_HALF, 128), small.reshape(2, 8, 2, SMALL_HALF, 128),
      wide0, wide1, final, stats, table)


def high_dot(a, b, dims=((1,), (0,))):
    return lax.dot_general(a, b, (dims, ((), ())), precision=HIGH, preferred_element_type=FULL)


PIECES = 7
FRONT = 48


def update_kernel(owners, factor_ref, norm, big, small, gram_old, basis_old, params, moment, second,
                  clipped, moment_new, second_new, params_new, gram_new, basis_new, length,
                  tiles, low, grad, held, rotated, weights, gram, in_sem, out_sem, tile_sem):
    factor = factor_ref[0:1, :]
    length[0, 0] = jnp.max(norm[...])
    block, section = owners[0, lax.axis_index("dp")], lax.axis_index("pipe")
    even = lax.rem(section, 2) == 0
    span = params.shape[0]
    piece = held.shape[0] // PIECES

    @pl.when(even)
    def _():
        pltpu.make_async_copy(big, tiles.at[pl.ds(0, BIG_ROWS)], tile_sem).start()

    def loads(i):
        part = pl.ds(piece * i, min(piece, span - piece * i))
        for n, (src, dst) in enumerate(((params, weights), (moment, held), (second, rotated))):
            yield pltpu.make_async_copy(src.at[part, 0, :], dst.at[part], in_sem.at[n, i])

    def stores(i):
        count = min(piece, span - piece * i)
        part = pl.ds(piece * i, count)
        yield pltpu.make_async_copy(
            grad.at[pl.ds(FRONT + piece * i, count)], clipped.at[part, 0, :], out_sem.at[3, i])
        pairs = ((held, moment_new), (rotated, second_new), (weights, params_new))
        for n, (src, dst) in enumerate(pairs):
            yield pltpu.make_async_copy(src.at[part], dst.at[part, 0, :], out_sem.at[n, i])

    for i in range(PIECES):
        for load in loads(i):
            load.start()

    @pl.when(even)
    def _():
        pltpu.make_async_copy(big, tiles.at[pl.ds(0, BIG_ROWS)], tile_sem).wait()

    @pl.when(jnp.logical_not(even))
    def _():
        low[...] = jnp.zeros_like(low)

        @pl.when(block == 0)
        def _():
            copy = pltpu.make_async_copy(small.at[0:20], low, tile_sem)
            copy.start()
            copy.wait()

        @pl.when(block == 1)
        def _():
            copy = pltpu.make_async_copy(small.at[19:33], low.at[0:14], tile_sem)
            copy.start()
            copy.wait()

        @pl.loop(0, WINDOW)
        def _(r):
            tiles[pl.ds(pl.multiple_of(TILE * r, TILE), TILE), :] = low[r].astype(FULL)

    @pl.loop(0, WINDOW)
    def _(r):
        narrow, plain = tile_forms(section, STRIDE * block + r)
        edge = even & (r == STRIDE)
        narrow, plain = narrow & jnp.logical_not(edge), plain | edge
        base = FRONT - 6 * block + TILE * r
        here = pl.multiple_of(TILE * r, TILE)

        @pl.when(narrow)
        def _():
            for j in range(4):
                grad[pl.ds(base + j, 64, 4), :] = tiles[pl.ds(here + 64 * j, 64), :]

        @pl.when(plain)
        def _():
            grad[pl.ds(base, TILE), :] = tiles[pl.ds(here, TILE), :]

        @pl.when(jnp.logical_not(narrow | plain))
        def _():
            for j in range(16):
                grad[pl.ds(base + j, 16, 16), :] = tiles[pl.ds(here + 16 * j, 16), :]

    tail = piece * PIECES - 8
    rest = lax.broadcasted_iota(jnp.int32, (8, 128), 0) + tail
    grad[FRONT + tail : FRONT + tail + 8, :] = jnp.where(
        rest < span, grad[FRONT + tail : FRONT + tail + 8, :], 0.0
    )
    gram[...] = jnp.zeros_like(gram)

    def halves(value):
        high = value.astype(LOW)
        return high, (value - high.astype(FULL)).astype(LOW)

    def split_dot(a, b, dims=((1,), (0,))):
        def dot(left, right):
            return lax.dot_general(left, right, (dims, ((), ())), preferred_element_type=FULL)

        return dot(a[0], b[0]) + (dot(a[0], b[1]) + dot(a[1], b[0]))

    @pl.loop(0, PIECES)
    def _(i):
        part = halves(grad[pl.ds(pl.multiple_of(FRONT + piece * i, 8), piece), :])
        gram[...] += split_dot(part, part, ((0,), (0,)))

    old = basis_old[...]
    fresh = DECAY_STATS * gram_old[...] + (1.0 - DECAY_STATS) * (gram[...] * (factor * factor))
    gram_new[...] = fresh
    product = high_dot(fresh, old)
    rotation = product / jnp.sqrt(jnp.sum(product * product))
    for repeat in range(NS_STEPS):
        parts = halves(rotation)
        square = split_dot(parts, parts, ((0,), (0,)))
        rotation = 1.5 * rotation - 0.5 * split_dot(parts, halves(square))
    basis_new[...] = rotation
    change = halves(high_dot(old, rotation, ((0,), (0,))))
    turn = halves(rotation)
    correction = math.sqrt(1.0 - DECAY_SECOND**STEP) / (1.0 - DECAY_FIRST**STEP)
    for i in range(PIECES):
        for load in loads(i):
            load.wait()
        at = slice(FRONT + piece * i, FRONT + piece * i + piece)
        part = slice(piece * i, piece * i + piece)
        clip = grad[at, :] * factor
        grad[at, :] = clip
        turned = split_dot(halves(clip), turn)
        first = DECAY_FIRST * split_dot(halves(held[part, :]), change) + (1.0 - DECAY_FIRST) * turned
        power = DECAY_SECOND * rotated[part, :] + (1.0 - DECAY_SECOND) * turned * turned
        held[part, :] = first
        rotated[part, :] = power
        scaled = halves(first / (jnp.sqrt(power) + ADAM_EPS))
        direction = split_dot(scaled, turn, ((1,), (1,))) * correction
        before = weights[part, :]
        weights[part, :] = before - LEARN_RATE * (direction + WEIGHT_DECAY * before)
        for store in stores(i):
            store.start()
    for i in range(PIECES):
        for store in stores(i):
            store.wait()


def update(owners, factor, norm, big, small, gram_old, basis_old, params, moment, second):
    span = params.shape[1] // 128
    rows = -(-span // (8 * PIECES)) * 8 * PIECES
    flat_shape = jax.ShapeDtypeStruct((span, 1, 128), FULL)
    square = jax.ShapeDtypeStruct((128, 128), FULL)
    sem = pltpu.SemaphoreType.DMA
    vm = pltpu.VMEM
    outs = pl.pallas_call(
        update_kernel,
        name="update",
        out_shape=(flat_shape,) * 4 + (square,) * 2 + (jax.ShapeDtypeStruct((1, 1), FULL),),
        in_specs=[smem_spec()] + [vmem_spec()] * 2 + [any_spec()] * 2 + [vmem_spec()] * 2 + [any_spec()] * 3,
        out_specs=(any_spec(),) * 4 + (vmem_spec(),) * 2 + (smem_spec(),),
        scratch_shapes=[
            vm((WINDOW * TILE, 128), FULL), vm((WINDOW, TILE, 128), LOW),
            vm((FRONT + WINDOW * TILE, 128), FULL), vm((rows, 128), FULL), vm((rows, 128), FULL),
            vm((rows, 128), FULL), vm((128, 128), FULL), sem((3, PIECES)), sem((4, PIECES)), sem,
        ],
        compiler_params=pltpu.CompilerParams(vmem_limit_bytes=60 << 20),
    )(owners, factor, norm, big.reshape(BIG_ROWS, 128), small.reshape(USED_TILES[1], TILE, 128),
      gram_old, basis_old, params.reshape(span, 1, 128), moment.reshape(span, 1, 128),
      second.reshape(span, 1, 128))
    return tuple(out.reshape(1, span * 128) for out in outs[:4]) + outs[4:]


def to_phases(teach, stud):
    def split(part, axes):
        crops, high, across, channels = part.shape
        part = part.reshape(crops, high // 2, 2, across // 2, 2, channels).transpose(axes)
        return part.reshape(4, -1, channels)

    zeros = jnp.zeros((4, PADDED - ROWS, teach.shape[-1]), teach.dtype)
    parts = [split(stud, (2, 4, 0, 1, 3, 5)), split(teach, (2, 4, 1, 3, 0, 5)), zeros]
    return jnp.concatenate(parts, axis=1)


def from_phases(phases, shape, crops_last):
    crops, high, across, channels = shape
    if crops_last:
        part = phases.reshape(2, 2, high // 2, across // 2, crops, channels).transpose(4, 2, 0, 3, 1, 5)
    else:
        part = phases.reshape(2, 2, crops, high // 2, across // 2, channels).transpose(2, 3, 0, 4, 1, 5)
    return part.reshape(shape)


def on_small_slice(
    teach_in,
    stud_in,
    params,
    owners,
    depth_gates,
    teach_ids,
    stud_ids,
    targets,
    moment,
    second,
    gram_stats,
    eigen_basis,
):
    phases = to_phases(teach_in[0], stud_in[0])
    big, small, ids = prepare(owners, params)
    all_big, all_small, table = gather_all(big, small, ids)
    wide_0, wide_1, final, stats, grad_x, out_big, out_small = run_step(
        table,
        depth_gates,
        teach_ids.T,
        stud_ids,
        all_big.reshape(2, 8, BIG_ROWS, 128),
        all_small.reshape(2, USED_TILES[1], TILE, 128),
        phases,
        targets,
    )
    sum_big, sum_small, segment_stud, segment_teach, stats, norm, factor = reduce_all(
        out_big, out_small, wide_0, wide_1, final, stats, table
    )
    clipped, moment_new, second_new, params_new, gram_new, rotation, length = update(
        owners, factor, norm, sum_big, sum_small, gram_stats[0], eigen_basis[0], params, moment, second
    )
    teach_shape, stud_shape = teach_in.shape[1:], stud_in.shape[1:]
    small_teach = (teach_shape[1] // 2, teach_shape[2] // 2, teach_shape[0], C_OUT)
    small_stud = (stud_shape[0], stud_shape[1] // 2, stud_shape[2] // 2, C_OUT)
    segment_teach = segment_teach[:, : ROWS - STUD_ROWS].reshape((4,) + small_teach).transpose(0, 3, 1, 2, 4)
    segment_stud = segment_stud.reshape((4,) + small_stud)
    stats = stats[:, 0:2]
    teach_grad = from_phases(grad_x[:, STUD_ROWS:ROWS], teach_shape, True)
    stud_grad = from_phases(grad_x[:, :STUD_ROWS], stud_shape, False)
    grad_norm = length.reshape(())
    return (
        segment_teach[None],
        segment_stud[None],
        teach_grad[None],
        stud_grad[None],
        stats[None, :, None],
        grad_norm,
        clipped,
        moment_new,
        second_new,
        params_new,
        gram_new[None],
        rotation[None],
    )


def solution(mesh):
    placed = (
        P("pipe", "dp", None, None, None),
        P("pipe", "dp", None, None, None),
        P("pipe", "dp"),
        P("pipe", None),
        P(),
        P(None, "dp"),
        P(None, "dp"),
        P(),
        P("pipe", "dp"),
        P("pipe", "dp"),
        P("pipe", "dp", None),
        P("pipe", "dp", None),
    )
    small_slice = mesh.shape["dp"] == 8 and mesh.shape["pipe"] == 4
    return jax.shard_map(
        on_small_slice if small_slice else on_device,
        mesh=mesh,
        in_specs=placed,
        out_specs=(
            P("pipe", None, "dp", None, None, None),
            P("pipe", None, "dp", None, None, None),
            P("pipe", "dp", None, None, None),
            P("pipe", "dp", None, None, None),
            P("pipe", None, "dp", None, None),
            P(),
            P("pipe", "dp"),
            P("pipe", "dp"),
            P("pipe", "dp"),
            P("pipe", "dp"),
            P("pipe", "dp", None),
            P("pipe", "dp", None),
        ),
        check_vma=False,
    )
```

```python
import functools
import math

import jax
import jax.numpy as jnp
import numpy as np
from jax import lax
from jax.experimental import pallas as pl
from jax.experimental.pallas import tpu as pltpu
from jax.sharding import PartitionSpec as P

C_IN = 1024
MID = 512
C_OUT = 2048
STEP = 10
NS_STEPS = 5


HIGH = lax.Precision.HIGHEST
NORM_EPS = 1e-05
POOL_EPS = 1e-06
CLIP_NORM = 1.0
LEARN_RATE = 0.02
DECAY_FIRST = 0.9
DECAY_SECOND = 0.95
DECAY_STATS = 0.95
ADAM_EPS = 1e-08
WEIGHT_DECAY = 0.01


def section_shapes(section):
    if section == 0:
        return [
            ("first_conv", (C_IN, MID)),
            ("middle_conv", (9 * MID, MID)),
            ("skip_conv", (C_IN, C_OUT)),
            ("first_gain", (MID,)),
            ("first_bias", (MID,)),
            ("middle_gain", (MID,)),
            ("middle_bias", (MID,)),
            ("skip_gain", (C_OUT,)),
            ("skip_bias", (C_OUT,)),
        ]
    if section == 2:
        return [
            ("first_conv", (C_OUT, MID)),
            ("middle_conv", (9 * MID, MID)),
            ("first_gain", (MID,)),
            ("first_bias", (MID,)),
            ("middle_gain", (MID,)),
            ("middle_bias", (MID,)),
        ]
    return [("last_conv", (MID, C_OUT)), ("last_gain", (C_OUT,)), ("last_bias", (C_OUT,))]


def unpack(flat_vector, section):
    pieces = {}
    offset = 0
    for entry_name, entry_shape in section_shapes(section):
        entry_size = math.prod(entry_shape)
        pieces[entry_name] = flat_vector[offset : offset + entry_size].reshape(entry_shape)
        offset = offset + entry_size
    return pieces


def pack(grads, section, flat_size):
    parts = [grads[entry_name].reshape(-1) for entry_name, entry_shape in section_shapes(section)]
    used = sum((math.prod(entry_shape) for entry_name, entry_shape in section_shapes(section)))
    parts.append(jnp.zeros((flat_size - used,), jnp.float32))
    return jnp.concatenate(parts)


def as_float(vector):
    return vector.astype(jnp.float32)


def to_low(groups):
    return tuple((portion.astype(jnp.bfloat16) for portion in groups))


def to_high(groups):
    return tuple((portion.astype(jnp.float32) for portion in groups))


def point_conv(groups, weight):
    return tuple(
        (
            jnp.einsum("khwc,cd->khwd", portion, weight, preferred_element_type=jnp.float32)
            for portion in groups
        )
    )


def point_back(grad_out, groups, weight):
    low_grads = to_low(grad_out)
    grad_input = tuple(
        (
            jnp.einsum("khwd,cd->khwc", grad_part, weight, preferred_element_type=jnp.float32)
            for grad_part in low_grads
        )
    )
    grad_weight = sum(
        (
            jnp.einsum("khwc,khwd->cd", in_part, grad_part, preferred_element_type=jnp.float32)
            for in_part, grad_part in zip(groups, low_grads)
        )
    )
    return (grad_input, grad_weight)


def patches(portion, stride):
    height = portion.shape[1]
    across = portion.shape[2]
    padded = jnp.pad(portion, ((0, 0), (1, 1), (1, 1), (0, 0)))
    shifted = [
        padded[:, row_off : row_off + height : stride, col_off : col_off + across : stride, :]
        for row_off in range(3)
        for col_off in range(3)
    ]
    return jnp.concatenate(shifted, axis=-1)


def area_conv(groups, weight, stride):
    columns = tuple((patches(portion, stride) for portion in groups))
    return (point_conv(columns, weight), columns)


def unpatch(grad_cols, height, across, stride):
    channels = grad_cols.shape[-1] // 9
    padded = jnp.zeros((grad_cols.shape[0], height + 2, across + 2, channels), jnp.float32)
    for row_off in range(3):
        for col_off in range(3):
            offset = (3 * row_off + col_off) * channels
            padded = padded.at[
                :, row_off : row_off + height : stride, col_off : col_off + across : stride, :
            ].add(grad_cols[..., offset : offset + channels])
    return padded[:, 1 : height + 1, 1 : across + 1, :]


def area_back(grad_out, columns, weight, stride, in_shapes):
    grad_cols, grad_weight = point_back(grad_out, columns, weight)
    grad_input = tuple(
        (
            unpatch(grad_part, shape_item[1], shape_item[2], stride)
            for grad_part, shape_item in zip(grad_cols, in_shapes)
        )
    )
    return (grad_input, grad_weight)


def batch_norm(groups, gain, bias):
    rows_total = sum((portion.shape[0] * portion.shape[1] * portion.shape[2] for portion in groups))
    centre = sum((jnp.sum(portion, axis=(0, 1, 2)) for portion in groups)) / rows_total
    spread = (
        sum((jnp.sum(jnp.square(portion - centre), axis=(0, 1, 2)) for portion in groups))
        / rows_total
    )
    inverse = lax.rsqrt(spread + NORM_EPS)
    standard = tuple(((portion - centre) * inverse for portion in groups))
    normed = tuple((gain * std_part + bias for std_part in standard))
    return (normed, (centre, spread, inverse, standard))


def norm_back(grad_out, gain, saved):
    centre, spread, inverse, standard = saved
    rows_total = sum(
        (portion.shape[0] * portion.shape[1] * portion.shape[2] for portion in standard)
    )
    grad_sum = sum((jnp.sum(grad_part, axis=(0, 1, 2)) for grad_part in grad_out))
    grad_dot = sum(
        (
            jnp.sum(grad_part * std_part, axis=(0, 1, 2))
            for grad_part, std_part in zip(grad_out, standard)
        )
    )
    grad_input = tuple(
        (
            gain
            * inverse
            * (grad_part - grad_sum / rows_total - std_part * (grad_dot / rows_total))
            for grad_part, std_part in zip(grad_out, standard)
        )
    )
    return (grad_input, grad_dot, grad_sum)


def through_softplus(grad_out, pre_values):
    return tuple(
        (grad_part * jax.nn.sigmoid(pre_part) for grad_part, pre_part in zip(grad_out, pre_values))
    )


def front_forward(pieces, inputs):
    first = point_conv(inputs, pieces["first_conv"])
    normed_a, saved_a = batch_norm(
        first, as_float(pieces["first_gain"]), as_float(pieces["first_bias"])
    )
    hidden = tuple((jax.nn.softplus(portion).astype(jnp.bfloat16) for portion in normed_a))
    middle, columns = area_conv(hidden, pieces["middle_conv"], 2)
    normed_b, saved_b = batch_norm(
        middle, as_float(pieces["middle_gain"]), as_float(pieces["middle_bias"])
    )
    narrow = tuple((jax.nn.softplus(portion) for portion in normed_b))
    reduced = tuple((portion[:, ::2, ::2, :] for portion in inputs))
    skipped = point_conv(reduced, pieces["skip_conv"])
    wide, saved_p = batch_norm(
        skipped, as_float(pieces["skip_gain"]), as_float(pieces["skip_bias"])
    )
    norm_rows = jnp.stack(
        [
            jnp.concatenate([saved_a[0], saved_b[0], saved_p[0]]),
            jnp.concatenate([saved_a[1], saved_b[1], saved_p[1]]),
        ]
    )
    kept = (normed_a, hidden, columns, normed_b, reduced, saved_a, saved_b, saved_p)
    return (wide, narrow, norm_rows, kept)


def front_backward(pieces, inputs, grad_wide, grad_narrow):
    wide, narrow, norm_rows, kept = front_forward(pieces, inputs)
    normed_a, hidden, columns, normed_b, reduced, saved_a, saved_b, saved_p = kept
    grads = {}
    grad_pre_b = through_softplus(grad_narrow, normed_b)
    grad_mid, grads["middle_gain"], grads["middle_bias"] = norm_back(
        grad_pre_b, as_float(pieces["middle_gain"]), saved_b
    )
    grad_hidden, grads["middle_conv"] = area_back(
        grad_mid, columns, pieces["middle_conv"], 2, [portion.shape for portion in hidden]
    )
    grad_pre_a = through_softplus(grad_hidden, normed_a)
    grad_first, grads["first_gain"], grads["first_bias"] = norm_back(
        grad_pre_a, as_float(pieces["first_gain"]), saved_a
    )
    grad_inputs, grads["first_conv"] = point_back(grad_first, inputs, pieces["first_conv"])
    grad_skip, grads["skip_gain"], grads["skip_bias"] = norm_back(
        grad_wide, as_float(pieces["skip_gain"]), saved_p
    )
    grad_reduced, grads["skip_conv"] = point_back(grad_skip, reduced, pieces["skip_conv"])
    grad_inputs = tuple(
        (
            full_part.at[:, ::2, ::2, :].add(part_reduced)
            for full_part, part_reduced in zip(grad_inputs, grad_reduced)
        )
    )
    return (grad_inputs, grads)


def join_forward(pieces, wide, narrow):
    last = point_conv(narrow, pieces["last_conv"])
    normed, saved = batch_norm(last, as_float(pieces["last_gain"]), as_float(pieces["last_bias"]))
    pre_values = tuple(
        (
            skip_part.astype(jnp.float32) + branch_part
            for skip_part, branch_part in zip(wide, normed)
        )
    )
    ending = tuple((jax.nn.softplus(pre_part) for pre_part in pre_values))
    filler = jnp.zeros((2 * MID,), jnp.float32)
    norm_rows = jnp.stack(
        [jnp.concatenate([saved[0], filler]), jnp.concatenate([saved[1], filler])]
    )
    return (ending, norm_rows, (pre_values, saved))


def join_grads(pieces, narrow, kept, grad_out, gate):
    pre_values, saved = kept
    grad_pre = tuple(
        (
            grad_part * jax.nn.sigmoid(pre_part) * gate
            for grad_part, pre_part in zip(grad_out, pre_values)
        )
    )
    grad_wide = tuple(
        (pre_grad + grad_part * (1.0 - gate) for pre_grad, grad_part in zip(grad_pre, grad_out))
    )
    grad_last, gain_grad, bias_grad = norm_back(grad_pre, as_float(pieces["last_gain"]), saved)
    grad_narrow, weight_grad = point_back(grad_last, narrow, pieces["last_conv"])
    grads = {"last_conv": weight_grad, "last_gain": gain_grad, "last_bias": bias_grad}
    return (grad_wide, grad_narrow, grads)


def split_forward(pieces, wide):
    first = point_conv(wide, pieces["first_conv"])
    normed_a, saved_a = batch_norm(
        first, as_float(pieces["first_gain"]), as_float(pieces["first_bias"])
    )
    hidden = tuple((jax.nn.softplus(portion).astype(jnp.bfloat16) for portion in normed_a))
    middle, columns = area_conv(hidden, pieces["middle_conv"], 1)
    normed_b, saved_b = batch_norm(
        middle, as_float(pieces["middle_gain"]), as_float(pieces["middle_bias"])
    )
    narrow = tuple((jax.nn.softplus(portion) for portion in normed_b))
    filler = jnp.zeros((C_OUT,), jnp.float32)
    norm_rows = jnp.stack(
        [
            jnp.concatenate([saved_a[0], saved_b[0], filler]),
            jnp.concatenate([saved_a[1], saved_b[1], filler]),
        ]
    )
    return (narrow, norm_rows, (normed_a, hidden, columns, normed_b, saved_a, saved_b))


def split_backward(pieces, wide, grad_relay, grad_narrow):
    narrow, norm_rows, kept = split_forward(pieces, wide)
    normed_a, hidden, columns, normed_b, saved_a, saved_b = kept
    grads = {}
    grad_pre_b = through_softplus(grad_narrow, normed_b)
    grad_mid, grads["middle_gain"], grads["middle_bias"] = norm_back(
        grad_pre_b, as_float(pieces["middle_gain"]), saved_b
    )
    grad_hidden, grads["middle_conv"] = area_back(
        grad_mid, columns, pieces["middle_conv"], 1, [portion.shape for portion in hidden]
    )
    grad_pre_a = through_softplus(grad_hidden, normed_a)
    grad_first, grads["first_gain"], grads["first_bias"] = norm_back(
        grad_pre_a, as_float(pieces["first_gain"]), saved_a
    )
    grad_conv_in, grads["first_conv"] = point_back(grad_first, wide, pieces["first_conv"])
    grad_wide = tuple(
        (relay_part + conv_part for relay_part, conv_part in zip(grad_relay, grad_conv_in))
    )
    return (grad_wide, grads)


def pool_grad(final, targets, picks):
    result = []
    for portion, pick_ids in zip(final, picks):
        cubes = jnp.mean(portion * portion * portion, axis=(1, 2)) + POOL_EPS
        factor = jnp.exp(jnp.log(cubes) * (-2.0 / 3.0)) * targets[pick_ids]
        result.append(factor[:, None, None, :] * portion * portion)
    return tuple(result)


def used_size(section):
    return sum((math.prod(entry_shape) for entry_name, entry_shape in section_shapes(section)))


def batch_pass(reals, inputs, gate, targets, picks):
    pieces = [unpack(reals[section], section) for section in range(4)]
    wide_f, narrow_f, rows_0, _ = front_forward(pieces[0], inputs)
    wide_0, narrow_0 = to_low(wide_f), to_low(narrow_f)
    ending_1, rows_1, kept_1 = join_forward(pieces[1], wide_0, narrow_0)
    wide_1 = to_low(ending_1)
    narrow_f, rows_2, _ = split_forward(pieces[2], wide_1)
    narrow_2 = to_low(narrow_f)
    ending_3, rows_3, kept_3 = join_forward(pieces[3], wide_1, narrow_2)
    final = tuple(
        (
            jnp.where(gate > 0, end_part, relay_part.astype(jnp.float32))
            for end_part, relay_part in zip(ending_3, wide_1)
        )
    )
    cotangent = pool_grad(final, targets, picks)
    grad_wide, grad_narrow, grads_3 = join_grads(pieces[3], narrow_2, kept_3, cotangent, gate)
    grad_wide, grads_2 = split_backward(
        pieces[2], wide_1, to_high(to_low(grad_wide)), to_high(to_low(grad_narrow))
    )
    grad_wide, grad_narrow, grads_1 = join_grads(
        pieces[1], narrow_0, kept_1, to_high(to_low(grad_wide)), 1.0
    )
    grad_inputs, grads_0 = front_backward(
        pieces[0], inputs, to_high(to_low(grad_wide)), to_high(to_low(grad_narrow))
    )
    outs = (wide_0, wide_1, wide_1, to_low(final))
    stats = jnp.stack([rows_0, rows_1, rows_2 * gate, rows_3 * gate])
    return (outs, stats, to_low(grad_inputs), (grads_0, grads_1, grads_2, grads_3))


def on_device(
    teach_in,
    stud_in,
    params,
    owners,
    depth_gates,
    teach_ids,
    stud_ids,
    targets,
    moment,
    second,
    gram_stats,
    eigen_basis,
):
    sections = lax.axis_size("pipe")
    rank = lax.axis_index("pipe")
    owner_count = lax.axis_size("dp")
    span_size = params.shape[1]
    flat_size = span_size * owner_count
    owner_rows = lax.all_gather(owners, "pipe", axis=0, tiled=True)
    gathered = lax.all_gather(params[0].astype(jnp.bfloat16), ("pipe", "dp"), axis=0)
    gathered = gathered.reshape(sections, owner_count, span_size)
    reals = []
    for section in range(sections):
        inverse = jnp.argsort(owner_rows[section]).astype(jnp.int32)
        blocks = -(-used_size(section) // span_size)
        reals.append(gathered[section][inverse[:blocks]].reshape(blocks * span_size))
    inputs = (teach_in[0], stud_in[0])
    gate = depth_gates[rank].astype(jnp.float32)
    outs, stats, (teach_grad, stud_grad), grads = batch_pass(
        reals, inputs, gate, targets, (teach_ids[rank], stud_ids[rank])
    )
    segment_teach = lax.all_to_all(
        jnp.stack([part[0] for part in outs]), "pipe", split_axis=0, concat_axis=0, tiled=True
    )
    segment_stud = lax.all_to_all(
        jnp.stack([part[1] for part in outs]), "pipe", split_axis=0, concat_axis=0, tiled=True
    )
    stats = lax.all_to_all(stats, "pipe", split_axis=0, concat_axis=0, tiled=True)
    rows = []
    for section in range(sections):
        flat = pack(grads[section], section, flat_size).reshape(owner_count, span_size)
        rows.append(flat[owner_rows[section]])
    span_total = lax.psum_scatter(
        jnp.stack(rows).reshape(sections * owner_count, span_size),
        ("pipe", "dp"),
        scatter_dimension=0,
        tiled=True,
    ).reshape(span_size)
    total_squares = lax.psum(jnp.sum(span_total * span_total), ("dp", "pipe"))
    grad_norm = jnp.sqrt(total_squares)
    factor = jnp.minimum(1.0, CLIP_NORM / grad_norm)
    clipped = span_total * factor
    matrix = clipped.reshape(span_size // 128, 128)
    gram_old = gram_stats[0]
    basis_old = eigen_basis[0]
    gram_new = DECAY_STATS * gram_old + (1.0 - DECAY_STATS) * jnp.dot(
        matrix.T, matrix, precision=HIGH
    )
    product = jnp.dot(gram_new, basis_old, precision=HIGH)
    rotation = product / jnp.sqrt(jnp.sum(product * product))
    for repeat in range(NS_STEPS):
        square = jnp.dot(rotation.T, rotation, precision=HIGH)
        rotation = 1.5 * rotation - 0.5 * jnp.dot(rotation, square, precision=HIGH)
    moment_old = moment.reshape(span_size // 128, 128)
    initial = jnp.dot(moment_old, basis_old.T, precision=HIGH)
    blended = DECAY_FIRST * initial + (1.0 - DECAY_FIRST) * matrix
    moment_new = jnp.dot(blended, rotation, precision=HIGH)
    rotated = jnp.dot(matrix, rotation, precision=HIGH)
    second_new = (
        DECAY_SECOND * second.reshape(span_size // 128, 128)
        + (1.0 - DECAY_SECOND) * rotated * rotated
    )
    correction = math.sqrt(1.0 - DECAY_SECOND**STEP) / (1.0 - DECAY_FIRST**STEP)
    direction = (
        jnp.dot(moment_new / (jnp.sqrt(second_new) + ADAM_EPS), rotation.T, precision=HIGH)
        * correction
    )
    weights = params.reshape(span_size // 128, 128)
    params_new = weights - LEARN_RATE * (direction + WEIGHT_DECAY * weights)
    return (
        segment_teach[None],
        segment_stud[None],
        teach_grad[None],
        stud_grad[None],
        stats[None, :, None],
        grad_norm,
        clipped.reshape(1, span_size),
        moment_new.reshape(1, span_size),
        second_new.reshape(1, span_size),
        params_new.reshape(1, span_size),
        gram_new[None],
        rotation[None],
    )


MESH = pl.DeviceIdType.MESH
LOW = jnp.bfloat16
FULL = jnp.float32
TILE = 256
WINDOW = 20
STRIDE = 19
EDGE = 64
BIG_ROWS = STRIDE * TILE + EDGE
VEC_TILE = (152, 32, 104, 32)
USED_TILES = (153, 33, 105, 33)
FRONT_WIDE = 88
SMALL_ROWS = 1056
ROWS = 120
PADDED = 128
STUD_ROWS = 48
TEACH_END = 80


def any_spec():
    return pl.BlockSpec(memory_space=pl.ANY)


def smem_spec():
    return pl.BlockSpec(memory_space=pltpu.SMEM)


def vmem_spec():
    return pl.BlockSpec(memory_space=pltpu.VMEM)


def tile_forms(section, tile):
    even = lax.rem(section, 2) == 0
    vector = jnp.where(section == 0, 152, jnp.where(section == 2, 104, 32))
    narrow_end = jnp.where(section == 0, FRONT_WIDE, jnp.where(section == 2, 104, 0))
    narrow = even & (tile < narrow_end)
    plain = tile == vector
    return narrow, plain


def prepare_kernel(owners, params, big, small, ids, flat, sem):
    block, section = owners[0, lax.axis_index("dp")], lax.axis_index("pipe")

    even = lax.rem(section, 2) == 0
    flat[0:EDGE, :] = jnp.zeros((EDGE, 128), FULL)
    flat[STRIDE * TILE : WINDOW * TILE, :] = jnp.zeros((TILE, 128), FULL)
    copy = pltpu.make_async_copy(params.at[:, 0, :], flat.at[pl.ds(6 * block, params.shape[0])], sem)
    copy.start()

    @pl.when(jnp.logical_not(even))
    def _():
        @pl.loop(0, small.shape[0])
        def _(r):
            small[r] = jnp.zeros((TILE, 128), LOW)

    lane = lax.broadcasted_iota(jnp.int32, (8, 128), 1)
    row = jnp.zeros((8, 128), jnp.int32)
    for j in range(8):
        row = jnp.where(lane == j, owners[0, j], row)
    ids[...] = row
    copy.wait()

    def wide_tile(base):
        return [flat[pl.ds(base + j, 16, 16), :].astype(LOW) for j in range(16)]

    @pl.when(even)
    def _():
        @pl.loop(0, STRIDE)
        def _(r):
            narrow, plain = tile_forms(section, STRIDE * block + r)
            base = pl.multiple_of(TILE * r, TILE)

            @pl.when(narrow)
            def _():
                for j in range(4):
                    big[pl.ds(base + 64 * j, 64), :] = flat[pl.ds(base + j, 64, 4), :].astype(LOW)

            @pl.when(plain)
            def _():
                big[pl.ds(base, TILE), :] = flat[pl.ds(base, TILE), :].astype(LOW)

            @pl.when(jnp.logical_not(narrow | plain))
            def _():
                for j, part in enumerate(wide_tile(base)):
                    big[pl.ds(base + 16 * j, 16), :] = part

        big[STRIDE * TILE : BIG_ROWS, :] = flat[STRIDE * TILE : BIG_ROWS, :].astype(LOW)

    @pl.when(jnp.logical_not(even))
    def _():
        @pl.loop(0, WINDOW)
        def _(r):
            tile = STRIDE * block + r
            base = pl.multiple_of(TILE * r, TILE)

            @pl.when(tile == VEC_TILE[1])
            def _():
                small[tile] = flat[pl.ds(base, TILE), :].astype(LOW)

            @pl.when(tile < VEC_TILE[1])
            def _():
                for j, part in enumerate(wide_tile(base)):
                    small[tile, 16 * j : 16 * j + 16, :] = part


def prepare(owners, params):
    return pl.pallas_call(
        prepare_kernel,
        name="prepare",
        out_shape=(
            jax.ShapeDtypeStruct((BIG_ROWS, 128), LOW),
            jax.ShapeDtypeStruct((USED_TILES[1], TILE, 128), LOW),
            jax.ShapeDtypeStruct((8, 128), jnp.int32),
        ),
        in_specs=[smem_spec(), any_spec()],
        out_specs=(vmem_spec(),) * 3,
        scratch_shapes=[pltpu.VMEM((WINDOW * TILE, 128), FULL), pltpu.SemaphoreType.DMA],
        compiler_params=pltpu.CompilerParams(vmem_limit_bytes=60 << 20),
    )(owners, params.reshape(-1, 1, 128))


class Place:
    def __init__(self):
        self.dp = lax.axis_index("dp")
        self.pipe = lax.axis_index("pipe")
        self.x, self.core = self.pipe // 2, self.pipe % 2
        self.z, self.y = self.dp // 2, self.dp % 2

    def device(self, x=None, core=None, z=None, y=None):
        x = self.x if x is None else x
        core = self.core if core is None else core
        z = self.z if z is None else z
        y = self.y if y is None else y
        return {"dp": 2 * z + y, "pipe": 2 * x + core}

    def enter(self):
        barrier = pltpu.get_barrier_semaphore()
        for step in range(1, 8):
            other = lax.rem(self.dp + step, 8)
            pl.semaphore_signal(
                barrier, inc=1, device_id={"dp": other, "pipe": self.pipe}, device_id_type=MESH
            )
        for step in range(1, 4):
            other = lax.rem(self.pipe + step, 4)
            pl.semaphore_signal(
                barrier, inc=1, device_id={"dp": self.dp, "pipe": other}, device_id_type=MESH
            )
        pl.semaphore_wait(barrier, 10)


def remote(src, dst, send, recv, target):
    return pltpu.make_async_remote_copy(
        src_ref=src, dst_ref=dst, send_sem=send, recv_sem=recv, device_id=target, device_id_type=MESH
    )


BIG_HALF = BIG_ROWS // 2
SMALL_HALF = SMALL_ROWS // 2
BULK_CUT = 1104
LIGHT_CUT = 256
BACK_CUT = 1424
GATHER_ORDER = (
    "X0", "EY", "EC0", "Z1", "X1", "Y0", "Y1", "EC1", "EC2", "EC3", "L0", "R0", "Z2", "L1", "S0",
    "X2", "L2", "Y2", "Z3", "R1", "X3", "S1", "Y3", "M1", "S2", "M2", "D0", "R2", "D1", "M3", "S3",
    "R3", "D2", "D3",
)
REDUCE_ORDER = (
    "A0", "A1", "A2", "A3", "L0", "C0", "B0", "L1", "L2", "B1", "L3", "C1", "O0", "E0", "LS", "B2",
    "O1", "C2", "LE", "I0", "C3", "T1", "E1", "B3", "I1", "O2", "I2", "T2", "G", "E2", "O3", "T3",
)


def gather_kernel(big, small, ids, all_big, all_small, table, held_big, held_small, k_sem, early, chunk, rising, falling,
                  early_send, early_recv, eu_send, eu_recv, ed_send, ed_recv,
                  z_send, z_recv, x_send, x_recv, y_send, y_recv, dx_send, dx_recv, dy_send, dy_recv,
                  s_send, s_recv, first_send, first_recv, own_sem, id_send, id_recv, lz_send, lz_recv):
    me = Place()
    me.enter()
    x, y, z, core = me.x, me.y, me.z, me.core
    up, down = me.device(z=z + 1), me.device(z=z - 1)
    x_side, y_side, sibling = me.device(x=1 - x), me.device(y=1 - y), me.device(core=1 - core)

    class Stream:
        def __init__(self, n, held, out, cut):
            self.n, self.held, self.out, self.cut, self.rows = n, held, out, cut, out.shape[3]

        def block(self, xo, origin, yo):
            return self.held.at[xo, 2 * origin + yo]

        def move_x(self, origin):
            block = self.block(x, origin, y)
            return remote(block, block, x_send.at[self.n, origin], x_recv.at[self.n, origin], x_side)

        def move_y(self, origin):
            block = self.block(x, origin, y)
            return remote(block, block, y_send.at[self.n, origin], y_recv.at[self.n, origin], y_side)

        def copies(self, xo, origin, yo):
            block, at = self.block(xo, origin, yo), 8 * xo + 2 * origin + yo
            result = self.out.at[xo, 2 * origin + yo, core]
            return (
                remote(block, result, s_send.at[self.n, at], s_recv.at[self.n, at], sibling),
                pltpu.make_async_copy(block, result, k_sem.at[self.n, at]),
            )

        def share(self, xo, origin, yo):
            for copy in self.copies(xo, origin, yo):
                copy.start()

        def move_z(self, origin, target, way):
            block = self.block(x, origin, y)
            return remote(block, block, z_send.at[self.n, way, origin], z_recv.at[self.n, origin], target)

        def half_x(self, origin, xo, yo):
            part = self.held.at[xo, 2 * origin + yo, pl.ds(self.cut, self.rows - self.cut)]
            return remote(part, part, dx_send.at[self.n, origin], dx_recv.at[self.n, origin], x_side)

        def half_y(self, origin, xo, yo):
            part = self.held.at[xo, 2 * origin + yo, pl.ds(0, self.cut)]
            return remote(part, part, dy_send.at[self.n, origin], dy_recv.at[self.n, origin], y_side)

        def to_x(self, origin):
            self.move_x(origin).start()

        def to_y(self, origin):
            self.move_y(origin).start()

        def from_x(self, origin):
            self.move_x(origin).wait_recv()
            self.half_y(origin, 1 - x, y).start()
            self.share(1 - x, origin, y)

        def from_y(self, origin):
            self.move_y(origin).wait_recv()
            self.half_x(origin, x, 1 - y).start()
            self.share(x, origin, 1 - y)

        def from_diagonal(self, origin):
            self.half_x(origin, 1 - x, 1 - y).wait_recv()
            self.half_y(origin, 1 - x, 1 - y).wait_recv()
            self.share(1 - x, origin, 1 - y)

        def each(self, step, action):
            if step == 0:
                action(z)
            else:
                pl.when(z >= step)(lambda: action(z - step))
                pl.when(z + step <= 3)(lambda: action(z + step))

        def begin(self):
            pl.when(z < 3)(lambda: self.move_z(z, up, 0).start())
            pl.when(z > 0)(lambda: self.move_z(z, down, 1).start())
            self.share(x, z, y)

        def from_z(self, k):
            @pl.when(z >= k)
            def _():
                self.move_z(z - k, up, 0).wait_recv()
                pl.when(z < 3)(lambda: self.move_z(z - k, up, 0).start())
                self.share(x, z - k, y)

            @pl.when(z + k <= 3)
            def _():
                self.move_z(z + k, down, 1).wait_recv()
                pl.when(z > 0)(lambda: self.move_z(z + k, down, 1).start())
                self.share(x, z + k, y)

        def close(self):
            for origin in range(4):
                self.move_x(origin).wait_send()
                self.move_y(origin).wait_send()
                self.half_x(origin, x, 1 - y).wait_send()
                self.half_y(origin, 1 - x, y).wait_send()
                pl.when((z < 3) & (origin <= z))(lambda: self.move_z(origin, up, 0).wait_send())
                pl.when((z > 0) & (origin >= z))(lambda: self.move_z(origin, down, 1).wait_send())
            self.close_shares()

        def close_shares(self):
            for origin in range(4):
                for xo in range(2):
                    for yo in range(2):
                        away, home = self.copies(xo, origin, yo)
                        away.wait_send()
                        home.wait()
                        theirs = self.out.at[xo, 2 * origin + yo, 1 - core]
                        at = 8 * xo + 2 * origin + yo
                        remote(theirs, theirs, s_send.at[self.n, at], s_recv.at[self.n, at], sibling).wait_recv()

    class Late(Stream):
        def column_z(self, xo, origin, yo, target, way):
            block = self.block(xo, origin, yo)
            at = 2 * xo + yo
            return remote(
                block, block, lz_send.at[way, at, origin], lz_recv.at[at, origin], target
            )

        def leave(self, xo, yo):
            pl.when(z < 3)(lambda: self.column_z(xo, z, yo, up, 0).start())
            pl.when(z > 0)(lambda: self.column_z(xo, z, yo, down, 1).start())
            self.share(xo, z, yo)

        def step(self, k):
            if k == 0:
                self.move_x(z).start()
                self.move_y(z).start()
                self.leave(x, y)
            elif k == 1:
                self.move_x(z).wait_recv()
                self.half_y(z, 1 - x, y).start()
                self.leave(1 - x, y)
                self.move_y(z).wait_recv()
                self.half_x(z, x, 1 - y).start()
                self.leave(x, 1 - y)
            elif k == 2:
                self.half_x(z, 1 - x, 1 - y).wait_recv()
                self.half_y(z, 1 - x, 1 - y).wait_recv()
                self.leave(1 - x, 1 - y)
            else:
                gap = k - 2

                @pl.when(z >= gap)
                def _():
                    for xo, yo in columns:
                        self.column_z(xo, z - gap, yo, up, 0).wait_recv()
                        pl.when(z < 3)(lambda: self.column_z(xo, z - gap, yo, up, 0).start())
                        self.share(xo, z - gap, yo)

                @pl.when(z + gap <= 3)
                def _():
                    for xo, yo in columns:
                        self.column_z(xo, z + gap, yo, down, 1).wait_recv()
                        pl.when(z > 0)(lambda: self.column_z(xo, z + gap, yo, down, 1).start())
                        self.share(xo, z + gap, yo)

        def close(self):
            self.move_x(z).wait_send()
            self.move_y(z).wait_send()
            self.half_x(z, x, 1 - y).wait_send()
            self.half_y(z, 1 - x, y).wait_send()
            for origin in range(4):
                for xo, yo in columns:
                    pl.when((z < 3) & (origin <= z))(
                        lambda: self.column_z(xo, origin, yo, up, 0).wait_send())
                    pl.when((z > 0) & (origin >= z))(
                        lambda: self.column_z(xo, origin, yo, down, 1).wait_send())
            self.close_shares()

    columns = ((x, y), (1 - x, y), (x, 1 - y), (1 - x, 1 - y))
    bulk = Stream(0, held_big, all_big, BULK_CUT)
    light = Late(1, held_small, all_small, LIGHT_CUT)

    order = [
        jnp.where(z < 2, 3, 0),
        jnp.where(z == 0, 2, jnp.where(z == 1, 0, jnp.where(z == 2, 3, 1))),
        jnp.where(z == 0, 1, jnp.where(z == 1, 2, jnp.where(z == 2, 1, 2))),
        z,
    ]

    def cross(k):
        return remote(small.at[2 * order[k] + (1 - y)], early.at[k], early_send.at[k], early_recv.at[k], y_side)

    def own_early(k):
        return pltpu.make_async_copy(small.at[2 * order[k] + y], chunk.at[k], own_sem.at[3 + k])

    def rise(k):
        slot = order[k] - 1
        return remote(chunk.at[k], rising.at[slot], eu_send.at[slot], eu_recv.at[slot], up)

    def fall(k):
        slot = order[k]
        return remote(chunk.at[k], falling.at[slot], ed_send.at[slot], ed_recv.at[slot], down)

    def merge(k, ref, slot):
        @pl.loop(0, 3)
        def _(i):
            part = pl.ds(pl.multiple_of(352 * i, 16), 352)
            chunk[k, part, :] = (chunk[k, part, :].astype(FULL) + ref[slot, part, :].astype(FULL)).astype(LOW)

    big_half = held_big.at[x, me.dp]
    big_first = remote(big.at[pl.ds(BIG_HALF, BIG_HALF)], big_half, first_send.at[0], first_recv.at[0], sibling)
    small_half = held_small.at[x, me.dp]
    small_first = remote(
        chunk.at[3, pl.ds(0, SMALL_HALF)], small_half, first_send.at[1], first_recv.at[1], sibling)

    def early_cross():
        @pl.when(core == 1)
        def _():
            for k in range(4):
                own_early(k).wait()
                cross(k).wait_recv()
                merge(k, early, k)

    def early_chain(k):
        @pl.when(core == 1)
        def _():
            if k < 3:

                @pl.when(order[k] > z)
                def _():
                    @pl.when(z > 0)
                    def _():
                        rise(k).wait_recv()
                        merge(k, rising, order[k] - 1)

                    rise(k).start()

                @pl.when(order[k] < z)
                def _():
                    @pl.when(z < 3)
                    def _():
                        fall(k).wait_recv()
                        merge(k, falling, order[k])

                    fall(k).start()

            else:

                @pl.when(z > 0)
                def _():
                    rise(k).wait_recv()
                    merge(k, rising, z - 1)

                @pl.when(z < 3)
                def _():
                    fall(k).wait_recv()
                    merge(k, falling, z)

                small_first.start()
                copy = pltpu.make_async_copy(
                    chunk.at[3, pl.ds(SMALL_HALF, SMALL_HALF)], small_half, own_sem.at[0])
                copy.start()
                copy.wait()

    def light_begin():
        @pl.when(core == 0)
        def _():
            small_first.wait_recv()

        light.step(0)

    @pl.when(core == 0)
    def _():
        big_first.start()
        copy = pltpu.make_async_copy(big.at[pl.ds(0, BIG_HALF)], big_half, own_sem.at[0])
        copy.start()
        copy.wait()

    @pl.when(core == 1)
    def _():
        for k in range(4):
            cross(k).start()
            own_early(k).start()
        big_first.wait_recv()

    bulk.begin()
    row = pltpu.make_async_copy(ids, table.at[me.pipe], own_sem.at[2])
    row.start()
    for step in range(1, 4):
        remote(
            ids, table.at[me.pipe], id_send.at[step], id_recv.at[step],
            {"dp": me.dp, "pipe": lax.rem(me.pipe + step, 4)},
        ).start()

    actions = {"EY": early_cross, "L0": light_begin}
    for k in range(4):
        actions["EC%d" % k] = functools.partial(early_chain, k)
        actions["X%d" % k] = functools.partial(bulk.each, k, bulk.to_x)
        actions["Y%d" % k] = functools.partial(bulk.each, k, bulk.to_y)
        actions["S%d" % k] = functools.partial(bulk.each, k, bulk.from_x)
        actions["R%d" % k] = functools.partial(bulk.each, k, bulk.from_y)
        actions["D%d" % k] = functools.partial(bulk.each, k, bulk.from_diagonal)
        if k:
            actions["Z%d" % k] = functools.partial(bulk.from_z, k)
            actions["M%d" % k] = functools.partial(light.step, k + 2)
            if k < 3:
                actions["L%d" % k] = functools.partial(light.step, k)
    for event in GATHER_ORDER:
        actions[event]()
    bulk.close()
    light.close()
    row.wait()
    for step in range(1, 4):
        here = lax.rem(me.pipe + 4 - step, 4)
        move = remote(
            ids, table.at[here], id_send.at[step], id_recv.at[step],
            {"dp": me.dp, "pipe": lax.rem(me.pipe + step, 4)},
        )
        move.wait_recv()
        move.wait_send()

    @pl.when(core == 0)
    def _():
        big_first.wait_send()

    @pl.when(core == 1)
    def _():
        small_first.wait_send()
        for k in range(4):
            cross(k).wait_send()
        for k in range(3):
            pl.when(order[k] > z)(lambda: rise(k).wait_send())
            pl.when(order[k] < z)(lambda: fall(k).wait_send())


def gather_all(big, small, ids):
    sem = pltpu.SemaphoreType.DMA
    return pl.pallas_call(
        gather_kernel,
        name="gather_all",
        out_shape=(
            jax.ShapeDtypeStruct((2, 8, 2, BIG_HALF, 128), LOW),
            jax.ShapeDtypeStruct((2, 8, 2, SMALL_HALF, 128), LOW),
            jax.ShapeDtypeStruct((4, 8, 128), jnp.int32),
        ),
        in_specs=[any_spec()] * 3,
        out_specs=(any_spec(),) * 3,
        scratch_shapes=[
            pltpu.VMEM((2, 8, BIG_HALF, 128), LOW), pltpu.VMEM((2, 8, SMALL_HALF, 128), LOW), sem((2, 16)),
            pltpu.VMEM((4, SMALL_ROWS, 128), LOW), pltpu.VMEM((4, SMALL_ROWS, 128), LOW),
            pltpu.VMEM((3, SMALL_ROWS, 128), LOW), pltpu.VMEM((3, SMALL_ROWS, 128), LOW),
            sem((4,)), sem((4,)), sem((3,)), sem((3,)), sem((3,)), sem((3,)),
            sem((2, 2, 4)), sem((2, 4)),
            sem((2, 4)), sem((2, 4)), sem((2, 4)), sem((2, 4)),
            sem((2, 4)), sem((2, 4)), sem((2, 4)), sem((2, 4)),
            sem((2, 16)), sem((2, 16)),
            sem((2,)), sem((2,)), sem((7,)), sem((4,)), sem((4,)), sem((2, 4, 4)), sem((4, 4)),
        ],
        compiler_params=pltpu.CompilerParams(
            collective_id=0, has_side_effects=True, vmem_limit_bytes=60 << 20
        ),
    )(big, small.reshape(8, SMALL_ROWS, 128), ids)


def soft(value):
    return jnp.maximum(value, 0.0) + jnp.log1p(jnp.exp(-jnp.abs(value)))


def gate_of(value):
    small = jnp.exp(-jnp.abs(value))
    share = 1.0 / (1.0 + small)
    return jnp.where(value >= 0, share, small * share)


def standardize(z):
    count = z.shape[0]
    centre = jnp.sum(z, axis=0, keepdims=True) / count
    away = z - centre
    spread = jnp.sum(away * away, axis=0, keepdims=True) / count
    inverse = lax.rsqrt(spread + NORM_EPS)
    return away * inverse, centre, spread, inverse


def unstandardize(grad, standard, gain, inverse):
    count = grad.shape[0]
    grad_sum = jnp.sum(grad, axis=0, keepdims=True)
    grad_dot = jnp.sum(grad * standard, axis=0, keepdims=True)
    result = gain * inverse * (grad - grad_sum / count - standard * (grad_dot / count))
    return result, grad_dot, grad_sum


def pad_low(value):
    zeros = jnp.zeros((PADDED - ROWS, value.shape[1]), FULL)
    return jnp.concatenate([value, zeros], axis=0).astype(LOW)


def mul(a, b):
    return jnp.dot(a, b, preferred_element_type=FULL)


def mul_t(a, b):
    return lax.dot_general(a, b, (((1,), (1,)), ((), ())), preferred_element_type=FULL)


def narrow_part(ref, start, count, blocks=range(4)):
    return jnp.concatenate(
        [ref[pl.ds(start, count), 64 * j : 64 * j + 64, :].reshape(64 * count, 128) for j in blocks],
        axis=1,
    )


def put_narrow(ref, start, count, value):
    for j in range(4):
        ref[pl.ds(start, count), 64 * j : 64 * j + 64, :] = (
            value[:, 128 * j : 128 * j + 128].astype(LOW).reshape(count, 64, 128)
        )


def wide_part(ref, start, count, c):
    return jnp.concatenate(
        [
            ref[start : start + count, 32 * c + 16 * h : 32 * c + 16 * h + 16, :].reshape(
                16 * count, 128
            )
            for h in range(2)
        ],
        axis=1,
    )


def put_wide(ref, start, count, c, value):
    for h in range(2):
        ref[start : start + count, 32 * c + 16 * h : 32 * c + 16 * h + 16, :] = (
            value[:, 128 * h : 128 * h + 128].astype(LOW).reshape(count, 16, 128)
        )


def chunks(count):
    def run(body):
        for c in range(count):
            body(c)

    return run


def step_kernel(table, gates, teach_ids, stud_ids, all_big, all_small, x, targets, grid,
                wide0, wide1, final, stats, grad_x, out_big, out_small,
                w0, w1, w2, w3, edges, loose, vec, grad_vec, raw,
                std_a, std_b, std_p, std_1, std_c, std_d, hidden, cols0, cols2,
                nar0, nar2, turned, relay, dz_a, dz_n, acc, acc_x, grad_h,
                wanted, inv, in_sem, edge_sem, out_sem):
    rank = lax.axis_index("pipe")
    gate = gates[rank].astype(FULL)
    for group in range(2):
        for j in range(8):
            inv[8 * group + table[2 * group, 0, j]] = j
    picks = [teach_ids[k, rank] for k in range(2)] + [stud_ids[rank, k] for k in range(3)]
    rows = [
        pltpu.make_async_copy(targets.at[pl.ds(pick, 1)], wanted.at[pl.ds(k, 1)], edge_sem.at[12 + k])
        for k, pick in enumerate(picks)
    ]
    for fetched in rows:
        fetched.start()
    weights = (w0, w1, w2, w3)
    loads = {0: [], 1: [], 2: [], 3: []}
    front, split = w0.reshape(USED_TILES[0] * TILE, 128), w2.reshape(115 * TILE, 128)
    for group, weight, blocks in ((0, front, 8), (1, split, 6)):
        for b in range(blocks):
            at, here = 8 * group + b, inv[8 * group + b]
            count = min(STRIDE, VEC_TILE[2 * group] + 1 - STRIDE * b) * TILE
            loads[2 * group].append(pltpu.make_async_copy(
                all_big.at[group, here, pl.ds(0, count)], weight.at[pl.ds(STRIDE * TILE * b, count)],
                in_sem.at[0, at]))
            if b < blocks - 1:
                loads[2 * group].append(pltpu.make_async_copy(
                    all_big.at[group, here, pl.ds(STRIDE * TILE, EDGE)], edges.at[7 * group + b],
                    edge_sem.at[7 * group + b]))
            elif group == 0:
                loads[0].append(pltpu.make_async_copy(
                    all_big.at[0, here, pl.ds(STRIDE * TILE, EDGE)],
                    front.at[pl.ds(VEC_TILE[0] * TILE, EDGE)], edge_sem.at[17]))
    loads[1].append(pltpu.make_async_copy(all_small.at[0], w1, in_sem.at[0, 14]))
    loads[3].append(pltpu.make_async_copy(all_small.at[1], w3, in_sem.at[0, 15]))
    for section in range(4):
        for load in loads[section]:
            load.start()

    raw[...] = jnp.zeros_like(raw)
    loose[...] = jnp.zeros_like(loose)
    grad_vec[...] = jnp.zeros_like(grad_vec)

    def edge_parts(tile, is_narrow):
        count, size = (4, 64) if is_narrow else (16, 16)
        for j in range(count):
            yield pl.ds(j, 16, count), slice(size * j, size * j + 16)

    def is_narrow(section, tile):
        return section == 2 or tile < FRONT_WIDE

    def merge_edge(section, tile, at):
        ref = weights[section]
        loose[0:EDGE, :] = edges[at].astype(FULL)
        for lying, here in edge_parts(tile, is_narrow(section, tile)):
            ref[tile, here, :] = (ref[tile, here, :].astype(FULL) + loose[lying, :]).astype(LOW)

    def take_edge(section, tile, at):
        ref = weights[section]
        for lying, here in edge_parts(tile, is_narrow(section, tile)):
            loose[lying, :] = ref[tile, here, :].astype(FULL)
        edges[at] = loose[0:EDGE, :].astype(LOW)

    def settle(section, blocks=None):
        if section == 0:
            for b in blocks:
                for load in loads[0][2 * b : 2 * b + 2]:
                    load.wait()
            if 7 in blocks:
                vec[0] = w0[VEC_TILE[0], 0:48, :].astype(FULL)
            else:
                for b in range(7):
                    merge_edge(0, 19 * b + 19, b)
            return
        for load in loads[section]:
            load.wait()
        if section == 2:
            for b in range(5):
                merge_edge(2, 19 * b + 19, 7 + b)
        vec[section] = weights[section][VEC_TILE[section], 0:48, :].astype(FULL)

    def row(section, start):
        return jnp.concatenate(
            [vec[section, pl.ds(start + h, 1), :] for h in range(2)], axis=1
        )

    def put_row(section, start, value):
        for h in range(2):
            grad_vec[section, pl.ds(start + h, 1), :] = value[:, 128 * h : 128 * h + 128]

    def put_stats(section, column, centre, spread):
        raw[2 * section : 2 * section + 1, pl.ds(column, 256)] = centre
        raw[2 * section + 1 : 2 * section + 2, pl.ds(column, 256)] = spread

    def inverse_of(section, column):
        return lax.rsqrt(raw[2 * section + 1 : 2 * section + 2, pl.ds(column, 256)] + NORM_EPS)

    def lanes(c):
        return slice(256 * c, 256 * c + 256)

    at_row, at_col, side = grid[0], grid[1], grid[2]

    def masked(value, dr, dc):
        ok = (at_row + dr >= 0) & (at_row + dr < side) & (at_col + dc >= 0) & (at_col + dc < side)
        return jnp.concatenate(
            [jnp.where(ok, value[:, 128 * j : 128 * j + 128], 0.0) for j in range(4)], axis=1
        )

    def rolled(value, sign, dr, dc):
        parts = []
        for start, end, across, down in ((0, STUD_ROWS, 1, 4), (STUD_ROWS, ROWS, 2, 12)):
            by = (sign * (dr * down + dc * across)) % (end - start)
            part = value[start:end]
            parts.append(part if by == 0 else pltpu.roll(part, by, 0))
        return jnp.concatenate(parts, axis=0)

    def taps(stride):
        for t in range(9):
            r, q = t // 3, t % 3
            if stride == 1:
                yield t, 0, r - 1, q - 1
            else:
                phase = 2 * (1 if r != 1 else 0) + (1 if q != 1 else 0)
                yield t, phase, -1 if r == 0 else 0, -1 if q == 0 else 0

    settle(0, (0, 7))
    whole_x = x[...].reshape(4 * PADDED, C_IN)
    for c in range(2):
        z = mul(whole_x, narrow_part(w0, 0, 16, (2 * c, 2 * c + 1)))
        z = jnp.concatenate([z[PADDED * p : PADDED * p + ROWS] for p in range(4)], axis=0)
        standard, centre, spread, _ = standardize(z)
        put_stats(0, 256 * c, centre, spread)
        std_a[:, 256 * c : 256 * c + 256] = standard
        hidden[:, 256 * c : 256 * c + 256] = (
            soft(row(0, 2 * c) * standard + row(0, 4 + 2 * c)).astype(LOW).astype(FULL)
        )

    for t, phase, dr, dc in taps(2):
        cols0[t] = pad_low(masked(rolled(hidden[ROWS * phase : ROWS * phase + ROWS, :], -1, dr, dc), dr, dc))
    acc[...] = jnp.zeros_like(acc)
    settle(0, (1, 2, 3, 4, 5, 6))

    @chunks(9)
    def _(t):
        acc[...] += mul(cols0[t], narrow_part(w0, 16 + 8 * t, 8))

    def middle(section, std, nar):
        for c in range(2):
            at = slice(256 * c, 256 * c + 256)
            standard, centre, spread, _ = standardize(acc[0:ROWS, at])
            put_stats(section, MID + 256 * c, centre, spread)
            std[:, at] = standard
            nar[:, at] = pad_low(soft(row(section, 8 + 2 * c) * standard + row(section, 12 + 2 * c)))

    middle(0, std_b, nar0)
    acc[...] = jnp.zeros_like(acc)
    settle(1)
    settle(2)

    @chunks(8)
    def _(c):
        at = lanes(c)
        standard, centre, spread, _ = standardize(mul(x[0], wide_part(w0, FRONT_WIDE, 64, c))[0:ROWS])
        put_stats(0, 2 * MID + 256 * c, centre, spread)
        std_p[:, at] = standard
        low = pad_low(row(0, 16 + 2 * c) * standard + row(0, 32 + 2 * c))
        wide0[:, at] = low
        standard, centre, spread, _ = standardize(mul(nar0[...], wide_part(w1, 0, 32, c))[0:ROWS])
        put_stats(1, 256 * c, centre, spread)
        std_1[:, at] = standard
        pre = low.astype(FULL)[0:ROWS] + row(1, 2 * c) * standard + row(1, 16 + 2 * c)
        low = pad_low(soft(pre))
        wide1[:, at] = low
        acc[...] += mul(low, narrow_part(w2, 4 * c, 4))

    for c in range(2):
        at = slice(256 * c, 256 * c + 256)
        standard, centre, spread, _ = standardize(acc[0:ROWS, at])
        put_stats(2, 256 * c, centre, spread)
        std_c[:, at] = standard
        hidden[0:ROWS, at] = soft(row(2, 2 * c) * standard + row(2, 4 + 2 * c)).astype(LOW).astype(FULL)
    for t, phase, dr, dc in taps(1):
        cols2[t] = pad_low(masked(rolled(hidden[0:ROWS, :], -1, dr, dc), dr, dc))
    acc[...] = jnp.zeros_like(acc)

    @chunks(9)
    def _(t):
        acc[...] += mul(cols2[t], narrow_part(w2, 32 + 8 * t, 8))

    middle(2, std_d, nar2)

    turned[...] = nar2[...].T
    acc[...] = jnp.zeros_like(acc)
    settle(3)
    for fetched in rows:
        fetched.wait()

    teach_rows = ROWS - STUD_ROWS
    first_crop = lax.rem(lax.broadcasted_iota(jnp.int32, (teach_rows, 256), 0), 2) == 0

    def spread_rows(values):
        first, second = (jnp.broadcast_to(value, (teach_rows, 256)) for value in values[0:2])
        parts = [jnp.broadcast_to(value, (16, 256)) for value in values[2:5]]
        parts.append(jnp.where(first_crop, first, second))
        return jnp.concatenate(parts, axis=0)

    def crop_sums(value):
        def total(part):
            return jnp.sum(part, axis=0, keepdims=True)

        teach = value[STUD_ROWS:ROWS]
        return [
            total(jnp.where(first_crop, teach, 0.0)),
            total(jnp.where(first_crop, 0.0, teach)),
            total(value[0:16]),
            total(value[16:32]),
            total(value[32:48]),
        ]

    @chunks(8)
    def _(c):
        at = lanes(c)
        weight = wide_part(w3, 0, 32, c)
        standard, centre, spread, inverse = standardize(mul(nar2[...], weight)[0:ROWS])
        put_stats(3, 256 * c, centre, spread)
        gain = row(3, 2 * c)
        before = wide1[:, at].astype(FULL)[0:ROWS]
        pre = before + gain * standard + row(3, 16 + 2 * c)
        ending = jnp.where(gate > 0, soft(pre), before)
        final[:, at] = pad_low(ending)
        square = ending * ending
        factors = []
        for crop, total in enumerate(crop_sums(square * ending)):
            mean = total / (36.0 if crop < 2 else 16.0) + POOL_EPS
            factors.append(jnp.exp(jnp.log(mean) * (-2.0 / 3.0)) * wanted[crop : crop + 1, at])
        cotangent = spread_rows(factors) * square
        grad_pre = cotangent * gate_of(pre) * gate
        relay[:, at] = pad_low(grad_pre + cotangent * (1.0 - gate))
        result, grad_gain, grad_bias = unstandardize(grad_pre, standard, gain, inverse)
        put_row(3, 2 * c, grad_gain)
        put_row(3, 16 + 2 * c, grad_bias)
        low = pad_low(result)
        acc[...] += mul_t(low, weight)
        put_wide(w3, 0, 32, c, mul(turned[...], low))

    def flush(section):
        weights[section][VEC_TILE[section]] = grad_vec[section].astype(LOW)

    flush(3)
    stores = [pltpu.make_async_copy(w3, out_small.at[1], out_sem.at[16])]
    stores[-1].start()

    def middle_back(section, std):
        for c in range(2):
            at = slice(256 * c, 256 * c + 256)
            gain, bias = row(section, 8 + 2 * c), row(section, 12 + 2 * c)
            grad = acc[0:ROWS, at].astype(LOW).astype(FULL) * gate_of(gain * std[:, at] + bias)
            result, grad_gain, grad_bias = unstandardize(
                grad, std[:, at], gain, inverse_of(section, MID + 256 * c)
            )
            put_row(section, 8 + 2 * c, grad_gain)
            put_row(section, 12 + 2 * c, grad_bias)
            dz_n[:, at] = pad_low(result)

    def taps_back(weight, start, cols, stride, phases):
        grad_h[0 : ROWS * phases, :] = jnp.zeros((ROWS * phases, MID), FULL)
        for t, phase, dr, dc in taps(stride):
            part = mul_t(dz_n[...], narrow_part(weight, start + 8 * t, 8))[0:ROWS]
            at = slice(ROWS * phase, ROWS * phase + ROWS)
            grad_h[at, :] += rolled(masked(part, dr, dc), 1, dr, dc)
            put_narrow(weight, start + 8 * t, 8, mul(cols[t].T, dz_n[...]))

    middle_back(2, std_d)
    taps_back(w2, 32, cols2, 1, 1)
    for c in range(2):
        at = slice(256 * c, 256 * c + 256)
        gain, bias = row(2, 2 * c), row(2, 4 + 2 * c)
        grad = grad_h[0:ROWS, at] * gate_of(gain * std_c[:, at] + bias)
        result, grad_gain, grad_bias = unstandardize(grad, std_c[:, at], gain, inverse_of(2, 256 * c))
        put_row(2, 2 * c, grad_gain)
        put_row(2, 4 + 2 * c, grad_bias)
        dz_n[:, at] = pad_low(result)
    turned[...] = nar0[...].T
    acc[...] = jnp.zeros_like(acc)
    acc_x[...] = jnp.zeros_like(acc_x)

    @chunks(8)
    def _(c):
        at = lanes(c)
        low = dz_n[...]
        grad = relay[:, at].astype(FULL) + mul_t(low, narrow_part(w2, 4 * c, 4))
        put_narrow(w2, 4 * c, 4, mul(wide1[:, at].T, low))
        grad = grad.astype(LOW).astype(FULL)[0:ROWS]
        gain = row(1, 2 * c)
        pre = wide0[:, at].astype(FULL)[0:ROWS] + gain * std_1[:, at] + row(1, 16 + 2 * c)
        grad = grad * gate_of(pre)
        result, grad_gain, grad_bias = unstandardize(
            grad, std_1[:, at], gain, inverse_of(1, 256 * c)
        )
        put_row(1, 2 * c, grad_gain)
        put_row(1, 16 + 2 * c, grad_bias)
        low = pad_low(result)
        acc[...] += mul_t(low, wide_part(w1, 0, 32, c))
        put_wide(w1, 0, 32, c, mul(turned[...], low))
        grad = grad.astype(LOW).astype(FULL)
        result, grad_gain, grad_bias = unstandardize(
            grad, std_p[:, at], row(0, 16 + 2 * c), inverse_of(0, 2 * MID + 256 * c)
        )
        put_row(0, 16 + 2 * c, grad_gain)
        put_row(0, 32 + 2 * c, grad_bias)
        low = pad_low(result)
        acc_x[...] += mul_t(low, wide_part(w0, FRONT_WIDE, 64, c))
        put_wide(w0, FRONT_WIDE, 64, c, mul(x[0].T, low))

    flush(1)
    flush(2)
    w2[105:115] = jnp.zeros((10, TILE, 128), LOW)
    stores.append(pltpu.make_async_copy(w1, out_small.at[0], out_sem.at[17]))
    stores[-1].start()
    def store(source, group, b, start, semaphore):
        count = source.shape[0]
        stores.append(pltpu.make_async_copy(
            source, out_big.at[group, inv[8 * group + b], pl.ds(start, count)], out_sem.at[semaphore]))
        stores[-1].start()

    for b in range(8):
        if b < 5:
            take_edge(2, 19 * b + 19, 7 + b)
            store(split.at[pl.ds(STRIDE * TILE * b, STRIDE * TILE)], 1, b, 0, 8 + b)
            store(edges.at[7 + b], 1, b, STRIDE * TILE, 20 + b)
        else:
            first = 95 if b == 5 else 105
            store(split.at[pl.ds(TILE * first, 10 * TILE)], 1, b, 0, 8 + b)
            store(split.at[pl.ds(TILE * 105, BIG_ROWS - 10 * TILE)], 1, b, 10 * TILE, 20 + b)

    def store_front(blocks):
        for b in blocks:
            if b == 7:
                edges[12] = w0[VEC_TILE[0], 0:EDGE, :]
            else:
                take_edge(0, 19 * b + 19, b)
            store(front.at[pl.ds(STRIDE * TILE * b, STRIDE * TILE)], 0, b, 0, b)
            store(edges.at[12 if b == 7 else b], 0, b, STRIDE * TILE, 28 + b)

    store_front((5, 6))
    middle_back(0, std_b)
    taps_back(w0, 16, cols0, 2, 4)
    store_front((1, 2, 3, 4))
    for c in range(2):
        at = slice(256 * c, 256 * c + 256)
        gain, bias = row(0, 2 * c), row(0, 4 + 2 * c)
        grad = grad_h[:, at] * gate_of(gain * std_a[:, at] + bias)
        result, grad_gain, grad_bias = unstandardize(grad, std_a[:, at], gain, inverse_of(0, 256 * c))
        put_row(0, 2 * c, grad_gain)
        put_row(0, 4 + 2 * c, grad_bias)
        for p in range(4):
            dz_a[PADDED * p : PADDED * p + PADDED, at] = pad_low(result[ROWS * p : ROWS * p + ROWS])

    @chunks(4)
    def _(c):
        at = lanes(c)
        low = dz_a[...]
        part = mul_t(low, narrow_part(w0, 4 * c, 4))
        grad_x[0, :, at] = (part[0:PADDED] + acc_x[:, at]).astype(LOW)
        for p in range(1, 4):
            grad_x[p, :, at] = part[PADDED * p : PADDED * p + PADDED].astype(LOW)
        turned_x = x[:, :, at].reshape(4 * PADDED, 256).T
        put_narrow(w0, 4 * c, 4, mul(turned_x, low))

    flush(0)
    store_front((0, 7))
    for section in range(4):
        part = raw[2 * section : 2 * section + 2]
        stats[section, 0:2] = part if section < 2 else part * gate
        stats[section, 2:8] = jnp.zeros((6, 2 * MID + C_OUT), FULL)
    for store in stores:
        store.wait()


def run_step(table, gates, teach_ids, stud_ids, all_big, all_small, phases, targets):
    spots = np.zeros((3, ROWS, 128), np.int32)
    for r in range(ROWS):
        width = 4 if r < STUD_ROWS else 6
        at = r % 16 if r < STUD_ROWS else (r - STUD_ROWS) // 2
        spots[0, r], spots[1, r], spots[2, r] = at // width, at % width, width
    sem = pltpu.SemaphoreType.DMA
    wide = jax.ShapeDtypeStruct((PADDED, C_OUT), LOW)
    vm = pltpu.VMEM
    return pl.pallas_call(
        step_kernel,
        name="step",
        out_shape=(
            wide, wide, wide,
            jax.ShapeDtypeStruct((4, 8, 2 * MID + C_OUT), FULL),
            jax.ShapeDtypeStruct((4, PADDED, C_IN), LOW),
            jax.ShapeDtypeStruct((2, 8, BIG_ROWS, 128), LOW),
            jax.ShapeDtypeStruct((2, USED_TILES[1], TILE, 128), LOW),
        ),
        in_specs=[smem_spec()] * 4 + [any_spec(), any_spec(), vmem_spec(), any_spec(), vmem_spec()],
        out_specs=(vmem_spec(),) * 5 + (any_spec(),) * 2,
        scratch_shapes=[
            vm((153, TILE, 128), LOW), vm((33, TILE, 128), LOW), vm((115, TILE, 128), LOW), vm((33, TILE, 128), LOW),
            vm((13, EDGE, 128), LOW), vm((TILE, 128), FULL), vm((4, 48, 128), FULL), vm((4, TILE, 128), FULL),
            vm((8, 2 * MID + C_OUT), FULL),
            vm((4 * ROWS, MID), FULL), vm((ROWS, MID), FULL), vm((ROWS, C_OUT), FULL), vm((ROWS, C_OUT), FULL),
            vm((ROWS, MID), FULL), vm((ROWS, MID), FULL), vm((4 * ROWS, MID), FULL),
            vm((9, PADDED, MID), LOW), vm((9, PADDED, MID), LOW),
            vm((PADDED, MID), LOW), vm((PADDED, MID), LOW), vm((MID, PADDED), LOW),
            vm((PADDED, C_OUT), LOW), vm((4 * PADDED, MID), LOW), vm((PADDED, MID), LOW),
            vm((PADDED, MID), FULL), vm((PADDED, C_IN), FULL), vm((4 * ROWS, MID), FULL),
            vm((8, C_OUT), FULL), pltpu.SMEM((16,), jnp.int32),
            sem((2, 16)), sem((18,)), sem((36,)),
        ],
        compiler_params=pltpu.CompilerParams(vmem_limit_bytes=60 << 20),
    )(table, gates, teach_ids, stud_ids, all_big, all_small, phases, targets, jnp.asarray(spots))


def reduce_kernel(big, small, wide0, wide1, final, stats, table,
                  out_big, out_small, seg_stud, seg_teach, out_stats, norm, factor,
                  got, halves_x, halves_y, from_x, from_y, from_low, from_high, stage, total,
                  l_got, l_stage, l_low, l_high, l_halves_x, l_halves_y, l_from_x, l_from_y, l_total,
                  late, late_half, owner_row, by_pipe, by_dp, mine, part_sum,
                  s_send, s_recv, hx_send, hx_recv, hy_send, hy_recv, x_send, x_recv, y_send, y_recv,
                  zu_send, zu_recv, zd_send, zd_recv, lu_send, lu_recv, ld_send, ld_recv,
                  stage_sem, l_stage_sem, out_sem, late_send, late_recv, join_send, join_recv,
                  seg_send, seg_recv, stat_send, stat_recv, p_send, p_recv, d_send, d_recv):
    me = Place()
    me.enter()
    x, y, z, core = me.x, me.y, me.z, me.core
    up, down = me.device(z=z + 1), me.device(z=z - 1)
    x_side, y_side, sibling = me.device(x=1 - x), me.device(y=1 - y), me.device(core=1 - core)
    order = [
        jnp.where(z < 2, 3, 0),
        jnp.where(z == 0, 2, jnp.where(z == 1, 0, jnp.where(z == 2, 3, 1))),
        jnp.where(z == 0, 1, jnp.where(z == 1, 2, jnp.where(z == 2, 1, 2))),
        z,
    ]
    columns = ((1 - x, 1 - y), (x, 1 - y), (1 - x, y), (x, y))
    groups = {"A": (0,), "C": (1,), "B": (2,), "O": (3,)}
    sequence = [
        (group, int(event[1])) for event in REDUCE_ORDER for group in groups.get(event[0], ())
    ]
    l_sequence = [(group, k) for k in range(4) for group in range(4)]

    def all_of(copies, act):
        for copy in copies:
            act(copy)

    def over(start, count, piece):
        whole = count // 512
        if whole:

            @pl.loop(0, whole)
            def _(i):
                piece(pl.multiple_of(start + 512 * i, 16), 512)

        if count % 512:
            piece(start + 512 * whole, count % 512)

    def source(array, group, k, half):
        xo, yo = columns[group]
        return array.at[xo, 2 * order[k] + yo, half]

    def share(group, k):
        at = 4 * group + k
        return remote(source(big, group, k, 1 - core), got.at[at], s_send.at[0, at], s_recv.at[0, at], sibling)

    def l_share(group, k):
        at = 4 * group + k
        return remote(source(small, group, k, 1 - core), l_got.at[at], s_send.at[1, at], s_recv.at[1, at], sibling)

    def fetch(n):
        return pltpu.make_async_copy(source(big, *sequence[n], core), stage.at[n % 4], stage_sem.at[n % 4])

    def l_fetch(group, k):
        at = 4 * group + k
        return pltpu.make_async_copy(source(small, group, k, core), l_stage.at[at], l_stage_sem.at[at])

    def add(target, at, other, slot, start, count, extras):
        def piece(begin, size):
            part = pl.ds(begin, size)
            sums = target[at, part, :].astype(FULL) + other[slot, part, :].astype(FULL)
            for ref, k in extras:
                sums = sums + ref[k, pl.ds(begin - start, size), :].astype(FULL)
            target[at, part, :] = sums.astype(LOW)

        over(start, count, piece)

    def send_half_x(k):
        return remote(got.at[k, pl.ds(BACK_CUT, BIG_HALF - BACK_CUT)], halves_x.at[k],
                      hx_send.at[k], hx_recv.at[k], x_side)

    def send_half_y(k):
        return remote(got.at[k, pl.ds(0, BACK_CUT)], halves_y.at[k], hy_send.at[k], hy_recv.at[k], y_side)

    def send_y(k):
        return remote(got.at[4 + k], from_y.at[k], y_send.at[k], y_recv.at[k], y_side)

    def send_x(k):
        return remote(got.at[8 + k], from_x.at[k], x_send.at[k], x_recv.at[k], x_side)

    def send_up(at, zd):
        return remote(got.at[at], from_low.at[zd - 1], zu_send.at[zd - 1], zu_recv.at[zd - 1], up)

    def send_down(at, zd):
        return remote(got.at[at], from_high.at[zd], zd_send.at[zd], zd_recv.at[zd], down)

    def l_column(group):
        xo, yo = columns[group]
        return 2 * xo + yo

    def l_up(group, k):
        at, zd = l_column(group), order[k] - 1
        return remote(l_got.at[4 * group + k], l_low.at[at, zd], lu_send.at[at, zd], lu_recv.at[at, zd], up)

    def l_down(group, k):
        at, zd = l_column(group), order[k]
        return remote(l_got.at[4 * group + k], l_high.at[at, zd], ld_send.at[at, zd], ld_recv.at[at, zd], down)

    def l_half_x():
        return remote(l_got.at[3, pl.ds(LIGHT_CUT, SMALL_HALF - LIGHT_CUT)], l_halves_x,
                      hx_send.at[4], hx_recv.at[4], x_side)

    def l_half_y():
        return remote(l_got.at[3, pl.ds(0, LIGHT_CUT)], l_halves_y, hy_send.at[4], hy_recv.at[4], y_side)

    def l_send_y():
        return remote(l_got.at[7], l_from_y, y_send.at[4], y_recv.at[4], y_side)

    def l_send_x():
        return remote(l_got.at[11], l_from_x, x_send.at[4], x_recv.at[4], x_side)

    leaving = (wide0, wide1, wide1, final)

    def pairs(section, micro):
        source = leaving[section]
        yield source.at[pl.ds(0, STUD_ROWS)], seg_stud.at[micro], seg_send.at[0, section], seg_recv.at[0, micro]
        yield source.at[pl.ds(STUD_ROWS, TEACH_END)], seg_teach.at[micro], seg_send.at[1, section], seg_recv.at[1, micro]
        yield stats.at[section], out_stats.at[micro], stat_send.at[section], stat_recv.at[micro]

    def exchange(section):
        return [remote(*pair, {"dp": me.dp, "pipe": section}) for pair in pairs(section, me.pipe)]

    def keep(section):
        return [pltpu.make_async_copy(src, dst, send) for src, dst, send, _ in pairs(section, me.pipe)]

    def arriving(micro):
        return [remote(*pair, {"dp": me.dp, "pipe": micro}) for pair in pairs(micro, micro)]

    for n in range(16):
        share(*sequence[n]).start()
        if n == 3:
            for item in l_sequence:
                l_share(*item).start()
    for n in range(2):
        fetch(n).start()
    for group, k in l_sequence:
        l_fetch(group, k).start()
    row_copy = pltpu.make_async_copy(table.at[2 * x], owner_row, out_sem.at[2])
    row_copy.start()

    def bulk_item(n):
        group, k = sequence[n]
        at, slot = 4 * group + k, n % 4
        if n + 2 < 16:
            fetch(n + 2).start()
        fetch(n).wait()
        share(group, k).wait_recv()
        if group == 0:
            add(got, at, stage, slot, 0, BIG_HALF, [])
            send_half_x(k).start()
            send_half_y(k).start()
        elif group == 1:
            send_half_x(k).wait_recv()
            add(got, at, stage, slot, 0, BACK_CUT, [])
            add(got, at, stage, slot, BACK_CUT, BIG_HALF - BACK_CUT, [(halves_x, k)])
            send_y(k).start()
        elif group == 2:
            send_half_y(k).wait_recv()
            add(got, at, stage, slot, 0, BACK_CUT, [(halves_y, k)])
            add(got, at, stage, slot, BACK_CUT, BIG_HALF - BACK_CUT, [])
            send_x(k).start()
        else:
            send_x(k).wait_recv()
            send_y(k).wait_recv()
            add(got, at, stage, slot, 0, BIG_HALF, [(from_x, k), (from_y, k)])

    def bulk_z(k):
        at, zd = 12 + k, order[k]

        @pl.when(zd > z)
        def _():
            @pl.when(z > 0)
            def _():
                send_up(at, zd).wait_recv()
                add(got, at, from_low, zd - 1, 0, BIG_HALF, [])

            send_up(at, zd).start()

        @pl.when(zd < z)
        def _():
            @pl.when(z < 3)
            def _():
                send_down(at, zd).wait_recv()
                add(got, at, from_high, zd, 0, BIG_HALF, [])

            send_down(at, zd).start()

    def light_item(group, k):
        at, zd, column = 4 * group + k, order[k], l_column(group)
        l_fetch(group, k).wait()
        l_share(group, k).wait_recv()
        add(l_got, at, l_stage, at, 0, SMALL_HALF, [])

        def merge(ref, slot):
            l_got[at] = (l_got[at].astype(FULL) + ref[column, slot].astype(FULL)).astype(LOW)

        if k < 3:

            @pl.when(zd > z)
            def _():
                @pl.when(z > 0)
                def _():
                    l_up(group, k).wait_recv()
                    merge(l_low, zd - 1)

                l_up(group, k).start()

            @pl.when(zd < z)
            def _():
                @pl.when(z < 3)
                def _():
                    l_down(group, k).wait_recv()
                    merge(l_high, zd)

                l_down(group, k).start()

        else:

            @pl.when(z > 0)
            def _():
                l_up(group, k).wait_recv()
                merge(l_low, zd - 1)

            @pl.when(z < 3)
            def _():
                l_down(group, k).wait_recv()
                merge(l_high, zd)

            if group == 0:
                l_half_x().start()
                l_half_y().start()

    def light_sides():
        l_half_x().wait_recv()
        l_got[7, LIGHT_CUT:SMALL_HALF, :] = (
            l_got[7, LIGHT_CUT:SMALL_HALF, :].astype(FULL) + l_halves_x[...].astype(FULL)
        ).astype(LOW)
        l_send_y().start()
        l_half_y().wait_recv()
        l_got[11, 0:LIGHT_CUT, :] = (
            l_got[11, 0:LIGHT_CUT, :].astype(FULL) + l_halves_y[...].astype(FULL)
        ).astype(LOW)
        l_send_x().start()

    def light_end():
        l_send_x().wait_recv()
        l_send_y().wait_recv()
        l_total[...] = l_got[15].astype(FULL) + l_from_x[...].astype(FULL) + l_from_y[...].astype(FULL)

    small_join = remote(late_half, late.at[pl.ds(0, SMALL_HALF)], join_send.at[1], join_recv.at[1], sibling)
    own_late = pltpu.make_async_copy(late, out_small.at[me.dp], out_sem.at[1])

    def late_z(origin, target, way):
        block = out_small.at[2 * origin + y]
        return remote(block, block, late_send.at[way, origin], late_recv.at[0, origin], target)

    def late_y(origin, yo):
        block = out_small.at[2 * origin + yo]
        return remote(block, block, late_send.at[2, origin], late_recv.at[1, origin], y_side)

    def late_step(k):
        @pl.when((core == 1) & (z >= k))
        def _():
            late_z(z - k, up, 0).wait_recv()
            pl.when(z < 3)(lambda: late_z(z - k, up, 0).start())
            late_y(z - k, y).start()

        @pl.when((core == 1) & (z + k <= 3))
        def _():
            late_z(z + k, down, 1).wait_recv()
            pl.when(z > 0)(lambda: late_z(z + k, down, 1).start())
            late_y(z + k, y).start()

    def leave():
        for section in range(4):
            @pl.when(me.pipe == section)
            def _(section=section):
                all_of(keep(section), lambda copy: copy.start())

            @pl.when(me.pipe != section)
            def _(section=section):
                all_of(exchange(section), lambda copy: copy.start())

    def late_start():
        light_end()

        @pl.when(core == 0)
        def _():
            late_half[...] = l_total[...].astype(LOW)
            small_join.start()

        @pl.when(core == 1)
        def _():
            late[SMALL_HALF:SMALL_ROWS, :] = l_total[...].astype(LOW)
            small_join.wait_recv()
            own_late.start()
            own_late.wait()
            pl.when(z < 3)(lambda: late_z(z, up, 0).start())
            pl.when(z > 0)(lambda: late_z(z, down, 1).start())
            late_y(z, y).start()

    def light_round(k):
        for n in range(4 * k, 4 * k + 4):
            light_item(*l_sequence[n])

    edge = (z == 0) | (z == 3)

    def early_z(k):
        pl.when(edge)(lambda: bulk_z(k))

    def inner_z(k):
        pl.when(jnp.logical_not(edge))(lambda: bulk_z(k))

    actions = {"LS": [light_sides], "LE": [late_start], "G": [leave]}
    numbered = {item: n for n, item in enumerate(sequence)}
    for k in range(4):
        actions["A%d" % k] = [functools.partial(bulk_item, numbered[0, k])]
        actions["C%d" % k] = [functools.partial(bulk_item, numbered[1, k])]
        actions["B%d" % k] = [functools.partial(bulk_item, numbered[2, k])]
        actions["O%d" % k] = [functools.partial(bulk_item, numbered[3, k])]
        actions["L%d" % k] = [functools.partial(light_round, k)]
        if k < 3:
            actions["E%d" % k] = [functools.partial(early_z, k)]
            actions["I%d" % k] = [functools.partial(inner_z, k)]
        if k:
            actions["T%d" % k] = [functools.partial(late_step, k)]
    for event in REDUCE_ORDER:
        for action in actions[event]:
            action()

    row_copy.wait()
    part_sum[...] = jnp.sum((l_total[...] * l_total[...]).reshape(SMALL_HALF // 8, 8, 128), axis=0)
    lane = lax.broadcasted_iota(jnp.int32, (8, 128), 1)
    is_last = jnp.where((lane == me.dp) & (owner_row[...] == 7), 1.0, 0.0)
    weight = jnp.broadcast_to(jnp.sum(is_last, axis=1, keepdims=True), (8, 128))
    weight = jnp.where(core == 0, jnp.ones((8, 128), FULL), weight)

    def end(low, high):
        def piece(begin, size, scale):
            part = pl.ds(begin, size)
            sums = got[15, part, :].astype(FULL)
            if low:
                sums = sums + from_low[z - 1, part, :].astype(FULL)
            if high:
                sums = sums + from_high[z, part, :].astype(FULL)
            total[part, :] = sums
            squares = jnp.sum((sums * sums).reshape(size // 8, 8, 128), axis=0)
            part_sum[...] += squares if scale is None else squares * scale

        over(0, BIG_HALF - EDGE, lambda begin, size: piece(begin, size, None))
        piece(BIG_HALF - EDGE, EDGE, weight)

    @pl.when(z == 0)
    def _():
        send_down(15, z).wait_recv()
        end(False, True)

    @pl.when((z > 0) & (z < 3))
    def _():
        send_up(15, z).wait_recv()
        send_down(15, z).wait_recv()
        end(True, True)

    @pl.when(z == 3)
    def _():
        send_up(15, z).wait_recv()
        end(True, False)

    big_join = remote(total, out_big.at[1], join_send.at[0], join_recv.at[0], sibling)
    own_big = pltpu.make_async_copy(total, out_big.at[0], out_sem.at[0])

    @pl.when(core == 0)
    def _():
        own_big.start()

    @pl.when(core == 1)
    def _():
        big_join.start()

    def along_pipe(step, slot):
        target = {"dp": me.dp, "pipe": lax.rem(me.pipe + step, 4)}
        return remote(part_sum, by_pipe.at[slot], p_send.at[step], p_recv.at[step], target)

    def along_dp(step, slot):
        target = {"dp": lax.rem(me.dp + step, 8), "pipe": me.pipe}
        return remote(mine, by_dp.at[slot], d_send.at[step], d_recv.at[step], target)

    for step in range(1, 4):
        along_pipe(step, me.pipe).start()
    by_pipe[me.pipe] = part_sum[...]
    for step in range(1, 4):
        along_pipe(step, lax.rem(me.pipe + 4 - step, 4)).wait_recv()
    mine[...] = jnp.sum(by_pipe[...], axis=0)
    for step in range(1, 8):
        along_dp(step, me.dp).start()
    by_dp[me.dp] = mine[...]
    for step in range(1, 8):
        along_dp(step, lax.rem(me.dp + 8 - step, 8)).wait_recv()
    whole = jnp.sum(jnp.sum(by_dp[...], axis=0), axis=0, keepdims=True)
    length = jnp.sqrt(jnp.broadcast_to(jnp.sum(whole, axis=1, keepdims=True), (8, 128)))
    norm[...] = length
    factor[...] = jnp.minimum(1.0, CLIP_NORM / length)

    @pl.when(core == 0)
    def _():
        own_big.wait()
        big_join.wait_recv()
        small_join.wait_send()

    @pl.when(core == 1)
    def _():
        big_join.wait_send()
        for origin in range(4):
            late_y(origin, 1 - y).wait_recv()
            late_y(origin, y).wait_send()
            pl.when((z < 3) & (origin <= z))(lambda: late_z(origin, up, 0).wait_send())
            pl.when((z > 0) & (origin >= z))(lambda: late_z(origin, down, 1).wait_send())

    for other in range(4):
        @pl.when(me.pipe == other)
        def _(other=other):
            all_of(keep(other), lambda copy: copy.wait())

        @pl.when(me.pipe != other)
        def _(other=other):
            all_of(exchange(other), lambda copy: copy.wait_send())
            all_of(arriving(other), lambda copy: copy.wait_recv())

    for step in range(1, 4):
        along_pipe(step, me.pipe).wait_send()
    for step in range(1, 8):
        along_dp(step, me.dp).wait_send()
    for copy in (l_half_x(), l_half_y(), l_send_x(), l_send_y()):
        copy.wait_send()
    for k in range(4):
        send_half_x(k).wait_send()
        send_half_y(k).wait_send()
        send_x(k).wait_send()
        send_y(k).wait_send()
        for group in range(4):
            share(group, k).wait_send()
            l_share(group, k).wait_send()
    for k in range(3):
        zd, at = order[k], 12 + k

        @pl.when(zd > z)
        def _(at=at, zd=zd, k=k):
            send_up(at, zd).wait_send()
            for group in range(4):
                l_up(group, k).wait_send()

        @pl.when(zd < z)
        def _(at=at, zd=zd, k=k):
            send_down(at, zd).wait_send()
            for group in range(4):
                l_down(group, k).wait_send()


def reduce_all(big, small, wide0, wide1, final, stats, table):
    sem = pltpu.SemaphoreType.DMA
    vm = pltpu.VMEM
    lane_tile = jax.ShapeDtypeStruct((8, 128), FULL)
    return pl.pallas_call(
        reduce_kernel,
        name="reduce_all",
        out_shape=(
            jax.ShapeDtypeStruct((2, BIG_HALF, 128), FULL),
            jax.ShapeDtypeStruct((8, SMALL_ROWS, 128), LOW),
            jax.ShapeDtypeStruct((4, STUD_ROWS, C_OUT), LOW),
            jax.ShapeDtypeStruct((4, TEACH_END, C_OUT), LOW),
            jax.ShapeDtypeStruct((4,) + stats.shape[1:], FULL),
            lane_tile,
            lane_tile,
        ),
        in_specs=[any_spec()] * 7,
        out_specs=(any_spec(),) * 5 + (vmem_spec(),) * 2,
        scratch_shapes=[
            vm((16, BIG_HALF, 128), LOW), vm((4, BIG_HALF - BACK_CUT, 128), LOW), vm((4, BACK_CUT, 128), LOW),
            vm((4, BIG_HALF, 128), LOW), vm((4, BIG_HALF, 128), LOW),
            vm((3, BIG_HALF, 128), LOW), vm((3, BIG_HALF, 128), LOW),
            vm((4, BIG_HALF, 128), LOW), vm((BIG_HALF, 128), FULL),
            vm((16, SMALL_HALF, 128), LOW), vm((16, SMALL_HALF, 128), LOW),
            vm((4, 3, SMALL_HALF, 128), LOW), vm((4, 3, SMALL_HALF, 128), LOW),
            vm((SMALL_HALF - LIGHT_CUT, 128), LOW), vm((LIGHT_CUT, 128), LOW),
            vm((SMALL_HALF, 128), LOW), vm((SMALL_HALF, 128), LOW), vm((SMALL_HALF, 128), FULL),
            vm((SMALL_ROWS, 128), LOW), vm((SMALL_HALF, 128), LOW), vm((8, 128), jnp.int32),
            vm((4, 8, 128), FULL), vm((8, 8, 128), FULL), vm((8, 128), FULL), vm((8, 128), FULL),
            sem((2, 16)), sem((2, 16)),
            sem((5,)), sem((5,)), sem((5,)), sem((5,)), sem((5,)), sem((5,)), sem((5,)), sem((5,)),
            sem((3,)), sem((3,)), sem((3,)), sem((3,)),
            sem((4, 3)), sem((4, 3)), sem((4, 3)), sem((4, 3)),
            sem((4,)), sem((16,)), sem((3,)), sem((3, 4)), sem((2, 4)), sem((2,)), sem((2,)),
            sem((2, 4)), sem((2, 4)), sem((4,)), sem((4,)), sem((4,)), sem((4,)), sem((8,)), sem((8,)),
        ],
        compiler_params=pltpu.CompilerParams(
            collective_id=1, has_side_effects=True, vmem_limit_bytes=62 << 20
        ),
    )(big.reshape(2, 8, 2, BIG_HALF, 128), small.reshape(2, 8, 2, SMALL_HALF, 128),
      wide0, wide1, final, stats, table)


def high_dot(a, b, dims=((1,), (0,))):
    return lax.dot_general(a, b, (dims, ((), ())), precision=HIGH, preferred_element_type=FULL)


PIECES = 7
FRONT = 48


def update_kernel(owners, factor_ref, norm, big, small, gram_old, basis_old, params, moment, second,
                  clipped, moment_new, second_new, params_new, gram_new, basis_new, length,
                  tiles, low, grad, held, rotated, weights, gram, in_sem, out_sem, tile_sem):
    factor = factor_ref[0:1, :]
    length[0, 0] = jnp.max(norm[...])
    block, section = owners[0, lax.axis_index("dp")], lax.axis_index("pipe")
    even = lax.rem(section, 2) == 0
    span = params.shape[0]
    piece = held.shape[0] // PIECES

    @pl.when(even)
    def _():
        pltpu.make_async_copy(big, tiles.at[pl.ds(0, BIG_ROWS)], tile_sem).start()

    def loads(i):
        part = pl.ds(piece * i, min(piece, span - piece * i))
        for n, (src, dst) in enumerate(((params, weights), (moment, held), (second, rotated))):
            yield pltpu.make_async_copy(src.at[part, 0, :], dst.at[part], in_sem.at[n, i])

    def stores(i):
        count = min(piece, span - piece * i)
        part = pl.ds(piece * i, count)
        yield pltpu.make_async_copy(
            grad.at[pl.ds(FRONT + piece * i, count)], clipped.at[part, 0, :], out_sem.at[3, i])
        pairs = ((held, moment_new), (rotated, second_new), (weights, params_new))
        for n, (src, dst) in enumerate(pairs):
            yield pltpu.make_async_copy(src.at[part], dst.at[part, 0, :], out_sem.at[n, i])

    for i in range(PIECES):
        for load in loads(i):
            load.start()

    @pl.when(even)
    def _():
        pltpu.make_async_copy(big, tiles.at[pl.ds(0, BIG_ROWS)], tile_sem).wait()

    @pl.when(jnp.logical_not(even))
    def _():
        low[...] = jnp.zeros_like(low)

        @pl.when(block == 0)
        def _():
            copy = pltpu.make_async_copy(small.at[0:20], low, tile_sem)
            copy.start()
            copy.wait()

        @pl.when(block == 1)
        def _():
            copy = pltpu.make_async_copy(small.at[19:33], low.at[0:14], tile_sem)
            copy.start()
            copy.wait()

        @pl.loop(0, WINDOW)
        def _(r):
            tiles[pl.ds(pl.multiple_of(TILE * r, TILE), TILE), :] = low[r].astype(FULL)

    @pl.loop(0, WINDOW)
    def _(r):
        narrow, plain = tile_forms(section, STRIDE * block + r)
        edge = even & (r == STRIDE)
        narrow, plain = narrow & jnp.logical_not(edge), plain | edge
        base = FRONT - 6 * block + TILE * r
        here = pl.multiple_of(TILE * r, TILE)

        @pl.when(narrow)
        def _():
            for j in range(4):
                grad[pl.ds(base + j, 64, 4), :] = tiles[pl.ds(here + 64 * j, 64), :]

        @pl.when(plain)
        def _():
            grad[pl.ds(base, TILE), :] = tiles[pl.ds(here, TILE), :]

        @pl.when(jnp.logical_not(narrow | plain))
        def _():
            for j in range(16):
                grad[pl.ds(base + j, 16, 16), :] = tiles[pl.ds(here + 16 * j, 16), :]

    tail = piece * PIECES - 8
    rest = lax.broadcasted_iota(jnp.int32, (8, 128), 0) + tail
    grad[FRONT + tail : FRONT + tail + 8, :] = jnp.where(
        rest < span, grad[FRONT + tail : FRONT + tail + 8, :], 0.0
    )
    gram[...] = jnp.zeros_like(gram)

    def halves(value):
        high = value.astype(LOW)
        return high, (value - high.astype(FULL)).astype(LOW)

    def split_dot(a, b, dims=((1,), (0,))):
        def dot(left, right):
            return lax.dot_general(left, right, (dims, ((), ())), preferred_element_type=FULL)

        return dot(a[0], b[0]) + (dot(a[0], b[1]) + dot(a[1], b[0]))

    @pl.loop(0, PIECES)
    def _(i):
        part = halves(grad[pl.ds(pl.multiple_of(FRONT + piece * i, 8), piece), :])
        gram[...] += split_dot(part, part, ((0,), (0,)))

    old = basis_old[...]
    fresh = DECAY_STATS * gram_old[...] + (1.0 - DECAY_STATS) * (gram[...] * (factor * factor))
    gram_new[...] = fresh
    product = high_dot(fresh, old)
    rotation = product / jnp.sqrt(jnp.sum(product * product))
    for repeat in range(NS_STEPS):
        parts = halves(rotation)
        square = split_dot(parts, parts, ((0,), (0,)))
        rotation = 1.5 * rotation - 0.5 * split_dot(parts, halves(square))
    basis_new[...] = rotation
    change = halves(high_dot(old, rotation, ((0,), (0,))))
    turn = halves(rotation)
    correction = math.sqrt(1.0 - DECAY_SECOND**STEP) / (1.0 - DECAY_FIRST**STEP)
    for i in range(PIECES):
        for load in loads(i):
            load.wait()
        at = slice(FRONT + piece * i, FRONT + piece * i + piece)
        part = slice(piece * i, piece * i + piece)
        clip = grad[at, :] * factor
        grad[at, :] = clip
        turned = split_dot(halves(clip), turn)
        first = DECAY_FIRST * split_dot(halves(held[part, :]), change) + (1.0 - DECAY_FIRST) * turned
        power = DECAY_SECOND * rotated[part, :] + (1.0 - DECAY_SECOND) * turned * turned
        held[part, :] = first
        rotated[part, :] = power
        scaled = halves(first / (jnp.sqrt(power) + ADAM_EPS))
        direction = split_dot(scaled, turn, ((1,), (1,))) * correction
        before = weights[part, :]
        weights[part, :] = before - LEARN_RATE * (direction + WEIGHT_DECAY * before)
        for store in stores(i):
            store.start()
    for i in range(PIECES):
        for store in stores(i):
            store.wait()


def update(owners, factor, norm, big, small, gram_old, basis_old, params, moment, second):
    span = params.shape[1] // 128
    rows = -(-span // (8 * PIECES)) * 8 * PIECES
    flat_shape = jax.ShapeDtypeStruct((span, 1, 128), FULL)
    square = jax.ShapeDtypeStruct((128, 128), FULL)
    sem = pltpu.SemaphoreType.DMA
    vm = pltpu.VMEM
    outs = pl.pallas_call(
        update_kernel,
        name="update",
        out_shape=(flat_shape,) * 4 + (square,) * 2 + (jax.ShapeDtypeStruct((1, 1), FULL),),
        in_specs=[smem_spec()] + [vmem_spec()] * 2 + [any_spec()] * 2 + [vmem_spec()] * 2 + [any_spec()] * 3,
        out_specs=(any_spec(),) * 4 + (vmem_spec(),) * 2 + (smem_spec(),),
        scratch_shapes=[
            vm((WINDOW * TILE, 128), FULL), vm((WINDOW, TILE, 128), LOW),
            vm((FRONT + WINDOW * TILE, 128), FULL), vm((rows, 128), FULL), vm((rows, 128), FULL),
            vm((rows, 128), FULL), vm((128, 128), FULL), sem((3, PIECES)), sem((4, PIECES)), sem,
        ],
        compiler_params=pltpu.CompilerParams(vmem_limit_bytes=60 << 20),
    )(owners, factor, norm, big.reshape(BIG_ROWS, 128), small.reshape(USED_TILES[1], TILE, 128),
      gram_old, basis_old, params.reshape(span, 1, 128), moment.reshape(span, 1, 128),
      second.reshape(span, 1, 128))
    return tuple(out.reshape(1, span * 128) for out in outs[:4]) + outs[4:]


def to_phases(teach, stud):
    def split(part, axes):
        crops, high, across, channels = part.shape
        part = part.reshape(crops, high // 2, 2, across // 2, 2, channels).transpose(axes)
        return part.reshape(4, -1, channels)

    zeros = jnp.zeros((4, PADDED - ROWS, teach.shape[-1]), teach.dtype)
    parts = [split(stud, (2, 4, 0, 1, 3, 5)), split(teach, (2, 4, 1, 3, 0, 5)), zeros]
    return jnp.concatenate(parts, axis=1)


def from_phases(phases, shape, crops_last):
    crops, high, across, channels = shape
    if crops_last:
        part = phases.reshape(2, 2, high // 2, across // 2, crops, channels).transpose(4, 2, 0, 3, 1, 5)
    else:
        part = phases.reshape(2, 2, crops, high // 2, across // 2, channels).transpose(2, 3, 0, 4, 1, 5)
    return part.reshape(shape)


def on_small_slice(
    teach_in,
    stud_in,
    params,
    owners,
    depth_gates,
    teach_ids,
    stud_ids,
    targets,
    moment,
    second,
    gram_stats,
    eigen_basis,
):
    phases = to_phases(teach_in[0], stud_in[0])
    big, small, ids = prepare(owners, params)
    all_big, all_small, table = gather_all(big, small, ids)
    wide_0, wide_1, final, stats, grad_x, out_big, out_small = run_step(
        table,
        depth_gates,
        teach_ids.T,
        stud_ids,
        all_big.reshape(2, 8, BIG_ROWS, 128),
        all_small.reshape(2, USED_TILES[1], TILE, 128),
        phases,
        targets,
    )
    sum_big, sum_small, segment_stud, segment_teach, stats, norm, factor = reduce_all(
        out_big, out_small, wide_0, wide_1, final, stats, table
    )
    clipped, moment_new, second_new, params_new, gram_new, rotation, length = update(
        owners, factor, norm, sum_big, sum_small, gram_stats[0], eigen_basis[0], params, moment, second
    )
    teach_shape, stud_shape = teach_in.shape[1:], stud_in.shape[1:]
    small_teach = (teach_shape[1] // 2, teach_shape[2] // 2, teach_shape[0], C_OUT)
    small_stud = (stud_shape[0], stud_shape[1] // 2, stud_shape[2] // 2, C_OUT)
    segment_teach = segment_teach[:, : ROWS - STUD_ROWS].reshape((4,) + small_teach).transpose(0, 3, 1, 2, 4)
    segment_stud = segment_stud.reshape((4,) + small_stud)
    stats = stats[:, 0:2]
    teach_grad = from_phases(grad_x[:, STUD_ROWS:ROWS], teach_shape, True)
    stud_grad = from_phases(grad_x[:, :STUD_ROWS], stud_shape, False)
    grad_norm = length.reshape(())
    return (
        segment_teach[None],
        segment_stud[None],
        teach_grad[None],
        stud_grad[None],
        stats[None, :, None],
        grad_norm,
        clipped,
        moment_new,
        second_new,
        params_new,
        gram_new[None],
        rotation[None],
    )


def solution(mesh):
    placed = (
        P("pipe", "dp", None, None, None),
        P("pipe", "dp", None, None, None),
        P("pipe", "dp"),
        P("pipe", None),
        P(),
        P(None, "dp"),
        P(None, "dp"),
        P(),
        P("pipe", "dp"),
        P("pipe", "dp"),
        P("pipe", "dp", None),
        P("pipe", "dp", None),
    )
    small_slice = mesh.shape["dp"] == 8 and mesh.shape["pipe"] == 4
    return jax.shard_map(
        on_small_slice if small_slice else on_device,
        mesh=mesh,
        in_specs=placed,
        out_specs=(
            P("pipe", None, "dp", None, None, None),
            P("pipe", None, "dp", None, None, None),
            P("pipe", "dp", None, None, None),
            P("pipe", "dp", None, None, None),
            P("pipe", None, "dp", None, None),
            P(),
            P("pipe", "dp"),
            P("pipe", "dp"),
            P("pipe", "dp"),
            P("pipe", "dp"),
            P("pipe", "dp", None),
            P("pipe", "dp", None),
        ),
        check_vma=False,
    )
```

```python
import functools
import math

import jax
import jax.numpy as jnp
import numpy as np
from jax import lax
from jax.experimental import pallas as pl
from jax.experimental.pallas import tpu as pltpu
from jax.sharding import PartitionSpec as P

C_IN = 1024
MID = 512
C_OUT = 2048
STEP = 10
NS_STEPS = 5


HIGH = lax.Precision.HIGHEST
NORM_EPS = 1e-05
POOL_EPS = 1e-06
CLIP_NORM = 1.0
LEARN_RATE = 0.02
DECAY_FIRST = 0.9
DECAY_SECOND = 0.95
DECAY_STATS = 0.95
ADAM_EPS = 1e-08
WEIGHT_DECAY = 0.01


def section_shapes(section):
    if section == 0:
        return [
            ("first_conv", (C_IN, MID)),
            ("middle_conv", (9 * MID, MID)),
            ("skip_conv", (C_IN, C_OUT)),
            ("first_gain", (MID,)),
            ("first_bias", (MID,)),
            ("middle_gain", (MID,)),
            ("middle_bias", (MID,)),
            ("skip_gain", (C_OUT,)),
            ("skip_bias", (C_OUT,)),
        ]
    if section == 2:
        return [
            ("first_conv", (C_OUT, MID)),
            ("middle_conv", (9 * MID, MID)),
            ("first_gain", (MID,)),
            ("first_bias", (MID,)),
            ("middle_gain", (MID,)),
            ("middle_bias", (MID,)),
        ]
    return [("last_conv", (MID, C_OUT)), ("last_gain", (C_OUT,)), ("last_bias", (C_OUT,))]


def unpack(flat_vector, section):
    pieces = {}
    offset = 0
    for entry_name, entry_shape in section_shapes(section):
        entry_size = math.prod(entry_shape)
        pieces[entry_name] = flat_vector[offset : offset + entry_size].reshape(entry_shape)
        offset = offset + entry_size
    return pieces


def pack(grads, section, flat_size):
    parts = [grads[entry_name].reshape(-1) for entry_name, entry_shape in section_shapes(section)]
    used = sum((math.prod(entry_shape) for entry_name, entry_shape in section_shapes(section)))
    parts.append(jnp.zeros((flat_size - used,), jnp.float32))
    return jnp.concatenate(parts)


def as_float(vector):
    return vector.astype(jnp.float32)


def to_low(groups):
    return tuple((portion.astype(jnp.bfloat16) for portion in groups))


def to_high(groups):
    return tuple((portion.astype(jnp.float32) for portion in groups))


def point_conv(groups, weight):
    return tuple(
        (
            jnp.einsum("khwc,cd->khwd", portion, weight, preferred_element_type=jnp.float32)
            for portion in groups
        )
    )


def point_back(grad_out, groups, weight):
    low_grads = to_low(grad_out)
    grad_input = tuple(
        (
            jnp.einsum("khwd,cd->khwc", grad_part, weight, preferred_element_type=jnp.float32)
            for grad_part in low_grads
        )
    )
    grad_weight = sum(
        (
            jnp.einsum("khwc,khwd->cd", in_part, grad_part, preferred_element_type=jnp.float32)
            for in_part, grad_part in zip(groups, low_grads)
        )
    )
    return (grad_input, grad_weight)


def patches(portion, stride):
    height = portion.shape[1]
    across = portion.shape[2]
    padded = jnp.pad(portion, ((0, 0), (1, 1), (1, 1), (0, 0)))
    shifted = [
        padded[:, row_off : row_off + height : stride, col_off : col_off + across : stride, :]
        for row_off in range(3)
        for col_off in range(3)
    ]
    return jnp.concatenate(shifted, axis=-1)


def area_conv(groups, weight, stride):
    columns = tuple((patches(portion, stride) for portion in groups))
    return (point_conv(columns, weight), columns)


def unpatch(grad_cols, height, across, stride):
    channels = grad_cols.shape[-1] // 9
    padded = jnp.zeros((grad_cols.shape[0], height + 2, across + 2, channels), jnp.float32)
    for row_off in range(3):
        for col_off in range(3):
            offset = (3 * row_off + col_off) * channels
            padded = padded.at[
                :, row_off : row_off + height : stride, col_off : col_off + across : stride, :
            ].add(grad_cols[..., offset : offset + channels])
    return padded[:, 1 : height + 1, 1 : across + 1, :]


def area_back(grad_out, columns, weight, stride, in_shapes):
    grad_cols, grad_weight = point_back(grad_out, columns, weight)
    grad_input = tuple(
        (
            unpatch(grad_part, shape_item[1], shape_item[2], stride)
            for grad_part, shape_item in zip(grad_cols, in_shapes)
        )
    )
    return (grad_input, grad_weight)


def batch_norm(groups, gain, bias):
    rows_total = sum((portion.shape[0] * portion.shape[1] * portion.shape[2] for portion in groups))
    centre = sum((jnp.sum(portion, axis=(0, 1, 2)) for portion in groups)) / rows_total
    spread = (
        sum((jnp.sum(jnp.square(portion - centre), axis=(0, 1, 2)) for portion in groups))
        / rows_total
    )
    inverse = lax.rsqrt(spread + NORM_EPS)
    standard = tuple(((portion - centre) * inverse for portion in groups))
    normed = tuple((gain * std_part + bias for std_part in standard))
    return (normed, (centre, spread, inverse, standard))


def norm_back(grad_out, gain, saved):
    centre, spread, inverse, standard = saved
    rows_total = sum(
        (portion.shape[0] * portion.shape[1] * portion.shape[2] for portion in standard)
    )
    grad_sum = sum((jnp.sum(grad_part, axis=(0, 1, 2)) for grad_part in grad_out))
    grad_dot = sum(
        (
            jnp.sum(grad_part * std_part, axis=(0, 1, 2))
            for grad_part, std_part in zip(grad_out, standard)
        )
    )
    grad_input = tuple(
        (
            gain
            * inverse
            * (grad_part - grad_sum / rows_total - std_part * (grad_dot / rows_total))
            for grad_part, std_part in zip(grad_out, standard)
        )
    )
    return (grad_input, grad_dot, grad_sum)


def through_softplus(grad_out, pre_values):
    return tuple(
        (grad_part * jax.nn.sigmoid(pre_part) for grad_part, pre_part in zip(grad_out, pre_values))
    )


def front_forward(pieces, inputs):
    first = point_conv(inputs, pieces["first_conv"])
    normed_a, saved_a = batch_norm(
        first, as_float(pieces["first_gain"]), as_float(pieces["first_bias"])
    )
    hidden = tuple((jax.nn.softplus(portion).astype(jnp.bfloat16) for portion in normed_a))
    middle, columns = area_conv(hidden, pieces["middle_conv"], 2)
    normed_b, saved_b = batch_norm(
        middle, as_float(pieces["middle_gain"]), as_float(pieces["middle_bias"])
    )
    narrow = tuple((jax.nn.softplus(portion) for portion in normed_b))
    reduced = tuple((portion[:, ::2, ::2, :] for portion in inputs))
    skipped = point_conv(reduced, pieces["skip_conv"])
    wide, saved_p = batch_norm(
        skipped, as_float(pieces["skip_gain"]), as_float(pieces["skip_bias"])
    )
    norm_rows = jnp.stack(
        [
            jnp.concatenate([saved_a[0], saved_b[0], saved_p[0]]),
            jnp.concatenate([saved_a[1], saved_b[1], saved_p[1]]),
        ]
    )
    kept = (normed_a, hidden, columns, normed_b, reduced, saved_a, saved_b, saved_p)
    return (wide, narrow, norm_rows, kept)


def front_backward(pieces, inputs, grad_wide, grad_narrow):
    wide, narrow, norm_rows, kept = front_forward(pieces, inputs)
    normed_a, hidden, columns, normed_b, reduced, saved_a, saved_b, saved_p = kept
    grads = {}
    grad_pre_b = through_softplus(grad_narrow, normed_b)
    grad_mid, grads["middle_gain"], grads["middle_bias"] = norm_back(
        grad_pre_b, as_float(pieces["middle_gain"]), saved_b
    )
    grad_hidden, grads["middle_conv"] = area_back(
        grad_mid, columns, pieces["middle_conv"], 2, [portion.shape for portion in hidden]
    )
    grad_pre_a = through_softplus(grad_hidden, normed_a)
    grad_first, grads["first_gain"], grads["first_bias"] = norm_back(
        grad_pre_a, as_float(pieces["first_gain"]), saved_a
    )
    grad_inputs, grads["first_conv"] = point_back(grad_first, inputs, pieces["first_conv"])
    grad_skip, grads["skip_gain"], grads["skip_bias"] = norm_back(
        grad_wide, as_float(pieces["skip_gain"]), saved_p
    )
    grad_reduced, grads["skip_conv"] = point_back(grad_skip, reduced, pieces["skip_conv"])
    grad_inputs = tuple(
        (
            full_part.at[:, ::2, ::2, :].add(part_reduced)
            for full_part, part_reduced in zip(grad_inputs, grad_reduced)
        )
    )
    return (grad_inputs, grads)


def join_forward(pieces, wide, narrow):
    last = point_conv(narrow, pieces["last_conv"])
    normed, saved = batch_norm(last, as_float(pieces["last_gain"]), as_float(pieces["last_bias"]))
    pre_values = tuple(
        (
            skip_part.astype(jnp.float32) + branch_part
            for skip_part, branch_part in zip(wide, normed)
        )
    )
    ending = tuple((jax.nn.softplus(pre_part) for pre_part in pre_values))
    filler = jnp.zeros((2 * MID,), jnp.float32)
    norm_rows = jnp.stack(
        [jnp.concatenate([saved[0], filler]), jnp.concatenate([saved[1], filler])]
    )
    return (ending, norm_rows, (pre_values, saved))


def join_grads(pieces, narrow, kept, grad_out, gate):
    pre_values, saved = kept
    grad_pre = tuple(
        (
            grad_part * jax.nn.sigmoid(pre_part) * gate
            for grad_part, pre_part in zip(grad_out, pre_values)
        )
    )
    grad_wide = tuple(
        (pre_grad + grad_part * (1.0 - gate) for pre_grad, grad_part in zip(grad_pre, grad_out))
    )
    grad_last, gain_grad, bias_grad = norm_back(grad_pre, as_float(pieces["last_gain"]), saved)
    grad_narrow, weight_grad = point_back(grad_last, narrow, pieces["last_conv"])
    grads = {"last_conv": weight_grad, "last_gain": gain_grad, "last_bias": bias_grad}
    return (grad_wide, grad_narrow, grads)


def split_forward(pieces, wide):
    first = point_conv(wide, pieces["first_conv"])
    normed_a, saved_a = batch_norm(
        first, as_float(pieces["first_gain"]), as_float(pieces["first_bias"])
    )
    hidden = tuple((jax.nn.softplus(portion).astype(jnp.bfloat16) for portion in normed_a))
    middle, columns = area_conv(hidden, pieces["middle_conv"], 1)
    normed_b, saved_b = batch_norm(
        middle, as_float(pieces["middle_gain"]), as_float(pieces["middle_bias"])
    )
    narrow = tuple((jax.nn.softplus(portion) for portion in normed_b))
    filler = jnp.zeros((C_OUT,), jnp.float32)
    norm_rows = jnp.stack(
        [
            jnp.concatenate([saved_a[0], saved_b[0], filler]),
            jnp.concatenate([saved_a[1], saved_b[1], filler]),
        ]
    )
    return (narrow, norm_rows, (normed_a, hidden, columns, normed_b, saved_a, saved_b))


def split_backward(pieces, wide, grad_relay, grad_narrow):
    narrow, norm_rows, kept = split_forward(pieces, wide)
    normed_a, hidden, columns, normed_b, saved_a, saved_b = kept
    grads = {}
    grad_pre_b = through_softplus(grad_narrow, normed_b)
    grad_mid, grads["middle_gain"], grads["middle_bias"] = norm_back(
        grad_pre_b, as_float(pieces["middle_gain"]), saved_b
    )
    grad_hidden, grads["middle_conv"] = area_back(
        grad_mid, columns, pieces["middle_conv"], 1, [portion.shape for portion in hidden]
    )
    grad_pre_a = through_softplus(grad_hidden, normed_a)
    grad_first, grads["first_gain"], grads["first_bias"] = norm_back(
        grad_pre_a, as_float(pieces["first_gain"]), saved_a
    )
    grad_conv_in, grads["first_conv"] = point_back(grad_first, wide, pieces["first_conv"])
    grad_wide = tuple(
        (relay_part + conv_part for relay_part, conv_part in zip(grad_relay, grad_conv_in))
    )
    return (grad_wide, grads)


def pool_grad(final, targets, picks):
    result = []
    for portion, pick_ids in zip(final, picks):
        cubes = jnp.mean(portion * portion * portion, axis=(1, 2)) + POOL_EPS
        factor = jnp.exp(jnp.log(cubes) * (-2.0 / 3.0)) * targets[pick_ids]
        result.append(factor[:, None, None, :] * portion * portion)
    return tuple(result)


def used_size(section):
    return sum((math.prod(entry_shape) for entry_name, entry_shape in section_shapes(section)))


def batch_pass(reals, inputs, gate, targets, picks):
    pieces = [unpack(reals[section], section) for section in range(4)]
    wide_f, narrow_f, rows_0, _ = front_forward(pieces[0], inputs)
    wide_0, narrow_0 = to_low(wide_f), to_low(narrow_f)
    ending_1, rows_1, kept_1 = join_forward(pieces[1], wide_0, narrow_0)
    wide_1 = to_low(ending_1)
    narrow_f, rows_2, _ = split_forward(pieces[2], wide_1)
    narrow_2 = to_low(narrow_f)
    ending_3, rows_3, kept_3 = join_forward(pieces[3], wide_1, narrow_2)
    final = tuple(
        (
            jnp.where(gate > 0, end_part, relay_part.astype(jnp.float32))
            for end_part, relay_part in zip(ending_3, wide_1)
        )
    )
    cotangent = pool_grad(final, targets, picks)
    grad_wide, grad_narrow, grads_3 = join_grads(pieces[3], narrow_2, kept_3, cotangent, gate)
    grad_wide, grads_2 = split_backward(
        pieces[2], wide_1, to_high(to_low(grad_wide)), to_high(to_low(grad_narrow))
    )
    grad_wide, grad_narrow, grads_1 = join_grads(
        pieces[1], narrow_0, kept_1, to_high(to_low(grad_wide)), 1.0
    )
    grad_inputs, grads_0 = front_backward(
        pieces[0], inputs, to_high(to_low(grad_wide)), to_high(to_low(grad_narrow))
    )
    outs = (wide_0, wide_1, wide_1, to_low(final))
    stats = jnp.stack([rows_0, rows_1, rows_2 * gate, rows_3 * gate])
    return (outs, stats, to_low(grad_inputs), (grads_0, grads_1, grads_2, grads_3))


def on_device(
    teach_in,
    stud_in,
    params,
    owners,
    depth_gates,
    teach_ids,
    stud_ids,
    targets,
    moment,
    second,
    gram_stats,
    eigen_basis,
):
    sections = lax.axis_size("pipe")
    rank = lax.axis_index("pipe")
    owner_count = lax.axis_size("dp")
    span_size = params.shape[1]
    flat_size = span_size * owner_count
    owner_rows = lax.all_gather(owners, "pipe", axis=0, tiled=True)
    gathered = lax.all_gather(params[0].astype(jnp.bfloat16), ("pipe", "dp"), axis=0)
    gathered = gathered.reshape(sections, owner_count, span_size)
    reals = []
    for section in range(sections):
        inverse = jnp.argsort(owner_rows[section]).astype(jnp.int32)
        blocks = -(-used_size(section) // span_size)
        reals.append(gathered[section][inverse[:blocks]].reshape(blocks * span_size))
    inputs = (teach_in[0], stud_in[0])
    gate = depth_gates[rank].astype(jnp.float32)
    outs, stats, (teach_grad, stud_grad), grads = batch_pass(
        reals, inputs, gate, targets, (teach_ids[rank], stud_ids[rank])
    )
    segment_teach = lax.all_to_all(
        jnp.stack([part[0] for part in outs]), "pipe", split_axis=0, concat_axis=0, tiled=True
    )
    segment_stud = lax.all_to_all(
        jnp.stack([part[1] for part in outs]), "pipe", split_axis=0, concat_axis=0, tiled=True
    )
    stats = lax.all_to_all(stats, "pipe", split_axis=0, concat_axis=0, tiled=True)
    rows = []
    for section in range(sections):
        flat = pack(grads[section], section, flat_size).reshape(owner_count, span_size)
        rows.append(flat[owner_rows[section]])
    span_total = lax.psum_scatter(
        jnp.stack(rows).reshape(sections * owner_count, span_size),
        ("pipe", "dp"),
        scatter_dimension=0,
        tiled=True,
    ).reshape(span_size)
    total_squares = lax.psum(jnp.sum(span_total * span_total), ("dp", "pipe"))
    grad_norm = jnp.sqrt(total_squares)
    factor = jnp.minimum(1.0, CLIP_NORM / grad_norm)
    clipped = span_total * factor
    matrix = clipped.reshape(span_size // 128, 128)
    gram_old = gram_stats[0]
    basis_old = eigen_basis[0]
    gram_new = DECAY_STATS * gram_old + (1.0 - DECAY_STATS) * jnp.dot(
        matrix.T, matrix, precision=HIGH
    )
    product = jnp.dot(gram_new, basis_old, precision=HIGH)
    rotation = product / jnp.sqrt(jnp.sum(product * product))
    for repeat in range(NS_STEPS):
        square = jnp.dot(rotation.T, rotation, precision=HIGH)
        rotation = 1.5 * rotation - 0.5 * jnp.dot(rotation, square, precision=HIGH)
    moment_old = moment.reshape(span_size // 128, 128)
    initial = jnp.dot(moment_old, basis_old.T, precision=HIGH)
    blended = DECAY_FIRST * initial + (1.0 - DECAY_FIRST) * matrix
    moment_new = jnp.dot(blended, rotation, precision=HIGH)
    rotated = jnp.dot(matrix, rotation, precision=HIGH)
    second_new = (
        DECAY_SECOND * second.reshape(span_size // 128, 128)
        + (1.0 - DECAY_SECOND) * rotated * rotated
    )
    correction = math.sqrt(1.0 - DECAY_SECOND**STEP) / (1.0 - DECAY_FIRST**STEP)
    direction = (
        jnp.dot(moment_new / (jnp.sqrt(second_new) + ADAM_EPS), rotation.T, precision=HIGH)
        * correction
    )
    weights = params.reshape(span_size // 128, 128)
    params_new = weights - LEARN_RATE * (direction + WEIGHT_DECAY * weights)
    return (
        segment_teach[None],
        segment_stud[None],
        teach_grad[None],
        stud_grad[None],
        stats[None, :, None],
        grad_norm,
        clipped.reshape(1, span_size),
        moment_new.reshape(1, span_size),
        second_new.reshape(1, span_size),
        params_new.reshape(1, span_size),
        gram_new[None],
        rotation[None],
    )


MESH = pl.DeviceIdType.MESH
LOW = jnp.bfloat16
FULL = jnp.float32
TILE = 256
WINDOW = 20
STRIDE = 19
EDGE = 64
BIG_ROWS = STRIDE * TILE + EDGE
VEC_TILE = (152, 32, 104, 32)
USED_TILES = (153, 33, 105, 33)
FRONT_WIDE = 88
SMALL_ROWS = 1056
ROWS = 120
PADDED = 128
STUD_ROWS = 48
TEACH_END = 80


def any_spec():
    return pl.BlockSpec(memory_space=pl.ANY)


def smem_spec():
    return pl.BlockSpec(memory_space=pltpu.SMEM)


def vmem_spec():
    return pl.BlockSpec(memory_space=pltpu.VMEM)


def tile_forms(section, tile):
    even = lax.rem(section, 2) == 0
    vector = jnp.where(section == 0, 152, jnp.where(section == 2, 104, 32))
    narrow_end = jnp.where(section == 0, FRONT_WIDE, jnp.where(section == 2, 104, 0))
    narrow = even & (tile < narrow_end)
    plain = tile == vector
    return narrow, plain


def prepare_kernel(owners, params, big, small, ids, flat, sem):
    block, section = owners[0, lax.axis_index("dp")], lax.axis_index("pipe")

    even = lax.rem(section, 2) == 0
    flat[0:EDGE, :] = jnp.zeros((EDGE, 128), FULL)
    flat[STRIDE * TILE : WINDOW * TILE, :] = jnp.zeros((TILE, 128), FULL)
    copy = pltpu.make_async_copy(params.at[:, 0, :], flat.at[pl.ds(6 * block, params.shape[0])], sem)
    copy.start()

    @pl.when(jnp.logical_not(even))
    def _():
        @pl.loop(0, small.shape[0])
        def _(r):
            small[r] = jnp.zeros((TILE, 128), LOW)

    lane = lax.broadcasted_iota(jnp.int32, (8, 128), 1)
    row = jnp.zeros((8, 128), jnp.int32)
    for j in range(8):
        row = jnp.where(lane == j, owners[0, j], row)
    ids[...] = row
    copy.wait()

    def wide_tile(base):
        return [flat[pl.ds(base + j, 16, 16), :].astype(LOW) for j in range(16)]

    @pl.when(even)
    def _():
        @pl.loop(0, STRIDE)
        def _(r):
            narrow, plain = tile_forms(section, STRIDE * block + r)
            base = pl.multiple_of(TILE * r, TILE)

            @pl.when(narrow)
            def _():
                for j in range(4):
                    big[pl.ds(base + 64 * j, 64), :] = flat[pl.ds(base + j, 64, 4), :].astype(LOW)

            @pl.when(plain)
            def _():
                big[pl.ds(base, TILE), :] = flat[pl.ds(base, TILE), :].astype(LOW)

            @pl.when(jnp.logical_not(narrow | plain))
            def _():
                for j, part in enumerate(wide_tile(base)):
                    big[pl.ds(base + 16 * j, 16), :] = part

        big[STRIDE * TILE : BIG_ROWS, :] = flat[STRIDE * TILE : BIG_ROWS, :].astype(LOW)

    @pl.when(jnp.logical_not(even))
    def _():
        @pl.loop(0, WINDOW)
        def _(r):
            tile = STRIDE * block + r
            base = pl.multiple_of(TILE * r, TILE)

            @pl.when(tile == VEC_TILE[1])
            def _():
                small[tile] = flat[pl.ds(base, TILE), :].astype(LOW)

            @pl.when(tile < VEC_TILE[1])
            def _():
                for j, part in enumerate(wide_tile(base)):
                    small[tile, 16 * j : 16 * j + 16, :] = part


def prepare(owners, params):
    return pl.pallas_call(
        prepare_kernel,
        name="prepare",
        out_shape=(
            jax.ShapeDtypeStruct((BIG_ROWS, 128), LOW),
            jax.ShapeDtypeStruct((USED_TILES[1], TILE, 128), LOW),
            jax.ShapeDtypeStruct((8, 128), jnp.int32),
        ),
        in_specs=[smem_spec(), any_spec()],
        out_specs=(vmem_spec(),) * 3,
        scratch_shapes=[pltpu.VMEM((WINDOW * TILE, 128), FULL), pltpu.SemaphoreType.DMA],
        compiler_params=pltpu.CompilerParams(vmem_limit_bytes=60 << 20),
    )(owners, params.reshape(-1, 1, 128))


class Place:
    def __init__(self):
        self.dp = lax.axis_index("dp")
        self.pipe = lax.axis_index("pipe")
        self.x, self.core = self.pipe // 2, self.pipe % 2
        self.z, self.y = self.dp // 2, self.dp % 2

    def device(self, x=None, core=None, z=None, y=None):
        x = self.x if x is None else x
        core = self.core if core is None else core
        z = self.z if z is None else z
        y = self.y if y is None else y
        return {"dp": 2 * z + y, "pipe": 2 * x + core}

    def enter(self):
        barrier = pltpu.get_barrier_semaphore()
        for step in range(1, 8):
            other = lax.rem(self.dp + step, 8)
            pl.semaphore_signal(
                barrier, inc=1, device_id={"dp": other, "pipe": self.pipe}, device_id_type=MESH
            )
        for step in range(1, 4):
            other = lax.rem(self.pipe + step, 4)
            pl.semaphore_signal(
                barrier, inc=1, device_id={"dp": self.dp, "pipe": other}, device_id_type=MESH
            )
        pl.semaphore_wait(barrier, 10)


def remote(src, dst, send, recv, target):
    return pltpu.make_async_remote_copy(
        src_ref=src, dst_ref=dst, send_sem=send, recv_sem=recv, device_id=target, device_id_type=MESH
    )


BIG_HALF = BIG_ROWS // 2
SMALL_HALF = SMALL_ROWS // 2
PARTS = 2
PART_ROWS = BIG_HALF // PARTS
BULK_CUT = 480
LIGHT_CUT = 256
BACK_CUT = 720
GATHER_ORDER = (
    "X1", "Z2", "EY", "EC0", "Z3", "Y0", "X2", "EC1", "X3", "Y1", "Y2", "R0", "EC2", "R1", "EC3",
    "Y3", "Z4", "L0", "X4", "Z5", "L1", "S0", "X5", "Y4", "R2", "S1", "L2", "S2", "Y5", "Z6", "R3",
    "Y6", "X6", "S3", "Z7", "Y7", "M1", "S4", "S5", "D0", "D1", "X7", "R4", "S6", "M2", "D2", "S7",
    "D3", "R5", "R6", "R7", "M3", "D4", "D5", "D6", "D7",
)
REDUCE_ORDER = (
    "A0", "A1", "A2", "A3", "A4", "A5", "L0", "A6", "C0", "B0", "C1", "B1", "C2", "L1", "B2", "B3",
    "L2", "L3", "A7", "C3", "O0", "LS", "B4", "C4", "O1", "E0", "C5", "O2", "E1", "B5", "LE", "I0",
    "I1", "B6", "T1", "I2", "C6", "C7", "B7", "E2", "G", "O3", "O4", "I3", "I4", "O5", "T2", "I5",
    "E3", "E4", "E5", "T3", "O6", "O7",
)


def gather_kernel(big, small, ids, all_big, all_small, table, held_big, held_small, k_sem, big_sem, early, chunk, rising, falling,
                  early_send, early_recv, eu_send, eu_recv, ed_send, ed_recv,
                  z_send, z_recv, x_send, x_recv, y_send, y_recv, dx_send, dx_recv, dy_send, dy_recv,
                  s_send, s_recv, first_send, first_recv, own_sem, id_send, id_recv, lz_send, lz_recv):
    me = Place()
    me.enter()
    x, y, z, core = me.x, me.y, me.z, me.core
    up, down = me.device(z=z + 1), me.device(z=z - 1)
    x_side, y_side, sibling = me.device(x=1 - x), me.device(y=1 - y), me.device(core=1 - core)

    class Stream:
        def __init__(self, n, held, out, start, rows, cut):
            self.n, self.held, self.out, self.start, self.rows, self.cut = n, held, out, start, rows, cut

        def block(self, xo, origin, yo):
            return self.held.at[xo, 2 * origin + yo, pl.ds(self.start, self.rows)]

        def move_x(self, origin):
            block = self.block(x, origin, y)
            return remote(block, block, x_send.at[self.n, origin], x_recv.at[self.n, origin], x_side)

        def move_y(self, origin):
            block = self.block(x, origin, y)
            return remote(block, block, y_send.at[self.n, origin], y_recv.at[self.n, origin], y_side)

        def copies(self, xo, origin, yo):
            block, at = self.block(xo, origin, yo), 8 * xo + 2 * origin + yo
            result = self.out.at[xo, 2 * origin + yo, core, pl.ds(self.start, self.rows)]
            return (
                remote(block, result, s_send.at[self.n, at], s_recv.at[self.n, at], sibling),
                pltpu.make_async_copy(block, result, k_sem.at[self.n, at]),
            )

        def share(self, xo, origin, yo):
            for copy in self.copies(xo, origin, yo):
                copy.start()

        def move_z(self, origin, target, way):
            block = self.block(x, origin, y)
            return remote(block, block, z_send.at[self.n, way, origin], z_recv.at[self.n, origin], target)

        def half_x(self, origin, xo, yo):
            part = self.held.at[xo, 2 * origin + yo, pl.ds(self.start + self.cut, self.rows - self.cut)]
            return remote(part, part, dx_send.at[self.n, origin], dx_recv.at[self.n, origin], x_side)

        def half_y(self, origin, xo, yo):
            part = self.held.at[xo, 2 * origin + yo, pl.ds(self.start, self.cut)]
            return remote(part, part, dy_send.at[self.n, origin], dy_recv.at[self.n, origin], y_side)

        def to_x(self, origin):
            self.move_x(origin).start()

        def to_y(self, origin):
            self.move_y(origin).start()

        def from_x(self, origin):
            self.move_x(origin).wait_recv()
            self.half_y(origin, 1 - x, y).start()
            self.share(1 - x, origin, y)

        def from_y(self, origin):
            self.move_y(origin).wait_recv()
            self.half_x(origin, x, 1 - y).start()
            self.share(x, origin, 1 - y)

        def from_diagonal(self, origin):
            self.half_x(origin, 1 - x, 1 - y).wait_recv()
            self.half_y(origin, 1 - x, 1 - y).wait_recv()
            self.share(1 - x, origin, 1 - y)

        def each(self, step, action):
            if step == 0:
                action(z)
            else:
                pl.when(z >= step)(lambda: action(z - step))
                pl.when(z + step <= 3)(lambda: action(z + step))

        def begin(self):
            pl.when(z < 3)(lambda: self.move_z(z, up, 0).start())
            pl.when(z > 0)(lambda: self.move_z(z, down, 1).start())
            self.share(x, z, y)

        def from_z(self, k):
            @pl.when(z >= k)
            def _():
                self.move_z(z - k, up, 0).wait_recv()
                pl.when(z < 3)(lambda: self.move_z(z - k, up, 0).start())
                self.share(x, z - k, y)

            @pl.when(z + k <= 3)
            def _():
                self.move_z(z + k, down, 1).wait_recv()
                pl.when(z > 0)(lambda: self.move_z(z + k, down, 1).start())
                self.share(x, z + k, y)

        def close(self):
            for origin in range(4):
                self.move_x(origin).wait_send()
                self.move_y(origin).wait_send()
                self.half_x(origin, x, 1 - y).wait_send()
                self.half_y(origin, 1 - x, y).wait_send()
                pl.when((z < 3) & (origin <= z))(lambda: self.move_z(origin, up, 0).wait_send())
                pl.when((z > 0) & (origin >= z))(lambda: self.move_z(origin, down, 1).wait_send())
            self.close_shares()

        def close_shares(self):
            for origin in range(4):
                for xo in range(2):
                    for yo in range(2):
                        away, home = self.copies(xo, origin, yo)
                        away.wait_send()
                        home.wait()
                        theirs = self.out.at[xo, 2 * origin + yo, 1 - core, pl.ds(self.start, self.rows)]
                        at = 8 * xo + 2 * origin + yo
                        remote(theirs, theirs, s_send.at[self.n, at], s_recv.at[self.n, at], sibling).wait_recv()

    class Late(Stream):
        def column_z(self, xo, origin, yo, target, way):
            block = self.block(xo, origin, yo)
            at = 2 * xo + yo
            return remote(
                block, block, lz_send.at[way, at, origin], lz_recv.at[at, origin], target
            )

        def leave(self, xo, yo):
            pl.when(z < 3)(lambda: self.column_z(xo, z, yo, up, 0).start())
            pl.when(z > 0)(lambda: self.column_z(xo, z, yo, down, 1).start())
            self.share(xo, z, yo)

        def step(self, k):
            if k == 0:
                self.move_x(z).start()
                self.move_y(z).start()
                self.leave(x, y)
            elif k == 1:
                self.move_x(z).wait_recv()
                self.half_y(z, 1 - x, y).start()
                self.leave(1 - x, y)
                self.move_y(z).wait_recv()
                self.half_x(z, x, 1 - y).start()
                self.leave(x, 1 - y)
            elif k == 2:
                self.half_x(z, 1 - x, 1 - y).wait_recv()
                self.half_y(z, 1 - x, 1 - y).wait_recv()
                self.leave(1 - x, 1 - y)
            else:
                gap = k - 2

                @pl.when(z >= gap)
                def _():
                    for xo, yo in columns:
                        self.column_z(xo, z - gap, yo, up, 0).wait_recv()
                        pl.when(z < 3)(lambda: self.column_z(xo, z - gap, yo, up, 0).start())
                        self.share(xo, z - gap, yo)

                @pl.when(z + gap <= 3)
                def _():
                    for xo, yo in columns:
                        self.column_z(xo, z + gap, yo, down, 1).wait_recv()
                        pl.when(z > 0)(lambda: self.column_z(xo, z + gap, yo, down, 1).start())
                        self.share(xo, z + gap, yo)

        def close(self):
            self.move_x(z).wait_send()
            self.move_y(z).wait_send()
            self.half_x(z, x, 1 - y).wait_send()
            self.half_y(z, 1 - x, y).wait_send()
            for origin in range(4):
                for xo, yo in columns:
                    pl.when((z < 3) & (origin <= z))(
                        lambda: self.column_z(xo, origin, yo, up, 0).wait_send())
                    pl.when((z > 0) & (origin >= z))(
                        lambda: self.column_z(xo, origin, yo, down, 1).wait_send())
            self.close_shares()

    columns = ((x, y), (1 - x, y), (x, 1 - y), (1 - x, 1 - y))
    bulks = [
        Stream(n, held_big, all_big, PART_ROWS * n, PART_ROWS, BULK_CUT) for n in range(PARTS)
    ]
    light = Late(PARTS, held_small, all_small, 0, SMALL_HALF, LIGHT_CUT)

    order = [
        jnp.where(z < 2, 3, 0),
        jnp.where(z == 0, 2, jnp.where(z == 1, 0, jnp.where(z == 2, 3, 1))),
        jnp.where(z == 0, 1, jnp.where(z == 1, 2, jnp.where(z == 2, 1, 2))),
        z,
    ]

    def cross(k):
        return remote(small.at[2 * order[k] + (1 - y)], early.at[k], early_send.at[k], early_recv.at[k], y_side)

    def own_early(k):
        return pltpu.make_async_copy(small.at[2 * order[k] + y], chunk.at[k], own_sem.at[3 + k])

    def rise(k):
        slot = order[k] - 1
        return remote(chunk.at[k], rising.at[slot], eu_send.at[slot], eu_recv.at[slot], up)

    def fall(k):
        slot = order[k]
        return remote(chunk.at[k], falling.at[slot], ed_send.at[slot], ed_recv.at[slot], down)

    def merge(k, ref, slot):
        @pl.loop(0, 3)
        def _(i):
            part = pl.ds(pl.multiple_of(352 * i, 16), 352)
            chunk[k, part, :] = (chunk[k, part, :].astype(FULL) + ref[slot, part, :].astype(FULL)).astype(LOW)

    def big_part(n):
        return held_big.at[x, me.dp, pl.ds(PART_ROWS * n, PART_ROWS)]

    def big_first(n):
        source = big.at[pl.ds(BIG_HALF + PART_ROWS * n, PART_ROWS)]
        return remote(source, big_part(n), first_send.at[n], first_recv.at[n], sibling)

    def big_own(n):
        return pltpu.make_async_copy(big.at[pl.ds(PART_ROWS * n, PART_ROWS)], big_part(n), big_sem.at[n])

    small_half = held_small.at[x, me.dp]
    small_first = remote(
        chunk.at[3, pl.ds(0, SMALL_HALF)], small_half, first_send.at[PARTS], first_recv.at[PARTS], sibling)

    def early_cross():
        @pl.when(core == 1)
        def _():
            for k in range(4):
                own_early(k).wait()
                cross(k).wait_recv()
                merge(k, early, k)

    def early_chain(k):
        @pl.when(core == 1)
        def _():
            if k < 3:

                @pl.when(order[k] > z)
                def _():
                    @pl.when(z > 0)
                    def _():
                        rise(k).wait_recv()
                        merge(k, rising, order[k] - 1)

                    rise(k).start()

                @pl.when(order[k] < z)
                def _():
                    @pl.when(z < 3)
                    def _():
                        fall(k).wait_recv()
                        merge(k, falling, order[k])

                    fall(k).start()

            else:

                @pl.when(z > 0)
                def _():
                    rise(k).wait_recv()
                    merge(k, rising, z - 1)

                @pl.when(z < 3)
                def _():
                    fall(k).wait_recv()
                    merge(k, falling, z)

                small_first.start()
                copy = pltpu.make_async_copy(
                    chunk.at[3, pl.ds(SMALL_HALF, SMALL_HALF)], small_half, own_sem.at[0])
                copy.start()
                copy.wait()

    def light_begin():
        @pl.when(core == 0)
        def _():
            small_first.wait_recv()

        light.step(0)

    @pl.when(core == 0)
    def _():
        for n in range(PARTS):
            big_first(n).start()
            big_own(n).start()

    @pl.when(core == 1)
    def _():
        for k in range(4):
            cross(k).start()
            own_early(k).start()

    for n in range(PARTS):
        pl.when(core == 0)(lambda: big_own(n).wait())
        pl.when(core == 1)(lambda: big_first(n).wait_recv())
        bulks[n].begin()
        if n == 0:
            bulks[n].to_x(z)
    row = pltpu.make_async_copy(ids, table.at[me.pipe], own_sem.at[2])
    row.start()
    for step in range(1, 4):
        remote(
            ids, table.at[me.pipe], id_send.at[step], id_recv.at[step],
            {"dp": me.dp, "pipe": lax.rem(me.pipe + step, 4)},
        ).start()

    actions = {"EY": early_cross, "L0": light_begin}
    for k in range(4):
        actions["EC%d" % k] = functools.partial(early_chain, k)
        if k:
            actions["M%d" % k] = functools.partial(light.step, k + 2)
            if k < 3:
                actions["L%d" % k] = functools.partial(light.step, k)
        for n, bulk in enumerate(bulks):
            name = str(PARTS * k + n)
            for letter, action in zip("XYSRD", (bulk.to_x, bulk.to_y, bulk.from_x, bulk.from_y, bulk.from_diagonal)):
                actions[letter + name] = functools.partial(bulk.each, k, action)
            if k:
                actions["Z" + name] = functools.partial(bulk.from_z, k)
    for event in GATHER_ORDER:
        actions[event]()
    for bulk in bulks:
        bulk.close()
    light.close()
    row.wait()
    for step in range(1, 4):
        here = lax.rem(me.pipe + 4 - step, 4)
        move = remote(
            ids, table.at[here], id_send.at[step], id_recv.at[step],
            {"dp": me.dp, "pipe": lax.rem(me.pipe + step, 4)},
        )
        move.wait_recv()
        move.wait_send()

    @pl.when(core == 0)
    def _():
        for n in range(PARTS):
            big_first(n).wait_send()

    @pl.when(core == 1)
    def _():
        small_first.wait_send()
        for k in range(4):
            cross(k).wait_send()
        for k in range(3):
            pl.when(order[k] > z)(lambda: rise(k).wait_send())
            pl.when(order[k] < z)(lambda: fall(k).wait_send())


def gather_all(big, small, ids):
    sem = pltpu.SemaphoreType.DMA
    return pl.pallas_call(
        gather_kernel,
        name="gather_all",
        out_shape=(
            jax.ShapeDtypeStruct((2, 8, 2, BIG_HALF, 128), LOW),
            jax.ShapeDtypeStruct((2, 8, 2, SMALL_HALF, 128), LOW),
            jax.ShapeDtypeStruct((4, 8, 128), jnp.int32),
        ),
        in_specs=[any_spec()] * 3,
        out_specs=(any_spec(),) * 3,
        scratch_shapes=[
            pltpu.VMEM((2, 8, BIG_HALF, 128), LOW), pltpu.VMEM((2, 8, SMALL_HALF, 128), LOW),
            sem((PARTS + 1, 16)), sem((PARTS,)),
            pltpu.VMEM((4, SMALL_ROWS, 128), LOW), pltpu.VMEM((4, SMALL_ROWS, 128), LOW),
            pltpu.VMEM((3, SMALL_ROWS, 128), LOW), pltpu.VMEM((3, SMALL_ROWS, 128), LOW),
            sem((4,)), sem((4,)), sem((3,)), sem((3,)), sem((3,)), sem((3,)),
            sem((PARTS + 1, 2, 4)), sem((PARTS + 1, 4)),
            sem((PARTS + 1, 4)), sem((PARTS + 1, 4)), sem((PARTS + 1, 4)), sem((PARTS + 1, 4)),
            sem((PARTS + 1, 4)), sem((PARTS + 1, 4)), sem((PARTS + 1, 4)), sem((PARTS + 1, 4)),
            sem((PARTS + 1, 16)), sem((PARTS + 1, 16)),
            sem((PARTS + 1,)), sem((PARTS + 1,)), sem((7,)), sem((4,)), sem((4,)),
            sem((2, 4, 4)), sem((4, 4)),
        ],
        compiler_params=pltpu.CompilerParams(
            collective_id=0, has_side_effects=True, vmem_limit_bytes=60 << 20
        ),
    )(big, small.reshape(8, SMALL_ROWS, 128), ids)


def soft(value):
    return jnp.maximum(value, 0.0) + jnp.log1p(jnp.exp(-jnp.abs(value)))


def gate_of(value):
    small = jnp.exp(-jnp.abs(value))
    share = 1.0 / (1.0 + small)
    return jnp.where(value >= 0, share, small * share)


def standardize(z):
    count = z.shape[0]
    centre = jnp.sum(z, axis=0, keepdims=True) / count
    away = z - centre
    spread = jnp.sum(away * away, axis=0, keepdims=True) / count
    inverse = lax.rsqrt(spread + NORM_EPS)
    return away * inverse, centre, spread, inverse


def unstandardize(grad, standard, gain, inverse):
    count = grad.shape[0]
    grad_sum = jnp.sum(grad, axis=0, keepdims=True)
    grad_dot = jnp.sum(grad * standard, axis=0, keepdims=True)
    result = gain * inverse * (grad - grad_sum / count - standard * (grad_dot / count))
    return result, grad_dot, grad_sum


def pad_low(value):
    zeros = jnp.zeros((PADDED - ROWS, value.shape[1]), FULL)
    return jnp.concatenate([value, zeros], axis=0).astype(LOW)


def mul(a, b):
    return jnp.dot(a, b, preferred_element_type=FULL)


def mul_t(a, b):
    return lax.dot_general(a, b, (((1,), (1,)), ((), ())), preferred_element_type=FULL)


def narrow_part(ref, start, count, blocks=range(4)):
    return jnp.concatenate(
        [ref[pl.ds(start, count), 64 * j : 64 * j + 64, :].reshape(64 * count, 128) for j in blocks],
        axis=1,
    )


def put_narrow(ref, start, count, value):
    for j in range(4):
        ref[pl.ds(start, count), 64 * j : 64 * j + 64, :] = (
            value[:, 128 * j : 128 * j + 128].astype(LOW).reshape(count, 64, 128)
        )


def wide_part(ref, start, count, c):
    return jnp.concatenate(
        [
            ref[start : start + count, 32 * c + 16 * h : 32 * c + 16 * h + 16, :].reshape(
                16 * count, 128
            )
            for h in range(2)
        ],
        axis=1,
    )


def put_wide(ref, start, count, c, value):
    for h in range(2):
        ref[start : start + count, 32 * c + 16 * h : 32 * c + 16 * h + 16, :] = (
            value[:, 128 * h : 128 * h + 128].astype(LOW).reshape(count, 16, 128)
        )


def chunks(count):
    def run(body):
        for c in range(count):
            body(c)

    return run


def step_kernel(table, gates, teach_ids, stud_ids, all_big, all_small, x, targets, grid,
                wide0, wide1, final, stats, grad_x, out_big, out_small,
                w0, w1, w2, w3, edges, loose, vec, grad_vec, raw,
                std_a, std_b, std_p, std_1, std_c, std_d, hidden, cols0, cols2,
                nar0, nar2, turned, turned_x, relay, dz_a, dz_n, acc, acc_x, grad_h,
                wanted, inv, in_sem, edge_sem, out_sem):
    rank = lax.axis_index("pipe")
    gate = gates[rank].astype(FULL)
    for group in range(2):
        for j in range(8):
            inv[8 * group + table[2 * group, 0, j]] = j
    picks = [teach_ids[k, rank] for k in range(2)] + [stud_ids[rank, k] for k in range(3)]
    rows = [
        pltpu.make_async_copy(targets.at[pl.ds(pick, 1)], wanted.at[pl.ds(k, 1)], edge_sem.at[12 + k])
        for k, pick in enumerate(picks)
    ]
    for fetched in rows:
        fetched.start()
    weights = (w0, w1, w2, w3)
    loads = {0: [], 1: [], 2: [], 3: []}
    front, split = w0.reshape(USED_TILES[0] * TILE, 128), w2.reshape(115 * TILE, 128)
    for group, weight, blocks in ((0, front, 8), (1, split, 6)):
        for b in range(blocks):
            at, here = 8 * group + b, inv[8 * group + b]
            count = min(STRIDE, VEC_TILE[2 * group] + 1 - STRIDE * b) * TILE
            loads[2 * group].append(pltpu.make_async_copy(
                all_big.at[group, here, pl.ds(0, count)], weight.at[pl.ds(STRIDE * TILE * b, count)],
                in_sem.at[0, at]))
            if b < blocks - 1:
                loads[2 * group].append(pltpu.make_async_copy(
                    all_big.at[group, here, pl.ds(STRIDE * TILE, EDGE)], edges.at[7 * group + b],
                    edge_sem.at[7 * group + b]))
            elif group == 0:
                loads[0].append(pltpu.make_async_copy(
                    all_big.at[0, here, pl.ds(STRIDE * TILE, EDGE)],
                    front.at[pl.ds(VEC_TILE[0] * TILE, EDGE)], edge_sem.at[17]))
    loads[1].append(pltpu.make_async_copy(all_small.at[0], w1, in_sem.at[0, 14]))
    loads[3].append(pltpu.make_async_copy(all_small.at[1], w3, in_sem.at[0, 15]))
    for section in range(4):
        for load in loads[section]:
            load.start()

    raw[...] = jnp.zeros_like(raw)
    loose[...] = jnp.zeros_like(loose)
    grad_vec[...] = jnp.zeros_like(grad_vec)

    def edge_parts(tile, is_narrow):
        count, size = (4, 64) if is_narrow else (16, 16)
        for j in range(count):
            yield pl.ds(j, 16, count), slice(size * j, size * j + 16)

    def is_narrow(section, tile):
        return section == 2 or tile < FRONT_WIDE

    def merge_edge(section, tile, at):
        ref = weights[section]
        loose[0:EDGE, :] = edges[at].astype(FULL)
        for lying, here in edge_parts(tile, is_narrow(section, tile)):
            ref[tile, here, :] = (ref[tile, here, :].astype(FULL) + loose[lying, :]).astype(LOW)

    def take_edge(section, tile, at):
        ref = weights[section]
        for lying, here in edge_parts(tile, is_narrow(section, tile)):
            loose[lying, :] = ref[tile, here, :].astype(FULL)
        edges[at] = loose[0:EDGE, :].astype(LOW)

    def settle(section, blocks=None):
        if section == 0:
            for b in blocks:
                for load in loads[0][2 * b : 2 * b + 2]:
                    load.wait()
            if 7 in blocks:
                vec[0] = w0[VEC_TILE[0], 0:48, :].astype(FULL)
            else:
                for b in range(7):
                    merge_edge(0, 19 * b + 19, b)
            return
        for load in loads[section]:
            load.wait()
        if section == 2:
            for b in range(5):
                merge_edge(2, 19 * b + 19, 7 + b)
        vec[section] = weights[section][VEC_TILE[section], 0:48, :].astype(FULL)

    def row(section, start):
        return jnp.concatenate(
            [vec[section, pl.ds(start + h, 1), :] for h in range(2)], axis=1
        )

    def put_row(section, start, value):
        for h in range(2):
            grad_vec[section, pl.ds(start + h, 1), :] = value[:, 128 * h : 128 * h + 128]

    def put_stats(section, column, centre, spread):
        raw[2 * section : 2 * section + 1, pl.ds(column, 256)] = centre
        raw[2 * section + 1 : 2 * section + 2, pl.ds(column, 256)] = spread

    def inverse_of(section, column):
        return lax.rsqrt(raw[2 * section + 1 : 2 * section + 2, pl.ds(column, 256)] + NORM_EPS)

    def lanes(c):
        return slice(256 * c, 256 * c + 256)

    at_row, at_col, side = grid[0], grid[1], grid[2]

    def masked(value, dr, dc):
        ok = (at_row + dr >= 0) & (at_row + dr < side) & (at_col + dc >= 0) & (at_col + dc < side)
        return jnp.concatenate(
            [jnp.where(ok, value[:, 128 * j : 128 * j + 128], 0.0) for j in range(4)], axis=1
        )

    def rolled(value, sign, dr, dc):
        parts = []
        for start, end, across, down in ((0, STUD_ROWS, 1, 4), (STUD_ROWS, ROWS, 2, 12)):
            by = (sign * (dr * down + dc * across)) % (end - start)
            part = value[start:end]
            parts.append(part if by == 0 else pltpu.roll(part, by, 0))
        return jnp.concatenate(parts, axis=0)

    def taps(stride):
        for t in range(9):
            r, q = t // 3, t % 3
            if stride == 1:
                yield t, 0, r - 1, q - 1
            else:
                phase = 2 * (1 if r != 1 else 0) + (1 if q != 1 else 0)
                yield t, phase, -1 if r == 0 else 0, -1 if q == 0 else 0

    settle(0, (0, 7))
    whole_x = x[...].reshape(4 * PADDED, C_IN)
    for c in range(2):
        z = mul(whole_x, narrow_part(w0, 0, 16, (2 * c, 2 * c + 1)))
        z = jnp.concatenate([z[PADDED * p : PADDED * p + ROWS] for p in range(4)], axis=0)
        standard, centre, spread, _ = standardize(z)
        put_stats(0, 256 * c, centre, spread)
        std_a[:, 256 * c : 256 * c + 256] = standard
        hidden[:, 256 * c : 256 * c + 256] = (
            soft(row(0, 2 * c) * standard + row(0, 4 + 2 * c)).astype(LOW).astype(FULL)
        )

    for t, phase, dr, dc in taps(2):
        cols0[t] = pad_low(masked(rolled(hidden[ROWS * phase : ROWS * phase + ROWS, :], -1, dr, dc), dr, dc))
    acc[...] = jnp.zeros_like(acc)
    settle(0, (1, 2, 3, 4, 5, 6))

    @chunks(9)
    def _(t):
        acc[...] += mul(cols0[t], narrow_part(w0, 16 + 8 * t, 8))

    def middle(section, std, nar):
        for c in range(2):
            at = slice(256 * c, 256 * c + 256)
            standard, centre, spread, _ = standardize(acc[0:ROWS, at])
            put_stats(section, MID + 256 * c, centre, spread)
            std[:, at] = standard
            nar[:, at] = pad_low(soft(row(section, 8 + 2 * c) * standard + row(section, 12 + 2 * c)))

    middle(0, std_b, nar0)
    acc[...] = jnp.zeros_like(acc)
    settle(1)
    settle(2)

    @chunks(8)
    def _(c):
        at = lanes(c)
        standard, centre, spread, _ = standardize(mul(x[0], wide_part(w0, FRONT_WIDE, 64, c))[0:ROWS])
        put_stats(0, 2 * MID + 256 * c, centre, spread)
        std_p[:, at] = standard
        low = pad_low(row(0, 16 + 2 * c) * standard + row(0, 32 + 2 * c))
        wide0[:, at] = low
        standard, centre, spread, _ = standardize(mul(nar0[...], wide_part(w1, 0, 32, c))[0:ROWS])
        put_stats(1, 256 * c, centre, spread)
        std_1[:, at] = standard
        pre = low.astype(FULL)[0:ROWS] + row(1, 2 * c) * standard + row(1, 16 + 2 * c)
        low = pad_low(soft(pre))
        wide1[:, at] = low
        acc[...] += mul(low, narrow_part(w2, 4 * c, 4))

    for c in range(2):
        at = slice(256 * c, 256 * c + 256)
        standard, centre, spread, _ = standardize(acc[0:ROWS, at])
        put_stats(2, 256 * c, centre, spread)
        std_c[:, at] = standard
        hidden[0:ROWS, at] = soft(row(2, 2 * c) * standard + row(2, 4 + 2 * c)).astype(LOW).astype(FULL)
    for t, phase, dr, dc in taps(1):
        cols2[t] = pad_low(masked(rolled(hidden[0:ROWS, :], -1, dr, dc), dr, dc))
    acc[...] = jnp.zeros_like(acc)

    @chunks(9)
    def _(t):
        acc[...] += mul(cols2[t], narrow_part(w2, 32 + 8 * t, 8))

    middle(2, std_d, nar2)

    turned[...] = nar2[...].T
    acc[...] = jnp.zeros_like(acc)
    settle(3)
    for fetched in rows:
        fetched.wait()

    teach_rows = ROWS - STUD_ROWS
    first_crop = lax.rem(lax.broadcasted_iota(jnp.int32, (teach_rows, 256), 0), 2) == 0

    def spread_rows(values):
        first, second = (jnp.broadcast_to(value, (teach_rows, 256)) for value in values[0:2])
        parts = [jnp.broadcast_to(value, (16, 256)) for value in values[2:5]]
        parts.append(jnp.where(first_crop, first, second))
        return jnp.concatenate(parts, axis=0)

    def crop_sums(value):
        def total(part):
            return jnp.sum(part, axis=0, keepdims=True)

        teach = value[STUD_ROWS:ROWS]
        return [
            total(jnp.where(first_crop, teach, 0.0)),
            total(jnp.where(first_crop, 0.0, teach)),
            total(value[0:16]),
            total(value[16:32]),
            total(value[32:48]),
        ]

    @chunks(8)
    def _(c):
        at = lanes(c)
        weight = wide_part(w3, 0, 32, c)
        standard, centre, spread, inverse = standardize(mul(nar2[...], weight)[0:ROWS])
        put_stats(3, 256 * c, centre, spread)
        gain = row(3, 2 * c)
        before = wide1[:, at].astype(FULL)[0:ROWS]
        pre = before + gain * standard + row(3, 16 + 2 * c)
        ending = jnp.where(gate > 0, soft(pre), before)
        final[:, at] = pad_low(ending)
        square = ending * ending
        factors = []
        for crop, total in enumerate(crop_sums(square * ending)):
            mean = total / (36.0 if crop < 2 else 16.0) + POOL_EPS
            factors.append(jnp.exp(jnp.log(mean) * (-2.0 / 3.0)) * wanted[crop : crop + 1, at])
        cotangent = spread_rows(factors) * square
        grad_pre = cotangent * gate_of(pre) * gate
        relay[:, at] = pad_low(grad_pre + cotangent * (1.0 - gate))
        result, grad_gain, grad_bias = unstandardize(grad_pre, standard, gain, inverse)
        put_row(3, 2 * c, grad_gain)
        put_row(3, 16 + 2 * c, grad_bias)
        low = pad_low(result)
        acc[...] += mul_t(low, weight)
        put_wide(w3, 0, 32, c, mul(turned[...], low))

    def flush(section):
        weights[section][VEC_TILE[section]] = grad_vec[section].astype(LOW)

    flush(3)
    stores = [pltpu.make_async_copy(w3, out_small.at[1], out_sem.at[16])]
    stores[-1].start()

    def middle_back(section, std):
        for c in range(2):
            at = slice(256 * c, 256 * c + 256)
            gain, bias = row(section, 8 + 2 * c), row(section, 12 + 2 * c)
            grad = acc[0:ROWS, at].astype(LOW).astype(FULL) * gate_of(gain * std[:, at] + bias)
            result, grad_gain, grad_bias = unstandardize(
                grad, std[:, at], gain, inverse_of(section, MID + 256 * c)
            )
            put_row(section, 8 + 2 * c, grad_gain)
            put_row(section, 12 + 2 * c, grad_bias)
            dz_n[:, at] = pad_low(result)

    def taps_back(weight, start, cols, stride, phases):
        grad_h[0 : ROWS * phases, :] = jnp.zeros((ROWS * phases, MID), FULL)
        for t, phase, dr, dc in taps(stride):
            part = mul_t(dz_n[...], narrow_part(weight, start + 8 * t, 8))[0:ROWS]
            at = slice(ROWS * phase, ROWS * phase + ROWS)
            grad_h[at, :] += rolled(masked(part, dr, dc), 1, dr, dc)
            put_narrow(weight, start + 8 * t, 8, mul(cols[t].T, dz_n[...]))

    middle_back(2, std_d)
    taps_back(w2, 32, cols2, 1, 1)
    for c in range(2):
        at = slice(256 * c, 256 * c + 256)
        gain, bias = row(2, 2 * c), row(2, 4 + 2 * c)
        grad = grad_h[0:ROWS, at] * gate_of(gain * std_c[:, at] + bias)
        result, grad_gain, grad_bias = unstandardize(grad, std_c[:, at], gain, inverse_of(2, 256 * c))
        put_row(2, 2 * c, grad_gain)
        put_row(2, 4 + 2 * c, grad_bias)
        dz_n[:, at] = pad_low(result)
    turned[...] = nar0[...].T
    turned_x[...] = x[0].T
    acc[...] = jnp.zeros_like(acc)
    acc_x[...] = jnp.zeros_like(acc_x)

    @chunks(8)
    def _(c):
        at = lanes(c)
        low = dz_n[...]
        grad = relay[:, at].astype(FULL) + mul_t(low, narrow_part(w2, 4 * c, 4))
        put_narrow(w2, 4 * c, 4, mul(wide1[:, at].T, low))
        grad = grad.astype(LOW).astype(FULL)[0:ROWS]
        gain = row(1, 2 * c)
        pre = wide0[:, at].astype(FULL)[0:ROWS] + gain * std_1[:, at] + row(1, 16 + 2 * c)
        grad = grad * gate_of(pre)
        result, grad_gain, grad_bias = unstandardize(
            grad, std_1[:, at], gain, inverse_of(1, 256 * c)
        )
        put_row(1, 2 * c, grad_gain)
        put_row(1, 16 + 2 * c, grad_bias)
        low = pad_low(result)
        acc[...] += mul_t(low, wide_part(w1, 0, 32, c))
        put_wide(w1, 0, 32, c, mul(turned[...], low))
        grad = grad.astype(LOW).astype(FULL)
        result, grad_gain, grad_bias = unstandardize(
            grad, std_p[:, at], row(0, 16 + 2 * c), inverse_of(0, 2 * MID + 256 * c)
        )
        put_row(0, 16 + 2 * c, grad_gain)
        put_row(0, 32 + 2 * c, grad_bias)
        low = pad_low(result)
        acc_x[...] += mul_t(low, wide_part(w0, FRONT_WIDE, 64, c))
        put_wide(w0, FRONT_WIDE, 64, c, mul(turned_x[...], low))

    flush(1)
    flush(2)
    w2[105:115] = jnp.zeros((10, TILE, 128), LOW)
    stores.append(pltpu.make_async_copy(w1, out_small.at[0], out_sem.at[17]))
    stores[-1].start()
    def store(source, group, b, start, semaphore):
        count = source.shape[0]
        stores.append(pltpu.make_async_copy(
            source, out_big.at[group, inv[8 * group + b], pl.ds(start, count)], out_sem.at[semaphore]))
        stores[-1].start()

    for b in range(8):
        if b < 5:
            take_edge(2, 19 * b + 19, 7 + b)
            store(split.at[pl.ds(STRIDE * TILE * b, STRIDE * TILE)], 1, b, 0, 8 + b)
            store(edges.at[7 + b], 1, b, STRIDE * TILE, 20 + b)
        else:
            first = 95 if b == 5 else 105
            store(split.at[pl.ds(TILE * first, 10 * TILE)], 1, b, 0, 8 + b)
            store(split.at[pl.ds(TILE * 105, BIG_ROWS - 10 * TILE)], 1, b, 10 * TILE, 20 + b)

    def store_front(blocks):
        for b in blocks:
            if b == 7:
                edges[12] = w0[VEC_TILE[0], 0:EDGE, :]
            else:
                take_edge(0, 19 * b + 19, b)
            store(front.at[pl.ds(STRIDE * TILE * b, STRIDE * TILE)], 0, b, 0, b)
            store(edges.at[12 if b == 7 else b], 0, b, STRIDE * TILE, 28 + b)

    store_front((5, 6))
    middle_back(0, std_b)
    taps_back(w0, 16, cols0, 2, 4)
    store_front((1, 2, 3, 4))
    for c in range(2):
        at = slice(256 * c, 256 * c + 256)
        gain, bias = row(0, 2 * c), row(0, 4 + 2 * c)
        grad = grad_h[:, at] * gate_of(gain * std_a[:, at] + bias)
        result, grad_gain, grad_bias = unstandardize(grad, std_a[:, at], gain, inverse_of(0, 256 * c))
        put_row(0, 2 * c, grad_gain)
        put_row(0, 4 + 2 * c, grad_bias)
        for p in range(4):
            dz_a[PADDED * p : PADDED * p + PADDED, at] = pad_low(result[ROWS * p : ROWS * p + ROWS])

    @chunks(4)
    def _(c):
        at = lanes(c)
        low = dz_a[...]
        part = mul_t(low, narrow_part(w0, 4 * c, 4))
        grad_x[0, :, at] = (part[0:PADDED] + acc_x[:, at]).astype(LOW)
        for p in range(1, 4):
            grad_x[p, :, at] = part[PADDED * p : PADDED * p + PADDED].astype(LOW)
        put_narrow(w0, 4 * c, 4, mul(x[:, :, at].reshape(4 * PADDED, 256).T, low))

    flush(0)
    store_front((0, 7))
    for section in range(4):
        part = raw[2 * section : 2 * section + 2]
        stats[section, 0:2] = part if section < 2 else part * gate
        stats[section, 2:8] = jnp.zeros((6, 2 * MID + C_OUT), FULL)
    for store in stores:
        store.wait()


def run_step(table, gates, teach_ids, stud_ids, all_big, all_small, phases, targets):
    spots = np.zeros((3, ROWS, 128), np.int32)
    for r in range(ROWS):
        width = 4 if r < STUD_ROWS else 6
        at = r % 16 if r < STUD_ROWS else (r - STUD_ROWS) // 2
        spots[0, r], spots[1, r], spots[2, r] = at // width, at % width, width
    sem = pltpu.SemaphoreType.DMA
    wide = jax.ShapeDtypeStruct((PADDED, C_OUT), LOW)
    vm = pltpu.VMEM
    return pl.pallas_call(
        step_kernel,
        name="step",
        out_shape=(
            wide, wide, wide,
            jax.ShapeDtypeStruct((4, 8, 2 * MID + C_OUT), FULL),
            jax.ShapeDtypeStruct((4, PADDED, C_IN), LOW),
            jax.ShapeDtypeStruct((2, 8, BIG_ROWS, 128), LOW),
            jax.ShapeDtypeStruct((2, USED_TILES[1], TILE, 128), LOW),
        ),
        in_specs=[smem_spec()] * 4 + [any_spec(), any_spec(), vmem_spec(), any_spec(), vmem_spec()],
        out_specs=(vmem_spec(),) * 5 + (any_spec(),) * 2,
        scratch_shapes=[
            vm((153, TILE, 128), LOW), vm((33, TILE, 128), LOW), vm((115, TILE, 128), LOW), vm((33, TILE, 128), LOW),
            vm((13, EDGE, 128), LOW), vm((TILE, 128), FULL), vm((4, 48, 128), FULL), vm((4, TILE, 128), FULL),
            vm((8, 2 * MID + C_OUT), FULL),
            vm((4 * ROWS, MID), FULL), vm((ROWS, MID), FULL), vm((ROWS, C_OUT), FULL), vm((ROWS, C_OUT), FULL),
            vm((ROWS, MID), FULL), vm((ROWS, MID), FULL), vm((4 * ROWS, MID), FULL),
            vm((9, PADDED, MID), LOW), vm((9, PADDED, MID), LOW),
            vm((PADDED, MID), LOW), vm((PADDED, MID), LOW), vm((MID, PADDED), LOW), vm((C_IN, PADDED), LOW),
            vm((PADDED, C_OUT), LOW), vm((4 * PADDED, MID), LOW), vm((PADDED, MID), LOW),
            vm((PADDED, MID), FULL), vm((PADDED, C_IN), FULL), vm((4 * ROWS, MID), FULL),
            vm((8, C_OUT), FULL), pltpu.SMEM((16,), jnp.int32),
            sem((2, 16)), sem((18,)), sem((36,)),
        ],
        compiler_params=pltpu.CompilerParams(vmem_limit_bytes=60 << 20),
    )(table, gates, teach_ids, stud_ids, all_big, all_small, phases, targets, jnp.asarray(spots))


def reduce_kernel(big, small, wide0, wide1, final, stats, table,
                  out_big, out_small, seg_stud, seg_teach, out_stats, norm, factor,
                  got, halves_x, halves_y, from_x, from_y, from_low, from_high, stage, total,
                  l_got, l_stage, l_low, l_high, l_halves_x, l_halves_y, l_from_x, l_from_y, l_total,
                  late, late_half, owner_row, by_pipe, by_dp, mine, part_sum,
                  s_send, s_recv, ls_send, ls_recv, hx_send, hx_recv, hy_send, hy_recv, x_send, x_recv, y_send, y_recv,
                  zu_send, zu_recv, zd_send, zd_recv, lu_send, lu_recv, ld_send, ld_recv,
                  stage_sem, l_stage_sem, out_sem, big_sem, late_send, late_recv, join_send, join_recv,
                  seg_send, seg_recv, stat_send, stat_recv, p_send, p_recv, d_send, d_recv):
    me = Place()
    me.enter()
    x, y, z, core = me.x, me.y, me.z, me.core
    up, down = me.device(z=z + 1), me.device(z=z - 1)
    x_side, y_side, sibling = me.device(x=1 - x), me.device(y=1 - y), me.device(core=1 - core)
    order = [
        jnp.where(z < 2, 3, 0),
        jnp.where(z == 0, 2, jnp.where(z == 1, 0, jnp.where(z == 2, 3, 1))),
        jnp.where(z == 0, 1, jnp.where(z == 1, 2, jnp.where(z == 2, 1, 2))),
        z,
    ]
    columns = ((1 - x, 1 - y), (x, 1 - y), (1 - x, y), (x, y))
    groups = {"A": (0,), "C": (1,), "B": (2,), "O": (3,)}
    sequence = [
        (group, int(event[1])) for event in REDUCE_ORDER for group in groups.get(event[0], ())
    ]
    l_sequence = [(group, k) for k in range(4) for group in range(4)]

    def all_of(copies, act):
        for copy in copies:
            act(copy)

    def over(start, count, piece):
        whole = count // 512
        if whole:

            @pl.loop(0, whole)
            def _(i):
                piece(pl.multiple_of(start + 512 * i, 16), 512)

        if count % 512:
            piece(start + 512 * whole, count % 512)

    items = 4 * PARTS

    def source(group, q, half):
        xo, yo = columns[group]
        part = pl.ds(PART_ROWS * (q % PARTS), PART_ROWS)
        return big.at[xo, 2 * order[q // PARTS] + yo, half, part]

    def l_source(group, k, half):
        xo, yo = columns[group]
        return small.at[xo, 2 * order[k] + yo, half]

    def share(group, q):
        at = items * group + q
        return remote(source(group, q, 1 - core), got.at[at], s_send.at[at], s_recv.at[at], sibling)

    def l_share(group, k):
        at = 4 * group + k
        return remote(l_source(group, k, 1 - core), l_got.at[at], ls_send.at[at], ls_recv.at[at], sibling)

    def fetch(n):
        return pltpu.make_async_copy(source(*sequence[n], core), stage.at[n % 4], stage_sem.at[n % 4])

    def l_fetch(group, k):
        at = 4 * group + k
        return pltpu.make_async_copy(l_source(group, k, core), l_stage.at[at], l_stage_sem.at[at])

    def add(target, at, other, slot, start, count, extras):
        def piece(begin, size):
            part = pl.ds(begin, size)
            sums = target[at, part, :].astype(FULL) + other[slot, part, :].astype(FULL)
            for ref, k in extras:
                sums = sums + ref[k, pl.ds(begin - start, size), :].astype(FULL)
            target[at, part, :] = sums.astype(LOW)

        over(start, count, piece)

    def send_half_x(k):
        return remote(got.at[k, pl.ds(BACK_CUT, PART_ROWS - BACK_CUT)], halves_x.at[k],
                      hx_send.at[k], hx_recv.at[k], x_side)

    def send_half_y(k):
        return remote(got.at[k, pl.ds(0, BACK_CUT)], halves_y.at[k], hy_send.at[k], hy_recv.at[k], y_side)

    def send_y(k):
        return remote(got.at[items + k], from_y.at[k], y_send.at[k], y_recv.at[k], y_side)

    def send_x(k):
        return remote(got.at[2 * items + k], from_x.at[k], x_send.at[k], x_recv.at[k], x_side)

    def low_slot(q):
        return PARTS * (order[q // PARTS] - 1) + q % PARTS

    def high_slot(q):
        return PARTS * order[q // PARTS] + q % PARTS

    def send_up(q):
        slot = low_slot(q)
        return remote(got.at[3 * items + q], from_low.at[slot], zu_send.at[slot], zu_recv.at[slot], up)

    def send_down(q):
        slot = high_slot(q)
        return remote(got.at[3 * items + q], from_high.at[slot], zd_send.at[slot], zd_recv.at[slot], down)

    def l_column(group):
        xo, yo = columns[group]
        return 2 * xo + yo

    def l_up(group, k):
        at, zd = l_column(group), order[k] - 1
        return remote(l_got.at[4 * group + k], l_low.at[at, zd], lu_send.at[at, zd], lu_recv.at[at, zd], up)

    def l_down(group, k):
        at, zd = l_column(group), order[k]
        return remote(l_got.at[4 * group + k], l_high.at[at, zd], ld_send.at[at, zd], ld_recv.at[at, zd], down)

    def l_half_x():
        return remote(l_got.at[3, pl.ds(LIGHT_CUT, SMALL_HALF - LIGHT_CUT)], l_halves_x,
                      hx_send.at[items], hx_recv.at[items], x_side)

    def l_half_y():
        return remote(l_got.at[3, pl.ds(0, LIGHT_CUT)], l_halves_y, hy_send.at[items], hy_recv.at[items], y_side)

    def l_send_y():
        return remote(l_got.at[7], l_from_y, y_send.at[items], y_recv.at[items], y_side)

    def l_send_x():
        return remote(l_got.at[11], l_from_x, x_send.at[items], x_recv.at[items], x_side)

    leaving = (wide0, wide1, wide1, final)

    def pairs(section, micro):
        source = leaving[section]
        yield source.at[pl.ds(0, STUD_ROWS)], seg_stud.at[micro], seg_send.at[0, section], seg_recv.at[0, micro]
        yield source.at[pl.ds(STUD_ROWS, TEACH_END)], seg_teach.at[micro], seg_send.at[1, section], seg_recv.at[1, micro]
        yield stats.at[section], out_stats.at[micro], stat_send.at[section], stat_recv.at[micro]

    def exchange(section):
        return [remote(*pair, {"dp": me.dp, "pipe": section}) for pair in pairs(section, me.pipe)]

    def keep(section):
        return [pltpu.make_async_copy(src, dst, send) for src, dst, send, _ in pairs(section, me.pipe)]

    def arriving(micro):
        return [remote(*pair, {"dp": me.dp, "pipe": micro}) for pair in pairs(micro, micro)]

    for n in range(4 * items):
        share(*sequence[n]).start()
        if n == 5:
            for item in l_sequence:
                l_share(*item).start()
    for n in range(2):
        fetch(n).start()
    for group, k in l_sequence:
        l_fetch(group, k).start()
    row_copy = pltpu.make_async_copy(table.at[2 * x], owner_row, out_sem.at[2])
    row_copy.start()

    def bulk_item(n):
        group, k = sequence[n]
        at, slot = items * group + k, n % 4
        if n + 2 < 4 * items:
            fetch(n + 2).start()
        fetch(n).wait()
        share(group, k).wait_recv()
        if group == 0:
            add(got, at, stage, slot, 0, PART_ROWS, [])
            send_half_x(k).start()
            send_half_y(k).start()
        elif group == 1:
            send_half_x(k).wait_recv()
            add(got, at, stage, slot, 0, BACK_CUT, [])
            add(got, at, stage, slot, BACK_CUT, PART_ROWS - BACK_CUT, [(halves_x, k)])
            send_y(k).start()
        elif group == 2:
            send_half_y(k).wait_recv()
            add(got, at, stage, slot, 0, BACK_CUT, [(halves_y, k)])
            add(got, at, stage, slot, BACK_CUT, PART_ROWS - BACK_CUT, [])
            send_x(k).start()
        else:
            send_x(k).wait_recv()
            send_y(k).wait_recv()
            add(got, at, stage, slot, 0, PART_ROWS, [(from_x, k), (from_y, k)])

    def bulk_z(q):
        at, zd = 3 * items + q, order[q // PARTS]

        @pl.when(zd > z)
        def _():
            @pl.when(z > 0)
            def _():
                send_up(q).wait_recv()
                add(got, at, from_low, low_slot(q), 0, PART_ROWS, [])

            send_up(q).start()

        @pl.when(zd < z)
        def _():
            @pl.when(z < 3)
            def _():
                send_down(q).wait_recv()
                add(got, at, from_high, high_slot(q), 0, PART_ROWS, [])

            send_down(q).start()

    def light_item(group, k):
        at, zd, column = 4 * group + k, order[k], l_column(group)
        l_fetch(group, k).wait()
        l_share(group, k).wait_recv()
        add(l_got, at, l_stage, at, 0, SMALL_HALF, [])

        def merge(ref, slot):
            l_got[at] = (l_got[at].astype(FULL) + ref[column, slot].astype(FULL)).astype(LOW)

        if k < 3:

            @pl.when(zd > z)
            def _():
                @pl.when(z > 0)
                def _():
                    l_up(group, k).wait_recv()
                    merge(l_low, zd - 1)

                l_up(group, k).start()

            @pl.when(zd < z)
            def _():
                @pl.when(z < 3)
                def _():
                    l_down(group, k).wait_recv()
                    merge(l_high, zd)

                l_down(group, k).start()

        else:

            @pl.when(z > 0)
            def _():
                l_up(group, k).wait_recv()
                merge(l_low, zd - 1)

            @pl.when(z < 3)
            def _():
                l_down(group, k).wait_recv()
                merge(l_high, zd)

            if group == 0:
                l_half_x().start()
                l_half_y().start()

    def light_sides():
        l_half_x().wait_recv()
        l_got[7, LIGHT_CUT:SMALL_HALF, :] = (
            l_got[7, LIGHT_CUT:SMALL_HALF, :].astype(FULL) + l_halves_x[...].astype(FULL)
        ).astype(LOW)
        l_send_y().start()
        l_half_y().wait_recv()
        l_got[11, 0:LIGHT_CUT, :] = (
            l_got[11, 0:LIGHT_CUT, :].astype(FULL) + l_halves_y[...].astype(FULL)
        ).astype(LOW)
        l_send_x().start()

    def light_end():
        l_send_x().wait_recv()
        l_send_y().wait_recv()
        l_total[...] = l_got[15].astype(FULL) + l_from_x[...].astype(FULL) + l_from_y[...].astype(FULL)

    small_join = remote(late_half, late.at[pl.ds(0, SMALL_HALF)], join_send.at[0], join_recv.at[0], sibling)
    own_late = pltpu.make_async_copy(late, out_small.at[me.dp], out_sem.at[1])

    def late_z(origin, target, way):
        block = out_small.at[2 * origin + y]
        return remote(block, block, late_send.at[way, origin], late_recv.at[0, origin], target)

    def late_y(origin, yo):
        block = out_small.at[2 * origin + yo]
        return remote(block, block, late_send.at[2, origin], late_recv.at[1, origin], y_side)

    def late_step(k):
        @pl.when((core == 1) & (z >= k))
        def _():
            late_z(z - k, up, 0).wait_recv()
            pl.when(z < 3)(lambda: late_z(z - k, up, 0).start())
            late_y(z - k, y).start()

        @pl.when((core == 1) & (z + k <= 3))
        def _():
            late_z(z + k, down, 1).wait_recv()
            pl.when(z > 0)(lambda: late_z(z + k, down, 1).start())
            late_y(z + k, y).start()

    def leave():
        for section in range(4):
            @pl.when(me.pipe == section)
            def _(section=section):
                all_of(keep(section), lambda copy: copy.start())

            @pl.when(me.pipe != section)
            def _(section=section):
                all_of(exchange(section), lambda copy: copy.start())

    def late_start():
        light_end()

        @pl.when(core == 0)
        def _():
            late_half[...] = l_total[...].astype(LOW)
            small_join.start()

        @pl.when(core == 1)
        def _():
            late[SMALL_HALF:SMALL_ROWS, :] = l_total[...].astype(LOW)
            small_join.wait_recv()
            own_late.start()
            own_late.wait()
            pl.when(z < 3)(lambda: late_z(z, up, 0).start())
            pl.when(z > 0)(lambda: late_z(z, down, 1).start())
            late_y(z, y).start()

    def light_round(k):
        for n in range(4 * k, 4 * k + 4):
            light_item(*l_sequence[n])

    edge = (z == 0) | (z == 3)

    def early_z(k):
        pl.when(edge)(lambda: bulk_z(k))

    def inner_z(k):
        pl.when(jnp.logical_not(edge))(lambda: bulk_z(k))

    actions = {"LS": [light_sides], "LE": [late_start], "G": [leave]}
    numbered = {item: n for n, item in enumerate(sequence)}
    for k in range(4):
        actions["L%d" % k] = [functools.partial(light_round, k)]
        if k:
            actions["T%d" % k] = [functools.partial(late_step, k)]
    for q in range(items):
        for letter, group in (("A", 0), ("C", 1), ("B", 2), ("O", 3)):
            actions["%s%d" % (letter, q)] = [functools.partial(bulk_item, numbered[group, q])]
        if q < 3 * PARTS:
            actions["E%d" % q] = [functools.partial(early_z, q)]
            actions["I%d" % q] = [functools.partial(inner_z, q)]
    for event in REDUCE_ORDER:
        for action in actions[event]:
            action()

    row_copy.wait()
    part_sum[...] = jnp.sum((l_total[...] * l_total[...]).reshape(SMALL_HALF // 8, 8, 128), axis=0)
    lane = lax.broadcasted_iota(jnp.int32, (8, 128), 1)
    is_last = jnp.where((lane == me.dp) & (owner_row[...] == 7), 1.0, 0.0)
    weight = jnp.broadcast_to(jnp.sum(is_last, axis=1, keepdims=True), (8, 128))
    weight = jnp.where(core == 0, jnp.ones((8, 128), FULL), weight)

    big_parts = [pl.ds(PART_ROWS * n, PART_ROWS) for n in range(PARTS)]

    def big_join(n):
        return remote(total.at[big_parts[n]], out_big.at[1, big_parts[n]],
                      join_send.at[1 + n], join_recv.at[1 + n], sibling)

    def own_big(n):
        return pltpu.make_async_copy(total.at[big_parts[n]], out_big.at[0, big_parts[n]], big_sem.at[n])

    def end(n, low, high):
        q = 3 * PARTS + n

        def piece(begin, size, scale):
            part = pl.ds(begin, size)
            sums = got[3 * items + q, part, :].astype(FULL)
            if low:
                sums = sums + from_low[low_slot(q), part, :].astype(FULL)
            if high:
                sums = sums + from_high[high_slot(q), part, :].astype(FULL)
            total[pl.ds(PART_ROWS * n + begin, size), :] = sums
            squares = jnp.sum((sums * sums).reshape(size // 8, 8, 128), axis=0)
            part_sum[...] += squares if scale is None else squares * scale

        def plain(begin, size):
            piece(begin, size, None)

        if n < PARTS - 1:
            over(0, PART_ROWS, plain)
        else:
            over(0, PART_ROWS - EDGE, plain)
            piece(PART_ROWS - EDGE, EDGE, weight)

    for n in range(PARTS):
        q = 3 * PARTS + n

        @pl.when(z == 0)
        def _(n=n, q=q):
            send_down(q).wait_recv()
            end(n, False, True)

        @pl.when((z > 0) & (z < 3))
        def _(n=n, q=q):
            send_up(q).wait_recv()
            send_down(q).wait_recv()
            end(n, True, True)

        @pl.when(z == 3)
        def _(n=n, q=q):
            send_up(q).wait_recv()
            end(n, True, False)

        @pl.when(core == 0)
        def _(n=n):
            own_big(n).start()

        @pl.when(core == 1)
        def _(n=n):
            big_join(n).start()

    def along_pipe(step, slot):
        target = {"dp": me.dp, "pipe": lax.rem(me.pipe + step, 4)}
        return remote(part_sum, by_pipe.at[slot], p_send.at[step], p_recv.at[step], target)

    def along_dp(step, slot):
        target = {"dp": lax.rem(me.dp + step, 8), "pipe": me.pipe}
        return remote(mine, by_dp.at[slot], d_send.at[step], d_recv.at[step], target)

    for step in range(1, 4):
        along_pipe(step, me.pipe).start()
    by_pipe[me.pipe] = part_sum[...]
    for step in range(1, 4):
        along_pipe(step, lax.rem(me.pipe + 4 - step, 4)).wait_recv()
    mine[...] = jnp.sum(by_pipe[...], axis=0)
    for step in range(1, 8):
        along_dp(step, me.dp).start()
    by_dp[me.dp] = mine[...]
    for step in range(1, 8):
        along_dp(step, lax.rem(me.dp + 8 - step, 8)).wait_recv()
    whole = jnp.sum(jnp.sum(by_dp[...], axis=0), axis=0, keepdims=True)
    length = jnp.sqrt(jnp.broadcast_to(jnp.sum(whole, axis=1, keepdims=True), (8, 128)))
    norm[...] = length
    factor[...] = jnp.minimum(1.0, CLIP_NORM / length)

    @pl.when(core == 0)
    def _():
        for n in range(PARTS):
            own_big(n).wait()
            big_join(n).wait_recv()
        small_join.wait_send()

    @pl.when(core == 1)
    def _():
        for n in range(PARTS):
            big_join(n).wait_send()
        for origin in range(4):
            late_y(origin, 1 - y).wait_recv()
            late_y(origin, y).wait_send()
            pl.when((z < 3) & (origin <= z))(lambda: late_z(origin, up, 0).wait_send())
            pl.when((z > 0) & (origin >= z))(lambda: late_z(origin, down, 1).wait_send())

    for other in range(4):
        @pl.when(me.pipe == other)
        def _(other=other):
            all_of(keep(other), lambda copy: copy.wait())

        @pl.when(me.pipe != other)
        def _(other=other):
            all_of(exchange(other), lambda copy: copy.wait_send())
            all_of(arriving(other), lambda copy: copy.wait_recv())

    for step in range(1, 4):
        along_pipe(step, me.pipe).wait_send()
    for step in range(1, 8):
        along_dp(step, me.dp).wait_send()
    for copy in (l_half_x(), l_half_y(), l_send_x(), l_send_y()):
        copy.wait_send()
    for q in range(items):
        send_half_x(q).wait_send()
        send_half_y(q).wait_send()
        send_x(q).wait_send()
        send_y(q).wait_send()
        for group in range(4):
            share(group, q).wait_send()
    for group, k in l_sequence:
        l_share(group, k).wait_send()
    for k in range(3):
        zd = order[k]

        @pl.when(zd > z)
        def _(k=k):
            for n in range(PARTS):
                send_up(PARTS * k + n).wait_send()
            for group in range(4):
                l_up(group, k).wait_send()

        @pl.when(zd < z)
        def _(k=k):
            for n in range(PARTS):
                send_down(PARTS * k + n).wait_send()
            for group in range(4):
                l_down(group, k).wait_send()


def reduce_all(big, small, wide0, wide1, final, stats, table):
    sem = pltpu.SemaphoreType.DMA
    vm = pltpu.VMEM
    items = 4 * PARTS
    lane_tile = jax.ShapeDtypeStruct((8, 128), FULL)
    return pl.pallas_call(
        reduce_kernel,
        name="reduce_all",
        out_shape=(
            jax.ShapeDtypeStruct((2, BIG_HALF, 128), FULL),
            jax.ShapeDtypeStruct((8, SMALL_ROWS, 128), LOW),
            jax.ShapeDtypeStruct((4, STUD_ROWS, C_OUT), LOW),
            jax.ShapeDtypeStruct((4, TEACH_END, C_OUT), LOW),
            jax.ShapeDtypeStruct((4,) + stats.shape[1:], FULL),
            lane_tile,
            lane_tile,
        ),
        in_specs=[any_spec()] * 7,
        out_specs=(any_spec(),) * 5 + (vmem_spec(),) * 2,
        scratch_shapes=[
            vm((4 * items, PART_ROWS, 128), LOW),
            vm((items, PART_ROWS - BACK_CUT, 128), LOW), vm((items, BACK_CUT, 128), LOW),
            vm((items, PART_ROWS, 128), LOW), vm((items, PART_ROWS, 128), LOW),
            vm((3 * PARTS, PART_ROWS, 128), LOW), vm((3 * PARTS, PART_ROWS, 128), LOW),
            vm((4, PART_ROWS, 128), LOW), vm((BIG_HALF, 128), FULL),
            vm((16, SMALL_HALF, 128), LOW), vm((16, SMALL_HALF, 128), LOW),
            vm((4, 3, SMALL_HALF, 128), LOW), vm((4, 3, SMALL_HALF, 128), LOW),
            vm((SMALL_HALF - LIGHT_CUT, 128), LOW), vm((LIGHT_CUT, 128), LOW),
            vm((SMALL_HALF, 128), LOW), vm((SMALL_HALF, 128), LOW), vm((SMALL_HALF, 128), FULL),
            vm((SMALL_ROWS, 128), LOW), vm((SMALL_HALF, 128), LOW), vm((8, 128), jnp.int32),
            vm((4, 8, 128), FULL), vm((8, 8, 128), FULL), vm((8, 128), FULL), vm((8, 128), FULL),
            sem((4 * items,)), sem((4 * items,)), sem((16,)), sem((16,)),
            sem((items + 1,)), sem((items + 1,)), sem((items + 1,)), sem((items + 1,)),
            sem((items + 1,)), sem((items + 1,)), sem((items + 1,)), sem((items + 1,)),
            sem((3 * PARTS,)), sem((3 * PARTS,)), sem((3 * PARTS,)), sem((3 * PARTS,)),
            sem((4, 3)), sem((4, 3)), sem((4, 3)), sem((4, 3)),
            sem((4,)), sem((16,)), sem((3,)), sem((PARTS,)), sem((3, 4)), sem((2, 4)),
            sem((1 + PARTS,)), sem((1 + PARTS,)),
            sem((2, 4)), sem((2, 4)), sem((4,)), sem((4,)), sem((4,)), sem((4,)), sem((8,)), sem((8,)),
        ],
        compiler_params=pltpu.CompilerParams(
            collective_id=1, has_side_effects=True, vmem_limit_bytes=62 << 20
        ),
    )(big.reshape(2, 8, 2, BIG_HALF, 128), small.reshape(2, 8, 2, SMALL_HALF, 128),
      wide0, wide1, final, stats, table)


def high_dot(a, b, dims=((1,), (0,))):
    return lax.dot_general(a, b, (dims, ((), ())), precision=HIGH, preferred_element_type=FULL)


PIECES = 7
FRONT = 48


def update_kernel(owners, factor_ref, norm, big, small, gram_old, basis_old, params, moment, second,
                  clipped, moment_new, second_new, params_new, gram_new, basis_new, length,
                  tiles, low, grad, held, rotated, weights, gram, in_sem, out_sem, tile_sem):
    factor = factor_ref[0:1, :]
    length[0, 0] = jnp.max(norm[...])
    block, section = owners[0, lax.axis_index("dp")], lax.axis_index("pipe")
    even = lax.rem(section, 2) == 0
    span = params.shape[0]
    piece = held.shape[0] // PIECES

    quarter = WINDOW // 4 * TILE

    def big_load(i):
        part = pl.ds(quarter * i, min(quarter, BIG_ROWS - quarter * i))
        return pltpu.make_async_copy(big.at[part], tiles.at[part], tile_sem.at[i])

    @pl.when(even)
    def _():
        for i in range(4):
            big_load(i).start()

    def loads(i):
        part = pl.ds(piece * i, min(piece, span - piece * i))
        for n, (src, dst) in enumerate(((params, weights), (moment, held), (second, rotated))):
            yield pltpu.make_async_copy(src.at[part, 0, :], dst.at[part], in_sem.at[n, i])

    def stores(i):
        count = min(piece, span - piece * i)
        part = pl.ds(piece * i, count)
        yield pltpu.make_async_copy(
            grad.at[pl.ds(FRONT + piece * i, count)], clipped.at[part, 0, :], out_sem.at[3, i])
        pairs = ((held, moment_new), (rotated, second_new), (weights, params_new))
        for n, (src, dst) in enumerate(pairs):
            yield pltpu.make_async_copy(src.at[part], dst.at[part, 0, :], out_sem.at[n, i])

    for i in range(PIECES):
        for load in loads(i):
            load.start()

    @pl.when(jnp.logical_not(even))
    def _():
        low[...] = jnp.zeros_like(low)

        @pl.when(block == 0)
        def _():
            copy = pltpu.make_async_copy(small.at[0:20], low, tile_sem.at[0])
            copy.start()
            copy.wait()

        @pl.when(block == 1)
        def _():
            copy = pltpu.make_async_copy(small.at[19:33], low.at[0:14], tile_sem.at[0])
            copy.start()
            copy.wait()

        @pl.loop(0, WINDOW)
        def _(r):
            tiles[pl.ds(pl.multiple_of(TILE * r, TILE), TILE), :] = low[r].astype(FULL)

    def lay_flat(r):
        narrow, plain = tile_forms(section, STRIDE * block + r)
        edge = even & (r == STRIDE)
        narrow, plain = narrow & jnp.logical_not(edge), plain | edge
        base = FRONT - 6 * block + TILE * r
        here = pl.multiple_of(TILE * r, TILE)

        @pl.when(narrow)
        def _():
            for j in range(4):
                grad[pl.ds(base + j, 64, 4), :] = tiles[pl.ds(here + 64 * j, 64), :]

        @pl.when(plain)
        def _():
            grad[pl.ds(base, TILE), :] = tiles[pl.ds(here, TILE), :]

        @pl.when(jnp.logical_not(narrow | plain))
        def _():
            for j in range(16):
                grad[pl.ds(base + j, 16, 16), :] = tiles[pl.ds(here + 16 * j, 16), :]

    for i in range(4):
        pl.when(even)(lambda: big_load(i).wait())
        pl.loop(WINDOW // 4 * i, WINDOW // 4 * (i + 1))(lay_flat)

    tail = piece * PIECES - 8
    rest = lax.broadcasted_iota(jnp.int32, (8, 128), 0) + tail
    grad[FRONT + tail : FRONT + tail + 8, :] = jnp.where(
        rest < span, grad[FRONT + tail : FRONT + tail + 8, :], 0.0
    )
    gram[...] = jnp.zeros_like(gram)

    def halves(value):
        high = value.astype(LOW)
        return high, (value - high.astype(FULL)).astype(LOW)

    def split_dot(a, b, dims=((1,), (0,))):
        def dot(left, right):
            return lax.dot_general(left, right, (dims, ((), ())), preferred_element_type=FULL)

        return dot(a[0], b[0]) + (dot(a[0], b[1]) + dot(a[1], b[0]))

    @pl.loop(0, PIECES)
    def _(i):
        part = halves(grad[pl.ds(pl.multiple_of(FRONT + piece * i, 8), piece), :])
        gram[...] += split_dot(part, part, ((0,), (0,)))

    old = basis_old[...]
    fresh = DECAY_STATS * gram_old[...] + (1.0 - DECAY_STATS) * (gram[...] * (factor * factor))
    gram_new[...] = fresh
    product = high_dot(fresh, old)
    rotation = product / jnp.sqrt(jnp.sum(product * product))
    for repeat in range(NS_STEPS):
        parts = halves(rotation)
        square = split_dot(parts, parts, ((0,), (0,)))
        rotation = 1.5 * rotation - 0.5 * split_dot(parts, halves(square))
    basis_new[...] = rotation
    change = halves(high_dot(old, rotation, ((0,), (0,))))
    turn = halves(rotation)
    correction = math.sqrt(1.0 - DECAY_SECOND**STEP) / (1.0 - DECAY_FIRST**STEP)
    for i in range(PIECES):
        for load in loads(i):
            load.wait()
        at = slice(FRONT + piece * i, FRONT + piece * i + piece)
        part = slice(piece * i, piece * i + piece)
        clip = grad[at, :] * factor
        grad[at, :] = clip
        turned = split_dot(halves(clip), turn)
        first = DECAY_FIRST * split_dot(halves(held[part, :]), change) + (1.0 - DECAY_FIRST) * turned
        power = DECAY_SECOND * rotated[part, :] + (1.0 - DECAY_SECOND) * turned * turned
        held[part, :] = first
        rotated[part, :] = power
        scaled = halves(first / (jnp.sqrt(power) + ADAM_EPS))
        direction = split_dot(scaled, turn, ((1,), (1,))) * correction
        before = weights[part, :]
        weights[part, :] = before - LEARN_RATE * (direction + WEIGHT_DECAY * before)
        for store in stores(i):
            store.start()
    for i in range(PIECES):
        for store in stores(i):
            store.wait()


def update(owners, factor, norm, big, small, gram_old, basis_old, params, moment, second):
    span = params.shape[1] // 128
    rows = -(-span // (8 * PIECES)) * 8 * PIECES
    flat_shape = jax.ShapeDtypeStruct((span, 1, 128), FULL)
    square = jax.ShapeDtypeStruct((128, 128), FULL)
    sem = pltpu.SemaphoreType.DMA
    vm = pltpu.VMEM
    outs = pl.pallas_call(
        update_kernel,
        name="update",
        out_shape=(flat_shape,) * 4 + (square,) * 2 + (jax.ShapeDtypeStruct((1, 1), FULL),),
        in_specs=[smem_spec()] + [vmem_spec()] * 2 + [any_spec()] * 2 + [vmem_spec()] * 2 + [any_spec()] * 3,
        out_specs=(any_spec(),) * 4 + (vmem_spec(),) * 2 + (smem_spec(),),
        scratch_shapes=[
            vm((WINDOW * TILE, 128), FULL), vm((WINDOW, TILE, 128), LOW),
            vm((FRONT + WINDOW * TILE, 128), FULL), vm((rows, 128), FULL), vm((rows, 128), FULL),
            vm((rows, 128), FULL), vm((128, 128), FULL), sem((3, PIECES)), sem((4, PIECES)), sem((4,)),
        ],
        compiler_params=pltpu.CompilerParams(vmem_limit_bytes=60 << 20),
    )(owners, factor, norm, big.reshape(BIG_ROWS, 128), small.reshape(USED_TILES[1], TILE, 128),
      gram_old, basis_old, params.reshape(span, 1, 128), moment.reshape(span, 1, 128),
      second.reshape(span, 1, 128))
    return tuple(out.reshape(1, span * 128) for out in outs[:4]) + outs[4:]


def to_phases(teach, stud):
    def split(part, axes):
        crops, high, across, channels = part.shape
        part = part.reshape(crops, high // 2, 2, across // 2, 2, channels).transpose(axes)
        return part.reshape(4, -1, channels)

    zeros = jnp.zeros((4, PADDED - ROWS, teach.shape[-1]), teach.dtype)
    parts = [split(stud, (2, 4, 0, 1, 3, 5)), split(teach, (2, 4, 1, 3, 0, 5)), zeros]
    return jnp.concatenate(parts, axis=1)


def from_phases(phases, shape, crops_last):
    crops, high, across, channels = shape
    if crops_last:
        part = phases.reshape(2, 2, high // 2, across // 2, crops, channels).transpose(4, 2, 0, 3, 1, 5)
    else:
        part = phases.reshape(2, 2, crops, high // 2, across // 2, channels).transpose(2, 3, 0, 4, 1, 5)
    return part.reshape(shape)


def on_small_slice(
    teach_in,
    stud_in,
    params,
    owners,
    depth_gates,
    teach_ids,
    stud_ids,
    targets,
    moment,
    second,
    gram_stats,
    eigen_basis,
):
    phases = to_phases(teach_in[0], stud_in[0])
    big, small, ids = prepare(owners, params)
    all_big, all_small, table = gather_all(big, small, ids)
    wide_0, wide_1, final, stats, grad_x, out_big, out_small = run_step(
        table,
        depth_gates,
        teach_ids.T,
        stud_ids,
        all_big.reshape(2, 8, BIG_ROWS, 128),
        all_small.reshape(2, USED_TILES[1], TILE, 128),
        phases,
        targets,
    )
    sum_big, sum_small, segment_stud, segment_teach, stats, norm, factor = reduce_all(
        out_big, out_small, wide_0, wide_1, final, stats, table
    )
    clipped, moment_new, second_new, params_new, gram_new, rotation, length = update(
        owners, factor, norm, sum_big, sum_small, gram_stats[0], eigen_basis[0], params, moment, second
    )
    teach_shape, stud_shape = teach_in.shape[1:], stud_in.shape[1:]
    small_teach = (teach_shape[1] // 2, teach_shape[2] // 2, teach_shape[0], C_OUT)
    small_stud = (stud_shape[0], stud_shape[1] // 2, stud_shape[2] // 2, C_OUT)
    segment_teach = segment_teach[:, : ROWS - STUD_ROWS].reshape((4,) + small_teach).transpose(0, 3, 1, 2, 4)
    segment_stud = segment_stud.reshape((4,) + small_stud)
    stats = stats[:, 0:2]
    teach_grad = from_phases(grad_x[:, STUD_ROWS:ROWS], teach_shape, True)
    stud_grad = from_phases(grad_x[:, :STUD_ROWS], stud_shape, False)
    grad_norm = length.reshape(())
    return (
        segment_teach[None],
        segment_stud[None],
        teach_grad[None],
        stud_grad[None],
        stats[None, :, None],
        grad_norm,
        clipped,
        moment_new,
        second_new,
        params_new,
        gram_new[None],
        rotation[None],
    )


def solution(mesh):
    placed = (
        P("pipe", "dp", None, None, None),
        P("pipe", "dp", None, None, None),
        P("pipe", "dp"),
        P("pipe", None),
        P(),
        P(None, "dp"),
        P(None, "dp"),
        P(),
        P("pipe", "dp"),
        P("pipe", "dp"),
        P("pipe", "dp", None),
        P("pipe", "dp", None),
    )
    small_slice = mesh.shape["dp"] == 8 and mesh.shape["pipe"] == 4
    return jax.shard_map(
        on_small_slice if small_slice else on_device,
        mesh=mesh,
        in_specs=placed,
        out_specs=(
            P("pipe", None, "dp", None, None, None),
            P("pipe", None, "dp", None, None, None),
            P("pipe", "dp", None, None, None),
            P("pipe", "dp", None, None, None),
            P("pipe", None, "dp", None, None),
            P(),
            P("pipe", "dp"),
            P("pipe", "dp"),
            P("pipe", "dp"),
            P("pipe", "dp"),
            P("pipe", "dp", None),
            P("pipe", "dp", None),
        ),
        check_vma=False,
    )
```

```python
import functools
import math

import jax
import jax.numpy as jnp
import numpy as np
from jax import lax
from jax.experimental import pallas as pl
from jax.experimental.pallas import tpu as pltpu
from jax.sharding import PartitionSpec as P

C_IN = 1024
MID = 512
C_OUT = 2048
STEP = 10
NS_STEPS = 5


HIGH = lax.Precision.HIGHEST
NORM_EPS = 1e-05
POOL_EPS = 1e-06
CLIP_NORM = 1.0
LEARN_RATE = 0.02
DECAY_FIRST = 0.9
DECAY_SECOND = 0.95
DECAY_STATS = 0.95
ADAM_EPS = 1e-08
WEIGHT_DECAY = 0.01


def section_shapes(section):
    if section == 0:
        return [
            ("first_conv", (C_IN, MID)),
            ("middle_conv", (9 * MID, MID)),
            ("skip_conv", (C_IN, C_OUT)),
            ("first_gain", (MID,)),
            ("first_bias", (MID,)),
            ("middle_gain", (MID,)),
            ("middle_bias", (MID,)),
            ("skip_gain", (C_OUT,)),
            ("skip_bias", (C_OUT,)),
        ]
    if section == 2:
        return [
            ("first_conv", (C_OUT, MID)),
            ("middle_conv", (9 * MID, MID)),
            ("first_gain", (MID,)),
            ("first_bias", (MID,)),
            ("middle_gain", (MID,)),
            ("middle_bias", (MID,)),
        ]
    return [("last_conv", (MID, C_OUT)), ("last_gain", (C_OUT,)), ("last_bias", (C_OUT,))]


def unpack(flat_vector, section):
    pieces = {}
    offset = 0
    for entry_name, entry_shape in section_shapes(section):
        entry_size = math.prod(entry_shape)
        pieces[entry_name] = flat_vector[offset : offset + entry_size].reshape(entry_shape)
        offset = offset + entry_size
    return pieces


def pack(grads, section, flat_size):
    parts = [grads[entry_name].reshape(-1) for entry_name, entry_shape in section_shapes(section)]
    used = sum((math.prod(entry_shape) for entry_name, entry_shape in section_shapes(section)))
    parts.append(jnp.zeros((flat_size - used,), jnp.float32))
    return jnp.concatenate(parts)


def as_float(vector):
    return vector.astype(jnp.float32)


def to_low(groups):
    return tuple((portion.astype(jnp.bfloat16) for portion in groups))


def to_high(groups):
    return tuple((portion.astype(jnp.float32) for portion in groups))


def point_conv(groups, weight):
    return tuple(
        (
            jnp.einsum("khwc,cd->khwd", portion, weight, preferred_element_type=jnp.float32)
            for portion in groups
        )
    )


def point_back(grad_out, groups, weight):
    low_grads = to_low(grad_out)
    grad_input = tuple(
        (
            jnp.einsum("khwd,cd->khwc", grad_part, weight, preferred_element_type=jnp.float32)
            for grad_part in low_grads
        )
    )
    grad_weight = sum(
        (
            jnp.einsum("khwc,khwd->cd", in_part, grad_part, preferred_element_type=jnp.float32)
            for in_part, grad_part in zip(groups, low_grads)
        )
    )
    return (grad_input, grad_weight)


def patches(portion, stride):
    height = portion.shape[1]
    across = portion.shape[2]
    padded = jnp.pad(portion, ((0, 0), (1, 1), (1, 1), (0, 0)))
    shifted = [
        padded[:, row_off : row_off + height : stride, col_off : col_off + across : stride, :]
        for row_off in range(3)
        for col_off in range(3)
    ]
    return jnp.concatenate(shifted, axis=-1)


def area_conv(groups, weight, stride):
    columns = tuple((patches(portion, stride) for portion in groups))
    return (point_conv(columns, weight), columns)


def unpatch(grad_cols, height, across, stride):
    channels = grad_cols.shape[-1] // 9
    padded = jnp.zeros((grad_cols.shape[0], height + 2, across + 2, channels), jnp.float32)
    for row_off in range(3):
        for col_off in range(3):
            offset = (3 * row_off + col_off) * channels
            padded = padded.at[
                :, row_off : row_off + height : stride, col_off : col_off + across : stride, :
            ].add(grad_cols[..., offset : offset + channels])
    return padded[:, 1 : height + 1, 1 : across + 1, :]


def area_back(grad_out, columns, weight, stride, in_shapes):
    grad_cols, grad_weight = point_back(grad_out, columns, weight)
    grad_input = tuple(
        (
            unpatch(grad_part, shape_item[1], shape_item[2], stride)
            for grad_part, shape_item in zip(grad_cols, in_shapes)
        )
    )
    return (grad_input, grad_weight)


def batch_norm(groups, gain, bias):
    rows_total = sum((portion.shape[0] * portion.shape[1] * portion.shape[2] for portion in groups))
    centre = sum((jnp.sum(portion, axis=(0, 1, 2)) for portion in groups)) / rows_total
    spread = (
        sum((jnp.sum(jnp.square(portion - centre), axis=(0, 1, 2)) for portion in groups))
        / rows_total
    )
    inverse = lax.rsqrt(spread + NORM_EPS)
    standard = tuple(((portion - centre) * inverse for portion in groups))
    normed = tuple((gain * std_part + bias for std_part in standard))
    return (normed, (centre, spread, inverse, standard))


def norm_back(grad_out, gain, saved):
    centre, spread, inverse, standard = saved
    rows_total = sum(
        (portion.shape[0] * portion.shape[1] * portion.shape[2] for portion in standard)
    )
    grad_sum = sum((jnp.sum(grad_part, axis=(0, 1, 2)) for grad_part in grad_out))
    grad_dot = sum(
        (
            jnp.sum(grad_part * std_part, axis=(0, 1, 2))
            for grad_part, std_part in zip(grad_out, standard)
        )
    )
    grad_input = tuple(
        (
            gain
            * inverse
            * (grad_part - grad_sum / rows_total - std_part * (grad_dot / rows_total))
            for grad_part, std_part in zip(grad_out, standard)
        )
    )
    return (grad_input, grad_dot, grad_sum)


def through_softplus(grad_out, pre_values):
    return tuple(
        (grad_part * jax.nn.sigmoid(pre_part) for grad_part, pre_part in zip(grad_out, pre_values))
    )


def front_forward(pieces, inputs):
    first = point_conv(inputs, pieces["first_conv"])
    normed_a, saved_a = batch_norm(
        first, as_float(pieces["first_gain"]), as_float(pieces["first_bias"])
    )
    hidden = tuple((jax.nn.softplus(portion).astype(jnp.bfloat16) for portion in normed_a))
    middle, columns = area_conv(hidden, pieces["middle_conv"], 2)
    normed_b, saved_b = batch_norm(
        middle, as_float(pieces["middle_gain"]), as_float(pieces["middle_bias"])
    )
    narrow = tuple((jax.nn.softplus(portion) for portion in normed_b))
    reduced = tuple((portion[:, ::2, ::2, :] for portion in inputs))
    skipped = point_conv(reduced, pieces["skip_conv"])
    wide, saved_p = batch_norm(
        skipped, as_float(pieces["skip_gain"]), as_float(pieces["skip_bias"])
    )
    norm_rows = jnp.stack(
        [
            jnp.concatenate([saved_a[0], saved_b[0], saved_p[0]]),
            jnp.concatenate([saved_a[1], saved_b[1], saved_p[1]]),
        ]
    )
    kept = (normed_a, hidden, columns, normed_b, reduced, saved_a, saved_b, saved_p)
    return (wide, narrow, norm_rows, kept)


def front_backward(pieces, inputs, grad_wide, grad_narrow):
    wide, narrow, norm_rows, kept = front_forward(pieces, inputs)
    normed_a, hidden, columns, normed_b, reduced, saved_a, saved_b, saved_p = kept
    grads = {}
    grad_pre_b = through_softplus(grad_narrow, normed_b)
    grad_mid, grads["middle_gain"], grads["middle_bias"] = norm_back(
        grad_pre_b, as_float(pieces["middle_gain"]), saved_b
    )
    grad_hidden, grads["middle_conv"] = area_back(
        grad_mid, columns, pieces["middle_conv"], 2, [portion.shape for portion in hidden]
    )
    grad_pre_a = through_softplus(grad_hidden, normed_a)
    grad_first, grads["first_gain"], grads["first_bias"] = norm_back(
        grad_pre_a, as_float(pieces["first_gain"]), saved_a
    )
    grad_inputs, grads["first_conv"] = point_back(grad_first, inputs, pieces["first_conv"])
    grad_skip, grads["skip_gain"], grads["skip_bias"] = norm_back(
        grad_wide, as_float(pieces["skip_gain"]), saved_p
    )
    grad_reduced, grads["skip_conv"] = point_back(grad_skip, reduced, pieces["skip_conv"])
    grad_inputs = tuple(
        (
            full_part.at[:, ::2, ::2, :].add(part_reduced)
            for full_part, part_reduced in zip(grad_inputs, grad_reduced)
        )
    )
    return (grad_inputs, grads)


def join_forward(pieces, wide, narrow):
    last = point_conv(narrow, pieces["last_conv"])
    normed, saved = batch_norm(last, as_float(pieces["last_gain"]), as_float(pieces["last_bias"]))
    pre_values = tuple(
        (
            skip_part.astype(jnp.float32) + branch_part
            for skip_part, branch_part in zip(wide, normed)
        )
    )
    ending = tuple((jax.nn.softplus(pre_part) for pre_part in pre_values))
    filler = jnp.zeros((2 * MID,), jnp.float32)
    norm_rows = jnp.stack(
        [jnp.concatenate([saved[0], filler]), jnp.concatenate([saved[1], filler])]
    )
    return (ending, norm_rows, (pre_values, saved))


def join_grads(pieces, narrow, kept, grad_out, gate):
    pre_values, saved = kept
    grad_pre = tuple(
        (
            grad_part * jax.nn.sigmoid(pre_part) * gate
            for grad_part, pre_part in zip(grad_out, pre_values)
        )
    )
    grad_wide = tuple(
        (pre_grad + grad_part * (1.0 - gate) for pre_grad, grad_part in zip(grad_pre, grad_out))
    )
    grad_last, gain_grad, bias_grad = norm_back(grad_pre, as_float(pieces["last_gain"]), saved)
    grad_narrow, weight_grad = point_back(grad_last, narrow, pieces["last_conv"])
    grads = {"last_conv": weight_grad, "last_gain": gain_grad, "last_bias": bias_grad}
    return (grad_wide, grad_narrow, grads)


def split_forward(pieces, wide):
    first = point_conv(wide, pieces["first_conv"])
    normed_a, saved_a = batch_norm(
        first, as_float(pieces["first_gain"]), as_float(pieces["first_bias"])
    )
    hidden = tuple((jax.nn.softplus(portion).astype(jnp.bfloat16) for portion in normed_a))
    middle, columns = area_conv(hidden, pieces["middle_conv"], 1)
    normed_b, saved_b = batch_norm(
        middle, as_float(pieces["middle_gain"]), as_float(pieces["middle_bias"])
    )
    narrow = tuple((jax.nn.softplus(portion) for portion in normed_b))
    filler = jnp.zeros((C_OUT,), jnp.float32)
    norm_rows = jnp.stack(
        [
            jnp.concatenate([saved_a[0], saved_b[0], filler]),
            jnp.concatenate([saved_a[1], saved_b[1], filler]),
        ]
    )
    return (narrow, norm_rows, (normed_a, hidden, columns, normed_b, saved_a, saved_b))


def split_backward(pieces, wide, grad_relay, grad_narrow):
    narrow, norm_rows, kept = split_forward(pieces, wide)
    normed_a, hidden, columns, normed_b, saved_a, saved_b = kept
    grads = {}
    grad_pre_b = through_softplus(grad_narrow, normed_b)
    grad_mid, grads["middle_gain"], grads["middle_bias"] = norm_back(
        grad_pre_b, as_float(pieces["middle_gain"]), saved_b
    )
    grad_hidden, grads["middle_conv"] = area_back(
        grad_mid, columns, pieces["middle_conv"], 1, [portion.shape for portion in hidden]
    )
    grad_pre_a = through_softplus(grad_hidden, normed_a)
    grad_first, grads["first_gain"], grads["first_bias"] = norm_back(
        grad_pre_a, as_float(pieces["first_gain"]), saved_a
    )
    grad_conv_in, grads["first_conv"] = point_back(grad_first, wide, pieces["first_conv"])
    grad_wide = tuple(
        (relay_part + conv_part for relay_part, conv_part in zip(grad_relay, grad_conv_in))
    )
    return (grad_wide, grads)


def pool_grad(final, targets, picks):
    result = []
    for portion, pick_ids in zip(final, picks):
        cubes = jnp.mean(portion * portion * portion, axis=(1, 2)) + POOL_EPS
        factor = jnp.exp(jnp.log(cubes) * (-2.0 / 3.0)) * targets[pick_ids]
        result.append(factor[:, None, None, :] * portion * portion)
    return tuple(result)


def used_size(section):
    return sum((math.prod(entry_shape) for entry_name, entry_shape in section_shapes(section)))


def batch_pass(reals, inputs, gate, targets, picks):
    pieces = [unpack(reals[section], section) for section in range(4)]
    wide_f, narrow_f, rows_0, _ = front_forward(pieces[0], inputs)
    wide_0, narrow_0 = to_low(wide_f), to_low(narrow_f)
    ending_1, rows_1, kept_1 = join_forward(pieces[1], wide_0, narrow_0)
    wide_1 = to_low(ending_1)
    narrow_f, rows_2, _ = split_forward(pieces[2], wide_1)
    narrow_2 = to_low(narrow_f)
    ending_3, rows_3, kept_3 = join_forward(pieces[3], wide_1, narrow_2)
    final = tuple(
        (
            jnp.where(gate > 0, end_part, relay_part.astype(jnp.float32))
            for end_part, relay_part in zip(ending_3, wide_1)
        )
    )
    cotangent = pool_grad(final, targets, picks)
    grad_wide, grad_narrow, grads_3 = join_grads(pieces[3], narrow_2, kept_3, cotangent, gate)
    grad_wide, grads_2 = split_backward(
        pieces[2], wide_1, to_high(to_low(grad_wide)), to_high(to_low(grad_narrow))
    )
    grad_wide, grad_narrow, grads_1 = join_grads(
        pieces[1], narrow_0, kept_1, to_high(to_low(grad_wide)), 1.0
    )
    grad_inputs, grads_0 = front_backward(
        pieces[0], inputs, to_high(to_low(grad_wide)), to_high(to_low(grad_narrow))
    )
    outs = (wide_0, wide_1, wide_1, to_low(final))
    stats = jnp.stack([rows_0, rows_1, rows_2 * gate, rows_3 * gate])
    return (outs, stats, to_low(grad_inputs), (grads_0, grads_1, grads_2, grads_3))


def on_device(
    teach_in,
    stud_in,
    params,
    owners,
    depth_gates,
    teach_ids,
    stud_ids,
    targets,
    moment,
    second,
    gram_stats,
    eigen_basis,
):
    sections = lax.axis_size("pipe")
    rank = lax.axis_index("pipe")
    owner_count = lax.axis_size("dp")
    span_size = params.shape[1]
    flat_size = span_size * owner_count
    owner_rows = lax.all_gather(owners, "pipe", axis=0, tiled=True)
    gathered = lax.all_gather(params[0].astype(jnp.bfloat16), ("pipe", "dp"), axis=0)
    gathered = gathered.reshape(sections, owner_count, span_size)
    reals = []
    for section in range(sections):
        inverse = jnp.argsort(owner_rows[section]).astype(jnp.int32)
        blocks = -(-used_size(section) // span_size)
        reals.append(gathered[section][inverse[:blocks]].reshape(blocks * span_size))
    inputs = (teach_in[0], stud_in[0])
    gate = depth_gates[rank].astype(jnp.float32)
    outs, stats, (teach_grad, stud_grad), grads = batch_pass(
        reals, inputs, gate, targets, (teach_ids[rank], stud_ids[rank])
    )
    segment_teach = lax.all_to_all(
        jnp.stack([part[0] for part in outs]), "pipe", split_axis=0, concat_axis=0, tiled=True
    )
    segment_stud = lax.all_to_all(
        jnp.stack([part[1] for part in outs]), "pipe", split_axis=0, concat_axis=0, tiled=True
    )
    stats = lax.all_to_all(stats, "pipe", split_axis=0, concat_axis=0, tiled=True)
    rows = []
    for section in range(sections):
        flat = pack(grads[section], section, flat_size).reshape(owner_count, span_size)
        rows.append(flat[owner_rows[section]])
    span_total = lax.psum_scatter(
        jnp.stack(rows).reshape(sections * owner_count, span_size),
        ("pipe", "dp"),
        scatter_dimension=0,
        tiled=True,
    ).reshape(span_size)
    total_squares = lax.psum(jnp.sum(span_total * span_total), ("dp", "pipe"))
    grad_norm = jnp.sqrt(total_squares)
    factor = jnp.minimum(1.0, CLIP_NORM / grad_norm)
    clipped = span_total * factor
    matrix = clipped.reshape(span_size // 128, 128)
    gram_old = gram_stats[0]
    basis_old = eigen_basis[0]
    gram_new = DECAY_STATS * gram_old + (1.0 - DECAY_STATS) * jnp.dot(
        matrix.T, matrix, precision=HIGH
    )
    product = jnp.dot(gram_new, basis_old, precision=HIGH)
    rotation = product / jnp.sqrt(jnp.sum(product * product))
    for repeat in range(NS_STEPS):
        square = jnp.dot(rotation.T, rotation, precision=HIGH)
        rotation = 1.5 * rotation - 0.5 * jnp.dot(rotation, square, precision=HIGH)
    moment_old = moment.reshape(span_size // 128, 128)
    initial = jnp.dot(moment_old, basis_old.T, precision=HIGH)
    blended = DECAY_FIRST * initial + (1.0 - DECAY_FIRST) * matrix
    moment_new = jnp.dot(blended, rotation, precision=HIGH)
    rotated = jnp.dot(matrix, rotation, precision=HIGH)
    second_new = (
        DECAY_SECOND * second.reshape(span_size // 128, 128)
        + (1.0 - DECAY_SECOND) * rotated * rotated
    )
    correction = math.sqrt(1.0 - DECAY_SECOND**STEP) / (1.0 - DECAY_FIRST**STEP)
    direction = (
        jnp.dot(moment_new / (jnp.sqrt(second_new) + ADAM_EPS), rotation.T, precision=HIGH)
        * correction
    )
    weights = params.reshape(span_size // 128, 128)
    params_new = weights - LEARN_RATE * (direction + WEIGHT_DECAY * weights)
    return (
        segment_teach[None],
        segment_stud[None],
        teach_grad[None],
        stud_grad[None],
        stats[None, :, None],
        grad_norm,
        clipped.reshape(1, span_size),
        moment_new.reshape(1, span_size),
        second_new.reshape(1, span_size),
        params_new.reshape(1, span_size),
        gram_new[None],
        rotation[None],
    )


MESH = pl.DeviceIdType.MESH
LOW = jnp.bfloat16
FULL = jnp.float32
TILE = 256
WINDOW = 20
STRIDE = 19
EDGE = 64
BIG_ROWS = STRIDE * TILE + EDGE
VEC_TILE = (152, 32, 104, 32)
USED_TILES = (153, 33, 105, 33)
FRONT_WIDE = 88
SMALL_ROWS = 1056
ROWS = 120
PADDED = 128
STUD_ROWS = 48
TEACH_END = 80


def any_spec():
    return pl.BlockSpec(memory_space=pl.ANY)


def smem_spec():
    return pl.BlockSpec(memory_space=pltpu.SMEM)


def vmem_spec():
    return pl.BlockSpec(memory_space=pltpu.VMEM)


def tile_forms(section, tile):
    even = lax.rem(section, 2) == 0
    vector = jnp.where(section == 0, 152, jnp.where(section == 2, 104, 32))
    narrow_end = jnp.where(section == 0, FRONT_WIDE, jnp.where(section == 2, 104, 0))
    narrow = even & (tile < narrow_end)
    plain = tile == vector
    return narrow, plain


def prepare_kernel(owners, params, big, small, ids, flat, sem):
    block, section = owners[0, lax.axis_index("dp")], lax.axis_index("pipe")

    even = lax.rem(section, 2) == 0
    flat[0:EDGE, :] = jnp.zeros((EDGE, 128), FULL)
    flat[STRIDE * TILE : WINDOW * TILE, :] = jnp.zeros((TILE, 128), FULL)
    copy = pltpu.make_async_copy(params.at[:, 0, :], flat.at[pl.ds(6 * block, params.shape[0])], sem)
    copy.start()

    @pl.when(jnp.logical_not(even))
    def _():
        @pl.loop(0, small.shape[0])
        def _(r):
            small[r] = jnp.zeros((TILE, 128), LOW)

    lane = lax.broadcasted_iota(jnp.int32, (8, 128), 1)
    row = jnp.zeros((8, 128), jnp.int32)
    for j in range(8):
        row = jnp.where(lane == j, owners[0, j], row)
    ids[...] = row
    copy.wait()

    def wide_tile(base):
        return [flat[pl.ds(base + j, 16, 16), :].astype(LOW) for j in range(16)]

    @pl.when(even)
    def _():
        @pl.loop(0, STRIDE)
        def _(r):
            narrow, plain = tile_forms(section, STRIDE * block + r)
            base = pl.multiple_of(TILE * r, TILE)

            @pl.when(narrow)
            def _():
                for j in range(4):
                    big[pl.ds(base + 64 * j, 64), :] = flat[pl.ds(base + j, 64, 4), :].astype(LOW)

            @pl.when(plain)
            def _():
                big[pl.ds(base, TILE), :] = flat[pl.ds(base, TILE), :].astype(LOW)

            @pl.when(jnp.logical_not(narrow | plain))
            def _():
                for j, part in enumerate(wide_tile(base)):
                    big[pl.ds(base + 16 * j, 16), :] = part

        big[STRIDE * TILE : BIG_ROWS, :] = flat[STRIDE * TILE : BIG_ROWS, :].astype(LOW)

    @pl.when(jnp.logical_not(even))
    def _():
        @pl.loop(0, WINDOW)
        def _(r):
            tile = STRIDE * block + r
            base = pl.multiple_of(TILE * r, TILE)

            @pl.when(tile == VEC_TILE[1])
            def _():
                small[tile] = flat[pl.ds(base, TILE), :].astype(LOW)

            @pl.when(tile < VEC_TILE[1])
            def _():
                for j, part in enumerate(wide_tile(base)):
                    small[tile, 16 * j : 16 * j + 16, :] = part


def prepare(owners, params):
    return pl.pallas_call(
        prepare_kernel,
        name="prepare",
        out_shape=(
            jax.ShapeDtypeStruct((BIG_ROWS, 128), LOW),
            jax.ShapeDtypeStruct((USED_TILES[1], TILE, 128), LOW),
            jax.ShapeDtypeStruct((8, 128), jnp.int32),
        ),
        in_specs=[smem_spec(), any_spec()],
        out_specs=(vmem_spec(),) * 3,
        scratch_shapes=[pltpu.VMEM((WINDOW * TILE, 128), FULL), pltpu.SemaphoreType.DMA],
        compiler_params=pltpu.CompilerParams(vmem_limit_bytes=60 << 20),
    )(owners, params.reshape(-1, 1, 128))


class Place:
    def __init__(self):
        self.dp = lax.axis_index("dp")
        self.pipe = lax.axis_index("pipe")
        self.x, self.core = self.pipe // 2, self.pipe % 2
        self.z, self.y = self.dp // 2, self.dp % 2

    def device(self, x=None, core=None, z=None, y=None):
        x = self.x if x is None else x
        core = self.core if core is None else core
        z = self.z if z is None else z
        y = self.y if y is None else y
        return {"dp": 2 * z + y, "pipe": 2 * x + core}

    def enter(self):
        barrier = pltpu.get_barrier_semaphore()
        for step in range(1, 8):
            other = lax.rem(self.dp + step, 8)
            pl.semaphore_signal(
                barrier, inc=1, device_id={"dp": other, "pipe": self.pipe}, device_id_type=MESH
            )
        for step in range(1, 4):
            other = lax.rem(self.pipe + step, 4)
            pl.semaphore_signal(
                barrier, inc=1, device_id={"dp": self.dp, "pipe": other}, device_id_type=MESH
            )
        pl.semaphore_wait(barrier, 10)


def remote(src, dst, send, recv, target):
    return pltpu.make_async_remote_copy(
        src_ref=src, dst_ref=dst, send_sem=send, recv_sem=recv, device_id=target, device_id_type=MESH
    )


BIG_HALF = BIG_ROWS // 2
SMALL_HALF = SMALL_ROWS // 2
PARTS = 2
PART_ROWS = BIG_HALF // PARTS
BULK_CUT = 480
LIGHT_CUT = 256
BACK_CUT = 768
GATHER_ORDER = (
    "X1", "Z2", "X2", "Y0", "EY", "EC0", "EC1", "R0", "Z3", "Y1", "Z4", "Y2", "X3", "EC2", "R1",
    "EC3", "Y3", "L0", "X4", "Z5", "L1", "Z6", "X5", "S0", "S1", "R2", "Y4", "Y5", "S2", "L2",
    "Y6", "R3", "Z7", "X6", "Y7", "M1", "S3", "S4", "R4", "X7", "D0", "D1", "S5", "S6", "R5", "M2",
    "R6", "D2", "S7", "D3", "R7", "D4", "D5", "M3", "D6", "D7",
)
REDUCE_ORDER = (
    "A0", "A1", "A2", "A3", "A4", "A5", "L0", "B0", "C0", "C1", "B1", "B2", "B3", "C2", "L1", "L2",
    "A6", "L3", "B4", "C3", "O0", "LS", "A7", "O1", "B5", "B6", "E0", "C4", "O2", "O3", "E1", "E2",
    "C5", "C6", "I0", "B7", "LE", "C7", "I1", "E3", "T1", "I2", "I3", "O4", "O5", "G", "T2", "E4",
    "I4", "O6", "I5", "E5", "O7", "T3",
)


def gather_kernel(big, small, ids, all_big, all_small, table, held_big, held_small, k_sem, big_sem, early, chunk, rising, falling,
                  early_send, early_recv, eu_send, eu_recv, ed_send, ed_recv,
                  z_send, z_recv, x_send, x_recv, y_send, y_recv, dx_send, dx_recv, dy_send, dy_recv,
                  s_send, s_recv, first_send, first_recv, own_sem, id_send, id_recv, lz_send, lz_recv):
    me = Place()
    me.enter()
    x, y, z, core = me.x, me.y, me.z, me.core
    up, down = me.device(z=z + 1), me.device(z=z - 1)
    x_side, y_side, sibling = me.device(x=1 - x), me.device(y=1 - y), me.device(core=1 - core)

    class Stream:
        def __init__(self, n, held, out, start, rows, cut):
            self.n, self.held, self.out, self.start, self.rows, self.cut = n, held, out, start, rows, cut

        def block(self, xo, origin, yo):
            return self.held.at[xo, 2 * origin + yo, pl.ds(self.start, self.rows)]

        def move_x(self, origin):
            block = self.block(x, origin, y)
            return remote(block, block, x_send.at[self.n, origin], x_recv.at[self.n, origin], x_side)

        def move_y(self, origin):
            block = self.block(x, origin, y)
            return remote(block, block, y_send.at[self.n, origin], y_recv.at[self.n, origin], y_side)

        def copies(self, xo, origin, yo):
            block, at = self.block(xo, origin, yo), 8 * xo + 2 * origin + yo
            result = self.out.at[xo, 2 * origin + yo, core, pl.ds(self.start, self.rows)]
            return (
                remote(block, result, s_send.at[self.n, at], s_recv.at[self.n, at], sibling),
                pltpu.make_async_copy(block, result, k_sem.at[self.n, at]),
            )

        def share(self, xo, origin, yo):
            for copy in self.copies(xo, origin, yo):
                copy.start()

        def move_z(self, origin, target, way):
            block = self.block(x, origin, y)
            return remote(block, block, z_send.at[self.n, way, origin], z_recv.at[self.n, origin], target)

        def half_x(self, origin, xo, yo):
            part = self.held.at[xo, 2 * origin + yo, pl.ds(self.start + self.cut, self.rows - self.cut)]
            return remote(part, part, dx_send.at[self.n, origin], dx_recv.at[self.n, origin], x_side)

        def half_y(self, origin, xo, yo):
            part = self.held.at[xo, 2 * origin + yo, pl.ds(self.start, self.cut)]
            return remote(part, part, dy_send.at[self.n, origin], dy_recv.at[self.n, origin], y_side)

        def to_x(self, origin):
            self.move_x(origin).start()

        def to_y(self, origin):
            self.move_y(origin).start()

        def from_x(self, origin):
            self.move_x(origin).wait_recv()
            self.half_y(origin, 1 - x, y).start()
            self.share(1 - x, origin, y)

        def from_y(self, origin):
            self.move_y(origin).wait_recv()
            self.half_x(origin, x, 1 - y).start()
            self.share(x, origin, 1 - y)

        def from_diagonal(self, origin):
            self.half_x(origin, 1 - x, 1 - y).wait_recv()
            self.half_y(origin, 1 - x, 1 - y).wait_recv()
            self.share(1 - x, origin, 1 - y)

        def each(self, step, action):
            if step == 0:
                action(z)
            else:
                pl.when(z >= step)(lambda: action(z - step))
                pl.when(z + step <= 3)(lambda: action(z + step))

        def begin(self):
            pl.when(z < 3)(lambda: self.move_z(z, up, 0).start())
            pl.when(z > 0)(lambda: self.move_z(z, down, 1).start())
            self.share(x, z, y)

        def from_z(self, k):
            @pl.when(z >= k)
            def _():
                self.move_z(z - k, up, 0).wait_recv()
                pl.when(z < 3)(lambda: self.move_z(z - k, up, 0).start())
                self.share(x, z - k, y)

            @pl.when(z + k <= 3)
            def _():
                self.move_z(z + k, down, 1).wait_recv()
                pl.when(z > 0)(lambda: self.move_z(z + k, down, 1).start())
                self.share(x, z + k, y)

        def close(self):
            for origin in range(4):
                self.move_x(origin).wait_send()
                self.move_y(origin).wait_send()
                self.half_x(origin, x, 1 - y).wait_send()
                self.half_y(origin, 1 - x, y).wait_send()
                pl.when((z < 3) & (origin <= z))(lambda: self.move_z(origin, up, 0).wait_send())
                pl.when((z > 0) & (origin >= z))(lambda: self.move_z(origin, down, 1).wait_send())
            self.close_shares()

        def close_shares(self):
            for origin in range(4):
                for xo in range(2):
                    for yo in range(2):
                        away, home = self.copies(xo, origin, yo)
                        away.wait_send()
                        home.wait()
                        theirs = self.out.at[xo, 2 * origin + yo, 1 - core, pl.ds(self.start, self.rows)]
                        at = 8 * xo + 2 * origin + yo
                        remote(theirs, theirs, s_send.at[self.n, at], s_recv.at[self.n, at], sibling).wait_recv()

    class Late(Stream):
        def column_z(self, xo, origin, yo, target, way):
            block = self.block(xo, origin, yo)
            at = 2 * xo + yo
            return remote(
                block, block, lz_send.at[way, at, origin], lz_recv.at[at, origin], target
            )

        def leave(self, xo, yo):
            pl.when(z < 3)(lambda: self.column_z(xo, z, yo, up, 0).start())
            pl.when(z > 0)(lambda: self.column_z(xo, z, yo, down, 1).start())
            self.share(xo, z, yo)

        def step(self, k):
            if k == 0:
                self.move_x(z).start()
                self.move_y(z).start()
                self.leave(x, y)
            elif k == 1:
                self.move_x(z).wait_recv()
                self.half_y(z, 1 - x, y).start()
                self.leave(1 - x, y)
                self.move_y(z).wait_recv()
                self.half_x(z, x, 1 - y).start()
                self.leave(x, 1 - y)
            elif k == 2:
                self.half_x(z, 1 - x, 1 - y).wait_recv()
                self.half_y(z, 1 - x, 1 - y).wait_recv()
                self.leave(1 - x, 1 - y)
            else:
                gap = k - 2

                @pl.when(z >= gap)
                def _():
                    for xo, yo in columns:
                        self.column_z(xo, z - gap, yo, up, 0).wait_recv()
                        pl.when(z < 3)(lambda: self.column_z(xo, z - gap, yo, up, 0).start())
                        self.share(xo, z - gap, yo)

                @pl.when(z + gap <= 3)
                def _():
                    for xo, yo in columns:
                        self.column_z(xo, z + gap, yo, down, 1).wait_recv()
                        pl.when(z > 0)(lambda: self.column_z(xo, z + gap, yo, down, 1).start())
                        self.share(xo, z + gap, yo)

        def close(self):
            self.move_x(z).wait_send()
            self.move_y(z).wait_send()
            self.half_x(z, x, 1 - y).wait_send()
            self.half_y(z, 1 - x, y).wait_send()
            for origin in range(4):
                for xo, yo in columns:
                    pl.when((z < 3) & (origin <= z))(
                        lambda: self.column_z(xo, origin, yo, up, 0).wait_send())
                    pl.when((z > 0) & (origin >= z))(
                        lambda: self.column_z(xo, origin, yo, down, 1).wait_send())
            self.close_shares()

    columns = ((x, y), (1 - x, y), (x, 1 - y), (1 - x, 1 - y))
    bulks = [
        Stream(n, held_big, all_big, PART_ROWS * n, PART_ROWS, BULK_CUT) for n in range(PARTS)
    ]
    light = Late(PARTS, held_small, all_small, 0, SMALL_HALF, LIGHT_CUT)

    order = [
        jnp.where(z < 2, 3, 0),
        jnp.where(z == 0, 2, jnp.where(z == 1, 0, jnp.where(z == 2, 3, 1))),
        jnp.where(z == 0, 1, jnp.where(z == 1, 2, jnp.where(z == 2, 1, 2))),
        z,
    ]

    def cross(k):
        return remote(small.at[2 * order[k] + (1 - y)], early.at[k], early_send.at[k], early_recv.at[k], y_side)

    def own_early(k):
        return pltpu.make_async_copy(small.at[2 * order[k] + y], chunk.at[k], own_sem.at[3 + k])

    def rise(k):
        slot = order[k] - 1
        return remote(chunk.at[k], rising.at[slot], eu_send.at[slot], eu_recv.at[slot], up)

    def fall(k):
        slot = order[k]
        return remote(chunk.at[k], falling.at[slot], ed_send.at[slot], ed_recv.at[slot], down)

    def merge(k, ref, slot):
        @pl.loop(0, 3)
        def _(i):
            part = pl.ds(pl.multiple_of(352 * i, 16), 352)
            chunk[k, part, :] = (chunk[k, part, :].astype(FULL) + ref[slot, part, :].astype(FULL)).astype(LOW)

    def big_part(n):
        return held_big.at[x, me.dp, pl.ds(PART_ROWS * n, PART_ROWS)]

    def big_first(n):
        source = big.at[pl.ds(BIG_HALF + PART_ROWS * n, PART_ROWS)]
        return remote(source, big_part(n), first_send.at[n], first_recv.at[n], sibling)

    def big_own(n):
        return pltpu.make_async_copy(big.at[pl.ds(PART_ROWS * n, PART_ROWS)], big_part(n), big_sem.at[n])

    small_half = held_small.at[x, me.dp]
    small_first = remote(
        chunk.at[3, pl.ds(0, SMALL_HALF)], small_half, first_send.at[PARTS], first_recv.at[PARTS], sibling)

    def early_cross():
        @pl.when(core == 1)
        def _():
            for k in range(4):
                own_early(k).wait()
                cross(k).wait_recv()
                merge(k, early, k)

    def early_chain(k):
        @pl.when(core == 1)
        def _():
            if k < 3:

                @pl.when(order[k] > z)
                def _():
                    @pl.when(z > 0)
                    def _():
                        rise(k).wait_recv()
                        merge(k, rising, order[k] - 1)

                    rise(k).start()

                @pl.when(order[k] < z)
                def _():
                    @pl.when(z < 3)
                    def _():
                        fall(k).wait_recv()
                        merge(k, falling, order[k])

                    fall(k).start()

            else:

                @pl.when(z > 0)
                def _():
                    rise(k).wait_recv()
                    merge(k, rising, z - 1)

                @pl.when(z < 3)
                def _():
                    fall(k).wait_recv()
                    merge(k, falling, z)

                small_first.start()
                copy = pltpu.make_async_copy(
                    chunk.at[3, pl.ds(SMALL_HALF, SMALL_HALF)], small_half, own_sem.at[0])
                copy.start()
                copy.wait()

    def light_begin():
        @pl.when(core == 0)
        def _():
            small_first.wait_recv()

        light.step(0)

    @pl.when(core == 0)
    def _():
        for n in range(PARTS):
            big_first(n).start()
            big_own(n).start()

    @pl.when(core == 1)
    def _():
        for k in range(4):
            cross(k).start()
            own_early(k).start()

    for n in range(PARTS):
        pl.when(core == 0)(lambda: big_own(n).wait())
        pl.when(core == 1)(lambda: big_first(n).wait_recv())
        bulks[n].begin()
        if n == 0:
            bulks[n].to_x(z)
    row = pltpu.make_async_copy(ids, table.at[me.pipe], own_sem.at[2])
    row.start()
    for step in range(1, 4):
        remote(
            ids, table.at[me.pipe], id_send.at[step], id_recv.at[step],
            {"dp": me.dp, "pipe": lax.rem(me.pipe + step, 4)},
        ).start()

    actions = {"EY": early_cross, "L0": light_begin}
    for k in range(4):
        actions["EC%d" % k] = functools.partial(early_chain, k)
        if k:
            actions["M%d" % k] = functools.partial(light.step, k + 2)
            if k < 3:
                actions["L%d" % k] = functools.partial(light.step, k)
        for n, bulk in enumerate(bulks):
            name = str(PARTS * k + n)
            for letter, action in zip("XYSRD", (bulk.to_x, bulk.to_y, bulk.from_x, bulk.from_y, bulk.from_diagonal)):
                actions[letter + name] = functools.partial(bulk.each, k, action)
            if k:
                actions["Z" + name] = functools.partial(bulk.from_z, k)
    for event in GATHER_ORDER:
        actions[event]()
    for bulk in bulks:
        bulk.close()
    light.close()
    row.wait()
    for step in range(1, 4):
        here = lax.rem(me.pipe + 4 - step, 4)
        move = remote(
            ids, table.at[here], id_send.at[step], id_recv.at[step],
            {"dp": me.dp, "pipe": lax.rem(me.pipe + step, 4)},
        )
        move.wait_recv()
        move.wait_send()

    @pl.when(core == 0)
    def _():
        for n in range(PARTS):
            big_first(n).wait_send()

    @pl.when(core == 1)
    def _():
        small_first.wait_send()
        for k in range(4):
            cross(k).wait_send()
        for k in range(3):
            pl.when(order[k] > z)(lambda: rise(k).wait_send())
            pl.when(order[k] < z)(lambda: fall(k).wait_send())


def gather_all(big, small, ids):
    sem = pltpu.SemaphoreType.DMA
    return pl.pallas_call(
        gather_kernel,
        name="gather_all",
        out_shape=(
            jax.ShapeDtypeStruct((2, 8, 2, BIG_HALF, 128), LOW),
            jax.ShapeDtypeStruct((2, 8, 2, SMALL_HALF, 128), LOW),
            jax.ShapeDtypeStruct((4, 8, 128), jnp.int32),
        ),
        in_specs=[any_spec()] * 3,
        out_specs=(any_spec(),) * 3,
        scratch_shapes=[
            pltpu.VMEM((2, 8, BIG_HALF, 128), LOW), pltpu.VMEM((2, 8, SMALL_HALF, 128), LOW),
            sem((PARTS + 1, 16)), sem((PARTS,)),
            pltpu.VMEM((4, SMALL_ROWS, 128), LOW), pltpu.VMEM((4, SMALL_ROWS, 128), LOW),
            pltpu.VMEM((3, SMALL_ROWS, 128), LOW), pltpu.VMEM((3, SMALL_ROWS, 128), LOW),
            sem((4,)), sem((4,)), sem((3,)), sem((3,)), sem((3,)), sem((3,)),
            sem((PARTS + 1, 2, 4)), sem((PARTS + 1, 4)),
            sem((PARTS + 1, 4)), sem((PARTS + 1, 4)), sem((PARTS + 1, 4)), sem((PARTS + 1, 4)),
            sem((PARTS + 1, 4)), sem((PARTS + 1, 4)), sem((PARTS + 1, 4)), sem((PARTS + 1, 4)),
            sem((PARTS + 1, 16)), sem((PARTS + 1, 16)),
            sem((PARTS + 1,)), sem((PARTS + 1,)), sem((7,)), sem((4,)), sem((4,)),
            sem((2, 4, 4)), sem((4, 4)),
        ],
        compiler_params=pltpu.CompilerParams(
            collective_id=0, has_side_effects=True, vmem_limit_bytes=60 << 20
        ),
    )(big, small.reshape(8, SMALL_ROWS, 128), ids)


def soft(value):
    return jnp.maximum(value, 0.0) + jnp.log1p(jnp.exp(-jnp.abs(value)))


def gate_of(value):
    small = jnp.exp(-jnp.abs(value))
    share = 1.0 / (1.0 + small)
    return jnp.where(value >= 0, share, small * share)


def standardize(z):
    count = z.shape[0]
    centre = jnp.sum(z, axis=0, keepdims=True) / count
    away = z - centre
    spread = jnp.sum(away * away, axis=0, keepdims=True) / count
    inverse = lax.rsqrt(spread + NORM_EPS)
    return away * inverse, centre, spread, inverse


def unstandardize(grad, standard, gain, inverse):
    count = grad.shape[0]
    grad_sum = jnp.sum(grad, axis=0, keepdims=True)
    grad_dot = jnp.sum(grad * standard, axis=0, keepdims=True)
    result = gain * inverse * (grad - grad_sum / count - standard * (grad_dot / count))
    return result, grad_dot, grad_sum


def pad_low(value):
    zeros = jnp.zeros((PADDED - ROWS, value.shape[1]), FULL)
    return jnp.concatenate([value, zeros], axis=0).astype(LOW)


def mul(a, b):
    return jnp.dot(a, b, preferred_element_type=FULL)


def mul_t(a, b):
    return lax.dot_general(a, b, (((1,), (1,)), ((), ())), preferred_element_type=FULL)


def narrow_part(ref, start, count, blocks=range(4)):
    return jnp.concatenate(
        [ref[pl.ds(start, count), 64 * j : 64 * j + 64, :].reshape(64 * count, 128) for j in blocks],
        axis=1,
    )


def put_narrow(ref, start, count, value):
    for j in range(4):
        ref[pl.ds(start, count), 64 * j : 64 * j + 64, :] = (
            value[:, 128 * j : 128 * j + 128].astype(LOW).reshape(count, 64, 128)
        )


def wide_part(ref, start, count, c):
    return jnp.concatenate(
        [
            ref[start : start + count, 32 * c + 16 * h : 32 * c + 16 * h + 16, :].reshape(
                16 * count, 128
            )
            for h in range(2)
        ],
        axis=1,
    )


def put_wide(ref, start, count, c, value):
    for h in range(2):
        ref[start : start + count, 32 * c + 16 * h : 32 * c + 16 * h + 16, :] = (
            value[:, 128 * h : 128 * h + 128].astype(LOW).reshape(count, 16, 128)
        )


def chunks(count):
    def run(body):
        for c in range(count):
            body(c)

    return run


def step_kernel(table, gates, teach_ids, stud_ids, all_big, all_small, teach_x, stud_x, targets, grid,
                moves,
                wide0, wide1, final, stats, grad_teach, grad_stud, out_big, out_small,
                x,
                w0, w1, w2, w3, edges, loose, vec, grad_vec, raw,
                std_a, std_b, std_p, std_1, std_c, std_d, hidden, cols0, cols2,
                nar0, nar2, turned, turned_x, relay, dz_a, dz_n, acc, acc_x, grad_h,
                wanted, inv, in_sem, edge_sem, out_sem):
    rank = lax.axis_index("pipe")
    gate = gates[rank].astype(FULL)
    for group in range(2):
        for j in range(8):
            inv[8 * group + table[2 * group, 0, j]] = j
    picks = [teach_ids[k, rank] for k in range(2)] + [stud_ids[rank, k] for k in range(3)]
    rows = [
        pltpu.make_async_copy(targets.at[pl.ds(pick, 1)], wanted.at[pl.ds(k, 1)], edge_sem.at[12 + k])
        for k, pick in enumerate(picks)
    ]
    for fetched in rows:
        fetched.start()
    weights = (w0, w1, w2, w3)
    loads = {0: [], 1: [], 2: [], 3: []}
    front, split = w0.reshape(USED_TILES[0] * TILE, 128), w2.reshape(115 * TILE, 128)
    for group, weight, blocks in ((0, front, 8), (1, split, 6)):
        for b in range(blocks):
            at, here = 8 * group + b, inv[8 * group + b]
            count = min(STRIDE, VEC_TILE[2 * group] + 1 - STRIDE * b) * TILE
            loads[2 * group].append(pltpu.make_async_copy(
                all_big.at[group, here, pl.ds(0, count)], weight.at[pl.ds(STRIDE * TILE * b, count)],
                in_sem.at[0, at]))
            if b < blocks - 1:
                loads[2 * group].append(pltpu.make_async_copy(
                    all_big.at[group, here, pl.ds(STRIDE * TILE, EDGE)], edges.at[7 * group + b],
                    edge_sem.at[7 * group + b]))
            elif group == 0:
                loads[0].append(pltpu.make_async_copy(
                    all_big.at[0, here, pl.ds(STRIDE * TILE, EDGE)],
                    front.at[pl.ds(VEC_TILE[0] * TILE, EDGE)], edge_sem.at[17]))
    loads[1].append(pltpu.make_async_copy(all_small.at[0], w1, in_sem.at[0, 14]))
    loads[3].append(pltpu.make_async_copy(all_small.at[1], w3, in_sem.at[0, 15]))
    for section in range(4):
        for load in loads[section]:
            load.start()

    raw[...] = jnp.zeros_like(raw)
    loose[...] = jnp.zeros_like(loose)
    grad_vec[...] = jnp.zeros_like(grad_vec)

    def edge_parts(tile, is_narrow):
        count, size = (4, 64) if is_narrow else (16, 16)
        for j in range(count):
            yield pl.ds(j, 16, count), slice(size * j, size * j + 16)

    def is_narrow(section, tile):
        return section == 2 or tile < FRONT_WIDE

    def merge_edge(section, tile, at):
        ref = weights[section]
        loose[0:EDGE, :] = edges[at].astype(FULL)
        for lying, here in edge_parts(tile, is_narrow(section, tile)):
            ref[tile, here, :] = (ref[tile, here, :].astype(FULL) + loose[lying, :]).astype(LOW)

    def take_edge(section, tile, at):
        ref = weights[section]
        for lying, here in edge_parts(tile, is_narrow(section, tile)):
            loose[lying, :] = ref[tile, here, :].astype(FULL)
        edges[at] = loose[0:EDGE, :].astype(LOW)

    def settle(section, blocks=None):
        if section == 0:
            for b in blocks:
                for load in loads[0][2 * b : 2 * b + 2]:
                    load.wait()
            if 7 in blocks:
                vec[0] = w0[VEC_TILE[0], 0:48, :].astype(FULL)
            else:
                for b in range(7):
                    merge_edge(0, 19 * b + 19, b)
            return
        for load in loads[section]:
            load.wait()
        if section == 2:
            for b in range(5):
                merge_edge(2, 19 * b + 19, 7 + b)
        vec[section] = weights[section][VEC_TILE[section], 0:48, :].astype(FULL)

    def row(section, start):
        return jnp.concatenate(
            [vec[section, pl.ds(start + h, 1), :] for h in range(2)], axis=1
        )

    def put_row(section, start, value):
        for h in range(2):
            grad_vec[section, pl.ds(start + h, 1), :] = value[:, 128 * h : 128 * h + 128]

    def put_stats(section, column, centre, spread):
        raw[2 * section : 2 * section + 1, pl.ds(column, 256)] = centre
        raw[2 * section + 1 : 2 * section + 2, pl.ds(column, 256)] = spread

    def inverse_of(section, column):
        return lax.rsqrt(raw[2 * section + 1 : 2 * section + 2, pl.ds(column, 256)] + NORM_EPS)

    def lanes(c):
        return slice(256 * c, 256 * c + 256)

    at_row, at_col, side = grid[0], grid[1], grid[2]

    def masked(value, dr, dc):
        ok = (at_row + dr >= 0) & (at_row + dr < side) & (at_col + dc >= 0) & (at_col + dc < side)
        return jnp.concatenate(
            [jnp.where(ok, value[:, 128 * j : 128 * j + 128], 0.0) for j in range(4)], axis=1
        )

    def rolled(value, sign, dr, dc):
        parts = []
        for start, end, across, down in ((0, STUD_ROWS, 1, 4), (STUD_ROWS, ROWS, 2, 12)):
            by = (sign * (dr * down + dc * across)) % (end - start)
            part = value[start:end]
            parts.append(part if by == 0 else pltpu.roll(part, by, 0))
        return jnp.concatenate(parts, axis=0)

    def taps(stride):
        for t in range(9):
            r, q = t // 3, t % 3
            if stride == 1:
                yield t, 0, r - 1, q - 1
            else:
                phase = 2 * (1 if r != 1 else 0) + (1 if q != 1 else 0)
                yield t, phase, -1 if r == 0 else 0, -1 if q == 0 else 0

    def one_hot(index, width):
        lane = lax.broadcasted_iota(jnp.int32, index.shape, 1)
        parts = [jnp.where(lane + start == index, 1.0, 0.0) for start in range(0, width, 128)]
        return jnp.concatenate(parts, axis=1)[:, 0:width].astype(LOW)

    for p in range(4):
        at = slice(PADDED * p, PADDED * p + PADDED)
        from_teach = mul(one_hot(moves[0, at, :], teach_x.shape[0]), teach_x[...])
        x[p] = (from_teach + mul(one_hot(moves[1, at, :], stud_x.shape[0]), stud_x[...])).astype(LOW)

    settle(0, (0, 7))
    whole_x = x[...].reshape(4 * PADDED, C_IN)
    for c in range(2):
        z = mul(whole_x, narrow_part(w0, 0, 16, (2 * c, 2 * c + 1)))
        z = jnp.concatenate([z[PADDED * p : PADDED * p + ROWS] for p in range(4)], axis=0)
        standard, centre, spread, _ = standardize(z)
        put_stats(0, 256 * c, centre, spread)
        std_a[:, 256 * c : 256 * c + 256] = standard
        hidden[:, 256 * c : 256 * c + 256] = (
            soft(row(0, 2 * c) * standard + row(0, 4 + 2 * c)).astype(LOW).astype(FULL)
        )

    for t, phase, dr, dc in taps(2):
        cols0[t] = pad_low(masked(rolled(hidden[ROWS * phase : ROWS * phase + ROWS, :], -1, dr, dc), dr, dc))
    acc[...] = jnp.zeros_like(acc)
    settle(0, (1, 2, 3, 4, 5, 6))

    @chunks(9)
    def _(t):
        acc[...] += mul(cols0[t], narrow_part(w0, 16 + 8 * t, 8))

    def middle(section, std, nar):
        for c in range(2):
            at = slice(256 * c, 256 * c + 256)
            standard, centre, spread, _ = standardize(acc[0:ROWS, at])
            put_stats(section, MID + 256 * c, centre, spread)
            std[:, at] = standard
            nar[:, at] = pad_low(soft(row(section, 8 + 2 * c) * standard + row(section, 12 + 2 * c)))

    middle(0, std_b, nar0)
    acc[...] = jnp.zeros_like(acc)
    settle(1)
    settle(2)

    @chunks(8)
    def _(c):
        at = lanes(c)
        standard, centre, spread, _ = standardize(mul(x[0], wide_part(w0, FRONT_WIDE, 64, c))[0:ROWS])
        put_stats(0, 2 * MID + 256 * c, centre, spread)
        std_p[:, at] = standard
        low = pad_low(row(0, 16 + 2 * c) * standard + row(0, 32 + 2 * c))
        wide0[:, at] = low
        standard, centre, spread, _ = standardize(mul(nar0[...], wide_part(w1, 0, 32, c))[0:ROWS])
        put_stats(1, 256 * c, centre, spread)
        std_1[:, at] = standard
        pre = low.astype(FULL)[0:ROWS] + row(1, 2 * c) * standard + row(1, 16 + 2 * c)
        low = pad_low(soft(pre))
        wide1[:, at] = low
        acc[...] += mul(low, narrow_part(w2, 4 * c, 4))

    for c in range(2):
        at = slice(256 * c, 256 * c + 256)
        standard, centre, spread, _ = standardize(acc[0:ROWS, at])
        put_stats(2, 256 * c, centre, spread)
        std_c[:, at] = standard
        hidden[0:ROWS, at] = soft(row(2, 2 * c) * standard + row(2, 4 + 2 * c)).astype(LOW).astype(FULL)
    for t, phase, dr, dc in taps(1):
        cols2[t] = pad_low(masked(rolled(hidden[0:ROWS, :], -1, dr, dc), dr, dc))
    acc[...] = jnp.zeros_like(acc)

    @chunks(9)
    def _(t):
        acc[...] += mul(cols2[t], narrow_part(w2, 32 + 8 * t, 8))

    middle(2, std_d, nar2)

    turned[...] = nar2[...].T
    acc[...] = jnp.zeros_like(acc)
    settle(3)
    for fetched in rows:
        fetched.wait()

    teach_rows = ROWS - STUD_ROWS
    first_crop = lax.rem(lax.broadcasted_iota(jnp.int32, (teach_rows, 256), 0), 2) == 0

    def spread_rows(values):
        first, second = (jnp.broadcast_to(value, (teach_rows, 256)) for value in values[0:2])
        parts = [jnp.broadcast_to(value, (16, 256)) for value in values[2:5]]
        parts.append(jnp.where(first_crop, first, second))
        return jnp.concatenate(parts, axis=0)

    def crop_sums(value):
        def total(part):
            return jnp.sum(part, axis=0, keepdims=True)

        teach = value[STUD_ROWS:ROWS]
        return [
            total(jnp.where(first_crop, teach, 0.0)),
            total(jnp.where(first_crop, 0.0, teach)),
            total(value[0:16]),
            total(value[16:32]),
            total(value[32:48]),
        ]

    @chunks(8)
    def _(c):
        at = lanes(c)
        weight = wide_part(w3, 0, 32, c)
        standard, centre, spread, inverse = standardize(mul(nar2[...], weight)[0:ROWS])
        put_stats(3, 256 * c, centre, spread)
        gain = row(3, 2 * c)
        before = wide1[:, at].astype(FULL)[0:ROWS]
        pre = before + gain * standard + row(3, 16 + 2 * c)
        ending = jnp.where(gate > 0, soft(pre), before)
        final[:, at] = pad_low(ending)
        square = ending * ending
        factors = []
        for crop, total in enumerate(crop_sums(square * ending)):
            mean = total / (36.0 if crop < 2 else 16.0) + POOL_EPS
            factors.append(jnp.exp(jnp.log(mean) * (-2.0 / 3.0)) * wanted[crop : crop + 1, at])
        cotangent = spread_rows(factors) * square
        grad_pre = cotangent * gate_of(pre) * gate
        relay[:, at] = pad_low(grad_pre + cotangent * (1.0 - gate))
        result, grad_gain, grad_bias = unstandardize(grad_pre, standard, gain, inverse)
        put_row(3, 2 * c, grad_gain)
        put_row(3, 16 + 2 * c, grad_bias)
        low = pad_low(result)
        acc[...] += mul_t(low, weight)
        put_wide(w3, 0, 32, c, mul(turned[...], low))

    def flush(section):
        weights[section][VEC_TILE[section]] = grad_vec[section].astype(LOW)

    flush(3)
    stores = [pltpu.make_async_copy(w3, out_small.at[1], out_sem.at[16])]
    stores[-1].start()

    def middle_back(section, std):
        for c in range(2):
            at = slice(256 * c, 256 * c + 256)
            gain, bias = row(section, 8 + 2 * c), row(section, 12 + 2 * c)
            grad = acc[0:ROWS, at].astype(LOW).astype(FULL) * gate_of(gain * std[:, at] + bias)
            result, grad_gain, grad_bias = unstandardize(
                grad, std[:, at], gain, inverse_of(section, MID + 256 * c)
            )
            put_row(section, 8 + 2 * c, grad_gain)
            put_row(section, 12 + 2 * c, grad_bias)
            dz_n[:, at] = pad_low(result)

    def taps_back(weight, start, cols, stride, phases):
        grad_h[0 : ROWS * phases, :] = jnp.zeros((ROWS * phases, MID), FULL)
        for t, phase, dr, dc in taps(stride):
            part = mul_t(dz_n[...], narrow_part(weight, start + 8 * t, 8))[0:ROWS]
            at = slice(ROWS * phase, ROWS * phase + ROWS)
            grad_h[at, :] += rolled(masked(part, dr, dc), 1, dr, dc)
            put_narrow(weight, start + 8 * t, 8, mul(cols[t].T, dz_n[...]))

    middle_back(2, std_d)
    taps_back(w2, 32, cols2, 1, 1)
    for c in range(2):
        at = slice(256 * c, 256 * c + 256)
        gain, bias = row(2, 2 * c), row(2, 4 + 2 * c)
        grad = grad_h[0:ROWS, at] * gate_of(gain * std_c[:, at] + bias)
        result, grad_gain, grad_bias = unstandardize(grad, std_c[:, at], gain, inverse_of(2, 256 * c))
        put_row(2, 2 * c, grad_gain)
        put_row(2, 4 + 2 * c, grad_bias)
        dz_n[:, at] = pad_low(result)
    turned[...] = nar0[...].T
    turned_x[...] = x[0].T
    acc[...] = jnp.zeros_like(acc)
    acc_x[...] = jnp.zeros_like(acc_x)

    @chunks(8)
    def _(c):
        at = lanes(c)
        low = dz_n[...]
        grad = relay[:, at].astype(FULL) + mul_t(low, narrow_part(w2, 4 * c, 4))
        put_narrow(w2, 4 * c, 4, mul(wide1[:, at].T, low))
        grad = grad.astype(LOW).astype(FULL)[0:ROWS]
        gain = row(1, 2 * c)
        pre = wide0[:, at].astype(FULL)[0:ROWS] + gain * std_1[:, at] + row(1, 16 + 2 * c)
        grad = grad * gate_of(pre)
        result, grad_gain, grad_bias = unstandardize(
            grad, std_1[:, at], gain, inverse_of(1, 256 * c)
        )
        put_row(1, 2 * c, grad_gain)
        put_row(1, 16 + 2 * c, grad_bias)
        low = pad_low(result)
        acc[...] += mul_t(low, wide_part(w1, 0, 32, c))
        put_wide(w1, 0, 32, c, mul(turned[...], low))
        grad = grad.astype(LOW).astype(FULL)
        result, grad_gain, grad_bias = unstandardize(
            grad, std_p[:, at], row(0, 16 + 2 * c), inverse_of(0, 2 * MID + 256 * c)
        )
        put_row(0, 16 + 2 * c, grad_gain)
        put_row(0, 32 + 2 * c, grad_bias)
        low = pad_low(result)
        acc_x[...] += mul_t(low, wide_part(w0, FRONT_WIDE, 64, c))
        put_wide(w0, FRONT_WIDE, 64, c, mul(turned_x[...], low))

    flush(1)
    flush(2)
    w2[105:115] = jnp.zeros((10, TILE, 128), LOW)
    stores.append(pltpu.make_async_copy(w1, out_small.at[0], out_sem.at[17]))
    stores[-1].start()
    def store(source, group, b, start, semaphore):
        count = source.shape[0]
        stores.append(pltpu.make_async_copy(
            source, out_big.at[group, inv[8 * group + b], pl.ds(start, count)], out_sem.at[semaphore]))
        stores[-1].start()

    for b in range(8):
        if b < 5:
            take_edge(2, 19 * b + 19, 7 + b)
            store(split.at[pl.ds(STRIDE * TILE * b, STRIDE * TILE)], 1, b, 0, 8 + b)
            store(edges.at[7 + b], 1, b, STRIDE * TILE, 20 + b)
        else:
            first = 95 if b == 5 else 105
            store(split.at[pl.ds(TILE * first, 10 * TILE)], 1, b, 0, 8 + b)
            store(split.at[pl.ds(TILE * 105, BIG_ROWS - 10 * TILE)], 1, b, 10 * TILE, 20 + b)

    def store_front(blocks):
        for b in blocks:
            if b == 7:
                edges[12] = w0[VEC_TILE[0], 0:EDGE, :]
            else:
                take_edge(0, 19 * b + 19, b)
            store(front.at[pl.ds(STRIDE * TILE * b, STRIDE * TILE)], 0, b, 0, b)
            store(edges.at[12 if b == 7 else b], 0, b, STRIDE * TILE, 28 + b)

    store_front((5, 6))
    middle_back(0, std_b)
    taps_back(w0, 16, cols0, 2, 4)
    store_front((1, 2, 3, 4))
    for c in range(2):
        at = slice(256 * c, 256 * c + 256)
        gain, bias = row(0, 2 * c), row(0, 4 + 2 * c)
        grad = grad_h[:, at] * gate_of(gain * std_a[:, at] + bias)
        result, grad_gain, grad_bias = unstandardize(grad, std_a[:, at], gain, inverse_of(0, 256 * c))
        put_row(0, 2 * c, grad_gain)
        put_row(0, 4 + 2 * c, grad_bias)
        for p in range(4):
            dz_a[PADDED * p : PADDED * p + PADDED, at] = pad_low(result[ROWS * p : ROWS * p + ROWS])

    place_teach = one_hot(moves[2, 0 : teach_x.shape[0], :], 4 * PADDED)
    place_stud = one_hot(moves[3, 0 : stud_x.shape[0], :], 4 * PADDED)

    @chunks(4)
    def _(c):
        at = lanes(c)
        low = dz_a[...]
        part = mul_t(low, narrow_part(w0, 4 * c, 4))
        part = jnp.concatenate([part[0:PADDED] + acc_x[:, at], part[PADDED:]], axis=0).astype(LOW)
        grad_teach[:, at] = mul(place_teach, part).astype(LOW)
        grad_stud[:, at] = mul(place_stud, part).astype(LOW)
        put_narrow(w0, 4 * c, 4, mul(x[:, :, at].reshape(4 * PADDED, 256).T, low))

    flush(0)
    store_front((0, 7))
    for section in range(4):
        part = raw[2 * section : 2 * section + 2]
        stats[section, 0:2] = part if section < 2 else part * gate
        stats[section, 2:8] = jnp.zeros((6, 2 * MID + C_OUT), FULL)
    for store in stores:
        store.wait()


def run_step(table, gates, teach_ids, stud_ids, all_big, all_small, teach_x, stud_x, targets):
    spots = np.zeros((3, ROWS, 128), np.int32)
    for r in range(ROWS):
        width = 4 if r < STUD_ROWS else 6
        at = r % 16 if r < STUD_ROWS else (r - STUD_ROWS) // 2
        spots[0, r], spots[1, r], spots[2, r] = at // width, at % width, width
    moves = np.full((4, 4 * PADDED, 128), -1, np.int32)
    for p in range(4):
        for r in range(ROWS):
            high, across = 2 * spots[0, r, 0] + p // 2, 2 * spots[1, r, 0] + p % 2
            group, lies = 1, 64 * (r // 16) + 8 * high + across
            if r >= STUD_ROWS:
                group, lies = 0, 2 * (12 * high + across) + (r - STUD_ROWS) % 2
            moves[group, PADDED * p + r] = lies
            moves[2 + group, lies] = PADDED * p + r
    sem = pltpu.SemaphoreType.DMA
    wide = jax.ShapeDtypeStruct((PADDED, C_OUT), LOW)
    vm = pltpu.VMEM
    return pl.pallas_call(
        step_kernel,
        name="step",
        out_shape=(
            wide, wide, wide,
            jax.ShapeDtypeStruct((4, 8, 2 * MID + C_OUT), FULL),
            jax.ShapeDtypeStruct(teach_x.shape, LOW),
            jax.ShapeDtypeStruct(stud_x.shape, LOW),
            jax.ShapeDtypeStruct((2, 8, BIG_ROWS, 128), LOW),
            jax.ShapeDtypeStruct((2, USED_TILES[1], TILE, 128), LOW),
        ),
        in_specs=[smem_spec()] * 4 + [any_spec()] * 2 + [vmem_spec()] * 2 + [any_spec()] + [vmem_spec()] * 2,
        out_specs=(vmem_spec(),) * 6 + (any_spec(),) * 2,
        scratch_shapes=[
            vm((4, PADDED, C_IN), LOW),
            vm((153, TILE, 128), LOW), vm((33, TILE, 128), LOW), vm((115, TILE, 128), LOW), vm((33, TILE, 128), LOW),
            vm((13, EDGE, 128), LOW), vm((TILE, 128), FULL), vm((4, 48, 128), FULL), vm((4, TILE, 128), FULL),
            vm((8, 2 * MID + C_OUT), FULL),
            vm((4 * ROWS, MID), FULL), vm((ROWS, MID), FULL), vm((ROWS, C_OUT), FULL), vm((ROWS, C_OUT), FULL),
            vm((ROWS, MID), FULL), vm((ROWS, MID), FULL), vm((4 * ROWS, MID), FULL),
            vm((9, PADDED, MID), LOW), vm((9, PADDED, MID), LOW),
            vm((PADDED, MID), LOW), vm((PADDED, MID), LOW), vm((MID, PADDED), LOW), vm((C_IN, PADDED), LOW),
            vm((PADDED, C_OUT), LOW), vm((4 * PADDED, MID), LOW), vm((PADDED, MID), LOW),
            vm((PADDED, MID), FULL), vm((PADDED, C_IN), FULL), vm((4 * ROWS, MID), FULL),
            vm((8, C_OUT), FULL), pltpu.SMEM((16,), jnp.int32),
            sem((2, 16)), sem((18,)), sem((36,)),
        ],
        compiler_params=pltpu.CompilerParams(vmem_limit_bytes=60 << 20),
    )(table, gates, teach_ids, stud_ids, all_big, all_small, teach_x, stud_x, targets, jnp.asarray(spots), jnp.asarray(moves))


def reduce_kernel(big, small, wide0, wide1, final, stats, table,
                  out_big, out_small, seg_stud, seg_teach, out_stats, norm, factor,
                  got, halves_x, halves_y, from_x, from_y, from_low, from_high, stage, total,
                  l_got, l_stage, l_low, l_high, l_halves_x, l_halves_y, l_from_x, l_from_y, l_total,
                  late, late_half, owner_row, by_pipe, by_dp, mine, part_sum,
                  s_send, s_recv, ls_send, ls_recv, hx_send, hx_recv, hy_send, hy_recv, x_send, x_recv, y_send, y_recv,
                  zu_send, zu_recv, zd_send, zd_recv, lu_send, lu_recv, ld_send, ld_recv,
                  stage_sem, l_stage_sem, out_sem, big_sem, late_send, late_recv, join_send, join_recv,
                  seg_send, seg_recv, stat_send, stat_recv, p_send, p_recv, d_send, d_recv):
    me = Place()
    me.enter()
    x, y, z, core = me.x, me.y, me.z, me.core
    up, down = me.device(z=z + 1), me.device(z=z - 1)
    x_side, y_side, sibling = me.device(x=1 - x), me.device(y=1 - y), me.device(core=1 - core)
    order = [
        jnp.where(z < 2, 3, 0),
        jnp.where(z == 0, 2, jnp.where(z == 1, 0, jnp.where(z == 2, 3, 1))),
        jnp.where(z == 0, 1, jnp.where(z == 1, 2, jnp.where(z == 2, 1, 2))),
        z,
    ]
    columns = ((1 - x, 1 - y), (x, 1 - y), (1 - x, y), (x, y))
    groups = {"A": (0,), "C": (1,), "B": (2,), "O": (3,)}
    sequence = [
        (group, int(event[1])) for event in REDUCE_ORDER for group in groups.get(event[0], ())
    ]
    l_sequence = [(group, k) for k in range(4) for group in range(4)]

    def all_of(copies, act):
        for copy in copies:
            act(copy)

    def over(start, count, piece):
        whole = count // 512
        if whole:

            @pl.loop(0, whole)
            def _(i):
                piece(pl.multiple_of(start + 512 * i, 16), 512)

        if count % 512:
            piece(start + 512 * whole, count % 512)

    items = 4 * PARTS

    def source(group, q, half):
        xo, yo = columns[group]
        part = pl.ds(PART_ROWS * (q % PARTS), PART_ROWS)
        return big.at[xo, 2 * order[q // PARTS] + yo, half, part]

    def l_source(group, k, half):
        xo, yo = columns[group]
        return small.at[xo, 2 * order[k] + yo, half]

    def share(group, q):
        at = items * group + q
        return remote(source(group, q, 1 - core), got.at[at], s_send.at[at], s_recv.at[at], sibling)

    def l_share(group, k):
        at = 4 * group + k
        return remote(l_source(group, k, 1 - core), l_got.at[at], ls_send.at[at], ls_recv.at[at], sibling)

    def fetch(n):
        return pltpu.make_async_copy(source(*sequence[n], core), stage.at[n % 4], stage_sem.at[n % 4])

    def l_fetch(group, k):
        at = 4 * group + k
        return pltpu.make_async_copy(l_source(group, k, core), l_stage.at[at], l_stage_sem.at[at])

    def add(target, at, other, slot, start, count, extras):
        def piece(begin, size):
            part = pl.ds(begin, size)
            sums = target[at, part, :].astype(FULL) + other[slot, part, :].astype(FULL)
            for ref, k in extras:
                sums = sums + ref[k, pl.ds(begin - start, size), :].astype(FULL)
            target[at, part, :] = sums.astype(LOW)

        over(start, count, piece)

    def send_half_x(k):
        return remote(got.at[k, pl.ds(BACK_CUT, PART_ROWS - BACK_CUT)], halves_x.at[k],
                      hx_send.at[k], hx_recv.at[k], x_side)

    def send_half_y(k):
        return remote(got.at[k, pl.ds(0, BACK_CUT)], halves_y.at[k], hy_send.at[k], hy_recv.at[k], y_side)

    def send_y(k):
        return remote(got.at[items + k], from_y.at[k], y_send.at[k], y_recv.at[k], y_side)

    def send_x(k):
        return remote(got.at[2 * items + k], from_x.at[k], x_send.at[k], x_recv.at[k], x_side)

    def low_slot(q):
        return PARTS * (order[q // PARTS] - 1) + q % PARTS

    def high_slot(q):
        return PARTS * order[q // PARTS] + q % PARTS

    def send_up(q):
        slot = low_slot(q)
        return remote(got.at[3 * items + q], from_low.at[slot], zu_send.at[slot], zu_recv.at[slot], up)

    def send_down(q):
        slot = high_slot(q)
        return remote(got.at[3 * items + q], from_high.at[slot], zd_send.at[slot], zd_recv.at[slot], down)

    def l_column(group):
        xo, yo = columns[group]
        return 2 * xo + yo

    def l_up(group, k):
        at, zd = l_column(group), order[k] - 1
        return remote(l_got.at[4 * group + k], l_low.at[at, zd], lu_send.at[at, zd], lu_recv.at[at, zd], up)

    def l_down(group, k):
        at, zd = l_column(group), order[k]
        return remote(l_got.at[4 * group + k], l_high.at[at, zd], ld_send.at[at, zd], ld_recv.at[at, zd], down)

    def l_half_x():
        return remote(l_got.at[3, pl.ds(LIGHT_CUT, SMALL_HALF - LIGHT_CUT)], l_halves_x,
                      hx_send.at[items], hx_recv.at[items], x_side)

    def l_half_y():
        return remote(l_got.at[3, pl.ds(0, LIGHT_CUT)], l_halves_y, hy_send.at[items], hy_recv.at[items], y_side)

    def l_send_y():
        return remote(l_got.at[7], l_from_y, y_send.at[items], y_recv.at[items], y_side)

    def l_send_x():
        return remote(l_got.at[11], l_from_x, x_send.at[items], x_recv.at[items], x_side)

    leaving = (wide0, wide1, wide1, final)

    def pairs(section, micro):
        source = leaving[section]
        yield source.at[pl.ds(0, STUD_ROWS)], seg_stud.at[micro], seg_send.at[0, section], seg_recv.at[0, micro]
        yield source.at[pl.ds(STUD_ROWS, TEACH_END)], seg_teach.at[micro], seg_send.at[1, section], seg_recv.at[1, micro]
        yield stats.at[section], out_stats.at[micro], stat_send.at[section], stat_recv.at[micro]

    def exchange(section):
        return [remote(*pair, {"dp": me.dp, "pipe": section}) for pair in pairs(section, me.pipe)]

    def keep(section):
        return [pltpu.make_async_copy(src, dst, send) for src, dst, send, _ in pairs(section, me.pipe)]

    def arriving(micro):
        return [remote(*pair, {"dp": me.dp, "pipe": micro}) for pair in pairs(micro, micro)]

    for n in range(4 * items):
        share(*sequence[n]).start()
        if n == 5:
            for item in l_sequence:
                l_share(*item).start()
    for n in range(2):
        fetch(n).start()
    for group, k in l_sequence:
        l_fetch(group, k).start()
    row_copy = pltpu.make_async_copy(table.at[2 * x], owner_row, out_sem.at[2])
    row_copy.start()

    def bulk_item(n):
        group, k = sequence[n]
        at, slot = items * group + k, n % 4
        if n + 2 < 4 * items:
            fetch(n + 2).start()
        fetch(n).wait()
        share(group, k).wait_recv()
        if group == 0:
            add(got, at, stage, slot, 0, PART_ROWS, [])
            send_half_x(k).start()
            send_half_y(k).start()
        elif group == 1:
            send_half_x(k).wait_recv()
            add(got, at, stage, slot, 0, BACK_CUT, [])
            add(got, at, stage, slot, BACK_CUT, PART_ROWS - BACK_CUT, [(halves_x, k)])
            send_y(k).start()
        elif group == 2:
            send_half_y(k).wait_recv()
            add(got, at, stage, slot, 0, BACK_CUT, [(halves_y, k)])
            add(got, at, stage, slot, BACK_CUT, PART_ROWS - BACK_CUT, [])
            send_x(k).start()
        else:
            send_x(k).wait_recv()
            send_y(k).wait_recv()
            add(got, at, stage, slot, 0, PART_ROWS, [(from_x, k), (from_y, k)])

    def bulk_z(q):
        at, zd = 3 * items + q, order[q // PARTS]

        @pl.when(zd > z)
        def _():
            @pl.when(z > 0)
            def _():
                send_up(q).wait_recv()
                add(got, at, from_low, low_slot(q), 0, PART_ROWS, [])

            send_up(q).start()

        @pl.when(zd < z)
        def _():
            @pl.when(z < 3)
            def _():
                send_down(q).wait_recv()
                add(got, at, from_high, high_slot(q), 0, PART_ROWS, [])

            send_down(q).start()

    def light_item(group, k):
        at, zd, column = 4 * group + k, order[k], l_column(group)
        l_fetch(group, k).wait()
        l_share(group, k).wait_recv()
        add(l_got, at, l_stage, at, 0, SMALL_HALF, [])

        def merge(ref, slot):
            l_got[at] = (l_got[at].astype(FULL) + ref[column, slot].astype(FULL)).astype(LOW)

        if k < 3:

            @pl.when(zd > z)
            def _():
                @pl.when(z > 0)
                def _():
                    l_up(group, k).wait_recv()
                    merge(l_low, zd - 1)

                l_up(group, k).start()

            @pl.when(zd < z)
            def _():
                @pl.when(z < 3)
                def _():
                    l_down(group, k).wait_recv()
                    merge(l_high, zd)

                l_down(group, k).start()

        else:

            @pl.when(z > 0)
            def _():
                l_up(group, k).wait_recv()
                merge(l_low, zd - 1)

            @pl.when(z < 3)
            def _():
                l_down(group, k).wait_recv()
                merge(l_high, zd)

            if group == 0:
                l_half_x().start()
                l_half_y().start()

    def light_sides():
        l_half_x().wait_recv()
        l_got[7, LIGHT_CUT:SMALL_HALF, :] = (
            l_got[7, LIGHT_CUT:SMALL_HALF, :].astype(FULL) + l_halves_x[...].astype(FULL)
        ).astype(LOW)
        l_send_y().start()
        l_half_y().wait_recv()
        l_got[11, 0:LIGHT_CUT, :] = (
            l_got[11, 0:LIGHT_CUT, :].astype(FULL) + l_halves_y[...].astype(FULL)
        ).astype(LOW)
        l_send_x().start()

    def light_end():
        l_send_x().wait_recv()
        l_send_y().wait_recv()
        l_total[...] = l_got[15].astype(FULL) + l_from_x[...].astype(FULL) + l_from_y[...].astype(FULL)

    small_join = remote(late_half, late.at[pl.ds(0, SMALL_HALF)], join_send.at[0], join_recv.at[0], sibling)
    own_late = pltpu.make_async_copy(late, out_small.at[me.dp], out_sem.at[1])

    def late_z(origin, target, way):
        block = out_small.at[2 * origin + y]
        return remote(block, block, late_send.at[way, origin], late_recv.at[0, origin], target)

    def late_y(origin, yo):
        block = out_small.at[2 * origin + yo]
        return remote(block, block, late_send.at[2, origin], late_recv.at[1, origin], y_side)

    def late_step(k):
        @pl.when((core == 1) & (z >= k))
        def _():
            late_z(z - k, up, 0).wait_recv()
            pl.when(z < 3)(lambda: late_z(z - k, up, 0).start())
            late_y(z - k, y).start()

        @pl.when((core == 1) & (z + k <= 3))
        def _():
            late_z(z + k, down, 1).wait_recv()
            pl.when(z > 0)(lambda: late_z(z + k, down, 1).start())
            late_y(z + k, y).start()

    def leave():
        for section in range(4):
            @pl.when(me.pipe == section)
            def _(section=section):
                all_of(keep(section), lambda copy: copy.start())

            @pl.when(me.pipe != section)
            def _(section=section):
                all_of(exchange(section), lambda copy: copy.start())

    def late_start():
        light_end()

        @pl.when(core == 0)
        def _():
            late_half[...] = l_total[...].astype(LOW)
            small_join.start()

        @pl.when(core == 1)
        def _():
            late[SMALL_HALF:SMALL_ROWS, :] = l_total[...].astype(LOW)
            small_join.wait_recv()
            own_late.start()
            own_late.wait()
            pl.when(z < 3)(lambda: late_z(z, up, 0).start())
            pl.when(z > 0)(lambda: late_z(z, down, 1).start())
            late_y(z, y).start()

    def light_round(k):
        for n in range(4 * k, 4 * k + 4):
            light_item(*l_sequence[n])

    edge = (z == 0) | (z == 3)

    def early_z(k):
        pl.when(edge)(lambda: bulk_z(k))

    def inner_z(k):
        pl.when(jnp.logical_not(edge))(lambda: bulk_z(k))

    actions = {"LS": [light_sides], "LE": [late_start], "G": [leave]}
    numbered = {item: n for n, item in enumerate(sequence)}
    for k in range(4):
        actions["L%d" % k] = [functools.partial(light_round, k)]
        if k:
            actions["T%d" % k] = [functools.partial(late_step, k)]
    for q in range(items):
        for letter, group in (("A", 0), ("C", 1), ("B", 2), ("O", 3)):
            actions["%s%d" % (letter, q)] = [functools.partial(bulk_item, numbered[group, q])]
        if q < 3 * PARTS:
            actions["E%d" % q] = [functools.partial(early_z, q)]
            actions["I%d" % q] = [functools.partial(inner_z, q)]
    for event in REDUCE_ORDER:
        for action in actions[event]:
            action()

    row_copy.wait()
    part_sum[...] = jnp.sum((l_total[...] * l_total[...]).reshape(SMALL_HALF // 8, 8, 128), axis=0)
    lane = lax.broadcasted_iota(jnp.int32, (8, 128), 1)
    is_last = jnp.where((lane == me.dp) & (owner_row[...] == 7), 1.0, 0.0)
    weight = jnp.broadcast_to(jnp.sum(is_last, axis=1, keepdims=True), (8, 128))
    weight = jnp.where(core == 0, jnp.ones((8, 128), FULL), weight)

    big_parts = [pl.ds(PART_ROWS * n, PART_ROWS) for n in range(PARTS)]

    def big_join(n):
        return remote(total.at[big_parts[n]], out_big.at[1, big_parts[n]],
                      join_send.at[1 + n], join_recv.at[1 + n], sibling)

    def own_big(n):
        return pltpu.make_async_copy(total.at[big_parts[n]], out_big.at[0, big_parts[n]], big_sem.at[n])

    def end(n, low, high):
        q = 3 * PARTS + n

        def piece(begin, size, scale):
            part = pl.ds(begin, size)
            sums = got[3 * items + q, part, :].astype(FULL)
            if low:
                sums = sums + from_low[low_slot(q), part, :].astype(FULL)
            if high:
                sums = sums + from_high[high_slot(q), part, :].astype(FULL)
            total[pl.ds(PART_ROWS * n + begin, size), :] = sums
            squares = jnp.sum((sums * sums).reshape(size // 8, 8, 128), axis=0)
            part_sum[...] += squares if scale is None else squares * scale

        def plain(begin, size):
            piece(begin, size, None)

        if n < PARTS - 1:
            over(0, PART_ROWS, plain)
        else:
            over(0, PART_ROWS - EDGE, plain)
            piece(PART_ROWS - EDGE, EDGE, weight)

    for n in range(PARTS):
        q = 3 * PARTS + n

        @pl.when(z == 0)
        def _(n=n, q=q):
            send_down(q).wait_recv()
            end(n, False, True)

        @pl.when((z > 0) & (z < 3))
        def _(n=n, q=q):
            send_up(q).wait_recv()
            send_down(q).wait_recv()
            end(n, True, True)

        @pl.when(z == 3)
        def _(n=n, q=q):
            send_up(q).wait_recv()
            end(n, True, False)

        @pl.when(core == 0)
        def _(n=n):
            own_big(n).start()

        @pl.when(core == 1)
        def _(n=n):
            big_join(n).start()

    def along_pipe(step, slot):
        target = {"dp": me.dp, "pipe": lax.rem(me.pipe + step, 4)}
        return remote(part_sum, by_pipe.at[slot], p_send.at[step], p_recv.at[step], target)

    def along_dp(step, slot):
        target = {"dp": lax.rem(me.dp + step, 8), "pipe": me.pipe}
        return remote(mine, by_dp.at[slot], d_send.at[step], d_recv.at[step], target)

    for step in range(1, 4):
        along_pipe(step, me.pipe).start()
    by_pipe[me.pipe] = part_sum[...]
    for step in range(1, 4):
        along_pipe(step, lax.rem(me.pipe + 4 - step, 4)).wait_recv()
    mine[...] = jnp.sum(by_pipe[...], axis=0)
    for step in range(1, 8):
        along_dp(step, me.dp).start()
    by_dp[me.dp] = mine[...]
    for step in range(1, 8):
        along_dp(step, lax.rem(me.dp + 8 - step, 8)).wait_recv()
    whole = jnp.sum(jnp.sum(by_dp[...], axis=0), axis=0, keepdims=True)
    length = jnp.sqrt(jnp.broadcast_to(jnp.sum(whole, axis=1, keepdims=True), (8, 128)))
    norm[...] = length
    factor[...] = jnp.minimum(1.0, CLIP_NORM / length)

    @pl.when(core == 0)
    def _():
        for n in range(PARTS):
            own_big(n).wait()
            big_join(n).wait_recv()
        small_join.wait_send()

    @pl.when(core == 1)
    def _():
        for n in range(PARTS):
            big_join(n).wait_send()
        for origin in range(4):
            late_y(origin, 1 - y).wait_recv()
            late_y(origin, y).wait_send()
            pl.when((z < 3) & (origin <= z))(lambda: late_z(origin, up, 0).wait_send())
            pl.when((z > 0) & (origin >= z))(lambda: late_z(origin, down, 1).wait_send())

    for other in range(4):
        @pl.when(me.pipe == other)
        def _(other=other):
            all_of(keep(other), lambda copy: copy.wait())

        @pl.when(me.pipe != other)
        def _(other=other):
            all_of(exchange(other), lambda copy: copy.wait_send())
            all_of(arriving(other), lambda copy: copy.wait_recv())

    for step in range(1, 4):
        along_pipe(step, me.pipe).wait_send()
    for step in range(1, 8):
        along_dp(step, me.dp).wait_send()
    for copy in (l_half_x(), l_half_y(), l_send_x(), l_send_y()):
        copy.wait_send()
    for q in range(items):
        send_half_x(q).wait_send()
        send_half_y(q).wait_send()
        send_x(q).wait_send()
        send_y(q).wait_send()
        for group in range(4):
            share(group, q).wait_send()
    for group, k in l_sequence:
        l_share(group, k).wait_send()
    for k in range(3):
        zd = order[k]

        @pl.when(zd > z)
        def _(k=k):
            for n in range(PARTS):
                send_up(PARTS * k + n).wait_send()
            for group in range(4):
                l_up(group, k).wait_send()

        @pl.when(zd < z)
        def _(k=k):
            for n in range(PARTS):
                send_down(PARTS * k + n).wait_send()
            for group in range(4):
                l_down(group, k).wait_send()


def reduce_all(big, small, wide0, wide1, final, stats, table):
    sem = pltpu.SemaphoreType.DMA
    vm = pltpu.VMEM
    items = 4 * PARTS
    lane_tile = jax.ShapeDtypeStruct((8, 128), FULL)
    return pl.pallas_call(
        reduce_kernel,
        name="reduce_all",
        out_shape=(
            jax.ShapeDtypeStruct((2, BIG_HALF, 128), FULL),
            jax.ShapeDtypeStruct((8, SMALL_ROWS, 128), LOW),
            jax.ShapeDtypeStruct((4, STUD_ROWS, C_OUT), LOW),
            jax.ShapeDtypeStruct((4, TEACH_END, C_OUT), LOW),
            jax.ShapeDtypeStruct((4,) + stats.shape[1:], FULL),
            lane_tile,
            lane_tile,
        ),
        in_specs=[any_spec()] * 7,
        out_specs=(any_spec(),) * 5 + (vmem_spec(),) * 2,
        scratch_shapes=[
            vm((4 * items, PART_ROWS, 128), LOW),
            vm((items, PART_ROWS - BACK_CUT, 128), LOW), vm((items, BACK_CUT, 128), LOW),
            vm((items, PART_ROWS, 128), LOW), vm((items, PART_ROWS, 128), LOW),
            vm((3 * PARTS, PART_ROWS, 128), LOW), vm((3 * PARTS, PART_ROWS, 128), LOW),
            vm((4, PART_ROWS, 128), LOW), vm((BIG_HALF, 128), FULL),
            vm((16, SMALL_HALF, 128), LOW), vm((16, SMALL_HALF, 128), LOW),
            vm((4, 3, SMALL_HALF, 128), LOW), vm((4, 3, SMALL_HALF, 128), LOW),
            vm((SMALL_HALF - LIGHT_CUT, 128), LOW), vm((LIGHT_CUT, 128), LOW),
            vm((SMALL_HALF, 128), LOW), vm((SMALL_HALF, 128), LOW), vm((SMALL_HALF, 128), FULL),
            vm((SMALL_ROWS, 128), LOW), vm((SMALL_HALF, 128), LOW), vm((8, 128), jnp.int32),
            vm((4, 8, 128), FULL), vm((8, 8, 128), FULL), vm((8, 128), FULL), vm((8, 128), FULL),
            sem((4 * items,)), sem((4 * items,)), sem((16,)), sem((16,)),
            sem((items + 1,)), sem((items + 1,)), sem((items + 1,)), sem((items + 1,)),
            sem((items + 1,)), sem((items + 1,)), sem((items + 1,)), sem((items + 1,)),
            sem((3 * PARTS,)), sem((3 * PARTS,)), sem((3 * PARTS,)), sem((3 * PARTS,)),
            sem((4, 3)), sem((4, 3)), sem((4, 3)), sem((4, 3)),
            sem((4,)), sem((16,)), sem((3,)), sem((PARTS,)), sem((3, 4)), sem((2, 4)),
            sem((1 + PARTS,)), sem((1 + PARTS,)),
            sem((2, 4)), sem((2, 4)), sem((4,)), sem((4,)), sem((4,)), sem((4,)), sem((8,)), sem((8,)),
        ],
        compiler_params=pltpu.CompilerParams(
            collective_id=1, has_side_effects=True, vmem_limit_bytes=62 << 20
        ),
    )(big.reshape(2, 8, 2, BIG_HALF, 128), small.reshape(2, 8, 2, SMALL_HALF, 128),
      wide0, wide1, final, stats, table)


def high_dot(a, b, dims=((1,), (0,))):
    return lax.dot_general(a, b, (dims, ((), ())), precision=HIGH, preferred_element_type=FULL)


PIECES = 7
FRONT = 48


def update_kernel(owners, factor_ref, norm, big, small, gram_old, basis_old, params, moment, second, stats,
                  clipped, moment_new, second_new, params_new, gram_new, basis_new, length, out_stats,
                  tiles, low, grad, held, rotated, weights, gram, in_sem, out_sem, tile_sem, stat_sem):
    factor = factor_ref[0:1, :]
    length[0, 0] = jnp.max(norm[...])
    block, section = owners[0, lax.axis_index("dp")], lax.axis_index("pipe")
    even = lax.rem(section, 2) == 0
    span = params.shape[0]
    piece = held.shape[0] // PIECES

    stat_copies = [
        pltpu.make_async_copy(stats.at[m, pl.ds(0, 2)], out_stats.at[m], stat_sem.at[m])
        for m in range(stats.shape[0])
    ]
    for copy in stat_copies:
        copy.start()
    quarter = WINDOW // 4 * TILE

    def big_load(i):
        part = pl.ds(quarter * i, min(quarter, BIG_ROWS - quarter * i))
        return pltpu.make_async_copy(big.at[part], tiles.at[part], tile_sem.at[i])

    @pl.when(even)
    def _():
        for i in range(4):
            big_load(i).start()

    def loads(i):
        part = pl.ds(piece * i, min(piece, span - piece * i))
        for n, (src, dst) in enumerate(((params, weights), (moment, held), (second, rotated))):
            yield pltpu.make_async_copy(src.at[part, 0, :], dst.at[part], in_sem.at[n, i])

    def stores(i):
        count = min(piece, span - piece * i)
        part = pl.ds(piece * i, count)
        yield pltpu.make_async_copy(
            grad.at[pl.ds(FRONT + piece * i, count)], clipped.at[part, 0, :], out_sem.at[3, i])
        pairs = ((held, moment_new), (rotated, second_new), (weights, params_new))
        for n, (src, dst) in enumerate(pairs):
            yield pltpu.make_async_copy(src.at[part], dst.at[part, 0, :], out_sem.at[n, i])

    for i in range(PIECES):
        for load in loads(i):
            load.start()

    @pl.when(jnp.logical_not(even))
    def _():
        low[...] = jnp.zeros_like(low)

        @pl.when(block == 0)
        def _():
            copy = pltpu.make_async_copy(small.at[0:20], low, tile_sem.at[0])
            copy.start()
            copy.wait()

        @pl.when(block == 1)
        def _():
            copy = pltpu.make_async_copy(small.at[19:33], low.at[0:14], tile_sem.at[0])
            copy.start()
            copy.wait()

        @pl.loop(0, WINDOW)
        def _(r):
            tiles[pl.ds(pl.multiple_of(TILE * r, TILE), TILE), :] = low[r].astype(FULL)

    def lay_flat(r):
        narrow, plain = tile_forms(section, STRIDE * block + r)
        edge = even & (r == STRIDE)
        narrow, plain = narrow & jnp.logical_not(edge), plain | edge
        base = FRONT - 6 * block + TILE * r
        here = pl.multiple_of(TILE * r, TILE)

        @pl.when(narrow)
        def _():
            for j in range(4):
                grad[pl.ds(base + j, 64, 4), :] = tiles[pl.ds(here + 64 * j, 64), :]

        @pl.when(plain)
        def _():
            grad[pl.ds(base, TILE), :] = tiles[pl.ds(here, TILE), :]

        @pl.when(jnp.logical_not(narrow | plain))
        def _():
            for j in range(16):
                grad[pl.ds(base + j, 16, 16), :] = tiles[pl.ds(here + 16 * j, 16), :]

    for i in range(4):
        pl.when(even)(lambda: big_load(i).wait())
        pl.loop(WINDOW // 4 * i, WINDOW // 4 * (i + 1))(lay_flat)

    tail = piece * PIECES - 8
    rest = lax.broadcasted_iota(jnp.int32, (8, 128), 0) + tail
    grad[FRONT + tail : FRONT + tail + 8, :] = jnp.where(
        rest < span, grad[FRONT + tail : FRONT + tail + 8, :], 0.0
    )
    gram[...] = jnp.zeros_like(gram)

    def halves(value):
        high = value.astype(LOW)
        return high, (value - high.astype(FULL)).astype(LOW)

    def split_dot(a, b, dims=((1,), (0,))):
        def dot(left, right):
            return lax.dot_general(left, right, (dims, ((), ())), preferred_element_type=FULL)

        return dot(a[0], b[0]) + (dot(a[0], b[1]) + dot(a[1], b[0]))

    @pl.loop(0, PIECES)
    def _(i):
        part = halves(grad[pl.ds(pl.multiple_of(FRONT + piece * i, 8), piece), :])
        gram[...] += split_dot(part, part, ((0,), (0,)))

    old = basis_old[...]
    fresh = DECAY_STATS * gram_old[...] + (1.0 - DECAY_STATS) * (gram[...] * (factor * factor))
    gram_new[...] = fresh
    product = high_dot(fresh, old)
    rotation = product / jnp.sqrt(jnp.sum(product * product))
    for repeat in range(NS_STEPS):
        parts = halves(rotation)
        square = split_dot(parts, parts, ((0,), (0,)))
        rotation = 1.5 * rotation - 0.5 * split_dot(parts, halves(square))
    basis_new[...] = rotation
    change = halves(high_dot(old, rotation, ((0,), (0,))))
    turn = halves(rotation)
    correction = math.sqrt(1.0 - DECAY_SECOND**STEP) / (1.0 - DECAY_FIRST**STEP)
    for i in range(PIECES):
        for load in loads(i):
            load.wait()
        at = slice(FRONT + piece * i, FRONT + piece * i + piece)
        part = slice(piece * i, piece * i + piece)
        clip = grad[at, :] * factor
        grad[at, :] = clip
        turned = split_dot(halves(clip), turn)
        first = DECAY_FIRST * split_dot(halves(held[part, :]), change) + (1.0 - DECAY_FIRST) * turned
        power = DECAY_SECOND * rotated[part, :] + (1.0 - DECAY_SECOND) * turned * turned
        held[part, :] = first
        rotated[part, :] = power
        scaled = halves(first / (jnp.sqrt(power) + ADAM_EPS))
        direction = split_dot(scaled, turn, ((1,), (1,))) * correction
        before = weights[part, :]
        weights[part, :] = before - LEARN_RATE * (direction + WEIGHT_DECAY * before)
        for store in stores(i):
            store.start()
    for i in range(PIECES):
        for store in stores(i):
            store.wait()
    for copy in stat_copies:
        copy.wait()


def update(owners, factor, norm, big, small, gram_old, basis_old, params, moment, second, stats):
    span = params.shape[1] // 128
    rows = -(-span // (8 * PIECES)) * 8 * PIECES
    flat_shape = jax.ShapeDtypeStruct((span, 1, 128), FULL)
    square = jax.ShapeDtypeStruct((128, 128), FULL)
    sem = pltpu.SemaphoreType.DMA
    vm = pltpu.VMEM
    outs = pl.pallas_call(
        update_kernel,
        name="update",
        out_shape=(flat_shape,) * 4 + (square,) * 2 + (jax.ShapeDtypeStruct((1, 1), FULL), jax.ShapeDtypeStruct((4, 2) + stats.shape[2:], FULL)),
        in_specs=[smem_spec()] + [vmem_spec()] * 2 + [any_spec()] * 2 + [vmem_spec()] * 2 + [any_spec()] * 4,
        out_specs=(any_spec(),) * 4 + (vmem_spec(),) * 2 + (smem_spec(), any_spec()),
        scratch_shapes=[
            vm((WINDOW * TILE, 128), FULL), vm((WINDOW, TILE, 128), LOW),
            vm((FRONT + WINDOW * TILE, 128), FULL), vm((rows, 128), FULL), vm((rows, 128), FULL),
            vm((rows, 128), FULL), vm((128, 128), FULL), sem((3, PIECES)), sem((4, PIECES)), sem((4,)), sem((4,)),
        ],
        compiler_params=pltpu.CompilerParams(vmem_limit_bytes=60 << 20),
    )(owners, factor, norm, big.reshape(BIG_ROWS, 128), small.reshape(USED_TILES[1], TILE, 128),
      gram_old, basis_old, params.reshape(span, 1, 128), moment.reshape(span, 1, 128),
      second.reshape(span, 1, 128), stats)
    return tuple(out.reshape(1, span * 128) for out in outs[:4]) + outs[4:]


def on_small_slice(
    teach_in,
    stud_in,
    params,
    owners,
    depth_gates,
    teach_ids,
    stud_ids,
    targets,
    moment,
    second,
    gram_stats,
    eigen_basis,
):
    teach_shape, stud_shape = teach_in.shape[1:], stud_in.shape[1:]
    teach_x = teach_in[0].transpose(1, 2, 0, 3).reshape(-1, C_IN)
    stud_x = stud_in[0].reshape(-1, C_IN)
    big, small, ids = prepare(owners, params)
    all_big, all_small, table = gather_all(big, small, ids)
    wide_0, wide_1, final, stats, teach_grad, stud_grad, out_big, out_small = run_step(
        table,
        depth_gates,
        teach_ids.T,
        stud_ids,
        all_big.reshape(2, 8, BIG_ROWS, 128),
        all_small.reshape(2, USED_TILES[1], TILE, 128),
        teach_x,
        stud_x,
        targets,
    )
    sum_big, sum_small, segment_stud, segment_teach, stats, norm, factor = reduce_all(
        out_big, out_small, wide_0, wide_1, final, stats, table
    )
    clipped, moment_new, second_new, params_new, gram_new, rotation, length, stats = update(
        owners, factor, norm, sum_big, sum_small, gram_stats[0], eigen_basis[0], params, moment, second, stats
    )
    small_teach = (teach_shape[1] // 2, teach_shape[2] // 2, teach_shape[0], C_OUT)
    small_stud = (stud_shape[0], stud_shape[1] // 2, stud_shape[2] // 2, C_OUT)
    segment_teach = segment_teach[:, : ROWS - STUD_ROWS].reshape((4,) + small_teach).transpose(0, 3, 1, 2, 4)
    segment_stud = segment_stud.reshape((4,) + small_stud)
    teach_grad = teach_grad.reshape(teach_shape[1:3] + (teach_shape[0], C_IN)).transpose(2, 0, 1, 3)
    stud_grad = stud_grad.reshape(stud_shape)
    grad_norm = length.reshape(())
    return (
        segment_teach[None],
        segment_stud[None],
        teach_grad[None],
        stud_grad[None],
        stats[None, :, None],
        grad_norm,
        clipped,
        moment_new,
        second_new,
        params_new,
        gram_new[None],
        rotation[None],
    )


def solution(mesh):
    placed = (
        P("pipe", "dp", None, None, None),
        P("pipe", "dp", None, None, None),
        P("pipe", "dp"),
        P("pipe", None),
        P(),
        P(None, "dp"),
        P(None, "dp"),
        P(),
        P("pipe", "dp"),
        P("pipe", "dp"),
        P("pipe", "dp", None),
        P("pipe", "dp", None),
    )
    small_slice = mesh.shape["dp"] == 8 and mesh.shape["pipe"] == 4
    return jax.shard_map(
        on_small_slice if small_slice else on_device,
        mesh=mesh,
        in_specs=placed,
        out_specs=(
            P("pipe", None, "dp", None, None, None),
            P("pipe", None, "dp", None, None, None),
            P("pipe", "dp", None, None, None),
            P("pipe", "dp", None, None, None),
            P("pipe", None, "dp", None, None),
            P(),
            P("pipe", "dp"),
            P("pipe", "dp"),
            P("pipe", "dp"),
            P("pipe", "dp"),
            P("pipe", "dp", None),
            P("pipe", "dp", None),
        ),
        check_vma=False,
    )
```

```python
import functools
import math

import jax
import jax.numpy as jnp
import numpy as np
from jax import lax
from jax.experimental import pallas as pl
from jax.experimental.pallas import tpu as pltpu
from jax.sharding import PartitionSpec as P

C_IN = 1024
MID = 512
C_OUT = 2048
STEP = 10
NS_STEPS = 5


HIGH = lax.Precision.HIGHEST
NORM_EPS = 1e-05
POOL_EPS = 1e-06
CLIP_NORM = 1.0
LEARN_RATE = 0.02
DECAY_FIRST = 0.9
DECAY_SECOND = 0.95
DECAY_STATS = 0.95
ADAM_EPS = 1e-08
WEIGHT_DECAY = 0.01


def section_shapes(section):
    if section == 0:
        return [
            ("first_conv", (C_IN, MID)),
            ("middle_conv", (9 * MID, MID)),
            ("skip_conv", (C_IN, C_OUT)),
            ("first_gain", (MID,)),
            ("first_bias", (MID,)),
            ("middle_gain", (MID,)),
            ("middle_bias", (MID,)),
            ("skip_gain", (C_OUT,)),
            ("skip_bias", (C_OUT,)),
        ]
    if section == 2:
        return [
            ("first_conv", (C_OUT, MID)),
            ("middle_conv", (9 * MID, MID)),
            ("first_gain", (MID,)),
            ("first_bias", (MID,)),
            ("middle_gain", (MID,)),
            ("middle_bias", (MID,)),
        ]
    return [("last_conv", (MID, C_OUT)), ("last_gain", (C_OUT,)), ("last_bias", (C_OUT,))]


def unpack(flat_vector, section):
    pieces = {}
    offset = 0
    for entry_name, entry_shape in section_shapes(section):
        entry_size = math.prod(entry_shape)
        pieces[entry_name] = flat_vector[offset : offset + entry_size].reshape(entry_shape)
        offset = offset + entry_size
    return pieces


def pack(grads, section, flat_size):
    parts = [grads[entry_name].reshape(-1) for entry_name, entry_shape in section_shapes(section)]
    used = sum((math.prod(entry_shape) for entry_name, entry_shape in section_shapes(section)))
    parts.append(jnp.zeros((flat_size - used,), jnp.float32))
    return jnp.concatenate(parts)


def as_float(vector):
    return vector.astype(jnp.float32)


def to_low(groups):
    return tuple((portion.astype(jnp.bfloat16) for portion in groups))


def to_high(groups):
    return tuple((portion.astype(jnp.float32) for portion in groups))


def point_conv(groups, weight):
    return tuple(
        (
            jnp.einsum("khwc,cd->khwd", portion, weight, preferred_element_type=jnp.float32)
            for portion in groups
        )
    )


def point_back(grad_out, groups, weight):
    low_grads = to_low(grad_out)
    grad_input = tuple(
        (
            jnp.einsum("khwd,cd->khwc", grad_part, weight, preferred_element_type=jnp.float32)
            for grad_part in low_grads
        )
    )
    grad_weight = sum(
        (
            jnp.einsum("khwc,khwd->cd", in_part, grad_part, preferred_element_type=jnp.float32)
            for in_part, grad_part in zip(groups, low_grads)
        )
    )
    return (grad_input, grad_weight)


def patches(portion, stride):
    height = portion.shape[1]
    across = portion.shape[2]
    padded = jnp.pad(portion, ((0, 0), (1, 1), (1, 1), (0, 0)))
    shifted = [
        padded[:, row_off : row_off + height : stride, col_off : col_off + across : stride, :]
        for row_off in range(3)
        for col_off in range(3)
    ]
    return jnp.concatenate(shifted, axis=-1)


def area_conv(groups, weight, stride):
    columns = tuple((patches(portion, stride) for portion in groups))
    return (point_conv(columns, weight), columns)


def unpatch(grad_cols, height, across, stride):
    channels = grad_cols.shape[-1] // 9
    padded = jnp.zeros((grad_cols.shape[0], height + 2, across + 2, channels), jnp.float32)
    for row_off in range(3):
        for col_off in range(3):
            offset = (3 * row_off + col_off) * channels
            padded = padded.at[
                :, row_off : row_off + height : stride, col_off : col_off + across : stride, :
            ].add(grad_cols[..., offset : offset + channels])
    return padded[:, 1 : height + 1, 1 : across + 1, :]


def area_back(grad_out, columns, weight, stride, in_shapes):
    grad_cols, grad_weight = point_back(grad_out, columns, weight)
    grad_input = tuple(
        (
            unpatch(grad_part, shape_item[1], shape_item[2], stride)
            for grad_part, shape_item in zip(grad_cols, in_shapes)
        )
    )
    return (grad_input, grad_weight)


def batch_norm(groups, gain, bias):
    rows_total = sum((portion.shape[0] * portion.shape[1] * portion.shape[2] for portion in groups))
    centre = sum((jnp.sum(portion, axis=(0, 1, 2)) for portion in groups)) / rows_total
    spread = (
        sum((jnp.sum(jnp.square(portion - centre), axis=(0, 1, 2)) for portion in groups))
        / rows_total
    )
    inverse = lax.rsqrt(spread + NORM_EPS)
    standard = tuple(((portion - centre) * inverse for portion in groups))
    normed = tuple((gain * std_part + bias for std_part in standard))
    return (normed, (centre, spread, inverse, standard))


def norm_back(grad_out, gain, saved):
    centre, spread, inverse, standard = saved
    rows_total = sum(
        (portion.shape[0] * portion.shape[1] * portion.shape[2] for portion in standard)
    )
    grad_sum = sum((jnp.sum(grad_part, axis=(0, 1, 2)) for grad_part in grad_out))
    grad_dot = sum(
        (
            jnp.sum(grad_part * std_part, axis=(0, 1, 2))
            for grad_part, std_part in zip(grad_out, standard)
        )
    )
    grad_input = tuple(
        (
            gain
            * inverse
            * (grad_part - grad_sum / rows_total - std_part * (grad_dot / rows_total))
            for grad_part, std_part in zip(grad_out, standard)
        )
    )
    return (grad_input, grad_dot, grad_sum)


def through_softplus(grad_out, pre_values):
    return tuple(
        (grad_part * jax.nn.sigmoid(pre_part) for grad_part, pre_part in zip(grad_out, pre_values))
    )


def front_forward(pieces, inputs):
    first = point_conv(inputs, pieces["first_conv"])
    normed_a, saved_a = batch_norm(
        first, as_float(pieces["first_gain"]), as_float(pieces["first_bias"])
    )
    hidden = tuple((jax.nn.softplus(portion).astype(jnp.bfloat16) for portion in normed_a))
    middle, columns = area_conv(hidden, pieces["middle_conv"], 2)
    normed_b, saved_b = batch_norm(
        middle, as_float(pieces["middle_gain"]), as_float(pieces["middle_bias"])
    )
    narrow = tuple((jax.nn.softplus(portion) for portion in normed_b))
    reduced = tuple((portion[:, ::2, ::2, :] for portion in inputs))
    skipped = point_conv(reduced, pieces["skip_conv"])
    wide, saved_p = batch_norm(
        skipped, as_float(pieces["skip_gain"]), as_float(pieces["skip_bias"])
    )
    norm_rows = jnp.stack(
        [
            jnp.concatenate([saved_a[0], saved_b[0], saved_p[0]]),
            jnp.concatenate([saved_a[1], saved_b[1], saved_p[1]]),
        ]
    )
    kept = (normed_a, hidden, columns, normed_b, reduced, saved_a, saved_b, saved_p)
    return (wide, narrow, norm_rows, kept)


def front_backward(pieces, inputs, grad_wide, grad_narrow):
    wide, narrow, norm_rows, kept = front_forward(pieces, inputs)
    normed_a, hidden, columns, normed_b, reduced, saved_a, saved_b, saved_p = kept
    grads = {}
    grad_pre_b = through_softplus(grad_narrow, normed_b)
    grad_mid, grads["middle_gain"], grads["middle_bias"] = norm_back(
        grad_pre_b, as_float(pieces["middle_gain"]), saved_b
    )
    grad_hidden, grads["middle_conv"] = area_back(
        grad_mid, columns, pieces["middle_conv"], 2, [portion.shape for portion in hidden]
    )
    grad_pre_a = through_softplus(grad_hidden, normed_a)
    grad_first, grads["first_gain"], grads["first_bias"] = norm_back(
        grad_pre_a, as_float(pieces["first_gain"]), saved_a
    )
    grad_inputs, grads["first_conv"] = point_back(grad_first, inputs, pieces["first_conv"])
    grad_skip, grads["skip_gain"], grads["skip_bias"] = norm_back(
        grad_wide, as_float(pieces["skip_gain"]), saved_p
    )
    grad_reduced, grads["skip_conv"] = point_back(grad_skip, reduced, pieces["skip_conv"])
    grad_inputs = tuple(
        (
            full_part.at[:, ::2, ::2, :].add(part_reduced)
            for full_part, part_reduced in zip(grad_inputs, grad_reduced)
        )
    )
    return (grad_inputs, grads)


def join_forward(pieces, wide, narrow):
    last = point_conv(narrow, pieces["last_conv"])
    normed, saved = batch_norm(last, as_float(pieces["last_gain"]), as_float(pieces["last_bias"]))
    pre_values = tuple(
        (
            skip_part.astype(jnp.float32) + branch_part
            for skip_part, branch_part in zip(wide, normed)
        )
    )
    ending = tuple((jax.nn.softplus(pre_part) for pre_part in pre_values))
    filler = jnp.zeros((2 * MID,), jnp.float32)
    norm_rows = jnp.stack(
        [jnp.concatenate([saved[0], filler]), jnp.concatenate([saved[1], filler])]
    )
    return (ending, norm_rows, (pre_values, saved))


def join_grads(pieces, narrow, kept, grad_out, gate):
    pre_values, saved = kept
    grad_pre = tuple(
        (
            grad_part * jax.nn.sigmoid(pre_part) * gate
            for grad_part, pre_part in zip(grad_out, pre_values)
        )
    )
    grad_wide = tuple(
        (pre_grad + grad_part * (1.0 - gate) for pre_grad, grad_part in zip(grad_pre, grad_out))
    )
    grad_last, gain_grad, bias_grad = norm_back(grad_pre, as_float(pieces["last_gain"]), saved)
    grad_narrow, weight_grad = point_back(grad_last, narrow, pieces["last_conv"])
    grads = {"last_conv": weight_grad, "last_gain": gain_grad, "last_bias": bias_grad}
    return (grad_wide, grad_narrow, grads)


def split_forward(pieces, wide):
    first = point_conv(wide, pieces["first_conv"])
    normed_a, saved_a = batch_norm(
        first, as_float(pieces["first_gain"]), as_float(pieces["first_bias"])
    )
    hidden = tuple((jax.nn.softplus(portion).astype(jnp.bfloat16) for portion in normed_a))
    middle, columns = area_conv(hidden, pieces["middle_conv"], 1)
    normed_b, saved_b = batch_norm(
        middle, as_float(pieces["middle_gain"]), as_float(pieces["middle_bias"])
    )
    narrow = tuple((jax.nn.softplus(portion) for portion in normed_b))
    filler = jnp.zeros((C_OUT,), jnp.float32)
    norm_rows = jnp.stack(
        [
            jnp.concatenate([saved_a[0], saved_b[0], filler]),
            jnp.concatenate([saved_a[1], saved_b[1], filler]),
        ]
    )
    return (narrow, norm_rows, (normed_a, hidden, columns, normed_b, saved_a, saved_b))


def split_backward(pieces, wide, grad_relay, grad_narrow):
    narrow, norm_rows, kept = split_forward(pieces, wide)
    normed_a, hidden, columns, normed_b, saved_a, saved_b = kept
    grads = {}
    grad_pre_b = through_softplus(grad_narrow, normed_b)
    grad_mid, grads["middle_gain"], grads["middle_bias"] = norm_back(
        grad_pre_b, as_float(pieces["middle_gain"]), saved_b
    )
    grad_hidden, grads["middle_conv"] = area_back(
        grad_mid, columns, pieces["middle_conv"], 1, [portion.shape for portion in hidden]
    )
    grad_pre_a = through_softplus(grad_hidden, normed_a)
    grad_first, grads["first_gain"], grads["first_bias"] = norm_back(
        grad_pre_a, as_float(pieces["first_gain"]), saved_a
    )
    grad_conv_in, grads["first_conv"] = point_back(grad_first, wide, pieces["first_conv"])
    grad_wide = tuple(
        (relay_part + conv_part for relay_part, conv_part in zip(grad_relay, grad_conv_in))
    )
    return (grad_wide, grads)


def pool_grad(final, targets, picks):
    result = []
    for portion, pick_ids in zip(final, picks):
        cubes = jnp.mean(portion * portion * portion, axis=(1, 2)) + POOL_EPS
        factor = jnp.exp(jnp.log(cubes) * (-2.0 / 3.0)) * targets[pick_ids]
        result.append(factor[:, None, None, :] * portion * portion)
    return tuple(result)


def used_size(section):
    return sum((math.prod(entry_shape) for entry_name, entry_shape in section_shapes(section)))


def batch_pass(reals, inputs, gate, targets, picks):
    pieces = [unpack(reals[section], section) for section in range(4)]
    wide_f, narrow_f, rows_0, _ = front_forward(pieces[0], inputs)
    wide_0, narrow_0 = to_low(wide_f), to_low(narrow_f)
    ending_1, rows_1, kept_1 = join_forward(pieces[1], wide_0, narrow_0)
    wide_1 = to_low(ending_1)
    narrow_f, rows_2, _ = split_forward(pieces[2], wide_1)
    narrow_2 = to_low(narrow_f)
    ending_3, rows_3, kept_3 = join_forward(pieces[3], wide_1, narrow_2)
    final = tuple(
        (
            jnp.where(gate > 0, end_part, relay_part.astype(jnp.float32))
            for end_part, relay_part in zip(ending_3, wide_1)
        )
    )
    cotangent = pool_grad(final, targets, picks)
    grad_wide, grad_narrow, grads_3 = join_grads(pieces[3], narrow_2, kept_3, cotangent, gate)
    grad_wide, grads_2 = split_backward(
        pieces[2], wide_1, to_high(to_low(grad_wide)), to_high(to_low(grad_narrow))
    )
    grad_wide, grad_narrow, grads_1 = join_grads(
        pieces[1], narrow_0, kept_1, to_high(to_low(grad_wide)), 1.0
    )
    grad_inputs, grads_0 = front_backward(
        pieces[0], inputs, to_high(to_low(grad_wide)), to_high(to_low(grad_narrow))
    )
    outs = (wide_0, wide_1, wide_1, to_low(final))
    stats = jnp.stack([rows_0, rows_1, rows_2 * gate, rows_3 * gate])
    return (outs, stats, to_low(grad_inputs), (grads_0, grads_1, grads_2, grads_3))


def on_device(
    teach_in,
    stud_in,
    params,
    owners,
    depth_gates,
    teach_ids,
    stud_ids,
    targets,
    moment,
    second,
    gram_stats,
    eigen_basis,
):
    sections = lax.axis_size("pipe")
    rank = lax.axis_index("pipe")
    owner_count = lax.axis_size("dp")
    span_size = params.shape[1]
    flat_size = span_size * owner_count
    owner_rows = lax.all_gather(owners, "pipe", axis=0, tiled=True)
    gathered = lax.all_gather(params[0].astype(jnp.bfloat16), ("pipe", "dp"), axis=0)
    gathered = gathered.reshape(sections, owner_count, span_size)
    reals = []
    for section in range(sections):
        inverse = jnp.argsort(owner_rows[section]).astype(jnp.int32)
        blocks = -(-used_size(section) // span_size)
        reals.append(gathered[section][inverse[:blocks]].reshape(blocks * span_size))
    inputs = (teach_in[0], stud_in[0])
    gate = depth_gates[rank].astype(jnp.float32)
    outs, stats, (teach_grad, stud_grad), grads = batch_pass(
        reals, inputs, gate, targets, (teach_ids[rank], stud_ids[rank])
    )
    segment_teach = lax.all_to_all(
        jnp.stack([part[0] for part in outs]), "pipe", split_axis=0, concat_axis=0, tiled=True
    )
    segment_stud = lax.all_to_all(
        jnp.stack([part[1] for part in outs]), "pipe", split_axis=0, concat_axis=0, tiled=True
    )
    stats = lax.all_to_all(stats, "pipe", split_axis=0, concat_axis=0, tiled=True)
    rows = []
    for section in range(sections):
        flat = pack(grads[section], section, flat_size).reshape(owner_count, span_size)
        rows.append(flat[owner_rows[section]])
    span_total = lax.psum_scatter(
        jnp.stack(rows).reshape(sections * owner_count, span_size),
        ("pipe", "dp"),
        scatter_dimension=0,
        tiled=True,
    ).reshape(span_size)
    total_squares = lax.psum(jnp.sum(span_total * span_total), ("dp", "pipe"))
    grad_norm = jnp.sqrt(total_squares)
    factor = jnp.minimum(1.0, CLIP_NORM / grad_norm)
    clipped = span_total * factor
    matrix = clipped.reshape(span_size // 128, 128)
    gram_old = gram_stats[0]
    basis_old = eigen_basis[0]
    gram_new = DECAY_STATS * gram_old + (1.0 - DECAY_STATS) * jnp.dot(
        matrix.T, matrix, precision=HIGH
    )
    product = jnp.dot(gram_new, basis_old, precision=HIGH)
    rotation = product / jnp.sqrt(jnp.sum(product * product))
    for repeat in range(NS_STEPS):
        square = jnp.dot(rotation.T, rotation, precision=HIGH)
        rotation = 1.5 * rotation - 0.5 * jnp.dot(rotation, square, precision=HIGH)
    moment_old = moment.reshape(span_size // 128, 128)
    initial = jnp.dot(moment_old, basis_old.T, precision=HIGH)
    blended = DECAY_FIRST * initial + (1.0 - DECAY_FIRST) * matrix
    moment_new = jnp.dot(blended, rotation, precision=HIGH)
    rotated = jnp.dot(matrix, rotation, precision=HIGH)
    second_new = (
        DECAY_SECOND * second.reshape(span_size // 128, 128)
        + (1.0 - DECAY_SECOND) * rotated * rotated
    )
    correction = math.sqrt(1.0 - DECAY_SECOND**STEP) / (1.0 - DECAY_FIRST**STEP)
    direction = (
        jnp.dot(moment_new / (jnp.sqrt(second_new) + ADAM_EPS), rotation.T, precision=HIGH)
        * correction
    )
    weights = params.reshape(span_size // 128, 128)
    params_new = weights - LEARN_RATE * (direction + WEIGHT_DECAY * weights)
    return (
        segment_teach[None],
        segment_stud[None],
        teach_grad[None],
        stud_grad[None],
        stats[None, :, None],
        grad_norm,
        clipped.reshape(1, span_size),
        moment_new.reshape(1, span_size),
        second_new.reshape(1, span_size),
        params_new.reshape(1, span_size),
        gram_new[None],
        rotation[None],
    )


MESH = pl.DeviceIdType.MESH
LOW = jnp.bfloat16
FULL = jnp.float32
TILE = 256
WINDOW = 20
STRIDE = 19
EDGE = 64
BIG_ROWS = STRIDE * TILE + EDGE
VEC_TILE = (152, 32, 104, 32)
USED_TILES = (153, 33, 105, 33)
FRONT_WIDE = 88
SMALL_ROWS = 1056
ROWS = 120
PADDED = 128
STUD_ROWS = 48
TEACH_END = 80


def any_spec():
    return pl.BlockSpec(memory_space=pl.ANY)


def smem_spec():
    return pl.BlockSpec(memory_space=pltpu.SMEM)


def vmem_spec():
    return pl.BlockSpec(memory_space=pltpu.VMEM)


def tile_forms(section, tile):
    even = lax.rem(section, 2) == 0
    vector = jnp.where(section == 0, 152, jnp.where(section == 2, 104, 32))
    narrow_end = jnp.where(section == 0, FRONT_WIDE, jnp.where(section == 2, 104, 0))
    narrow = even & (tile < narrow_end)
    plain = tile == vector
    return narrow, plain


def prepare_kernel(owners, params, big, small, ids, flat, sem):
    block, section = owners[0, lax.axis_index("dp")], lax.axis_index("pipe")

    even = lax.rem(section, 2) == 0
    flat[0:EDGE, :] = jnp.zeros((EDGE, 128), FULL)
    flat[STRIDE * TILE : WINDOW * TILE, :] = jnp.zeros((TILE, 128), FULL)
    copy = pltpu.make_async_copy(params.at[:, 0, :], flat.at[pl.ds(6 * block, params.shape[0])], sem)
    copy.start()

    @pl.when(jnp.logical_not(even))
    def _():
        @pl.loop(0, small.shape[0])
        def _(r):
            small[r] = jnp.zeros((TILE, 128), LOW)

    lane = lax.broadcasted_iota(jnp.int32, (8, 128), 1)
    row = jnp.zeros((8, 128), jnp.int32)
    for j in range(8):
        row = jnp.where(lane == j, owners[0, j], row)
    ids[...] = row
    copy.wait()

    def wide_tile(base):
        return [flat[pl.ds(base + j, 16, 16), :].astype(LOW) for j in range(16)]

    @pl.when(even)
    def _():
        @pl.loop(0, STRIDE)
        def _(r):
            narrow, plain = tile_forms(section, STRIDE * block + r)
            base = pl.multiple_of(TILE * r, TILE)

            @pl.when(narrow)
            def _():
                for j in range(4):
                    big[pl.ds(base + 64 * j, 64), :] = flat[pl.ds(base + j, 64, 4), :].astype(LOW)

            @pl.when(plain)
            def _():
                big[pl.ds(base, TILE), :] = flat[pl.ds(base, TILE), :].astype(LOW)

            @pl.when(jnp.logical_not(narrow | plain))
            def _():
                for j, part in enumerate(wide_tile(base)):
                    big[pl.ds(base + 16 * j, 16), :] = part

        big[STRIDE * TILE : BIG_ROWS, :] = flat[STRIDE * TILE : BIG_ROWS, :].astype(LOW)

    @pl.when(jnp.logical_not(even))
    def _():
        @pl.loop(0, WINDOW)
        def _(r):
            tile = STRIDE * block + r
            base = pl.multiple_of(TILE * r, TILE)

            @pl.when(tile == VEC_TILE[1])
            def _():
                small[tile] = flat[pl.ds(base, TILE), :].astype(LOW)

            @pl.when(tile < VEC_TILE[1])
            def _():
                for j, part in enumerate(wide_tile(base)):
                    small[tile, 16 * j : 16 * j + 16, :] = part


def prepare(owners, params):
    return pl.pallas_call(
        prepare_kernel,
        name="prepare",
        out_shape=(
            jax.ShapeDtypeStruct((BIG_ROWS, 128), LOW),
            jax.ShapeDtypeStruct((USED_TILES[1], TILE, 128), LOW),
            jax.ShapeDtypeStruct((8, 128), jnp.int32),
        ),
        in_specs=[smem_spec(), any_spec()],
        out_specs=(vmem_spec(),) * 3,
        scratch_shapes=[pltpu.VMEM((WINDOW * TILE, 128), FULL), pltpu.SemaphoreType.DMA],
        compiler_params=pltpu.CompilerParams(vmem_limit_bytes=60 << 20),
    )(owners, params.reshape(-1, 1, 128))


class Place:
    def __init__(self):
        self.dp = lax.axis_index("dp")
        self.pipe = lax.axis_index("pipe")
        self.x, self.core = self.pipe // 2, self.pipe % 2
        self.z, self.y = self.dp // 2, self.dp % 2

    def device(self, x=None, core=None, z=None, y=None):
        x = self.x if x is None else x
        core = self.core if core is None else core
        z = self.z if z is None else z
        y = self.y if y is None else y
        return {"dp": 2 * z + y, "pipe": 2 * x + core}

    def enter(self):
        barrier = pltpu.get_barrier_semaphore()
        for step in range(1, 8):
            other = lax.rem(self.dp + step, 8)
            pl.semaphore_signal(
                barrier, inc=1, device_id={"dp": other, "pipe": self.pipe}, device_id_type=MESH
            )
        for step in range(1, 4):
            other = lax.rem(self.pipe + step, 4)
            pl.semaphore_signal(
                barrier, inc=1, device_id={"dp": self.dp, "pipe": other}, device_id_type=MESH
            )
        pl.semaphore_wait(barrier, 10)


def remote(src, dst, send, recv, target):
    return pltpu.make_async_remote_copy(
        src_ref=src, dst_ref=dst, send_sem=send, recv_sem=recv, device_id=target, device_id_type=MESH
    )


BIG_HALF = BIG_ROWS // 2
SMALL_HALF = SMALL_ROWS // 2
PARTS = 2
PART_ROWS = BIG_HALF // PARTS
BULK_CUT = 480
LIGHT_CUT = 256
BACK_CUT = 768
GATHER_ORDER = (
    "X1", "Z2", "X2", "Y0", "EY", "EC0", "EC1", "R0", "Z3", "Y1", "Z4", "Y2", "X3", "EC2", "R1",
    "EC3", "Y3", "L0", "X4", "Z5", "L1", "Z6", "X5", "S0", "S1", "R2", "Y4", "Y5", "S2", "L2",
    "Y6", "R3", "Z7", "X6", "Y7", "M1", "S3", "S4", "R4", "X7", "D0", "D1", "S5", "S6", "R5", "M2",
    "R6", "D2", "S7", "D3", "R7", "D4", "D5", "M3", "D6", "D7",
)
REDUCE_ORDER = (
    "A0", "A1", "A2", "A3", "A4", "A5", "L0", "B0", "C0", "C1", "B1", "B2", "B3", "C2", "L1", "L2",
    "A6", "L3", "B4", "C3", "O0", "LS", "A7", "O1", "B5", "B6", "E0", "C4", "O2", "O3", "E1", "E2",
    "C5", "C6", "I0", "B7", "LE", "C7", "I1", "E3", "T1", "I2", "I3", "O4", "O5", "G", "T2", "E4",
    "I4", "O6", "I5", "E5", "O7", "T3",
)


def gather_kernel(big, small, ids, all_big, all_small, table, held_big, held_small, k_sem, big_sem, early, chunk, rising, falling,
                  early_send, early_recv, eu_send, eu_recv, ed_send, ed_recv,
                  z_send, z_recv, x_send, x_recv, y_send, y_recv, dx_send, dx_recv, dy_send, dy_recv,
                  s_send, s_recv, first_send, first_recv, own_sem, id_send, id_recv, lz_send, lz_recv):
    me = Place()
    me.enter()
    x, y, z, core = me.x, me.y, me.z, me.core
    up, down = me.device(z=z + 1), me.device(z=z - 1)
    x_side, y_side, sibling = me.device(x=1 - x), me.device(y=1 - y), me.device(core=1 - core)

    class Stream:
        def __init__(self, n, held, out, start, rows, cut):
            self.n, self.held, self.out, self.start, self.rows, self.cut = n, held, out, start, rows, cut

        def block(self, xo, origin, yo):
            return self.held.at[xo, 2 * origin + yo, pl.ds(self.start, self.rows)]

        def move_x(self, origin):
            block = self.block(x, origin, y)
            return remote(block, block, x_send.at[self.n, origin], x_recv.at[self.n, origin], x_side)

        def move_y(self, origin):
            block = self.block(x, origin, y)
            return remote(block, block, y_send.at[self.n, origin], y_recv.at[self.n, origin], y_side)

        def copies(self, xo, origin, yo):
            block, at = self.block(xo, origin, yo), 8 * xo + 2 * origin + yo
            result = self.out.at[xo, 2 * origin + yo, core, pl.ds(self.start, self.rows)]
            return (
                remote(block, result, s_send.at[self.n, at], s_recv.at[self.n, at], sibling),
                pltpu.make_async_copy(block, result, k_sem.at[self.n, at]),
            )

        def share(self, xo, origin, yo):
            for copy in self.copies(xo, origin, yo):
                copy.start()

        def move_z(self, origin, target, way):
            block = self.block(x, origin, y)
            return remote(block, block, z_send.at[self.n, way, origin], z_recv.at[self.n, origin], target)

        def half_x(self, origin, xo, yo):
            part = self.held.at[xo, 2 * origin + yo, pl.ds(self.start + self.cut, self.rows - self.cut)]
            return remote(part, part, dx_send.at[self.n, origin], dx_recv.at[self.n, origin], x_side)

        def half_y(self, origin, xo, yo):
            part = self.held.at[xo, 2 * origin + yo, pl.ds(self.start, self.cut)]
            return remote(part, part, dy_send.at[self.n, origin], dy_recv.at[self.n, origin], y_side)

        def to_x(self, origin):
            self.move_x(origin).start()

        def to_y(self, origin):
            self.move_y(origin).start()

        def from_x(self, origin):
            self.move_x(origin).wait_recv()
            self.half_y(origin, 1 - x, y).start()
            self.share(1 - x, origin, y)

        def from_y(self, origin):
            self.move_y(origin).wait_recv()
            self.half_x(origin, x, 1 - y).start()
            self.share(x, origin, 1 - y)

        def from_diagonal(self, origin):
            self.half_x(origin, 1 - x, 1 - y).wait_recv()
            self.half_y(origin, 1 - x, 1 - y).wait_recv()
            self.share(1 - x, origin, 1 - y)

        def each(self, step, action):
            if step == 0:
                action(z)
            else:
                pl.when(z >= step)(lambda: action(z - step))
                pl.when(z + step <= 3)(lambda: action(z + step))

        def begin(self):
            pl.when(z < 3)(lambda: self.move_z(z, up, 0).start())
            pl.when(z > 0)(lambda: self.move_z(z, down, 1).start())
            self.share(x, z, y)

        def from_z(self, k):
            @pl.when(z >= k)
            def _():
                self.move_z(z - k, up, 0).wait_recv()
                pl.when(z < 3)(lambda: self.move_z(z - k, up, 0).start())
                self.share(x, z - k, y)

            @pl.when(z + k <= 3)
            def _():
                self.move_z(z + k, down, 1).wait_recv()
                pl.when(z > 0)(lambda: self.move_z(z + k, down, 1).start())
                self.share(x, z + k, y)

        def close(self):
            for origin in range(4):
                self.move_x(origin).wait_send()
                self.move_y(origin).wait_send()
                self.half_x(origin, x, 1 - y).wait_send()
                self.half_y(origin, 1 - x, y).wait_send()
                pl.when((z < 3) & (origin <= z))(lambda: self.move_z(origin, up, 0).wait_send())
                pl.when((z > 0) & (origin >= z))(lambda: self.move_z(origin, down, 1).wait_send())
            self.close_shares()

        def close_shares(self):
            for origin in range(4):
                for xo in range(2):
                    for yo in range(2):
                        away, home = self.copies(xo, origin, yo)
                        away.wait_send()
                        home.wait()
                        theirs = self.out.at[xo, 2 * origin + yo, 1 - core, pl.ds(self.start, self.rows)]
                        at = 8 * xo + 2 * origin + yo
                        remote(theirs, theirs, s_send.at[self.n, at], s_recv.at[self.n, at], sibling).wait_recv()

    class Late(Stream):
        def column_z(self, xo, origin, yo, target, way):
            block = self.block(xo, origin, yo)
            at = 2 * xo + yo
            return remote(
                block, block, lz_send.at[way, at, origin], lz_recv.at[at, origin], target
            )

        def leave(self, xo, yo):
            pl.when(z < 3)(lambda: self.column_z(xo, z, yo, up, 0).start())
            pl.when(z > 0)(lambda: self.column_z(xo, z, yo, down, 1).start())
            self.share(xo, z, yo)

        def step(self, k):
            if k == 0:
                self.move_x(z).start()
                self.move_y(z).start()
                self.leave(x, y)
            elif k == 1:
                self.move_x(z).wait_recv()
                self.half_y(z, 1 - x, y).start()
                self.leave(1 - x, y)
                self.move_y(z).wait_recv()
                self.half_x(z, x, 1 - y).start()
                self.leave(x, 1 - y)
            elif k == 2:
                self.half_x(z, 1 - x, 1 - y).wait_recv()
                self.half_y(z, 1 - x, 1 - y).wait_recv()
                self.leave(1 - x, 1 - y)
            else:
                gap = k - 2

                @pl.when(z >= gap)
                def _():
                    for xo, yo in columns:
                        self.column_z(xo, z - gap, yo, up, 0).wait_recv()
                        pl.when(z < 3)(lambda: self.column_z(xo, z - gap, yo, up, 0).start())
                        self.share(xo, z - gap, yo)

                @pl.when(z + gap <= 3)
                def _():
                    for xo, yo in columns:
                        self.column_z(xo, z + gap, yo, down, 1).wait_recv()
                        pl.when(z > 0)(lambda: self.column_z(xo, z + gap, yo, down, 1).start())
                        self.share(xo, z + gap, yo)

        def close(self):
            self.move_x(z).wait_send()
            self.move_y(z).wait_send()
            self.half_x(z, x, 1 - y).wait_send()
            self.half_y(z, 1 - x, y).wait_send()
            for origin in range(4):
                for xo, yo in columns:
                    pl.when((z < 3) & (origin <= z))(
                        lambda: self.column_z(xo, origin, yo, up, 0).wait_send())
                    pl.when((z > 0) & (origin >= z))(
                        lambda: self.column_z(xo, origin, yo, down, 1).wait_send())
            self.close_shares()

    columns = ((x, y), (1 - x, y), (x, 1 - y), (1 - x, 1 - y))
    bulks = [
        Stream(n, held_big, all_big, PART_ROWS * n, PART_ROWS, BULK_CUT) for n in range(PARTS)
    ]
    light = Late(PARTS, held_small, all_small, 0, SMALL_HALF, LIGHT_CUT)

    order = [
        jnp.where(z < 2, 3, 0),
        jnp.where(z == 0, 2, jnp.where(z == 1, 0, jnp.where(z == 2, 3, 1))),
        jnp.where(z == 0, 1, jnp.where(z == 1, 2, jnp.where(z == 2, 1, 2))),
        z,
    ]

    def cross(k):
        return remote(small.at[2 * order[k] + (1 - y)], early.at[k], early_send.at[k], early_recv.at[k], y_side)

    def own_early(k):
        return pltpu.make_async_copy(small.at[2 * order[k] + y], chunk.at[k], own_sem.at[3 + k])

    def rise(k):
        slot = order[k] - 1
        return remote(chunk.at[k], rising.at[slot], eu_send.at[slot], eu_recv.at[slot], up)

    def fall(k):
        slot = order[k]
        return remote(chunk.at[k], falling.at[slot], ed_send.at[slot], ed_recv.at[slot], down)

    def merge(k, ref, slot):
        @pl.loop(0, 3)
        def _(i):
            part = pl.ds(pl.multiple_of(352 * i, 16), 352)
            chunk[k, part, :] = (chunk[k, part, :].astype(FULL) + ref[slot, part, :].astype(FULL)).astype(LOW)

    def big_part(n):
        return held_big.at[x, me.dp, pl.ds(PART_ROWS * n, PART_ROWS)]

    def big_first(n):
        source = big.at[pl.ds(BIG_HALF + PART_ROWS * n, PART_ROWS)]
        return remote(source, big_part(n), first_send.at[n], first_recv.at[n], sibling)

    def big_own(n):
        return pltpu.make_async_copy(big.at[pl.ds(PART_ROWS * n, PART_ROWS)], big_part(n), big_sem.at[n])

    small_half = held_small.at[x, me.dp]
    small_first = remote(
        chunk.at[3, pl.ds(0, SMALL_HALF)], small_half, first_send.at[PARTS], first_recv.at[PARTS], sibling)

    def early_cross():
        @pl.when(core == 1)
        def _():
            for k in range(4):
                own_early(k).wait()
                cross(k).wait_recv()
                merge(k, early, k)

    def early_chain(k):
        @pl.when(core == 1)
        def _():
            if k < 3:

                @pl.when(order[k] > z)
                def _():
                    @pl.when(z > 0)
                    def _():
                        rise(k).wait_recv()
                        merge(k, rising, order[k] - 1)

                    rise(k).start()

                @pl.when(order[k] < z)
                def _():
                    @pl.when(z < 3)
                    def _():
                        fall(k).wait_recv()
                        merge(k, falling, order[k])

                    fall(k).start()

            else:

                @pl.when(z > 0)
                def _():
                    rise(k).wait_recv()
                    merge(k, rising, z - 1)

                @pl.when(z < 3)
                def _():
                    fall(k).wait_recv()
                    merge(k, falling, z)

                small_first.start()
                copy = pltpu.make_async_copy(
                    chunk.at[3, pl.ds(SMALL_HALF, SMALL_HALF)], small_half, own_sem.at[0])
                copy.start()
                copy.wait()

    def light_begin():
        @pl.when(core == 0)
        def _():
            small_first.wait_recv()

        light.step(0)

    @pl.when(core == 0)
    def _():
        for n in range(PARTS):
            big_first(n).start()
            big_own(n).start()

    @pl.when(core == 1)
    def _():
        for k in range(4):
            cross(k).start()
            own_early(k).start()

    for n in range(PARTS):
        pl.when(core == 0)(lambda: big_own(n).wait())
        pl.when(core == 1)(lambda: big_first(n).wait_recv())
        bulks[n].begin()
        if n == 0:
            bulks[n].to_x(z)
    row = pltpu.make_async_copy(ids, table.at[me.pipe], own_sem.at[2])
    row.start()
    for step in range(1, 4):
        remote(
            ids, table.at[me.pipe], id_send.at[step], id_recv.at[step],
            {"dp": me.dp, "pipe": lax.rem(me.pipe + step, 4)},
        ).start()

    actions = {"EY": early_cross, "L0": light_begin}
    for k in range(4):
        actions["EC%d" % k] = functools.partial(early_chain, k)
        if k:
            actions["M%d" % k] = functools.partial(light.step, k + 2)
            if k < 3:
                actions["L%d" % k] = functools.partial(light.step, k)
        for n, bulk in enumerate(bulks):
            name = str(PARTS * k + n)
            for letter, action in zip("XYSRD", (bulk.to_x, bulk.to_y, bulk.from_x, bulk.from_y, bulk.from_diagonal)):
                actions[letter + name] = functools.partial(bulk.each, k, action)
            if k:
                actions["Z" + name] = functools.partial(bulk.from_z, k)
    for event in GATHER_ORDER:
        actions[event]()
    for bulk in bulks:
        bulk.close()
    light.close()
    row.wait()
    for step in range(1, 4):
        here = lax.rem(me.pipe + 4 - step, 4)
        move = remote(
            ids, table.at[here], id_send.at[step], id_recv.at[step],
            {"dp": me.dp, "pipe": lax.rem(me.pipe + step, 4)},
        )
        move.wait_recv()
        move.wait_send()

    @pl.when(core == 0)
    def _():
        for n in range(PARTS):
            big_first(n).wait_send()

    @pl.when(core == 1)
    def _():
        small_first.wait_send()
        for k in range(4):
            cross(k).wait_send()
        for k in range(3):
            pl.when(order[k] > z)(lambda: rise(k).wait_send())
            pl.when(order[k] < z)(lambda: fall(k).wait_send())


def gather_all(big, small, ids):
    sem = pltpu.SemaphoreType.DMA
    return pl.pallas_call(
        gather_kernel,
        name="gather_all",
        out_shape=(
            jax.ShapeDtypeStruct((2, 8, 2, BIG_HALF, 128), LOW),
            jax.ShapeDtypeStruct((2, 8, 2, SMALL_HALF, 128), LOW),
            jax.ShapeDtypeStruct((4, 8, 128), jnp.int32),
        ),
        in_specs=[any_spec()] * 3,
        out_specs=(any_spec(),) * 3,
        scratch_shapes=[
            pltpu.VMEM((2, 8, BIG_HALF, 128), LOW), pltpu.VMEM((2, 8, SMALL_HALF, 128), LOW),
            sem((PARTS + 1, 16)), sem((PARTS,)),
            pltpu.VMEM((4, SMALL_ROWS, 128), LOW), pltpu.VMEM((4, SMALL_ROWS, 128), LOW),
            pltpu.VMEM((3, SMALL_ROWS, 128), LOW), pltpu.VMEM((3, SMALL_ROWS, 128), LOW),
            sem((4,)), sem((4,)), sem((3,)), sem((3,)), sem((3,)), sem((3,)),
            sem((PARTS + 1, 2, 4)), sem((PARTS + 1, 4)),
            sem((PARTS + 1, 4)), sem((PARTS + 1, 4)), sem((PARTS + 1, 4)), sem((PARTS + 1, 4)),
            sem((PARTS + 1, 4)), sem((PARTS + 1, 4)), sem((PARTS + 1, 4)), sem((PARTS + 1, 4)),
            sem((PARTS + 1, 16)), sem((PARTS + 1, 16)),
            sem((PARTS + 1,)), sem((PARTS + 1,)), sem((7,)), sem((4,)), sem((4,)),
            sem((2, 4, 4)), sem((4, 4)),
        ],
        compiler_params=pltpu.CompilerParams(
            collective_id=0, has_side_effects=True, vmem_limit_bytes=60 << 20
        ),
    )(big, small.reshape(8, SMALL_ROWS, 128), ids)


def soft(value):
    return jnp.maximum(value, 0.0) + jnp.log1p(jnp.exp(-jnp.abs(value)))


def gate_of(value):
    small = jnp.exp(-jnp.abs(value))
    share = 1.0 / (1.0 + small)
    return jnp.where(value >= 0, share, small * share)


def standardize(z):
    count = z.shape[0]
    centre = jnp.sum(z, axis=0, keepdims=True) / count
    away = z - centre
    spread = jnp.sum(away * away, axis=0, keepdims=True) / count
    inverse = lax.rsqrt(spread + NORM_EPS)
    return away * inverse, centre, spread, inverse


def unstandardize(grad, standard, gain, inverse):
    count = grad.shape[0]
    grad_sum = jnp.sum(grad, axis=0, keepdims=True)
    grad_dot = jnp.sum(grad * standard, axis=0, keepdims=True)
    result = gain * inverse * (grad - grad_sum / count - standard * (grad_dot / count))
    return result, grad_dot, grad_sum


def pad_low(value):
    zeros = jnp.zeros((PADDED - ROWS, value.shape[1]), FULL)
    return jnp.concatenate([value, zeros], axis=0).astype(LOW)


def mul(a, b):
    return jnp.dot(a, b, preferred_element_type=FULL)


def mul_t(a, b):
    return lax.dot_general(a, b, (((1,), (1,)), ((), ())), preferred_element_type=FULL)


def narrow_part(ref, start, count, blocks=range(4)):
    return jnp.concatenate(
        [ref[pl.ds(start, count), 64 * j : 64 * j + 64, :].reshape(64 * count, 128) for j in blocks],
        axis=1,
    )


def put_narrow(ref, start, count, value):
    for j in range(4):
        ref[pl.ds(start, count), 64 * j : 64 * j + 64, :] = (
            value[:, 128 * j : 128 * j + 128].astype(LOW).reshape(count, 64, 128)
        )


def wide_part(ref, start, count, c):
    return jnp.concatenate(
        [
            ref[start : start + count, 32 * c + 16 * h : 32 * c + 16 * h + 16, :].reshape(
                16 * count, 128
            )
            for h in range(2)
        ],
        axis=1,
    )


def put_wide(ref, start, count, c, value):
    for h in range(2):
        ref[start : start + count, 32 * c + 16 * h : 32 * c + 16 * h + 16, :] = (
            value[:, 128 * h : 128 * h + 128].astype(LOW).reshape(count, 16, 128)
        )


def chunks(count):
    def run(body):
        for c in range(count):
            body(c)

    return run


def step_kernel(table, gates, teach_ids, stud_ids, all_big, all_small, teach_x, stud_x, targets, grid,
                moves,
                wide0, wide1, final, stats, grad_teach, grad_stud, out_big, out_small,
                x,
                w0, w1, w2, w3, edges, loose, vec, grad_vec, raw,
                std_a, std_b, std_p, std_1, std_c, std_d, hidden, cols0, cols2,
                nar0, nar2, turned, turned_x, relay, dz_a, dz_n, acc, acc_x, grad_h,
                wanted, inv, in_sem, edge_sem, out_sem):
    rank = lax.axis_index("pipe")
    gate = gates[rank].astype(FULL)
    for group in range(2):
        for j in range(8):
            inv[8 * group + table[2 * group, 0, j]] = j
    picks = [teach_ids[k, rank] for k in range(2)] + [stud_ids[rank, k] for k in range(3)]
    rows = [
        pltpu.make_async_copy(targets.at[pl.ds(pick, 1)], wanted.at[pl.ds(k, 1)], edge_sem.at[12 + k])
        for k, pick in enumerate(picks)
    ]
    for fetched in rows:
        fetched.start()
    weights = (w0, w1, w2, w3)
    loads = {0: [], 1: [], 2: [], 3: []}
    front, split = w0.reshape(USED_TILES[0] * TILE, 128), w2.reshape(115 * TILE, 128)
    for group, weight, blocks in ((0, front, 8), (1, split, 6)):
        for b in range(blocks):
            at, here = 8 * group + b, inv[8 * group + b]
            count = min(STRIDE, VEC_TILE[2 * group] + 1 - STRIDE * b) * TILE
            loads[2 * group].append(pltpu.make_async_copy(
                all_big.at[group, here, pl.ds(0, count)], weight.at[pl.ds(STRIDE * TILE * b, count)],
                in_sem.at[0, at]))
            if b < blocks - 1:
                loads[2 * group].append(pltpu.make_async_copy(
                    all_big.at[group, here, pl.ds(STRIDE * TILE, EDGE)], edges.at[7 * group + b],
                    edge_sem.at[7 * group + b]))
            elif group == 0:
                loads[0].append(pltpu.make_async_copy(
                    all_big.at[0, here, pl.ds(STRIDE * TILE, EDGE)],
                    front.at[pl.ds(VEC_TILE[0] * TILE, EDGE)], edge_sem.at[17]))
    loads[1].append(pltpu.make_async_copy(all_small.at[0], w1, in_sem.at[0, 14]))
    loads[3].append(pltpu.make_async_copy(all_small.at[1], w3, in_sem.at[0, 15]))
    for section in range(4):
        for load in loads[section]:
            load.start()

    raw[...] = jnp.zeros_like(raw)
    loose[...] = jnp.zeros_like(loose)
    grad_vec[...] = jnp.zeros_like(grad_vec)

    def edge_parts(tile, is_narrow):
        count, size = (4, 64) if is_narrow else (16, 16)
        for j in range(count):
            yield pl.ds(j, 16, count), slice(size * j, size * j + 16)

    def is_narrow(section, tile):
        return section == 2 or tile < FRONT_WIDE

    def merge_edge(section, tile, at):
        ref = weights[section]
        loose[0:EDGE, :] = edges[at].astype(FULL)
        for lying, here in edge_parts(tile, is_narrow(section, tile)):
            ref[tile, here, :] = (ref[tile, here, :].astype(FULL) + loose[lying, :]).astype(LOW)

    def take_edge(section, tile, at):
        ref = weights[section]
        for lying, here in edge_parts(tile, is_narrow(section, tile)):
            loose[lying, :] = ref[tile, here, :].astype(FULL)
        edges[at] = loose[0:EDGE, :].astype(LOW)

    def settle(section, blocks=None):
        if section == 0:
            for b in blocks:
                for load in loads[0][2 * b : 2 * b + 2]:
                    load.wait()
            if 7 in blocks:
                vec[0] = w0[VEC_TILE[0], 0:48, :].astype(FULL)
            else:
                for b in range(7):
                    merge_edge(0, 19 * b + 19, b)
            return
        for load in loads[section]:
            load.wait()
        if section == 2:
            for b in range(5):
                merge_edge(2, 19 * b + 19, 7 + b)
        vec[section] = weights[section][VEC_TILE[section], 0:48, :].astype(FULL)

    def row(section, start):
        return jnp.concatenate(
            [vec[section, pl.ds(start + h, 1), :] for h in range(2)], axis=1
        )

    def put_row(section, start, value):
        for h in range(2):
            grad_vec[section, pl.ds(start + h, 1), :] = value[:, 128 * h : 128 * h + 128]

    def put_stats(section, column, centre, spread):
        raw[2 * section : 2 * section + 1, pl.ds(column, 256)] = centre
        raw[2 * section + 1 : 2 * section + 2, pl.ds(column, 256)] = spread

    def inverse_of(section, column):
        return lax.rsqrt(raw[2 * section + 1 : 2 * section + 2, pl.ds(column, 256)] + NORM_EPS)

    def lanes(c):
        return slice(256 * c, 256 * c + 256)

    at_row, at_col, side = grid[0], grid[1], grid[2]

    def masked(value, dr, dc):
        ok = (at_row + dr >= 0) & (at_row + dr < side) & (at_col + dc >= 0) & (at_col + dc < side)
        return jnp.concatenate(
            [jnp.where(ok, value[:, 128 * j : 128 * j + 128], 0.0) for j in range(4)], axis=1
        )

    def rolled(value, sign, dr, dc):
        parts = []
        for start, end, across, down in ((0, STUD_ROWS, 1, 4), (STUD_ROWS, ROWS, 2, 12)):
            by = (sign * (dr * down + dc * across)) % (end - start)
            part = value[start:end]
            parts.append(part if by == 0 else pltpu.roll(part, by, 0))
        return jnp.concatenate(parts, axis=0)

    def taps(stride):
        for t in range(9):
            r, q = t // 3, t % 3
            if stride == 1:
                yield t, 0, r - 1, q - 1
            else:
                phase = 2 * (1 if r != 1 else 0) + (1 if q != 1 else 0)
                yield t, phase, -1 if r == 0 else 0, -1 if q == 0 else 0

    def one_hot(index, width):
        lane = lax.broadcasted_iota(jnp.int32, index.shape, 1)
        parts = [jnp.where(lane + start == index, 1.0, 0.0) for start in range(0, width, 128)]
        return jnp.concatenate(parts, axis=1)[:, 0:width].astype(LOW)

    crops = [teach_x[:, crop, :] for crop in range(2)]
    for p in range(4):
        at = slice(PADDED * p, PADDED * p + PADDED)
        from_teach = sum(
            mul(one_hot(moves[crop, at, :], teach_x.shape[0]), crops[crop]) for crop in range(2)
        )
        x[p] = (from_teach + mul(one_hot(moves[2, at, :], stud_x.shape[0]), stud_x[...])).astype(LOW)

    settle(0, (0, 7))
    whole_x = x[...].reshape(4 * PADDED, C_IN)
    for c in range(2):
        z = mul(whole_x, narrow_part(w0, 0, 16, (2 * c, 2 * c + 1)))
        z = jnp.concatenate([z[PADDED * p : PADDED * p + ROWS] for p in range(4)], axis=0)
        standard, centre, spread, _ = standardize(z)
        put_stats(0, 256 * c, centre, spread)
        std_a[:, 256 * c : 256 * c + 256] = standard
        hidden[:, 256 * c : 256 * c + 256] = (
            soft(row(0, 2 * c) * standard + row(0, 4 + 2 * c)).astype(LOW).astype(FULL)
        )

    for t, phase, dr, dc in taps(2):
        cols0[t] = pad_low(masked(rolled(hidden[ROWS * phase : ROWS * phase + ROWS, :], -1, dr, dc), dr, dc))
    acc[...] = jnp.zeros_like(acc)
    settle(0, (1, 2, 3, 4, 5, 6))

    @chunks(9)
    def _(t):
        acc[...] += mul(cols0[t], narrow_part(w0, 16 + 8 * t, 8))

    def middle(section, std, nar):
        for c in range(2):
            at = slice(256 * c, 256 * c + 256)
            standard, centre, spread, _ = standardize(acc[0:ROWS, at])
            put_stats(section, MID + 256 * c, centre, spread)
            std[:, at] = standard
            nar[:, at] = pad_low(soft(row(section, 8 + 2 * c) * standard + row(section, 12 + 2 * c)))

    middle(0, std_b, nar0)
    acc[...] = jnp.zeros_like(acc)
    settle(1)
    settle(2)

    @chunks(8)
    def _(c):
        at = lanes(c)
        standard, centre, spread, _ = standardize(mul(x[0], wide_part(w0, FRONT_WIDE, 64, c))[0:ROWS])
        put_stats(0, 2 * MID + 256 * c, centre, spread)
        std_p[:, at] = standard
        low = pad_low(row(0, 16 + 2 * c) * standard + row(0, 32 + 2 * c))
        wide0[:, at] = low
        standard, centre, spread, _ = standardize(mul(nar0[...], wide_part(w1, 0, 32, c))[0:ROWS])
        put_stats(1, 256 * c, centre, spread)
        std_1[:, at] = standard
        pre = low.astype(FULL)[0:ROWS] + row(1, 2 * c) * standard + row(1, 16 + 2 * c)
        low = pad_low(soft(pre))
        wide1[:, at] = low
        acc[...] += mul(low, narrow_part(w2, 4 * c, 4))

    for c in range(2):
        at = slice(256 * c, 256 * c + 256)
        standard, centre, spread, _ = standardize(acc[0:ROWS, at])
        put_stats(2, 256 * c, centre, spread)
        std_c[:, at] = standard
        hidden[0:ROWS, at] = soft(row(2, 2 * c) * standard + row(2, 4 + 2 * c)).astype(LOW).astype(FULL)
    for t, phase, dr, dc in taps(1):
        cols2[t] = pad_low(masked(rolled(hidden[0:ROWS, :], -1, dr, dc), dr, dc))
    acc[...] = jnp.zeros_like(acc)

    @chunks(9)
    def _(t):
        acc[...] += mul(cols2[t], narrow_part(w2, 32 + 8 * t, 8))

    middle(2, std_d, nar2)

    turned[...] = nar2[...].T
    acc[...] = jnp.zeros_like(acc)
    settle(3)
    for fetched in rows:
        fetched.wait()

    teach_rows = ROWS - STUD_ROWS
    first_crop = lax.rem(lax.broadcasted_iota(jnp.int32, (teach_rows, 256), 0), 2) == 0

    def spread_rows(values):
        first, second = (jnp.broadcast_to(value, (teach_rows, 256)) for value in values[0:2])
        parts = [jnp.broadcast_to(value, (16, 256)) for value in values[2:5]]
        parts.append(jnp.where(first_crop, first, second))
        return jnp.concatenate(parts, axis=0)

    def crop_sums(value):
        def total(part):
            return jnp.sum(part, axis=0, keepdims=True)

        teach = value[STUD_ROWS:ROWS]
        return [
            total(jnp.where(first_crop, teach, 0.0)),
            total(jnp.where(first_crop, 0.0, teach)),
            total(value[0:16]),
            total(value[16:32]),
            total(value[32:48]),
        ]

    @chunks(8)
    def _(c):
        at = lanes(c)
        weight = wide_part(w3, 0, 32, c)
        standard, centre, spread, inverse = standardize(mul(nar2[...], weight)[0:ROWS])
        put_stats(3, 256 * c, centre, spread)
        gain = row(3, 2 * c)
        before = wide1[:, at].astype(FULL)[0:ROWS]
        pre = before + gain * standard + row(3, 16 + 2 * c)
        ending = jnp.where(gate > 0, soft(pre), before)
        final[:, at] = pad_low(ending)
        square = ending * ending
        factors = []
        for crop, total in enumerate(crop_sums(square * ending)):
            mean = total / (36.0 if crop < 2 else 16.0) + POOL_EPS
            factors.append(jnp.exp(jnp.log(mean) * (-2.0 / 3.0)) * wanted[crop : crop + 1, at])
        cotangent = spread_rows(factors) * square
        grad_pre = cotangent * gate_of(pre) * gate
        relay[:, at] = pad_low(grad_pre + cotangent * (1.0 - gate))
        result, grad_gain, grad_bias = unstandardize(grad_pre, standard, gain, inverse)
        put_row(3, 2 * c, grad_gain)
        put_row(3, 16 + 2 * c, grad_bias)
        low = pad_low(result)
        acc[...] += mul_t(low, weight)
        put_wide(w3, 0, 32, c, mul(turned[...], low))

    def flush(section):
        weights[section][VEC_TILE[section]] = grad_vec[section].astype(LOW)

    flush(3)
    stores = [pltpu.make_async_copy(w3, out_small.at[1], out_sem.at[16])]
    stores[-1].start()

    def middle_back(section, std):
        for c in range(2):
            at = slice(256 * c, 256 * c + 256)
            gain, bias = row(section, 8 + 2 * c), row(section, 12 + 2 * c)
            grad = acc[0:ROWS, at].astype(LOW).astype(FULL) * gate_of(gain * std[:, at] + bias)
            result, grad_gain, grad_bias = unstandardize(
                grad, std[:, at], gain, inverse_of(section, MID + 256 * c)
            )
            put_row(section, 8 + 2 * c, grad_gain)
            put_row(section, 12 + 2 * c, grad_bias)
            dz_n[:, at] = pad_low(result)

    def taps_back(weight, start, cols, stride, phases):
        grad_h[0 : ROWS * phases, :] = jnp.zeros((ROWS * phases, MID), FULL)
        for t, phase, dr, dc in taps(stride):
            part = mul_t(dz_n[...], narrow_part(weight, start + 8 * t, 8))[0:ROWS]
            at = slice(ROWS * phase, ROWS * phase + ROWS)
            grad_h[at, :] += rolled(masked(part, dr, dc), 1, dr, dc)
            put_narrow(weight, start + 8 * t, 8, mul(cols[t].T, dz_n[...]))

    middle_back(2, std_d)
    taps_back(w2, 32, cols2, 1, 1)
    for c in range(2):
        at = slice(256 * c, 256 * c + 256)
        gain, bias = row(2, 2 * c), row(2, 4 + 2 * c)
        grad = grad_h[0:ROWS, at] * gate_of(gain * std_c[:, at] + bias)
        result, grad_gain, grad_bias = unstandardize(grad, std_c[:, at], gain, inverse_of(2, 256 * c))
        put_row(2, 2 * c, grad_gain)
        put_row(2, 4 + 2 * c, grad_bias)
        dz_n[:, at] = pad_low(result)
    turned[...] = nar0[...].T
    turned_x[...] = x[0].T
    acc[...] = jnp.zeros_like(acc)
    acc_x[...] = jnp.zeros_like(acc_x)

    @chunks(8)
    def _(c):
        at = lanes(c)
        low = dz_n[...]
        grad = relay[:, at].astype(FULL) + mul_t(low, narrow_part(w2, 4 * c, 4))
        put_narrow(w2, 4 * c, 4, mul(wide1[:, at].T, low))
        grad = grad.astype(LOW).astype(FULL)[0:ROWS]
        gain = row(1, 2 * c)
        pre = wide0[:, at].astype(FULL)[0:ROWS] + gain * std_1[:, at] + row(1, 16 + 2 * c)
        grad = grad * gate_of(pre)
        result, grad_gain, grad_bias = unstandardize(
            grad, std_1[:, at], gain, inverse_of(1, 256 * c)
        )
        put_row(1, 2 * c, grad_gain)
        put_row(1, 16 + 2 * c, grad_bias)
        low = pad_low(result)
        acc[...] += mul_t(low, wide_part(w1, 0, 32, c))
        put_wide(w1, 0, 32, c, mul(turned[...], low))
        grad = grad.astype(LOW).astype(FULL)
        result, grad_gain, grad_bias = unstandardize(
            grad, std_p[:, at], row(0, 16 + 2 * c), inverse_of(0, 2 * MID + 256 * c)
        )
        put_row(0, 16 + 2 * c, grad_gain)
        put_row(0, 32 + 2 * c, grad_bias)
        low = pad_low(result)
        acc_x[...] += mul_t(low, wide_part(w0, FRONT_WIDE, 64, c))
        put_wide(w0, FRONT_WIDE, 64, c, mul(turned_x[...], low))

    flush(1)
    flush(2)
    w2[105:115] = jnp.zeros((10, TILE, 128), LOW)
    stores.append(pltpu.make_async_copy(w1, out_small.at[0], out_sem.at[17]))
    stores[-1].start()
    def store(source, group, b, start, semaphore):
        count = source.shape[0]
        stores.append(pltpu.make_async_copy(
            source, out_big.at[group, inv[8 * group + b], pl.ds(start, count)], out_sem.at[semaphore]))
        stores[-1].start()

    for b in range(8):
        if b < 5:
            take_edge(2, 19 * b + 19, 7 + b)
            store(split.at[pl.ds(STRIDE * TILE * b, STRIDE * TILE)], 1, b, 0, 8 + b)
            store(edges.at[7 + b], 1, b, STRIDE * TILE, 20 + b)
        else:
            first = 95 if b == 5 else 105
            store(split.at[pl.ds(TILE * first, 10 * TILE)], 1, b, 0, 8 + b)
            store(split.at[pl.ds(TILE * 105, BIG_ROWS - 10 * TILE)], 1, b, 10 * TILE, 20 + b)

    def store_front(blocks):
        for b in blocks:
            if b == 7:
                edges[12] = w0[VEC_TILE[0], 0:EDGE, :]
            else:
                take_edge(0, 19 * b + 19, b)
            store(front.at[pl.ds(STRIDE * TILE * b, STRIDE * TILE)], 0, b, 0, b)
            store(edges.at[12 if b == 7 else b], 0, b, STRIDE * TILE, 28 + b)

    store_front((5, 6))
    middle_back(0, std_b)
    taps_back(w0, 16, cols0, 2, 4)
    store_front((1, 2, 3, 4))
    for c in range(2):
        at = slice(256 * c, 256 * c + 256)
        gain, bias = row(0, 2 * c), row(0, 4 + 2 * c)
        grad = grad_h[:, at] * gate_of(gain * std_a[:, at] + bias)
        result, grad_gain, grad_bias = unstandardize(grad, std_a[:, at], gain, inverse_of(0, 256 * c))
        put_row(0, 2 * c, grad_gain)
        put_row(0, 4 + 2 * c, grad_bias)
        for p in range(4):
            dz_a[PADDED * p : PADDED * p + PADDED, at] = pad_low(result[ROWS * p : ROWS * p + ROWS])

    place_teach = one_hot(moves[3, 0 : grad_teach.shape[0], :], 4 * PADDED)
    place_stud = one_hot(moves[4, 0 : stud_x.shape[0], :], 4 * PADDED)

    @chunks(4)
    def _(c):
        at = lanes(c)
        low = dz_a[...]
        part = mul_t(low, narrow_part(w0, 4 * c, 4))
        part = jnp.concatenate([part[0:PADDED] + acc_x[:, at], part[PADDED:]], axis=0).astype(LOW)
        grad_teach[:, at] = mul(place_teach, part).astype(LOW)
        grad_stud[:, at] = mul(place_stud, part).astype(LOW)
        put_narrow(w0, 4 * c, 4, mul(x[:, :, at].reshape(4 * PADDED, 256).T, low))

    flush(0)
    store_front((0, 7))
    for section in range(4):
        part = raw[2 * section : 2 * section + 2]
        stats[section, 0:2] = part if section < 2 else part * gate
        stats[section, 2:8] = jnp.zeros((6, 2 * MID + C_OUT), FULL)
    for store in stores:
        store.wait()


def run_step(table, gates, teach_ids, stud_ids, all_big, all_small, teach_x, stud_x, targets):
    spots = np.zeros((3, ROWS, 128), np.int32)
    for r in range(ROWS):
        width = 4 if r < STUD_ROWS else 6
        at = r % 16 if r < STUD_ROWS else (r - STUD_ROWS) // 2
        spots[0, r], spots[1, r], spots[2, r] = at // width, at % width, width
    moves = np.full((5, 4 * PADDED, 128), -1, np.int32)
    for p in range(4):
        for r in range(ROWS):
            high, across = 2 * spots[0, r, 0] + p // 2, 2 * spots[1, r, 0] + p % 2
            if r < STUD_ROWS:
                lies = 64 * (r // 16) + 8 * high + across
                moves[2, PADDED * p + r] = lies
                moves[4, lies] = PADDED * p + r
            else:
                lies, crop = 12 * high + across, (r - STUD_ROWS) % 2
                moves[crop, PADDED * p + r] = lies
                moves[3, 2 * lies + crop] = PADDED * p + r
    sem = pltpu.SemaphoreType.DMA
    wide = jax.ShapeDtypeStruct((PADDED, C_OUT), LOW)
    vm = pltpu.VMEM
    return pl.pallas_call(
        step_kernel,
        name="step",
        out_shape=(
            wide, wide, wide,
            jax.ShapeDtypeStruct((4, 8, 2 * MID + C_OUT), FULL),
            jax.ShapeDtypeStruct((2 * teach_x.shape[0], C_IN), LOW),
            jax.ShapeDtypeStruct(stud_x.shape, LOW),
            jax.ShapeDtypeStruct((2, 8, BIG_ROWS, 128), LOW),
            jax.ShapeDtypeStruct((2, USED_TILES[1], TILE, 128), LOW),
        ),
        in_specs=[smem_spec()] * 4 + [any_spec()] * 2 + [vmem_spec()] * 2 + [any_spec()] + [vmem_spec()] * 2,
        out_specs=(vmem_spec(),) * 6 + (any_spec(),) * 2,
        scratch_shapes=[
            vm((4, PADDED, C_IN), LOW),
            vm((153, TILE, 128), LOW), vm((33, TILE, 128), LOW), vm((115, TILE, 128), LOW), vm((33, TILE, 128), LOW),
            vm((13, EDGE, 128), LOW), vm((TILE, 128), FULL), vm((4, 48, 128), FULL), vm((4, TILE, 128), FULL),
            vm((8, 2 * MID + C_OUT), FULL),
            vm((4 * ROWS, MID), FULL), vm((ROWS, MID), FULL), vm((ROWS, C_OUT), FULL), vm((ROWS, C_OUT), FULL),
            vm((ROWS, MID), FULL), vm((ROWS, MID), FULL), vm((4 * ROWS, MID), FULL),
            vm((9, PADDED, MID), LOW), vm((9, PADDED, MID), LOW),
            vm((PADDED, MID), LOW), vm((PADDED, MID), LOW), vm((MID, PADDED), LOW), vm((C_IN, PADDED), LOW),
            vm((PADDED, C_OUT), LOW), vm((4 * PADDED, MID), LOW), vm((PADDED, MID), LOW),
            vm((PADDED, MID), FULL), vm((PADDED, C_IN), FULL), vm((4 * ROWS, MID), FULL),
            vm((8, C_OUT), FULL), pltpu.SMEM((16,), jnp.int32),
            sem((2, 16)), sem((18,)), sem((36,)),
        ],
        compiler_params=pltpu.CompilerParams(vmem_limit_bytes=60 << 20),
    )(table, gates, teach_ids, stud_ids, all_big, all_small, teach_x, stud_x, targets, jnp.asarray(spots), jnp.asarray(moves))


def reduce_kernel(big, small, wide0, wide1, final, stats, table,
                  out_big, out_small, seg_stud, seg_teach, out_stats, norm, factor,
                  got, halves_x, halves_y, from_x, from_y, from_low, from_high, stage, total,
                  l_got, l_stage, l_low, l_high, l_halves_x, l_halves_y, l_from_x, l_from_y, l_total,
                  late, late_half, owner_row, by_pipe, by_dp, mine, part_sum,
                  s_send, s_recv, ls_send, ls_recv, hx_send, hx_recv, hy_send, hy_recv, x_send, x_recv, y_send, y_recv,
                  zu_send, zu_recv, zd_send, zd_recv, lu_send, lu_recv, ld_send, ld_recv,
                  stage_sem, l_stage_sem, out_sem, big_sem, late_send, late_recv, join_send, join_recv,
                  seg_send, seg_recv, stat_send, stat_recv, p_send, p_recv, d_send, d_recv):
    me = Place()
    me.enter()
    x, y, z, core = me.x, me.y, me.z, me.core
    up, down = me.device(z=z + 1), me.device(z=z - 1)
    x_side, y_side, sibling = me.device(x=1 - x), me.device(y=1 - y), me.device(core=1 - core)
    order = [
        jnp.where(z < 2, 3, 0),
        jnp.where(z == 0, 2, jnp.where(z == 1, 0, jnp.where(z == 2, 3, 1))),
        jnp.where(z == 0, 1, jnp.where(z == 1, 2, jnp.where(z == 2, 1, 2))),
        z,
    ]
    columns = ((1 - x, 1 - y), (x, 1 - y), (1 - x, y), (x, y))
    groups = {"A": (0,), "C": (1,), "B": (2,), "O": (3,)}
    sequence = [
        (group, int(event[1])) for event in REDUCE_ORDER for group in groups.get(event[0], ())
    ]
    l_sequence = [(group, k) for k in range(4) for group in range(4)]

    def all_of(copies, act):
        for copy in copies:
            act(copy)

    def over(start, count, piece):
        whole = count // 512
        if whole:

            @pl.loop(0, whole)
            def _(i):
                piece(pl.multiple_of(start + 512 * i, 16), 512)

        if count % 512:
            piece(start + 512 * whole, count % 512)

    items = 4 * PARTS

    def source(group, q, half):
        xo, yo = columns[group]
        part = pl.ds(PART_ROWS * (q % PARTS), PART_ROWS)
        return big.at[xo, 2 * order[q // PARTS] + yo, half, part]

    def l_source(group, k, half):
        xo, yo = columns[group]
        return small.at[xo, 2 * order[k] + yo, half]

    def share(group, q):
        at = items * group + q
        return remote(source(group, q, 1 - core), got.at[at], s_send.at[at], s_recv.at[at], sibling)

    def l_share(group, k):
        at = 4 * group + k
        return remote(l_source(group, k, 1 - core), l_got.at[at], ls_send.at[at], ls_recv.at[at], sibling)

    def fetch(n):
        return pltpu.make_async_copy(source(*sequence[n], core), stage.at[n % 4], stage_sem.at[n % 4])

    def l_fetch(group, k):
        at = 4 * group + k
        return pltpu.make_async_copy(l_source(group, k, core), l_stage.at[at], l_stage_sem.at[at])

    def add(target, at, other, slot, start, count, extras):
        def piece(begin, size):
            part = pl.ds(begin, size)
            sums = target[at, part, :].astype(FULL) + other[slot, part, :].astype(FULL)
            for ref, k in extras:
                sums = sums + ref[k, pl.ds(begin - start, size), :].astype(FULL)
            target[at, part, :] = sums.astype(LOW)

        over(start, count, piece)

    def send_half_x(k):
        return remote(got.at[k, pl.ds(BACK_CUT, PART_ROWS - BACK_CUT)], halves_x.at[k],
                      hx_send.at[k], hx_recv.at[k], x_side)

    def send_half_y(k):
        return remote(got.at[k, pl.ds(0, BACK_CUT)], halves_y.at[k], hy_send.at[k], hy_recv.at[k], y_side)

    def send_y(k):
        return remote(got.at[items + k], from_y.at[k], y_send.at[k], y_recv.at[k], y_side)

    def send_x(k):
        return remote(got.at[2 * items + k], from_x.at[k], x_send.at[k], x_recv.at[k], x_side)

    def low_slot(q):
        return PARTS * (order[q // PARTS] - 1) + q % PARTS

    def high_slot(q):
        return PARTS * order[q // PARTS] + q % PARTS

    def send_up(q):
        slot = low_slot(q)
        return remote(got.at[3 * items + q], from_low.at[slot], zu_send.at[slot], zu_recv.at[slot], up)

    def send_down(q):
        slot = high_slot(q)
        return remote(got.at[3 * items + q], from_high.at[slot], zd_send.at[slot], zd_recv.at[slot], down)

    def l_column(group):
        xo, yo = columns[group]
        return 2 * xo + yo

    def l_up(group, k):
        at, zd = l_column(group), order[k] - 1
        return remote(l_got.at[4 * group + k], l_low.at[at, zd], lu_send.at[at, zd], lu_recv.at[at, zd], up)

    def l_down(group, k):
        at, zd = l_column(group), order[k]
        return remote(l_got.at[4 * group + k], l_high.at[at, zd], ld_send.at[at, zd], ld_recv.at[at, zd], down)

    def l_half_x():
        return remote(l_got.at[3, pl.ds(LIGHT_CUT, SMALL_HALF - LIGHT_CUT)], l_halves_x,
                      hx_send.at[items], hx_recv.at[items], x_side)

    def l_half_y():
        return remote(l_got.at[3, pl.ds(0, LIGHT_CUT)], l_halves_y, hy_send.at[items], hy_recv.at[items], y_side)

    def l_send_y():
        return remote(l_got.at[7], l_from_y, y_send.at[items], y_recv.at[items], y_side)

    def l_send_x():
        return remote(l_got.at[11], l_from_x, x_send.at[items], x_recv.at[items], x_side)

    leaving = (wide0, wide1, wide1, final)

    def pairs(section, micro):
        source = leaving[section]
        yield source.at[pl.ds(0, STUD_ROWS)], seg_stud.at[micro], seg_send.at[0, section], seg_recv.at[0, micro]
        yield source.at[pl.ds(STUD_ROWS, TEACH_END)], seg_teach.at[micro], seg_send.at[1, section], seg_recv.at[1, micro]
        yield stats.at[section], out_stats.at[micro], stat_send.at[section], stat_recv.at[micro]

    def exchange(section):
        return [remote(*pair, {"dp": me.dp, "pipe": section}) for pair in pairs(section, me.pipe)]

    def keep(section):
        return [pltpu.make_async_copy(src, dst, send) for src, dst, send, _ in pairs(section, me.pipe)]

    def arriving(micro):
        return [remote(*pair, {"dp": me.dp, "pipe": micro}) for pair in pairs(micro, micro)]

    for n in range(4 * items):
        share(*sequence[n]).start()
        if n == 5:
            for item in l_sequence:
                l_share(*item).start()
    for n in range(2):
        fetch(n).start()
    for group, k in l_sequence:
        l_fetch(group, k).start()
    row_copy = pltpu.make_async_copy(table.at[2 * x], owner_row, out_sem.at[2])
    row_copy.start()

    def bulk_item(n):
        group, k = sequence[n]
        at, slot = items * group + k, n % 4
        if n + 2 < 4 * items:
            fetch(n + 2).start()
        fetch(n).wait()
        share(group, k).wait_recv()
        if group == 0:
            add(got, at, stage, slot, 0, PART_ROWS, [])
            send_half_x(k).start()
            send_half_y(k).start()
        elif group == 1:
            send_half_x(k).wait_recv()
            add(got, at, stage, slot, 0, BACK_CUT, [])
            add(got, at, stage, slot, BACK_CUT, PART_ROWS - BACK_CUT, [(halves_x, k)])
            send_y(k).start()
        elif group == 2:
            send_half_y(k).wait_recv()
            add(got, at, stage, slot, 0, BACK_CUT, [(halves_y, k)])
            add(got, at, stage, slot, BACK_CUT, PART_ROWS - BACK_CUT, [])
            send_x(k).start()
        else:
            send_x(k).wait_recv()
            send_y(k).wait_recv()
            add(got, at, stage, slot, 0, PART_ROWS, [(from_x, k), (from_y, k)])

    def bulk_z(q):
        at, zd = 3 * items + q, order[q // PARTS]

        @pl.when(zd > z)
        def _():
            @pl.when(z > 0)
            def _():
                send_up(q).wait_recv()
                add(got, at, from_low, low_slot(q), 0, PART_ROWS, [])

            send_up(q).start()

        @pl.when(zd < z)
        def _():
            @pl.when(z < 3)
            def _():
                send_down(q).wait_recv()
                add(got, at, from_high, high_slot(q), 0, PART_ROWS, [])

            send_down(q).start()

    def light_item(group, k):
        at, zd, column = 4 * group + k, order[k], l_column(group)
        l_fetch(group, k).wait()
        l_share(group, k).wait_recv()
        add(l_got, at, l_stage, at, 0, SMALL_HALF, [])

        def merge(ref, slot):
            l_got[at] = (l_got[at].astype(FULL) + ref[column, slot].astype(FULL)).astype(LOW)

        if k < 3:

            @pl.when(zd > z)
            def _():
                @pl.when(z > 0)
                def _():
                    l_up(group, k).wait_recv()
                    merge(l_low, zd - 1)

                l_up(group, k).start()

            @pl.when(zd < z)
            def _():
                @pl.when(z < 3)
                def _():
                    l_down(group, k).wait_recv()
                    merge(l_high, zd)

                l_down(group, k).start()

        else:

            @pl.when(z > 0)
            def _():
                l_up(group, k).wait_recv()
                merge(l_low, zd - 1)

            @pl.when(z < 3)
            def _():
                l_down(group, k).wait_recv()
                merge(l_high, zd)

            if group == 0:
                l_half_x().start()
                l_half_y().start()

    def light_sides():
        l_half_x().wait_recv()
        l_got[7, LIGHT_CUT:SMALL_HALF, :] = (
            l_got[7, LIGHT_CUT:SMALL_HALF, :].astype(FULL) + l_halves_x[...].astype(FULL)
        ).astype(LOW)
        l_send_y().start()
        l_half_y().wait_recv()
        l_got[11, 0:LIGHT_CUT, :] = (
            l_got[11, 0:LIGHT_CUT, :].astype(FULL) + l_halves_y[...].astype(FULL)
        ).astype(LOW)
        l_send_x().start()

    def light_end():
        l_send_x().wait_recv()
        l_send_y().wait_recv()
        l_total[...] = l_got[15].astype(FULL) + l_from_x[...].astype(FULL) + l_from_y[...].astype(FULL)

    small_join = remote(late_half, late.at[pl.ds(0, SMALL_HALF)], join_send.at[0], join_recv.at[0], sibling)
    own_late = pltpu.make_async_copy(late, out_small.at[me.dp], out_sem.at[1])

    def late_z(origin, target, way):
        block = out_small.at[2 * origin + y]
        return remote(block, block, late_send.at[way, origin], late_recv.at[0, origin], target)

    def late_y(origin, yo):
        block = out_small.at[2 * origin + yo]
        return remote(block, block, late_send.at[2, origin], late_recv.at[1, origin], y_side)

    def late_step(k):
        @pl.when((core == 1) & (z >= k))
        def _():
            late_z(z - k, up, 0).wait_recv()
            pl.when(z < 3)(lambda: late_z(z - k, up, 0).start())
            late_y(z - k, y).start()

        @pl.when((core == 1) & (z + k <= 3))
        def _():
            late_z(z + k, down, 1).wait_recv()
            pl.when(z > 0)(lambda: late_z(z + k, down, 1).start())
            late_y(z + k, y).start()

    def leave():
        for section in range(4):
            @pl.when(me.pipe == section)
            def _(section=section):
                all_of(keep(section), lambda copy: copy.start())

            @pl.when(me.pipe != section)
            def _(section=section):
                all_of(exchange(section), lambda copy: copy.start())

    def late_start():
        light_end()

        @pl.when(core == 0)
        def _():
            late_half[...] = l_total[...].astype(LOW)
            small_join.start()

        @pl.when(core == 1)
        def _():
            late[SMALL_HALF:SMALL_ROWS, :] = l_total[...].astype(LOW)
            small_join.wait_recv()
            own_late.start()
            own_late.wait()
            pl.when(z < 3)(lambda: late_z(z, up, 0).start())
            pl.when(z > 0)(lambda: late_z(z, down, 1).start())
            late_y(z, y).start()

    def light_round(k):
        for n in range(4 * k, 4 * k + 4):
            light_item(*l_sequence[n])

    edge = (z == 0) | (z == 3)

    def early_z(k):
        pl.when(edge)(lambda: bulk_z(k))

    def inner_z(k):
        pl.when(jnp.logical_not(edge))(lambda: bulk_z(k))

    actions = {"LS": [light_sides], "LE": [late_start], "G": [leave]}
    numbered = {item: n for n, item in enumerate(sequence)}
    for k in range(4):
        actions["L%d" % k] = [functools.partial(light_round, k)]
        if k:
            actions["T%d" % k] = [functools.partial(late_step, k)]
    for q in range(items):
        for letter, group in (("A", 0), ("C", 1), ("B", 2), ("O", 3)):
            actions["%s%d" % (letter, q)] = [functools.partial(bulk_item, numbered[group, q])]
        if q < 3 * PARTS:
            actions["E%d" % q] = [functools.partial(early_z, q)]
            actions["I%d" % q] = [functools.partial(inner_z, q)]
    for event in REDUCE_ORDER:
        for action in actions[event]:
            action()

    row_copy.wait()
    part_sum[...] = jnp.sum((l_total[...] * l_total[...]).reshape(SMALL_HALF // 8, 8, 128), axis=0)
    lane = lax.broadcasted_iota(jnp.int32, (8, 128), 1)
    is_last = jnp.where((lane == me.dp) & (owner_row[...] == 7), 1.0, 0.0)
    weight = jnp.broadcast_to(jnp.sum(is_last, axis=1, keepdims=True), (8, 128))
    weight = jnp.where(core == 0, jnp.ones((8, 128), FULL), weight)

    big_parts = [pl.ds(PART_ROWS * n, PART_ROWS) for n in range(PARTS)]

    def big_join(n):
        return remote(total.at[big_parts[n]], out_big.at[1, big_parts[n]],
                      join_send.at[1 + n], join_recv.at[1 + n], sibling)

    def own_big(n):
        return pltpu.make_async_copy(total.at[big_parts[n]], out_big.at[0, big_parts[n]], big_sem.at[n])

    def end(n, low, high):
        q = 3 * PARTS + n

        def piece(begin, size, scale):
            part = pl.ds(begin, size)
            sums = got[3 * items + q, part, :].astype(FULL)
            if low:
                sums = sums + from_low[low_slot(q), part, :].astype(FULL)
            if high:
                sums = sums + from_high[high_slot(q), part, :].astype(FULL)
            total[pl.ds(PART_ROWS * n + begin, size), :] = sums
            squares = jnp.sum((sums * sums).reshape(size // 8, 8, 128), axis=0)
            part_sum[...] += squares if scale is None else squares * scale

        def plain(begin, size):
            piece(begin, size, None)

        if n < PARTS - 1:
            over(0, PART_ROWS, plain)
        else:
            over(0, PART_ROWS - EDGE, plain)
            piece(PART_ROWS - EDGE, EDGE, weight)

    for n in range(PARTS):
        q = 3 * PARTS + n

        @pl.when(z == 0)
        def _(n=n, q=q):
            send_down(q).wait_recv()
            end(n, False, True)

        @pl.when((z > 0) & (z < 3))
        def _(n=n, q=q):
            send_up(q).wait_recv()
            send_down(q).wait_recv()
            end(n, True, True)

        @pl.when(z == 3)
        def _(n=n, q=q):
            send_up(q).wait_recv()
            end(n, True, False)

        @pl.when(core == 0)
        def _(n=n):
            own_big(n).start()

        @pl.when(core == 1)
        def _(n=n):
            big_join(n).start()

    def along_pipe(step, slot):
        target = {"dp": me.dp, "pipe": lax.rem(me.pipe + step, 4)}
        return remote(part_sum, by_pipe.at[slot], p_send.at[step], p_recv.at[step], target)

    def along_dp(step, slot):
        target = {"dp": lax.rem(me.dp + step, 8), "pipe": me.pipe}
        return remote(mine, by_dp.at[slot], d_send.at[step], d_recv.at[step], target)

    for step in range(1, 4):
        along_pipe(step, me.pipe).start()
    by_pipe[me.pipe] = part_sum[...]
    for step in range(1, 4):
        along_pipe(step, lax.rem(me.pipe + 4 - step, 4)).wait_recv()
    mine[...] = jnp.sum(by_pipe[...], axis=0)
    for step in range(1, 8):
        along_dp(step, me.dp).start()
    by_dp[me.dp] = mine[...]
    for step in range(1, 8):
        along_dp(step, lax.rem(me.dp + 8 - step, 8)).wait_recv()
    whole = jnp.sum(jnp.sum(by_dp[...], axis=0), axis=0, keepdims=True)
    length = jnp.sqrt(jnp.broadcast_to(jnp.sum(whole, axis=1, keepdims=True), (8, 128)))
    norm[...] = length
    factor[...] = jnp.minimum(1.0, CLIP_NORM / length)

    @pl.when(core == 0)
    def _():
        for n in range(PARTS):
            own_big(n).wait()
            big_join(n).wait_recv()
        small_join.wait_send()

    @pl.when(core == 1)
    def _():
        for n in range(PARTS):
            big_join(n).wait_send()
        for origin in range(4):
            late_y(origin, 1 - y).wait_recv()
            late_y(origin, y).wait_send()
            pl.when((z < 3) & (origin <= z))(lambda: late_z(origin, up, 0).wait_send())
            pl.when((z > 0) & (origin >= z))(lambda: late_z(origin, down, 1).wait_send())

    for other in range(4):
        @pl.when(me.pipe == other)
        def _(other=other):
            all_of(keep(other), lambda copy: copy.wait())

        @pl.when(me.pipe != other)
        def _(other=other):
            all_of(exchange(other), lambda copy: copy.wait_send())
            all_of(arriving(other), lambda copy: copy.wait_recv())

    for step in range(1, 4):
        along_pipe(step, me.pipe).wait_send()
    for step in range(1, 8):
        along_dp(step, me.dp).wait_send()
    for copy in (l_half_x(), l_half_y(), l_send_x(), l_send_y()):
        copy.wait_send()
    for q in range(items):
        send_half_x(q).wait_send()
        send_half_y(q).wait_send()
        send_x(q).wait_send()
        send_y(q).wait_send()
        for group in range(4):
            share(group, q).wait_send()
    for group, k in l_sequence:
        l_share(group, k).wait_send()
    for k in range(3):
        zd = order[k]

        @pl.when(zd > z)
        def _(k=k):
            for n in range(PARTS):
                send_up(PARTS * k + n).wait_send()
            for group in range(4):
                l_up(group, k).wait_send()

        @pl.when(zd < z)
        def _(k=k):
            for n in range(PARTS):
                send_down(PARTS * k + n).wait_send()
            for group in range(4):
                l_down(group, k).wait_send()


def reduce_all(big, small, wide0, wide1, final, stats, table):
    sem = pltpu.SemaphoreType.DMA
    vm = pltpu.VMEM
    items = 4 * PARTS
    lane_tile = jax.ShapeDtypeStruct((8, 128), FULL)
    return pl.pallas_call(
        reduce_kernel,
        name="reduce_all",
        out_shape=(
            jax.ShapeDtypeStruct((2, BIG_HALF, 128), FULL),
            jax.ShapeDtypeStruct((8, SMALL_ROWS, 128), LOW),
            jax.ShapeDtypeStruct((4, STUD_ROWS, C_OUT), LOW),
            jax.ShapeDtypeStruct((4, TEACH_END, C_OUT), LOW),
            jax.ShapeDtypeStruct((4,) + stats.shape[1:], FULL),
            lane_tile,
            lane_tile,
        ),
        in_specs=[any_spec()] * 7,
        out_specs=(any_spec(),) * 5 + (vmem_spec(),) * 2,
        scratch_shapes=[
            vm((4 * items, PART_ROWS, 128), LOW),
            vm((items, PART_ROWS - BACK_CUT, 128), LOW), vm((items, BACK_CUT, 128), LOW),
            vm((items, PART_ROWS, 128), LOW), vm((items, PART_ROWS, 128), LOW),
            vm((3 * PARTS, PART_ROWS, 128), LOW), vm((3 * PARTS, PART_ROWS, 128), LOW),
            vm((4, PART_ROWS, 128), LOW), vm((BIG_HALF, 128), FULL),
            vm((16, SMALL_HALF, 128), LOW), vm((16, SMALL_HALF, 128), LOW),
            vm((4, 3, SMALL_HALF, 128), LOW), vm((4, 3, SMALL_HALF, 128), LOW),
            vm((SMALL_HALF - LIGHT_CUT, 128), LOW), vm((LIGHT_CUT, 128), LOW),
            vm((SMALL_HALF, 128), LOW), vm((SMALL_HALF, 128), LOW), vm((SMALL_HALF, 128), FULL),
            vm((SMALL_ROWS, 128), LOW), vm((SMALL_HALF, 128), LOW), vm((8, 128), jnp.int32),
            vm((4, 8, 128), FULL), vm((8, 8, 128), FULL), vm((8, 128), FULL), vm((8, 128), FULL),
            sem((4 * items,)), sem((4 * items,)), sem((16,)), sem((16,)),
            sem((items + 1,)), sem((items + 1,)), sem((items + 1,)), sem((items + 1,)),
            sem((items + 1,)), sem((items + 1,)), sem((items + 1,)), sem((items + 1,)),
            sem((3 * PARTS,)), sem((3 * PARTS,)), sem((3 * PARTS,)), sem((3 * PARTS,)),
            sem((4, 3)), sem((4, 3)), sem((4, 3)), sem((4, 3)),
            sem((4,)), sem((16,)), sem((3,)), sem((PARTS,)), sem((3, 4)), sem((2, 4)),
            sem((1 + PARTS,)), sem((1 + PARTS,)),
            sem((2, 4)), sem((2, 4)), sem((4,)), sem((4,)), sem((4,)), sem((4,)), sem((8,)), sem((8,)),
        ],
        compiler_params=pltpu.CompilerParams(
            collective_id=1, has_side_effects=True, vmem_limit_bytes=62 << 20
        ),
    )(big.reshape(2, 8, 2, BIG_HALF, 128), small.reshape(2, 8, 2, SMALL_HALF, 128),
      wide0, wide1, final, stats, table)


def high_dot(a, b, dims=((1,), (0,))):
    return lax.dot_general(a, b, (dims, ((), ())), precision=HIGH, preferred_element_type=FULL)


PIECES = 7
FRONT = 48


def update_kernel(owners, factor_ref, norm, big, small, gram_old, basis_old, params, moment, second, stats,
                  clipped, moment_new, second_new, params_new, gram_new, basis_new, length, out_stats,
                  tiles, low, grad, held, rotated, weights, gram, in_sem, out_sem, tile_sem, stat_sem):
    factor = factor_ref[0:1, :]
    length[0, 0] = jnp.max(norm[...])
    block, section = owners[0, lax.axis_index("dp")], lax.axis_index("pipe")
    even = lax.rem(section, 2) == 0
    span = params.shape[0]
    piece = held.shape[0] // PIECES

    stat_copies = [
        pltpu.make_async_copy(stats.at[m, pl.ds(0, 2)], out_stats.at[m], stat_sem.at[m])
        for m in range(stats.shape[0])
    ]
    for copy in stat_copies:
        copy.start()
    quarter = WINDOW // 4 * TILE

    def big_load(i):
        part = pl.ds(quarter * i, min(quarter, BIG_ROWS - quarter * i))
        return pltpu.make_async_copy(big.at[part], tiles.at[part], tile_sem.at[i])

    @pl.when(even)
    def _():
        for i in range(4):
            big_load(i).start()

    first_small = pltpu.make_async_copy(small.at[0:20], low, tile_sem.at[0])
    second_small = pltpu.make_async_copy(small.at[19:33], low.at[0:14], tile_sem.at[0])

    @pl.when(jnp.logical_not(even))
    def _():
        pl.when(block == 0)(lambda: first_small.start())

        @pl.when(block == 1)
        def _():
            second_small.start()
            low[14:20] = jnp.zeros((6, TILE, 128), LOW)

        @pl.when(block > 1)
        def _():
            low[...] = jnp.zeros_like(low)

    def loads(i):
        part = pl.ds(piece * i, min(piece, span - piece * i))
        for n, (src, dst) in enumerate(((params, weights), (moment, held), (second, rotated))):
            yield pltpu.make_async_copy(src.at[part, 0, :], dst.at[part], in_sem.at[n, i])

    def stores(i):
        count = min(piece, span - piece * i)
        part = pl.ds(piece * i, count)
        yield pltpu.make_async_copy(
            grad.at[pl.ds(FRONT + piece * i, count)], clipped.at[part, 0, :], out_sem.at[3, i])
        pairs = ((held, moment_new), (rotated, second_new), (weights, params_new))
        for n, (src, dst) in enumerate(pairs):
            yield pltpu.make_async_copy(src.at[part], dst.at[part, 0, :], out_sem.at[n, i])

    for i in range(PIECES):
        for load in loads(i):
            load.start()

    @pl.when(jnp.logical_not(even))
    def _():
        pl.when(block == 0)(lambda: first_small.wait())
        pl.when(block == 1)(lambda: second_small.wait())

        @pl.loop(0, WINDOW)
        def _(r):
            tiles[pl.ds(pl.multiple_of(TILE * r, TILE), TILE), :] = low[r].astype(FULL)

    def lay_flat(r):
        narrow, plain = tile_forms(section, STRIDE * block + r)
        edge = even & (r == STRIDE)
        narrow, plain = narrow & jnp.logical_not(edge), plain | edge
        base = FRONT - 6 * block + TILE * r
        here = pl.multiple_of(TILE * r, TILE)

        @pl.when(narrow)
        def _():
            for j in range(4):
                grad[pl.ds(base + j, 64, 4), :] = tiles[pl.ds(here + 64 * j, 64), :]

        @pl.when(plain)
        def _():
            grad[pl.ds(base, TILE), :] = tiles[pl.ds(here, TILE), :]

        @pl.when(jnp.logical_not(narrow | plain))
        def _():
            for j in range(16):
                grad[pl.ds(base + j, 16, 16), :] = tiles[pl.ds(here + 16 * j, 16), :]

    for i in range(4):
        pl.when(even)(lambda: big_load(i).wait())
        pl.loop(WINDOW // 4 * i, WINDOW // 4 * (i + 1))(lay_flat)

    tail = piece * PIECES - 8
    rest = lax.broadcasted_iota(jnp.int32, (8, 128), 0) + tail
    grad[FRONT + tail : FRONT + tail + 8, :] = jnp.where(
        rest < span, grad[FRONT + tail : FRONT + tail + 8, :], 0.0
    )
    gram[...] = jnp.zeros_like(gram)

    def halves(value):
        high = value.astype(LOW)
        return high, (value - high.astype(FULL)).astype(LOW)

    def split_dot(a, b, dims=((1,), (0,))):
        def dot(left, right):
            return lax.dot_general(left, right, (dims, ((), ())), preferred_element_type=FULL)

        return dot(a[0], b[0]) + (dot(a[0], b[1]) + dot(a[1], b[0]))

    @pl.loop(0, PIECES)
    def _(i):
        part = halves(grad[pl.ds(pl.multiple_of(FRONT + piece * i, 8), piece), :])
        gram[...] += split_dot(part, part, ((0,), (0,)))

    old = basis_old[...]
    fresh = DECAY_STATS * gram_old[...] + (1.0 - DECAY_STATS) * (gram[...] * (factor * factor))
    gram_new[...] = fresh
    product = high_dot(fresh, old)
    rotation = product / jnp.sqrt(jnp.sum(product * product))
    for repeat in range(NS_STEPS):
        parts = halves(rotation)
        square = split_dot(parts, parts, ((0,), (0,)))
        rotation = 1.5 * rotation - 0.5 * split_dot(parts, halves(square))
    basis_new[...] = rotation
    change = halves(high_dot(old, rotation, ((0,), (0,))))
    turn = halves(rotation)
    correction = math.sqrt(1.0 - DECAY_SECOND**STEP) / (1.0 - DECAY_FIRST**STEP)
    for i in range(PIECES):
        for load in loads(i):
            load.wait()
        at = slice(FRONT + piece * i, FRONT + piece * i + piece)
        part = slice(piece * i, piece * i + piece)
        clip = grad[at, :] * factor
        grad[at, :] = clip
        turned = split_dot(halves(clip), turn)
        first = DECAY_FIRST * split_dot(halves(held[part, :]), change) + (1.0 - DECAY_FIRST) * turned
        power = DECAY_SECOND * rotated[part, :] + (1.0 - DECAY_SECOND) * turned * turned
        held[part, :] = first
        rotated[part, :] = power
        scaled = halves(first / (jnp.sqrt(power) + ADAM_EPS))
        direction = split_dot(scaled, turn, ((1,), (1,))) * correction
        before = weights[part, :]
        weights[part, :] = before - LEARN_RATE * (direction + WEIGHT_DECAY * before)
        for store in stores(i):
            store.start()
    for i in range(PIECES):
        for store in stores(i):
            store.wait()
    for copy in stat_copies:
        copy.wait()


def update(owners, factor, norm, big, small, gram_old, basis_old, params, moment, second, stats):
    span = params.shape[1] // 128
    rows = -(-span // (8 * PIECES)) * 8 * PIECES
    flat_shape = jax.ShapeDtypeStruct((span, 1, 128), FULL)
    square = jax.ShapeDtypeStruct((128, 128), FULL)
    sem = pltpu.SemaphoreType.DMA
    vm = pltpu.VMEM
    outs = pl.pallas_call(
        update_kernel,
        name="update",
        out_shape=(flat_shape,) * 4 + (square,) * 2 + (jax.ShapeDtypeStruct((1, 1), FULL), jax.ShapeDtypeStruct((4, 2) + stats.shape[2:], FULL)),
        in_specs=[smem_spec()] + [vmem_spec()] * 2 + [any_spec()] * 2 + [vmem_spec()] * 2 + [any_spec()] * 4,
        out_specs=(any_spec(),) * 4 + (vmem_spec(),) * 2 + (smem_spec(), any_spec()),
        scratch_shapes=[
            vm((WINDOW * TILE, 128), FULL), vm((WINDOW, TILE, 128), LOW),
            vm((FRONT + WINDOW * TILE, 128), FULL), vm((rows, 128), FULL), vm((rows, 128), FULL),
            vm((rows, 128), FULL), vm((128, 128), FULL), sem((3, PIECES)), sem((4, PIECES)), sem((4,)), sem((4,)),
        ],
        compiler_params=pltpu.CompilerParams(vmem_limit_bytes=60 << 20),
    )(owners, factor, norm, big.reshape(BIG_ROWS, 128), small.reshape(USED_TILES[1], TILE, 128),
      gram_old, basis_old, params.reshape(span, 1, 128), moment.reshape(span, 1, 128),
      second.reshape(span, 1, 128), stats)
    return tuple(out.reshape(1, span * 128) for out in outs[:4]) + outs[4:]


def on_small_slice(
    teach_in,
    stud_in,
    params,
    owners,
    depth_gates,
    teach_ids,
    stud_ids,
    targets,
    moment,
    second,
    gram_stats,
    eigen_basis,
):
    teach_shape, stud_shape = teach_in.shape[1:], stud_in.shape[1:]
    teach_x = teach_in[0].transpose(1, 2, 0, 3).reshape(-1, teach_shape[0], C_IN)
    stud_x = stud_in[0].reshape(-1, C_IN)
    big, small, ids = prepare(owners, params)
    all_big, all_small, table = gather_all(big, small, ids)
    wide_0, wide_1, final, stats, teach_grad, stud_grad, out_big, out_small = run_step(
        table,
        depth_gates,
        teach_ids.T,
        stud_ids,
        all_big.reshape(2, 8, BIG_ROWS, 128),
        all_small.reshape(2, USED_TILES[1], TILE, 128),
        teach_x,
        stud_x,
        targets,
    )
    sum_big, sum_small, segment_stud, segment_teach, stats, norm, factor = reduce_all(
        out_big, out_small, wide_0, wide_1, final, stats, table
    )
    clipped, moment_new, second_new, params_new, gram_new, rotation, length, stats = update(
        owners, factor, norm, sum_big, sum_small, gram_stats[0], eigen_basis[0], params, moment, second, stats
    )
    small_teach = (teach_shape[1] // 2, teach_shape[2] // 2, teach_shape[0], C_OUT)
    small_stud = (stud_shape[0], stud_shape[1] // 2, stud_shape[2] // 2, C_OUT)
    segment_teach = segment_teach[:, : ROWS - STUD_ROWS].reshape((4,) + small_teach).transpose(0, 3, 1, 2, 4)
    segment_stud = segment_stud.reshape((4,) + small_stud)
    teach_grad = teach_grad.reshape(teach_shape[1:3] + (teach_shape[0], C_IN)).transpose(2, 0, 1, 3)
    stud_grad = stud_grad.reshape(stud_shape)
    grad_norm = length.reshape(())
    return (
        segment_teach[None],
        segment_stud[None],
        teach_grad[None],
        stud_grad[None],
        stats[None, :, None],
        grad_norm,
        clipped,
        moment_new,
        second_new,
        params_new,
        gram_new[None],
        rotation[None],
    )


def solution(mesh):
    placed = (
        P("pipe", "dp", None, None, None),
        P("pipe", "dp", None, None, None),
        P("pipe", "dp"),
        P("pipe", None),
        P(),
        P(None, "dp"),
        P(None, "dp"),
        P(),
        P("pipe", "dp"),
        P("pipe", "dp"),
        P("pipe", "dp", None),
        P("pipe", "dp", None),
    )
    small_slice = mesh.shape["dp"] == 8 and mesh.shape["pipe"] == 4
    return jax.shard_map(
        on_small_slice if small_slice else on_device,
        mesh=mesh,
        in_specs=placed,
        out_specs=(
            P("pipe", None, "dp", None, None, None),
            P("pipe", None, "dp", None, None, None),
            P("pipe", "dp", None, None, None),
            P("pipe", "dp", None, None, None),
            P("pipe", None, "dp", None, None),
            P(),
            P("pipe", "dp"),
            P("pipe", "dp"),
            P("pipe", "dp"),
            P("pipe", "dp"),
            P("pipe", "dp", None),
            P("pipe", "dp", None),
        ),
        check_vma=False,
    )
```
